32 devices in a mesh: dp: 8 (over y, x, core), tensor: 4 (over z).
Axes of the slice: x: 2, y: 2, z: 4, core: 2. Of those that a mesh axis runs over, the one named last changes fastest.
Arguments:
- hidden_in: bfloat16 [8, 1024, 1152], P('dp', 'tensor'), may hold values from -6 to 6
- time_embed: float32 [8, 6, 1152], P('dp'), may hold values from -3 to 3
- caption_table: bfloat16 [32128, 1152], P('dp', 'tensor'), may hold values from -6 to 6
- caption_ids: int32 [8, 120], P('dp'), may hold values from 0 to 32127
- owners: int32 [64], replicated, may hold values from 0 to 7, as said below
- master: float32 [128, 288, 1152], P('dp', 'tensor')
- first_moment: float32 [128, 288, 1152], P('dp', 'tensor')
- second_moment: float32 [128, 288, 1152], P('dp', 'tensor'), as said below
- mod_table: float32 [6, 1152], replicated, may hold values from -3 to 3
- mod_first: float32 [6, 1152], replicated
- mod_second: float32 [6, 1152], replicated, as said below
- out_grad: bfloat16 [8, 1024, 1152], P('dp', 'tensor'), may hold values from -6 to 6
Outputs:
- block_out: float32 [8, 1024, 1152], P('dp', 'tensor')
- input_grad: float32 [8, 1024, 1152], P('dp', 'tensor')
- new_first: float32 [128, 288, 1152], P('dp', 'tensor')
- new_second: float32 [128, 288, 1152], P('dp', 'tensor')
- new_master: float32 [128, 288, 1152], P('dp', 'tensor')
- mod_new_first: float32 [6, 1152], replicated
- mod_new_second: float32 [6, 1152], replicated
- mod_new: float32 [6, 1152], replicated
The draws below stay inside these ranges and needn't reach their ends.
Inputs may be any that keep to these rules, and one draw needn't show every extreme that they name: `owners`: each index of dp owns at most 16 row blocks, and some index owns exactly 16. `second_moment`: positive in every entry. `mod_second`: positive in every entry.
All inputs are finite; a program needn't handle non-finite values.
Results may differ from the reference program's by a relative error of at most 0.03.
Values may be sent and summed in bfloat16 or wider, within the bound.
No kernel may reach another device: no remote copies, remote signals or barrier semaphores. Data moves between devices by JAX's collectives and lax.ppermute only.
A program may use at most 256 MiB of HBM per device.

```python
import math
import jax
import jax.numpy as jnp
import numpy as np
from jax import lax

D = 1152
HEADS = 16
HEAD_DIM = 72
FF = 4608
VOCAB = 32128
TXT = 120
LENGTH = 1024
BLOCK_ROWS = 72
STEP = 10
LATENTS = 8
UNITS = 64
CAP = 16
SLOTS = 128
WROWS = 288
N_TENSOR = 4


def owner_list(key):
    key = jax.random.fold_in(key, 101)
    dev_key, rank_key, map_key = jax.random.split(key, 3)
    device_total = SLOTS // CAP
    chosen_dev = jax.random.randint(dev_key, (), 0, device_total)
    priority = jax.random.permutation(rank_key, SLOTS).astype(jnp.int32)
    slot_ids = jnp.arange(SLOTS, dtype=jnp.int32)
    score = priority - SLOTS * (slot_ids // CAP == chosen_dev).astype(jnp.int32)
    picked = jnp.argsort(score)[:UNITS]
    mapping = jax.random.permutation(map_key, UNITS)
    return (picked[mapping] // CAP).astype(jnp.int32)


def section_rows(owners):
    index = jnp.arange(UNITS)
    before = (owners[None, :] == owners[:, None]) & (index[None, :] < index[:, None])
    slot_of = owners * CAP + jnp.sum(before.astype(jnp.int32), axis=1)
    match = slot_of[None, :] == jnp.arange(SLOTS)[:, None]
    unit_of = jnp.sum(jnp.where(match, index[None, :], 0), axis=1)
    lane_rows = jnp.arange(WROWS) % BLOCK_ROWS
    position = unit_of[:, None] * BLOCK_ROWS + lane_rows[None, :]
    ranks = WROWS // BLOCK_ROWS
    row_share = D // ranks
    hidden_share = FF // ranks
    bounds = jnp.array([row_share * step_k for step_k in range(1, 9)] + [8 * row_share + hidden_share], jnp.int32)
    return jnp.sum((position[:, :, None] >= bounds[None, None, :]).astype(jnp.int32), axis=2)


def weight_spread():
    return jnp.array([1.18, 1.18, 1.0, 3.6, 1.18, 1.18, 1.0, 1.6, 1.0, 1.7 * (D / FF) ** 0.5], jnp.float32) * D ** (-0.5)


def grad_spread():
    return jnp.array([0.6, 0.6, 0.8, 0.3, 0.6, 0.8, 1.2, 0.7, 0.45, 0.45], jnp.float32) * (LENGTH * LATENTS) ** 0.5


def draw_owners(key, part):
    return owner_list(key)


def draw_master(key, part):
    section = section_rows(owner_list(key))
    key = jax.random.fold_in(key, 1)
    noise = jax.random.normal(key, (SLOTS, WROWS, D), jnp.float32)
    return noise * weight_spread()[section][:, :, None]


def draw_first_moment(key, part):
    section = section_rows(owner_list(key))
    key = jax.random.fold_in(key, 2)
    noise = jax.random.normal(key, (SLOTS, WROWS, D), jnp.float32)
    return noise * (0.1111 * grad_spread()[section][:, :, None])


def draw_second_moment(key, part):
    section = section_rows(owner_list(key))
    key = jax.random.fold_in(key, 3)
    factor = jnp.exp(jax.random.uniform(key, (SLOTS, WROWS, D), jnp.float32, 0.0, 1.3862944))
    size_sq = grad_spread()[section][:, :, None] ** 2
    return 0.001001 * size_sq * factor


def draw_mod_first(key, part):
    key = jax.random.fold_in(key, 4)
    noise = jax.random.normal(key, (6, D), jnp.float32)
    return noise * (0.1111 * (LENGTH * LATENTS) ** 0.5)


def draw_mod_second(key, part):
    key = jax.random.fold_in(key, 5)
    factor = jnp.exp(jax.random.uniform(key, (6, D), jnp.float32, 0.0, 1.3862944))
    return 0.001001 * (LENGTH * LATENTS) * factor


def with_ends(values, rng, low, top_value):
    longest = values.shape.index(max(values.shape))
    spots = []
    for shift in (0, 1):
        where = [jax.random.randint(jax.random.fold_in(rng, axis), (), 0, length) for axis, length in enumerate(values.shape)]
        where[longest] = (where[longest] + shift) % values.shape[longest]
        spots.append(tuple(where))
    return values.at[spots[0]].set(low).at[spots[1]].set(top_value)


def block_scale(key, dims, cuts, low, high):
    def one(dim, blocks):
        steps = jax.random.uniform(jax.random.fold_in(jax.random.fold_in(key, 6), dim), (blocks,), jnp.float32, low / len(cuts), high / len(cuts))
        return jnp.repeat(jnp.exp(steps), dims[dim] // blocks).reshape((-1,) + (1,) * (len(dims) - dim - 1))

    factor_of = one(*cuts[0])
    for cut in cuts[1:]:
        factor_of = factor_of * one(*cut)
    return factor_of


def rank_table(number_of, slope):
    loads = [(1 << 20) // math.isqrt(standing ** slope) + 1 for standing in range(1, number_of + 1)]
    scale = 1 + sum(loads) // (1 << 30)
    return np.cumsum(np.array([max(1, weight // scale) for weight in loads]))


def ranked_ids(own_key, dims, count, slope):
    listing = rank_table(count, slope)
    ticket = jax.random.randint(jax.random.fold_in(own_key, 1), dims, 0, int(listing[count - 1]))
    grade = jnp.searchsorted(jnp.asarray(listing, jnp.int32), ticket, side="right")
    return jax.random.permutation(jax.random.fold_in(own_key, 2), count)[grade].astype(jnp.int32)


def gaussian(rng, shape, scale, most, cuts=(), held_as=jnp.bfloat16):
    drawn = scale * jax.random.normal(rng, shape, jnp.float32)
    if cuts:
        drawn = drawn * block_scale(rng, shape, cuts, -0.22, 0.18)
    return jnp.clip(drawn, -most, most).astype(held_as)


def setup_inputs(seed: int = 0) -> dict:
    key_list = jax.random.split(jax.random.key(seed), 13)
    hidden_in = gaussian(key_list[0], (LATENTS, LENGTH, D), 1.0, 6.0, ((0, 8), (1, 4)))
    time_embed = gaussian(key_list[1], (LATENTS, 6, D), 0.35, 3.0, ((0, 8),), jnp.float32)
    caption_table = gaussian(key_list[2], (VOCAB, D), 1.0, 6.0, ((0, 8), (1, 4)))
    caption_ids = with_ends(ranked_ids(key_list[3], (LATENTS, TXT), VOCAB, 1), jax.random.fold_in(key_list[3], 3), 0, VOCAB - 1).astype(jnp.int32)
    owners = draw_owners(jax.random.fold_in(key_list[12], 71), 0)
    master = draw_master(jax.random.fold_in(key_list[12], 71), 0)
    first_moment = draw_first_moment(jax.random.fold_in(key_list[12], 71), 0)
    second_moment = draw_second_moment(jax.random.fold_in(key_list[12], 71), 0)
    mod_table = gaussian(key_list[8], (6, D), 0.35, 3.0, (), jnp.float32)
    mod_first = draw_mod_first(jax.random.fold_in(key_list[12], 71), 0)
    mod_second = draw_mod_second(jax.random.fold_in(key_list[12], 71), 0)
    out_grad = gaussian(key_list[11], (LATENTS, LENGTH, D), 1.0, 6.0, ((0, 8), (1, 4)))
    return {"hidden_in": hidden_in, "time_embed": time_embed, "caption_table": caption_table, "caption_ids": caption_ids, "owners": owners, "master": master, "first_moment": first_moment, "second_moment": second_moment, "mod_table": mod_table, "mod_first": mod_first, "mod_second": mod_second, "out_grad": out_grad}


@jax.custom_vjp
def low(v):
    return lax.optimization_barrier(v.astype(jnp.bfloat16)).astype(jnp.float32)

@jax.custom_vjp
def low_back(v):
    return v

def low_keep(v):
    return (low(v), None)

def low_pass(kept, grad):
    return (grad,)

def back_keep(v):
    return (v, None)

def back_low(kept, grad):
    return (low(grad),)
low.defvjp(low_keep, low_pass)
low_back.defvjp(back_keep, back_low)
HIGH = lax.Precision.HIGHEST
norm_eps = 1e-06
beta_one = 0.9
beta_two = 0.999
rate = 0.03
table_rate = 0.3
decay = 0.01
adam_eps = 1e-08

def slot_table(owners):
    index = jnp.arange(owners.shape[0])
    before = (owners[None, :] == owners[:, None]) & (index[None, :] < index[:, None])
    return owners * CAP + lax.optimization_barrier(jnp.sum(before.astype(jnp.int32), axis=1))

def layer_norm(values):
    center = values - lax.optimization_barrier(jnp.mean(values, axis=-1, keepdims=True))
    spread = lax.optimization_barrier(jnp.mean(center * center, axis=-1, keepdims=True))
    return center * lax.rsqrt(spread + norm_eps)

def attention(q_rows, k_rows, v_rows):
    q_heads = q_rows.reshape(q_rows.shape[0], HEADS, HEAD_DIM)
    k_heads = k_rows.reshape(k_rows.shape[0], HEADS, HEAD_DIM)
    v_heads = v_rows.reshape(v_rows.shape[0], HEADS, HEAD_DIM)
    scores = jnp.einsum('qhd,khd->hqk', q_heads, k_heads, precision=HIGH) * HEAD_DIM ** (-0.5)
    scores = low_back(scores)
    probs = low(jax.nn.softmax(scores, axis=-1))
    mixed = jnp.einsum('hqk,khd->qhd', probs, v_heads, precision=HIGH)
    return mixed.reshape(q_rows.shape[0], HEADS * HEAD_DIM)

def project(rows, weight):
    return jnp.dot(rows, weight.T, precision=HIGH)

def block_forward(hidden, table, weights, time_row, caption):
    w_query, w_key, w_value, w_out, c_query, c_key, c_value, c_out, w_up, w_down = weights
    modulate = table + time_row
    h_one = low(layer_norm(hidden) * (1.0 + modulate[1]) + modulate[0])
    q_rows = low(low_back(project(h_one, w_query)))
    k_rows = low(low_back(project(h_one, w_key)))
    v_rows = low(low_back(project(h_one, w_value)))
    attended = low(low_back(attention(q_rows, k_rows, v_rows)))
    branch_one = low_back(jnp.dot(attended, w_out, precision=HIGH))
    first_res = hidden + modulate[2] * branch_one
    first_low = low(first_res)
    cq_rows = low(low_back(project(first_low, c_query)))
    ck_rows = low(low_back(project(caption, c_key)))
    cv_rows = low(low_back(project(caption, c_value)))
    crossed = low(low_back(attention(cq_rows, ck_rows, cv_rows)))
    second_res = first_res + low_back(jnp.dot(crossed, c_out, precision=HIGH))
    h_two = low(layer_norm(second_res) * (1.0 + modulate[4]) + modulate[3])
    pre_act = low_back(project(h_two, w_up))
    act_low = low(jax.nn.gelu(pre_act, approximate=True))
    branch_two = low_back(jnp.dot(act_low, w_down, precision=HIGH))
    return second_res + modulate[5] * branch_two

def split_sections(stack):
    ranks = stack.shape[0]
    row_share = D // ranks
    hidden_share = FF // ranks
    pieces = []
    offset = 0
    for piece_rows in [row_share] * 8 + [hidden_share, hidden_share]:
        pieces.append(stack[:, offset:offset + piece_rows].reshape(ranks * piece_rows, D))
        offset = offset + piece_rows
    return pieces

def join_sections(pieces, ranks):
    parts = [piece.reshape(ranks, piece.shape[0] // ranks, D) for piece in pieces]
    return jnp.concatenate(parts, axis=1)

def adamw(weight, moment_one, moment_two, gradient, filled, step_rate):
    new_one = beta_one * moment_one + (1.0 - beta_one) * gradient
    new_two = beta_two * moment_two + (1.0 - beta_two) * gradient * gradient
    fixed_one = new_one / (1.0 - beta_one ** STEP)
    fixed_two = new_two / (1.0 - beta_two ** STEP)
    updated = weight - step_rate * (fixed_one / (jnp.sqrt(fixed_two) + adam_eps) + decay * weight)
    return (new_one * filled, new_two * filled, updated * filled)

def reference(hidden_in, time_embed, caption_table, caption_ids, owners, master, first_moment, second_moment, mod_table, mod_first, mod_second, out_grad):
    slot_of = slot_table(owners)
    rounded = lax.optimization_barrier(master.astype(jnp.bfloat16)).astype(jnp.float32)
    picked = rounded[slot_of].reshape(UNITS, N_TENSOR, BLOCK_ROWS, D)
    stack = jnp.transpose(picked, (1, 0, 2, 3)).reshape(N_TENSOR, UNITS * BLOCK_ROWS, D)
    weights = tuple(split_sections(stack))
    captions = caption_table.astype(jnp.float32)[caption_ids]
    inputs = hidden_in.astype(jnp.float32)
    cotangent = out_grad.astype(jnp.float32)

    def per_latent(totals, item):
        latent, time_row, caption, upstream = item

        def forward(latent_in, table, weight_set):
            return block_forward(latent_in, table, weight_set, time_row, caption)
        result, pullback = jax.vjp(forward, latent, mod_table, weights)
        grad_in, grad_table, grad_weights = pullback(upstream)
        totals = jax.tree.map(jnp.add, totals, (grad_table, grad_weights))
        return (totals, (result, grad_in))
    start = (jnp.zeros_like(mod_table), tuple((jnp.zeros_like(piece) for piece in weights)))
    totals, (block_out, input_grad) = lax.scan(per_latent, start, (inputs, time_embed, captions, cotangent))
    grad_stack = join_sections(list(totals[1]), N_TENSOR)
    grad_units = jnp.transpose(grad_stack.reshape(N_TENSOR, UNITS, BLOCK_ROWS, D), (1, 0, 2, 3)).reshape(UNITS, N_TENSOR * BLOCK_ROWS, D)
    grad_slots = jnp.zeros_like(master).at[slot_of].set(grad_units)
    filled = jnp.zeros((SLOTS,), jnp.float32).at[slot_of].set(1.0)[:, None, None]
    new_first, new_second, new_master = adamw(master, first_moment, second_moment, grad_slots, filled, rate)
    mod_new_first, mod_new_second, mod_new = adamw(mod_table, mod_first, mod_second, totals[0], 1.0, table_rate)
    return (block_out, input_grad, new_first, new_second, new_master, mod_new_first, mod_new_second, mod_new)
```

```python
from functools import partial

import jax
import jax.numpy as jnp
from jax import lax
from jax.sharding import PartitionSpec as P

HEAD_DIM = 72
STEP = 10


norm_eps = 1e-06
beta_one = 0.9
beta_two = 0.999
rate = 0.03
table_rate = 0.3
decay = 0.01
adam_eps = 1e-08
gelu_tanh = partial(jax.nn.gelu, approximate=True)
low = jnp.bfloat16


def ranks_of(owners):
    index = jnp.arange(owners.shape[0])
    before = (owners[None, :] == owners[:, None]) & (index[None, :] < index[:, None])
    return jnp.sum(before.astype(jnp.int32), axis=1)


def layer_norm(values):
    center = values - jnp.mean(values, axis=-1, keepdims=True)
    inverse = lax.rsqrt(jnp.mean(center * center, axis=-1, keepdims=True) + norm_eps)
    return (center * inverse, inverse)


def norm_back(grad_rows, normed, inverse, scale_row):
    scaled = grad_rows * (1.0 + scale_row)
    mean_one = jnp.mean(scaled, axis=-1, keepdims=True)
    mean_two = jnp.mean(scaled * normed, axis=-1, keepdims=True)
    return inverse * (scaled - mean_one - normed * mean_two)


def project(rows, weight):
    return jnp.einsum("ld,rd->lr", rows, weight, preferred_element_type=jnp.float32)


def expand(rows, weight):
    return jnp.einsum("lr,rd->ld", rows, weight, preferred_element_type=jnp.float32)


def outer(left, right):
    return jnp.einsum("lr,ld->rd", left, right, preferred_element_type=jnp.float32)


def shift(values, step):
    count = lax.axis_size("tensor")
    return lax.ppermute(values, "tensor", [(i, (i + step) % count) for i in range(count)])


def ring(values):
    return [values] + [shift(values, k) for k in range(1, lax.axis_size("tensor"))]


def scatter_ring(parts):
    count = lax.axis_size("tensor")
    total = parts[0]
    for k in range(1, count):
        total = total + shift(parts[k].astype(low), count - k).astype(jnp.float32)
    return total


def to_ring(stacked):
    count = stacked.shape[0]
    twice = jnp.concatenate([stacked, stacked], axis=0)
    return lax.dynamic_slice_in_dim(twice, lax.axis_index("tensor"), count, 0)


def from_ring(stacked, sign):
    count = stacked.shape[0]
    me = lax.axis_index("tensor")
    place = lax.rem(sign * (jnp.arange(count) - me) + 2 * count, count)
    return jnp.take(stacked, place, axis=0, mode="clip")


def heads_of(rows):
    return rows.reshape(rows.shape[0], -1, HEAD_DIM)


def attend(q_rows, k_rows, v_rows):
    length, width_all = q_rows.shape
    heads = width_all // HEAD_DIM
    block_rows = min(512, length)
    blocks = length // block_rows
    scale = HEAD_DIM ** (-0.5)
    k_heads = heads_of(k_rows)
    v_heads = heads_of(v_rows)

    def one_block(q_block):
        scores = (
            jnp.einsum("qhd,khd->hqk", q_block, k_heads, preferred_element_type=jnp.float32)
            * scale
        )
        top = jnp.max(scores, axis=-1, keepdims=True)
        expo = jnp.exp(scores - top)
        total = jnp.sum(expo, axis=-1, keepdims=True)
        probs = (expo / total).astype(low)
        mixed = jnp.einsum("hqk,khd->qhd", probs, v_heads, preferred_element_type=jnp.float32)
        return (mixed.astype(low), (top + jnp.log(total))[..., 0])

    mixed, logsum = lax.map(one_block, q_rows.reshape(blocks, block_rows, heads, HEAD_DIM))
    return (mixed.reshape(length, width_all), logsum)


def attend_back(q_rows, k_rows, v_rows, grad_mixed, logsum):
    length, width_all = q_rows.shape
    heads = width_all // HEAD_DIM
    block_rows = min(512, length)
    blocks = length // block_rows
    scale = HEAD_DIM ** (-0.5)
    k_heads = heads_of(k_rows)
    v_heads = heads_of(v_rows)

    def one_block(carry, block_item):
        q_block, g_block, l_block = block_item
        scores = (
            jnp.einsum("qhd,khd->hqk", q_block, k_heads, preferred_element_type=jnp.float32)
            * scale
        )
        probs = jnp.exp(scores - l_block[..., None])
        grad_probs = jnp.einsum(
            "qhd,khd->hqk", g_block, v_heads, preferred_element_type=jnp.float32
        )
        inner = jnp.sum(probs * grad_probs, axis=-1, keepdims=True)
        grad_scores = (probs * (grad_probs - inner)).astype(low)
        grad_q = (
            jnp.einsum("hqk,khd->qhd", grad_scores, k_heads, preferred_element_type=jnp.float32)
            * scale
        )
        grad_k = (
            carry[0]
            + jnp.einsum("hqk,qhd->khd", grad_scores, q_block, preferred_element_type=jnp.float32)
            * scale
        )
        grad_v = carry[1] + jnp.einsum(
            "hqk,qhd->khd", probs.astype(low), g_block, preferred_element_type=jnp.float32
        )
        return ((grad_k, grad_v), grad_q)

    start = (jnp.zeros(k_heads.shape, jnp.float32), jnp.zeros(v_heads.shape, jnp.float32))
    (grad_k, grad_v), grad_q = lax.scan(
        one_block,
        start,
        (
            q_rows.reshape(blocks, block_rows, heads, HEAD_DIM),
            grad_mixed.reshape(blocks, block_rows, heads, HEAD_DIM),
            logsum,
        ),
    )
    return (
        grad_q.reshape(length, width_all),
        grad_k.reshape(-1, width_all),
        grad_v.reshape(-1, width_all),
    )


def adamw(weight, moment_one, moment_two, gradient, filled, step_rate):
    new_one = beta_one * moment_one + (1.0 - beta_one) * gradient
    new_two = beta_two * moment_two + (1.0 - beta_two) * gradient * gradient
    fixed_one = new_one / (1.0 - beta_one**STEP)
    fixed_two = new_two / (1.0 - beta_two**STEP)
    updated = weight - step_rate * (fixed_one / (jnp.sqrt(fixed_two) + adam_eps) + decay * weight)
    return (new_one * filled, new_two * filled, updated * filled)


def on_device(
    hidden_in,
    time_embed,
    caption_table,
    caption_ids,
    owners,
    master,
    first_moment,
    second_moment,
    mod_table,
    mod_first,
    mod_second,
    out_grad,
):
    count = lax.axis_size("tensor")
    dp_count = lax.axis_size("dp")
    me_dp = lax.axis_index("dp")
    capacity, unit_rows, width = master.shape
    units = owners.shape[0]
    tokens = hidden_in.shape[1]
    text_count = caption_ids.shape[1]
    share = width // count
    per = share // unit_rows
    ups = (units - 8 * per) // 2
    rank_of = ranks_of(owners)
    mine = owners == me_dp

    square = [list(range(i * per, (i + 1) * per)) for i in range(8)]
    group_attn = square[0] + square[1] + square[2] + square[5] + square[6]
    group_full = square[3] + square[4] + square[7]
    group_up = list(range(8 * per, 8 * per + ups))
    group_down = list(range(8 * per + ups, units))
    full_rows = len(group_full) * unit_rows
    padded = -(-full_rows // dp_count) * dp_count

    slots_low = master.astype(low)

    def picked(group):
        where = jnp.array(group)
        rows = jnp.take(slots_low, rank_of[where], axis=0, mode="clip")
        return jnp.where(mine[where][:, None, None], rows, jnp.zeros((), low))

    def own_weights(group):
        return lax.psum(picked(group), "dp").reshape(-1, width)

    latent_in = hidden_in[0].astype(jnp.float32)
    upstream = out_grad[0].astype(jnp.float32)
    modulate = mod_table + time_embed[0]

    def mod_row(which_row):
        return modulate[which_row][None, :]

    normed_one, inverse_one = layer_norm(latent_in)
    h_one = (normed_one * (1.0 + mod_row(1)) + mod_row(0)).astype(low)
    h_one_all = jnp.concatenate(ring(h_one), axis=0)

    w_attn = own_weights(group_attn)
    w_qkv = w_attn[: 3 * share]
    w_ckv = w_attn[3 * share :]
    full_part = picked(group_full).reshape(full_rows, width)
    full_part = jnp.pad(full_part, ((0, padded - full_rows), (0, 0)))
    full_part = full_part.reshape(dp_count, padded // dp_count, width)
    full_part = lax.psum_scatter(full_part, "dp", scatter_dimension=0, tiled=True)
    w_full = lax.all_gather(full_part, ("tensor", "dp"), axis=0, tiled=True)
    w_full = w_full.reshape(count, padded, width)
    w_out = w_full[:, :share].reshape(width, width)
    c_query = w_full[:, share : 2 * share].reshape(width, width)
    c_out = w_full[:, 2 * share : 3 * share].reshape(width, width)
    w_up = own_weights(group_up)
    w_down = own_weights(group_down)

    all_ids = lax.all_gather(caption_ids, "dp", axis=0, tiled=True)
    vocab_rows = caption_table.shape[0]
    chosen = all_ids - me_dp * vocab_rows
    onehot = (chosen.reshape(-1)[:, None] == jnp.arange(vocab_rows)[None, :]).astype(low)
    text_part = jnp.dot(onehot, caption_table, preferred_element_type=jnp.float32).astype(low)
    text_part = lax.psum_scatter(
        text_part.reshape(dp_count, text_count, -1), "dp", scatter_dimension=0, tiled=True
    )
    text_ring = jnp.stack(ring(text_part[0]))
    text_low = from_ring(text_ring, -1).transpose(1, 0, 2).reshape(text_count, width)

    qkv = project(h_one_all, w_qkv).astype(low)
    q_rows, k_rows, v_rows = qkv[:, :share], qkv[:, share : 2 * share], qkv[:, 2 * share :]
    attended, logsum_one = attend(q_rows, k_rows, v_rows)
    mixed_parts = attended.reshape(count, tokens, share)
    mixed_ring = jnp.stack(
        [mixed_parts[0]] + [shift(mixed_parts[k], count - k) for k in range(1, count)]
    )
    mixed_own = from_ring(mixed_ring, 1).transpose(1, 0, 2).reshape(tokens, width)
    branch_one = expand(mixed_own, w_out)
    first_res = latent_in + mod_row(2) * branch_one
    first_low = first_res.astype(low)

    ckv = project(text_low, w_ckv).astype(low)
    ckv_ring = from_ring(jnp.stack(ring(ckv)), -1)
    ck_rows = ckv_ring[:, :, :share].transpose(1, 0, 2).reshape(text_count, width)
    cv_rows = ckv_ring[:, :, share:].transpose(1, 0, 2).reshape(text_count, width)
    cq_rows = project(first_low, c_query).astype(low)
    crossed, logsum_two = attend(cq_rows, ck_rows, cv_rows)
    second_res = first_res + expand(crossed, c_out)
    normed_two, inverse_two = layer_norm(second_res)
    h_two = (normed_two * (1.0 + mod_row(4)) + mod_row(3)).astype(low)

    grad_mlp = (mod_row(5) * upstream).astype(low)
    grad_mlp_all = jnp.concatenate(ring(grad_mlp), axis=0)
    h_two_all = jnp.concatenate(ring(h_two), axis=0)
    pre_act = project(h_two_all, w_up)
    act_low = gelu_tanh(pre_act).astype(low)
    grad_down = outer(act_low, grad_mlp_all).astype(low)
    ignored, gelu_pull = jax.vjp(gelu_tanh, pre_act)
    grad_act = project(grad_mlp_all, w_down)
    grad_pre = gelu_pull(grad_act)[0].astype(low)
    grad_up = outer(grad_pre, h_two_all).astype(low)
    grad_h_two = scatter_ring(list(expand(grad_pre, w_up).reshape(count, tokens, width)))
    branch_two = scatter_ring(list(expand(act_low, w_down).reshape(count, tokens, width)))
    block_out = second_res + mod_row(5) * branch_two

    def owner_sum(values):
        return lax.psum(values.reshape(-1, unit_rows, width), "dp")

    sum_down = owner_sum(grad_down)
    sum_up = owner_sum(grad_up)
    second_grad = upstream + norm_back(grad_h_two, normed_two, inverse_two, mod_row(4))

    cross_grad = second_grad.astype(low)
    grad_c_out = outer(crossed, cross_grad)
    grad_crossed = project(cross_grad, c_out).astype(low)
    grad_cq, grad_ck, grad_cv = attend_back(cq_rows, ck_rows, cv_rows, grad_crossed, logsum_two)
    grad_cq = grad_cq.astype(low)
    grad_ckv = jnp.stack(
        [grad_ck.reshape(text_count, count, share), grad_cv.reshape(text_count, count, share)]
    ).transpose(2, 1, 0, 3)
    grad_ckv = to_ring(grad_ckv)
    grad_ckv_own = grad_ckv[0]
    for k in range(1, count):
        grad_ckv_own = grad_ckv_own + shift(grad_ckv[k].astype(low), k).astype(jnp.float32)
    grad_ckv_own = grad_ckv_own.astype(low).reshape(text_count, 2 * share)
    grad_c_query = outer(grad_cq, first_low)
    first_grad = second_grad + expand(grad_cq, c_query)

    attn_grad = (mod_row(2) * first_grad).astype(low)
    grad_w_out = outer(mixed_own, attn_grad)
    grad_mixed = project(attn_grad, w_out).astype(low)
    grad_mixed = to_ring(grad_mixed.reshape(tokens, count, share).transpose(1, 0, 2))
    grad_attended = jnp.concatenate(
        [grad_mixed[0]] + [shift(grad_mixed[k], k) for k in range(1, count)], axis=0
    )
    full_grad = jnp.concatenate(
        [g.astype(low).reshape(count, share, width) for g in (grad_w_out, grad_c_query, grad_c_out)],
        axis=1,
    )
    full_grad = jnp.pad(full_grad, ((0, 0), (0, padded - full_rows), (0, 0)))
    full_grad = full_grad.reshape(count * dp_count, padded // dp_count, width)
    full_grad = lax.psum_scatter(full_grad, ("tensor", "dp"), scatter_dimension=0, tiled=True)
    sum_full = lax.all_gather(full_grad, "dp", axis=0, tiled=True)
    sum_full = sum_full.reshape(padded, width)[:full_rows].reshape(-1, unit_rows, width)

    grads_qkv = attend_back(q_rows, k_rows, v_rows, grad_attended, logsum_one)
    grad_qkv = jnp.concatenate([g.astype(low) for g in grads_qkv], axis=1)
    grad_h_one = scatter_ring(list(expand(grad_qkv, w_qkv).reshape(count, tokens, width)))
    grad_attn = jnp.concatenate(
        [outer(grad_qkv, h_one_all), outer(grad_ckv_own, text_low)], axis=0
    ).astype(low)
    sum_attn = owner_sum(grad_attn)
    input_grad = first_grad + norm_back(grad_h_one, normed_one, inverse_one, mod_row(1))

    def summed(values):
        return jnp.sum(values, axis=0)

    mod_terms = jnp.stack(
        [
            summed(grad_h_one),
            summed(grad_h_one * normed_one),
            summed(branch_one * first_grad),
            summed(grad_h_two),
            summed(grad_h_two * normed_two),
            summed(branch_two * upstream),
        ]
    )
    mod_grad = lax.psum(mod_terms, ("dp", "tensor"))

    order = group_attn + group_full + group_up + group_down
    place = [0] * units
    for position, unit in enumerate(order):
        place[unit] = position
    sums = jnp.concatenate([sum_attn, sum_full, sum_up, sum_down], axis=0)
    match = (rank_of[None, :] == jnp.arange(capacity)[:, None]) & mine[None, :]
    place_of_slot = jnp.sum(jnp.where(match, jnp.array(place)[None, :], 0), axis=1)
    filled = jnp.any(match, axis=1)[:, None, None]
    owned = jnp.take(sums, place_of_slot, axis=0, mode="clip").astype(jnp.float32)
    new_first, new_second, new_master = adamw(
        master, first_moment, second_moment, owned, filled.astype(jnp.float32), rate
    )
    mod_new_first, mod_new_second, mod_new = adamw(
        mod_table, mod_first, mod_second, mod_grad, 1.0, table_rate
    )
    return (
        block_out[None],
        input_grad[None],
        new_first,
        new_second,
        new_master,
        mod_new_first,
        mod_new_second,
        mod_new,
    )


def solution(mesh):
    in_specs = (
        P("dp", "tensor", None),
        P("dp", None, None),
        P("dp", "tensor"),
        P("dp", None),
        P(),
        P("dp", "tensor", None),
        P("dp", "tensor", None),
        P("dp", "tensor", None),
        P(),
        P(),
        P(),
        P("dp", "tensor", None),
    )
    out_specs = (
        P("dp", "tensor", None),
        P("dp", "tensor", None),
        P("dp", "tensor", None),
        P("dp", "tensor", None),
        P("dp", "tensor", None),
        P(),
        P(),
        P(),
    )
    return jax.shard_map(
        on_device, mesh=mesh, in_specs=in_specs, out_specs=out_specs, check_vma=False
    )
```

```python
from functools import partial
import math

import jax
import jax.numpy as jnp
import numpy as np
from jax import lax
from jax.experimental import pallas as pl
from jax.experimental.pallas import tpu as pltpu
from jax.sharding import PartitionSpec as P

HEAD_DIM = 72
STEP = 10


norm_eps = 1e-06
beta_one = 0.9
beta_two = 0.999
rate = 0.03
table_rate = 0.3
decay = 0.01
adam_eps = 1e-08
gelu_tanh = partial(jax.nn.gelu, approximate=True)
low = jnp.bfloat16


def ranks_of(owners):
    index = jnp.arange(owners.shape[0])
    before = (owners[None, :] == owners[:, None]) & (index[None, :] < index[:, None])
    return jnp.sum(before.astype(jnp.int32), axis=1)


def layer_norm(values):
    center = values - jnp.mean(values, axis=-1, keepdims=True)
    inverse = lax.rsqrt(jnp.mean(center * center, axis=-1, keepdims=True) + norm_eps)
    return (center * inverse, inverse)


def norm_back(grad_rows, normed, inverse, scale_row):
    scaled = grad_rows * (1.0 + scale_row)
    mean_one = jnp.mean(scaled, axis=-1, keepdims=True)
    mean_two = jnp.mean(scaled * normed, axis=-1, keepdims=True)
    return inverse * (scaled - mean_one - normed * mean_two)


def project(rows, weight):
    return jnp.einsum("ld,rd->lr", rows, weight, preferred_element_type=jnp.float32)


def expand(rows, weight):
    return jnp.einsum("lr,rd->ld", rows, weight, preferred_element_type=jnp.float32)


def outer(left, right):
    return jnp.einsum("lr,ld->rd", left, right, preferred_element_type=jnp.float32)


def shift(values, step):
    count = lax.axis_size("tensor")
    return lax.ppermute(values, "tensor", [(i, (i + step) % count) for i in range(count)])


def ring(values):
    return [values] + [shift(values, k) for k in range(1, lax.axis_size("tensor"))]


def scatter_ring(parts):
    count = lax.axis_size("tensor")
    total = parts[0]
    for k in range(1, count):
        total = total + shift(parts[k].astype(low), count - k).astype(jnp.float32)
    return total


def to_ring(stacked):
    count = stacked.shape[0]
    twice = jnp.concatenate([stacked, stacked], axis=0)
    return lax.dynamic_slice_in_dim(twice, lax.axis_index("tensor"), count, 0)


def from_ring(stacked, sign):
    count = stacked.shape[0]
    me = lax.axis_index("tensor")
    place = lax.rem(sign * (jnp.arange(count) - me) + 2 * count, count)
    return jnp.take(stacked, place, axis=0, mode="clip")


def heads_of(rows):
    return rows.reshape(rows.shape[0], -1, HEAD_DIM)


def attend(q_rows, k_rows, v_rows):
    length, width_all = q_rows.shape
    heads = width_all // HEAD_DIM
    block_rows = min(512, length)
    blocks = length // block_rows
    scale = HEAD_DIM ** (-0.5)
    k_heads = heads_of(k_rows)
    v_heads = heads_of(v_rows)

    def one_block(q_block):
        scores = (
            jnp.einsum("qhd,khd->hqk", q_block, k_heads, preferred_element_type=jnp.float32)
            * scale
        )
        top = jnp.max(scores, axis=-1, keepdims=True)
        expo = jnp.exp(scores - top)
        total = jnp.sum(expo, axis=-1, keepdims=True)
        probs = (expo / total).astype(low)
        mixed = jnp.einsum("hqk,khd->qhd", probs, v_heads, preferred_element_type=jnp.float32)
        return (mixed.astype(low), (top + jnp.log(total))[..., 0])

    mixed, logsum = lax.map(one_block, q_rows.reshape(blocks, block_rows, heads, HEAD_DIM))
    return (mixed.reshape(length, width_all), logsum)


def attend_back(q_rows, k_rows, v_rows, grad_mixed, logsum):
    length, width_all = q_rows.shape
    heads = width_all // HEAD_DIM
    block_rows = min(512, length)
    blocks = length // block_rows
    scale = HEAD_DIM ** (-0.5)
    k_heads = heads_of(k_rows)
    v_heads = heads_of(v_rows)

    def one_block(carry, block_item):
        q_block, g_block, l_block = block_item
        scores = (
            jnp.einsum("qhd,khd->hqk", q_block, k_heads, preferred_element_type=jnp.float32)
            * scale
        )
        probs = jnp.exp(scores - l_block[..., None])
        grad_probs = jnp.einsum(
            "qhd,khd->hqk", g_block, v_heads, preferred_element_type=jnp.float32
        )
        inner = jnp.sum(probs * grad_probs, axis=-1, keepdims=True)
        grad_scores = (probs * (grad_probs - inner)).astype(low)
        grad_q = (
            jnp.einsum("hqk,khd->qhd", grad_scores, k_heads, preferred_element_type=jnp.float32)
            * scale
        )
        grad_k = (
            carry[0]
            + jnp.einsum("hqk,qhd->khd", grad_scores, q_block, preferred_element_type=jnp.float32)
            * scale
        )
        grad_v = carry[1] + jnp.einsum(
            "hqk,qhd->khd", probs.astype(low), g_block, preferred_element_type=jnp.float32
        )
        return ((grad_k, grad_v), grad_q)

    start = (jnp.zeros(k_heads.shape, jnp.float32), jnp.zeros(v_heads.shape, jnp.float32))
    (grad_k, grad_v), grad_q = lax.scan(
        one_block,
        start,
        (
            q_rows.reshape(blocks, block_rows, heads, HEAD_DIM),
            grad_mixed.reshape(blocks, block_rows, heads, HEAD_DIM),
            logsum,
        ),
    )
    return (
        grad_q.reshape(length, width_all),
        grad_k.reshape(-1, width_all),
        grad_v.reshape(-1, width_all),
    )


def adamw(weight, moment_one, moment_two, gradient, filled, step_rate):
    new_one = beta_one * moment_one + (1.0 - beta_one) * gradient
    new_two = beta_two * moment_two + (1.0 - beta_two) * gradient * gradient
    fixed_one = new_one / (1.0 - beta_one**STEP)
    fixed_two = new_two / (1.0 - beta_two**STEP)
    updated = weight - step_rate * (fixed_one / (jnp.sqrt(fixed_two) + adam_eps) + decay * weight)
    return (new_one * filled, new_two * filled, updated * filled)


def swap(values, axis, bit):
    count = lax.axis_size(axis)
    return lax.ppermute(values, axis, [(i, i ^ (1 << bit)) for i in range(count)])


def choose(values, index, axis):
    return lax.dynamic_index_in_dim(values, index, axis, keepdims=False)


def halve(values, axis, bit, dim):
    own_bit = (lax.axis_index(axis) >> bit) & 1
    sent = swap(choose(values, 1 - own_bit, dim), axis, bit)
    return choose(values, own_bit, dim) + sent


def total_sum(values):
    for axis in ("dp", "tensor"):
        for bit in range(lax.axis_size(axis).bit_length() - 1):
            values = values + swap(values, axis, bit)
    return values


def pick_units(master, slot_unit, mine, kind, place, sizes):
    capacity, unit_rows, width = master.shape
    units = mine.shape[0]
    group = math.gcd(capacity, 4)
    steps = capacity // group

    def body(slot_ref, mine_ref, kind_ref, place_ref, block, *rest):
        outs, (lows, zeros, sems) = rest[: len(sizes)], rest[len(sizes) :]
        step = pl.program_id(0)

        def start(source, unit):
            for which, out in enumerate(outs):

                @pl.when(kind_ref[unit] == which)
                def _():
                    pltpu.make_async_copy(source, out.at[place_ref[unit]], sems.at[unit]).start()

        @pl.when(step == 0)
        def _():
            zeros[...] = jnp.zeros_like(zeros)

            @pl.loop(0, units)
            def _(unit):
                @pl.when(mine_ref[unit] == 0)
                def _():
                    start(zeros, unit)

        for i in range(group):
            slot = step * group + i
            unit = slot_ref[slot]

            @pl.when(unit >= 0)
            def _():
                lows[slot] = block[i].astype(low)
                start(lows.at[slot], unit)

        @pl.when(step == steps - 1)
        def _():
            @pl.loop(0, units)
            def _(unit):
                pltpu.make_async_copy(zeros, outs[0].at[0], sems.at[unit]).wait()

    return pl.pallas_call(
        body,
        grid_spec=pltpu.PrefetchScalarGridSpec(
            num_scalar_prefetch=4,
            grid=(steps,),
            in_specs=[pl.BlockSpec((group, unit_rows, width), lambda s, *_: (s, 0, 0))],
            out_specs=[pl.BlockSpec(memory_space=pl.ANY)] * len(sizes),
            scratch_shapes=[
                pltpu.VMEM((capacity, unit_rows, width), low),
                pltpu.VMEM((unit_rows, width), low),
                pltpu.SemaphoreType.DMA((units,)),
            ],
        ),
        out_shape=[jax.ShapeDtypeStruct((size, unit_rows, width), low) for size in sizes],
        compiler_params=pltpu.CompilerParams(vmem_limit_bytes=32 * 2**20),
        name="pick_units",
    )(slot_unit, mine, kind, place, master)


def place_blocks(sources, which, position):
    amount = which.shape[0]
    shape = sources[0].shape[1:]

    def body(which_ref, position_ref, *rest):
        ins, (out, sems) = rest[: len(sources)], rest[len(sources) :]

        @pl.loop(0, amount)
        def _(i):
            for source, ref in enumerate(ins):

                @pl.when(which_ref[i] == source)
                def _():
                    pltpu.make_async_copy(ref.at[position_ref[i]], out.at[i], sems.at[i]).start()

        @pl.loop(0, amount)
        def _(i):
            pltpu.make_async_copy(ins[0].at[0], out.at[0], sems.at[i]).wait()

    return pl.pallas_call(
        body,
        grid_spec=pltpu.PrefetchScalarGridSpec(
            num_scalar_prefetch=2,
            grid=(1,),
            in_specs=[pl.BlockSpec(memory_space=pl.ANY)] * len(sources),
            out_specs=pl.BlockSpec(memory_space=pl.ANY),
            scratch_shapes=[pltpu.SemaphoreType.DMA((amount,))],
        ),
        out_shape=jax.ShapeDtypeStruct((amount,) + shape, low),
        name="place_blocks",
    )(which, position, *sources)


def gather_plane(first, second):
    first_all = jnp.concatenate([first, swap(first, "dp", 1)])
    second_all = jnp.concatenate([second, swap(second, "dp", 2)])
    first_far = swap(first_all, "dp", 2)
    second_far = swap(second_all, "dp", 1)
    pool = jnp.concatenate([first_all, first_far, second_all, second_far])
    return (pool, swap(pool, "dp", 0))


def in_pool(member, inner, inner_count):
    me = lax.axis_index("dp")
    half, core = member >> 3, ((member >> 2) & 1) ^ (me & 1)
    far_y, far_x = ((member >> 1) & 1) ^ ((me >> 2) & 1), (member & 1) ^ ((me >> 1) & 1)
    where_first = (far_y * 2 + far_x) * inner_count
    where_second = (4 + far_x * 2 + far_y) * inner_count
    return (core, jnp.where(half == 0, where_first, where_second) + inner)


def on_device(
    hidden_in,
    time_embed,
    caption_table,
    caption_ids,
    owners,
    master,
    first_moment,
    second_moment,
    mod_table,
    mod_first,
    mod_second,
    out_grad,
):
    count = lax.axis_size("tensor")
    dp_count = lax.axis_size("dp")
    me_dp = lax.axis_index("dp")
    me_tensor = lax.axis_index("tensor")
    capacity, unit_rows, width = master.shape
    units = owners.shape[0]
    tokens = hidden_in.shape[1]
    text_count = caption_ids.shape[1]
    share = width // count
    per = share // unit_rows
    ups = (units - 8 * per) // 2
    rank_of = ranks_of(owners)
    mine = owners == me_dp
    match = (rank_of[None, :] == jnp.arange(capacity)[:, None]) & mine[None, :]
    filled = jnp.any(match, axis=1)
    unit_of_slot = jnp.sum(jnp.where(match, jnp.arange(units)[None, :], 0), axis=1)

    square = [list(range(i * per, (i + 1) * per)) for i in range(8)]
    group_attn = square[0] + square[1] + square[2] + square[5]
    group_full = square[3] + square[4] + square[6] + square[7]
    group_mlp = list(range(8 * per, units))
    members = len(group_attn)
    plane = dp_count == 8 and members == 16 and len(group_mlp) % dp_count == 0
    member_of = np.zeros(units, np.int32)
    member_of[group_attn] = np.arange(members)
    member_of[group_full] = np.arange(members)
    is_attn = np.zeros(units, bool)
    is_attn[group_attn] = True
    is_mlp = np.zeros(units, bool)
    is_mlp[group_mlp] = True

    latent_in = hidden_in[0].astype(jnp.float32)
    upstream = out_grad[0].astype(jnp.float32)
    modulate = mod_table + time_embed[0]

    def mod_row(which_row):
        return modulate[which_row][None, :]

    normed_one, inverse_one = layer_norm(latent_in)
    normed_all = jnp.concatenate(ring(normed_one.astype(low)), axis=0)
    h_one_all = (normed_all.astype(jnp.float32) * (1.0 + mod_row(1)) + mod_row(0)).astype(low)

    if plane:
        core, far_x, far_y = (
            ((member_of >> 2) & 1) ^ (me_dp & 1),
            (member_of & 1) ^ ((me_dp >> 1) & 1),
            ((member_of >> 1) & 1) ^ ((me_dp >> 2) & 1),
        )
        place = jnp.where(is_attn, far_x * 4 + far_y * 2, 8 + far_y * 4 + far_x * 2)
        place = jnp.where(is_mlp, np.arange(units) - 8 * per, place + (member_of >> 3))
        kind = jnp.where(is_mlp, 2, core)
        kept, given, mlp_part = pick_units(
            master,
            jnp.where(filled, unit_of_slot, -1),
            mine.astype(jnp.int32),
            kind,
            place,
            (members, members, len(group_mlp)),
        )
        half = kept + swap(given, "dp", 0)
        attn_two = half[0:4] + swap(half[4:8], "dp", 1)
        full_two = half[8:12] + swap(half[12:16], "dp", 2)
        attn_one = attn_two[0:2] + swap(attn_two[2:4], "dp", 2)
        full_one = full_two[0:2] + swap(full_two[2:4], "dp", 1)
        mlp_part = lax.psum_scatter(mlp_part, "dp", scatter_dimension=0, tiled=True)
        w_mlp = lax.all_gather(mlp_part, "dp", axis=0, tiled=True)
        pools = gather_plane(attn_one[0:1], attn_one[1:2])
        w_attn = place_blocks(pools, *in_pool(np.arange(members), 0, 1))
        full_ring = ring(full_one)
        pools = gather_plane(
            jnp.concatenate([item[0:1] for item in full_ring]),
            jnp.concatenate([item[1:2] for item in full_ring]),
        )
        listing = np.arange(count * members)
        matrix, rank, head = listing // (count * per), listing // per % count, listing % per
        slot = lax.rem(me_tensor - rank + count, count)
        w_full = place_blocks(pools, *in_pool(matrix * per + head, slot, count))
        w_full = w_full.reshape(4, width, width)
    else:
        slots_low = master.astype(low)
        rows = jnp.take(slots_low, rank_of, axis=0, mode="clip")
        rows = lax.psum(jnp.where(mine[:, None, None], rows, jnp.zeros((), low)), "dp")
        w_attn = rows[np.array(group_attn)]
        w_full = lax.all_gather(rows[np.array(group_full)], "tensor", axis=0)
        w_full = w_full.reshape(count, 4, share, width).swapaxes(0, 1).reshape(4, width, width)
        w_mlp = rows[8 * per :]
    w_attn = w_attn.reshape(-1, width)
    w_qkv, c_key = w_attn[: 3 * share], w_attn[3 * share :]
    w_out, c_query, c_value, c_out = w_full
    w_up = w_mlp[:ups].reshape(-1, width)
    w_down = w_mlp[ups:].reshape(-1, width)

    bits = dp_count.bit_length() - 1
    all_ids = caption_ids
    for bit in range(bits):
        all_ids = jnp.concatenate([all_ids, swap(all_ids, "dp", bit)])
    vocab_rows = caption_table.shape[0]
    chosen = all_ids.reshape(-1) - me_dp * vocab_rows
    onehot = (chosen[:, None] == jnp.arange(vocab_rows)[None, :]).astype(low)
    text_part = jnp.dot(onehot, caption_table, preferred_element_type=jnp.float32).astype(low)
    text_part = text_part.reshape(dp_count, text_count, -1)
    for bit in reversed(range(bits)):
        text_part = text_part[: 1 << bit] + swap(text_part[1 << bit :], "dp", bit)
    text_ring = jnp.stack(ring(text_part[0]))
    text_low = from_ring(text_ring, -1).transpose(1, 0, 2).reshape(text_count, width)

    qkv = project(h_one_all, w_qkv).astype(low)
    q_rows, k_rows, v_rows = qkv[:, :share], qkv[:, share : 2 * share], qkv[:, 2 * share :]
    attended, logsum_one = attend(q_rows, k_rows, v_rows)
    mixed_parts = attended.reshape(count, tokens, share)
    mixed_ring = jnp.stack(
        [mixed_parts[0]] + [shift(mixed_parts[k], count - k) for k in range(1, count)]
    )
    mixed_own = from_ring(mixed_ring, 1).transpose(1, 0, 2).reshape(tokens, width)
    branch_one = expand(mixed_own, w_out)
    first_res = latent_in + mod_row(2) * branch_one
    first_low = first_res.astype(low)

    ck_ring = from_ring(jnp.stack(ring(project(text_low, c_key).astype(low))), -1)
    ck_rows = ck_ring.transpose(1, 0, 2).reshape(text_count, width)
    cv_rows = project(text_low, c_value).astype(low)
    cq_rows = project(first_low, c_query).astype(low)
    crossed, logsum_two = attend(cq_rows, ck_rows, cv_rows)
    second_res = first_res + expand(crossed, c_out)
    normed_two, inverse_two = layer_norm(second_res)
    h_two = (normed_two * (1.0 + mod_row(4)) + mod_row(3)).astype(low)

    grad_mlp = (mod_row(5) * upstream).astype(low)
    grad_mlp_all = jnp.concatenate(ring(grad_mlp), axis=0)
    h_two_all = jnp.concatenate(ring(h_two), axis=0)
    pre_act = project(h_two_all, w_up)
    act_low = gelu_tanh(pre_act).astype(low)
    grad_down = outer(act_low, grad_mlp_all).astype(low)
    ignored, gelu_pull = jax.vjp(gelu_tanh, pre_act)
    grad_act = project(grad_mlp_all, w_down)
    grad_pre = gelu_pull(grad_act)[0].astype(low)
    grad_up = outer(grad_pre, h_two_all).astype(low)
    grad_h_two = scatter_ring(list(expand(grad_pre, w_up).reshape(count, tokens, width)))
    branch_two = scatter_ring(list(expand(act_low, w_down).reshape(count, tokens, width)))
    block_out = second_res + mod_row(5) * branch_two
    mlp_grad = jnp.concatenate([grad_up, grad_down]).reshape(-1, unit_rows, width)
    second_grad = upstream + norm_back(grad_h_two, normed_two, inverse_two, mod_row(4))

    cross_grad = second_grad.astype(low)
    grad_c_out = outer(crossed, cross_grad)
    grad_crossed = project(cross_grad, c_out).astype(low)
    grad_cq, grad_ck, grad_cv = attend_back(cq_rows, ck_rows, cv_rows, grad_crossed, logsum_two)
    grad_cq = grad_cq.astype(low)
    grad_c_value = outer(grad_cv.astype(low), text_low)
    grad_ck_parts = to_ring(grad_ck.reshape(text_count, count, share).transpose(1, 0, 2))
    grad_ck_own = grad_ck_parts[0]
    for k in range(1, count):
        grad_ck_own = grad_ck_own + shift(grad_ck_parts[k].astype(low), k).astype(jnp.float32)
    grad_c_query = outer(grad_cq, first_low)
    first_grad = second_grad + expand(grad_cq, c_query)

    attn_grad = (mod_row(2) * first_grad).astype(low)
    grad_w_out = outer(mixed_own, attn_grad)
    grad_mixed = project(attn_grad, w_out).astype(low)
    grad_mixed = to_ring(grad_mixed.reshape(tokens, count, share).transpose(1, 0, 2))
    grad_attended = jnp.concatenate(
        [grad_mixed[0]] + [shift(grad_mixed[k], k) for k in range(1, count)], axis=0
    )
    grads_qkv = attend_back(q_rows, k_rows, v_rows, grad_attended, logsum_one)
    grad_qkv = jnp.concatenate([g.astype(low) for g in grads_qkv], axis=1)
    grad_h_parts = expand(grad_qkv, w_qkv)
    grad_h_one = scatter_ring(list(grad_h_parts.reshape(count, tokens, width)))
    grad_q, grad_k, grad_v = (
        outer(grad_qkv[:, i * share : (i + 1) * share], h_one_all).astype(low) for i in range(3)
    )
    grad_c_key = outer(grad_ck_own.astype(low), text_low).astype(low)
    input_grad = first_grad + norm_back(grad_h_one, normed_one, inverse_one, mod_row(1))

    full_grads = [g.astype(low) for g in (grad_w_out, grad_c_query, grad_c_value, grad_c_out)]
    attn_grads = [grad_q, grad_k, grad_v, grad_c_key]
    if plane:
        even = (me_dp & 1) == 0
        mlp_sum = lax.psum_scatter(mlp_grad, "dp", scatter_dimension=0, tiled=True)
        mlp_sum = lax.all_gather(mlp_sum, "dp", axis=0, tiled=True)

        def halves(grads, lead):
            out = []
            for own_one, own_two, bits_order in (
                (grads[0], grads[1], ((1, -3), (2, -3))),
                (grads[2], grads[3], ((2, -4), (1, -3))),
            ):
                given = jnp.where(even, own_two, own_one)
                kept = jnp.where(even, own_one, own_two)
                total = kept + swap(given, "dp", 0)
                total = total.reshape(lead + (2, 2, unit_rows, width))
                for bit, dim in bits_order:
                    total = halve(total, "dp", bit, total.ndim + dim)
                out.append(total)
            return out

        full_first, full_second = halves(full_grads, (count,))
        full_parts = to_ring(jnp.stack([full_first, full_second], axis=1))
        full_sum = full_parts[0].astype(jnp.float32)
        for k in range(1, count):
            full_sum = full_sum + shift(full_parts[k], k).astype(jnp.float32)
        full_sum = full_sum.astype(low)
        attn_first, attn_second = halves(attn_grads, ())
        pools = gather_plane(
            jnp.stack([attn_first, full_sum[0]]), jnp.stack([attn_second, full_sum[1]])
        )
        which, position = in_pool(member_of, np.where(is_attn, 0, 1), 2)
        which = jnp.where(is_mlp, 2, which)
        position = jnp.where(is_mlp, np.arange(units) - 8 * per, position)
        own = jnp.sum(jnp.where(match[:, :, None], jnp.stack([which, position], 1)[None], 0), axis=1)
        owned = place_blocks((*pools, mlp_sum), own[:, 0], own[:, 1])
    else:
        full_sum = jnp.stack([g.reshape(count, share, width) for g in full_grads], axis=1)
        full_sum = lax.psum_scatter(full_sum, "tensor", scatter_dimension=0, tiled=True)
        order = np.array(group_attn + group_full + group_mlp)
        sums = jnp.concatenate(
            [jnp.concatenate(attn_grads), full_sum.reshape(-1, width), mlp_grad.reshape(-1, width)]
        )
        sums = lax.psum(sums.reshape(units, unit_rows, width), "dp")
        owned = jnp.take(sums, jnp.array(np.argsort(order))[unit_of_slot], axis=0, mode="clip")

    def summed(values):
        return jnp.sum(values, axis=0)

    mod_grad = total_sum(
        jnp.stack(
            [
                summed(grad_h_parts),
                summed(grad_h_parts * normed_all.astype(jnp.float32)),
                summed(branch_one * first_grad),
                summed(grad_h_two),
                summed(grad_h_two * normed_two),
                summed(branch_two * upstream),
            ]
        )
    )

    new_first, new_second, new_master = adamw(
        master,
        first_moment,
        second_moment,
        owned.astype(jnp.float32),
        filled.astype(jnp.float32)[:, None, None],
        rate,
    )
    mod_new_first, mod_new_second, mod_new = adamw(
        mod_table, mod_first, mod_second, mod_grad, 1.0, table_rate
    )
    return (
        block_out[None],
        input_grad[None],
        new_first,
        new_second,
        new_master,
        mod_new_first,
        mod_new_second,
        mod_new,
    )


def solution(mesh):
    in_specs = (
        P("dp", "tensor", None),
        P("dp", None, None),
        P("dp", "tensor"),
        P("dp", None),
        P(),
        P("dp", "tensor", None),
        P("dp", "tensor", None),
        P("dp", "tensor", None),
        P(),
        P(),
        P(),
        P("dp", "tensor", None),
    )
    out_specs = (
        P("dp", "tensor", None),
        P("dp", "tensor", None),
        P("dp", "tensor", None),
        P("dp", "tensor", None),
        P("dp", "tensor", None),
        P(),
        P(),
        P(),
    )
    return jax.shard_map(
        on_device, mesh=mesh, in_specs=in_specs, out_specs=out_specs, check_vma=False
    )
```

```python
from functools import partial
import math

import jax
import jax.numpy as jnp
import numpy as np
from jax import lax
from jax.experimental import pallas as pl
from jax.experimental.pallas import tpu as pltpu
from jax.sharding import PartitionSpec as P

HEAD_DIM = 72
STEP = 10


norm_eps = 1e-06
beta_one = 0.9
beta_two = 0.999
rate = 0.03
table_rate = 0.3
decay = 0.01
adam_eps = 1e-08
gelu_tanh = partial(jax.nn.gelu, approximate=True)
low = jnp.bfloat16


def ranks_of(owners):
    index = jnp.arange(owners.shape[0])
    before = (owners[None, :] == owners[:, None]) & (index[None, :] < index[:, None])
    return jnp.sum(before.astype(jnp.int32), axis=1)


def layer_norm(values):
    center = values - jnp.mean(values, axis=-1, keepdims=True)
    inverse = lax.rsqrt(jnp.mean(center * center, axis=-1, keepdims=True) + norm_eps)
    return (center * inverse, inverse)


def norm_back(grad_rows, normed, inverse, scale_row):
    scaled = grad_rows * (1.0 + scale_row)
    mean_one = jnp.mean(scaled, axis=-1, keepdims=True)
    mean_two = jnp.mean(scaled * normed, axis=-1, keepdims=True)
    return inverse * (scaled - mean_one - normed * mean_two)


def project(rows, weight):
    return jnp.einsum("ld,rd->lr", rows, weight, preferred_element_type=jnp.float32)


def expand(rows, weight):
    return jnp.einsum("lr,rd->ld", rows, weight, preferred_element_type=jnp.float32)


def outer(left, right):
    return jnp.einsum("lr,ld->rd", left, right, preferred_element_type=jnp.float32)


def shift(values, step):
    count = lax.axis_size("tensor")
    return lax.ppermute(values, "tensor", [(i, (i + step) % count) for i in range(count)])


def ring(values):
    return [values] + [shift(values, k) for k in range(1, lax.axis_size("tensor"))]


def scatter_ring(parts):
    count = lax.axis_size("tensor")
    total = parts[0]
    for k in range(1, count):
        total = total + shift(parts[k].astype(low), count - k).astype(jnp.float32)
    return total


def to_ring(stacked):
    count = stacked.shape[0]
    twice = jnp.concatenate([stacked, stacked], axis=0)
    return lax.dynamic_slice_in_dim(twice, lax.axis_index("tensor"), count, 0)


def from_ring(stacked, sign):
    count = stacked.shape[0]
    me = lax.axis_index("tensor")
    place = lax.rem(sign * (jnp.arange(count) - me) + 2 * count, count)
    return jnp.take(stacked, place, axis=0, mode="clip")


def heads_of(rows):
    return rows.reshape(rows.shape[0], -1, HEAD_DIM)


def attend(q_rows, k_rows, v_rows):
    length, width_all = q_rows.shape
    heads = width_all // HEAD_DIM
    block_rows = min(512, length)
    blocks = length // block_rows
    scale = HEAD_DIM ** (-0.5)
    k_heads = heads_of(k_rows)
    v_heads = heads_of(v_rows)

    def one_block(q_block):
        scores = (
            jnp.einsum("qhd,khd->hqk", q_block, k_heads, preferred_element_type=jnp.float32)
            * scale
        )
        top = jnp.max(scores, axis=-1, keepdims=True)
        expo = jnp.exp(scores - top)
        total = jnp.sum(expo, axis=-1, keepdims=True)
        probs = (expo / total).astype(low)
        mixed = jnp.einsum("hqk,khd->qhd", probs, v_heads, preferred_element_type=jnp.float32)
        return (mixed.astype(low), (top + jnp.log(total))[..., 0])

    mixed, logsum = lax.map(one_block, q_rows.reshape(blocks, block_rows, heads, HEAD_DIM))
    return (mixed.reshape(length, width_all), logsum)


def attend_back(q_rows, k_rows, v_rows, grad_mixed, logsum):
    length, width_all = q_rows.shape
    heads = width_all // HEAD_DIM
    block_rows = min(512, length)
    blocks = length // block_rows
    scale = HEAD_DIM ** (-0.5)
    k_heads = heads_of(k_rows)
    v_heads = heads_of(v_rows)

    def one_block(carry, block_item):
        q_block, g_block, l_block = block_item
        scores = (
            jnp.einsum("qhd,khd->hqk", q_block, k_heads, preferred_element_type=jnp.float32)
            * scale
        )
        probs = jnp.exp(scores - l_block[..., None])
        grad_probs = jnp.einsum(
            "qhd,khd->hqk", g_block, v_heads, preferred_element_type=jnp.float32
        )
        inner = jnp.sum(probs * grad_probs, axis=-1, keepdims=True)
        grad_scores = (probs * (grad_probs - inner)).astype(low)
        grad_q = (
            jnp.einsum("hqk,khd->qhd", grad_scores, k_heads, preferred_element_type=jnp.float32)
            * scale
        )
        grad_k = (
            carry[0]
            + jnp.einsum("hqk,qhd->khd", grad_scores, q_block, preferred_element_type=jnp.float32)
            * scale
        )
        grad_v = carry[1] + jnp.einsum(
            "hqk,qhd->khd", probs.astype(low), g_block, preferred_element_type=jnp.float32
        )
        return ((grad_k, grad_v), grad_q)

    start = (jnp.zeros(k_heads.shape, jnp.float32), jnp.zeros(v_heads.shape, jnp.float32))
    (grad_k, grad_v), grad_q = lax.scan(
        one_block,
        start,
        (
            q_rows.reshape(blocks, block_rows, heads, HEAD_DIM),
            grad_mixed.reshape(blocks, block_rows, heads, HEAD_DIM),
            logsum,
        ),
    )
    return (
        grad_q.reshape(length, width_all),
        grad_k.reshape(-1, width_all),
        grad_v.reshape(-1, width_all),
    )


def adamw(weight, moment_one, moment_two, gradient, filled, step_rate):
    new_one = beta_one * moment_one + (1.0 - beta_one) * gradient
    new_two = beta_two * moment_two + (1.0 - beta_two) * gradient * gradient
    fixed_one = new_one / (1.0 - beta_one**STEP)
    fixed_two = new_two / (1.0 - beta_two**STEP)
    updated = weight - step_rate * (fixed_one / (jnp.sqrt(fixed_two) + adam_eps) + decay * weight)
    return (new_one * filled, new_two * filled, updated * filled)


def swap(values, axis, bit):
    count = lax.axis_size(axis)
    return lax.ppermute(values, axis, [(i, i ^ (1 << bit)) for i in range(count)])


def choose(values, index, axis):
    return lax.dynamic_index_in_dim(values, index, axis, keepdims=False)


def halve(values, axis, bit, dim):
    own_bit = (lax.axis_index(axis) >> bit) & 1
    sent = swap(choose(values, 1 - own_bit, dim), axis, bit)
    return choose(values, own_bit, dim) + sent


def total_sum(values):
    for axis in ("dp", "tensor"):
        for bit in range(lax.axis_size(axis).bit_length() - 1):
            values = values + swap(values, axis, bit)
    return values


def pick_units(master, slot_unit, state, kind, place, sizes):
    capacity, unit_rows, width = master.shape
    units = state.shape[0]

    def body(slot_ref, state_ref, kind_ref, place_ref, blocks, *rest):
        outs, (highs, lows, zeros, read, sems) = rest[: len(sizes)], rest[len(sizes) :]

        def start(source, unit):
            for which, out in enumerate(outs):

                @pl.when(kind_ref[unit] == which)
                def _():
                    pltpu.make_async_copy(source, out.at[place_ref[unit]], sems.at[unit]).start()

        @pl.loop(0, capacity)
        def _(slot):
            @pl.when(slot_ref[slot] >= 0)
            def _():
                pltpu.make_async_copy(blocks.at[slot], highs.at[slot], read.at[slot]).start()

        zeros[...] = jnp.zeros_like(zeros)

        @pl.loop(0, units)
        def _(unit):
            @pl.when(state_ref[unit] == 0)
            def _():
                start(zeros, unit)

        @pl.loop(0, capacity)
        def _(slot):
            @pl.when(slot_ref[slot] >= 0)
            def _():
                pltpu.make_async_copy(blocks.at[slot], highs.at[slot], read.at[slot]).wait()
                lows[slot] = highs[slot].astype(low)
                start(lows.at[slot], slot_ref[slot])

        @pl.loop(0, units)
        def _(unit):
            @pl.when(state_ref[unit] < 2)
            def _():
                pltpu.make_async_copy(zeros, outs[0].at[0], sems.at[unit]).wait()

    return pl.pallas_call(
        body,
        grid_spec=pltpu.PrefetchScalarGridSpec(
            num_scalar_prefetch=4,
            grid=(1,),
            in_specs=[pl.BlockSpec(memory_space=pl.ANY)],
            out_specs=[pl.BlockSpec(memory_space=pl.ANY)] * len(sizes),
            scratch_shapes=[
                pltpu.VMEM((capacity, unit_rows, width), jnp.float32),
                pltpu.VMEM((capacity, unit_rows, width), low),
                pltpu.VMEM((unit_rows, width), low),
                pltpu.SemaphoreType.DMA((capacity,)),
                pltpu.SemaphoreType.DMA((units,)),
            ],
        ),
        out_shape=[jax.ShapeDtypeStruct((size, unit_rows, width), low) for size in sizes],
        compiler_params=pltpu.CompilerParams(vmem_limit_bytes=32 * 2**20),
        name="pick_units",
    )(slot_unit, state, kind, place, master)


def place_blocks(sources, which, position):
    amount = which.shape[0]
    shape = sources[0].shape[1:]

    def body(which_ref, position_ref, *rest):
        ins, (out, held, read, sems) = rest[: len(sources)], rest[len(sources) :]

        @pl.loop(0, amount)
        def _(i):
            for source, ref in enumerate(ins):

                @pl.when(which_ref[i] == source)
                def _():
                    pltpu.make_async_copy(ref.at[position_ref[i]], held.at[i], read.at[i]).start()

        @pl.loop(0, amount)
        def _(i):
            pltpu.make_async_copy(ins[0].at[0], held.at[i], read.at[i]).wait()
            pltpu.make_async_copy(held.at[i], out.at[i], sems.at[i]).start()

        @pl.loop(0, amount)
        def _(i):
            pltpu.make_async_copy(held.at[i], out.at[i], sems.at[i]).wait()

    return pl.pallas_call(
        body,
        grid_spec=pltpu.PrefetchScalarGridSpec(
            num_scalar_prefetch=2,
            grid=(1,),
            in_specs=[pl.BlockSpec(memory_space=pl.ANY)] * len(sources),
            out_specs=pl.BlockSpec(memory_space=pl.ANY),
            scratch_shapes=[
                pltpu.VMEM((amount,) + shape, low),
                pltpu.SemaphoreType.DMA((amount,)),
                pltpu.SemaphoreType.DMA((amount,)),
            ],
        ),
        out_shape=jax.ShapeDtypeStruct((amount,) + shape, low),
        compiler_params=pltpu.CompilerParams(vmem_limit_bytes=32 * 2**20),
        name="place_blocks",
    )(which, position, *sources)


def hops(values, step, turn):
    count = lax.axis_size("tensor")
    if step > 0:
        pairs = [(i, i + 1) for i in range(turn - 1, count - 1)]
    else:
        pairs = [(i, i - 1) for i in range(1, count - turn + 1)]
    return lax.ppermute(values, "tensor", pairs)


def slots_of(own, ups, downs):
    count = lax.axis_size("tensor")
    me = lax.axis_index("tensor")
    return [own] + [jnp.where(me >= k, ups[k - 1], downs[count - k - 1]) for k in range(1, count)]


fence = lax.optimization_barrier


def gather_plane(first, second):
    first_all = jnp.concatenate([first, swap(first, "dp", 1)])
    second_all = jnp.concatenate([second, swap(second, "dp", 2)])
    first_far = swap(first_all, "dp", 2)
    second_far = swap(second_all, "dp", 1)
    pool = jnp.concatenate([first_all, first_far, second_all, second_far])
    return (pool, swap(pool, "dp", 0))


def in_pool(member, inner, inner_count):
    me = lax.axis_index("dp")
    half, core = member >> 3, ((member >> 2) & 1) ^ (me & 1)
    far_y, far_x = ((member >> 1) & 1) ^ ((me >> 2) & 1), (member & 1) ^ ((me >> 1) & 1)
    where_first = (far_y * 2 + far_x) * inner_count
    where_second = (4 + far_x * 2 + far_y) * inner_count
    return (core, jnp.where(half == 0, where_first, where_second) + inner)


def on_device(
    hidden_in,
    time_embed,
    caption_table,
    caption_ids,
    owners,
    master,
    first_moment,
    second_moment,
    mod_table,
    mod_first,
    mod_second,
    out_grad,
):
    count = lax.axis_size("tensor")
    dp_count = lax.axis_size("dp")
    me_dp = lax.axis_index("dp")
    me_tensor = lax.axis_index("tensor")
    capacity, unit_rows, width = master.shape
    units = owners.shape[0]
    tokens = hidden_in.shape[1]
    text_count = caption_ids.shape[1]
    share = width // count
    per = share // unit_rows
    ups = (units - 8 * per) // 2
    rank_of = ranks_of(owners)
    mine = owners == me_dp
    match = (rank_of[None, :] == jnp.arange(capacity)[:, None]) & mine[None, :]
    filled = jnp.any(match, axis=1)
    unit_of_slot = jnp.sum(jnp.where(match, jnp.arange(units)[None, :], 0), axis=1)

    square = [list(range(i * per, (i + 1) * per)) for i in range(8)]
    group_attn = square[0] + square[1] + square[2] + square[5]
    group_full = square[3] + square[4] + square[6] + square[7]
    group_mlp = list(range(8 * per, units))
    members = len(group_attn)
    plane = dp_count == 8 and members == 16 and len(group_mlp) % dp_count == 0
    member_of = np.zeros(units, np.int32)
    member_of[group_attn] = np.arange(members)
    member_of[group_full] = np.arange(members)
    is_attn = np.zeros(units, bool)
    is_attn[group_attn] = True
    is_mlp = np.zeros(units, bool)
    is_mlp[group_mlp] = True

    latent_in = hidden_in[0].astype(jnp.float32)
    upstream = out_grad[0].astype(jnp.float32)
    modulate = mod_table + time_embed[0]

    def mod_row(which_row):
        return modulate[which_row][None, :]

    normed_one, inverse_one = layer_norm(latent_in)
    bits = dp_count.bit_length() - 1
    vocab_rows = caption_table.shape[0]

    def caption_terms(ids):
        chosen = ids.reshape(-1) - me_dp * vocab_rows
        onehot = (chosen[:, None] == jnp.arange(vocab_rows)[None, :]).astype(low)
        terms = jnp.dot(onehot, caption_table, preferred_element_type=jnp.float32).astype(low)
        return terms.reshape(dp_count, text_count, -1)

    grad_mlp = (mod_row(5) * upstream).astype(low)

    n_low = normed_one.astype(low)
    if plane:
        core, far_x, far_y = (
            ((member_of >> 2) & 1) ^ (me_dp & 1),
            (member_of & 1) ^ ((me_dp >> 1) & 1),
            ((member_of >> 1) & 1) ^ ((me_dp >> 2) & 1),
        )
        place = jnp.where(is_attn, far_x * 4 + far_y * 2, 8 + far_y * 4 + far_x * 2)
        place = jnp.where(is_mlp, np.arange(units) - 8 * per, place + (member_of >> 3))
        kind = jnp.where(is_mlp, 0, core)
        slot_mlp = unit_of_slot >= 8 * per
        owned_state = mine.astype(jnp.int32)
        up, down = hops(n_low, 1, 1), hops(n_low, -1, 1)
        kept, given = pick_units(
            master,
            jnp.where(filled & ~slot_mlp, unit_of_slot, -1),
            jnp.where(is_mlp, 2, owned_state),
            kind,
            place,
            (members, members),
        )
        got = swap(given, "dp", 0)
        ids = jnp.concatenate([caption_ids, swap(caption_ids, "dp", 0)])
        (mlp_part,) = pick_units(
            master,
            jnp.where(filled & slot_mlp, unit_of_slot, -1),
            jnp.where(is_mlp, owned_state, 2),
            kind,
            place,
            (len(group_mlp),),
        )
        mlp_part = lax.psum_scatter(mlp_part, "dp", scatter_dimension=0, tiled=True)
        n_up, n_down = [up], [down]
        half = kept + got
        half, up, down, ids = fence((half, up, down, ids))
        up, down = hops(up, 1, 2), hops(down, -1, 2)
        attn_two = half[0:4] + swap(half[4:8], "dp", 1)
        full_two = half[8:12] + swap(half[12:16], "dp", 2)
        ids = jnp.concatenate([ids, swap(ids, "dp", 1)])
        n_up.append(up), n_down.append(down)
        attn_two, full_two, up, down, ids = fence((attn_two, full_two, up, down, ids))
        up, down = hops(up, 1, 3), hops(down, -1, 3)
        attn_one = attn_two[0:2] + swap(attn_two[2:4], "dp", 2)
        full_one = full_two[0:2] + swap(full_two[2:4], "dp", 1)
        ids = jnp.concatenate([ids, swap(ids, "dp", 2)])
        n_up.append(up), n_down.append(down)
        attn_one, full_one, up, down, ids = fence((attn_one, full_one, up, down, ids))
        grad_mlp_whole = lax.all_gather(fence((grad_mlp, up))[0], "tensor", axis=0)
        first = jnp.concatenate([attn_one[0:1], swap(attn_one[0:1], "dp", 1)])
        second = jnp.concatenate([attn_one[1:2], swap(attn_one[1:2], "dp", 2)])
        up, down = hops(full_one, 1, 1), hops(full_one, -1, 1)
        text = caption_terms(ids)
        text = text[0:4] + swap(text[4:8], "dp", 2)
        f_up, f_down = [up], [down]
        first, second, up, down, text = fence((first, second, up, down, text))
        pool = jnp.concatenate([first, swap(first, "dp", 2), second, swap(second, "dp", 1)])
        up, down = hops(up, 1, 2), hops(down, -1, 2)
        text = text[0:2] + swap(text[2:4], "dp", 1)
        f_up.append(up), f_down.append(down)
        pool, up, down, text = fence((pool, up, down, text))
        other = swap(pool, "dp", 0)
        up, down = hops(up, 1, 3), hops(down, -1, 3)
        text = text[0] + swap(text[1], "dp", 0)
        f_up.append(up), f_down.append(down)
        pool, other, up, down, text = fence((pool, other, up, down, text))
        w_attn = place_blocks((pool, other), *in_pool(np.arange(members), 0, 1))
        full_ring = slots_of(full_one, f_up, f_down)
        first = jnp.concatenate([item[0:1] for item in full_ring])
        second = jnp.concatenate([item[1:2] for item in full_ring])
        first = jnp.concatenate([first, swap(first, "dp", 1)])
        second = jnp.concatenate([second, swap(second, "dp", 2)])
        text_ring = jnp.stack(ring(text))
        first, second, text_ring = fence((first, second, text_ring))
        pool = jnp.concatenate([first, swap(first, "dp", 2), second, swap(second, "dp", 1)])
        other = swap(pool, "dp", 0)
        mlp_part = fence((mlp_part, pool))[0]
        w_mlp = lax.all_gather(mlp_part, "dp", axis=0, tiled=True)
        listing = np.arange(count * members)
        matrix, rank, head = listing // (count * per), listing // per % count, listing % per
        slot = lax.rem(me_tensor - rank + count, count)
        w_full = place_blocks((pool, other), *in_pool(matrix * per + head, slot, count))
        w_full = w_full.reshape(4, width, width)
        normed_all = jnp.concatenate(slots_of(n_low, n_up, n_down))
    else:
        slots_low = master.astype(low)
        rows = jnp.take(slots_low, rank_of, axis=0, mode="clip")
        rows = lax.psum(jnp.where(mine[:, None, None], rows, jnp.zeros((), low)), "dp")
        w_attn = rows[np.array(group_attn)]
        w_full = lax.all_gather(rows[np.array(group_full)], "tensor", axis=0)
        w_full = w_full.reshape(count, 4, share, width).swapaxes(0, 1).reshape(4, width, width)
        w_mlp = rows[8 * per :]
        normed_all = jnp.concatenate(ring(n_low))
        grad_mlp_whole = lax.all_gather(grad_mlp, "tensor", axis=0)
        ids = caption_ids
        for bit in range(bits):
            ids = jnp.concatenate([ids, swap(ids, "dp", bit)])
        text = caption_terms(ids)
        for bit in reversed(range(bits)):
            text = text[: 1 << bit] + swap(text[1 << bit :], "dp", bit)
        text_ring = jnp.stack(ring(text[0]))
    h_one_all = (normed_all.astype(jnp.float32) * (1.0 + mod_row(1)) + mod_row(0)).astype(low)
    grad_mlp_all = from_ring(grad_mlp_whole, -1).reshape(-1, width)
    w_attn = w_attn.reshape(-1, width)
    w_qkv, c_key = w_attn[: 3 * share], w_attn[3 * share :]
    w_out, c_query, c_value, c_out = w_full
    w_up = w_mlp[:ups].reshape(-1, width)
    w_down = w_mlp[ups:].reshape(-1, width)
    text_low = from_ring(text_ring, -1).transpose(1, 0, 2).reshape(text_count, width)

    qkv = project(h_one_all, w_qkv).astype(low)
    q_rows, k_rows, v_rows = qkv[:, :share], qkv[:, share : 2 * share], qkv[:, 2 * share :]
    attended, logsum_one = attend(q_rows, k_rows, v_rows)
    mixed_parts = attended.reshape(count, tokens, share)
    mixed_ring = jnp.stack(
        [mixed_parts[0]] + [shift(mixed_parts[k], count - k) for k in range(1, count)]
    )
    mixed_own = from_ring(mixed_ring, 1).transpose(1, 0, 2).reshape(tokens, width)
    branch_one = expand(mixed_own, w_out)
    first_res = latent_in + mod_row(2) * branch_one
    first_low = first_res.astype(low)

    ck_ring = from_ring(jnp.stack(ring(project(text_low, c_key).astype(low))), -1)
    ck_rows = ck_ring.transpose(1, 0, 2).reshape(text_count, width)
    cv_rows = project(text_low, c_value).astype(low)
    cq_rows = project(first_low, c_query).astype(low)
    crossed, logsum_two = attend(cq_rows, ck_rows, cv_rows)
    second_res = first_res + expand(crossed, c_out)
    normed_two, inverse_two = layer_norm(second_res)
    h_two = (normed_two * (1.0 + mod_row(4)) + mod_row(3)).astype(low)

    h_two_all = jnp.concatenate(ring(h_two), axis=0)
    pre_act = project(h_two_all, w_up)
    act_low = gelu_tanh(pre_act).astype(low)
    ignored, gelu_pull = jax.vjp(gelu_tanh, pre_act)
    grad_act = project(grad_mlp_all, w_down)
    grad_pre = gelu_pull(grad_act)[0].astype(low)
    grad_terms = expand(grad_pre, w_up).astype(low)
    grad_terms, act_low, grad_pre = fence((grad_terms, act_low, grad_pre))
    grad_terms = grad_terms.reshape(count, tokens, width)
    grad_h_two = grad_terms[0].astype(jnp.float32)
    for k in range(1, count):
        grad_h_two = grad_h_two + shift(grad_terms[k], count - k).astype(jnp.float32)
    grad_up = outer(grad_pre, h_two_all).astype(low)
    grad_down = outer(act_low, grad_mlp_all).astype(low)
    mlp_grad = jnp.concatenate([grad_up, grad_down]).reshape(-1, unit_rows, width)
    mlp_grad, act_low = fence((mlp_grad, act_low))
    branch_terms = expand(act_low, w_down).astype(low).reshape(count, tokens, width)
    branch_terms = from_ring(branch_terms, -1).reshape(-1, width)
    branch_two = lax.psum_scatter(branch_terms, "tensor", scatter_dimension=0, tiled=True)
    branch_two = branch_two.astype(jnp.float32)
    if plane:
        mlp_sum = lax.psum_scatter(mlp_grad, "dp", scatter_dimension=0, tiled=True)
        mlp_sum = lax.all_gather(mlp_sum, "dp", axis=0, tiled=True)
    block_out = second_res + mod_row(5) * branch_two
    second_grad = upstream + norm_back(grad_h_two, normed_two, inverse_two, mod_row(4))

    cross_grad = second_grad.astype(low)
    grad_c_out = outer(crossed, cross_grad)
    grad_crossed = project(cross_grad, c_out).astype(low)
    grad_cq, grad_ck, grad_cv = attend_back(cq_rows, ck_rows, cv_rows, grad_crossed, logsum_two)
    grad_cq = grad_cq.astype(low)
    grad_c_value = outer(grad_cv.astype(low), text_low)
    grad_ck_parts = to_ring(grad_ck.reshape(text_count, count, share).transpose(1, 0, 2))
    grad_ck_own = grad_ck_parts[0]
    for k in range(1, count):
        grad_ck_own = grad_ck_own + shift(grad_ck_parts[k].astype(low), k).astype(jnp.float32)
    grad_c_query = outer(grad_cq, first_low)
    first_grad = second_grad + expand(grad_cq, c_query)

    attn_grad = (mod_row(2) * first_grad).astype(low)
    grad_w_out = outer(mixed_own, attn_grad)
    grad_mixed = project(attn_grad, w_out).astype(low)
    grad_mixed = to_ring(grad_mixed.reshape(tokens, count, share).transpose(1, 0, 2))
    grad_attended = jnp.concatenate(
        [grad_mixed[0]] + [shift(grad_mixed[k], k) for k in range(1, count)], axis=0
    )
    grads_qkv = attend_back(q_rows, k_rows, v_rows, grad_attended, logsum_one)
    grad_qkv = jnp.concatenate([g.astype(low) for g in grads_qkv], axis=1)
    grad_h_parts = expand(grad_qkv, w_qkv)
    grad_h_one = scatter_ring(list(grad_h_parts.reshape(count, tokens, width)))
    grad_q, grad_k, grad_v = (
        outer(grad_qkv[:, i * share : (i + 1) * share], h_one_all).astype(low) for i in range(3)
    )
    grad_c_key = outer(grad_ck_own.astype(low), text_low).astype(low)
    input_grad = first_grad + norm_back(grad_h_one, normed_one, inverse_one, mod_row(1))

    full_grads = [g.astype(low) for g in (grad_w_out, grad_c_query, grad_c_value, grad_c_out)]
    attn_grads = [grad_q, grad_k, grad_v, grad_c_key]
    if plane:
        even = (me_dp & 1) == 0
        def halves(grads, lead):
            out = []
            for own_one, own_two, bits_order in (
                (grads[0], grads[1], ((1, -3), (2, -3))),
                (grads[2], grads[3], ((2, -4), (1, -3))),
            ):
                given = jnp.where(even, own_two, own_one)
                kept = jnp.where(even, own_one, own_two)
                total = kept + swap(given, "dp", 0)
                total = total.reshape(lead + (2, 2, unit_rows, width))
                for bit, dim in bits_order:
                    total = halve(total, "dp", bit, total.ndim + dim)
                out.append(total)
            return out

        full_first, full_second = halves(full_grads, (count,))
        full_parts = to_ring(jnp.stack([full_first, full_second], axis=1))
        full_sum = full_parts[0].astype(jnp.float32)
        for k in range(1, count):
            full_sum = full_sum + shift(full_parts[k], k).astype(jnp.float32)
        full_sum = full_sum.astype(low)
        attn_first, attn_second = halves(attn_grads, ())
        pools = gather_plane(
            jnp.stack([attn_first, full_sum[0]]), jnp.stack([attn_second, full_sum[1]])
        )
        which, position = in_pool(member_of, np.where(is_attn, 0, 1), 2)
        which = jnp.where(is_mlp, 2, which)
        position = jnp.where(is_mlp, np.arange(units) - 8 * per, position)
        own = jnp.sum(jnp.where(match[:, :, None], jnp.stack([which, position], 1)[None], 0), axis=1)
        owned = place_blocks((*pools, mlp_sum), own[:, 0], own[:, 1])
    else:
        full_sum = jnp.stack([g.reshape(count, share, width) for g in full_grads], axis=1)
        full_sum = lax.psum_scatter(full_sum, "tensor", scatter_dimension=0, tiled=True)
        order = np.array(group_attn + group_full + group_mlp)
        sums = jnp.concatenate(
            [jnp.concatenate(attn_grads), full_sum.reshape(-1, width), mlp_grad.reshape(-1, width)]
        )
        sums = lax.psum(sums.reshape(units, unit_rows, width), "dp")
        owned = jnp.take(sums, jnp.array(np.argsort(order))[unit_of_slot], axis=0, mode="clip")

    def summed(values):
        return jnp.sum(values, axis=0)

    mod_grad = total_sum(
        jnp.stack(
            [
                summed(grad_h_parts),
                summed(grad_h_parts * normed_all.astype(jnp.float32)),
                summed(branch_one * first_grad),
                summed(grad_h_two),
                summed(grad_h_two * normed_two),
                summed(branch_two * upstream),
            ]
        )
    )

    new_first, new_second, new_master = adamw(
        master,
        first_moment,
        second_moment,
        owned.astype(jnp.float32),
        filled.astype(jnp.float32)[:, None, None],
        rate,
    )
    mod_new_first, mod_new_second, mod_new = adamw(
        mod_table, mod_first, mod_second, mod_grad, 1.0, table_rate
    )
    return (
        block_out[None],
        input_grad[None],
        new_first,
        new_second,
        new_master,
        mod_new_first,
        mod_new_second,
        mod_new,
    )


def solution(mesh):
    in_specs = (
        P("dp", "tensor", None),
        P("dp", None, None),
        P("dp", "tensor"),
        P("dp", None),
        P(),
        P("dp", "tensor", None),
        P("dp", "tensor", None),
        P("dp", "tensor", None),
        P(),
        P(),
        P(),
        P("dp", "tensor", None),
    )
    out_specs = (
        P("dp", "tensor", None),
        P("dp", "tensor", None),
        P("dp", "tensor", None),
        P("dp", "tensor", None),
        P("dp", "tensor", None),
        P(),
        P(),
        P(),
    )
    return jax.shard_map(
        on_device, mesh=mesh, in_specs=in_specs, out_specs=out_specs, check_vma=False
    )
```

```python
import math

import jax
import jax.numpy as jnp
import numpy as np
from jax import lax
from jax.experimental import pallas as pl
from jax.experimental.pallas import tpu as pltpu
from jax.sharding import PartitionSpec as P

HEAD_DIM = 72
STEP = 10


norm_eps = 1e-06
beta_one = 0.9
beta_two = 0.999
rate = 0.03
table_rate = 0.3
decay = 0.01
adam_eps = 1e-08
low = jnp.bfloat16


def ranks_of(owners):
    index = jnp.arange(owners.shape[0])
    before = (owners[None, :] == owners[:, None]) & (index[None, :] < index[:, None])
    return jnp.sum(before.astype(jnp.int32), axis=1)


def layer_norm(values):
    center = values - jnp.mean(values, axis=-1, keepdims=True)
    inverse = lax.rsqrt(jnp.mean(center * center, axis=-1, keepdims=True) + norm_eps)
    return (center * inverse, inverse)


def norm_back(grad_rows, normed, inverse, scale_row):
    scaled = grad_rows * (1.0 + scale_row)
    mean_one = jnp.mean(scaled, axis=-1, keepdims=True)
    mean_two = jnp.mean(scaled * normed, axis=-1, keepdims=True)
    return inverse * (scaled - mean_one - normed * mean_two)


def project(rows, weight):
    return jnp.einsum("ld,rd->lr", rows, weight, preferred_element_type=jnp.float32)


def expand(rows, weight):
    return jnp.einsum("lr,rd->ld", rows, weight, preferred_element_type=jnp.float32)


def outer(left, right):
    return jnp.einsum("lr,ld->rd", left, right, preferred_element_type=jnp.float32)


def shift(values, step):
    count = lax.axis_size("tensor")
    return lax.ppermute(values, "tensor", [(i, (i + step) % count) for i in range(count)])


def ring(values):
    return [values] + [shift(values, k) for k in range(1, lax.axis_size("tensor"))]


def to_ring(stacked):
    count = stacked.shape[0]
    twice = jnp.concatenate([stacked, stacked], axis=0)
    return lax.dynamic_slice_in_dim(twice, lax.axis_index("tensor"), count, 0)


def from_ring(stacked, sign):
    count = stacked.shape[0]
    me = lax.axis_index("tensor")
    place = lax.rem(sign * (jnp.arange(count) - me) + 2 * count, count)
    return jnp.take(stacked, place, axis=0, mode="clip")


def heads_of(rows):
    return rows.reshape(rows.shape[0], -1, HEAD_DIM)


cheap = pl.CostEstimate(flops=1000, bytes_accessed=1000, transcendentals=0)


def self_attend(qkv):
    length, width_all = qkv.shape
    share = width_all // 3
    heads = share // HEAD_DIM
    rows = min(256, length)
    scale = HEAD_DIM ** (-0.5)

    def body(qkv_ref, out_ref):
        @pl.loop(0, length // rows)
        def _(step):
            here = pl.ds(pl.multiple_of(step * rows, rows), rows)
            parts = []
            for head in range(heads):
                at = head * HEAD_DIM
                q = qkv_ref[here, at : at + HEAD_DIM]
                k = qkv_ref[:, share + at : share + at + HEAD_DIM]
                v = qkv_ref[:, 2 * share + at : 2 * share + at + HEAD_DIM]
                scores = scale * lax.dot_general(
                    k, q, (((1,), (1,)), ((), ())), preferred_element_type=jnp.float32
                )
                expo = jnp.exp(scores - jnp.max(scores, axis=0, keepdims=True))
                inverse = 1.0 / jnp.sum(expo, axis=0, keepdims=True)
                probs = (expo * inverse).astype(low)
                mixed = lax.dot_general(
                    v, probs, (((0,), (0,)), ((), ())), preferred_element_type=jnp.float32
                )
                parts.append(mixed.T)
            out_ref[here, :] = jnp.concatenate(parts, axis=1).astype(low)

    return pl.pallas_call(
        body,
        out_shape=jax.ShapeDtypeStruct((length, share), low),
        compiler_params=pltpu.CompilerParams(vmem_limit_bytes=32 * 2**20),
        cost_estimate=cheap,
        name="self_attend",
    )(qkv)


def self_attend_back(qkv, grad_mixed):
    length, width_all = qkv.shape
    share = width_all // 3
    heads = share // HEAD_DIM
    rows = min(256, length)
    steps = length // rows
    scale = HEAD_DIM ** (-0.5)

    def body(qkv_ref, grad_ref, out_ref, grad_k, grad_v):
        grad_k[...] = jnp.zeros_like(grad_k)
        grad_v[...] = jnp.zeros_like(grad_v)

        @pl.loop(0, steps)
        def _(step):
            here = pl.ds(pl.multiple_of(step * rows, rows), rows)
            parts = []
            for head in range(heads):
                at = head * HEAD_DIM
                q = qkv_ref[here, at : at + HEAD_DIM]
                k = qkv_ref[:, share + at : share + at + HEAD_DIM]
                v = qkv_ref[:, 2 * share + at : 2 * share + at + HEAD_DIM]
                g = grad_ref[here, at : at + HEAD_DIM]
                scores = scale * lax.dot_general(
                    k, q, (((1,), (1,)), ((), ())), preferred_element_type=jnp.float32
                )
                expo = jnp.exp(scores - jnp.max(scores, axis=0, keepdims=True))
                probs = expo * (1.0 / jnp.sum(expo, axis=0, keepdims=True))
                grad_probs = lax.dot_general(
                    v, g, (((1,), (1,)), ((), ())), preferred_element_type=jnp.float32
                )
                inner = jnp.sum(probs * grad_probs, axis=0, keepdims=True)
                grad_scores = (probs * (grad_probs - inner)).astype(low)
                grad_v[head] += jnp.dot(
                    probs.astype(low), g, preferred_element_type=jnp.float32
                )
                grad_k[head] += jnp.dot(grad_scores, q, preferred_element_type=jnp.float32)
                grad_q = lax.dot_general(
                    k, grad_scores, (((0,), (0,)), ((), ())), preferred_element_type=jnp.float32
                )
                parts.append(grad_q.T * scale)
            out_ref[here, :share] = jnp.concatenate(parts, axis=1).astype(low)

        both = [grad_k[head] * scale for head in range(heads)]
        out_ref[:, share : 2 * share] = jnp.concatenate(both, axis=1).astype(low)
        both = [grad_v[head] for head in range(heads)]
        out_ref[:, 2 * share :] = jnp.concatenate(both, axis=1).astype(low)

    return pl.pallas_call(
        body,
        out_shape=jax.ShapeDtypeStruct((length, width_all), low),
        scratch_shapes=[pltpu.VMEM((heads, length, HEAD_DIM), jnp.float32)] * 2,
        compiler_params=pltpu.CompilerParams(vmem_limit_bytes=40 * 2**20),
        cost_estimate=cheap,
        name="self_attend_back",
    )(qkv, grad_mixed)


def mlp_core(rows_in, grads_in, w_mlp):
    groups = len(rows_in)
    tokens, width = rows_in[0].shape
    hidden = w_mlp.shape[0] // 2
    chunk = 384 if hidden % 384 == 0 else hidden
    steps = hidden // chunk
    curve = 0.7978845608028654

    def body(*refs):
        rows, grads = refs[:groups], refs[groups : 2 * groups]
        up, down = refs[2 * groups : 2 * groups + 2]
        act, grad_pre = refs[2 * groups + 2 : 2 * groups + 4]
        outs = refs[2 * groups + 4 : 3 * groups + 4]
        total = refs[-1]
        step = pl.program_id(0)
        for i in range(groups):
            pre = lax.dot_general(
                rows[i][...], up[...], (((1,), (1,)), ((), ())), preferred_element_type=jnp.float32
            )
            square = pre * pre
            bend = jnp.tanh(curve * pre * (1.0 + 0.044715 * square))
            half = 0.5 * (1.0 + bend)
            here = pl.ds(i * tokens, tokens)
            act[here, :] = (pre * half).astype(low)
            slope = half + (0.5 * curve) * pre * (1.0 - bend * bend) * (1.0 + 0.134145 * square)
            grad_act = lax.dot_general(
                grads[i][...], down[...], (((1,), (1,)), ((), ())), preferred_element_type=jnp.float32
            )
            grad_low = (grad_act * slope).astype(low)
            grad_pre[here, :] = grad_low
            term = jnp.dot(grad_low, up[...], preferred_element_type=jnp.float32)

            @pl.when(step == 0)
            def _():
                total[here, :] = term

            @pl.when(step > 0)
            def _():
                total[here, :] += term

            @pl.when(step == steps - 1)
            def _():
                outs[i][...] = total[here, :].astype(low)

    whole = pl.BlockSpec((tokens, width), lambda s: (0, 0))
    across = pl.BlockSpec((groups * tokens, chunk), lambda s: (0, s))
    return pl.pallas_call(
        body,
        grid=(steps,),
        in_specs=[whole] * (2 * groups)
        + [
            pl.BlockSpec((chunk, width), lambda s: (s, 0)),
            pl.BlockSpec((chunk, width), lambda s: (steps + s, 0)),
        ],
        out_specs=[across, across] + [whole] * groups,
        out_shape=[jax.ShapeDtypeStruct((groups * tokens, hidden), low)] * 2
        + [jax.ShapeDtypeStruct((tokens, width), low)] * groups,
        scratch_shapes=[pltpu.VMEM((groups * tokens, width), jnp.float32)],
        compiler_params=pltpu.CompilerParams(vmem_limit_bytes=40 * 2**20),
        cost_estimate=cheap,
        name="mlp_core",
    )(*rows_in, *grads_in, w_mlp, w_mlp)


def update_slots(master, first_moment, second_moment, filled, which, position, sources):
    capacity, unit_rows, width = master.shape

    def body(filled_ref, which_ref, position_ref, weight, one, two, *rest):
        ins = rest[: len(sources)]
        new_one, new_two, new_weight, held, sems = rest[len(sources) :]
        slot = pl.program_id(0)

        def fetch(other):
            for source, ref in enumerate(ins):

                @pl.when(which_ref[other] == source)
                def _():
                    pltpu.make_async_copy(
                        ref.at[position_ref[other]], held.at[other % 2], sems.at[other % 2]
                    ).start()

        @pl.when(slot == 0)
        def _():
            fetch(slot)

        @pl.when(slot < capacity - 1)
        def _():
            fetch(slot + 1)

        pltpu.make_async_copy(ins[0].at[0], held.at[slot % 2], sems.at[slot % 2]).wait()
        mask = (filled_ref[slot] > 0).astype(jnp.float32)
        grad = held[slot % 2].astype(jnp.float32)
        results = adamw(weight[0], one[0], two[0], grad, mask, rate)
        new_one[0], new_two[0], new_weight[0] = results

    block = pl.BlockSpec((1, unit_rows, width), lambda s, *_: (s, 0, 0))
    return pl.pallas_call(
        body,
        grid_spec=pltpu.PrefetchScalarGridSpec(
            num_scalar_prefetch=3,
            grid=(capacity,),
            in_specs=[block] * 3 + [pl.BlockSpec(memory_space=pl.ANY)] * len(sources),
            out_specs=[block] * 3,
            scratch_shapes=[
                pltpu.VMEM((2, unit_rows, width), low),
                pltpu.SemaphoreType.DMA((2,)),
            ],
        ),
        out_shape=[jax.ShapeDtypeStruct(master.shape, jnp.float32)] * 3,
        compiler_params=pltpu.CompilerParams(vmem_limit_bytes=56 * 2**20),
        name="update_slots",
    )(filled, which, position, master, first_moment, second_moment, *sources)


def attend(q_rows, k_rows, v_rows):
    length, width_all = q_rows.shape
    heads = width_all // HEAD_DIM
    block_rows = min(512, length)
    blocks = length // block_rows
    scale = HEAD_DIM ** (-0.5)
    k_heads = heads_of(k_rows)
    v_heads = heads_of(v_rows)

    def one_block(q_block):
        scores = (
            jnp.einsum("qhd,khd->hqk", q_block, k_heads, preferred_element_type=jnp.float32)
            * scale
        )
        top = jnp.max(scores, axis=-1, keepdims=True)
        expo = jnp.exp(scores - top)
        total = jnp.sum(expo, axis=-1, keepdims=True)
        probs = (expo / total).astype(low)
        mixed = jnp.einsum("hqk,khd->qhd", probs, v_heads, preferred_element_type=jnp.float32)
        return (mixed.astype(low), (top + jnp.log(total))[..., 0])

    mixed, logsum = lax.map(one_block, q_rows.reshape(blocks, block_rows, heads, HEAD_DIM))
    return (mixed.reshape(length, width_all), logsum)


def attend_back(q_rows, k_rows, v_rows, grad_mixed, logsum):
    length, width_all = q_rows.shape
    heads = width_all // HEAD_DIM
    block_rows = min(512, length)
    blocks = length // block_rows
    scale = HEAD_DIM ** (-0.5)
    k_heads = heads_of(k_rows)
    v_heads = heads_of(v_rows)

    def one_block(carry, block_item):
        q_block, g_block, l_block = block_item
        scores = (
            jnp.einsum("qhd,khd->hqk", q_block, k_heads, preferred_element_type=jnp.float32)
            * scale
        )
        probs = jnp.exp(scores - l_block[..., None])
        grad_probs = jnp.einsum(
            "qhd,khd->hqk", g_block, v_heads, preferred_element_type=jnp.float32
        )
        inner = jnp.sum(probs * grad_probs, axis=-1, keepdims=True)
        grad_scores = (probs * (grad_probs - inner)).astype(low)
        grad_q = (
            jnp.einsum("hqk,khd->qhd", grad_scores, k_heads, preferred_element_type=jnp.float32)
            * scale
        )
        grad_k = (
            carry[0]
            + jnp.einsum("hqk,qhd->khd", grad_scores, q_block, preferred_element_type=jnp.float32)
            * scale
        )
        grad_v = carry[1] + jnp.einsum(
            "hqk,qhd->khd", probs.astype(low), g_block, preferred_element_type=jnp.float32
        )
        return ((grad_k, grad_v), grad_q)

    start = (jnp.zeros(k_heads.shape, jnp.float32), jnp.zeros(v_heads.shape, jnp.float32))
    (grad_k, grad_v), grad_q = lax.scan(
        one_block,
        start,
        (
            q_rows.reshape(blocks, block_rows, heads, HEAD_DIM),
            grad_mixed.reshape(blocks, block_rows, heads, HEAD_DIM),
            logsum,
        ),
    )
    return (
        grad_q.reshape(length, width_all),
        grad_k.reshape(-1, width_all),
        grad_v.reshape(-1, width_all),
    )


def adamw(weight, moment_one, moment_two, gradient, filled, step_rate):
    new_one = beta_one * moment_one + (1.0 - beta_one) * gradient
    new_two = beta_two * moment_two + (1.0 - beta_two) * gradient * gradient
    fixed_one = new_one / (1.0 - beta_one**STEP)
    fixed_two = new_two / (1.0 - beta_two**STEP)
    updated = weight - step_rate * (fixed_one / (jnp.sqrt(fixed_two) + adam_eps) + decay * weight)
    return (new_one * filled, new_two * filled, updated * filled)


def swap(values, axis, bit):
    count = lax.axis_size(axis)
    return lax.ppermute(values, axis, [(i, i ^ (1 << bit)) for i in range(count)])


def choose(values, index, axis):
    return lax.dynamic_index_in_dim(values, index, axis, keepdims=False)


def total_sum(values):
    for axis in ("dp", "tensor"):
        for bit in range(lax.axis_size(axis).bit_length() - 1):
            values = values + swap(values, axis, bit)
    return values


def pick_units(master, slot_unit, state, kind, place, sizes):
    capacity, unit_rows, width = master.shape
    units = state.shape[0]

    def body(slot_ref, state_ref, kind_ref, place_ref, blocks, *rest):
        outs, (highs, lows, zeros, read, sems) = rest[: len(sizes)], rest[len(sizes) :]

        def start(source, unit):
            for which, out in enumerate(outs):

                @pl.when(kind_ref[unit] == which)
                def _():
                    pltpu.make_async_copy(source, out.at[place_ref[unit]], sems.at[unit]).start()

        @pl.loop(0, capacity)
        def _(slot):
            @pl.when(slot_ref[slot] >= 0)
            def _():
                pltpu.make_async_copy(blocks.at[slot], highs.at[slot], read.at[slot]).start()

        zeros[...] = jnp.zeros_like(zeros)

        @pl.loop(0, units)
        def _(unit):
            @pl.when(state_ref[unit] == 0)
            def _():
                start(zeros, unit)

        @pl.loop(0, capacity)
        def _(slot):
            @pl.when(slot_ref[slot] >= 0)
            def _():
                pltpu.make_async_copy(blocks.at[slot], highs.at[slot], read.at[slot]).wait()
                lows[slot] = highs[slot].astype(low)
                start(lows.at[slot], slot_ref[slot])

        @pl.loop(0, units)
        def _(unit):
            @pl.when(state_ref[unit] < 2)
            def _():
                pltpu.make_async_copy(zeros, outs[0].at[0], sems.at[unit]).wait()

    return pl.pallas_call(
        body,
        grid_spec=pltpu.PrefetchScalarGridSpec(
            num_scalar_prefetch=4,
            grid=(1,),
            in_specs=[pl.BlockSpec(memory_space=pl.ANY)],
            out_specs=[pl.BlockSpec(memory_space=pl.ANY)] * len(sizes),
            scratch_shapes=[
                pltpu.VMEM((capacity, unit_rows, width), jnp.float32),
                pltpu.VMEM((capacity, unit_rows, width), low),
                pltpu.VMEM((unit_rows, width), low),
                pltpu.SemaphoreType.DMA((capacity,)),
                pltpu.SemaphoreType.DMA((units,)),
            ],
        ),
        out_shape=[jax.ShapeDtypeStruct((size, unit_rows, width), low) for size in sizes],
        compiler_params=pltpu.CompilerParams(vmem_limit_bytes=56 * 2**20),
        cost_estimate=cheap,
        name="pick_units",
    )(slot_unit, state, kind, place, master)


def place_blocks(sources, which, position, parts=1):
    amount = which.shape[0]
    shape = sources[0].shape[1:]
    size = amount // parts

    def body(which_ref, position_ref, *rest):
        ins, outs = rest[: len(sources)], rest[len(sources) : len(sources) + parts]
        held, read, sems = rest[len(sources) + parts :]

        @pl.loop(0, amount)
        def _(i):
            for source, ref in enumerate(ins):

                @pl.when(which_ref[i] == source)
                def _():
                    pltpu.make_async_copy(ref.at[position_ref[i]], held.at[i], read.at[i]).start()

        for part, out in enumerate(outs):

            @pl.loop(0, size)
            def _(j):
                i = part * size + j
                pltpu.make_async_copy(ins[0].at[0], held.at[i], read.at[i]).wait()
                pltpu.make_async_copy(held.at[i], out.at[j], sems.at[i]).start()

        @pl.loop(0, amount)
        def _(i):
            pltpu.make_async_copy(held.at[i], outs[0].at[0], sems.at[i]).wait()

    return pl.pallas_call(
        body,
        grid_spec=pltpu.PrefetchScalarGridSpec(
            num_scalar_prefetch=2,
            grid=(1,),
            in_specs=[pl.BlockSpec(memory_space=pl.ANY)] * len(sources),
            out_specs=[pl.BlockSpec(memory_space=pl.ANY)] * parts,
            scratch_shapes=[
                pltpu.VMEM((amount,) + shape, low),
                pltpu.SemaphoreType.DMA((amount,)),
                pltpu.SemaphoreType.DMA((amount,)),
            ],
        ),
        out_shape=[jax.ShapeDtypeStruct((size,) + shape, low)] * parts,
        compiler_params=pltpu.CompilerParams(vmem_limit_bytes=56 * 2**20),
        cost_estimate=cheap,
        name="place_blocks",
    )(which, position, *sources)


def hops(values, step, turn):
    count = lax.axis_size("tensor")
    if step > 0:
        pairs = [(i, i + 1) for i in range(turn - 1, count - 1)]
    else:
        pairs = [(i, i - 1) for i in range(1, count - turn + 1)]
    return lax.ppermute(values, "tensor", pairs)


def slots_of(own, ups, downs):
    count = lax.axis_size("tensor")
    me = lax.axis_index("tensor")
    return [own] + [jnp.where(me >= k, ups[k - 1], downs[count - k - 1]) for k in range(1, count)]


fence = lax.optimization_barrier


def in_pool(member, inner, inner_count):
    me = lax.axis_index("dp")
    half, core = member >> 3, ((member >> 2) & 1) ^ (me & 1)
    far_y, far_x = ((member >> 1) & 1) ^ ((me >> 2) & 1), (member & 1) ^ ((me >> 1) & 1)
    where_first = (far_y * 2 + far_x) * inner_count
    where_second = (4 + far_x * 2 + far_y) * inner_count
    return (core, jnp.where(half == 0, where_first, where_second) + inner)


def on_device(
    hidden_in,
    time_embed,
    caption_table,
    caption_ids,
    owners,
    master,
    first_moment,
    second_moment,
    mod_table,
    mod_first,
    mod_second,
    out_grad,
):
    count = lax.axis_size("tensor")
    dp_count = lax.axis_size("dp")
    me_dp = lax.axis_index("dp")
    me_tensor = lax.axis_index("tensor")
    capacity, unit_rows, width = master.shape
    units = owners.shape[0]
    tokens = hidden_in.shape[1]
    text_count = caption_ids.shape[1]
    share = width // count
    per = share // unit_rows
    ups = (units - 8 * per) // 2
    rank_of = ranks_of(owners)
    mine = owners == me_dp
    match = (rank_of[None, :] == jnp.arange(capacity)[:, None]) & mine[None, :]
    filled = jnp.any(match, axis=1)
    unit_of_slot = jnp.sum(jnp.where(match, jnp.arange(units)[None, :], 0), axis=1)

    square = [list(range(i * per, (i + 1) * per)) for i in range(8)]
    group_attn = square[0] + square[1] + square[2] + square[5]
    group_full = square[3] + square[4] + square[6] + square[7]
    group_mlp = list(range(8 * per, units))
    members = len(group_attn)
    plane = dp_count == 8 and members == 16 and len(group_mlp) % dp_count == 0
    member_of = np.zeros(units, np.int32)
    member_of[group_attn] = np.arange(members)
    member_of[group_full] = np.arange(members)
    is_attn = np.zeros(units, bool)
    is_attn[group_attn] = True
    is_mlp = np.zeros(units, bool)
    is_mlp[group_mlp] = True

    latent_in = hidden_in[0].astype(jnp.float32)
    upstream = out_grad[0].astype(jnp.float32)
    modulate = mod_table + time_embed[0]

    def mod_row(which_row):
        return modulate[which_row][None, :]

    normed_one, inverse_one = layer_norm(latent_in)
    bits = dp_count.bit_length() - 1
    vocab_rows = caption_table.shape[0]

    def caption_terms(ids):
        chosen = ids.reshape(-1) - me_dp * vocab_rows
        onehot = (chosen[:, None] == jnp.arange(vocab_rows)[None, :]).astype(low)
        terms = jnp.dot(onehot, caption_table, preferred_element_type=jnp.float32).astype(low)
        return terms.reshape(dp_count, text_count, -1)

    n_low = normed_one.astype(low)
    if plane:
        core, far_x, far_y = (
            ((member_of >> 2) & 1) ^ (me_dp & 1),
            (member_of & 1) ^ ((me_dp >> 1) & 1),
            ((member_of >> 1) & 1) ^ ((me_dp >> 2) & 1),
        )
        place = jnp.where(is_attn, far_x * 4 + far_y * 2, 8 + far_y * 4 + far_x * 2)
        place = jnp.where(is_mlp, np.arange(units) - 8 * per, place + (member_of >> 3))
        kind = jnp.where(is_mlp, 0, core)
        slot_mlp = unit_of_slot >= 8 * per
        owned_state = mine.astype(jnp.int32)
        up, down = hops(n_low, 1, 1), hops(n_low, -1, 1)
        kept, given = pick_units(
            master,
            jnp.where(filled & ~slot_mlp, unit_of_slot, -1),
            jnp.where(is_mlp, 2, owned_state),
            kind,
            place,
            (members, members),
        )
        got = swap(given, "dp", 0)
        ids = jnp.concatenate([caption_ids, swap(caption_ids, "dp", 0)])
        n_up, n_down = [up], [down]
        kept, got, up, down, ids = fence((kept, got, up, down, ids))
        pieces = [kept[i : i + 4] + got[i : i + 4] for i in range(0, members, 4)]
        attn_two, attn_send, full_two, full_send = fence(tuple(pieces))
        up, down = hops(up, 1, 2), hops(down, -1, 2)
        attn_got = swap(attn_send, "dp", 1)
        full_got = swap(full_send, "dp", 2)
        ids = jnp.concatenate([ids, swap(ids, "dp", 1)])
        (mlp_part,) = pick_units(
            fence((master, got))[0],
            jnp.where(filled & slot_mlp, unit_of_slot, -1),
            jnp.where(is_mlp, owned_state, 2),
            kind,
            place,
            (len(group_mlp),),
        )
        n_up.append(up), n_down.append(down)
        attn_two, attn_got, full_two, full_got, up, down, ids, mlp_part = fence(
            (attn_two, attn_got, full_two, full_got, up, down, ids, mlp_part)
        )
        pieces = [x[i : i + 2] + y[i : i + 2] for x, y in ((attn_two, attn_got), (full_two, full_got)) for i in (0, 2)]
        attn_one, attn_send, full_one, full_send = fence(tuple(pieces))
        up, down = hops(up, 1, 3), hops(down, -1, 3)
        attn_got = swap(attn_send, "dp", 2)
        full_got = swap(full_send, "dp", 1)
        ids = jnp.concatenate([ids, swap(ids, "dp", 2)])
        n_up.append(up), n_down.append(down)
        attn_one, attn_got, full_one, full_got, up, down, ids, mlp_part = fence(
            (attn_one, attn_got, full_one, full_got, up, down, ids, mlp_part)
        )
        attn_one, full_one = attn_one + attn_got, full_one + full_got
        grad_whole = lax.all_gather(fence((out_grad[0], up))[0], "tensor", axis=0)
        mlp_part = lax.psum_scatter(mlp_part, "dp", scatter_dimension=0, tiled=True)
        first = jnp.concatenate([attn_one[0:1], swap(attn_one[0:1], "dp", 1)])
        second = jnp.concatenate([attn_one[1:2], swap(attn_one[1:2], "dp", 2)])
        up, down = hops(full_one, 1, 1), hops(full_one, -1, 1)
        text = caption_terms(ids)
        text = text[0:4] + swap(text[4:8], "dp", 2)
        f_up, f_down = [up], [down]
        first, second, up, down, text = fence((first, second, up, down, text))
        pool = jnp.concatenate([first, swap(first, "dp", 2), second, swap(second, "dp", 1)])
        up, down = hops(up, 1, 2), hops(down, -1, 2)
        text = text[0:2] + swap(text[2:4], "dp", 1)
        f_up.append(up), f_down.append(down)
        pool, up, down, text = fence((pool, up, down, text))
        other = swap(pool, "dp", 0)
        up, down = hops(up, 1, 3), hops(down, -1, 3)
        text = text[0] + swap(text[1], "dp", 0)
        f_up.append(up), f_down.append(down)
        pool, other, up, down, text = fence((pool, other, up, down, text))
        (w_attn,) = place_blocks((pool, other), *in_pool(np.arange(members), 0, 1))
        full_ring = slots_of(full_one, f_up, f_down)
        first = jnp.concatenate([item[0:1] for item in full_ring])
        second = jnp.concatenate([item[1:2] for item in full_ring])
        first_got = swap(first, "dp", 1)
        second_got = swap(second, "dp", 2)
        text_ring = jnp.stack(ring(text))
        first = jnp.concatenate([first, first_got])
        second = jnp.concatenate([second, second_got])
        first, second, text_ring = fence((first, second, text_ring))
        first_far, second_far = swap(first, "dp", 2), swap(second, "dp", 1)
        first_other, second_other = swap(first, "dp", 0), swap(second, "dp", 0)
        first_far, second_far, first_other, second_other = fence(
            (first_far, second_far, first_other, second_other)
        )
        first_last, second_last = swap(first_far, "dp", 0), swap(second_far, "dp", 0)
        mlp_part = fence((mlp_part, first_far))[0]
        w_mlp = lax.all_gather(mlp_part, "dp", axis=0, tiled=True)
        listing = np.arange(count * members)
        matrix, rank, head = listing // (count * per), listing // per % count, listing % per
        slot = lax.rem(me_tensor - rank + count, count)
        which, position = in_pool(matrix * per + head, slot, count)
        blocks = 2 * count
        w_full = place_blocks(
            (first, first_far, second, second_far, first_other, first_last, second_other, second_last),
            which * 4 + position // blocks,
            position % blocks,
            parts=4,
        )
        w_full = [part.reshape(width, width) for part in w_full]
        normed_all = jnp.concatenate(slots_of(n_low, n_up, n_down))
    else:
        slots_low = master.astype(low)
        rows = jnp.take(slots_low, rank_of, axis=0, mode="clip")
        rows = lax.psum(jnp.where(mine[:, None, None], rows, jnp.zeros((), low)), "dp")
        w_attn = rows[np.array(group_attn)]
        w_full = lax.all_gather(rows[np.array(group_full)], "tensor", axis=0)
        w_full = w_full.reshape(count, 4, share, width).swapaxes(0, 1).reshape(4, width, width)
        w_full = [w_full[i] for i in range(4)]
        w_mlp = rows[8 * per :]
        normed_all = jnp.concatenate(ring(n_low))
        grad_whole = lax.all_gather(out_grad[0], "tensor", axis=0)
        ids = caption_ids
        for bit in range(bits):
            ids = jnp.concatenate([ids, swap(ids, "dp", bit)])
        text = caption_terms(ids)
        for bit in reversed(range(bits)):
            text = text[: 1 << bit] + swap(text[1 << bit :], "dp", bit)
        text_ring = jnp.stack(ring(text[0]))
    h_one_all = (normed_all.astype(jnp.float32) * (1.0 + mod_row(1)) + mod_row(0)).astype(low)
    w_attn = w_attn.reshape(-1, width)
    w_qkv, c_key = w_attn[: 3 * share], w_attn[3 * share :]
    w_out, c_query, c_value, c_out = w_full
    w_mlp = w_mlp.reshape(-1, width)
    w_down = w_mlp[w_mlp.shape[0] // 2 :]
    text_low = from_ring(text_ring, -1).transpose(1, 0, 2).reshape(text_count, width)

    qkv = project(h_one_all, w_qkv).astype(low)
    attended = self_attend(qkv)
    mixed_parts = attended.reshape(count, tokens, share)
    mixed_ring = jnp.stack(
        [mixed_parts[0]] + [shift(mixed_parts[k], count - k) for k in range(1, count)]
    )
    mixed_own = from_ring(mixed_ring, 1).transpose(1, 0, 2).reshape(tokens, width)
    branch_one = expand(mixed_own, w_out)
    first_res = latent_in + mod_row(2) * branch_one
    first_low = first_res.astype(low)

    ck_ring = from_ring(jnp.stack(ring(project(text_low, c_key).astype(low))), -1)
    ck_rows = ck_ring.transpose(1, 0, 2).reshape(text_count, width)
    cv_rows = project(text_low, c_value).astype(low)
    cq_rows = project(first_low, c_query).astype(low)
    crossed, logsum_two = attend(cq_rows, ck_rows, cv_rows)
    second_res = first_res + expand(crossed, c_out)
    normed_two, inverse_two = layer_norm(second_res)
    h_two = (normed_two * (1.0 + mod_row(4)) + mod_row(3)).astype(low)

    h_slots = ring(h_two)
    out_slots = [
        choose(grad_whole, lax.rem(me_tensor - k + count, count), 0) for k in range(count)
    ]
    grad_slots = [(mod_row(5) * item.astype(jnp.float32)).astype(low) for item in out_slots]
    early = [k for k in range(count) if k == 0 or k != count // 2]
    late = [k for k in range(count) if k not in early]
    act, grad_pre, *terms = mlp_core(
        [h_slots[k] for k in early], [grad_slots[k] for k in early], w_mlp
    )
    grad_terms = dict(zip(early, terms))
    acts, grad_pres = [act], [grad_pre]
    grad_h_two = grad_terms[0].astype(jnp.float32)
    sent = {k: shift(grad_terms[k], count - k) for k in early[1:]}
    held = fence((*[h_slots[k] for k in late], act))
    act, grad_pre, *terms = mlp_core(held[:-1], [grad_slots[k] for k in late], w_mlp)
    grad_terms = dict(zip(late, terms))
    acts.append(act), grad_pres.append(grad_pre)
    sent.update({k: shift(grad_terms[k], count - k) for k in late})
    for k in range(1, count):
        grad_h_two = grad_h_two + sent[k].astype(jnp.float32)
    act_low = jnp.concatenate(acts)
    grad_pre = jnp.concatenate(grad_pres)
    order = early + late
    h_two_all = jnp.concatenate([h_slots[k] for k in order])
    grad_mlp_all = jnp.concatenate([grad_slots[k] for k in order])
    grad_up = outer(grad_pre, h_two_all).astype(low)
    grad_down = outer(act_low, grad_mlp_all).astype(low)
    mlp_grad = jnp.concatenate([grad_up, grad_down]).reshape(-1, unit_rows, width)
    branch_terms = expand(act_low, w_down)
    out_all = jnp.concatenate([out_slots[k] for k in order])
    branch_row = jnp.sum(branch_terms * out_all.astype(jnp.float32), axis=0)
    branch_terms = branch_terms.astype(low).reshape(count, tokens, width)
    back = np.argsort(order)
    branch_terms = jnp.take(
        branch_terms,
        jnp.array(back)[lax.rem(me_tensor - jnp.arange(count) + count, count)],
        axis=0,
        mode="clip",
    ).reshape(-1, width)
    if plane:
        mlp_sum = lax.psum_scatter(mlp_grad, "dp", scatter_dimension=0, tiled=True)
        branch_terms = fence((branch_terms, grad_h_two))[0]
    branch_two = lax.psum_scatter(branch_terms, "tensor", scatter_dimension=0, tiled=True)
    second_grad = upstream + norm_back(grad_h_two, normed_two, inverse_two, mod_row(4))

    cross_grad = second_grad.astype(low)
    grad_c_out = outer(crossed, cross_grad)
    grad_crossed = project(cross_grad, c_out).astype(low)
    grad_cq, grad_ck, grad_cv = attend_back(cq_rows, ck_rows, cv_rows, grad_crossed, logsum_two)
    grad_cq = grad_cq.astype(low)
    first_grad = second_grad + expand(grad_cq, c_query)
    attn_grad = (mod_row(2) * first_grad).astype(low)
    grad_mixed = project(attn_grad, w_out).astype(low)
    grad_mixed = to_ring(grad_mixed.reshape(tokens, count, share).transpose(1, 0, 2))
    grad_parts = [grad_mixed[0]] + [shift(grad_mixed[k], k) for k in range(1, count)]
    grad_c_value = outer(grad_cv.astype(low), text_low).astype(low)
    grad_c_out = outer(crossed, cross_grad).astype(low)
    grad_c_query = outer(grad_cq, first_low).astype(low)
    grad_w_out = outer(mixed_own, attn_grad).astype(low)
    grad_ck_parts = to_ring(grad_ck.reshape(text_count, count, share).transpose(1, 0, 2)).astype(low)

    def sum_ck(parts):
        total = grad_ck_parts[0].astype(jnp.float32)
        for k in range(1, count):
            total = total + parts[k - 1].astype(jnp.float32)
        return total.astype(low)

    def scattered(terms):
        total = terms[0].astype(jnp.float32)
        for k in range(1, count):
            total = total + shift(terms[k], count - k).astype(jnp.float32)
        return total

    normed_wide = normed_all.astype(jnp.float32)

    def summed(values):
        return jnp.sum(values, axis=0)

    if plane:
        even = (me_dp & 1) == 0
        x_bit, y_bit = (me_dp >> 1) & 1, (me_dp >> 2) & 1

        def core_halves(one, two):
            return (jnp.where(even, one, two), jnp.where(even, two, one))

        def split(total, bit, axis):
            return (choose(total, bit, axis), choose(total, 1 - bit, axis))

        kept_two, given_two = core_halves(grad_c_value, grad_c_out)
        got_two = swap(given_two, "dp", 0)
        kept_one, given_one = core_halves(grad_w_out, grad_c_query)
        got_one = swap(given_one, "dp", 0)
        grad_parts, kept_one, kept_two, got_one, got_two = fence(
            (grad_parts, kept_one, kept_two, got_one, got_two)
        )
        box = (count, 2, 2, unit_rows, width)
        kept_one, given_one = split((kept_one + got_one).reshape(box), x_bit, 2)
        kept_two, given_two = split((kept_two + got_two).reshape(box), y_bit, 1)
        kept_one, given_one, kept_two, given_two, grad_parts = fence(
            (kept_one, given_one, kept_two, given_two, grad_parts)
        )
        got_one, got_two = swap(given_one, "dp", 1), swap(given_two, "dp", 2)
        ck_parts = [shift(grad_ck_parts[k], k) for k in range(1, count)]
        grad_qkv = self_attend_back(qkv, jnp.concatenate(grad_parts, axis=0))
        kept_one, got_one, kept_two, got_two, ck_parts, grad_qkv, mlp_sum = fence(
            (kept_one, got_one, kept_two, got_two, ck_parts, grad_qkv, mlp_sum)
        )
        mlp_sum = lax.all_gather(mlp_sum, "dp", axis=0, tiled=True)
        kept_one, given_one = split(kept_one + got_one, y_bit, 1)
        kept_two, given_two = split(kept_two + got_two, x_bit, 1)
        got_one, got_two = swap(given_one, "dp", 2), swap(given_two, "dp", 1)
        grad_q, grad_k, grad_v = (
            outer(grad_qkv[:, i * share : (i + 1) * share], h_one_all).astype(low)
            for i in range(3)
        )
        grad_c_key = outer(sum_ck(ck_parts), text_low).astype(low)
        attn_kept, attn_given = core_halves(
            jnp.stack([grad_q, grad_v]), jnp.stack([grad_k, grad_c_key])
        )
        attn_got = swap(attn_given, "dp", 0)
        grad_h_terms = expand(grad_qkv, w_qkv)
        kept_one, got_one, kept_two, got_two, attn_kept, attn_got, grad_h_terms = fence(
            (kept_one, got_one, kept_two, got_two, attn_kept, attn_got, grad_h_terms)
        )
        full_parts = jnp.stack([kept_one + got_one, kept_two + got_two], axis=1)
        full_parts = to_ring(full_parts)
        full_got = [shift(full_parts[k], k) for k in range(1, count)]
        attn_all = (attn_kept + attn_got).reshape(2, 2, 2, unit_rows, width)
        one_kept, one_given = split(attn_all[0], x_bit, 1)
        two_kept, two_given = split(attn_all[1], y_bit, 0)
        one_got, two_got = swap(one_given, "dp", 1), swap(two_given, "dp", 2)
        mod_terms = jnp.stack(
            [
                summed(grad_h_terms),
                summed(grad_h_terms * normed_wide),
                summed(branch_one * first_grad),
                summed(grad_h_two),
                summed(grad_h_two * normed_two),
                branch_row,
            ]
        )
        full_own = full_parts[0]
        full_own, full_got, one_kept, one_got, two_kept, two_got, mod_terms = fence(
            (full_own, full_got, one_kept, one_got, two_kept, two_got, mod_terms)
        )
        full_sum = full_own.astype(jnp.float32)
        for part in full_got:
            full_sum = full_sum + part.astype(jnp.float32)
        full_sum = full_sum.astype(low)
        one_kept, one_given = split(one_kept + one_got, y_bit, 0)
        two_kept, two_given = split(two_kept + two_got, x_bit, 0)
        one_got, two_got = swap(one_given, "dp", 2), swap(two_given, "dp", 1)
        mod_terms = mod_terms + swap(mod_terms, "dp", 0)
        one_kept, one_got, two_kept, two_got, mod_terms, full_sum = fence(
            (one_kept, one_got, two_kept, two_got, mod_terms, full_sum)
        )
        grad_h_terms = fence((grad_h_terms, one_got))[0]
        grad_h_one = scattered(grad_h_terms.astype(low).reshape(count, tokens, width))
        first = jnp.stack([one_kept + one_got, full_sum[0]])
        second = jnp.stack([two_kept + two_got, full_sum[1]])
        first_got, second_got = swap(first, "dp", 1), swap(second, "dp", 2)
        first = jnp.concatenate([first, first_got])
        second = jnp.concatenate([second, second_got])
        mod_terms = mod_terms + swap(mod_terms, "dp", 1)
        first, second, mod_terms = fence((first, second, mod_terms))
        first_far, second_far = swap(first, "dp", 2), swap(second, "dp", 1)
        mod_terms = mod_terms + swap(mod_terms, "dp", 2)
        first, first_far, second, second_far, mod_terms = fence(
            (first, first_far, second, second_far, mod_terms)
        )
        pool = jnp.concatenate([first, first_far, second, second_far])
        other = swap(pool, "dp", 0)
        for bit in range(count.bit_length() - 1):
            mod_terms = mod_terms + swap(mod_terms, "tensor", bit)
        mod_grad = mod_terms
        which, position = in_pool(member_of, np.where(is_attn, 0, 1), 2)
        which = jnp.where(is_mlp, 2, which)
        position = jnp.where(is_mlp, np.arange(units) - 8 * per, position)
        own = jnp.sum(jnp.where(match[:, :, None], jnp.stack([which, position], 1)[None], 0), axis=1)
        new_first, new_second, new_master = update_slots(
            master,
            first_moment,
            second_moment,
            filled.astype(jnp.int32),
            own[:, 0],
            own[:, 1],
            (pool, other, mlp_sum),
        )
    else:
        grad_qkv = self_attend_back(qkv, jnp.concatenate(grad_parts, axis=0))
        grad_c_key = sum_ck([shift(grad_ck_parts[k], k) for k in range(1, count)])
        grad_c_key = outer(grad_c_key, text_low).astype(low)
        attn_grads = [outer(grad_qkv, h_one_all).astype(low), grad_c_key]
        grad_h_terms = expand(grad_qkv, w_qkv)
        grad_h_one = scattered(grad_h_terms.astype(low).reshape(count, tokens, width))
        full_grads = (grad_w_out, grad_c_query, grad_c_value, grad_c_out)
        full_sum = jnp.stack([g.reshape(count, share, width) for g in full_grads], axis=1)
        full_sum = lax.psum_scatter(full_sum, "tensor", scatter_dimension=0, tiled=True)
        order = np.array(group_attn + group_full + group_mlp)
        sums = jnp.concatenate(
            [jnp.concatenate(attn_grads), full_sum.reshape(-1, width), mlp_grad.reshape(-1, width)]
        )
        sums = lax.psum(sums.reshape(units, unit_rows, width), "dp")
        owned = jnp.take(sums, jnp.array(np.argsort(order))[unit_of_slot], axis=0, mode="clip")
        mod_grad = total_sum(
            jnp.stack(
                [
                    summed(grad_h_terms),
                    summed(grad_h_terms * normed_wide),
                    summed(branch_one * first_grad),
                    summed(grad_h_two),
                    summed(grad_h_two * normed_two),
                    branch_row,
                ]
            )
        )
        new_first, new_second, new_master = adamw(
            master,
            first_moment,
            second_moment,
            owned.astype(jnp.float32),
            filled.astype(jnp.float32)[:, None, None],
            rate,
        )
    branch_two, second_res, grad_h_one = fence((branch_two, second_res, grad_h_one))
    block_out = second_res + mod_row(5) * branch_two.astype(jnp.float32)
    input_grad = first_grad + norm_back(grad_h_one, normed_one, inverse_one, mod_row(1))
    mod_new_first, mod_new_second, mod_new = adamw(
        mod_table, mod_first, mod_second, mod_grad, 1.0, table_rate
    )
    return (
        block_out[None],
        input_grad[None],
        new_first,
        new_second,
        new_master,
        mod_new_first,
        mod_new_second,
        mod_new,
    )


def solution(mesh):
    in_specs = (
        P("dp", "tensor", None),
        P("dp", None, None),
        P("dp", "tensor"),
        P("dp", None),
        P(),
        P("dp", "tensor", None),
        P("dp", "tensor", None),
        P("dp", "tensor", None),
        P(),
        P(),
        P(),
        P("dp", "tensor", None),
    )
    out_specs = (
        P("dp", "tensor", None),
        P("dp", "tensor", None),
        P("dp", "tensor", None),
        P("dp", "tensor", None),
        P("dp", "tensor", None),
        P(),
        P(),
        P(),
    )
    return jax.shard_map(
        on_device, mesh=mesh, in_specs=in_specs, out_specs=out_specs, check_vma=False
    )
```

```python
import math

import jax
import jax.numpy as jnp
import numpy as np
from jax import lax
from jax.experimental import pallas as pl
from jax.experimental.pallas import tpu as pltpu
from jax.sharding import PartitionSpec as P

HEAD_DIM = 72
STEP = 10


norm_eps = 1e-06
beta_one = 0.9
beta_two = 0.999
rate = 0.03
table_rate = 0.3
decay = 0.01
adam_eps = 1e-08
low = jnp.bfloat16


def ranks_of(owners):
    index = jnp.arange(owners.shape[0])
    before = (owners[None, :] == owners[:, None]) & (index[None, :] < index[:, None])
    return jnp.sum(before.astype(jnp.int32), axis=1)


def layer_norm(values):
    center = values - jnp.mean(values, axis=-1, keepdims=True)
    inverse = lax.rsqrt(jnp.mean(center * center, axis=-1, keepdims=True) + norm_eps)
    return (center * inverse, inverse)


def norm_back(grad_rows, normed, inverse, scale_row):
    scaled = grad_rows * (1.0 + scale_row)
    mean_one = jnp.mean(scaled, axis=-1, keepdims=True)
    mean_two = jnp.mean(scaled * normed, axis=-1, keepdims=True)
    return inverse * (scaled - mean_one - normed * mean_two)


def project(rows, weight):
    return jnp.einsum("ld,rd->lr", rows, weight, preferred_element_type=jnp.float32)


def expand(rows, weight):
    return jnp.einsum("lr,rd->ld", rows, weight, preferred_element_type=jnp.float32)


def outer(left, right):
    return jnp.einsum("lr,ld->rd", left, right, preferred_element_type=jnp.float32)


def shift(values, step):
    count = lax.axis_size("tensor")
    return lax.ppermute(values, "tensor", [(i, (i + step) % count) for i in range(count)])


def ring(values):
    return [values] + [shift(values, k) for k in range(1, lax.axis_size("tensor"))]


def to_ring(stacked):
    count = stacked.shape[0]
    twice = jnp.concatenate([stacked, stacked], axis=0)
    return lax.dynamic_slice_in_dim(twice, lax.axis_index("tensor"), count, 0)


def from_ring(stacked, sign):
    count = stacked.shape[0]
    me = lax.axis_index("tensor")
    place = lax.rem(sign * (jnp.arange(count) - me) + 2 * count, count)
    return jnp.take(stacked, place, axis=0, mode="clip")


def heads_of(rows):
    return rows.reshape(rows.shape[0], -1, HEAD_DIM)


cheap = pl.CostEstimate(flops=1000, bytes_accessed=1000, transcendentals=0)


def self_attend(qkv):
    length, width_all = qkv.shape
    share = width_all // 3
    heads = share // HEAD_DIM
    rows = min(256, length)
    scale = HEAD_DIM ** (-0.5)

    def body(qkv_ref, out_ref):
        @pl.loop(0, length // rows)
        def _(step):
            here = pl.ds(pl.multiple_of(step * rows, rows), rows)
            parts = []
            for head in range(heads):
                at = head * HEAD_DIM
                q = qkv_ref[here, at : at + HEAD_DIM]
                k = qkv_ref[:, share + at : share + at + HEAD_DIM]
                v = qkv_ref[:, 2 * share + at : 2 * share + at + HEAD_DIM]
                scores = scale * lax.dot_general(
                    k, q, (((1,), (1,)), ((), ())), preferred_element_type=jnp.float32
                )
                expo = jnp.exp(scores - jnp.max(scores, axis=0, keepdims=True))
                inverse = 1.0 / jnp.sum(expo, axis=0, keepdims=True)
                probs = (expo * inverse).astype(low)
                mixed = lax.dot_general(
                    v, probs, (((0,), (0,)), ((), ())), preferred_element_type=jnp.float32
                )
                parts.append(mixed.T)
            out_ref[here, :] = jnp.concatenate(parts, axis=1).astype(low)

    return pl.pallas_call(
        body,
        out_shape=jax.ShapeDtypeStruct((length, share), low),
        compiler_params=pltpu.CompilerParams(vmem_limit_bytes=32 * 2**20),
        cost_estimate=cheap,
        name="self_attend",
    )(qkv)


def self_attend_back(qkv, grad_mixed):
    length, width_all = qkv.shape
    share = width_all // 3
    heads = share // HEAD_DIM
    rows = min(256, length)
    steps = length // rows
    scale = HEAD_DIM ** (-0.5)

    def body(qkv_ref, grad_ref, out_ref, grad_k, grad_v):
        grad_k[...] = jnp.zeros_like(grad_k)
        grad_v[...] = jnp.zeros_like(grad_v)

        @pl.loop(0, steps)
        def _(step):
            here = pl.ds(pl.multiple_of(step * rows, rows), rows)
            parts = []
            for head in range(heads):
                at = head * HEAD_DIM
                q = qkv_ref[here, at : at + HEAD_DIM]
                k = qkv_ref[:, share + at : share + at + HEAD_DIM]
                v = qkv_ref[:, 2 * share + at : 2 * share + at + HEAD_DIM]
                g = grad_ref[here, at : at + HEAD_DIM]
                scores = scale * lax.dot_general(
                    k, q, (((1,), (1,)), ((), ())), preferred_element_type=jnp.float32
                )
                expo = jnp.exp(scores - jnp.max(scores, axis=0, keepdims=True))
                probs = expo * (1.0 / jnp.sum(expo, axis=0, keepdims=True))
                grad_probs = lax.dot_general(
                    v, g, (((1,), (1,)), ((), ())), preferred_element_type=jnp.float32
                )
                inner = jnp.sum(probs * grad_probs, axis=0, keepdims=True)
                grad_scores = (probs * (grad_probs - inner)).astype(low)
                grad_v[head] += jnp.dot(
                    probs.astype(low), g, preferred_element_type=jnp.float32
                )
                grad_k[head] += jnp.dot(grad_scores, q, preferred_element_type=jnp.float32)
                grad_q = lax.dot_general(
                    k, grad_scores, (((0,), (0,)), ((), ())), preferred_element_type=jnp.float32
                )
                parts.append(grad_q.T * scale)
            out_ref[here, :share] = jnp.concatenate(parts, axis=1).astype(low)

        both = [grad_k[head] * scale for head in range(heads)]
        out_ref[:, share : 2 * share] = jnp.concatenate(both, axis=1).astype(low)
        both = [grad_v[head] for head in range(heads)]
        out_ref[:, 2 * share :] = jnp.concatenate(both, axis=1).astype(low)

    return pl.pallas_call(
        body,
        out_shape=jax.ShapeDtypeStruct((length, width_all), low),
        scratch_shapes=[pltpu.VMEM((heads, length, HEAD_DIM), jnp.float32)] * 2,
        compiler_params=pltpu.CompilerParams(vmem_limit_bytes=40 * 2**20),
        cost_estimate=cheap,
        name="self_attend_back",
    )(qkv, grad_mixed)


def mlp_core(rows_in, grads_in, w_mlp):
    groups = len(rows_in)
    tokens, width = rows_in[0].shape
    hidden = w_mlp.shape[0] // 2
    chunk = 384 if hidden % 384 == 0 else hidden
    steps = hidden // chunk
    curve = 0.7978845608028654

    def body(*refs):
        rows, grads = refs[:groups], refs[groups : 2 * groups]
        up, down = refs[2 * groups : 2 * groups + 2]
        act, grad_pre = refs[2 * groups + 2 : 2 * groups + 4]
        outs = refs[2 * groups + 4 : 3 * groups + 4]
        total = refs[-1]
        step = pl.program_id(0)
        for i in range(groups):
            pre = lax.dot_general(
                rows[i][...], up[...], (((1,), (1,)), ((), ())), preferred_element_type=jnp.float32
            )
            square = pre * pre
            bend = jnp.tanh(curve * pre * (1.0 + 0.044715 * square))
            half = 0.5 * (1.0 + bend)
            here = pl.ds(i * tokens, tokens)
            act[here, :] = (pre * half).astype(low)
            slope = half + (0.5 * curve) * pre * (1.0 - bend * bend) * (1.0 + 0.134145 * square)
            grad_act = lax.dot_general(
                grads[i][...], down[...], (((1,), (1,)), ((), ())), preferred_element_type=jnp.float32
            )
            grad_low = (grad_act * slope).astype(low)
            grad_pre[here, :] = grad_low
            term = jnp.dot(grad_low, up[...], preferred_element_type=jnp.float32)

            @pl.when(step == 0)
            def _():
                total[here, :] = term

            @pl.when(step > 0)
            def _():
                total[here, :] += term

            @pl.when(step == steps - 1)
            def _():
                outs[i][...] = total[here, :].astype(low)

    whole = pl.BlockSpec((tokens, width), lambda s: (0, 0))
    across = pl.BlockSpec((groups * tokens, chunk), lambda s: (0, s))
    return pl.pallas_call(
        body,
        grid=(steps,),
        in_specs=[whole] * (2 * groups)
        + [
            pl.BlockSpec((chunk, width), lambda s: (s, 0)),
            pl.BlockSpec((chunk, width), lambda s: (steps + s, 0)),
        ],
        out_specs=[across, across] + [whole] * groups,
        out_shape=[jax.ShapeDtypeStruct((groups * tokens, hidden), low)] * 2
        + [jax.ShapeDtypeStruct((tokens, width), low)] * groups,
        scratch_shapes=[pltpu.VMEM((groups * tokens, width), jnp.float32)],
        compiler_params=pltpu.CompilerParams(vmem_limit_bytes=40 * 2**20),
        cost_estimate=cheap,
        name="mlp_core",
    )(*rows_in, *grads_in, w_mlp, w_mlp)


def update_slots(master, first_moment, second_moment, filled, which, position, sources):
    capacity, unit_rows, width = master.shape

    group = math.gcd(capacity, 2)
    steps = capacity // group

    def body(filled_ref, which_ref, position_ref, weight, one, two, *rest):
        ins = rest[: len(sources)]
        new_one, new_two, new_weight, held, sems = rest[len(sources) :]
        step = pl.program_id(0)

        def fetch(turn):
            for i in range(group):
                slot = turn * group + i
                for source, ref in enumerate(ins):

                    @pl.when(which_ref[slot] == source)
                    def _():
                        pltpu.make_async_copy(
                            ref.at[position_ref[slot]], held.at[turn % 2, i], sems.at[turn % 2, i]
                        ).start()

        @pl.when(step == 0)
        def _():
            fetch(step)

        @pl.when(step < steps - 1)
        def _():
            fetch(step + 1)

        for i in range(group):
            pltpu.make_async_copy(
                ins[0].at[0], held.at[step % 2, i], sems.at[step % 2, i]
            ).wait()
            mask = (filled_ref[step * group + i] > 0).astype(jnp.float32)
            grad = held[step % 2, i].astype(jnp.float32)
            results = adamw(weight[i], one[i], two[i], grad, mask, rate)
            new_one[i], new_two[i], new_weight[i] = results

    block = pl.BlockSpec((group, unit_rows, width), lambda s, *_: (s, 0, 0))
    return pl.pallas_call(
        body,
        grid_spec=pltpu.PrefetchScalarGridSpec(
            num_scalar_prefetch=3,
            grid=(steps,),
            in_specs=[block] * 3 + [pl.BlockSpec(memory_space=pl.ANY)] * len(sources),
            out_specs=[block] * 3,
            scratch_shapes=[
                pltpu.VMEM((2, group, unit_rows, width), low),
                pltpu.SemaphoreType.DMA((2, group)),
            ],
        ),
        out_shape=[jax.ShapeDtypeStruct(master.shape, jnp.float32)] * 3,
        compiler_params=pltpu.CompilerParams(vmem_limit_bytes=56 * 2**20),
        cost_estimate=cheap,
        name="update_slots",
    )(filled, which, position, master, first_moment, second_moment, *sources)


def attend(q_rows, k_rows, v_rows):
    length, width_all = q_rows.shape
    heads = width_all // HEAD_DIM
    block_rows = min(512, length)
    blocks = length // block_rows
    scale = HEAD_DIM ** (-0.5)
    k_heads = heads_of(k_rows)
    v_heads = heads_of(v_rows)

    def one_block(q_block):
        scores = (
            jnp.einsum("qhd,khd->hqk", q_block, k_heads, preferred_element_type=jnp.float32)
            * scale
        )
        top = jnp.max(scores, axis=-1, keepdims=True)
        expo = jnp.exp(scores - top)
        total = jnp.sum(expo, axis=-1, keepdims=True)
        probs = (expo / total).astype(low)
        mixed = jnp.einsum("hqk,khd->qhd", probs, v_heads, preferred_element_type=jnp.float32)
        return (mixed.astype(low), (top + jnp.log(total))[..., 0])

    mixed, logsum = lax.map(one_block, q_rows.reshape(blocks, block_rows, heads, HEAD_DIM))
    return (mixed.reshape(length, width_all), logsum)


def attend_back(q_rows, k_rows, v_rows, grad_mixed, logsum):
    length, width_all = q_rows.shape
    heads = width_all // HEAD_DIM
    block_rows = min(512, length)
    blocks = length // block_rows
    scale = HEAD_DIM ** (-0.5)
    k_heads = heads_of(k_rows)
    v_heads = heads_of(v_rows)

    def one_block(carry, block_item):
        q_block, g_block, l_block = block_item
        scores = (
            jnp.einsum("qhd,khd->hqk", q_block, k_heads, preferred_element_type=jnp.float32)
            * scale
        )
        probs = jnp.exp(scores - l_block[..., None])
        grad_probs = jnp.einsum(
            "qhd,khd->hqk", g_block, v_heads, preferred_element_type=jnp.float32
        )
        inner = jnp.sum(probs * grad_probs, axis=-1, keepdims=True)
        grad_scores = (probs * (grad_probs - inner)).astype(low)
        grad_q = (
            jnp.einsum("hqk,khd->qhd", grad_scores, k_heads, preferred_element_type=jnp.float32)
            * scale
        )
        grad_k = (
            carry[0]
            + jnp.einsum("hqk,qhd->khd", grad_scores, q_block, preferred_element_type=jnp.float32)
            * scale
        )
        grad_v = carry[1] + jnp.einsum(
            "hqk,qhd->khd", probs.astype(low), g_block, preferred_element_type=jnp.float32
        )
        return ((grad_k, grad_v), grad_q)

    start = (jnp.zeros(k_heads.shape, jnp.float32), jnp.zeros(v_heads.shape, jnp.float32))
    (grad_k, grad_v), grad_q = lax.scan(
        one_block,
        start,
        (
            q_rows.reshape(blocks, block_rows, heads, HEAD_DIM),
            grad_mixed.reshape(blocks, block_rows, heads, HEAD_DIM),
            logsum,
        ),
    )
    return (
        grad_q.reshape(length, width_all),
        grad_k.reshape(-1, width_all),
        grad_v.reshape(-1, width_all),
    )


def adamw(weight, moment_one, moment_two, gradient, filled, step_rate):
    new_one = beta_one * moment_one + (1.0 - beta_one) * gradient
    new_two = beta_two * moment_two + (1.0 - beta_two) * gradient * gradient
    fixed_one = new_one / (1.0 - beta_one**STEP)
    fixed_two = new_two / (1.0 - beta_two**STEP)
    updated = weight - step_rate * (fixed_one / (jnp.sqrt(fixed_two) + adam_eps) + decay * weight)
    return (new_one * filled, new_two * filled, updated * filled)


def swap(values, axis, bit):
    count = lax.axis_size(axis)
    return lax.ppermute(values, axis, [(i, i ^ (1 << bit)) for i in range(count)])


def choose(values, index, axis):
    return lax.dynamic_index_in_dim(values, index, axis, keepdims=False)


def total_sum(values):
    for axis in ("dp", "tensor"):
        for bit in range(lax.axis_size(axis).bit_length() - 1):
            values = values + swap(values, axis, bit)
    return values


def pick_units(master, slot_unit, state, kind, place, sizes):
    capacity, unit_rows, width = master.shape
    units = state.shape[0]

    def body(slot_ref, state_ref, kind_ref, place_ref, blocks, *rest):
        outs, (highs, lows, zeros, read, sems) = rest[: len(sizes)], rest[len(sizes) :]

        def start(source, unit):
            for which, out in enumerate(outs):

                @pl.when(kind_ref[unit] == which)
                def _():
                    pltpu.make_async_copy(source, out.at[place_ref[unit]], sems.at[unit]).start()

        @pl.loop(0, capacity)
        def _(slot):
            @pl.when(slot_ref[slot] >= 0)
            def _():
                pltpu.make_async_copy(blocks.at[slot], highs.at[slot], read.at[slot]).start()

        zeros[...] = jnp.zeros_like(zeros)

        @pl.loop(0, units)
        def _(unit):
            @pl.when(state_ref[unit] == 0)
            def _():
                start(zeros, unit)

        @pl.loop(0, capacity)
        def _(slot):
            @pl.when(slot_ref[slot] >= 0)
            def _():
                pltpu.make_async_copy(blocks.at[slot], highs.at[slot], read.at[slot]).wait()
                lows[slot] = highs[slot].astype(low)
                start(lows.at[slot], slot_ref[slot])

        @pl.loop(0, units)
        def _(unit):
            @pl.when(state_ref[unit] < 2)
            def _():
                pltpu.make_async_copy(zeros, outs[0].at[0], sems.at[unit]).wait()

    return pl.pallas_call(
        body,
        grid_spec=pltpu.PrefetchScalarGridSpec(
            num_scalar_prefetch=4,
            grid=(1,),
            in_specs=[pl.BlockSpec(memory_space=pl.ANY)],
            out_specs=[pl.BlockSpec(memory_space=pl.ANY)] * len(sizes),
            scratch_shapes=[
                pltpu.VMEM((capacity, unit_rows, width), jnp.float32),
                pltpu.VMEM((capacity, unit_rows, width), low),
                pltpu.VMEM((unit_rows, width), low),
                pltpu.SemaphoreType.DMA((capacity,)),
                pltpu.SemaphoreType.DMA((units,)),
            ],
        ),
        out_shape=[jax.ShapeDtypeStruct((size, unit_rows, width), low) for size in sizes],
        compiler_params=pltpu.CompilerParams(vmem_limit_bytes=56 * 2**20),
        cost_estimate=cheap,
        name="pick_units",
    )(slot_unit, state, kind, place, master)


def place_blocks(sources, which, position, parts=1):
    amount = which.shape[0]
    shape = sources[0].shape[1:]
    size = amount // parts

    def body(which_ref, position_ref, *rest):
        ins, outs = rest[: len(sources)], rest[len(sources) : len(sources) + parts]
        held, read, sems = rest[len(sources) + parts :]

        @pl.loop(0, amount)
        def _(i):
            for source, ref in enumerate(ins):

                @pl.when(which_ref[i] == source)
                def _():
                    pltpu.make_async_copy(ref.at[position_ref[i]], held.at[i], read.at[i]).start()

        for part, out in enumerate(outs):

            @pl.loop(0, size)
            def _(j):
                i = part * size + j
                pltpu.make_async_copy(ins[0].at[0], held.at[i], read.at[i]).wait()
                pltpu.make_async_copy(held.at[i], out.at[j], sems.at[i]).start()

        @pl.loop(0, amount)
        def _(i):
            pltpu.make_async_copy(held.at[i], outs[0].at[0], sems.at[i]).wait()

    return pl.pallas_call(
        body,
        grid_spec=pltpu.PrefetchScalarGridSpec(
            num_scalar_prefetch=2,
            grid=(1,),
            in_specs=[pl.BlockSpec(memory_space=pl.ANY)] * len(sources),
            out_specs=[pl.BlockSpec(memory_space=pl.ANY)] * parts,
            scratch_shapes=[
                pltpu.VMEM((amount,) + shape, low),
                pltpu.SemaphoreType.DMA((amount,)),
                pltpu.SemaphoreType.DMA((amount,)),
            ],
        ),
        out_shape=[jax.ShapeDtypeStruct((size,) + shape, low)] * parts,
        compiler_params=pltpu.CompilerParams(vmem_limit_bytes=56 * 2**20),
        cost_estimate=cheap,
        name="place_blocks",
    )(which, position, *sources)


def hops(values, step, turn):
    count = lax.axis_size("tensor")
    if step > 0:
        pairs = [(i, i + 1) for i in range(turn - 1, count - 1)]
    else:
        pairs = [(i, i - 1) for i in range(1, count - turn + 1)]
    return lax.ppermute(values, "tensor", pairs)


def slots_of(own, ups, downs):
    count = lax.axis_size("tensor")
    me = lax.axis_index("tensor")
    return [own] + [jnp.where(me >= k, ups[k - 1], downs[count - k - 1]) for k in range(1, count)]


fence = lax.optimization_barrier


def in_pool(member, inner, inner_count):
    me = lax.axis_index("dp")
    half, core = member >> 3, ((member >> 2) & 1) ^ (me & 1)
    far_y, far_x = ((member >> 1) & 1) ^ ((me >> 2) & 1), (member & 1) ^ ((me >> 1) & 1)
    where_first = (far_y * 2 + far_x) * inner_count
    where_second = (4 + far_x * 2 + far_y) * inner_count
    return (core, jnp.where(half == 0, where_first, where_second) + inner)


def on_device(
    hidden_in,
    time_embed,
    caption_table,
    caption_ids,
    owners,
    master,
    first_moment,
    second_moment,
    mod_table,
    mod_first,
    mod_second,
    out_grad,
):
    count = lax.axis_size("tensor")
    dp_count = lax.axis_size("dp")
    me_dp = lax.axis_index("dp")
    me_tensor = lax.axis_index("tensor")
    capacity, unit_rows, width = master.shape
    units = owners.shape[0]
    tokens = hidden_in.shape[1]
    text_count = caption_ids.shape[1]
    share = width // count
    per = share // unit_rows
    ups = (units - 8 * per) // 2
    rank_of = ranks_of(owners)
    mine = owners == me_dp
    match = (rank_of[None, :] == jnp.arange(capacity)[:, None]) & mine[None, :]
    filled = jnp.any(match, axis=1)
    unit_of_slot = jnp.sum(jnp.where(match, jnp.arange(units)[None, :], 0), axis=1)

    square = [list(range(i * per, (i + 1) * per)) for i in range(8)]
    group_attn = square[0] + square[1] + square[2] + square[5]
    group_full = square[3] + square[4] + square[6] + square[7]
    group_mlp = list(range(8 * per, units))
    members = len(group_attn)
    plane = dp_count == 8 and members == 16 and len(group_mlp) % dp_count == 0
    member_of = np.zeros(units, np.int32)
    member_of[group_attn] = np.arange(members)
    member_of[group_full] = np.arange(members)
    is_attn = np.zeros(units, bool)
    is_attn[group_attn] = True
    is_mlp = np.zeros(units, bool)
    is_mlp[group_mlp] = True

    latent_in = hidden_in[0].astype(jnp.float32)
    upstream = out_grad[0].astype(jnp.float32)
    modulate = mod_table + time_embed[0]

    def mod_row(which_row):
        return modulate[which_row][None, :]

    normed_one, inverse_one = layer_norm(latent_in)
    bits = dp_count.bit_length() - 1
    vocab_rows = caption_table.shape[0]

    def caption_terms(ids):
        chosen = ids.reshape(-1) - me_dp * vocab_rows
        onehot = (chosen[:, None] == jnp.arange(vocab_rows)[None, :]).astype(low)
        terms = jnp.dot(onehot, caption_table, preferred_element_type=jnp.float32).astype(low)
        return terms.reshape(dp_count, text_count, -1)

    def modulated(normed):
        return (normed.astype(jnp.float32) * (1.0 + mod_row(1)) + mod_row(0)).astype(low)

    def split_attn(w_attn):
        rows = w_attn.reshape(-1, width)
        return (rows[: 3 * share], rows[3 * share :])

    def whole_text(text_ring):
        return from_ring(text_ring, -1).transpose(1, 0, 2).reshape(text_count, width)

    def own_keys(text_ring, c_key):
        return project(whole_text(text_ring), c_key).astype(low)

    n_low = normed_one.astype(low)
    if plane:
        core, far_x, far_y = (
            ((member_of >> 2) & 1) ^ (me_dp & 1),
            (member_of & 1) ^ ((me_dp >> 1) & 1),
            ((member_of >> 1) & 1) ^ ((me_dp >> 2) & 1),
        )
        place = jnp.where(is_attn, far_x * 4 + far_y * 2, 8 + far_y * 4 + far_x * 2)
        place = jnp.where(is_mlp, np.arange(units) - 8 * per, place + (member_of >> 3))
        kind = jnp.where(is_mlp, 0, core)
        slot_mlp = unit_of_slot >= 8 * per
        owned_state = mine.astype(jnp.int32)
        up, down = hops(n_low, 1, 1), hops(n_low, -1, 1)
        kept, given = pick_units(
            master,
            jnp.where(filled & ~slot_mlp, unit_of_slot, -1),
            jnp.where(is_mlp, 2, owned_state),
            kind,
            place,
            (members, members),
        )
        got = swap(given, "dp", 0)
        ids = jnp.concatenate([caption_ids, swap(caption_ids, "dp", 0)])
        n_up, n_down = [up], [down]
        kept, got, up, down, ids = fence((kept, got, up, down, ids))
        pieces = [kept[i : i + 4] + got[i : i + 4] for i in range(0, members, 4)]
        attn_two, attn_send, full_two, full_send = fence(tuple(pieces))
        up, down = hops(up, 1, 2), hops(down, -1, 2)
        attn_got = swap(attn_send, "dp", 1)
        full_got = swap(full_send, "dp", 2)
        ids = jnp.concatenate([ids, swap(ids, "dp", 1)])
        (mlp_part,) = pick_units(
            fence((master, got))[0],
            jnp.where(filled & slot_mlp, unit_of_slot, -1),
            jnp.where(is_mlp, owned_state, 2),
            kind,
            place,
            (len(group_mlp),),
        )
        n_up.append(up), n_down.append(down)
        attn_two, attn_got, full_two, full_got, up, down, ids, mlp_part = fence(
            (attn_two, attn_got, full_two, full_got, up, down, ids, mlp_part)
        )
        pieces = [x[i : i + 2] + y[i : i + 2] for x, y in ((attn_two, attn_got), (full_two, full_got)) for i in (0, 2)]
        attn_one, attn_send, full_one, full_send = fence(tuple(pieces))
        up, down = hops(up, 1, 3), hops(down, -1, 3)
        attn_got = swap(attn_send, "dp", 2)
        full_got = swap(full_send, "dp", 1)
        ids = jnp.concatenate([ids, swap(ids, "dp", 2)])
        n_up.append(up), n_down.append(down)
        attn_one, attn_got, full_one, full_got, up, down, ids, mlp_part = fence(
            (attn_one, attn_got, full_one, full_got, up, down, ids, mlp_part)
        )
        attn_one, full_one = attn_one + attn_got, full_one + full_got
        mlp_part = lax.psum_scatter(mlp_part, "dp", scatter_dimension=0, tiled=True)
        first = jnp.concatenate([attn_one[0:1], swap(attn_one[0:1], "dp", 1)])
        second = jnp.concatenate([attn_one[1:2], swap(attn_one[1:2], "dp", 2)])
        up, down = hops(full_one, 1, 1), hops(full_one, -1, 1)
        text = caption_terms(ids)
        text = text[0:4] + swap(text[4:8], "dp", 2)
        f_up, f_down = [up], [down]
        first, second, up, down, text = fence((first, second, up, down, text))
        pool = jnp.concatenate([first, swap(first, "dp", 2), second, swap(second, "dp", 1)])
        up, down = hops(up, 1, 2), hops(down, -1, 2)
        text = text[0:2] + swap(text[2:4], "dp", 1)
        f_up.append(up), f_down.append(down)
        pool, up, down, text = fence((pool, up, down, text))
        other = swap(pool, "dp", 0)
        up, down = hops(up, 1, 3), hops(down, -1, 3)
        text = text[0] + swap(text[1], "dp", 0)
        f_up.append(up), f_down.append(down)
        pool, other, up, down, text = fence((pool, other, up, down, text))
        (w_attn,) = place_blocks((pool, other), *in_pool(np.arange(members), 0, 1))
        grad_whole = lax.all_gather(fence((out_grad[0], up))[0], "tensor", axis=0)
        full_ring = slots_of(full_one, f_up, f_down)
        first = jnp.concatenate([item[0:1] for item in full_ring])
        second = jnp.concatenate([item[1:2] for item in full_ring])
        first_got = swap(first, "dp", 1)
        second_got = swap(second, "dp", 2)
        text_ring = jnp.stack(ring(text))
        first = jnp.concatenate([first, first_got])
        second = jnp.concatenate([second, second_got])
        normed_all = jnp.concatenate(slots_of(n_low, n_up, n_down))
        h_one_all = modulated(normed_all)
        w_qkv, c_key = split_attn(w_attn)
        qkv = project(h_one_all, w_qkv).astype(low)
        first, second, text_ring, qkv = fence((first, second, text_ring, qkv))
        first_far, second_far = swap(first, "dp", 2), swap(second, "dp", 1)
        first_other, second_other = swap(first, "dp", 0), swap(second, "dp", 0)
        attended = self_attend(qkv)
        ck_own = own_keys(text_ring, c_key)
        first_far, second_far, first_other, second_other, attended, ck_own = fence(
            (first_far, second_far, first_other, second_other, attended, ck_own)
        )
        first_last, second_last = swap(first_far, "dp", 0), swap(second_far, "dp", 0)
        mlp_part = fence((mlp_part, first_far))[0]
        w_mlp = lax.all_gather(mlp_part, "dp", axis=0, tiled=True)
        listing = np.arange(count * members)
        matrix, rank, head = listing // (count * per), listing // per % count, listing % per
        slot = lax.rem(me_tensor - rank + count, count)
        which, position = in_pool(matrix * per + head, slot, count)
        blocks = 2 * count
        w_full = place_blocks(
            (first, first_far, second, second_far, first_other, first_last, second_other, second_last),
            which * 4 + position // blocks,
            position % blocks,
            parts=4,
        )
        w_full = [part.reshape(width, width) for part in w_full]
    else:
        slots_low = master.astype(low)
        rows = jnp.take(slots_low, rank_of, axis=0, mode="clip")
        rows = lax.psum(jnp.where(mine[:, None, None], rows, jnp.zeros((), low)), "dp")
        w_attn = rows[np.array(group_attn)]
        w_full = lax.all_gather(rows[np.array(group_full)], "tensor", axis=0)
        w_full = w_full.reshape(count, 4, share, width).swapaxes(0, 1).reshape(4, width, width)
        w_full = [w_full[i] for i in range(4)]
        w_mlp = rows[8 * per :]
        normed_all = jnp.concatenate(ring(n_low))
        grad_whole = lax.all_gather(out_grad[0], "tensor", axis=0)
        ids = caption_ids
        for bit in range(bits):
            ids = jnp.concatenate([ids, swap(ids, "dp", bit)])
        text = caption_terms(ids)
        for bit in reversed(range(bits)):
            text = text[: 1 << bit] + swap(text[1 << bit :], "dp", bit)
        text_ring = jnp.stack(ring(text[0]))
        h_one_all = modulated(normed_all)
        w_qkv, c_key = split_attn(w_attn)
        qkv = project(h_one_all, w_qkv).astype(low)
        attended = self_attend(qkv)
        ck_own = own_keys(text_ring, c_key)
    w_out, c_query, c_value, c_out = w_full
    w_mlp = w_mlp.reshape(-1, width)
    w_down = w_mlp[w_mlp.shape[0] // 2 :]
    text_low = whole_text(text_ring)

    mixed_parts = attended.reshape(count, tokens, share)
    mixed_ring = jnp.stack(
        [mixed_parts[0]] + [shift(mixed_parts[k], count - k) for k in range(1, count)]
    )
    mixed_own = from_ring(mixed_ring, 1).transpose(1, 0, 2).reshape(tokens, width)
    branch_one = expand(mixed_own, w_out)
    first_res = latent_in + mod_row(2) * branch_one
    first_low = first_res.astype(low)

    ck_ring = from_ring(jnp.stack(ring(ck_own)), -1)
    ck_rows = ck_ring.transpose(1, 0, 2).reshape(text_count, width)
    cv_rows = project(text_low, c_value).astype(low)
    cq_rows = project(first_low, c_query).astype(low)
    crossed, logsum_two = attend(cq_rows, ck_rows, cv_rows)
    second_res = first_res + expand(crossed, c_out)
    normed_two, inverse_two = layer_norm(second_res)
    h_two = (normed_two * (1.0 + mod_row(4)) + mod_row(3)).astype(low)

    h_slots = ring(h_two)
    out_slots = [
        choose(grad_whole, lax.rem(me_tensor - k + count, count), 0) for k in range(count)
    ]
    grad_slots = [(mod_row(5) * item.astype(jnp.float32)).astype(low) for item in out_slots]
    early = [k for k in range(count) if k == 0 or k != count // 2]
    late = [k for k in range(count) if k not in early]
    act, grad_pre, *terms = mlp_core(
        [h_slots[k] for k in early], [grad_slots[k] for k in early], w_mlp
    )
    grad_terms = dict(zip(early, terms))
    acts, grad_pres = [act], [grad_pre]
    grad_h_two = grad_terms[0].astype(jnp.float32)
    sent = {k: shift(grad_terms[k], count - k) for k in early[1:]}
    held = fence((*[h_slots[k] for k in late], act))
    act, grad_pre, *terms = mlp_core(held[:-1], [grad_slots[k] for k in late], w_mlp)
    grad_terms = dict(zip(late, terms))
    acts.append(act), grad_pres.append(grad_pre)
    sent.update({k: shift(grad_terms[k], count - k) for k in late})
    for k in range(1, count):
        grad_h_two = grad_h_two + sent[k].astype(jnp.float32)
    act_low = jnp.concatenate(acts)
    grad_pre = jnp.concatenate(grad_pres)
    order = early + late
    h_two_all = jnp.concatenate([h_slots[k] for k in order])
    grad_mlp_all = jnp.concatenate([grad_slots[k] for k in order])
    grad_up = outer(grad_pre, h_two_all).astype(low)
    grad_down = outer(act_low, grad_mlp_all).astype(low)
    mlp_grad = jnp.concatenate([grad_up, grad_down]).reshape(-1, unit_rows, width)
    branch_terms = expand(act_low, w_down)
    out_all = jnp.concatenate([out_slots[k] for k in order])
    branch_row = jnp.sum(branch_terms * out_all.astype(jnp.float32), axis=0)
    branch_terms = branch_terms.astype(low).reshape(count, tokens, width)
    back = np.argsort(order)
    branch_terms = jnp.take(
        branch_terms,
        jnp.array(back)[lax.rem(me_tensor - jnp.arange(count) + count, count)],
        axis=0,
        mode="clip",
    ).reshape(-1, width)
    if plane:
        mlp_sum = lax.psum_scatter(mlp_grad, "dp", scatter_dimension=0, tiled=True)
        branch_terms = fence((branch_terms, grad_h_two))[0]
    branch_two = lax.psum_scatter(branch_terms, "tensor", scatter_dimension=0, tiled=True)
    second_grad = upstream + norm_back(grad_h_two, normed_two, inverse_two, mod_row(4))

    cross_grad = second_grad.astype(low)
    grad_c_out = outer(crossed, cross_grad)
    grad_crossed = project(cross_grad, c_out).astype(low)
    grad_cq, grad_ck, grad_cv = attend_back(cq_rows, ck_rows, cv_rows, grad_crossed, logsum_two)
    grad_cq = grad_cq.astype(low)
    first_grad = second_grad + expand(grad_cq, c_query)
    attn_grad = (mod_row(2) * first_grad).astype(low)
    grad_mixed = project(attn_grad, w_out).astype(low)
    grad_mixed = to_ring(grad_mixed.reshape(tokens, count, share).transpose(1, 0, 2))
    grad_parts = [grad_mixed[0]] + [shift(grad_mixed[k], k) for k in range(1, count)]
    grad_c_value = outer(grad_cv.astype(low), text_low).astype(low)
    grad_c_out = outer(crossed, cross_grad).astype(low)
    grad_c_query = outer(grad_cq, first_low).astype(low)
    grad_w_out = outer(mixed_own, attn_grad).astype(low)
    grad_ck_parts = to_ring(grad_ck.reshape(text_count, count, share).transpose(1, 0, 2)).astype(low)

    def sum_ck(parts):
        total = grad_ck_parts[0].astype(jnp.float32)
        for k in range(1, count):
            total = total + parts[k - 1].astype(jnp.float32)
        return total.astype(low)

    def scattered(terms):
        total = terms[0].astype(jnp.float32)
        for k in range(1, count):
            total = total + shift(terms[k], count - k).astype(jnp.float32)
        return total

    normed_wide = normed_all.astype(jnp.float32)

    def summed(values):
        return jnp.sum(values, axis=0)

    if plane:
        even = (me_dp & 1) == 0
        x_bit, y_bit = (me_dp >> 1) & 1, (me_dp >> 2) & 1

        def core_halves(one, two):
            return (jnp.where(even, one, two), jnp.where(even, two, one))

        def split(total, bit, axis):
            return (choose(total, bit, axis), choose(total, 1 - bit, axis))

        kept_two, given_two = core_halves(grad_c_value, grad_c_out)
        got_two = swap(given_two, "dp", 0)
        kept_one, given_one = core_halves(grad_w_out, grad_c_query)
        got_one = swap(given_one, "dp", 0)
        grad_parts, kept_one, kept_two, got_one, got_two = fence(
            (grad_parts, kept_one, kept_two, got_one, got_two)
        )
        box = (count, 2, 2, unit_rows, width)
        kept_one, given_one = split((kept_one + got_one).reshape(box), x_bit, 2)
        kept_two, given_two = split((kept_two + got_two).reshape(box), y_bit, 1)
        kept_one, given_one, kept_two, given_two, grad_parts = fence(
            (kept_one, given_one, kept_two, given_two, grad_parts)
        )
        got_one, got_two = swap(given_one, "dp", 1), swap(given_two, "dp", 2)
        ck_parts = [shift(grad_ck_parts[k], k) for k in range(1, count)]
        grad_qkv = self_attend_back(qkv, jnp.concatenate(grad_parts, axis=0))
        kept_one, got_one, kept_two, got_two, ck_parts, grad_qkv, mlp_sum = fence(
            (kept_one, got_one, kept_two, got_two, ck_parts, grad_qkv, mlp_sum)
        )
        mlp_sum = lax.all_gather(mlp_sum, "dp", axis=0, tiled=True)
        kept_one, given_one = split(kept_one + got_one, y_bit, 1)
        kept_two, given_two = split(kept_two + got_two, x_bit, 1)
        got_one, got_two = swap(given_one, "dp", 2), swap(given_two, "dp", 1)
        grad_q, grad_k, grad_v = (
            outer(grad_qkv[:, i * share : (i + 1) * share], h_one_all).astype(low)
            for i in range(3)
        )
        grad_c_key = outer(sum_ck(ck_parts), text_low).astype(low)
        attn_kept, attn_given = core_halves(
            jnp.stack([grad_q, grad_v]), jnp.stack([grad_k, grad_c_key])
        )
        attn_got = swap(attn_given, "dp", 0)
        grad_h_terms = expand(grad_qkv, w_qkv)
        mod_terms = jnp.stack(
            [
                summed(grad_h_terms),
                summed(grad_h_terms * normed_wide),
                summed(branch_one * first_grad),
                summed(grad_h_two),
                summed(grad_h_two * normed_two),
                branch_row,
            ]
        )
        for bit in range(3):
            mod_terms = mod_terms + swap(mod_terms, "dp", bit)
        grad_h_terms = grad_h_terms.astype(low)
        kept_one, got_one, kept_two, got_two, attn_kept, attn_got, grad_h_terms, mod_terms = fence(
            (kept_one, got_one, kept_two, got_two, attn_kept, attn_got, grad_h_terms, mod_terms)
        )
        full_parts = jnp.stack([kept_one + got_one, kept_two + got_two], axis=1)
        full_parts = to_ring(full_parts)
        full_got = [shift(full_parts[k], k) for k in range(1, count)]
        attn_all = (attn_kept + attn_got).reshape(2, 2, 2, unit_rows, width)
        one_kept, one_given = split(attn_all[0], x_bit, 1)
        two_kept, two_given = split(attn_all[1], y_bit, 0)
        one_got, two_got = swap(one_given, "dp", 1), swap(two_given, "dp", 2)
        full_own = full_parts[0]
        full_own, full_got, one_kept, one_got, two_kept, two_got = fence(
            (full_own, full_got, one_kept, one_got, two_kept, two_got)
        )
        full_sum = full_own.astype(jnp.float32)
        for part in full_got:
            full_sum = full_sum + part.astype(jnp.float32)
        full_sum = full_sum.astype(low)
        one_kept, one_given = split(one_kept + one_got, y_bit, 0)
        two_kept, two_given = split(two_kept + two_got, x_bit, 0)
        one_got, two_got = swap(one_given, "dp", 2), swap(two_given, "dp", 1)
        grad_h_terms = fence((grad_h_terms, full_sum))[0].reshape(count, tokens, width)
        grad_h_got = [shift(grad_h_terms[k], count - k) for k in range(1, count)]
        one_kept, one_got, two_kept, two_got, full_sum = fence(
            (one_kept, one_got, two_kept, two_got, full_sum)
        )
        first = jnp.stack([one_kept + one_got, full_sum[0]])
        second = jnp.stack([two_kept + two_got, full_sum[1]])
        first_got, second_got = swap(first, "dp", 1), swap(second, "dp", 2)
        first = jnp.concatenate([first, first_got])
        second = jnp.concatenate([second, second_got])
        first, second = fence((first, second))
        first_far, second_far = swap(first, "dp", 2), swap(second, "dp", 1)
        first, first_far, second, second_far = fence((first, first_far, second, second_far))
        pool = jnp.concatenate([first, first_far, second, second_far])
        other = swap(pool, "dp", 0)
        mod_terms = mod_terms + swap(mod_terms, "tensor", 0)
        pool, other, mod_terms = fence((pool, other, mod_terms))
        for bit in range(1, count.bit_length() - 1):
            mod_terms = mod_terms + swap(mod_terms, "tensor", bit)
        mod_grad = mod_terms
        which, position = in_pool(member_of, np.where(is_attn, 0, 1), 2)
        which = jnp.where(is_mlp, 2, which)
        position = jnp.where(is_mlp, np.arange(units) - 8 * per, position)
        own = jnp.sum(jnp.where(match[:, :, None], jnp.stack([which, position], 1)[None], 0), axis=1)
        new_first, new_second, new_master = update_slots(
            master,
            first_moment,
            second_moment,
            filled.astype(jnp.int32),
            own[:, 0],
            own[:, 1],
            (pool, other, mlp_sum),
        )
        grad_h_got, new_first = fence((grad_h_got, new_first))
        grad_h_one = grad_h_terms[0].astype(jnp.float32)
        for part in grad_h_got:
            grad_h_one = grad_h_one + part.astype(jnp.float32)
    else:
        grad_qkv = self_attend_back(qkv, jnp.concatenate(grad_parts, axis=0))
        grad_c_key = sum_ck([shift(grad_ck_parts[k], k) for k in range(1, count)])
        grad_c_key = outer(grad_c_key, text_low).astype(low)
        attn_grads = [outer(grad_qkv, h_one_all).astype(low), grad_c_key]
        grad_h_terms = expand(grad_qkv, w_qkv)
        grad_h_one = scattered(grad_h_terms.astype(low).reshape(count, tokens, width))
        full_grads = (grad_w_out, grad_c_query, grad_c_value, grad_c_out)
        full_sum = jnp.stack([g.reshape(count, share, width) for g in full_grads], axis=1)
        full_sum = lax.psum_scatter(full_sum, "tensor", scatter_dimension=0, tiled=True)
        order = np.array(group_attn + group_full + group_mlp)
        sums = jnp.concatenate(
            [jnp.concatenate(attn_grads), full_sum.reshape(-1, width), mlp_grad.reshape(-1, width)]
        )
        sums = lax.psum(sums.reshape(units, unit_rows, width), "dp")
        owned = jnp.take(sums, jnp.array(np.argsort(order))[unit_of_slot], axis=0, mode="clip")
        mod_grad = total_sum(
            jnp.stack(
                [
                    summed(grad_h_terms),
                    summed(grad_h_terms * normed_wide),
                    summed(branch_one * first_grad),
                    summed(grad_h_two),
                    summed(grad_h_two * normed_two),
                    branch_row,
                ]
            )
        )
        new_first, new_second, new_master = adamw(
            master,
            first_moment,
            second_moment,
            owned.astype(jnp.float32),
            filled.astype(jnp.float32)[:, None, None],
            rate,
        )
    branch_two, second_res, grad_h_one = fence((branch_two, second_res, grad_h_one))
    block_out = second_res + mod_row(5) * branch_two.astype(jnp.float32)
    input_grad = first_grad + norm_back(grad_h_one, normed_one, inverse_one, mod_row(1))
    mod_new_first, mod_new_second, mod_new = adamw(
        mod_table, mod_first, mod_second, mod_grad, 1.0, table_rate
    )
    return (
        block_out[None],
        input_grad[None],
        new_first,
        new_second,
        new_master,
        mod_new_first,
        mod_new_second,
        mod_new,
    )


def solution(mesh):
    in_specs = (
        P("dp", "tensor", None),
        P("dp", None, None),
        P("dp", "tensor"),
        P("dp", None),
        P(),
        P("dp", "tensor", None),
        P("dp", "tensor", None),
        P("dp", "tensor", None),
        P(),
        P(),
        P(),
        P("dp", "tensor", None),
    )
    out_specs = (
        P("dp", "tensor", None),
        P("dp", "tensor", None),
        P("dp", "tensor", None),
        P("dp", "tensor", None),
        P("dp", "tensor", None),
        P(),
        P(),
        P(),
    )
    return jax.shard_map(
        on_device, mesh=mesh, in_specs=in_specs, out_specs=out_specs, check_vma=False
    )
```

```python
import math

import jax
import jax.numpy as jnp
import numpy as np
from jax import lax
from jax.experimental import pallas as pl
from jax.experimental.pallas import tpu as pltpu
from jax.sharding import PartitionSpec as P

HEAD_DIM = 72
STEP = 10


norm_eps = 1e-06
beta_one = 0.9
beta_two = 0.999
rate = 0.03
table_rate = 0.3
decay = 0.01
adam_eps = 1e-08
low = jnp.bfloat16


def ranks_of(owners):
    index = jnp.arange(owners.shape[0])
    before = (owners[None, :] == owners[:, None]) & (index[None, :] < index[:, None])
    return jnp.sum(before.astype(jnp.int32), axis=1)


def layer_norm(values):
    center = values - jnp.mean(values, axis=-1, keepdims=True)
    inverse = lax.rsqrt(jnp.mean(center * center, axis=-1, keepdims=True) + norm_eps)
    return (center * inverse, inverse)


def norm_back(grad_rows, normed, inverse, scale_row):
    scaled = grad_rows * (1.0 + scale_row)
    mean_one = jnp.mean(scaled, axis=-1, keepdims=True)
    mean_two = jnp.mean(scaled * normed, axis=-1, keepdims=True)
    return inverse * (scaled - mean_one - normed * mean_two)


def project(rows, weight):
    return jnp.einsum("ld,rd->lr", rows, weight, preferred_element_type=jnp.float32)


def expand(rows, weight):
    return jnp.einsum("lr,rd->ld", rows, weight, preferred_element_type=jnp.float32)


def outer(left, right):
    return jnp.einsum("lr,ld->rd", left, right, preferred_element_type=jnp.float32)


def shift(values, step):
    count = lax.axis_size("tensor")
    return lax.ppermute(values, "tensor", [(i, (i + step) % count) for i in range(count)])


def ring(values):
    return [values] + [shift(values, k) for k in range(1, lax.axis_size("tensor"))]


def to_ring(stacked):
    count = stacked.shape[0]
    twice = jnp.concatenate([stacked, stacked], axis=0)
    return lax.dynamic_slice_in_dim(twice, lax.axis_index("tensor"), count, 0)


def from_ring(stacked, sign):
    count = stacked.shape[0]
    me = lax.axis_index("tensor")
    place = lax.rem(sign * (jnp.arange(count) - me) + 2 * count, count)
    return jnp.take(stacked, place, axis=0, mode="clip")


cheap = pl.CostEstimate(flops=1000, bytes_accessed=1000, transcendentals=0)


def self_attend(qkv):
    length, width_all = qkv.shape
    share = width_all // 3
    heads = share // HEAD_DIM
    rows = min(256, length)
    scale = HEAD_DIM ** (-0.5)

    def body(qkv_ref, out_ref):
        @pl.loop(0, length // rows)
        def _(step):
            here = pl.ds(pl.multiple_of(step * rows, rows), rows)
            parts = []
            for head in range(heads):
                at = head * HEAD_DIM
                q = qkv_ref[here, at : at + HEAD_DIM]
                k = qkv_ref[:, share + at : share + at + HEAD_DIM]
                v = qkv_ref[:, 2 * share + at : 2 * share + at + HEAD_DIM]
                scores = scale * lax.dot_general(
                    k, q, (((1,), (1,)), ((), ())), preferred_element_type=jnp.float32
                )
                expo = jnp.exp(scores - jnp.max(scores, axis=0, keepdims=True))
                inverse = 1.0 / jnp.sum(expo, axis=0, keepdims=True)
                probs = (expo * inverse).astype(low)
                mixed = lax.dot_general(
                    v, probs, (((0,), (0,)), ((), ())), preferred_element_type=jnp.float32
                )
                parts.append(mixed.T)
            out_ref[here, :] = jnp.concatenate(parts, axis=1).astype(low)

    return pl.pallas_call(
        body,
        out_shape=jax.ShapeDtypeStruct((length, share), low),
        compiler_params=pltpu.CompilerParams(vmem_limit_bytes=32 * 2**20),
        cost_estimate=cheap,
        name="self_attend",
    )(qkv)


def self_attend_back(qkv, grad_mixed):
    length, width_all = qkv.shape
    share = width_all // 3
    heads = share // HEAD_DIM
    rows = min(256, length)
    steps = length // rows
    scale = HEAD_DIM ** (-0.5)

    def body(qkv_ref, grad_ref, out_ref, grad_k, grad_v):
        grad_k[...] = jnp.zeros_like(grad_k)
        grad_v[...] = jnp.zeros_like(grad_v)

        @pl.loop(0, steps)
        def _(step):
            here = pl.ds(pl.multiple_of(step * rows, rows), rows)
            parts = []
            for head in range(heads):
                at = head * HEAD_DIM
                q = qkv_ref[here, at : at + HEAD_DIM]
                k = qkv_ref[:, share + at : share + at + HEAD_DIM]
                v = qkv_ref[:, 2 * share + at : 2 * share + at + HEAD_DIM]
                g = grad_ref[here, at : at + HEAD_DIM]
                scores = scale * lax.dot_general(
                    k, q, (((1,), (1,)), ((), ())), preferred_element_type=jnp.float32
                )
                expo = jnp.exp(scores - jnp.max(scores, axis=0, keepdims=True))
                probs = expo * (1.0 / jnp.sum(expo, axis=0, keepdims=True))
                grad_probs = lax.dot_general(
                    v, g, (((1,), (1,)), ((), ())), preferred_element_type=jnp.float32
                )
                inner = jnp.sum(probs * grad_probs, axis=0, keepdims=True)
                grad_scores = (probs * (grad_probs - inner)).astype(low)
                grad_v[head] += jnp.dot(
                    probs.astype(low), g, preferred_element_type=jnp.float32
                )
                grad_k[head] += jnp.dot(grad_scores, q, preferred_element_type=jnp.float32)
                grad_q = lax.dot_general(
                    k, grad_scores, (((0,), (0,)), ((), ())), preferred_element_type=jnp.float32
                )
                parts.append(grad_q.T * scale)
            out_ref[here, :share] = jnp.concatenate(parts, axis=1).astype(low)

        both = [grad_k[head] * scale for head in range(heads)]
        out_ref[:, share : 2 * share] = jnp.concatenate(both, axis=1).astype(low)
        both = [grad_v[head] for head in range(heads)]
        out_ref[:, 2 * share :] = jnp.concatenate(both, axis=1).astype(low)

    return pl.pallas_call(
        body,
        out_shape=jax.ShapeDtypeStruct((length, width_all), low),
        scratch_shapes=[pltpu.VMEM((heads, length, HEAD_DIM), jnp.float32)] * 2,
        compiler_params=pltpu.CompilerParams(vmem_limit_bytes=40 * 2**20),
        cost_estimate=cheap,
        name="self_attend_back",
    )(qkv, grad_mixed)


def mlp_core(rows_in, grads_in, w_mlp):
    groups = len(rows_in)
    tokens, width = rows_in[0].shape
    hidden = w_mlp.shape[0] // 2
    chunk = 384 if hidden % 384 == 0 else hidden
    steps = hidden // chunk
    curve = 0.7978845608028654

    def body(*refs):
        rows, grads = refs[:groups], refs[groups : 2 * groups]
        up, down = refs[2 * groups : 2 * groups + 2]
        act, grad_pre = refs[2 * groups + 2 : 2 * groups + 4]
        outs = refs[2 * groups + 4 : 3 * groups + 4]
        total = refs[-1]
        step = pl.program_id(0)
        for i in range(groups):
            pre = lax.dot_general(
                rows[i][...], up[...], (((1,), (1,)), ((), ())), preferred_element_type=jnp.float32
            )
            square = pre * pre
            bend = jnp.tanh(curve * pre * (1.0 + 0.044715 * square))
            half = 0.5 * (1.0 + bend)
            here = pl.ds(i * tokens, tokens)
            act[here, :] = (pre * half).astype(low)
            slope = half + (0.5 * curve) * pre * (1.0 - bend * bend) * (1.0 + 0.134145 * square)
            grad_act = lax.dot_general(
                grads[i][...], down[...], (((1,), (1,)), ((), ())), preferred_element_type=jnp.float32
            )
            grad_low = (grad_act * slope).astype(low)
            grad_pre[here, :] = grad_low
            term = jnp.dot(grad_low, up[...], preferred_element_type=jnp.float32)

            @pl.when(step == 0)
            def _():
                total[here, :] = term

            @pl.when(step > 0)
            def _():
                total[here, :] += term

            @pl.when(step == steps - 1)
            def _():
                outs[i][...] = total[here, :].astype(low)

    whole = pl.BlockSpec((tokens, width), lambda s: (0, 0))
    across = pl.BlockSpec((groups * tokens, chunk), lambda s: (0, s))
    return pl.pallas_call(
        body,
        grid=(steps,),
        in_specs=[whole] * (2 * groups)
        + [
            pl.BlockSpec((chunk, width), lambda s: (s, 0)),
            pl.BlockSpec((chunk, width), lambda s: (steps + s, 0)),
        ],
        out_specs=[across, across] + [whole] * groups,
        out_shape=[jax.ShapeDtypeStruct((groups * tokens, hidden), low)] * 2
        + [jax.ShapeDtypeStruct((tokens, width), low)] * groups,
        scratch_shapes=[pltpu.VMEM((groups * tokens, width), jnp.float32)],
        compiler_params=pltpu.CompilerParams(vmem_limit_bytes=40 * 2**20),
        cost_estimate=cheap,
        name="mlp_core",
    )(*rows_in, *grads_in, w_mlp, w_mlp)


nt = (((1,), (1,)), ((), ()))
tn = (((0,), (0,)), ((), ()))


def dot(left, right, dims=(((1,), (0,)), ((), ()))):
    return lax.dot_general(left, right, dims, preferred_element_type=jnp.float32)


def softmax_keys(keys, queries):
    scores = dot(keys, queries, nt) * HEAD_DIM ** (-0.5)
    expo = jnp.exp(scores - jnp.max(scores, axis=0, keepdims=True))
    return expo * (1.0 / jnp.sum(expo, axis=0, keepdims=True))


def cuts_of(width):
    size = 384 if width % 384 == 0 else width
    return [slice(i, i + size) for i in range(0, width, size)]


def in_smem():
    return pl.BlockSpec(memory_space=pltpu.SMEM)


def in_vmem():
    return pl.BlockSpec(memory_space=pltpu.VMEM)


def cross_block(place, mixed, hidden, rows, key_ring, text, w_out, c_query, c_value, c_out):
    count, words, share = key_ring.shape
    tokens, width = hidden.shape
    per = share // HEAD_DIM

    def body(place_ref, *refs):
        parts = refs[:count]
        x_ref, rows_ref, ring_ref, text_ref, wo, wq, wv, wc = refs[count : count + 8]
        branch, res_low, cq, ck, cv, crossed, res, normed, inverse, out = refs[count + 8 :]
        me = place_ref[0]
        for cut in cuts_of(width):
            total = jnp.zeros((tokens, cut.stop - cut.start), jnp.float32)
            for k in range(count):
                rank = lax.rem(me + k, count)
                here = pl.ds(pl.multiple_of(rank * share, 32), share)
                total += dot(parts[k][...], wo[here, cut])
            branch[:, cut] = total
            first = x_ref[:, cut].astype(jnp.float32) + rows_ref[0:1, cut] * total
            res[:, cut] = first
            res_low[:, cut] = first.astype(low)
        for cut in cuts_of(width):
            cq[:, cut] = dot(res_low[...], wq[cut, :], nt).astype(low)
            cv[:, cut] = dot(text_ref[...], wv[cut, :], nt).astype(low)
        keys = [ring_ref[lax.rem(me - rank + count, count)] for rank in range(count)]
        ck[...] = jnp.concatenate(keys, axis=1)
        parts_out = []
        for at in range(0, width, HEAD_DIM):
            head = slice(at, at + HEAD_DIM)
            probs = softmax_keys(ck[:, head], cq[:, head]).astype(low)
            parts_out.append(dot(cv[:, head], probs, tn).T)
        crossed[...] = jnp.concatenate(parts_out, axis=1).astype(low)
        for cut in cuts_of(width):
            res[:, cut] += dot(crossed[...], wc[:, cut])
        second = res[...]
        center = second - jnp.mean(second, axis=-1, keepdims=True)
        spread = lax.rsqrt(jnp.mean(center * center, axis=-1, keepdims=True) + norm_eps)
        inverse[...] = spread
        scaled = center * spread
        normed[...] = scaled
        out[...] = (scaled * (1.0 + rows_ref[2:3, :]) + rows_ref[1:2, :]).astype(low)

    wide = (tokens, width)
    shapes = [
        (wide, jnp.float32),
        (wide, low),
        (wide, low),
        ((words, width), low),
        ((words, width), low),
        (wide, low),
        (wide, jnp.float32),
        (wide, jnp.float32),
        ((tokens, 1), jnp.float32),
        (wide, low),
    ]
    return pl.pallas_call(
        body,
        in_specs=[in_smem()] + [in_vmem()] * (count + 8),
        out_shape=[jax.ShapeDtypeStruct(*item) for item in shapes],
        compiler_params=pltpu.CompilerParams(vmem_limit_bytes=40 * 2**20),
        cost_estimate=cheap,
        name="cross_block",
    )(place, *mixed, hidden, rows, key_ring, text, w_out, c_query, c_value, c_out)


def cross_back(place, terms, grad, rows, normed, inverse, branch, cq, ck, cv, c_out, c_query, w_out):
    count = len(terms)
    tokens, width = grad.shape
    words = ck.shape[0]
    share = width // count
    scale = HEAD_DIM ** (-0.5)

    def body(place_ref, *refs):
        parts = refs[:count]
        grad_ref, rows_ref, n_ref, i_ref, b_ref, q_ref, k_ref, v_ref, wc, wq, wo = refs[
            count : count + 11
        ]
        first, cross_low, grad_q, grad_k, grad_v, attn_low, sums = refs[count + 11 : count + 18]
        outs, back = refs[count + 18 : -1], refs[-1]
        me = place_ref[0]
        total = parts[0][...].astype(jnp.float32)
        for part in parts[1:]:
            total += part[...].astype(jnp.float32)
        n = n_ref[...]
        sums[1:2, :] = jnp.sum(total, axis=0, keepdims=True)
        sums[2:3, :] = jnp.sum(total * n, axis=0, keepdims=True)
        second = grad_ref[...].astype(jnp.float32) + norm_back(total, n, i_ref[...], rows_ref[2:3, :])
        first[...] = second
        cross_low[...] = second.astype(low)
        for cut in cuts_of(width):
            back[:, cut] = dot(cross_low[...], wc[cut, :], nt).astype(low)
        grads = ([], [], [])
        for at in range(0, width, HEAD_DIM):
            head = slice(at, at + HEAD_DIM)
            q, k, v, g = q_ref[:, head], k_ref[:, head], v_ref[:, head], back[:, head]
            probs = softmax_keys(k, q)
            grad_probs = dot(v, g, nt)
            inner = jnp.sum(probs * grad_probs, axis=0, keepdims=True)
            grad_scores = (probs * (grad_probs - inner)).astype(low)
            grads[0].append((dot(k, grad_scores, tn) * scale).T)
            grads[1].append(dot(grad_scores, q) * scale)
            grads[2].append(dot(probs.astype(low), g))
        for out, pieces in zip((grad_q, grad_k, grad_v), grads):
            out[...] = jnp.concatenate(pieces, axis=1).astype(low)
        for cut in cuts_of(width):
            whole = first[:, cut] + dot(grad_q[...], wq[:, cut])
            first[:, cut] = whole
            attn_low[:, cut] = (rows_ref[0:1, cut] * whole).astype(low)
            sums[0:1, cut] = jnp.sum(b_ref[:, cut] * whole, axis=0, keepdims=True)
        for k in range(count):
            rank = lax.rem(me + k, count)
            here = pl.ds(pl.multiple_of(rank * share, 32), share)
            outs[k][...] = dot(attn_low[...], wo[here, :], nt).astype(low)

    wide = (tokens, width)
    shapes = [
        (wide, jnp.float32),
        (wide, low),
        (wide, low),
        ((words, width), low),
        ((words, width), low),
        (wide, low),
        ((3, width), jnp.float32),
    ] + [((tokens, share), low)] * count
    return pl.pallas_call(
        body,
        in_specs=[in_smem()] + [in_vmem()] * (count + 11),
        out_shape=[jax.ShapeDtypeStruct(*item) for item in shapes],
        scratch_shapes=[pltpu.VMEM(wide, low)],
        compiler_params=pltpu.CompilerParams(vmem_limit_bytes=40 * 2**20),
        cost_estimate=cheap,
        name="cross_back",
    )(place, *terms, grad, rows, normed, inverse, branch, cq, ck, cv, c_out, c_query, w_out)


def outer_halves(place, pairs, parts, name):
    width = pairs[0][1].shape[1]
    high = [left[0].shape[1] * len(left) for left, _ in pairs]
    size = high[0] // parts
    tokens = [right.shape[0] for _, right in pairs]
    flat = [array for left, right in pairs for array in (*left, right)]
    amount = len(pairs)

    def body(place_ref, *refs):
        ins, (kept, given), (held, sems) = refs[: len(flat)], refs[len(flat) :][:2], refs[-2:]
        turned = refs[len(flat) + 2 : -2]
        me, core = place_ref[0], place_ref[1]
        cursor = 0
        for i, (left, right) in enumerate(pairs):
            for k in range(len(left)):
                piece = ins[cursor + k][...].astype(jnp.float32).T.astype(low)
                rows = piece.shape[0]
                if len(left) == 1:
                    turned[i][...] = piece
                else:
                    rank = lax.rem(me + k, len(left))
                    turned[i][pl.ds(pl.multiple_of(rank * rows, 32), rows), :] = piece
            right_ref = ins[cursor + len(left)]
            cursor += len(left) + 1
            for part in range(parts):
                at = i * parts + part
                tile = dot(turned[i][part * size : (part + 1) * size, :], right_ref[...])
                held[at] = tile.astype(low)
                for out, side in ((kept, 0), (given, 1)):

                    @pl.when((core ^ (i & 1)) == side)
                    def _():
                        pltpu.make_async_copy(
                            held.at[at], out.at[i // 2, part], sems.at[at]
                        ).start()

        for at in range(amount * parts):
            pltpu.make_async_copy(held.at[at], kept.at[0, 0], sems.at[at]).wait()

    out = jax.ShapeDtypeStruct((amount // 2, parts, size, width), low)
    return pl.pallas_call(
        body,
        in_specs=[in_smem()] + [in_vmem()] * len(flat),
        out_specs=[pl.BlockSpec(memory_space=pl.ANY)] * 2,
        out_shape=[out, out],
        scratch_shapes=[pltpu.VMEM((high[i], tokens[i]), low) for i in range(amount)]
        + [
            pltpu.VMEM((amount * parts, size, width), low),
            pltpu.SemaphoreType.DMA((amount * parts,)),
        ],
        compiler_params=pltpu.CompilerParams(vmem_limit_bytes=48 * 2**20),
        cost_estimate=cheap,
        name=name,
    )(place, *flat)


def mlp_grads(grad_pres, acts, rows_in, grads_in):
    pieces, rights = len(acts), len(rows_in)
    tokens, width = rows_in[0].shape
    hidden = acts[0].shape[1]
    chunk = 384 if hidden % 384 == 0 else hidden
    steps = hidden // chunk

    def body(*refs):
        step = pl.program_id(0)
        out = refs[-1]

        def terms(lefts, turn, others):
            here = pl.ds(pl.multiple_of(turn * chunk, chunk), chunk)
            total = jnp.zeros((chunk, width), jnp.float32)
            cursor = 0
            for left in lefts:
                for i in range(left.shape[0] // tokens):
                    total += dot(left[i * tokens : (i + 1) * tokens, here], others[cursor][...], tn)
                    cursor += 1
            out[...] = total.astype(low)

        @pl.when(step < steps)
        def _():
            terms(refs[:pieces], step, refs[2 * pieces : 2 * pieces + rights])

        @pl.when(step >= steps)
        def _():
            terms(refs[pieces : 2 * pieces], step - steps, refs[2 * pieces + rights : -1])

    arrays = (*grad_pres, *acts, *rows_in, *grads_in)
    return pl.pallas_call(
        body,
        grid=(2 * steps,),
        in_specs=[pl.BlockSpec(array.shape, lambda s: (0, 0)) for array in arrays],
        out_specs=pl.BlockSpec((chunk, width), lambda s: (s, 0)),
        out_shape=jax.ShapeDtypeStruct((2 * hidden, width), low),
        compiler_params=pltpu.CompilerParams(vmem_limit_bytes=48 * 2**20),
        cost_estimate=cheap,
        name="mlp_grads",
    )(*arrays)


def ranked_terms(place, lefts, order, weight, start, factors, name):
    tokens, width = factors[0].shape
    count = len(factors)
    depth = lefts[0].shape[1]

    def body(place_ref, *refs):
        ins, weight_ref = refs[: len(lefts)], refs[len(lefts)]
        others = refs[len(lefts) + 1 : len(lefts) + 1 + count]
        out, sums = refs[-2:]
        me = place_ref[0]
        cursor = 0
        for left in ins:
            for i in range(left.shape[0] // tokens):
                slot = order[cursor]
                rank = lax.rem(me - slot + count, count)
                for cut in cuts_of(width):
                    term = dot(
                        left[i * tokens : (i + 1) * tokens, :], weight_ref[start : start + depth, cut]
                    )
                    out[rank, :, cut] = term.astype(low)
                    one = jnp.sum(term, axis=0, keepdims=True)
                    two = jnp.sum(
                        term * others[cursor][:, cut].astype(jnp.float32), axis=0, keepdims=True
                    )
                    if cursor:
                        one, two = one + sums[0:1, cut], two + sums[1:2, cut]
                    sums[0:1, cut], sums[1:2, cut] = one, two
                cursor += 1

    return pl.pallas_call(
        body,
        in_specs=[in_smem()] + [in_vmem()] * (len(lefts) + 1 + count),
        out_shape=[
            jax.ShapeDtypeStruct((count, tokens, width), low),
            jax.ShapeDtypeStruct((2, width), jnp.float32),
        ],
        compiler_params=pltpu.CompilerParams(vmem_limit_bytes=40 * 2**20),
        cost_estimate=cheap,
        name=name,
    )(place, *lefts, weight, *factors)


def update_slots(master, first_moment, second_moment, filled, which, position, sources):
    capacity, unit_rows, width = master.shape

    group = math.gcd(capacity, 2)
    steps = capacity // group

    def body(filled_ref, which_ref, position_ref, weight, one, two, *rest):
        ins = rest[: len(sources)]
        new_one, new_two, new_weight, held, sems = rest[len(sources) :]
        step = pl.program_id(0)

        def fetch(turn):
            for i in range(group):
                slot = turn * group + i
                for source, ref in enumerate(ins):

                    @pl.when(which_ref[slot] == source)
                    def _():
                        pltpu.make_async_copy(
                            ref.at[position_ref[slot]], held.at[turn % 2, i], sems.at[turn % 2, i]
                        ).start()

        @pl.when(step == 0)
        def _():
            fetch(step)

        @pl.when(step < steps - 1)
        def _():
            fetch(step + 1)

        for i in range(group):
            pltpu.make_async_copy(
                ins[0].at[0], held.at[step % 2, i], sems.at[step % 2, i]
            ).wait()
            mask = (filled_ref[step * group + i] > 0).astype(jnp.float32)
            grad = held[step % 2, i].astype(jnp.float32)
            results = adamw(weight[i], one[i], two[i], grad, mask, rate)
            new_one[i], new_two[i], new_weight[i] = results

    block = pl.BlockSpec((group, unit_rows, width), lambda s, *_: (s, 0, 0))
    return pl.pallas_call(
        body,
        grid_spec=pltpu.PrefetchScalarGridSpec(
            num_scalar_prefetch=3,
            grid=(steps,),
            in_specs=[block] * 3 + [pl.BlockSpec(memory_space=pl.ANY)] * len(sources),
            out_specs=[block] * 3,
            scratch_shapes=[
                pltpu.VMEM((2, group, unit_rows, width), low),
                pltpu.SemaphoreType.DMA((2, group)),
            ],
        ),
        out_shape=[jax.ShapeDtypeStruct(master.shape, jnp.float32)] * 3,
        compiler_params=pltpu.CompilerParams(vmem_limit_bytes=56 * 2**20),
        cost_estimate=cheap,
        name="update_slots",
    )(filled, which, position, master, first_moment, second_moment, *sources)


def adamw(weight, moment_one, moment_two, gradient, filled, step_rate):
    new_one = beta_one * moment_one + (1.0 - beta_one) * gradient
    new_two = beta_two * moment_two + (1.0 - beta_two) * gradient * gradient
    fixed_one = new_one / (1.0 - beta_one**STEP)
    fixed_two = new_two / (1.0 - beta_two**STEP)
    updated = weight - step_rate * (fixed_one / (jnp.sqrt(fixed_two) + adam_eps) + decay * weight)
    return (new_one * filled, new_two * filled, updated * filled)


def swap(values, axis, bit):
    count = lax.axis_size(axis)
    return lax.ppermute(values, axis, [(i, i ^ (1 << bit)) for i in range(count)])


def choose(values, index, axis):
    return lax.dynamic_index_in_dim(values, index, axis, keepdims=False)


def total_sum(values):
    for axis in ("dp", "tensor"):
        for bit in range(lax.axis_size(axis).bit_length() - 1):
            values = values + swap(values, axis, bit)
    return values


def pick_units(master, slot_unit, state, kind, place, sizes):
    capacity, unit_rows, width = master.shape
    units = state.shape[0]

    def body(slot_ref, state_ref, kind_ref, place_ref, blocks, *rest):
        outs, (highs, lows, zeros, read, sems) = rest[: len(sizes)], rest[len(sizes) :]

        def start(source, unit):
            for which, out in enumerate(outs):

                @pl.when(kind_ref[unit] == which)
                def _():
                    pltpu.make_async_copy(source, out.at[place_ref[unit]], sems.at[unit]).start()

        @pl.loop(0, capacity)
        def _(slot):
            @pl.when(slot_ref[slot] >= 0)
            def _():
                pltpu.make_async_copy(blocks.at[slot], highs.at[slot], read.at[slot]).start()

        zeros[...] = jnp.zeros_like(zeros)

        @pl.loop(0, units)
        def _(unit):
            @pl.when(state_ref[unit] == 0)
            def _():
                start(zeros, unit)

        @pl.loop(0, capacity)
        def _(slot):
            @pl.when(slot_ref[slot] >= 0)
            def _():
                pltpu.make_async_copy(blocks.at[slot], highs.at[slot], read.at[slot]).wait()
                lows[slot] = highs[slot].astype(low)
                start(lows.at[slot], slot_ref[slot])

        @pl.loop(0, units)
        def _(unit):
            @pl.when(state_ref[unit] < 2)
            def _():
                pltpu.make_async_copy(zeros, outs[0].at[0], sems.at[unit]).wait()

    return pl.pallas_call(
        body,
        grid_spec=pltpu.PrefetchScalarGridSpec(
            num_scalar_prefetch=4,
            grid=(1,),
            in_specs=[pl.BlockSpec(memory_space=pl.ANY)],
            out_specs=[pl.BlockSpec(memory_space=pl.ANY)] * len(sizes),
            scratch_shapes=[
                pltpu.VMEM((capacity, unit_rows, width), jnp.float32),
                pltpu.VMEM((capacity, unit_rows, width), low),
                pltpu.VMEM((unit_rows, width), low),
                pltpu.SemaphoreType.DMA((capacity,)),
                pltpu.SemaphoreType.DMA((units,)),
            ],
        ),
        out_shape=[jax.ShapeDtypeStruct((size, unit_rows, width), low) for size in sizes],
        compiler_params=pltpu.CompilerParams(vmem_limit_bytes=56 * 2**20),
        cost_estimate=cheap,
        name="pick_units",
    )(slot_unit, state, kind, place, master)


def place_blocks(sources, which, position, parts=1):
    amount = which.shape[0]
    shape = sources[0].shape[1:]
    size = amount // parts

    def body(which_ref, position_ref, *rest):
        ins, outs = rest[: len(sources)], rest[len(sources) : len(sources) + parts]
        held, read, sems = rest[len(sources) + parts :]

        @pl.loop(0, amount)
        def _(i):
            for source, ref in enumerate(ins):

                @pl.when(which_ref[i] == source)
                def _():
                    pltpu.make_async_copy(ref.at[position_ref[i]], held.at[i], read.at[i]).start()

        for part, out in enumerate(outs):

            @pl.loop(0, size)
            def _(j):
                i = part * size + j
                pltpu.make_async_copy(ins[0].at[0], held.at[i], read.at[i]).wait()
                pltpu.make_async_copy(held.at[i], out.at[j], sems.at[i]).start()

        @pl.loop(0, amount)
        def _(i):
            pltpu.make_async_copy(held.at[i], outs[0].at[0], sems.at[i]).wait()

    return pl.pallas_call(
        body,
        grid_spec=pltpu.PrefetchScalarGridSpec(
            num_scalar_prefetch=2,
            grid=(1,),
            in_specs=[pl.BlockSpec(memory_space=pl.ANY)] * len(sources),
            out_specs=[pl.BlockSpec(memory_space=pl.ANY)] * parts,
            scratch_shapes=[
                pltpu.VMEM((amount,) + shape, low),
                pltpu.SemaphoreType.DMA((amount,)),
                pltpu.SemaphoreType.DMA((amount,)),
            ],
        ),
        out_shape=[jax.ShapeDtypeStruct((size,) + shape, low)] * parts,
        compiler_params=pltpu.CompilerParams(vmem_limit_bytes=56 * 2**20),
        cost_estimate=cheap,
        name="place_blocks",
    )(which, position, *sources)


def hops(values, step, turn):
    count = lax.axis_size("tensor")
    if step > 0:
        pairs = [(i, i + 1) for i in range(turn - 1, count - 1)]
    else:
        pairs = [(i, i - 1) for i in range(1, count - turn + 1)]
    return lax.ppermute(values, "tensor", pairs)


def slots_of(own, ups, downs):
    count = lax.axis_size("tensor")
    me = lax.axis_index("tensor")
    return [own] + [jnp.where(me >= k, ups[k - 1], downs[count - k - 1]) for k in range(1, count)]


fence = lax.optimization_barrier


def in_pool(member, inner, inner_count):
    me = lax.axis_index("dp")
    half, core = member >> 3, ((member >> 2) & 1) ^ (me & 1)
    far_y, far_x = ((member >> 1) & 1) ^ ((me >> 2) & 1), (member & 1) ^ ((me >> 1) & 1)
    where_first = (far_y * 2 + far_x) * inner_count
    where_second = (4 + far_x * 2 + far_y) * inner_count
    return (core, jnp.where(half == 0, where_first, where_second) + inner)


def on_device(
    hidden_in,
    time_embed,
    caption_table,
    caption_ids,
    owners,
    master,
    first_moment,
    second_moment,
    mod_table,
    mod_first,
    mod_second,
    out_grad,
):
    count = lax.axis_size("tensor")
    dp_count = lax.axis_size("dp")
    me_dp = lax.axis_index("dp")
    me_tensor = lax.axis_index("tensor")
    capacity, unit_rows, width = master.shape
    units = owners.shape[0]
    tokens = hidden_in.shape[1]
    text_count = caption_ids.shape[1]
    share = width // count
    per = share // unit_rows
    ups = (units - 8 * per) // 2
    rank_of = ranks_of(owners)
    mine = owners == me_dp
    match = (rank_of[None, :] == jnp.arange(capacity)[:, None]) & mine[None, :]
    filled = jnp.any(match, axis=1)
    unit_of_slot = jnp.sum(jnp.where(match, jnp.arange(units)[None, :], 0), axis=1)

    square = [list(range(i * per, (i + 1) * per)) for i in range(8)]
    group_attn = square[0] + square[1] + square[2] + square[5]
    group_full = square[3] + square[4] + square[6] + square[7]
    group_mlp = list(range(8 * per, units))
    members = len(group_attn)
    plane = dp_count == 8 and members == 16 and len(group_mlp) % dp_count == 0
    member_of = np.zeros(units, np.int32)
    member_of[group_attn] = np.arange(members)
    member_of[group_full] = np.arange(members)
    is_attn = np.zeros(units, bool)
    is_attn[group_attn] = True
    is_mlp = np.zeros(units, bool)
    is_mlp[group_mlp] = True

    latent_in = hidden_in[0].astype(jnp.float32)
    modulate = mod_table + time_embed[0]

    def mod_row(which_row):
        return modulate[which_row][None, :]

    normed_one, inverse_one = layer_norm(latent_in)
    bits = dp_count.bit_length() - 1
    vocab_rows = caption_table.shape[0]

    def caption_terms(ids):
        chosen = ids.reshape(-1) - me_dp * vocab_rows
        onehot = (chosen[:, None] == jnp.arange(vocab_rows)[None, :]).astype(low)
        terms = jnp.dot(onehot, caption_table, preferred_element_type=jnp.float32).astype(low)
        return terms.reshape(dp_count, text_count, -1)

    def modulated(normed):
        return (normed.astype(jnp.float32) * (1.0 + mod_row(1)) + mod_row(0)).astype(low)

    def split_attn(w_attn):
        rows = w_attn.reshape(-1, width)
        return (rows[: 3 * share], rows[3 * share :])

    def whole_text(text_ring):
        return from_ring(text_ring, -1).transpose(1, 0, 2).reshape(text_count, width)

    def own_keys(text_ring, c_key):
        return project(whole_text(text_ring), c_key).astype(low)

    n_low = normed_one.astype(low)
    if plane:
        core, far_x, far_y = (
            ((member_of >> 2) & 1) ^ (me_dp & 1),
            (member_of & 1) ^ ((me_dp >> 1) & 1),
            ((member_of >> 1) & 1) ^ ((me_dp >> 2) & 1),
        )
        place = jnp.where(is_attn, far_x * 4 + far_y * 2, 8 + far_y * 4 + far_x * 2)
        place = jnp.where(is_mlp, np.arange(units) - 8 * per, place + (member_of >> 3))
        kind = jnp.where(is_mlp, 0, core)
        slot_mlp = unit_of_slot >= 8 * per
        owned_state = mine.astype(jnp.int32)
        up, down = hops(n_low, 1, 1), hops(n_low, -1, 1)
        kept, given = pick_units(
            master,
            jnp.where(filled & ~slot_mlp, unit_of_slot, -1),
            jnp.where(is_mlp, 2, owned_state),
            kind,
            place,
            (members, members),
        )
        got = swap(given, "dp", 0)
        ids = jnp.concatenate([caption_ids, swap(caption_ids, "dp", 0)])
        n_up, n_down = [up], [down]
        kept, got, up, down, ids = fence((kept, got, up, down, ids))
        pieces = [kept[i : i + 4] + got[i : i + 4] for i in range(0, members, 4)]
        attn_two, attn_send, full_two, full_send = fence(tuple(pieces))
        up, down = hops(up, 1, 2), hops(down, -1, 2)
        attn_got = swap(attn_send, "dp", 1)
        full_got = swap(full_send, "dp", 2)
        ids = jnp.concatenate([ids, swap(ids, "dp", 1)])
        (mlp_part,) = pick_units(
            fence((master, got))[0],
            jnp.where(filled & slot_mlp, unit_of_slot, -1),
            jnp.where(is_mlp, owned_state, 2),
            kind,
            place,
            (len(group_mlp),),
        )
        n_up.append(up), n_down.append(down)
        attn_two, attn_got, full_two, full_got, up, down, ids, mlp_part = fence(
            (attn_two, attn_got, full_two, full_got, up, down, ids, mlp_part)
        )
        pieces = [x[i : i + 2] + y[i : i + 2] for x, y in ((attn_two, attn_got), (full_two, full_got)) for i in (0, 2)]
        attn_one, attn_send, full_one, full_send = fence(tuple(pieces))
        up, down = hops(up, 1, 3), hops(down, -1, 3)
        attn_got = swap(attn_send, "dp", 2)
        full_got = swap(full_send, "dp", 1)
        ids = jnp.concatenate([ids, swap(ids, "dp", 2)])
        n_up.append(up), n_down.append(down)
        attn_one, attn_got, full_one, full_got, up, down, ids, mlp_part = fence(
            (attn_one, attn_got, full_one, full_got, up, down, ids, mlp_part)
        )
        attn_one, full_one = attn_one + attn_got, full_one + full_got
        mlp_part = lax.psum_scatter(mlp_part, "dp", scatter_dimension=0, tiled=True)
        first = jnp.concatenate([attn_one[0:1], swap(attn_one[0:1], "dp", 1)])
        second = jnp.concatenate([attn_one[1:2], swap(attn_one[1:2], "dp", 2)])
        up, down = hops(full_one, 1, 1), hops(full_one, -1, 1)
        text = caption_terms(ids)
        text = text[0:4] + swap(text[4:8], "dp", 2)
        f_up, f_down = [up], [down]
        first, second, up, down, text = fence((first, second, up, down, text))
        pool = jnp.concatenate([first, swap(first, "dp", 2), second, swap(second, "dp", 1)])
        up, down = hops(up, 1, 2), hops(down, -1, 2)
        text = text[0:2] + swap(text[2:4], "dp", 1)
        f_up.append(up), f_down.append(down)
        pool, up, down, text = fence((pool, up, down, text))
        other = swap(pool, "dp", 0)
        up, down = hops(up, 1, 3), hops(down, -1, 3)
        text = text[0] + swap(text[1], "dp", 0)
        f_up.append(up), f_down.append(down)
        grad_own = out_grad[0]
        pool, other, up, down, text, grad_own = fence((pool, other, up, down, text, grad_own))
        f_up[-1], f_down[-1] = up, down
        (w_attn,) = place_blocks((pool, other), *in_pool(np.arange(members), 0, 1))
        grad_whole = lax.all_gather(grad_own, "tensor", axis=0)
        full_ring = slots_of(full_one, f_up, f_down)
        first = jnp.concatenate([item[0:1] for item in full_ring])
        second = jnp.concatenate([item[1:2] for item in full_ring])
        first_got = swap(first, "dp", 1)
        second_got = swap(second, "dp", 2)
        text_ring = jnp.stack(ring(text))
        first = jnp.concatenate([first, first_got])
        second = jnp.concatenate([second, second_got])
        n_slots = slots_of(n_low, n_up, n_down)
        normed_all = jnp.concatenate(n_slots)
        h_one_all = modulated(normed_all)
        w_qkv, c_key = split_attn(w_attn)
        qkv = project(h_one_all, w_qkv).astype(low)
        first, second, text_ring, qkv = fence((first, second, text_ring, qkv))
        first_far, second_far = swap(first, "dp", 2), swap(second, "dp", 1)
        first_other, second_other = swap(first, "dp", 0), swap(second, "dp", 0)
        attended = self_attend(qkv)
        ck_own = own_keys(text_ring, c_key)
        first_far, second_far, first_other, second_other, attended, ck_own = fence(
            (first_far, second_far, first_other, second_other, attended, ck_own)
        )
        first_last, second_last = swap(first_far, "dp", 0), swap(second_far, "dp", 0)
        mlp_part = fence((mlp_part, first_far))[0]
        w_mlp = lax.all_gather(mlp_part, "dp", axis=0, tiled=True)
        listing = np.arange(count * members)
        matrix, rank, head = listing // (count * per), listing // per % count, listing % per
        slot = lax.rem(me_tensor - rank + count, count)
        which, position = in_pool(matrix * per + head, slot, count)
        blocks = 2 * count
        w_full = place_blocks(
            (first, first_far, second, second_far, first_other, first_last, second_other, second_last),
            which * 4 + position // blocks,
            position % blocks,
            parts=4,
        )
        w_full = [part.reshape(width, width) for part in w_full]
    else:
        slots_low = master.astype(low)
        rows = jnp.take(slots_low, rank_of, axis=0, mode="clip")
        rows = lax.psum(jnp.where(mine[:, None, None], rows, jnp.zeros((), low)), "dp")
        w_attn = rows[np.array(group_attn)]
        w_full = lax.all_gather(rows[np.array(group_full)], "tensor", axis=0)
        w_full = w_full.reshape(count, 4, share, width).swapaxes(0, 1).reshape(4, width, width)
        w_full = [w_full[i] for i in range(4)]
        w_mlp = rows[8 * per :]
        n_slots = ring(n_low)
        normed_all = jnp.concatenate(n_slots)
        grad_whole = lax.all_gather(out_grad[0], "tensor", axis=0)
        ids = caption_ids
        for bit in range(bits):
            ids = jnp.concatenate([ids, swap(ids, "dp", bit)])
        text = caption_terms(ids)
        for bit in reversed(range(bits)):
            text = text[: 1 << bit] + swap(text[1 << bit :], "dp", bit)
        text_ring = jnp.stack(ring(text[0]))
        h_one_all = modulated(normed_all)
        w_qkv, c_key = split_attn(w_attn)
        qkv = project(h_one_all, w_qkv).astype(low)
        attended = self_attend(qkv)
        ck_own = own_keys(text_ring, c_key)
    w_cross = w_full
    w_out, c_query, c_value, c_out = w_full
    w_mlp = w_mlp.reshape(-1, width)
    w_down = w_mlp[w_mlp.shape[0] // 2 :]
    text_low = whole_text(text_ring)

    mixed_parts = attended.reshape(count, tokens, share)
    mixed = [mixed_parts[0]] + [shift(mixed_parts[k], count - k) for k in range(1, count)]
    where = jnp.stack([me_tensor, me_dp & 1]).astype(jnp.int32)
    rows = jnp.concatenate([mod_row(2), mod_row(3), mod_row(4)])
    (
        branch_one,
        first_low,
        cq_rows,
        ck_rows,
        cv_rows,
        crossed,
        second_res,
        normed_two,
        inverse_two,
        h_two,
    ) = cross_block(
        where, mixed, hidden_in[0], rows, jnp.stack(ring(ck_own)), text_low, *w_cross
    )

    h_slots = ring(h_two)
    out_slots = [
        choose(grad_whole, lax.rem(me_tensor - k + count, count), 0) for k in range(count)
    ]
    grad_slots = [(mod_row(5) * item.astype(jnp.float32)).astype(low) for item in out_slots]
    near = [k for k in range(1, count) if 2 * k != count]
    far = [k for k in range(1, count) if 2 * k == count]
    acts, grad_pres, grad_terms, order = [], [], [], []
    for members_now in ([0], near, far):
        held = [h_slots[k] for k in members_now]
        if acts:
            held = fence((held, acts[-1]))[0]
        act, grad_pre, *terms = mlp_core(held, [grad_slots[k] for k in members_now], w_mlp)
        acts.append(act), grad_pres.append(grad_pre)
        order += members_now
        grad_terms += [
            shift(term, count - k) if k else term for k, term in zip(members_now, terms)
        ]
    mlp_grad = mlp_grads(
        grad_pres, acts, [h_slots[k] for k in order], [grad_slots[k] for k in order]
    ).reshape(-1, unit_rows, width)
    branch_terms, branch_sums = ranked_terms(
        where, acts, order, w_mlp, w_mlp.shape[0] // 2, [out_slots[k] for k in order], "mlp_out"
    )
    branch_row = branch_sums[1]
    grad_terms, mlp_grad, branch_terms = fence((grad_terms, mlp_grad, branch_terms))
    if plane:
        mlp_sum = lax.psum_scatter(mlp_grad, "dp", scatter_dimension=0, tiled=True)
    branch_two = lax.psum_scatter(
        branch_terms.reshape(-1, width), "tensor", scatter_dimension=0, tiled=True
    )

    (
        first_grad,
        cross_low,
        grad_cq,
        grad_ck,
        grad_cv,
        attn_low,
        row_sums,
        *grad_mixed,
    ) = cross_back(
        where,
        grad_terms,
        out_grad[0],
        rows,
        normed_two,
        inverse_two,
        branch_one,
        cq_rows,
        ck_rows,
        cv_rows,
        c_out,
        c_query,
        w_out,
    )

    grad_parts = [grad_mixed[0]] + [shift(grad_mixed[k], k) for k in range(1, count)]
    full_pairs = [
        (mixed, attn_low),
        ([grad_cq], first_low),
        ([grad_cv], text_low),
        ([crossed], cross_low),
    ]
    grad_ck_parts = to_ring(grad_ck.reshape(text_count, count, share).transpose(1, 0, 2)).astype(low)

    def sum_ck(parts):
        total = grad_ck_parts[0].astype(jnp.float32)
        for k in range(1, count):
            total = total + parts[k - 1].astype(jnp.float32)
        return total.astype(low)

    if plane:
        x_bit, y_bit = (me_dp >> 1) & 1, (me_dp >> 2) & 1

        def split(total, bit, axis):
            return (choose(total, bit, axis), choose(total, 1 - bit, axis))

        kept, given = outer_halves(where, full_pairs, count, "full_grads")
        got = swap(given, "dp", 0)
        grad_parts, kept, got = fence((grad_parts, kept, got))
        box = (2, count, 2, 2, unit_rows, width)
        kept, got = kept.reshape(box), got.reshape(box)
        kept_one = choose(kept[0], x_bit, 2) + choose(got[0], x_bit, 2)
        given_one = choose(kept[0], 1 - x_bit, 2) + choose(got[0], 1 - x_bit, 2)
        kept_two = choose(kept[1], y_bit, 1) + choose(got[1], y_bit, 1)
        given_two = choose(kept[1], 1 - y_bit, 1) + choose(got[1], 1 - y_bit, 1)
        kept_one, given_one, kept_two, given_two, grad_parts = fence(
            (kept_one, given_one, kept_two, given_two, grad_parts)
        )
        got_one, got_two = swap(given_one, "dp", 1), swap(given_two, "dp", 2)
        ck_parts = [shift(grad_ck_parts[k], k) for k in range(1, count)]
        grad_qkv = self_attend_back(qkv, jnp.concatenate(grad_parts, axis=0))
        kept_one, got_one, kept_two, got_two, ck_parts, grad_qkv, mlp_sum, branch_two = fence(
            (kept_one, got_one, kept_two, got_two, ck_parts, grad_qkv, mlp_sum, branch_two)
        )
        mlp_sum = lax.all_gather(mlp_sum, "dp", axis=0, tiled=True)
        kept_one, given_one = split(kept_one + got_one, y_bit, 1)
        kept_two, given_two = split(kept_two + got_two, x_bit, 1)
        got_one, got_two = swap(given_one, "dp", 2), swap(given_two, "dp", 1)
        attn_pairs = [([grad_qkv[:, i * share : (i + 1) * share]], h_one_all) for i in range(3)]
        attn_pairs.append(([sum_ck(ck_parts)], text_low))
        attn_kept, attn_given = outer_halves(where, attn_pairs, 1, "attn_grads")
        attn_got = swap(attn_given, "dp", 0)
        grad_h_terms, grad_h_sums = ranked_terms(
            where, [grad_qkv], range(count), w_attn.reshape(-1, width), 0, n_slots, "attn_terms"
        )
        mod_terms = jnp.concatenate([grad_h_sums, row_sums, branch_row[None]])
        for bit in range(3):
            mod_terms = mod_terms + swap(mod_terms, "dp", bit)
        grad_h_one = lax.psum_scatter(
            grad_h_terms.reshape(-1, width), "tensor", scatter_dimension=0, tiled=True
        )
        kept_one, got_one, kept_two, got_two, attn_kept, attn_got, mod_terms = fence(
            (kept_one, got_one, kept_two, got_two, attn_kept, attn_got, mod_terms)
        )
        full_parts = jnp.stack([kept_one + got_one, kept_two + got_two], axis=1)
        full_parts = to_ring(full_parts)
        full_got = [shift(full_parts[k], k) for k in range(1, count)]
        attn_all = (attn_kept + attn_got).reshape(2, 2, 2, unit_rows, width)
        one_kept, one_given = split(attn_all[0], x_bit, 1)
        two_kept, two_given = split(attn_all[1], y_bit, 0)
        one_got, two_got = swap(one_given, "dp", 1), swap(two_given, "dp", 2)
        full_own = full_parts[0]
        full_own, full_got, one_kept, one_got, two_kept, two_got = fence(
            (full_own, full_got, one_kept, one_got, two_kept, two_got)
        )
        full_sum = full_own.astype(jnp.float32)
        for part in full_got:
            full_sum = full_sum + part.astype(jnp.float32)
        full_sum = full_sum.astype(low)
        one_kept, one_given = split(one_kept + one_got, y_bit, 0)
        two_kept, two_given = split(two_kept + two_got, x_bit, 0)
        one_got, two_got = swap(one_given, "dp", 2), swap(two_given, "dp", 1)
        one_kept, one_got, two_kept, two_got, full_sum = fence(
            (one_kept, one_got, two_kept, two_got, full_sum)
        )
        first = jnp.stack([one_kept + one_got, full_sum[0]])
        second = jnp.stack([two_kept + two_got, full_sum[1]])
        first_got, second_got = swap(first, "dp", 1), swap(second, "dp", 2)
        first = jnp.concatenate([first, first_got])
        second = jnp.concatenate([second, second_got])
        first, second = fence((first, second))
        first_far, second_far = swap(first, "dp", 2), swap(second, "dp", 1)
        first, first_far, second, second_far, grad_h_one = fence(
            (first, first_far, second, second_far, grad_h_one)
        )
        pool = jnp.concatenate([first, first_far, second, second_far])
        other = swap(pool, "dp", 0)
        mod_terms = mod_terms + swap(mod_terms, "tensor", 0)
        pool, other, mod_terms = fence((pool, other, mod_terms))
        for bit in range(1, count.bit_length() - 1):
            mod_terms = mod_terms + swap(mod_terms, "tensor", bit)
        mod_grad = mod_terms
        which, position = in_pool(member_of, np.where(is_attn, 0, 1), 2)
        which = jnp.where(is_mlp, 2, which)
        position = jnp.where(is_mlp, np.arange(units) - 8 * per, position)
        own = jnp.sum(jnp.where(match[:, :, None], jnp.stack([which, position], 1)[None], 0), axis=1)
        new_first, new_second, new_master = update_slots(
            master,
            first_moment,
            second_moment,
            filled.astype(jnp.int32),
            own[:, 0],
            own[:, 1],
            (pool, other, mlp_sum),
        )
    else:
        grad_qkv = self_attend_back(qkv, jnp.concatenate(grad_parts, axis=0))
        grad_c_key = sum_ck([shift(grad_ck_parts[k], k) for k in range(1, count)])
        grad_c_key = outer(grad_c_key, text_low).astype(low)
        attn_grads = [outer(grad_qkv, h_one_all).astype(low), grad_c_key]
        grad_h_terms, grad_h_sums = ranked_terms(
            where, [grad_qkv], range(count), w_attn.reshape(-1, width), 0, n_slots, "attn_terms"
        )
        grad_h_one = lax.psum_scatter(
            grad_h_terms.reshape(-1, width), "tensor", scatter_dimension=0, tiled=True
        )
        mixed_all = from_ring(jnp.stack(mixed), 1).transpose(1, 0, 2).reshape(tokens, width)
        full_grads = [outer(mixed_all, attn_low)]
        full_grads += [outer(left[0], right) for left, right in full_pairs[1:]]
        full_sum = [g.astype(low).reshape(count, share, width) for g in full_grads]
        full_sum = jnp.stack(full_sum, axis=1)
        full_sum = lax.psum_scatter(full_sum, "tensor", scatter_dimension=0, tiled=True)
        order = np.array(group_attn + group_full + group_mlp)
        sums = jnp.concatenate(
            [jnp.concatenate(attn_grads), full_sum.reshape(-1, width), mlp_grad.reshape(-1, width)]
        )
        sums = lax.psum(sums.reshape(units, unit_rows, width), "dp")
        owned = jnp.take(sums, jnp.array(np.argsort(order))[unit_of_slot], axis=0, mode="clip")
        mod_grad = total_sum(jnp.concatenate([grad_h_sums, row_sums, branch_row[None]]))
        new_first, new_second, new_master = adamw(
            master,
            first_moment,
            second_moment,
            owned.astype(jnp.float32),
            filled.astype(jnp.float32)[:, None, None],
            rate,
        )
    branch_two, second_res, grad_h_one, new_first = fence(
        (branch_two, second_res, grad_h_one, new_first)
    )
    grad_h_one = grad_h_one.astype(jnp.float32)
    block_out = second_res + mod_row(5) * branch_two.astype(jnp.float32)
    input_grad = first_grad + norm_back(grad_h_one, normed_one, inverse_one, mod_row(1))
    mod_new_first, mod_new_second, mod_new = adamw(
        mod_table, mod_first, mod_second, mod_grad, 1.0, table_rate
    )
    return (
        block_out[None],
        input_grad[None],
        new_first,
        new_second,
        new_master,
        mod_new_first,
        mod_new_second,
        mod_new,
    )


def solution(mesh):
    in_specs = (
        P("dp", "tensor", None),
        P("dp", None, None),
        P("dp", "tensor"),
        P("dp", None),
        P(),
        P("dp", "tensor", None),
        P("dp", "tensor", None),
        P("dp", "tensor", None),
        P(),
        P(),
        P(),
        P("dp", "tensor", None),
    )
    out_specs = (
        P("dp", "tensor", None),
        P("dp", "tensor", None),
        P("dp", "tensor", None),
        P("dp", "tensor", None),
        P("dp", "tensor", None),
        P(),
        P(),
        P(),
    )
    return jax.shard_map(
        on_device, mesh=mesh, in_specs=in_specs, out_specs=out_specs, check_vma=False
    )
```

```python
import math

import jax
import jax.numpy as jnp
import numpy as np
from jax import lax
from jax.experimental import pallas as pl
from jax.experimental.pallas import tpu as pltpu
from jax.sharding import PartitionSpec as P

HEAD_DIM = 72
STEP = 10


norm_eps = 1e-06
beta_one = 0.9
beta_two = 0.999
rate = 0.03
table_rate = 0.3
decay = 0.01
adam_eps = 1e-08
low = jnp.bfloat16


def ranks_of(owners):
    index = jnp.arange(owners.shape[0])
    before = (owners[None, :] == owners[:, None]) & (index[None, :] < index[:, None])
    return jnp.sum(before.astype(jnp.int32), axis=1)


def layer_norm(values):
    center = values - jnp.mean(values, axis=-1, keepdims=True)
    inverse = lax.rsqrt(jnp.mean(center * center, axis=-1, keepdims=True) + norm_eps)
    return (center * inverse, inverse)


def norm_back(grad_rows, normed, inverse, scale_row):
    scaled = grad_rows * (1.0 + scale_row)
    mean_one = jnp.mean(scaled, axis=-1, keepdims=True)
    mean_two = jnp.mean(scaled * normed, axis=-1, keepdims=True)
    return inverse * (scaled - mean_one - normed * mean_two)


def project(rows, weight):
    return jnp.einsum("ld,rd->lr", rows, weight, preferred_element_type=jnp.float32)


def expand(rows, weight):
    return jnp.einsum("lr,rd->ld", rows, weight, preferred_element_type=jnp.float32)


def outer(left, right):
    return jnp.einsum("lr,ld->rd", left, right, preferred_element_type=jnp.float32)


def shift(values, step):
    count = lax.axis_size("tensor")
    return lax.ppermute(values, "tensor", [(i, (i + step) % count) for i in range(count)])


def ring(values):
    return [values] + [shift(values, k) for k in range(1, lax.axis_size("tensor"))]


def to_ring(stacked):
    count = stacked.shape[0]
    twice = jnp.concatenate([stacked, stacked], axis=0)
    return lax.dynamic_slice_in_dim(twice, lax.axis_index("tensor"), count, 0)


def from_ring(stacked, sign):
    count = stacked.shape[0]
    me = lax.axis_index("tensor")
    place = lax.rem(sign * (jnp.arange(count) - me) + 2 * count, count)
    return jnp.take(stacked, place, axis=0, mode="clip")


cheap = pl.CostEstimate(flops=1000, bytes_accessed=1000, transcendentals=0)
costly = pl.CostEstimate(flops=10**10, bytes_accessed=10**7, transcendentals=0)


def self_attend(qkv, share):
    length = qkv.shape[0]
    rows = min(256, length)

    def body(qkv_ref, out_ref):
        @pl.loop(0, length // rows)
        def _(step):
            here = pl.ds(pl.multiple_of(step * rows, rows), rows)
            parts = []
            for at in range(0, share, HEAD_DIM):
                q = qkv_ref[here, at : at + HEAD_DIM]
                k = qkv_ref[:, share + at : share + at + HEAD_DIM]
                v = qkv_ref[:, 2 * share + at : 2 * share + at + HEAD_DIM]
                probs = softmax_keys(k, q).astype(low)
                parts.append(dot(v, probs, tn).T)
            out_ref[here, :] = jnp.concatenate(parts, axis=1).astype(low)

    return pl.pallas_call(
        body,
        out_shape=jax.ShapeDtypeStruct((length, share), low),
        compiler_params=pltpu.CompilerParams(vmem_limit_bytes=32 * 2**20),
        cost_estimate=cheap,
        name="self_attend",
    )(qkv)


def self_attend_back(qkv, grads, share, begin, end):
    length = qkv.shape[0]
    rows = length // len(grads)
    span = end - begin
    scale = HEAD_DIM ** (-0.5)

    def body(qkv_ref, *refs):
        grad_refs, (out_ref, grad_k, grad_v) = refs[: len(grads)], refs[len(grads) :]
        for step, grad_ref in enumerate(grad_refs):
            here = slice(step * rows, (step + 1) * rows)
            parts = []
            for head, at in enumerate(range(begin, end, HEAD_DIM)):
                q = qkv_ref[here, at : at + HEAD_DIM]
                k = qkv_ref[:, share + at : share + at + HEAD_DIM]
                v = qkv_ref[:, 2 * share + at : 2 * share + at + HEAD_DIM]
                g = grad_ref[0:rows, at : at + HEAD_DIM]
                probs = softmax_keys(k, q)
                grad_probs = dot(v, g, nt)
                inner = jnp.sum(probs * grad_probs, axis=0, keepdims=True)
                grad_scores = (probs * (grad_probs - inner)).astype(low)
                to_v = dot(probs.astype(low), g)
                to_k = dot(grad_scores, q)
                if step:
                    grad_v[head] += to_v
                    grad_k[head] += to_k
                else:
                    grad_v[head] = to_v
                    grad_k[head] = to_k
                parts.append((dot(k, grad_scores, tn) * scale).T)
            out_ref[here, 0:span] = jnp.concatenate(parts, axis=1).astype(low)
        heads = range(span // HEAD_DIM)
        both = [grad_k[head] * scale for head in heads]
        out_ref[:, span : 2 * span] = jnp.concatenate(both, axis=1).astype(low)
        both = [grad_v[head] for head in heads]
        out_ref[:, 2 * span :] = jnp.concatenate(both, axis=1).astype(low)

    return pl.pallas_call(
        body,
        out_shape=jax.ShapeDtypeStruct((length, 3 * span), low),
        scratch_shapes=[pltpu.VMEM((span // HEAD_DIM, length, HEAD_DIM), jnp.float32)] * 2,
        compiler_params=pltpu.CompilerParams(vmem_limit_bytes=40 * 2**20),
        cost_estimate=cheap,
        name="self_attend_back",
    )(qkv, *grads)


def mlp_core(rows_in, grads_in, w_mlp):
    groups = len(rows_in)
    tokens, width = rows_in[0].shape
    hidden = w_mlp.shape[0] // 2
    chunk = 384 if hidden % 384 == 0 else hidden
    steps = hidden // chunk
    curve = 0.7978845608028654

    def body(*refs):
        rows, grads = refs[:groups], refs[groups : 2 * groups]
        up, down = refs[2 * groups : 2 * groups + 2]
        act, grad_pre = refs[2 * groups + 2 : 2 * groups + 4]
        outs = refs[2 * groups + 4 : 3 * groups + 4]
        total = refs[-1]
        step = pl.program_id(0)
        for i in range(groups):
            pre = lax.dot_general(
                rows[i][...], up[...], (((1,), (1,)), ((), ())), preferred_element_type=jnp.float32
            )
            square = pre * pre
            bend = jnp.tanh(curve * pre * (1.0 + 0.044715 * square))
            half = 0.5 * (1.0 + bend)
            here = pl.ds(i * tokens, tokens)
            act[here, :] = (pre * half).astype(low)
            slope = half + (0.5 * curve) * pre * (1.0 - bend * bend) * (1.0 + 0.134145 * square)
            grad_act = lax.dot_general(
                grads[i][...], down[...], (((1,), (1,)), ((), ())), preferred_element_type=jnp.float32
            )
            grad_low = (grad_act * slope).astype(low)
            grad_pre[here, :] = grad_low
            term = jnp.dot(grad_low, up[...], preferred_element_type=jnp.float32)

            @pl.when(step == 0)
            def _():
                total[here, :] = term

            @pl.when(step > 0)
            def _():
                total[here, :] += term

            @pl.when(step == steps - 1)
            def _():
                outs[i][...] = total[here, :].astype(low)

    whole = pl.BlockSpec((tokens, width), lambda s: (0, 0))
    across = pl.BlockSpec((groups * tokens, chunk), lambda s: (0, s))
    return pl.pallas_call(
        body,
        grid=(steps,),
        in_specs=[whole] * (2 * groups)
        + [
            pl.BlockSpec((chunk, width), lambda s: (s, 0)),
            pl.BlockSpec((chunk, width), lambda s: (steps + s, 0)),
        ],
        out_specs=[across, across] + [whole] * groups,
        out_shape=[jax.ShapeDtypeStruct((groups * tokens, hidden), low)] * 2
        + [jax.ShapeDtypeStruct((tokens, width), low)] * groups,
        scratch_shapes=[pltpu.VMEM((groups * tokens, width), jnp.float32)],
        compiler_params=pltpu.CompilerParams(vmem_limit_bytes=40 * 2**20),
        cost_estimate=cheap,
        name="mlp_core",
    )(*rows_in, *grads_in, w_mlp, w_mlp)


nt = (((1,), (1,)), ((), ()))
tn = (((0,), (0,)), ((), ()))


def dot(left, right, dims=(((1,), (0,)), ((), ()))):
    return lax.dot_general(left, right, dims, preferred_element_type=jnp.float32)


def softmax_keys(keys, queries):
    scores = dot(keys, queries, nt) * HEAD_DIM ** (-0.5)
    expo = jnp.exp(scores - jnp.max(scores, axis=0, keepdims=True))
    return expo * (1.0 / jnp.sum(expo, axis=0, keepdims=True))


def cuts_of(width):
    size = 384 if width % 384 == 0 else width
    return [slice(i, i + size) for i in range(0, width, size)]


def in_smem():
    return pl.BlockSpec(memory_space=pltpu.SMEM)


def in_vmem():
    return pl.BlockSpec(memory_space=pltpu.VMEM)


def cross_block(place, mixed, hidden, rows, text, w_out, c_query, c_value, c_out):
    count, share = len(mixed), mixed[0].shape[1]
    tokens, width = hidden.shape
    words = text.shape[0]
    per = share // HEAD_DIM

    def body(place_ref, *refs):
        parts = refs[:count]
        x_ref, rows_ref, text_ref, wo, wq, wv, wc = refs[count : count + 7]
        branch, res_low, cq, ck, cv, crossed, res, normed, inverse, out, held = refs[count + 7 :]
        me = place_ref[0]
        for cut in cuts_of(width):
            total = jnp.zeros((tokens, cut.stop - cut.start), jnp.float32)
            for k in range(count):
                rank = lax.rem(me + k, count)
                here = pl.ds(pl.multiple_of(rank * share, 32), share)
                total += dot(parts[k][0:tokens, :], wo[here, cut])
            branch[:, cut] = total
            first = x_ref[:, cut].astype(jnp.float32) + rows_ref[0:1, cut] * total
            res[:, cut] = first
            res_low[:, cut] = first.astype(low)
        for cut in cuts_of(width):
            cq[:, cut] = dot(res_low[...], wq[cut, :], nt).astype(low)
            cv[:, cut] = dot(text_ref[...], wv[cut, :], nt).astype(low)
        for k in range(count):
            held[lax.rem(me + k, count)] = parts[k][tokens:, :]
        ck[...] = jnp.concatenate([held[rank] for rank in range(count)], axis=1)
        parts_out = []
        for at in range(0, width, HEAD_DIM):
            head = slice(at, at + HEAD_DIM)
            probs = softmax_keys(ck[:, head], cq[:, head]).astype(low)
            parts_out.append(dot(cv[:, head], probs, tn).T)
        crossed[...] = jnp.concatenate(parts_out, axis=1).astype(low)
        for cut in cuts_of(width):
            res[:, cut] += dot(crossed[...], wc[:, cut])
        second = res[...]
        center = second - jnp.mean(second, axis=-1, keepdims=True)
        spread = lax.rsqrt(jnp.mean(center * center, axis=-1, keepdims=True) + norm_eps)
        inverse[...] = spread
        scaled = center * spread
        normed[...] = scaled
        out[...] = (scaled * (1.0 + rows_ref[2:3, :]) + rows_ref[1:2, :]).astype(low)

    wide = (tokens, width)
    shapes = [
        (wide, jnp.float32),
        (wide, low),
        (wide, low),
        ((words, width), low),
        ((words, width), low),
        (wide, low),
        (wide, jnp.float32),
        (wide, jnp.float32),
        ((tokens, 1), jnp.float32),
        (wide, low),
    ]
    return pl.pallas_call(
        body,
        in_specs=[in_smem()] + [in_vmem()] * (count + 7),
        out_shape=[jax.ShapeDtypeStruct(*item) for item in shapes],
        scratch_shapes=[pltpu.VMEM((count, words, share), low)],
        compiler_params=pltpu.CompilerParams(vmem_limit_bytes=40 * 2**20),
        cost_estimate=cheap,
        name="cross_block",
    )(place, *mixed, hidden, rows, text, w_out, c_query, c_value, c_out)


def cross_back(place, terms, grad, rows, normed, inverse, branch, cq, ck, cv, c_out, c_query, w_out):
    count = len(terms)
    tokens, width = grad.shape
    words = ck.shape[0]
    share = width // count
    scale = HEAD_DIM ** (-0.5)

    def body(place_ref, *refs):
        parts = refs[:count]
        grad_ref, rows_ref, n_ref, i_ref, b_ref, q_ref, k_ref, v_ref, wc, wq, wo = refs[
            count : count + 11
        ]
        first, cross_low, grad_q, grad_v, attn_low, sums = refs[count + 11 : count + 17]
        outs, back, held = refs[count + 17 : -2], refs[-2], refs[-1]
        me = place_ref[0]
        total = parts[0][...].astype(jnp.float32)
        for part in parts[1:]:
            total += part[...].astype(jnp.float32)
        n = n_ref[...]
        sums[1:2, :] = jnp.sum(total, axis=0, keepdims=True)
        sums[2:3, :] = jnp.sum(total * n, axis=0, keepdims=True)
        second = grad_ref[...].astype(jnp.float32) + norm_back(total, n, i_ref[...], rows_ref[2:3, :])
        first[...] = second
        cross_low[...] = second.astype(low)
        for cut in cuts_of(width):
            back[:, cut] = dot(cross_low[...], wc[cut, :], nt).astype(low)
        grads = ([], [], [])
        for at in range(0, width, HEAD_DIM):
            head = slice(at, at + HEAD_DIM)
            q, k, v, g = q_ref[:, head], k_ref[:, head], v_ref[:, head], back[:, head]
            probs = softmax_keys(k, q)
            grad_probs = dot(v, g, nt)
            inner = jnp.sum(probs * grad_probs, axis=0, keepdims=True)
            grad_scores = (probs * (grad_probs - inner)).astype(low)
            grads[0].append((dot(k, grad_scores, tn) * scale).T)
            grads[1].append(dot(grad_scores, q) * scale)
            grads[2].append(dot(probs.astype(low), g))
        grad_q[...] = jnp.concatenate(grads[0], axis=1).astype(low)
        grad_v[...] = jnp.concatenate(grads[2], axis=1).astype(low)
        heads = share // HEAD_DIM
        for rank in range(count):
            pieces = grads[1][rank * heads : (rank + 1) * heads]
            held[rank] = jnp.concatenate(pieces, axis=1).astype(low)
        for cut in cuts_of(width):
            whole = first[:, cut] + dot(grad_q[...], wq[:, cut])
            first[:, cut] = whole
            attn_low[:, cut] = (rows_ref[0:1, cut] * whole).astype(low)
            sums[0:1, cut] = jnp.sum(b_ref[:, cut] * whole, axis=0, keepdims=True)
        for k in range(count):
            rank = lax.rem(me + k, count)
            here = pl.ds(pl.multiple_of(rank * share, 32), share)
            outs[k][0:tokens, :] = dot(attn_low[...], wo[here, :], nt).astype(low)
            outs[k][tokens:, :] = held[rank]

    wide = (tokens, width)
    shapes = [
        (wide, jnp.float32),
        (wide, low),
        (wide, low),
        ((words, width), low),
        (wide, low),
        ((3, width), jnp.float32),
    ] + [((tokens + words, share), low)] * count
    return pl.pallas_call(
        body,
        in_specs=[in_smem()] + [in_vmem()] * (count + 11),
        out_shape=[jax.ShapeDtypeStruct(*item) for item in shapes],
        scratch_shapes=[pltpu.VMEM(wide, low), pltpu.VMEM((count, words, share), low)],
        compiler_params=pltpu.CompilerParams(vmem_limit_bytes=40 * 2**20),
        cost_estimate=cheap,
        name="cross_back",
    )(place, *terms, grad, rows, normed, inverse, branch, cq, ck, cv, c_out, c_query, w_out)


def outer_halves(place, pairs, parts, name):
    width = pairs[0][1].shape[1]
    high = [sum(piece[2] for piece in left) for left, _ in pairs]
    size = high[0] // parts
    tokens = [right.shape[0] for _, right in pairs]
    flat = []

    def index_of(array):
        for i, other in enumerate(flat):
            if other is array:
                return i
        flat.append(array)
        return len(flat) - 1

    plans = [
        ([(index_of(array), *rest) for array, *rest in left], index_of(right))
        for left, right in pairs
    ]
    amount = len(pairs)

    def body(place_ref, *refs):
        ins, (kept, given), (held, sems) = refs[: len(flat)], refs[len(flat) :][:2], refs[-2:]
        turned = refs[len(flat) + 2 : -2]
        me, core = place_ref[0], place_ref[1]
        for i, (left, right) in enumerate(plans):
            for k, (which, lane, lanes, row) in enumerate(left):
                piece = ins[which][0 : tokens[i], lane : lane + lanes]
                piece = piece.astype(jnp.float32).T.astype(low)
                if row is None:
                    rank = lax.rem(me + k, len(left))
                    turned[i][pl.ds(pl.multiple_of(rank * lanes, 32), lanes), :] = piece
                else:
                    turned[i][row : row + lanes, :] = piece
            for part in range(parts):
                at = i * parts + part
                tile = dot(turned[i][part * size : (part + 1) * size, :], ins[right][...])
                held[at] = tile.astype(low)
                for out, side in ((kept, 0), (given, 1)):

                    @pl.when((core ^ (i & 1)) == side)
                    def _():
                        pltpu.make_async_copy(
                            held.at[at], out.at[i // 2, part], sems.at[at]
                        ).start()

        for at in range(amount * parts):
            pltpu.make_async_copy(held.at[at], kept.at[0, 0], sems.at[at]).wait()

    out = jax.ShapeDtypeStruct((amount // 2, parts, size, width), low)
    return pl.pallas_call(
        body,
        in_specs=[in_smem()] + [in_vmem()] * len(flat),
        out_specs=[pl.BlockSpec(memory_space=pl.ANY)] * 2,
        out_shape=[out, out],
        scratch_shapes=[pltpu.VMEM((high[i], tokens[i]), low) for i in range(amount)]
        + [
            pltpu.VMEM((amount * parts, size, width), low),
            pltpu.SemaphoreType.DMA((amount * parts,)),
        ],
        compiler_params=pltpu.CompilerParams(vmem_limit_bytes=48 * 2**20),
        cost_estimate=cheap if parts > 1 else costly,
        name=name,
    )(place, *flat)


def mlp_grads(grad_pres, acts, rows_in, grads_in):
    pieces, rights = len(acts), len(rows_in)
    tokens, width = rows_in[0].shape
    hidden = acts[0].shape[1]
    chunk = 384 if hidden % 384 == 0 else hidden
    steps = hidden // chunk

    def body(*refs):
        step = pl.program_id(0)
        out = refs[-1]

        def terms(lefts, turn, others):
            here = pl.ds(pl.multiple_of(turn * chunk, chunk), chunk)
            total = jnp.zeros((chunk, width), jnp.float32)
            cursor = 0
            for left in lefts:
                for i in range(left.shape[0] // tokens):
                    total += dot(left[i * tokens : (i + 1) * tokens, here], others[cursor][...], tn)
                    cursor += 1
            out[...] = total.astype(low)

        @pl.when(step < steps)
        def _():
            terms(refs[:pieces], step, refs[2 * pieces : 2 * pieces + rights])

        @pl.when(step >= steps)
        def _():
            terms(refs[pieces : 2 * pieces], step - steps, refs[2 * pieces + rights : -1])

    arrays = (*grad_pres, *acts, *rows_in, *grads_in)
    return pl.pallas_call(
        body,
        grid=(2 * steps,),
        in_specs=[pl.BlockSpec(array.shape, lambda s: (0, 0)) for array in arrays],
        out_specs=pl.BlockSpec((chunk, width), lambda s: (s, 0)),
        out_shape=jax.ShapeDtypeStruct((2 * hidden, width), low),
        compiler_params=pltpu.CompilerParams(vmem_limit_bytes=48 * 2**20),
        cost_estimate=cheap,
        name="mlp_grads",
    )(*arrays)


def ranked_terms(place, lefts, order, pieces, weight, factors, name):
    tokens, width = factors[0].shape
    count = len(factors)

    def body(place_ref, *refs):
        ins, weight_ref = refs[: len(lefts)], refs[len(lefts)]
        others = refs[len(lefts) + 1 : len(lefts) + 1 + count]
        out, sums = refs[-2:]
        me = place_ref[0]
        for i, slot in enumerate(order):
            rank = lax.rem(me - slot + count, count)
            for cut in cuts_of(width):
                term = jnp.zeros((tokens, cut.stop - cut.start), jnp.float32)
                for which, row, lane, start, depth in pieces[i]:
                    term += dot(
                        ins[which][row : row + tokens, lane : lane + depth],
                        weight_ref[start : start + depth, cut],
                    )
                out[rank, :, cut] = term.astype(low)
                one = jnp.sum(term, axis=0, keepdims=True)
                two = jnp.sum(term * others[i][:, cut].astype(jnp.float32), axis=0, keepdims=True)
                if i:
                    one, two = one + sums[0:1, cut], two + sums[1:2, cut]
                sums[0:1, cut], sums[1:2, cut] = one, two

    return pl.pallas_call(
        body,
        in_specs=[in_smem()] + [in_vmem()] * (len(lefts) + 1 + count),
        out_shape=[
            jax.ShapeDtypeStruct((count, tokens, width), low),
            jax.ShapeDtypeStruct((2, width), jnp.float32),
        ],
        compiler_params=pltpu.CompilerParams(vmem_limit_bytes=40 * 2**20),
        cost_estimate=cheap if len(lefts) > 2 else costly,
        name=name,
    )(place, *lefts, weight, *factors)


def update_slots(master, first_moment, second_moment, filled, which, position, sources):
    capacity, unit_rows, width = master.shape

    group = math.gcd(capacity, 2)
    steps = capacity // group

    def body(filled_ref, which_ref, position_ref, weight, one, two, *rest):
        ins = rest[: len(sources)]
        new_one, new_two, new_weight, held, sems = rest[len(sources) :]
        step = pl.program_id(0)

        def fetch(turn):
            for i in range(group):
                slot = turn * group + i
                for source, ref in enumerate(ins):

                    @pl.when(which_ref[slot] == source)
                    def _():
                        pltpu.make_async_copy(
                            ref.at[position_ref[slot]], held.at[turn % 2, i], sems.at[turn % 2, i]
                        ).start()

        @pl.when(step == 0)
        def _():
            fetch(step)

        @pl.when(step < steps - 1)
        def _():
            fetch(step + 1)

        for i in range(group):
            pltpu.make_async_copy(
                ins[0].at[0], held.at[step % 2, i], sems.at[step % 2, i]
            ).wait()
            mask = (filled_ref[step * group + i] > 0).astype(jnp.float32)
            grad = held[step % 2, i].astype(jnp.float32)
            results = adamw(weight[i], one[i], two[i], grad, mask, rate)
            new_one[i], new_two[i], new_weight[i] = results

    block = pl.BlockSpec((group, unit_rows, width), lambda s, *_: (s, 0, 0))
    return pl.pallas_call(
        body,
        grid_spec=pltpu.PrefetchScalarGridSpec(
            num_scalar_prefetch=3,
            grid=(steps,),
            in_specs=[block] * 3 + [pl.BlockSpec(memory_space=pl.ANY)] * len(sources),
            out_specs=[block] * 3,
            scratch_shapes=[
                pltpu.VMEM((2, group, unit_rows, width), low),
                pltpu.SemaphoreType.DMA((2, group)),
            ],
        ),
        out_shape=[jax.ShapeDtypeStruct(master.shape, jnp.float32)] * 3,
        compiler_params=pltpu.CompilerParams(vmem_limit_bytes=56 * 2**20),
        cost_estimate=cheap,
        name="update_slots",
    )(filled, which, position, master, first_moment, second_moment, *sources)


def adamw(weight, moment_one, moment_two, gradient, filled, step_rate):
    new_one = beta_one * moment_one + (1.0 - beta_one) * gradient
    new_two = beta_two * moment_two + (1.0 - beta_two) * gradient * gradient
    fixed_one = new_one / (1.0 - beta_one**STEP)
    fixed_two = new_two / (1.0 - beta_two**STEP)
    updated = weight - step_rate * (fixed_one / (jnp.sqrt(fixed_two) + adam_eps) + decay * weight)
    return (new_one * filled, new_two * filled, updated * filled)


def swap(values, axis, bit):
    count = lax.axis_size(axis)
    return lax.ppermute(values, axis, [(i, i ^ (1 << bit)) for i in range(count)])


def choose(values, index, axis):
    return lax.dynamic_index_in_dim(values, index, axis, keepdims=False)


def total_sum(values):
    for axis in ("dp", "tensor"):
        for bit in range(lax.axis_size(axis).bit_length() - 1):
            values = values + swap(values, axis, bit)
    return values


def pick_units(master, slot_unit, state, kind, place, sizes):
    capacity, unit_rows, width = master.shape
    units = state.shape[0]

    def body(slot_ref, state_ref, kind_ref, place_ref, blocks, *rest):
        outs, (highs, lows, zeros, read, sems) = rest[: len(sizes)], rest[len(sizes) :]

        def start(source, unit):
            for which, out in enumerate(outs):

                @pl.when(kind_ref[unit] == which)
                def _():
                    pltpu.make_async_copy(source, out.at[place_ref[unit]], sems.at[unit]).start()

        @pl.loop(0, capacity)
        def _(slot):
            @pl.when(slot_ref[slot] >= 0)
            def _():
                pltpu.make_async_copy(blocks.at[slot], highs.at[slot], read.at[slot]).start()

        zeros[...] = jnp.zeros_like(zeros)

        @pl.loop(0, units)
        def _(unit):
            @pl.when(state_ref[unit] == 0)
            def _():
                start(zeros, unit)

        @pl.loop(0, capacity)
        def _(slot):
            @pl.when(slot_ref[slot] >= 0)
            def _():
                pltpu.make_async_copy(blocks.at[slot], highs.at[slot], read.at[slot]).wait()
                lows[slot] = highs[slot].astype(low)
                start(lows.at[slot], slot_ref[slot])

        @pl.loop(0, units)
        def _(unit):
            @pl.when(state_ref[unit] < 2)
            def _():
                pltpu.make_async_copy(zeros, outs[0].at[0], sems.at[unit]).wait()

    return pl.pallas_call(
        body,
        grid_spec=pltpu.PrefetchScalarGridSpec(
            num_scalar_prefetch=4,
            grid=(1,),
            in_specs=[pl.BlockSpec(memory_space=pl.ANY)],
            out_specs=[pl.BlockSpec(memory_space=pl.ANY)] * len(sizes),
            scratch_shapes=[
                pltpu.VMEM((capacity, unit_rows, width), jnp.float32),
                pltpu.VMEM((capacity, unit_rows, width), low),
                pltpu.VMEM((unit_rows, width), low),
                pltpu.SemaphoreType.DMA((capacity,)),
                pltpu.SemaphoreType.DMA((units,)),
            ],
        ),
        out_shape=[jax.ShapeDtypeStruct((size, unit_rows, width), low) for size in sizes],
        compiler_params=pltpu.CompilerParams(vmem_limit_bytes=56 * 2**20),
        cost_estimate=cheap,
        name="pick_units",
    )(slot_unit, state, kind, place, master)


def place_blocks(sources, which, position, parts=1):
    amount = which.shape[0]
    shape = sources[0].shape[1:]
    size = amount // parts

    def body(which_ref, position_ref, *rest):
        ins, outs = rest[: len(sources)], rest[len(sources) : len(sources) + parts]
        held, read, sems = rest[len(sources) + parts :]

        @pl.loop(0, amount)
        def _(i):
            for source, ref in enumerate(ins):

                @pl.when(which_ref[i] == source)
                def _():
                    pltpu.make_async_copy(ref.at[position_ref[i]], held.at[i], read.at[i]).start()

        for part, out in enumerate(outs):

            @pl.loop(0, size)
            def _(j):
                i = part * size + j
                pltpu.make_async_copy(ins[0].at[0], held.at[i], read.at[i]).wait()
                pltpu.make_async_copy(held.at[i], out.at[j], sems.at[i]).start()

        @pl.loop(0, amount)
        def _(i):
            pltpu.make_async_copy(held.at[i], outs[0].at[0], sems.at[i]).wait()

    return pl.pallas_call(
        body,
        grid_spec=pltpu.PrefetchScalarGridSpec(
            num_scalar_prefetch=2,
            grid=(1,),
            in_specs=[pl.BlockSpec(memory_space=pl.ANY)] * len(sources),
            out_specs=[pl.BlockSpec(memory_space=pl.ANY)] * parts,
            scratch_shapes=[
                pltpu.VMEM((amount,) + shape, low),
                pltpu.SemaphoreType.DMA((amount,)),
                pltpu.SemaphoreType.DMA((amount,)),
            ],
        ),
        out_shape=[jax.ShapeDtypeStruct((size,) + shape, low)] * parts,
        compiler_params=pltpu.CompilerParams(vmem_limit_bytes=56 * 2**20),
        cost_estimate=cheap,
        name="place_blocks",
    )(which, position, *sources)


def hops(values, step, turn):
    count = lax.axis_size("tensor")
    if step > 0:
        pairs = [(i, i + 1) for i in range(turn - 1, count - 1)]
    else:
        pairs = [(i, i - 1) for i in range(1, count - turn + 1)]
    return lax.ppermute(values, "tensor", pairs)


def slots_of(own, ups, downs):
    count = lax.axis_size("tensor")
    me = lax.axis_index("tensor")
    return [own] + [jnp.where(me >= k, ups[k - 1], downs[count - k - 1]) for k in range(1, count)]


fence = lax.optimization_barrier


def in_pool(member, inner, inner_count):
    me = lax.axis_index("dp")
    half, core = member >> 3, ((member >> 2) & 1) ^ (me & 1)
    far_y, far_x = ((member >> 1) & 1) ^ ((me >> 2) & 1), (member & 1) ^ ((me >> 1) & 1)
    where_first = (far_y * 2 + far_x) * inner_count
    where_second = (4 + far_x * 2 + far_y) * inner_count
    return (core, jnp.where(half == 0, where_first, where_second) + inner)


def on_device(
    hidden_in,
    time_embed,
    caption_table,
    caption_ids,
    owners,
    master,
    first_moment,
    second_moment,
    mod_table,
    mod_first,
    mod_second,
    out_grad,
):
    count = lax.axis_size("tensor")
    dp_count = lax.axis_size("dp")
    me_dp = lax.axis_index("dp")
    me_tensor = lax.axis_index("tensor")
    capacity, unit_rows, width = master.shape
    units = owners.shape[0]
    tokens = hidden_in.shape[1]
    text_count = caption_ids.shape[1]
    share = width // count
    per = share // unit_rows
    ups = (units - 8 * per) // 2
    rank_of = ranks_of(owners)
    mine = owners == me_dp
    match = (rank_of[None, :] == jnp.arange(capacity)[:, None]) & mine[None, :]
    filled = jnp.any(match, axis=1)
    unit_of_slot = jnp.sum(jnp.where(match, jnp.arange(units)[None, :], 0), axis=1)

    square = [list(range(i * per, (i + 1) * per)) for i in range(8)]
    group_attn = square[0] + square[1] + square[2] + square[5]
    group_full = square[3] + square[4] + square[6] + square[7]
    group_mlp = list(range(8 * per, units))
    members = len(group_attn)
    plane = dp_count == 8 and members == 16 and len(group_mlp) % dp_count == 0
    member_of = np.zeros(units, np.int32)
    member_of[group_attn] = np.arange(members)
    member_of[group_full] = np.arange(members)
    is_attn = np.zeros(units, bool)
    is_attn[group_attn] = True
    is_mlp = np.zeros(units, bool)
    is_mlp[group_mlp] = True

    latent_in = hidden_in[0].astype(jnp.float32)
    modulate = mod_table + time_embed[0]

    def mod_row(which_row):
        return modulate[which_row][None, :]

    normed_one, inverse_one = layer_norm(latent_in)
    bits = dp_count.bit_length() - 1
    vocab_rows = caption_table.shape[0]

    def caption_terms(ids):
        chosen = ids.reshape(-1) - me_dp * vocab_rows
        onehot = (chosen[:, None] == jnp.arange(vocab_rows)[None, :]).astype(low)
        terms = jnp.dot(onehot, caption_table, preferred_element_type=jnp.float32).astype(low)
        return terms.reshape(dp_count, text_count, -1)

    def modulated(normed):
        return (normed.astype(jnp.float32) * (1.0 + mod_row(1)) + mod_row(0)).astype(low)

    def whole_text(text_ring):
        return from_ring(text_ring, -1).transpose(1, 0, 2).reshape(text_count, width)

    def own_keys(text_low, w_attn):
        return project(text_low, w_attn)[:, 3 * share :].astype(low)

    n_low = normed_one.astype(low)
    if plane:
        core, far_x, far_y = (
            ((member_of >> 2) & 1) ^ (me_dp & 1),
            (member_of & 1) ^ ((me_dp >> 1) & 1),
            ((member_of >> 1) & 1) ^ ((me_dp >> 2) & 1),
        )
        place = jnp.where(is_attn, far_x * 4 + far_y * 2, 8 + far_y * 4 + far_x * 2)
        place = jnp.where(is_mlp, np.arange(units) - 8 * per, place + (member_of >> 3))
        kind = jnp.where(is_mlp, 0, core)
        slot_mlp = unit_of_slot >= 8 * per
        owned_state = mine.astype(jnp.int32)
        ids = lax.all_gather(caption_ids, "dp", axis=0, tiled=True)
        ids = jnp.take(ids, me_dp ^ jnp.arange(dp_count), axis=0, mode="clip")
        up, down = hops(n_low, 1, 1), hops(n_low, -1, 1)
        kept, given = pick_units(
            master,
            jnp.where(filled & ~slot_mlp, unit_of_slot, -1),
            jnp.where(is_mlp, 2, owned_state),
            kind,
            place,
            (members, members),
        )
        got = swap(given, "dp", 0)
        text = caption_terms(ids)
        text = text[0:4] + swap(text[4:8], "dp", 2)
        n_up, n_down = [up], [down]
        kept, got, up, down, text = fence((kept, got, up, down, text))
        pieces = [kept[i : i + 4] + got[i : i + 4] for i in range(0, members, 4)]
        attn_two, attn_send, full_two, full_send = fence(tuple(pieces))
        up, down = hops(up, 1, 2), hops(down, -1, 2)
        attn_got = swap(attn_send, "dp", 1)
        full_got = swap(full_send, "dp", 2)
        text = text[0:2] + swap(text[2:4], "dp", 1)
        (mlp_part,) = pick_units(
            fence((master, got))[0],
            jnp.where(filled & slot_mlp, unit_of_slot, -1),
            jnp.where(is_mlp, owned_state, 2),
            kind,
            place,
            (len(group_mlp),),
        )
        n_up.append(up), n_down.append(down)
        attn_two, attn_got, full_two, full_got, up, down, text, mlp_part = fence(
            (attn_two, attn_got, full_two, full_got, up, down, text, mlp_part)
        )
        pieces = [x[i : i + 2] + y[i : i + 2] for x, y in ((attn_two, attn_got), (full_two, full_got)) for i in (0, 2)]
        attn_one, attn_send, full_one, full_send = fence(tuple(pieces))
        up, down = hops(up, 1, 3), hops(down, -1, 3)
        attn_got = swap(attn_send, "dp", 2)
        full_got = swap(full_send, "dp", 1)
        text = text[0] + swap(text[1], "dp", 0)
        n_up.append(up), n_down.append(down)
        attn_one, attn_got, full_one, full_got, up, down, text, mlp_part = fence(
            (attn_one, attn_got, full_one, full_got, up, down, text, mlp_part)
        )
        attn_one, full_one = attn_one + attn_got, full_one + full_got
        n_up[-1], n_down[-1] = up, down
        mlp_part = lax.psum_scatter(mlp_part, "dp", scatter_dimension=0, tiled=True)
        lines = text_count * share // width
        text = jnp.pad(text.reshape(lines, width), ((0, -lines % 16), (0, 0)))
        parcel = jnp.concatenate([full_one.reshape(2 * unit_rows, width), text])
        parcels = [parcel] + [shift(parcel, k) for k in range(1, count)]
        first = jnp.concatenate([attn_one[0:1], swap(attn_one[0:1], "dp", 1)])
        second = jnp.concatenate([attn_one[1:2], swap(attn_one[1:2], "dp", 2)])
        pool = jnp.concatenate([first, swap(first, "dp", 2), second, swap(second, "dp", 1)])
        n_slots = slots_of(n_low, n_up, n_down)
        normed_all = jnp.concatenate(n_slots)
        h_one_all = modulated(normed_all)
        grad_own = out_grad[0]
        pool, parcels, h_one_all, grad_own = fence((pool, parcels, h_one_all, grad_own))
        grad_whole = lax.all_gather(grad_own, "tensor", axis=0)
        other = swap(pool, "dp", 0)
        full_ring = [item[: 2 * unit_rows].reshape(2, unit_rows, width) for item in parcels]
        first = jnp.concatenate([item[0:1] for item in full_ring])
        second = jnp.concatenate([item[1:2] for item in full_ring])
        first_got = swap(first, "dp", 1)
        second_got = swap(second, "dp", 2)
        first = jnp.concatenate([first, first_got])
        second = jnp.concatenate([second, second_got])
        text_ring = jnp.stack(
            [
                item[2 * unit_rows : 2 * unit_rows + lines].reshape(text_count, share)
                for item in parcels
            ]
        )
        text_low = whole_text(text_ring)
        first, second, text_low, pool, other = fence((first, second, text_low, pool, other))
        first_far, second_far = swap(first, "dp", 2), swap(second, "dp", 1)
        first_other, second_other = swap(first, "dp", 0), swap(second, "dp", 0)
        (w_attn,) = place_blocks((pool, other), *in_pool(np.arange(members), 0, 1))
        w_attn = w_attn.reshape(-1, width)
        qkv = project(h_one_all, w_attn).astype(low)
        attended = self_attend(qkv, share)
        ck_own = own_keys(text_low, w_attn)
        first_far, second_far, first_other, second_other, attended, ck_own, mlp_part = fence(
            (first_far, second_far, first_other, second_other, attended, ck_own, mlp_part)
        )
        first_last, second_last = swap(first_far, "dp", 0), swap(second_far, "dp", 0)
        w_mlp = lax.all_gather(mlp_part, "dp", axis=0, tiled=True)
        listing = np.arange(count * members)
        matrix, rank, head = listing // (count * per), listing // per % count, listing % per
        slot = lax.rem(me_tensor - rank + count, count)
        which, position = in_pool(matrix * per + head, slot, count)
        blocks = 2 * count
        w_full = place_blocks(
            (first, first_far, second, second_far, first_other, first_last, second_other, second_last),
            which * 4 + position // blocks,
            position % blocks,
            parts=4,
        )
        w_full = [part.reshape(width, width) for part in w_full]
    else:
        slots_low = master.astype(low)
        rows = jnp.take(slots_low, rank_of, axis=0, mode="clip")
        rows = lax.psum(jnp.where(mine[:, None, None], rows, jnp.zeros((), low)), "dp")
        w_attn = rows[np.array(group_attn)].reshape(-1, width)
        w_full = lax.all_gather(rows[np.array(group_full)], "tensor", axis=0)
        w_full = w_full.reshape(count, 4, share, width).swapaxes(0, 1).reshape(4, width, width)
        w_full = [w_full[i] for i in range(4)]
        w_mlp = rows[8 * per :]
        n_slots = ring(n_low)
        normed_all = jnp.concatenate(n_slots)
        grad_whole = lax.all_gather(out_grad[0], "tensor", axis=0)
        ids = caption_ids
        for bit in range(bits):
            ids = jnp.concatenate([ids, swap(ids, "dp", bit)])
        text = caption_terms(ids)
        for bit in reversed(range(bits)):
            text = text[: 1 << bit] + swap(text[1 << bit :], "dp", bit)
        text_low = whole_text(jnp.stack(ring(text[0])))
        h_one_all = modulated(normed_all)
        qkv = project(h_one_all, w_attn).astype(low)
        attended = self_attend(qkv, share)
        ck_own = own_keys(text_low, w_attn)
    w_cross = w_full
    w_out, c_query, c_value, c_out = w_full
    w_mlp = w_mlp.reshape(-1, width)

    mixed_parts = [
        jnp.concatenate([attended[k * tokens : (k + 1) * tokens], ck_own]) for k in range(count)
    ]
    mixed = [mixed_parts[0]] + [shift(mixed_parts[k], count - k) for k in range(1, count)]
    where = jnp.stack([me_tensor, me_dp & 1]).astype(jnp.int32)
    rows = jnp.concatenate([mod_row(2), mod_row(3), mod_row(4)])
    (
        branch_one,
        first_low,
        cq_rows,
        ck_rows,
        cv_rows,
        crossed,
        second_res,
        normed_two,
        inverse_two,
        h_two,
    ) = cross_block(
        where, mixed, hidden_in[0], rows, text_low, *w_cross
    )

    h_slots = ring(h_two)
    out_slots = [
        choose(grad_whole, lax.rem(me_tensor - k + count, count), 0) for k in range(count)
    ]
    grad_slots = [(mod_row(5) * item.astype(jnp.float32)).astype(low) for item in out_slots]
    near = [k for k in range(1, count) if 2 * k != count]
    far = [k for k in range(1, count) if 2 * k == count]
    acts, grad_pres, grad_terms, order = [], [], [], []
    for members_now in ([0], near, far):
        held = [h_slots[k] for k in members_now]
        if acts:
            held = fence((held, acts[-1]))[0]
        act, grad_pre, *terms = mlp_core(held, [grad_slots[k] for k in members_now], w_mlp)
        acts.append(act), grad_pres.append(grad_pre)
        order += members_now
        grad_terms += [
            shift(term, count - k) if k else term for k, term in zip(members_now, terms)
        ]
    mlp_grad = mlp_grads(
        grad_pres, acts, [h_slots[k] for k in order], [grad_slots[k] for k in order]
    ).reshape(-1, unit_rows, width)
    hidden_share = w_mlp.shape[0] // 2
    pieces = [
        [(which, row, 0, hidden_share, hidden_share)]
        for which, act in enumerate(acts)
        for row in range(0, act.shape[0], tokens)
    ]
    branch_terms, branch_sums = ranked_terms(
        where, acts, order, pieces, w_mlp, [out_slots[k] for k in order], "mlp_out"
    )
    branch_row = branch_sums[1]
    grad_terms, branch_terms, mlp_grad = fence((grad_terms, branch_terms, mlp_grad))
    if plane:
        mlp_sum = lax.psum(mlp_grad, "dp")

    (
        first_grad,
        cross_low,
        grad_cq,
        grad_cv,
        attn_low,
        row_sums,
        *grad_mixed,
    ) = cross_back(
        where,
        grad_terms,
        out_grad[0],
        rows,
        normed_two,
        inverse_two,
        branch_one,
        cq_rows,
        ck_rows,
        cv_rows,
        c_out,
        c_query,
        w_out,
    )

    grad_parts = [grad_mixed[0]] + [shift(grad_mixed[k], k) for k in range(1, count)]
    full_pairs = [
        ([(item, 0, share, None) for item in mixed], attn_low),
        ([(grad_cq, 0, width, 0)], first_low),
        ([(grad_cv, 0, width, 0)], text_low),
        ([(crossed, 0, width, 0)], cross_low),
    ]
    half = (share // HEAD_DIM // 2) * HEAD_DIM
    spans = [(0, half), (half, share)]

    def attention_pairs(grads, grad_parts):
        keys = sum(item[tokens:].astype(jnp.float32) for item in grad_parts).astype(low)
        pairs = [
            (
                [
                    (item, i * (end - begin), end - begin, begin)
                    for item, (begin, end) in zip(grads, spans)
                ],
                h_one_all,
            )
            for i in range(3)
        ]
        return pairs + [([(keys, 0, share, 0)], text_low)]

    def input_terms(grads):
        pieces = [
            [
                (which, slot * tokens, i * (end - begin), i * share + begin, end - begin)
                for which, (begin, end) in enumerate(spans)
                for i in range(3)
            ]
            for slot in range(count)
        ]
        return ranked_terms(where, grads, range(count), pieces, w_attn, n_slots, "attn_terms")

    if plane:
        x_bit, y_bit = (me_dp >> 1) & 1, (me_dp >> 2) & 1

        def split(total, bit, axis):
            return (choose(total, bit, axis), choose(total, 1 - bit, axis))

        branch_terms, grad_parts[0] = fence((branch_terms, grad_parts[0]))
        branch_two = lax.psum_scatter(
            branch_terms.reshape(-1, width), "tensor", scatter_dimension=0, tiled=True
        )
        kept, given = outer_halves(where, full_pairs, count, "full_grads")
        got = swap(given, "dp", 0)
        grad_parts, kept, got = fence((grad_parts, kept, got))
        box = (2, count, 2, 2, unit_rows, width)
        kept, got = kept.reshape(box), got.reshape(box)
        kept_one = choose(kept[0], x_bit, 2) + choose(got[0], x_bit, 2)
        given_one = choose(kept[0], 1 - x_bit, 2) + choose(got[0], 1 - x_bit, 2)
        kept_two = choose(kept[1], y_bit, 1) + choose(got[1], y_bit, 1)
        given_two = choose(kept[1], 1 - y_bit, 1) + choose(got[1], 1 - y_bit, 1)
        kept_one, given_one, kept_two, given_two, grad_parts = fence(
            (kept_one, given_one, kept_two, given_two, grad_parts)
        )
        got_one, got_two = swap(given_one, "dp", 1), swap(given_two, "dp", 2)
        grads_early = self_attend_back(qkv, grad_parts, share, *spans[0])
        kept_one, got_one, kept_two, got_two, grads_early, grad_parts, branch_two, mlp_sum = fence(
            (kept_one, got_one, kept_two, got_two, grads_early, grad_parts, branch_two, mlp_sum)
        )
        kept_one, given_one = split(kept_one + got_one, y_bit, 1)
        kept_two, given_two = split(kept_two + got_two, x_bit, 1)
        kept_one, given_one, kept_two, given_two, grad_parts = fence(
            (kept_one, given_one, kept_two, given_two, grad_parts)
        )
        got_one, got_two = swap(given_one, "dp", 2), swap(given_two, "dp", 1)
        grads_late = self_attend_back(qkv, grad_parts, share, *spans[1])
        kept_one, got_one, kept_two, got_two, grads_early, grads_late = fence(
            (kept_one, got_one, kept_two, got_two, grads_early, grads_late)
        )
        full_parts = jnp.stack([kept_one + got_one, kept_two + got_two], axis=1)
        full_parts, grads_early, grads_late = fence((full_parts, grads_early, grads_late))
        grads_qkv = [grads_early, grads_late]
        full_sum = lax.psum_scatter(full_parts, "tensor", scatter_dimension=0, tiled=True)[0]
        attn_kept, attn_given = outer_halves(
            where, attention_pairs(grads_qkv, grad_parts), 1, "attn_grads"
        )
        attn_got = swap(attn_given, "dp", 0)
        grad_h_terms, grad_h_sums = input_terms(grads_qkv)
        mod_terms = jnp.concatenate([grad_h_sums, row_sums, branch_row[None]])
        grad_h_one = lax.psum_scatter(
            grad_h_terms.reshape(-1, width), "tensor", scatter_dimension=0, tiled=True
        )
        attn_kept, attn_got, mod_terms = fence((attn_kept, attn_got, mod_terms))
        attn_all = (attn_kept + attn_got).reshape(2, 2, 2, unit_rows, width)
        one_kept, one_given = split(attn_all[0], x_bit, 1)
        two_kept, two_given = split(attn_all[1], y_bit, 0)
        one_got, two_got = swap(one_given, "dp", 1), swap(two_given, "dp", 2)
        mod_terms = mod_terms + swap(mod_terms, "dp", 0)
        one_kept, one_got, two_kept, two_got, mod_terms, full_sum = fence(
            (one_kept, one_got, two_kept, two_got, mod_terms, full_sum)
        )
        one_kept, one_given = split(one_kept + one_got, y_bit, 0)
        two_kept, two_given = split(two_kept + two_got, x_bit, 0)
        one_got, two_got = swap(one_given, "dp", 2), swap(two_given, "dp", 1)
        mod_terms = mod_terms + swap(mod_terms, "dp", 1)
        one_kept, one_got, two_kept, two_got, full_sum, mod_terms = fence(
            (one_kept, one_got, two_kept, two_got, full_sum, mod_terms)
        )
        first = jnp.stack([one_kept + one_got, full_sum[0]])
        second = jnp.stack([two_kept + two_got, full_sum[1]])
        first_got, second_got = swap(first, "dp", 1), swap(second, "dp", 2)
        first = jnp.concatenate([first, first_got])
        second = jnp.concatenate([second, second_got])
        mod_terms = mod_terms + swap(mod_terms, "dp", 2)
        first, second, mod_terms = fence((first, second, mod_terms))
        first_far, second_far = swap(first, "dp", 2), swap(second, "dp", 1)
        mod_terms = mod_terms + swap(mod_terms, "tensor", 0)
        first, first_far, second, second_far, grad_h_one, mod_terms = fence(
            (first, first_far, second, second_far, grad_h_one, mod_terms)
        )
        pool = jnp.concatenate([first, first_far, second, second_far])
        other = swap(pool, "dp", 0)
        for bit in range(1, count.bit_length() - 1):
            mod_terms = mod_terms + swap(mod_terms, "tensor", bit)
        pool, other, mod_grad = fence((pool, other, mod_terms))
        which, position = in_pool(member_of, np.where(is_attn, 0, 1), 2)
        which = jnp.where(is_mlp, 2, which)
        position = jnp.where(is_mlp, np.arange(units) - 8 * per, position)
        own = jnp.sum(jnp.where(match[:, :, None], jnp.stack([which, position], 1)[None], 0), axis=1)
        new_first, new_second, new_master = update_slots(
            master,
            first_moment,
            second_moment,
            filled.astype(jnp.int32),
            own[:, 0],
            own[:, 1],
            (pool, other, mlp_sum),
        )
    else:
        branch_two = lax.psum_scatter(
            branch_terms.reshape(-1, width), "tensor", scatter_dimension=0, tiled=True
        )
        grads_qkv = [self_attend_back(qkv, grad_parts, share, *span) for span in spans]
        attn_grads = [
            outer(array[:, lane : lane + lanes], right).astype(low)
            for left, right in attention_pairs(grads_qkv, grad_parts)
            for array, lane, lanes, row in left
        ]
        grad_h_terms, grad_h_sums = input_terms(grads_qkv)
        grad_h_one = lax.psum_scatter(
            grad_h_terms.reshape(-1, width), "tensor", scatter_dimension=0, tiled=True
        )
        mixed_all = from_ring(jnp.stack([item[:tokens] for item in mixed]), 1)
        mixed_all = mixed_all.transpose(1, 0, 2).reshape(tokens, width)
        full_grads = [outer(mixed_all, attn_low)]
        full_grads += [outer(left[0][0], right) for left, right in full_pairs[1:]]
        full_sum = [g.astype(low).reshape(count, share, width) for g in full_grads]
        full_sum = jnp.stack(full_sum, axis=1)
        full_sum = lax.psum_scatter(full_sum, "tensor", scatter_dimension=0, tiled=True)
        order = np.array(group_attn + group_full + group_mlp)
        sums = jnp.concatenate(
            [jnp.concatenate(attn_grads), full_sum.reshape(-1, width), mlp_grad.reshape(-1, width)]
        )
        sums = lax.psum(sums.reshape(units, unit_rows, width), "dp")
        owned = jnp.take(sums, jnp.array(np.argsort(order))[unit_of_slot], axis=0, mode="clip")
        mod_grad = total_sum(jnp.concatenate([grad_h_sums, row_sums, branch_row[None]]))
        new_first, new_second, new_master = adamw(
            master,
            first_moment,
            second_moment,
            owned.astype(jnp.float32),
            filled.astype(jnp.float32)[:, None, None],
            rate,
        )
    branch_two, second_res, grad_h_one, new_first = fence(
        (branch_two, second_res, grad_h_one, new_first)
    )
    grad_h_one = grad_h_one.astype(jnp.float32)
    block_out = second_res + mod_row(5) * branch_two.astype(jnp.float32)
    input_grad = first_grad + norm_back(grad_h_one, normed_one, inverse_one, mod_row(1))
    mod_new_first, mod_new_second, mod_new = adamw(
        mod_table, mod_first, mod_second, mod_grad, 1.0, table_rate
    )
    return (
        block_out[None],
        input_grad[None],
        new_first,
        new_second,
        new_master,
        mod_new_first,
        mod_new_second,
        mod_new,
    )


def solution(mesh):
    in_specs = (
        P("dp", "tensor", None),
        P("dp", None, None),
        P("dp", "tensor"),
        P("dp", None),
        P(),
        P("dp", "tensor", None),
        P("dp", "tensor", None),
        P("dp", "tensor", None),
        P(),
        P(),
        P(),
        P("dp", "tensor", None),
    )
    out_specs = (
        P("dp", "tensor", None),
        P("dp", "tensor", None),
        P("dp", "tensor", None),
        P("dp", "tensor", None),
        P("dp", "tensor", None),
        P(),
        P(),
        P(),
    )
    return jax.shard_map(
        on_device, mesh=mesh, in_specs=in_specs, out_specs=out_specs, check_vma=False
    )
```

```python
import math

import jax
import jax.numpy as jnp
import numpy as np
from jax import lax
from jax.experimental import pallas as pl
from jax.experimental.pallas import tpu as pltpu
from jax.sharding import PartitionSpec as P

HEAD_DIM = 72
STEP = 10


norm_eps = 1e-06
beta_one = 0.9
beta_two = 0.999
rate = 0.03
table_rate = 0.3
decay = 0.01
adam_eps = 1e-08
low = jnp.bfloat16


def ranks_of(owners):
    index = jnp.arange(owners.shape[0])
    before = (owners[None, :] == owners[:, None]) & (index[None, :] < index[:, None])
    return jnp.sum(before.astype(jnp.int32), axis=1)


def layer_norm(values):
    center = values - jnp.mean(values, axis=-1, keepdims=True)
    inverse = lax.rsqrt(jnp.mean(center * center, axis=-1, keepdims=True) + norm_eps)
    return (center * inverse, inverse)


def norm_back(grad_rows, normed, inverse, scale_row):
    scaled = grad_rows * (1.0 + scale_row)
    mean_one = jnp.mean(scaled, axis=-1, keepdims=True)
    mean_two = jnp.mean(scaled * normed, axis=-1, keepdims=True)
    return inverse * (scaled - mean_one - normed * mean_two)


def project(rows, weight):
    return jnp.einsum("ld,rd->lr", rows, weight, preferred_element_type=jnp.float32)


def expand(rows, weight):
    return jnp.einsum("lr,rd->ld", rows, weight, preferred_element_type=jnp.float32)


def outer(left, right):
    return jnp.einsum("lr,ld->rd", left, right, preferred_element_type=jnp.float32)


def shift(values, step):
    count = lax.axis_size("tensor")
    return lax.ppermute(values, "tensor", [(i, (i + step) % count) for i in range(count)])


def ring(values):
    return [values] + [shift(values, k) for k in range(1, lax.axis_size("tensor"))]


def to_ring(stacked):
    count = stacked.shape[0]
    twice = jnp.concatenate([stacked, stacked], axis=0)
    return lax.dynamic_slice_in_dim(twice, lax.axis_index("tensor"), count, 0)


def from_ring(stacked, sign):
    count = stacked.shape[0]
    me = lax.axis_index("tensor")
    place = lax.rem(sign * (jnp.arange(count) - me) + 2 * count, count)
    return jnp.take(stacked, place, axis=0, mode="clip")


cheap = pl.CostEstimate(flops=1000, bytes_accessed=1000, transcendentals=0)
costly = pl.CostEstimate(flops=10**10, bytes_accessed=10**7, transcendentals=0)


def self_attend(qkv, share):
    length = qkv.shape[0]
    rows = min(256, length)

    def body(qkv_ref, out_ref):
        @pl.loop(0, length // rows)
        def _(step):
            here = pl.ds(pl.multiple_of(step * rows, rows), rows)
            parts = []
            for at in range(0, share, HEAD_DIM):
                q = qkv_ref[here, at : at + HEAD_DIM]
                k = qkv_ref[:, share + at : share + at + HEAD_DIM]
                v = qkv_ref[:, 2 * share + at : 2 * share + at + HEAD_DIM]
                probs = softmax_keys(k, q).astype(low)
                parts.append(dot(v, probs, tn).T)
            out_ref[here, :] = jnp.concatenate(parts, axis=1).astype(low)

    return pl.pallas_call(
        body,
        out_shape=jax.ShapeDtypeStruct((length, share), low),
        compiler_params=pltpu.CompilerParams(vmem_limit_bytes=32 * 2**20),
        cost_estimate=cheap,
        name="self_attend",
    )(qkv)


def self_attend_back(qkv, grads, share, begin, end):
    length = qkv.shape[0]
    rows = length // len(grads)
    span = end - begin
    scale = HEAD_DIM ** (-0.5)

    def body(qkv_ref, *refs):
        grad_refs, (out_ref, grad_k, grad_v) = refs[: len(grads)], refs[len(grads) :]
        for step, grad_ref in enumerate(grad_refs):
            here = slice(step * rows, (step + 1) * rows)
            parts = []
            for head, at in enumerate(range(begin, end, HEAD_DIM)):
                q = qkv_ref[here, at : at + HEAD_DIM]
                k = qkv_ref[:, share + at : share + at + HEAD_DIM]
                v = qkv_ref[:, 2 * share + at : 2 * share + at + HEAD_DIM]
                g = grad_ref[0:rows, at : at + HEAD_DIM]
                probs = softmax_keys(k, q)
                grad_probs = dot(v, g, nt)
                inner = jnp.sum(probs * grad_probs, axis=0, keepdims=True)
                grad_scores = (probs * (grad_probs - inner)).astype(low)
                to_v = dot(probs.astype(low), g)
                to_k = dot(grad_scores, q)
                if step:
                    grad_v[head] += to_v
                    grad_k[head] += to_k
                else:
                    grad_v[head] = to_v
                    grad_k[head] = to_k
                parts.append((dot(k, grad_scores, tn) * scale).T)
            out_ref[here, 0:span] = jnp.concatenate(parts, axis=1).astype(low)
        heads = range(span // HEAD_DIM)
        both = [grad_k[head] * scale for head in heads]
        out_ref[:, span : 2 * span] = jnp.concatenate(both, axis=1).astype(low)
        both = [grad_v[head] for head in heads]
        out_ref[:, 2 * span :] = jnp.concatenate(both, axis=1).astype(low)

    return pl.pallas_call(
        body,
        out_shape=jax.ShapeDtypeStruct((length, 3 * span), low),
        scratch_shapes=[pltpu.VMEM((span // HEAD_DIM, length, HEAD_DIM), jnp.float32)] * 2,
        compiler_params=pltpu.CompilerParams(vmem_limit_bytes=40 * 2**20),
        cost_estimate=cheap,
        name="self_attend_back",
    )(qkv, *grads)


def mlp_core(rows_in, grads_in, w_mlp, after=()):
    groups = len(rows_in)
    tokens, width = rows_in[0].shape
    hidden = w_mlp.shape[0] // 2
    chunk = 384 if hidden % 384 == 0 else hidden
    steps = hidden // chunk
    curve = 0.7978845608028654

    def body(*refs):
        rows, grads = refs[:groups], refs[groups : 2 * groups]
        up, down = refs[2 * groups : 2 * groups + 2]
        act, grad_pre, *outs = refs[2 * groups + 2 + len(after) : -1]
        total = refs[-1]
        step = pl.program_id(0)
        for i in range(groups):
            pre = lax.dot_general(
                rows[i][...], up[...], (((1,), (1,)), ((), ())), preferred_element_type=jnp.float32
            )
            square = pre * pre
            bend = jnp.tanh(curve * pre * (1.0 + 0.044715 * square))
            half = 0.5 * (1.0 + bend)
            here = pl.ds(i * tokens, tokens)
            act[here, :] = (pre * half).astype(low)
            slope = half + (0.5 * curve) * pre * (1.0 - bend * bend) * (1.0 + 0.134145 * square)
            grad_act = lax.dot_general(
                grads[i][...], down[...], (((1,), (1,)), ((), ())), preferred_element_type=jnp.float32
            )
            grad_low = (grad_act * slope).astype(low)
            grad_pre[here, :] = grad_low
            term = jnp.dot(grad_low, up[...], preferred_element_type=jnp.float32)

            @pl.when(step == 0)
            def _():
                total[here, :] = term

            @pl.when(step > 0)
            def _():
                total[here, :] += term

            @pl.when(step == steps - 1)
            def _():
                outs[i][...] = total[here, :].astype(low)

    whole = pl.BlockSpec((tokens, width), lambda s: (0, 0))
    across = pl.BlockSpec((groups * tokens, chunk), lambda s: (0, s))
    return pl.pallas_call(
        body,
        grid=(steps,),
        in_specs=[whole] * (2 * groups)
        + [
            pl.BlockSpec((chunk, width), lambda s: (s, 0)),
            pl.BlockSpec((chunk, width), lambda s: (steps + s, 0)),
        ]
        + [pl.BlockSpec(array.shape, lambda s: (0, 0)) for array in after],
        out_specs=[across, across] + [whole] * groups,
        out_shape=[jax.ShapeDtypeStruct((groups * tokens, hidden), low)] * 2
        + [jax.ShapeDtypeStruct((tokens, width), low)] * groups,
        scratch_shapes=[pltpu.VMEM((groups * tokens, width), jnp.float32)],
        compiler_params=pltpu.CompilerParams(vmem_limit_bytes=60 * 2**20),
        cost_estimate=cheap,
        name="mlp_core",
    )(*rows_in, *grads_in, w_mlp, w_mlp, *after)


nt = (((1,), (1,)), ((), ()))
tn = (((0,), (0,)), ((), ()))


def dot(left, right, dims=(((1,), (0,)), ((), ()))):
    return lax.dot_general(left, right, dims, preferred_element_type=jnp.float32)


def softmax_keys(keys, queries):
    scores = dot(keys, queries, nt) * HEAD_DIM ** (-0.5)
    expo = jnp.exp(scores - jnp.max(scores, axis=0, keepdims=True))
    return expo * (1.0 / jnp.sum(expo, axis=0, keepdims=True))


def cuts_of(width):
    size = 384 if width % 384 == 0 else width
    return [slice(i, i + size) for i in range(0, width, size)]


def in_smem():
    return pl.BlockSpec(memory_space=pltpu.SMEM)


def in_vmem():
    return pl.BlockSpec(memory_space=pltpu.VMEM)


def cross_block(place, mixed, hidden, rows, text, w_out, c_query, c_value, c_out):
    count, share = len(mixed), mixed[0].shape[1]
    tokens, width = hidden.shape
    words = text.shape[0]
    per = share // HEAD_DIM

    def body(place_ref, *refs):
        parts = refs[:count]
        x_ref, rows_ref, text_ref = refs[count : count + 3]
        far = refs[count + 3 : count + 7]
        outs = refs[count + 7 : count + 16]
        inverse = refs[count + 16]
        wo, wq, wv, wc, *own = refs[count + 17 : -3]
        held, read, sems = refs[-3:]
        branch, res_low, cq, ck, cv, crossed, res, normed, out = own
        me = place_ref[0]
        loads = [
            pltpu.make_async_copy(source, target, read.at[i])
            for i, (source, target) in enumerate(zip(far, (wo, wq, wv, wc)))
        ]
        stores = [
            pltpu.make_async_copy(source, target, sems.at[i])
            for i, (source, target) in enumerate(zip(own, outs))
        ]
        for load in loads:
            load.start()
        loads[0].wait()
        for cut in cuts_of(width):
            total = jnp.zeros((tokens, cut.stop - cut.start), jnp.float32)
            for k in range(count):
                rank = lax.rem(me + k, count)
                here = pl.ds(pl.multiple_of(rank * share, 32), share)
                total += dot(parts[k][0:tokens, :], wo[here, cut])
            branch[:, cut] = total
            first = x_ref[:, cut].astype(jnp.float32) + rows_ref[0:1, cut] * total
            res[:, cut] = first
            res_low[:, cut] = first.astype(low)
        stores[0].start()
        stores[1].start()
        loads[1].wait()
        loads[2].wait()
        for cut in cuts_of(width):
            cq[:, cut] = dot(res_low[...], wq[cut, :], nt).astype(low)
            cv[:, cut] = dot(text_ref[...], wv[cut, :], nt).astype(low)
        for k in range(count):
            held[lax.rem(me + k, count)] = parts[k][tokens:, :]
        ck[...] = jnp.concatenate([held[rank] for rank in range(count)], axis=1)
        for i in (2, 3, 4):
            stores[i].start()
        parts_out = []
        for at in range(0, width, HEAD_DIM):
            head = slice(at, at + HEAD_DIM)
            probs = softmax_keys(ck[:, head], cq[:, head]).astype(low)
            parts_out.append(dot(cv[:, head], probs, tn).T)
        crossed[...] = jnp.concatenate(parts_out, axis=1).astype(low)
        stores[5].start()
        loads[3].wait()
        for cut in cuts_of(width):
            res[:, cut] += dot(crossed[...], wc[:, cut])
        second = res[...]
        center = second - jnp.mean(second, axis=-1, keepdims=True)
        spread = lax.rsqrt(jnp.mean(center * center, axis=-1, keepdims=True) + norm_eps)
        inverse[...] = spread
        scaled = center * spread
        normed[...] = scaled
        stores[6].start()
        stores[7].start()
        out[...] = (scaled * (1.0 + rows_ref[2:3, :]) + rows_ref[1:2, :]).astype(low)
        stores[8].start()
        for store in stores:
            store.wait()

    wide = (tokens, width)
    shapes = [
        (wide, jnp.float32),
        (wide, low),
        (wide, low),
        ((words, width), low),
        ((words, width), low),
        (wide, low),
        (wide, jnp.float32),
        (wide, jnp.float32),
        (wide, low),
    ]
    anywhere = pl.BlockSpec(memory_space=pl.ANY)
    return pl.pallas_call(
        body,
        in_specs=[in_smem()] + [in_vmem()] * (count + 3) + [anywhere] * 4,
        out_specs=[anywhere] * len(shapes) + [in_vmem()],
        out_shape=[jax.ShapeDtypeStruct(*item) for item in shapes]
        + [jax.ShapeDtypeStruct((tokens, 1), jnp.float32)],
        scratch_shapes=[pltpu.VMEM((width, width), low)] * 4
        + [pltpu.VMEM(*item) for item in shapes]
        + [
            pltpu.VMEM((count, words, share), low),
            pltpu.SemaphoreType.DMA((4,)),
            pltpu.SemaphoreType.DMA((len(shapes),)),
        ],
        compiler_params=pltpu.CompilerParams(vmem_limit_bytes=60 * 2**20),
        cost_estimate=cheap,
        name="cross_block",
    )(place, *mixed, hidden, rows, text, w_out, c_query, c_value, c_out)


def cross_back(place, terms, grad, rows, normed, inverse, branch, cq, ck, cv, c_out, c_query, w_out):
    count = len(terms)
    tokens, width = grad.shape
    words = ck.shape[0]
    share = width // count
    scale = HEAD_DIM ** (-0.5)

    def body(place_ref, *refs):
        parts = refs[:count]
        grad_ref, rows_ref, i_ref, k_ref, v_ref = refs[count : count + 5]
        far = refs[count + 5 : count + 11]
        stored = refs[count + 11 : count + 15]
        grad_v, sums = refs[count + 15 : count + 17]
        outs = refs[count + 17 : 2 * count + 17]
        near = refs[2 * count + 17 : 2 * count + 23]
        n_ref, wc, q_ref, wq, wo, b_ref = near
        own = refs[2 * count + 23 : 2 * count + 27]
        first, cross_low, grad_q, attn_low = own
        back, held, read, sems = refs[2 * count + 27 :]
        me = place_ref[0]
        loads = [
            pltpu.make_async_copy(source, target, read.at[i])
            for i, (source, target) in enumerate(zip(far, near))
        ]
        stores = [
            pltpu.make_async_copy(source, target, sems.at[i])
            for i, (source, target) in enumerate(zip(own, stored))
        ]
        for load in loads:
            load.start()
        loads[0].wait()
        total = parts[0][...].astype(jnp.float32)
        for part in parts[1:]:
            total += part[...].astype(jnp.float32)
        n = n_ref[...]
        sums[1:2, :] = jnp.sum(total, axis=0, keepdims=True)
        sums[2:3, :] = jnp.sum(total * n, axis=0, keepdims=True)
        second = grad_ref[...].astype(jnp.float32) + norm_back(total, n, i_ref[...], rows_ref[2:3, :])
        first[...] = second
        cross_low[...] = second.astype(low)
        stores[1].start()
        loads[1].wait()
        loads[2].wait()
        for cut in cuts_of(width):
            back[:, cut] = dot(cross_low[...], wc[cut, :], nt).astype(low)
        grads = ([], [], [])
        for at in range(0, width, HEAD_DIM):
            head = slice(at, at + HEAD_DIM)
            q, k, v, g = q_ref[:, head], k_ref[:, head], v_ref[:, head], back[:, head]
            probs = softmax_keys(k, q)
            grad_probs = dot(v, g, nt)
            inner = jnp.sum(probs * grad_probs, axis=0, keepdims=True)
            grad_scores = (probs * (grad_probs - inner)).astype(low)
            grads[0].append((dot(k, grad_scores, tn) * scale).T)
            grads[1].append(dot(grad_scores, q) * scale)
            grads[2].append(dot(probs.astype(low), g))
        grad_q[...] = jnp.concatenate(grads[0], axis=1).astype(low)
        grad_v[...] = jnp.concatenate(grads[2], axis=1).astype(low)
        heads = share // HEAD_DIM
        for rank in range(count):
            pieces = grads[1][rank * heads : (rank + 1) * heads]
            held[rank] = jnp.concatenate(pieces, axis=1).astype(low)
        stores[2].start()
        for load in loads[3:]:
            load.wait()
        for cut in cuts_of(width):
            whole = first[:, cut] + dot(grad_q[...], wq[:, cut])
            first[:, cut] = whole
            attn_low[:, cut] = (rows_ref[0:1, cut] * whole).astype(low)
            sums[0:1, cut] = jnp.sum(b_ref[:, cut] * whole, axis=0, keepdims=True)
        stores[0].start()
        stores[3].start()
        for k in range(count):
            rank = lax.rem(me + k, count)
            here = pl.ds(pl.multiple_of(rank * share, 32), share)
            outs[k][0:tokens, :] = dot(attn_low[...], wo[here, :], nt).astype(low)
            outs[k][tokens:, :] = held[rank]
        for store in stores:
            store.wait()

    wide, square = (tokens, width), (width, width)
    shapes = [
        (wide, jnp.float32),
        (wide, low),
        (wide, low),
        (wide, low),
        ((words, width), low),
        ((3, width), jnp.float32),
    ] + [((tokens + words, share), low)] * count
    anywhere = pl.BlockSpec(memory_space=pl.ANY)
    loaded = [
        pltpu.VMEM(wide, jnp.float32),
        pltpu.VMEM(square, low),
        pltpu.VMEM(wide, low),
        pltpu.VMEM(square, low),
        pltpu.VMEM(square, low),
        pltpu.VMEM(wide, jnp.float32),
    ]
    return pl.pallas_call(
        body,
        in_specs=[in_smem()] + [in_vmem()] * (count + 5) + [anywhere] * 6,
        out_specs=[anywhere] * 4 + [in_vmem()] * (2 + count),
        out_shape=[jax.ShapeDtypeStruct(*item) for item in shapes],
        scratch_shapes=loaded
        + [pltpu.VMEM(*item) for item in shapes[:4]]
        + [
            pltpu.VMEM(wide, low),
            pltpu.VMEM((count, words, share), low),
            pltpu.SemaphoreType.DMA((6,)),
            pltpu.SemaphoreType.DMA((4,)),
        ],
        compiler_params=pltpu.CompilerParams(vmem_limit_bytes=60 * 2**20),
        cost_estimate=cheap,
        name="cross_back",
    )(place, *terms, grad, rows, inverse, ck, cv, normed, c_out, cq, c_query, w_out, branch)


def outer_halves(place, pairs, parts, name):
    width = pairs[0][1].shape[1]
    high = [sum(piece[2] for piece in left) for left, _ in pairs]
    size = high[0] // parts
    tokens = [right.shape[0] for _, right in pairs]
    flat = []

    def index_of(array):
        for i, other in enumerate(flat):
            if other is array:
                return i
        flat.append(array)
        return len(flat) - 1

    plans = [
        ([(index_of(array), *rest) for array, *rest in left], index_of(right))
        for left, right in pairs
    ]
    amount = len(pairs)

    def body(place_ref, *refs):
        ins, (kept, given), (held, sems) = refs[: len(flat)], refs[len(flat) :][:2], refs[-2:]
        turned = refs[len(flat) + 2 : -2]
        me, core = place_ref[0], place_ref[1]
        for i, (left, right) in enumerate(plans):
            for k, (which, lane, lanes, row) in enumerate(left):
                piece = ins[which][0 : tokens[i], lane : lane + lanes]
                piece = piece.astype(jnp.float32).T.astype(low)
                if row is None:
                    rank = lax.rem(me + k, len(left))
                    turned[i][pl.ds(pl.multiple_of(rank * lanes, 32), lanes), :] = piece
                else:
                    turned[i][row : row + lanes, :] = piece
            for part in range(parts):
                at = i * parts + part
                tile = dot(turned[i][part * size : (part + 1) * size, :], ins[right][...])
                held[at] = tile.astype(low)
                for out, side in ((kept, 0), (given, 1)):

                    @pl.when((core ^ (i & 1)) == side)
                    def _():
                        pltpu.make_async_copy(
                            held.at[at], out.at[i // 2, part], sems.at[at]
                        ).start()

        for at in range(amount * parts):
            pltpu.make_async_copy(held.at[at], kept.at[0, 0], sems.at[at]).wait()

    out = jax.ShapeDtypeStruct((amount // 2, parts, size, width), low)
    return pl.pallas_call(
        body,
        in_specs=[in_smem()] + [in_vmem()] * len(flat),
        out_specs=[pl.BlockSpec(memory_space=pl.ANY)] * 2,
        out_shape=[out, out],
        scratch_shapes=[pltpu.VMEM((high[i], tokens[i]), low) for i in range(amount)]
        + [
            pltpu.VMEM((amount * parts, size, width), low),
            pltpu.SemaphoreType.DMA((amount * parts,)),
        ],
        compiler_params=pltpu.CompilerParams(vmem_limit_bytes=60 * 2**20),
        cost_estimate=cheap if parts > 1 else costly,
        name=name,
    )(place, *flat)


def mlp_grads(grad_pres, acts, rows_in, grads_in, sofar=()):
    pieces, rights = len(acts), len(rows_in)
    tokens, width = rows_in[0].shape
    hidden = acts[0].shape[1]
    chunk = 384 if hidden % 384 == 0 else hidden
    steps = hidden // chunk

    def body(*refs):
        step = pl.program_id(0)
        lefts_up, lefts_down = refs[:pieces], refs[pieces : 2 * pieces]
        rights_up = refs[2 * pieces : 2 * pieces + rights]
        rights_down = refs[2 * pieces + rights : 2 * pieces + 2 * rights]
        before = refs[2 * pieces + 2 * rights : -2]
        out, token = refs[-2:]
        token[...] = jnp.zeros_like(token)

        def terms(lefts, turn, others):
            here = pl.ds(pl.multiple_of(turn * chunk, chunk), chunk)
            total = jnp.zeros((chunk, width), jnp.float32)
            for item in before:
                total += item[...].astype(jnp.float32)
            cursor = 0
            for left in lefts:
                for i in range(left.shape[0] // tokens):
                    total += dot(left[i * tokens : (i + 1) * tokens, here], others[cursor][...], tn)
                    cursor += 1
            out[...] = total.astype(low)

        @pl.when(step < steps)
        def _():
            terms(lefts_up, step, rights_up)

        @pl.when(step >= steps)
        def _():
            terms(lefts_down, step - steps, rights_down)

    arrays = (*grad_pres, *acts, *rows_in, *grads_in)
    chunked = pl.BlockSpec((chunk, width), lambda s: (s, 0))
    return pl.pallas_call(
        body,
        grid=(2 * steps,),
        in_specs=[pl.BlockSpec(array.shape, lambda s: (0, 0)) for array in arrays]
        + [chunked] * len(sofar),
        out_specs=[chunked, pl.BlockSpec((8, 128), lambda s: (0, 0))],
        out_shape=[
            jax.ShapeDtypeStruct((2 * hidden, width), low),
            jax.ShapeDtypeStruct((8, 128), jnp.float32),
        ],
        compiler_params=pltpu.CompilerParams(vmem_limit_bytes=60 * 2**20),
        cost_estimate=cheap,
        name="mlp_grads",
    )(*arrays, *sofar)


def ranked_terms(place, lefts, order, pieces, weight, factors, name):
    tokens, width = factors[0].shape
    count = len(factors)

    def body(place_ref, *refs):
        ins, weight_ref = refs[: len(lefts)], refs[len(lefts)]
        others = refs[len(lefts) + 1 : len(lefts) + 1 + count]
        out, sums = refs[-2:]
        me = place_ref[0]
        for i, slot in enumerate(order):
            rank = lax.rem(me - slot + count, count)
            for cut in cuts_of(width):
                term = jnp.zeros((tokens, cut.stop - cut.start), jnp.float32)
                for which, row, lane, start, depth in pieces[i]:
                    term += dot(
                        ins[which][row : row + tokens, lane : lane + depth],
                        weight_ref[start : start + depth, cut],
                    )
                out[rank, :, cut] = term.astype(low)
                one = jnp.sum(term, axis=0, keepdims=True)
                two = jnp.sum(term * others[i][:, cut].astype(jnp.float32), axis=0, keepdims=True)
                if i:
                    one, two = one + sums[0:1, cut], two + sums[1:2, cut]
                sums[0:1, cut], sums[1:2, cut] = one, two

    return pl.pallas_call(
        body,
        in_specs=[in_smem()] + [in_vmem()] * (len(lefts) + 1 + count),
        out_shape=[
            jax.ShapeDtypeStruct((count, tokens, width), low),
            jax.ShapeDtypeStruct((2, width), jnp.float32),
        ],
        compiler_params=pltpu.CompilerParams(vmem_limit_bytes=60 * 2**20),
        cost_estimate=cheap if len(lefts) > 2 else costly,
        name=name,
    )(place, *lefts, weight, *factors)


def update_slots(master, first_moment, second_moment, filled, which, position, sources):
    capacity, unit_rows, width = master.shape

    group = math.gcd(capacity, 2)
    steps = capacity // group

    def body(filled_ref, which_ref, position_ref, weight, one, two, *rest):
        ins = rest[: len(sources)]
        new_one, new_two, new_weight, held, sems = rest[len(sources) :]
        step = pl.program_id(0)

        def fetch(turn):
            for i in range(group):
                slot = turn * group + i
                for source, ref in enumerate(ins):

                    @pl.when(which_ref[slot] == source)
                    def _():
                        pltpu.make_async_copy(
                            ref.at[position_ref[slot]], held.at[turn % 2, i], sems.at[turn % 2, i]
                        ).start()

        @pl.when(step == 0)
        def _():
            fetch(step)

        @pl.when(step < steps - 1)
        def _():
            fetch(step + 1)

        for i in range(group):
            pltpu.make_async_copy(
                ins[0].at[0], held.at[step % 2, i], sems.at[step % 2, i]
            ).wait()
            mask = (filled_ref[step * group + i] > 0).astype(jnp.float32)
            grad = held[step % 2, i].astype(jnp.float32)
            results = adamw(weight[i], one[i], two[i], grad, mask, rate)
            new_one[i], new_two[i], new_weight[i] = results

    block = pl.BlockSpec((group, unit_rows, width), lambda s, *_: (s, 0, 0))
    return pl.pallas_call(
        body,
        grid_spec=pltpu.PrefetchScalarGridSpec(
            num_scalar_prefetch=3,
            grid=(steps,),
            in_specs=[block] * 3 + [pl.BlockSpec(memory_space=pl.ANY)] * len(sources),
            out_specs=[block] * 3,
            scratch_shapes=[
                pltpu.VMEM((2, group, unit_rows, width), low),
                pltpu.SemaphoreType.DMA((2, group)),
            ],
        ),
        out_shape=[jax.ShapeDtypeStruct(master.shape, jnp.float32)] * 3,
        compiler_params=pltpu.CompilerParams(vmem_limit_bytes=56 * 2**20),
        cost_estimate=cheap,
        name="update_slots",
    )(filled, which, position, master, first_moment, second_moment, *sources)


def adamw(weight, moment_one, moment_two, gradient, filled, step_rate):
    new_one = beta_one * moment_one + (1.0 - beta_one) * gradient
    new_two = beta_two * moment_two + (1.0 - beta_two) * gradient * gradient
    fixed_one = new_one / (1.0 - beta_one**STEP)
    fixed_two = new_two / (1.0 - beta_two**STEP)
    updated = weight - step_rate * (fixed_one / (jnp.sqrt(fixed_two) + adam_eps) + decay * weight)
    return (new_one * filled, new_two * filled, updated * filled)


def swap(values, axis, bit):
    count = lax.axis_size(axis)
    return lax.ppermute(values, axis, [(i, i ^ (1 << bit)) for i in range(count)])


def choose(values, index, axis):
    return lax.dynamic_index_in_dim(values, index, axis, keepdims=False)


def total_sum(values):
    for axis in ("dp", "tensor"):
        for bit in range(lax.axis_size(axis).bit_length() - 1):
            values = values + swap(values, axis, bit)
    return values


def pick_units(master, slot_unit, state, kind, place, sizes):
    capacity, unit_rows, width = master.shape
    units = state.shape[0]

    def body(slot_ref, state_ref, kind_ref, place_ref, blocks, *rest):
        outs, (highs, lows, zeros, read, sems) = rest[: len(sizes)], rest[len(sizes) :]

        def start(source, unit):
            for which, out in enumerate(outs):

                @pl.when(kind_ref[unit] == which)
                def _():
                    pltpu.make_async_copy(source, out.at[place_ref[unit]], sems.at[unit]).start()

        @pl.loop(0, capacity)
        def _(slot):
            @pl.when(slot_ref[slot] >= 0)
            def _():
                pltpu.make_async_copy(blocks.at[slot], highs.at[slot], read.at[slot]).start()

        zeros[...] = jnp.zeros_like(zeros)

        @pl.loop(0, units)
        def _(unit):
            @pl.when(state_ref[unit] == 0)
            def _():
                start(zeros, unit)

        @pl.loop(0, capacity)
        def _(slot):
            @pl.when(slot_ref[slot] >= 0)
            def _():
                pltpu.make_async_copy(blocks.at[slot], highs.at[slot], read.at[slot]).wait()
                lows[slot] = highs[slot].astype(low)
                start(lows.at[slot], slot_ref[slot])

        @pl.loop(0, units)
        def _(unit):
            @pl.when(state_ref[unit] < 2)
            def _():
                pltpu.make_async_copy(zeros, outs[0].at[0], sems.at[unit]).wait()

    return pl.pallas_call(
        body,
        grid_spec=pltpu.PrefetchScalarGridSpec(
            num_scalar_prefetch=4,
            grid=(1,),
            in_specs=[pl.BlockSpec(memory_space=pl.ANY)],
            out_specs=[pl.BlockSpec(memory_space=pl.ANY)] * len(sizes),
            scratch_shapes=[
                pltpu.VMEM((capacity, unit_rows, width), jnp.float32),
                pltpu.VMEM((capacity, unit_rows, width), low),
                pltpu.VMEM((unit_rows, width), low),
                pltpu.SemaphoreType.DMA((capacity,)),
                pltpu.SemaphoreType.DMA((units,)),
            ],
        ),
        out_shape=[jax.ShapeDtypeStruct((size, unit_rows, width), low) for size in sizes],
        compiler_params=pltpu.CompilerParams(vmem_limit_bytes=56 * 2**20),
        cost_estimate=cheap,
        name="pick_units",
    )(slot_unit, state, kind, place, master)


def place_blocks(sources, which, position, parts=1):
    amount = which.shape[0]
    shape = sources[0].shape[1:]
    size = amount // parts

    def body(which_ref, position_ref, *rest):
        ins, outs = rest[: len(sources)], rest[len(sources) : len(sources) + parts]
        held, read, sems = rest[len(sources) + parts :]

        @pl.loop(0, amount)
        def _(i):
            for source, ref in enumerate(ins):

                @pl.when(which_ref[i] == source)
                def _():
                    pltpu.make_async_copy(ref.at[position_ref[i]], held.at[i], read.at[i]).start()

        for part, out in enumerate(outs):

            @pl.loop(0, size)
            def _(j):
                i = part * size + j
                pltpu.make_async_copy(ins[0].at[0], held.at[i], read.at[i]).wait()
                pltpu.make_async_copy(held.at[i], out.at[j], sems.at[i]).start()

        @pl.loop(0, amount)
        def _(i):
            pltpu.make_async_copy(held.at[i], outs[0].at[0], sems.at[i]).wait()

    return pl.pallas_call(
        body,
        grid_spec=pltpu.PrefetchScalarGridSpec(
            num_scalar_prefetch=2,
            grid=(1,),
            in_specs=[pl.BlockSpec(memory_space=pl.ANY)] * len(sources),
            out_specs=[pl.BlockSpec(memory_space=pl.ANY)] * parts,
            scratch_shapes=[
                pltpu.VMEM((amount,) + shape, low),
                pltpu.SemaphoreType.DMA((amount,)),
                pltpu.SemaphoreType.DMA((amount,)),
            ],
        ),
        out_shape=[jax.ShapeDtypeStruct((size,) + shape, low)] * parts,
        compiler_params=pltpu.CompilerParams(vmem_limit_bytes=56 * 2**20),
        cost_estimate=cheap,
        name="place_blocks",
    )(which, position, *sources)


def hops(values, step, turn):
    count = lax.axis_size("tensor")
    if step > 0:
        pairs = [(i, i + 1) for i in range(turn - 1, count - 1)]
    else:
        pairs = [(i, i - 1) for i in range(1, count - turn + 1)]
    return lax.ppermute(values, "tensor", pairs)


def slots_of(own, ups, downs):
    count = lax.axis_size("tensor")
    me = lax.axis_index("tensor")
    return [own] + [jnp.where(me >= k, ups[k - 1], downs[count - k - 1]) for k in range(1, count)]


fence = lax.optimization_barrier


def in_pool(member, inner, inner_count):
    me = lax.axis_index("dp")
    half, core = member >> 3, ((member >> 2) & 1) ^ (me & 1)
    far_y, far_x = ((member >> 1) & 1) ^ ((me >> 2) & 1), (member & 1) ^ ((me >> 1) & 1)
    where_first = (far_y * 2 + far_x) * inner_count
    where_second = (4 + far_x * 2 + far_y) * inner_count
    return (core, jnp.where(half == 0, where_first, where_second) + inner)


def on_device(
    hidden_in,
    time_embed,
    caption_table,
    caption_ids,
    owners,
    master,
    first_moment,
    second_moment,
    mod_table,
    mod_first,
    mod_second,
    out_grad,
):
    count = lax.axis_size("tensor")
    dp_count = lax.axis_size("dp")
    me_dp = lax.axis_index("dp")
    me_tensor = lax.axis_index("tensor")
    capacity, unit_rows, width = master.shape
    units = owners.shape[0]
    tokens = hidden_in.shape[1]
    text_count = caption_ids.shape[1]
    share = width // count
    per = share // unit_rows
    ups = (units - 8 * per) // 2
    rank_of = ranks_of(owners)
    mine = owners == me_dp
    match = (rank_of[None, :] == jnp.arange(capacity)[:, None]) & mine[None, :]
    filled = jnp.any(match, axis=1)
    unit_of_slot = jnp.sum(jnp.where(match, jnp.arange(units)[None, :], 0), axis=1)

    square = [list(range(i * per, (i + 1) * per)) for i in range(8)]
    group_attn = square[0] + square[1] + square[2] + square[5]
    group_full = square[3] + square[4] + square[6] + square[7]
    group_mlp = list(range(8 * per, units))
    members = len(group_attn)
    plane = dp_count == 8 and members == 16 and len(group_mlp) % dp_count == 0
    member_of = np.zeros(units, np.int32)
    member_of[group_attn] = np.arange(members)
    member_of[group_full] = np.arange(members)
    is_attn = np.zeros(units, bool)
    is_attn[group_attn] = True
    is_mlp = np.zeros(units, bool)
    is_mlp[group_mlp] = True

    latent_in = hidden_in[0].astype(jnp.float32)
    modulate = mod_table + time_embed[0]

    def mod_row(which_row):
        return modulate[which_row][None, :]

    normed_one, inverse_one = layer_norm(latent_in)
    bits = dp_count.bit_length() - 1
    vocab_rows = caption_table.shape[0]

    def caption_terms(ids):
        chosen = ids.reshape(-1) - me_dp * vocab_rows
        onehot = (chosen[:, None] == jnp.arange(vocab_rows)[None, :]).astype(low)
        terms = jnp.dot(onehot, caption_table, preferred_element_type=jnp.float32).astype(low)
        return terms.reshape(dp_count, text_count, -1)

    def modulated(normed):
        return (normed.astype(jnp.float32) * (1.0 + mod_row(1)) + mod_row(0)).astype(low)

    def whole_text(text_ring):
        return from_ring(text_ring, -1).transpose(1, 0, 2).reshape(text_count, width)

    def own_keys(text_low, w_attn):
        return project(text_low, w_attn)[:, 3 * share :].astype(low)

    def exchanged(attended, keys):
        parts = [
            jnp.concatenate([attended[k * tokens : (k + 1) * tokens], keys]) for k in range(count)
        ]
        return [parts[0]] + [shift(parts[k], count - k) for k in range(1, count)]

    n_low = normed_one.astype(low)
    if plane:
        core, far_x, far_y = (
            ((member_of >> 2) & 1) ^ (me_dp & 1),
            (member_of & 1) ^ ((me_dp >> 1) & 1),
            ((member_of >> 1) & 1) ^ ((me_dp >> 2) & 1),
        )
        place = jnp.where(is_attn, far_x * 4 + far_y * 2, 8 + far_y * 4 + far_x * 2)
        place = jnp.where(is_mlp, np.arange(units) - 8 * per, place + (member_of >> 3))
        kind = jnp.where(is_mlp, 0, core)
        slot_mlp = unit_of_slot >= 8 * per
        owned_state = mine.astype(jnp.int32)
        ids = lax.all_gather(caption_ids, "dp", axis=0, tiled=True)
        ids = jnp.take(ids, me_dp ^ jnp.arange(dp_count), axis=0, mode="clip")
        up, down = hops(n_low, 1, 1), hops(n_low, -1, 1)
        kept, given = pick_units(
            master,
            jnp.where(filled & ~slot_mlp, unit_of_slot, -1),
            jnp.where(is_mlp, 2, owned_state),
            kind,
            place,
            (members, members),
        )
        got = swap(given, "dp", 0)
        n_up, n_down = [up], [down]
        kept, got, up, down, ids = fence((kept, got, up, down, ids))
        pieces = [kept[i : i + 4] + got[i : i + 4] for i in range(0, members, 4)]
        attn_two, attn_send, full_two, full_send = fence(tuple(pieces))
        up, down = hops(up, 1, 2), hops(down, -1, 2)
        attn_got = swap(attn_send, "dp", 1)
        full_got = swap(full_send, "dp", 2)
        text = caption_terms(ids)
        text = text[0:4] + swap(text[4:8], "dp", 2)
        (mlp_part,) = pick_units(
            fence((master, got))[0],
            jnp.where(filled & slot_mlp, unit_of_slot, -1),
            jnp.where(is_mlp, owned_state, 2),
            kind,
            place,
            (len(group_mlp),),
        )
        n_up.append(up), n_down.append(down)
        attn_two, attn_got, full_two, full_got, up, down, text, mlp_part = fence(
            (attn_two, attn_got, full_two, full_got, up, down, text, mlp_part)
        )
        pieces = [x[i : i + 2] + y[i : i + 2] for x, y in ((attn_two, attn_got), (full_two, full_got)) for i in (0, 2)]
        attn_one, attn_send, full_one, full_send = fence(tuple(pieces))
        up, down = hops(up, 1, 3), hops(down, -1, 3)
        attn_got = swap(attn_send, "dp", 2)
        full_got = swap(full_send, "dp", 1)
        text = text[0:2] + swap(text[2:4], "dp", 1)
        n_up.append(up), n_down.append(down)
        attn_one, attn_got, full_one, full_got, up, down, text, mlp_part = fence(
            (attn_one, attn_got, full_one, full_got, up, down, text, mlp_part)
        )
        attn_one, full_one = attn_one + attn_got, full_one + full_got
        n_up[-1], n_down[-1] = up, down
        mlp_part = lax.psum_scatter(mlp_part, "dp", scatter_dimension=0, tiled=True)
        parcel = full_one.reshape(2 * unit_rows, width)
        parcels = [parcel] + [shift(parcel, k) for k in range(1, count)]
        first = jnp.concatenate([attn_one[0:1], swap(attn_one[0:1], "dp", 1)])
        second = jnp.concatenate([attn_one[1:2], swap(attn_one[1:2], "dp", 2)])
        pool = jnp.concatenate([first, swap(first, "dp", 2), second, swap(second, "dp", 1)])
        other = swap(pool, "dp", 0)
        text = text[0] + swap(text[1], "dp", 0)
        n_slots = slots_of(n_low, n_up, n_down)
        normed_all = jnp.concatenate(n_slots)
        h_one_all = modulated(normed_all)
        grad_own = out_grad[0]
        pool, other, parcels, h_one_all, grad_own, text = fence(
            (pool, other, parcels, h_one_all, grad_own, text)
        )
        grad_whole = lax.all_gather(grad_own, "tensor", axis=0)
        full_ring = [item.reshape(2, unit_rows, width) for item in parcels]
        first = jnp.concatenate([item[0:1] for item in full_ring])
        second = jnp.concatenate([item[1:2] for item in full_ring])
        first_got = swap(first, "dp", 1)
        second_got = swap(second, "dp", 2)
        text_ring = ring(text)
        (w_attn,) = place_blocks((pool, other), *in_pool(np.arange(members), 0, 1))
        w_attn = w_attn.reshape(-1, width)
        qkv = project(h_one_all, w_attn).astype(low)
        attended = self_attend(qkv, share)
        first = jnp.concatenate([first, first_got])
        second = jnp.concatenate([second, second_got])
        first, second, text_ring, attended, w_attn, mlp_part = fence(
            (first, second, text_ring, attended, w_attn, mlp_part)
        )
        w_mlp = lax.all_gather(mlp_part, "dp", axis=0, tiled=True)
        first_far, second_far = swap(first, "dp", 2), swap(second, "dp", 1)
        first_other, second_other = swap(first, "dp", 0), swap(second, "dp", 0)
        text_low = whole_text(jnp.stack(text_ring))
        mixed = exchanged(attended, own_keys(text_low, w_attn))
        first_far, second_far, first_other, second_other, mixed = fence(
            (first_far, second_far, first_other, second_other, mixed)
        )
        first_last, second_last = swap(first_far, "dp", 0), swap(second_far, "dp", 0)
        listing = np.arange(count * members)
        matrix, rank, head = listing // (count * per), listing // per % count, listing % per
        slot = lax.rem(me_tensor - rank + count, count)
        which, position = in_pool(matrix * per + head, slot, count)
        blocks = 2 * count
        w_full = place_blocks(
            (first, first_far, second, second_far, first_other, first_last, second_other, second_last),
            which * 4 + position // blocks,
            position % blocks,
            parts=4,
        )
        w_full = [part.reshape(width, width) for part in w_full]
    else:
        slots_low = master.astype(low)
        rows = jnp.take(slots_low, rank_of, axis=0, mode="clip")
        rows = lax.psum(jnp.where(mine[:, None, None], rows, jnp.zeros((), low)), "dp")
        w_attn = rows[np.array(group_attn)].reshape(-1, width)
        w_full = lax.all_gather(rows[np.array(group_full)], "tensor", axis=0)
        w_full = w_full.reshape(count, 4, share, width).swapaxes(0, 1).reshape(4, width, width)
        w_full = [w_full[i] for i in range(4)]
        w_mlp = rows[8 * per :]
        n_slots = ring(n_low)
        normed_all = jnp.concatenate(n_slots)
        grad_whole = lax.all_gather(out_grad[0], "tensor", axis=0)
        ids = caption_ids
        for bit in range(bits):
            ids = jnp.concatenate([ids, swap(ids, "dp", bit)])
        text = caption_terms(ids)
        for bit in reversed(range(bits)):
            text = text[: 1 << bit] + swap(text[1 << bit :], "dp", bit)
        text_low = whole_text(jnp.stack(ring(text[0])))
        h_one_all = modulated(normed_all)
        qkv = project(h_one_all, w_attn).astype(low)
        mixed = exchanged(self_attend(qkv, share), own_keys(text_low, w_attn))
    w_cross = w_full
    w_out, c_query, c_value, c_out = w_full
    w_mlp = w_mlp.reshape(-1, width)

    where = jnp.stack([me_tensor, me_dp & 1]).astype(jnp.int32)
    rows = jnp.concatenate([mod_row(2), mod_row(3), mod_row(4)])
    (
        branch_one,
        first_low,
        cq_rows,
        ck_rows,
        cv_rows,
        crossed,
        second_res,
        normed_two,
        h_two,
        inverse_two,
    ) = cross_block(
        where, mixed, hidden_in[0], rows, text_low, *w_cross
    )

    h_slots = ring(h_two)
    out_slots = [
        choose(grad_whole, lax.rem(me_tensor - k + count, count), 0) for k in range(count)
    ]
    grad_slots = [(mod_row(5) * item.astype(jnp.float32)).astype(low) for item in out_slots]
    near = [k for k in range(1, count) if 2 * k != count]
    far = [k for k in range(1, count) if 2 * k == count]
    acts, grad_pres, grad_terms, order = [], [], [], []
    sofar, after = (), ()
    for members_now in ([0], near, far):
        rows_now = [h_slots[k] for k in members_now]
        grads_now = [grad_slots[k] for k in members_now]
        if members_now == far:
            partial, token = mlp_grads(
                grad_pres, acts, [h_slots[k] for k in order], [grad_slots[k] for k in order]
            )
            sofar, after = (partial,), (token,)
        act, grad_pre, *terms = mlp_core(rows_now, grads_now, w_mlp, after)
        acts.append(act), grad_pres.append(grad_pre)
        order += members_now
        grad_terms += [
            shift(term, count - k) if k else term for k, term in zip(members_now, terms)
        ]
    mlp_grad, token = mlp_grads(grad_pres[-1:], acts[-1:], rows_now, grads_now, sofar)
    mlp_grad = mlp_grad.reshape(-1, unit_rows, width)
    hidden_share = w_mlp.shape[0] // 2
    pieces = [
        [(which, row, 0, hidden_share, hidden_share)]
        for which, act in enumerate(acts)
        for row in range(0, act.shape[0], tokens)
    ]
    branch_terms, branch_sums = ranked_terms(
        where, acts, order, pieces, w_mlp, [out_slots[k] for k in order], "mlp_out"
    )
    branch_row = branch_sums[1]
    grad_terms, branch_terms = fence((grad_terms, branch_terms))
    if plane:
        mlp_sum = lax.psum_scatter(mlp_grad, "dp", scatter_dimension=0, tiled=True)

    (
        first_grad,
        cross_low,
        grad_cq,
        attn_low,
        grad_cv,
        row_sums,
        *grad_mixed,
    ) = cross_back(
        where,
        grad_terms,
        out_grad[0],
        rows,
        normed_two,
        inverse_two,
        branch_one,
        cq_rows,
        ck_rows,
        cv_rows,
        c_out,
        c_query,
        w_out,
    )

    grad_parts = [grad_mixed[0]] + [shift(grad_mixed[k], k) for k in range(1, count)]
    full_pairs = [
        ([(item, 0, share, None) for item in mixed], attn_low),
        ([(grad_cq, 0, width, 0)], first_low),
        ([(grad_cv, 0, width, 0)], text_low),
        ([(crossed, 0, width, 0)], cross_low),
    ]
    half = (share // HEAD_DIM // 2) * HEAD_DIM
    spans = [(0, half), (half, share)]

    def attention_pairs(grads, grad_parts):
        keys = sum(item[tokens:].astype(jnp.float32) for item in grad_parts).astype(low)
        pairs = [
            (
                [
                    (item, i * (end - begin), end - begin, begin)
                    for item, (begin, end) in zip(grads, spans)
                ],
                h_one_all,
            )
            for i in range(3)
        ]
        return pairs + [([(keys, 0, share, 0)], text_low)]

    def input_terms(grads):
        pieces = [
            [
                (which, slot * tokens, i * (end - begin), i * share + begin, end - begin)
                for which, (begin, end) in enumerate(spans)
                for i in range(3)
            ]
            for slot in range(count)
        ]
        return ranked_terms(where, grads, range(count), pieces, w_attn, n_slots, "attn_terms")

    if plane:
        x_bit, y_bit = (me_dp >> 1) & 1, (me_dp >> 2) & 1

        def split(total, bit, axis):
            return (choose(total, bit, axis), choose(total, 1 - bit, axis))

        branch_terms, grad_parts[0], attn_low, mlp_sum = fence(
            (branch_terms, grad_parts[0], attn_low, mlp_sum)
        )
        full_pairs[0] = (full_pairs[0][0], attn_low)
        mlp_sum = lax.all_gather(mlp_sum, "dp", axis=0, tiled=True)
        branch_two = lax.psum_scatter(
            branch_terms.reshape(-1, width), "tensor", scatter_dimension=0, tiled=True
        )
        kept, given = outer_halves(where, full_pairs, count, "full_grads")
        got = swap(given, "dp", 0)
        grad_parts, kept, got = fence((grad_parts, kept, got))
        box = (2, count, 2, 2, unit_rows, width)
        kept, got = kept.reshape(box), got.reshape(box)
        kept_one = choose(kept[0], x_bit, 2) + choose(got[0], x_bit, 2)
        given_one = choose(kept[0], 1 - x_bit, 2) + choose(got[0], 1 - x_bit, 2)
        kept_two = choose(kept[1], y_bit, 1) + choose(got[1], y_bit, 1)
        given_two = choose(kept[1], 1 - y_bit, 1) + choose(got[1], 1 - y_bit, 1)
        kept_one, given_one, kept_two, given_two, grad_parts = fence(
            (kept_one, given_one, kept_two, given_two, grad_parts)
        )
        got_one, got_two = swap(given_one, "dp", 1), swap(given_two, "dp", 2)
        grads_early = self_attend_back(qkv, grad_parts, share, *spans[0])
        kept_one, got_one, kept_two, got_two, grads_early, grad_parts = fence(
            (kept_one, got_one, kept_two, got_two, grads_early, grad_parts)
        )
        kept_one, given_one = split(kept_one + got_one, y_bit, 1)
        kept_two, given_two = split(kept_two + got_two, x_bit, 1)
        kept_one, given_one, kept_two, given_two, grad_parts = fence(
            (kept_one, given_one, kept_two, given_two, grad_parts)
        )
        got_one, got_two = swap(given_one, "dp", 2), swap(given_two, "dp", 1)
        grads_late = self_attend_back(qkv, grad_parts, share, *spans[1])
        kept_one, got_one, kept_two, got_two, grads_early, grads_late, branch_two, mlp_sum = fence(
            (kept_one, got_one, kept_two, got_two, grads_early, grads_late, branch_two, mlp_sum)
        )
        full_parts = jnp.stack([kept_one + got_one, kept_two + got_two], axis=1)
        full_parts, grads_early, grads_late = fence((full_parts, grads_early, grads_late))
        grads_qkv = [grads_early, grads_late]
        full_sum = lax.psum_scatter(full_parts, "tensor", scatter_dimension=0, tiled=True)[0]
        attn_kept, attn_given = outer_halves(
            where, attention_pairs(grads_qkv, grad_parts), 1, "attn_grads"
        )
        attn_got = swap(attn_given, "dp", 0)
        grad_h_terms, grad_h_sums = input_terms(grads_qkv)
        mod_terms = jnp.concatenate([grad_h_sums, row_sums, branch_row[None]])
        grad_h_one = lax.psum_scatter(
            grad_h_terms.reshape(-1, width), "tensor", scatter_dimension=0, tiled=True
        )
        attn_kept, attn_got, mod_terms = fence((attn_kept, attn_got, mod_terms))
        attn_all = (attn_kept + attn_got).reshape(2, 2, 2, unit_rows, width)
        one_kept, one_given = split(attn_all[0], x_bit, 1)
        two_kept, two_given = split(attn_all[1], y_bit, 0)
        one_got, two_got = swap(one_given, "dp", 1), swap(two_given, "dp", 2)
        mod_terms = mod_terms + swap(mod_terms, "dp", 0)
        one_kept, one_got, two_kept, two_got, mod_terms, full_sum = fence(
            (one_kept, one_got, two_kept, two_got, mod_terms, full_sum)
        )
        one_kept, one_given = split(one_kept + one_got, y_bit, 0)
        two_kept, two_given = split(two_kept + two_got, x_bit, 0)
        one_got, two_got = swap(one_given, "dp", 2), swap(two_given, "dp", 1)
        mod_terms = mod_terms + swap(mod_terms, "dp", 1)
        one_kept, one_got, two_kept, two_got, full_sum, mod_terms = fence(
            (one_kept, one_got, two_kept, two_got, full_sum, mod_terms)
        )
        first = jnp.stack([one_kept + one_got, full_sum[0]])
        second = jnp.stack([two_kept + two_got, full_sum[1]])
        first_got, second_got = swap(first, "dp", 1), swap(second, "dp", 2)
        first = jnp.concatenate([first, first_got])
        second = jnp.concatenate([second, second_got])
        mod_terms = mod_terms + swap(mod_terms, "dp", 2)
        first, second, mod_terms = fence((first, second, mod_terms))
        first_far, second_far = swap(first, "dp", 2), swap(second, "dp", 1)
        mod_terms = mod_terms + swap(mod_terms, "tensor", 0)
        first, first_far, second, second_far, mod_terms = fence(
            (first, first_far, second, second_far, mod_terms)
        )
        pool = jnp.concatenate([first, first_far, second, second_far])
        other = swap(pool, "dp", 0)
        mod_terms, grad_h_one = fence((mod_terms, grad_h_one))
        for bit in range(1, count.bit_length() - 1):
            mod_terms = mod_terms + swap(mod_terms, "tensor", bit)
        pool, other, mod_grad, grad_h_one = fence((pool, other, mod_terms, grad_h_one))
        which, position = in_pool(member_of, np.where(is_attn, 0, 1), 2)
        which = jnp.where(is_mlp, 2, which)
        position = jnp.where(is_mlp, np.arange(units) - 8 * per, position)
        own = jnp.sum(jnp.where(match[:, :, None], jnp.stack([which, position], 1)[None], 0), axis=1)
        new_first, new_second, new_master = update_slots(
            master,
            first_moment,
            second_moment,
            filled.astype(jnp.int32),
            own[:, 0],
            own[:, 1],
            (pool, other, mlp_sum),
        )
    else:
        branch_two = lax.psum_scatter(
            branch_terms.reshape(-1, width), "tensor", scatter_dimension=0, tiled=True
        )
        grads_qkv = [self_attend_back(qkv, grad_parts, share, *span) for span in spans]
        attn_grads = [
            outer(array[:, lane : lane + lanes], right).astype(low)
            for left, right in attention_pairs(grads_qkv, grad_parts)
            for array, lane, lanes, row in left
        ]
        grad_h_terms, grad_h_sums = input_terms(grads_qkv)
        grad_h_one = lax.psum_scatter(
            grad_h_terms.reshape(-1, width), "tensor", scatter_dimension=0, tiled=True
        )
        mixed_all = from_ring(jnp.stack([item[:tokens] for item in mixed]), 1)
        mixed_all = mixed_all.transpose(1, 0, 2).reshape(tokens, width)
        full_grads = [outer(mixed_all, attn_low)]
        full_grads += [outer(left[0][0], right) for left, right in full_pairs[1:]]
        full_sum = [g.astype(low).reshape(count, share, width) for g in full_grads]
        full_sum = jnp.stack(full_sum, axis=1)
        full_sum = lax.psum_scatter(full_sum, "tensor", scatter_dimension=0, tiled=True)
        order = np.array(group_attn + group_full + group_mlp)
        sums = jnp.concatenate(
            [jnp.concatenate(attn_grads), full_sum.reshape(-1, width), mlp_grad.reshape(-1, width)]
        )
        sums = lax.psum(sums.reshape(units, unit_rows, width), "dp")
        owned = jnp.take(sums, jnp.array(np.argsort(order))[unit_of_slot], axis=0, mode="clip")
        mod_grad = total_sum(jnp.concatenate([grad_h_sums, row_sums, branch_row[None]]))
        new_first, new_second, new_master = adamw(
            master,
            first_moment,
            second_moment,
            owned.astype(jnp.float32),
            filled.astype(jnp.float32)[:, None, None],
            rate,
        )
    branch_two, second_res, grad_h_one, new_first = fence(
        (branch_two, second_res, grad_h_one, new_first)
    )
    grad_h_one = grad_h_one.astype(jnp.float32)
    block_out = second_res + mod_row(5) * branch_two.astype(jnp.float32)
    input_grad = first_grad + norm_back(grad_h_one, normed_one, inverse_one, mod_row(1))
    mod_new_first, mod_new_second, mod_new = adamw(
        mod_table, mod_first, mod_second, mod_grad, 1.0, table_rate
    )
    return (
        block_out[None],
        input_grad[None],
        new_first,
        new_second,
        new_master,
        mod_new_first,
        mod_new_second,
        mod_new,
    )


def solution(mesh):
    in_specs = (
        P("dp", "tensor", None),
        P("dp", None, None),
        P("dp", "tensor"),
        P("dp", None),
        P(),
        P("dp", "tensor", None),
        P("dp", "tensor", None),
        P("dp", "tensor", None),
        P(),
        P(),
        P(),
        P("dp", "tensor", None),
    )
    out_specs = (
        P("dp", "tensor", None),
        P("dp", "tensor", None),
        P("dp", "tensor", None),
        P("dp", "tensor", None),
        P("dp", "tensor", None),
        P(),
        P(),
        P(),
    )
    return jax.shard_map(
        on_device, mesh=mesh, in_specs=in_specs, out_specs=out_specs, check_vma=False
    )
```

```python
import math

import jax
import jax.numpy as jnp
import numpy as np
from jax import lax
from jax.experimental import pallas as pl
from jax.experimental.pallas import tpu as pltpu
from jax.sharding import PartitionSpec as P

HEAD_DIM = 72
STEP = 10


norm_eps = 1e-06
beta_one = 0.9
beta_two = 0.999
rate = 0.03
table_rate = 0.3
decay = 0.01
adam_eps = 1e-08
low = jnp.bfloat16


def ranks_of(owners):
    index = jnp.arange(owners.shape[0])
    before = (owners[None, :] == owners[:, None]) & (index[None, :] < index[:, None])
    return jnp.sum(before.astype(jnp.int32), axis=1)


def layer_norm(values):
    center = values - jnp.mean(values, axis=-1, keepdims=True)
    inverse = lax.rsqrt(jnp.mean(center * center, axis=-1, keepdims=True) + norm_eps)
    return (center * inverse, inverse)


def norm_back(grad_rows, normed, inverse, scale_row):
    scaled = grad_rows * (1.0 + scale_row)
    mean_one = jnp.mean(scaled, axis=-1, keepdims=True)
    mean_two = jnp.mean(scaled * normed, axis=-1, keepdims=True)
    return inverse * (scaled - mean_one - normed * mean_two)


def project(rows, weight):
    return jnp.einsum("ld,rd->lr", rows, weight, preferred_element_type=jnp.float32)


def expand(rows, weight):
    return jnp.einsum("lr,rd->ld", rows, weight, preferred_element_type=jnp.float32)


def outer(left, right):
    return jnp.einsum("lr,ld->rd", left, right, preferred_element_type=jnp.float32)


def shift(values, step):
    count = lax.axis_size("tensor")
    return lax.ppermute(values, "tensor", [(i, (i + step) % count) for i in range(count)])


def ring(values):
    return [values] + [shift(values, k) for k in range(1, lax.axis_size("tensor"))]


def to_ring(stacked):
    count = stacked.shape[0]
    twice = jnp.concatenate([stacked, stacked], axis=0)
    return lax.dynamic_slice_in_dim(twice, lax.axis_index("tensor"), count, 0)


def from_ring(stacked, sign):
    count = stacked.shape[0]
    me = lax.axis_index("tensor")
    place = lax.rem(sign * (jnp.arange(count) - me) + 2 * count, count)
    return jnp.take(stacked, place, axis=0, mode="clip")


cheap = pl.CostEstimate(flops=1000, bytes_accessed=1000, transcendentals=0)
costly = pl.CostEstimate(flops=10**10, bytes_accessed=10**7, transcendentals=0)


def self_attend(qkv, share):
    length = qkv.shape[0]
    rows = min(512, length)
    curve = HEAD_DIM ** (-0.5) * math.log2(math.e)
    heads = share // HEAD_DIM

    def body(qkv_ref, out_ref, log_ref):
        @pl.loop(0, length // rows)
        def _(step):
            here = pl.ds(pl.multiple_of(step * rows, rows), rows)
            parts = []
            for head in range(heads):
                at = head * HEAD_DIM
                q = qkv_ref[here, at : at + HEAD_DIM]
                k = qkv_ref[:, share + at : share + at + HEAD_DIM]
                v = qkv_ref[:, 2 * share + at : 2 * share + at + HEAD_DIM]
                scores = dot(k, q, nt)
                top = jnp.max(scores, axis=0, keepdims=True)
                expo = jnp.exp2((scores - top) * curve)
                total = jnp.sum(expo, axis=0, keepdims=True)
                log_ref[head : head + 1, here] = top * curve + jnp.log2(total)
                parts.append((dot(v, expo.astype(low), tn) * (1.0 / total)).T)
            out_ref[here, :] = jnp.concatenate(parts, axis=1).astype(low)

    return pl.pallas_call(
        body,
        out_shape=[
            jax.ShapeDtypeStruct((length, share), low),
            jax.ShapeDtypeStruct((heads, length), jnp.float32),
        ],
        compiler_params=pltpu.CompilerParams(vmem_limit_bytes=40 * 2**20),
        cost_estimate=cheap,
        name="self_attend",
    )(qkv)


def self_attend_back(qkv, grads, mixed, logs, share, begin, end):
    length = qkv.shape[0]
    rows = length // len(grads)
    span = end - begin
    scale = HEAD_DIM ** (-0.5)
    curve = scale * math.log2(math.e)

    def body(qkv_ref, mixed_ref, log_ref, *refs):
        grad_refs, (out_ref, grad_k, grad_v) = refs[: len(grads)], refs[len(grads) :]
        for step, grad_ref in enumerate(grad_refs):
            here = slice(step * rows, (step + 1) * rows)
            parts = []
            for head, at in enumerate(range(begin, end, HEAD_DIM)):
                q = qkv_ref[here, at : at + HEAD_DIM]
                k = qkv_ref[:, share + at : share + at + HEAD_DIM]
                v = qkv_ref[:, 2 * share + at : 2 * share + at + HEAD_DIM]
                g = grad_ref[0:rows, at : at + HEAD_DIM]
                o = mixed_ref[here, at : at + HEAD_DIM]
                inner = g.astype(jnp.float32) * o.astype(jnp.float32)
                inner = jnp.sum(inner.T, axis=0, keepdims=True)
                which = begin // HEAD_DIM + head
                probs = jnp.exp2(dot(k, q, nt) * curve - log_ref[which : which + 1, here])
                grad_scores = (probs * (dot(v, g, nt) - inner)).astype(low)
                to_v = dot(probs.astype(low), g)
                to_k = dot(grad_scores, q)
                if step:
                    grad_v[head] += to_v
                    grad_k[head] += to_k
                else:
                    grad_v[head] = to_v
                    grad_k[head] = to_k
                parts.append((dot(k, grad_scores, tn) * scale).T)
            out_ref[here, 0:span] = jnp.concatenate(parts, axis=1).astype(low)
        heads = range(span // HEAD_DIM)
        both = [grad_k[head] * scale for head in heads]
        out_ref[:, span : 2 * span] = jnp.concatenate(both, axis=1).astype(low)
        both = [grad_v[head] for head in heads]
        out_ref[:, 2 * span :] = jnp.concatenate(both, axis=1).astype(low)

    return pl.pallas_call(
        body,
        out_shape=jax.ShapeDtypeStruct((length, 3 * span), low),
        scratch_shapes=[pltpu.VMEM((span // HEAD_DIM, length, HEAD_DIM), jnp.float32)] * 2,
        compiler_params=pltpu.CompilerParams(vmem_limit_bytes=40 * 2**20),
        cost_estimate=cheap,
        name="self_attend_back",
    )(qkv, mixed, logs, *grads)


def mlp_core(rows_in, grads_in, w_mlp, after):
    groups = len(rows_in)
    tokens, width = rows_in[0].shape
    hidden = w_mlp.shape[0] // 2
    chunk = 384 if hidden % 384 == 0 else hidden
    steps = hidden // chunk
    curve = 0.7978845608028654

    def body(*refs):
        rows, grads = refs[:groups], refs[groups : 2 * groups]
        up, down = refs[2 * groups : 2 * groups + 2]
        act, grad_pre, *outs = refs[2 * groups + 2 + len(after) : -1]
        total = refs[-1]
        step = pl.program_id(0)
        for i in range(groups):
            pre = lax.dot_general(
                rows[i][...], up[...], (((1,), (1,)), ((), ())), preferred_element_type=jnp.float32
            )
            square = pre * pre
            bend = jnp.tanh(curve * pre * (1.0 + 0.044715 * square))
            half = 0.5 * (1.0 + bend)
            here = pl.ds(i * tokens, tokens)
            act[here, :] = (pre * half).astype(low)
            slope = half + (0.5 * curve) * pre * (1.0 - bend * bend) * (1.0 + 0.134145 * square)
            grad_act = lax.dot_general(
                grads[i][...], down[...], (((1,), (1,)), ((), ())), preferred_element_type=jnp.float32
            )
            grad_low = (grad_act * slope).astype(low)
            grad_pre[here, :] = grad_low
            term = jnp.dot(grad_low, up[...], preferred_element_type=jnp.float32)

            @pl.when(step == 0)
            def _():
                total[here, :] = term

            @pl.when(step > 0)
            def _():
                total[here, :] += term

            @pl.when(step == steps - 1)
            def _():
                outs[i][...] = total[here, :].astype(low)

    whole = pl.BlockSpec((tokens, width), lambda s: (0, 0))
    across = pl.BlockSpec((groups * tokens, chunk), lambda s: (0, s))
    return pl.pallas_call(
        body,
        grid=(steps,),
        in_specs=[whole] * (2 * groups)
        + [
            pl.BlockSpec((chunk, width), lambda s: (s, 0)),
            pl.BlockSpec((chunk, width), lambda s: (steps + s, 0)),
        ]
        + [pl.BlockSpec(memory_space=pl.ANY)] * len(after),
        out_specs=[across, across] + [whole] * groups,
        out_shape=[jax.ShapeDtypeStruct((groups * tokens, hidden), low)] * 2
        + [jax.ShapeDtypeStruct((tokens, width), low)] * groups,
        scratch_shapes=[pltpu.VMEM((groups * tokens, width), jnp.float32)],
        compiler_params=pltpu.CompilerParams(vmem_limit_bytes=60 * 2**20),
        cost_estimate=cheap,
        name="mlp_core",
    )(*rows_in, *grads_in, w_mlp, w_mlp, *after)


nt = (((1,), (1,)), ((), ()))
tn = (((0,), (0,)), ((), ()))


def dot(left, right, dims=(((1,), (0,)), ((), ()))):
    return lax.dot_general(left, right, dims, preferred_element_type=jnp.float32)


def softmax_keys(keys, queries):
    scores = dot(keys, queries, nt) * HEAD_DIM ** (-0.5)
    expo = jnp.exp(scores - jnp.max(scores, axis=0, keepdims=True))
    return expo * (1.0 / jnp.sum(expo, axis=0, keepdims=True))


def cuts_of(width):
    size = 384 if width % 384 == 0 else width
    return [slice(i, i + size) for i in range(0, width, size)]


def in_smem():
    return pl.BlockSpec(memory_space=pltpu.SMEM)


def in_vmem():
    return pl.BlockSpec(memory_space=pltpu.VMEM)


def line_slots(place, own, ups, downs, rows):
    count = len(ups) + 1
    tokens, width = own.shape

    def body(place_ref, *refs):
        own_ref, up_refs, down_refs = refs[0], refs[1:count], refs[count : 2 * count - 1]
        rows_ref, outs, out = refs[2 * count - 1], refs[2 * count : -1], refs[-1]
        me = place_ref[0]

        def modulate(slot, ref):
            value = ref[...].astype(jnp.float32)
            value = value * (1.0 + rows_ref[1:2, :]) + rows_ref[0:1, :]
            out[slot * tokens : (slot + 1) * tokens, :] = value.astype(low)

        modulate(0, own_ref)
        for k in range(1, count):
            for side, ref in ((me >= k, up_refs[k - 1]), (me < k, down_refs[count - k - 1])):

                @pl.when(side)
                def _():
                    outs[k - 1][...] = ref[...]
                    modulate(k, ref)

    shapes = [(tokens, width)] * (count - 1) + [(count * tokens, width)]
    return pl.pallas_call(
        body,
        in_specs=[in_smem()] + [in_vmem()] * (2 * count),
        out_shape=[jax.ShapeDtypeStruct(shape, low) for shape in shapes],
        compiler_params=pltpu.CompilerParams(vmem_limit_bytes=32 * 2**20),
        cost_estimate=cheap,
        name="line_slots",
    )(place, own, *ups, *downs, rows)


def cross_block(place, mixed, hidden, rows, text, w_out, c_query, c_value, c_out):
    count, share = len(mixed), mixed[0].shape[1]
    tokens, width = hidden.shape
    words = text.shape[0]
    per = share // HEAD_DIM

    def body(place_ref, *refs):
        parts = refs[:count]
        x_ref, rows_ref, text_ref = refs[count : count + 3]
        far = refs[count + 3 : count + 7]
        outs = refs[count + 7 : count + 16]
        inverse = refs[count + 16]
        wo, wq, wv, wc, *own = refs[count + 17 : -3]
        held, read, sems = refs[-3:]
        branch, res_low, cq, ck, cv, crossed, res, normed, out = own
        me = place_ref[0]
        loads = [
            pltpu.make_async_copy(source, target, read.at[i])
            for i, (source, target) in enumerate(zip(far, (wo, wq, wv, wc)))
        ]
        stores = [
            pltpu.make_async_copy(source, target, sems.at[i])
            for i, (source, target) in enumerate(zip(own, outs))
        ]
        for load in loads:
            load.start()
        loads[0].wait()
        for cut in cuts_of(width):
            total = jnp.zeros((tokens, cut.stop - cut.start), jnp.float32)
            for k in range(count):
                rank = lax.rem(me + k, count)
                here = pl.ds(pl.multiple_of(rank * share, 32), share)
                total += dot(parts[k][0:tokens, :], wo[here, cut])
            branch[:, cut] = total
            first = x_ref[:, cut].astype(jnp.float32) + rows_ref[0:1, cut] * total
            res[:, cut] = first
            res_low[:, cut] = first.astype(low)
        stores[0].start()
        stores[1].start()
        loads[1].wait()
        loads[2].wait()
        for cut in cuts_of(width):
            cq[:, cut] = dot(res_low[...], wq[cut, :], nt).astype(low)
            cv[:, cut] = dot(text_ref[...], wv[cut, :], nt).astype(low)
        for k in range(count):
            held[lax.rem(me + k, count)] = parts[k][tokens:, :]
        ck[...] = jnp.concatenate([held[rank] for rank in range(count)], axis=1)
        for i in (2, 3, 4):
            stores[i].start()
        parts_out = []
        for at in range(0, width, HEAD_DIM):
            head = slice(at, at + HEAD_DIM)
            probs = softmax_keys(ck[:, head], cq[:, head]).astype(low)
            parts_out.append(dot(cv[:, head], probs, tn).T)
        crossed[...] = jnp.concatenate(parts_out, axis=1).astype(low)
        stores[5].start()
        loads[3].wait()
        for cut in cuts_of(width):
            res[:, cut] += dot(crossed[...], wc[:, cut])
        second = res[...]
        center = second - jnp.mean(second, axis=-1, keepdims=True)
        spread = lax.rsqrt(jnp.mean(center * center, axis=-1, keepdims=True) + norm_eps)
        inverse[...] = spread
        scaled = center * spread
        normed[...] = scaled
        stores[6].start()
        stores[7].start()
        out[...] = (scaled * (1.0 + rows_ref[2:3, :]) + rows_ref[1:2, :]).astype(low)
        stores[8].start()
        for store in stores:
            store.wait()

    wide = (tokens, width)
    shapes = [
        (wide, jnp.float32),
        (wide, low),
        (wide, low),
        ((words, width), low),
        ((words, width), low),
        (wide, low),
        (wide, jnp.float32),
        (wide, jnp.float32),
        (wide, low),
    ]
    anywhere = pl.BlockSpec(memory_space=pl.ANY)
    return pl.pallas_call(
        body,
        in_specs=[in_smem()] + [in_vmem()] * (count + 3) + [anywhere] * 4,
        out_specs=[anywhere] * len(shapes) + [in_vmem()],
        out_shape=[jax.ShapeDtypeStruct(*item) for item in shapes]
        + [jax.ShapeDtypeStruct((tokens, 1), jnp.float32)],
        scratch_shapes=[pltpu.VMEM((width, width), low)] * 4
        + [pltpu.VMEM(*item) for item in shapes]
        + [
            pltpu.VMEM((count, words, share), low),
            pltpu.SemaphoreType.DMA((4,)),
            pltpu.SemaphoreType.DMA((len(shapes),)),
        ],
        compiler_params=pltpu.CompilerParams(vmem_limit_bytes=60 * 2**20),
        cost_estimate=cheap,
        name="cross_block",
    )(place, *mixed, hidden, rows, text, w_out, c_query, c_value, c_out)


def cross_back(place, terms, grad, rows, normed, inverse, branch, cq, ck, cv, c_out, c_query, w_out):
    count = len(terms)
    tokens, width = grad.shape
    words = ck.shape[0]
    share = width // count
    scale = HEAD_DIM ** (-0.5)

    def body(place_ref, *refs):
        parts = refs[:count]
        grad_ref, rows_ref, i_ref, k_ref, v_ref = refs[count : count + 5]
        far = refs[count + 5 : count + 11]
        stored = refs[count + 11 : count + 15]
        grad_v, sums = refs[count + 15 : count + 17]
        outs = refs[count + 17 : 2 * count + 17]
        near = refs[2 * count + 17 : 2 * count + 23]
        n_ref, wc, q_ref, wq, wo, b_ref = near
        own = refs[2 * count + 23 : 2 * count + 27]
        first, cross_low, grad_q, attn_low = own
        back, held, read, sems = refs[2 * count + 27 :]
        me = place_ref[0]
        loads = [
            pltpu.make_async_copy(source, target, read.at[i])
            for i, (source, target) in enumerate(zip(far, near))
        ]
        stores = [
            pltpu.make_async_copy(source, target, sems.at[i])
            for i, (source, target) in enumerate(zip(own, stored))
        ]
        for load in loads:
            load.start()
        loads[0].wait()
        total = parts[0][...].astype(jnp.float32)
        for part in parts[1:]:
            total += part[...].astype(jnp.float32)
        n = n_ref[...]
        sums[1:2, :] = jnp.sum(total, axis=0, keepdims=True)
        sums[2:3, :] = jnp.sum(total * n, axis=0, keepdims=True)
        second = grad_ref[...].astype(jnp.float32) + norm_back(total, n, i_ref[...], rows_ref[2:3, :])
        first[...] = second
        cross_low[...] = second.astype(low)
        stores[1].start()
        loads[1].wait()
        loads[2].wait()
        for cut in cuts_of(width):
            back[:, cut] = dot(cross_low[...], wc[cut, :], nt).astype(low)
        grads = ([], [], [])
        for at in range(0, width, HEAD_DIM):
            head = slice(at, at + HEAD_DIM)
            q, k, v, g = q_ref[:, head], k_ref[:, head], v_ref[:, head], back[:, head]
            probs = softmax_keys(k, q)
            grad_probs = dot(v, g, nt)
            inner = jnp.sum(probs * grad_probs, axis=0, keepdims=True)
            grad_scores = (probs * (grad_probs - inner)).astype(low)
            grads[0].append((dot(k, grad_scores, tn) * scale).T)
            grads[1].append(dot(grad_scores, q) * scale)
            grads[2].append(dot(probs.astype(low), g))
        grad_q[...] = jnp.concatenate(grads[0], axis=1).astype(low)
        grad_v[...] = jnp.concatenate(grads[2], axis=1).astype(low)
        heads = share // HEAD_DIM
        for rank in range(count):
            pieces = grads[1][rank * heads : (rank + 1) * heads]
            held[rank] = jnp.concatenate(pieces, axis=1).astype(low)
        stores[2].start()
        for load in loads[3:]:
            load.wait()
        for cut in cuts_of(width):
            whole = first[:, cut] + dot(grad_q[...], wq[:, cut])
            first[:, cut] = whole
            attn_low[:, cut] = (rows_ref[0:1, cut] * whole).astype(low)
            sums[0:1, cut] = jnp.sum(b_ref[:, cut] * whole, axis=0, keepdims=True)
        stores[0].start()
        stores[3].start()
        for k in range(count):
            rank = lax.rem(me + k, count)
            here = pl.ds(pl.multiple_of(rank * share, 32), share)
            outs[k][0:tokens, :] = dot(attn_low[...], wo[here, :], nt).astype(low)
            outs[k][tokens:, :] = held[rank]
        for store in stores:
            store.wait()

    wide, square = (tokens, width), (width, width)
    shapes = [
        (wide, jnp.float32),
        (wide, low),
        (wide, low),
        (wide, low),
        ((words, width), low),
        ((3, width), jnp.float32),
    ] + [((tokens + words, share), low)] * count
    anywhere = pl.BlockSpec(memory_space=pl.ANY)
    loaded = [
        pltpu.VMEM(wide, jnp.float32),
        pltpu.VMEM(square, low),
        pltpu.VMEM(wide, low),
        pltpu.VMEM(square, low),
        pltpu.VMEM(square, low),
        pltpu.VMEM(wide, jnp.float32),
    ]
    return pl.pallas_call(
        body,
        in_specs=[in_smem()] + [in_vmem()] * (count + 5) + [anywhere] * 6,
        out_specs=[anywhere] * 4 + [in_vmem()] * (2 + count),
        out_shape=[jax.ShapeDtypeStruct(*item) for item in shapes],
        scratch_shapes=loaded
        + [pltpu.VMEM(*item) for item in shapes[:4]]
        + [
            pltpu.VMEM(wide, low),
            pltpu.VMEM((count, words, share), low),
            pltpu.SemaphoreType.DMA((6,)),
            pltpu.SemaphoreType.DMA((4,)),
        ],
        compiler_params=pltpu.CompilerParams(vmem_limit_bytes=60 * 2**20),
        cost_estimate=cheap,
        name="cross_back",
    )(place, *terms, grad, rows, inverse, ck, cv, normed, c_out, cq, c_query, w_out, branch)


def outer_halves(place, pairs, parts, name):
    width = pairs[0][1].shape[1]
    high = [sum(piece[2] for piece in left) for left, _ in pairs]
    size = high[0] // parts
    tokens = [right.shape[0] for _, right in pairs]
    flat = []

    def index_of(array):
        for i, other in enumerate(flat):
            if other is array:
                return i
        flat.append(array)
        return len(flat) - 1

    plans = [
        ([(index_of(array), *rest) for array, *rest in left], index_of(right))
        for left, right in pairs
    ]
    amount = len(pairs)

    def body(place_ref, *refs):
        ins, (kept, given), (held, sems) = refs[: len(flat)], refs[len(flat) :][:2], refs[-2:]
        turned = refs[len(flat) + 2 : -2]
        me, core = place_ref[0], place_ref[1]
        for i, (left, right) in enumerate(plans):
            for k, (which, lane, lanes, row) in enumerate(left):
                piece = ins[which][0 : tokens[i], lane : lane + lanes]
                piece = piece.astype(jnp.float32).T.astype(low)
                if row is None:
                    rank = lax.rem(me + k, len(left))
                    turned[i][pl.ds(pl.multiple_of(rank * lanes, 32), lanes), :] = piece
                else:
                    turned[i][row : row + lanes, :] = piece
            for part in range(parts):
                at = i * parts + part
                tile = dot(turned[i][part * size : (part + 1) * size, :], ins[right][...])
                held[at] = tile.astype(low)
                for out, side in ((kept, 0), (given, 1)):

                    @pl.when((core ^ (i & 1)) == side)
                    def _():
                        pltpu.make_async_copy(
                            held.at[at], out.at[i // 2, part], sems.at[at]
                        ).start()

        for at in range(amount * parts):
            pltpu.make_async_copy(held.at[at], kept.at[0, 0], sems.at[at]).wait()

    out = jax.ShapeDtypeStruct((amount // 2, parts, size, width), low)
    return pl.pallas_call(
        body,
        in_specs=[in_smem()] + [in_vmem()] * len(flat),
        out_specs=[pl.BlockSpec(memory_space=pl.ANY)] * 2,
        out_shape=[out, out],
        scratch_shapes=[pltpu.VMEM((high[i], tokens[i]), low) for i in range(amount)]
        + [
            pltpu.VMEM((amount * parts, size, width), low),
            pltpu.SemaphoreType.DMA((amount * parts,)),
        ],
        compiler_params=pltpu.CompilerParams(vmem_limit_bytes=60 * 2**20),
        cost_estimate=cheap if parts > 1 else costly,
        name=name,
    )(place, *flat)


def mlp_grads(grad_pres, acts, rows_in, grads_in):
    pieces, rights = len(acts), len(rows_in)
    tokens, width = rows_in[0].shape
    hidden = acts[0].shape[1]
    chunk = 384 if hidden % 384 == 0 else hidden
    steps = hidden // chunk

    def body(*refs):
        step = pl.program_id(0)
        lefts_up, lefts_down = refs[:pieces], refs[pieces : 2 * pieces]
        rights_up = refs[2 * pieces : 2 * pieces + rights]
        rights_down = refs[2 * pieces + rights : -1]
        out = refs[-1]

        def terms(lefts, turn, others):
            here = pl.ds(pl.multiple_of(turn * chunk, chunk), chunk)
            total = jnp.zeros((chunk, width), jnp.float32)
            cursor = 0
            for left in lefts:
                for i in range(left.shape[0] // tokens):
                    total += dot(left[i * tokens : (i + 1) * tokens, here], others[cursor][...], tn)
                    cursor += 1
            out[...] = total.astype(low)

        @pl.when(step < steps)
        def _():
            terms(lefts_up, step, rights_up)

        @pl.when(step >= steps)
        def _():
            terms(lefts_down, step - steps, rights_down)

    arrays = (*grad_pres, *acts, *rows_in, *grads_in)
    chunked = pl.BlockSpec((chunk, width), lambda s: (s, 0))
    return pl.pallas_call(
        body,
        grid=(2 * steps,),
        in_specs=[pl.BlockSpec(array.shape, lambda s: (0, 0)) for array in arrays],
        out_specs=chunked,
        out_shape=jax.ShapeDtypeStruct((2 * hidden, width), low),
        compiler_params=pltpu.CompilerParams(vmem_limit_bytes=60 * 2**20),
        cost_estimate=cheap,
        name="mlp_grads",
    )(*arrays)


def ranked_terms(place, lefts, order, pieces, weight, factors, name):
    tokens, width = factors[0].shape
    count = len(factors)

    def body(place_ref, *refs):
        ins, weight_ref = refs[: len(lefts)], refs[len(lefts)]
        others = refs[len(lefts) + 1 : len(lefts) + 1 + count]
        out, sums = refs[-2:]
        me = place_ref[0]
        for i, slot in enumerate(order):
            rank = lax.rem(me - slot + count, count)
            for cut in cuts_of(width):
                term = jnp.zeros((tokens, cut.stop - cut.start), jnp.float32)
                for which, row, lane, start, depth in pieces[i]:
                    term += dot(
                        ins[which][row : row + tokens, lane : lane + depth],
                        weight_ref[start : start + depth, cut],
                    )
                out[rank, :, cut] = term.astype(low)
                one = jnp.sum(term, axis=0, keepdims=True)
                two = jnp.sum(term * others[i][:, cut].astype(jnp.float32), axis=0, keepdims=True)
                if i:
                    one, two = one + sums[0:1, cut], two + sums[1:2, cut]
                sums[0:1, cut], sums[1:2, cut] = one, two

    return pl.pallas_call(
        body,
        in_specs=[in_smem()] + [in_vmem()] * (len(lefts) + 1 + count),
        out_shape=[
            jax.ShapeDtypeStruct((count, tokens, width), low),
            jax.ShapeDtypeStruct((2, width), jnp.float32),
        ],
        compiler_params=pltpu.CompilerParams(vmem_limit_bytes=60 * 2**20),
        cost_estimate=cheap if len(lefts) > 2 else costly,
        name=name,
    )(place, *lefts, weight, *factors)


def update_slots(master, first_moment, second_moment, filled, which, position, sources):
    capacity, unit_rows, width = master.shape

    group = math.gcd(capacity, 2)
    steps = capacity // group

    def body(filled_ref, which_ref, position_ref, weight, one, two, *rest):
        ins = rest[: len(sources)]
        new_one, new_two, new_weight, held, sems = rest[len(sources) :]
        step = pl.program_id(0)

        def fetch(turn):
            for i in range(group):
                slot = turn * group + i
                for source, ref in enumerate(ins):

                    @pl.when(which_ref[slot] == source)
                    def _():
                        pltpu.make_async_copy(
                            ref.at[position_ref[slot]], held.at[turn % 2, i], sems.at[turn % 2, i]
                        ).start()

        @pl.when(step == 0)
        def _():
            fetch(step)

        @pl.when(step < steps - 1)
        def _():
            fetch(step + 1)

        for i in range(group):
            pltpu.make_async_copy(
                ins[0].at[0], held.at[step % 2, i], sems.at[step % 2, i]
            ).wait()
            mask = (filled_ref[step * group + i] > 0).astype(jnp.float32)
            grad = held[step % 2, i].astype(jnp.float32)
            results = adamw(weight[i], one[i], two[i], grad, mask, rate)
            new_one[i], new_two[i], new_weight[i] = results

    block = pl.BlockSpec((group, unit_rows, width), lambda s, *_: (s, 0, 0))
    return pl.pallas_call(
        body,
        grid_spec=pltpu.PrefetchScalarGridSpec(
            num_scalar_prefetch=3,
            grid=(steps,),
            in_specs=[block] * 3 + [pl.BlockSpec(memory_space=pl.ANY)] * len(sources),
            out_specs=[block] * 3,
            scratch_shapes=[
                pltpu.VMEM((2, group, unit_rows, width), low),
                pltpu.SemaphoreType.DMA((2, group)),
            ],
        ),
        out_shape=[jax.ShapeDtypeStruct(master.shape, jnp.float32)] * 3,
        compiler_params=pltpu.CompilerParams(vmem_limit_bytes=56 * 2**20),
        cost_estimate=cheap,
        name="update_slots",
    )(filled, which, position, master, first_moment, second_moment, *sources)


def adamw(weight, moment_one, moment_two, gradient, filled, step_rate):
    new_one = beta_one * moment_one + (1.0 - beta_one) * gradient
    new_two = beta_two * moment_two + (1.0 - beta_two) * gradient * gradient
    fixed_one = new_one / (1.0 - beta_one**STEP)
    fixed_two = new_two / (1.0 - beta_two**STEP)
    updated = weight - step_rate * (fixed_one / (jnp.sqrt(fixed_two) + adam_eps) + decay * weight)
    return (new_one * filled, new_two * filled, updated * filled)


def swap(values, axis, bit):
    count = lax.axis_size(axis)
    return lax.ppermute(values, axis, [(i, i ^ (1 << bit)) for i in range(count)])


def choose(values, index, axis):
    return lax.dynamic_index_in_dim(values, index, axis, keepdims=False)


def total_sum(values):
    for axis in ("dp", "tensor"):
        for bit in range(lax.axis_size(axis).bit_length() - 1):
            values = values + swap(values, axis, bit)
    return values


def pick_units(master, slot_unit, state, kind, place, sizes):
    capacity, unit_rows, width = master.shape
    units = state.shape[0]

    def body(slot_ref, state_ref, kind_ref, place_ref, blocks, *rest):
        outs, (highs, lows, zeros, read, sems) = rest[: len(sizes)], rest[len(sizes) :]

        def start(source, unit):
            for which, out in enumerate(outs):

                @pl.when(kind_ref[unit] == which)
                def _():
                    pltpu.make_async_copy(source, out.at[place_ref[unit]], sems.at[unit]).start()

        @pl.loop(0, capacity)
        def _(slot):
            @pl.when(slot_ref[slot] >= 0)
            def _():
                pltpu.make_async_copy(blocks.at[slot], highs.at[slot], read.at[slot]).start()

        zeros[...] = jnp.zeros_like(zeros)

        @pl.loop(0, units)
        def _(unit):
            @pl.when(state_ref[unit] == 0)
            def _():
                start(zeros, unit)

        @pl.loop(0, capacity)
        def _(slot):
            @pl.when(slot_ref[slot] >= 0)
            def _():
                pltpu.make_async_copy(blocks.at[slot], highs.at[slot], read.at[slot]).wait()
                lows[slot] = highs[slot].astype(low)
                start(lows.at[slot], slot_ref[slot])

        @pl.loop(0, units)
        def _(unit):
            @pl.when(state_ref[unit] < 2)
            def _():
                pltpu.make_async_copy(zeros, outs[0].at[0], sems.at[unit]).wait()

    return pl.pallas_call(
        body,
        grid_spec=pltpu.PrefetchScalarGridSpec(
            num_scalar_prefetch=4,
            grid=(1,),
            in_specs=[pl.BlockSpec(memory_space=pl.ANY)],
            out_specs=[pl.BlockSpec(memory_space=pl.ANY)] * len(sizes),
            scratch_shapes=[
                pltpu.VMEM((capacity, unit_rows, width), jnp.float32),
                pltpu.VMEM((capacity, unit_rows, width), low),
                pltpu.VMEM((unit_rows, width), low),
                pltpu.SemaphoreType.DMA((capacity,)),
                pltpu.SemaphoreType.DMA((units,)),
            ],
        ),
        out_shape=[jax.ShapeDtypeStruct((size, unit_rows, width), low) for size in sizes],
        compiler_params=pltpu.CompilerParams(vmem_limit_bytes=56 * 2**20),
        cost_estimate=cheap,
        name="pick_units",
    )(slot_unit, state, kind, place, master)


def place_blocks(sources, which, position, parts=1):
    amount = which.shape[0]
    shape = sources[0].shape[1:]
    size = amount // parts

    def body(which_ref, position_ref, *rest):
        ins, outs = rest[: len(sources)], rest[len(sources) : len(sources) + parts]
        held, read, sems = rest[len(sources) + parts :]

        @pl.loop(0, amount)
        def _(i):
            for source, ref in enumerate(ins):

                @pl.when(which_ref[i] == source)
                def _():
                    pltpu.make_async_copy(ref.at[position_ref[i]], held.at[i], read.at[i]).start()

        for part, out in enumerate(outs):

            @pl.loop(0, size)
            def _(j):
                i = part * size + j
                pltpu.make_async_copy(ins[0].at[0], held.at[i], read.at[i]).wait()
                pltpu.make_async_copy(held.at[i], out.at[j], sems.at[i]).start()

        @pl.loop(0, amount)
        def _(i):
            pltpu.make_async_copy(held.at[i], outs[0].at[0], sems.at[i]).wait()

    return pl.pallas_call(
        body,
        grid_spec=pltpu.PrefetchScalarGridSpec(
            num_scalar_prefetch=2,
            grid=(1,),
            in_specs=[pl.BlockSpec(memory_space=pl.ANY)] * len(sources),
            out_specs=[pl.BlockSpec(memory_space=pl.ANY)] * parts,
            scratch_shapes=[
                pltpu.VMEM((amount,) + shape, low),
                pltpu.SemaphoreType.DMA((amount,)),
                pltpu.SemaphoreType.DMA((amount,)),
            ],
        ),
        out_shape=[jax.ShapeDtypeStruct((size,) + shape, low)] * parts,
        compiler_params=pltpu.CompilerParams(vmem_limit_bytes=56 * 2**20),
        cost_estimate=cheap,
        name="place_blocks",
    )(which, position, *sources)


def stack_pairs(pairs):
    shape = (len(pairs),) + pairs[0].shape[1:]

    def body(*refs):
        for i, pair in enumerate(refs[:-2]):
            for half in range(2):
                refs[half - 2][i] = pair[half]

    return pl.pallas_call(
        body,
        out_shape=[jax.ShapeDtypeStruct(shape, low)] * 2,
        cost_estimate=costly,
        name="stack_pairs",
    )(*pairs)


def hops(values, step, turn):
    count = lax.axis_size("tensor")
    if step > 0:
        pairs = [(i, i + 1) for i in range(turn - 1, count - 1)]
    else:
        pairs = [(i, i - 1) for i in range(1, count - turn + 1)]
    return lax.ppermute(values, "tensor", pairs)


fence = lax.optimization_barrier


def in_pool(member, inner, inner_count):
    me = lax.axis_index("dp")
    half, core = member >> 3, ((member >> 2) & 1) ^ (me & 1)
    far_y, far_x = ((member >> 1) & 1) ^ ((me >> 2) & 1), (member & 1) ^ ((me >> 1) & 1)
    where_first = (far_y * 2 + far_x) * inner_count
    where_second = (4 + far_x * 2 + far_y) * inner_count
    return (core, jnp.where(half == 0, where_first, where_second) + inner)


def on_device(
    hidden_in,
    time_embed,
    caption_table,
    caption_ids,
    owners,
    master,
    first_moment,
    second_moment,
    mod_table,
    mod_first,
    mod_second,
    out_grad,
):
    count = lax.axis_size("tensor")
    dp_count = lax.axis_size("dp")
    me_dp = lax.axis_index("dp")
    me_tensor = lax.axis_index("tensor")
    capacity, unit_rows, width = master.shape
    units = owners.shape[0]
    tokens = hidden_in.shape[1]
    text_count = caption_ids.shape[1]
    share = width // count
    per = share // unit_rows
    ups = (units - 8 * per) // 2
    rank_of = ranks_of(owners)
    mine = owners == me_dp
    match = (rank_of[None, :] == jnp.arange(capacity)[:, None]) & mine[None, :]
    filled = jnp.any(match, axis=1)
    unit_of_slot = jnp.sum(jnp.where(match, jnp.arange(units)[None, :], 0), axis=1)

    square = [list(range(i * per, (i + 1) * per)) for i in range(8)]
    group_attn = square[0] + square[1] + square[2] + square[5]
    group_full = square[3] + square[4] + square[6] + square[7]
    group_mlp = list(range(8 * per, units))
    members = len(group_attn)
    plane = dp_count == 8 and members == 16 and len(group_mlp) % dp_count == 0
    member_of = np.zeros(units, np.int32)
    member_of[group_attn] = np.arange(members)
    member_of[group_full] = np.arange(members)
    is_attn = np.zeros(units, bool)
    is_attn[group_attn] = True
    is_mlp = np.zeros(units, bool)
    is_mlp[group_mlp] = True

    latent_in = hidden_in[0].astype(jnp.float32)
    modulate = mod_table + time_embed[0]

    def mod_row(which_row):
        return modulate[which_row][None, :]

    normed_one, inverse_one = layer_norm(latent_in)
    bits = dp_count.bit_length() - 1
    vocab_rows = caption_table.shape[0]

    def caption_terms(ids):
        chosen = ids.reshape(-1) - me_dp * vocab_rows
        onehot = (chosen[:, None] == jnp.arange(vocab_rows)[None, :]).astype(low)
        terms = jnp.dot(onehot, caption_table, preferred_element_type=jnp.float32).astype(low)
        return terms.reshape(dp_count, text_count, -1)

    def modulated(normed):
        return (normed.astype(jnp.float32) * (1.0 + mod_row(1)) + mod_row(0)).astype(low)

    def whole_text(text_ring):
        return from_ring(text_ring, -1).transpose(1, 0, 2).reshape(text_count, width)

    def own_keys(text_low, w_attn):
        return project(text_low, w_attn)[:, 3 * share :].astype(low)

    def exchanged(attended, keys):
        parts = [
            jnp.concatenate([attended[k * tokens : (k + 1) * tokens], keys]) for k in range(count)
        ]
        return [parts[0]] + [shift(parts[k], count - k) for k in range(1, count)]

    where = jnp.stack([me_tensor, me_dp & 1]).astype(jnp.int32)

    n_low = normed_one.astype(low)
    if plane:
        core, far_x, far_y = (
            ((member_of >> 2) & 1) ^ (me_dp & 1),
            (member_of & 1) ^ ((me_dp >> 1) & 1),
            ((member_of >> 1) & 1) ^ ((me_dp >> 2) & 1),
        )
        place = jnp.where(is_attn, far_x * 4 + far_y * 2, 8 + far_y * 4 + far_x * 2)
        place = jnp.where(is_mlp, np.arange(units) - 8 * per, place + (member_of >> 3))
        kind = jnp.where(is_mlp, 0, core)
        slot_mlp = unit_of_slot >= 8 * per
        owned_state = mine.astype(jnp.int32)
        grad_whole = lax.all_gather(out_grad[0], "tensor", axis=0)
        ids = lax.all_gather(caption_ids, "dp", axis=0, tiled=True)
        ids = jnp.take(ids, me_dp ^ jnp.arange(dp_count), axis=0, mode="clip")
        up, down = hops(n_low, 1, 1), hops(n_low, -1, 1)
        kept, given = pick_units(
            master,
            jnp.where(filled & ~slot_mlp, unit_of_slot, -1),
            jnp.where(is_mlp, 2, owned_state),
            kind,
            place,
            (members, members),
        )
        got = swap(given, "dp", 0)
        n_up, n_down = [up], [down]
        kept, got, up, down, ids = fence((kept, got, up, down, ids))
        pieces = [kept[i : i + 4] + got[i : i + 4] for i in range(0, members, 4)]
        attn_two, attn_send, full_two, full_send = fence(tuple(pieces))
        up, down = hops(up, 1, 2), hops(down, -1, 2)
        attn_got = swap(attn_send, "dp", 1)
        full_got = swap(full_send, "dp", 2)
        text = caption_terms(ids)
        text = text[0:4] + swap(text[4:8], "dp", 2)
        (mlp_part,) = pick_units(
            fence((master, got))[0],
            jnp.where(filled & slot_mlp, unit_of_slot, -1),
            jnp.where(is_mlp, owned_state, 2),
            kind,
            place,
            (len(group_mlp),),
        )
        n_up.append(up), n_down.append(down)
        attn_two, attn_got, full_two, full_got, up, down, text, mlp_part = fence(
            (attn_two, attn_got, full_two, full_got, up, down, text, mlp_part)
        )
        pieces = [x[i : i + 2] + y[i : i + 2] for x, y in ((attn_two, attn_got), (full_two, full_got)) for i in (0, 2)]
        attn_one, attn_send, full_one, full_send = fence(tuple(pieces))
        up, down = hops(up, 1, 3), hops(down, -1, 3)
        attn_got = swap(attn_send, "dp", 2)
        full_got = swap(full_send, "dp", 1)
        text = text[0:2] + swap(text[2:4], "dp", 1)
        n_up.append(up), n_down.append(down)
        attn_one, attn_got, full_one, full_got, up, down, text, mlp_part, grad_whole = fence(
            (attn_one, attn_got, full_one, full_got, up, down, text, mlp_part, grad_whole)
        )
        attn_one, full_one = attn_one + attn_got, full_one + full_got
        n_up[-1], n_down[-1] = up, down
        mlp_part = lax.psum_scatter(mlp_part, "dp", scatter_dimension=0, tiled=True)
        first_ring, second_ring = stack_pairs(ring(full_one))
        first = jnp.concatenate([attn_one[0:1], swap(attn_one[0:1], "dp", 1)])
        second = jnp.concatenate([attn_one[1:2], swap(attn_one[1:2], "dp", 2)])
        pool = jnp.concatenate([first, swap(first, "dp", 2), second, swap(second, "dp", 1)])
        other = swap(pool, "dp", 0)
        text = text[0] + swap(text[1], "dp", 0)
        *n_slots, h_one_all = line_slots(
            where, n_low, n_up, n_down, jnp.concatenate([mod_row(0), mod_row(1)])
        )
        n_slots = [n_low] + n_slots
        pool, other, first_ring, second_ring, h_one_all, text = fence(
            (pool, other, first_ring, second_ring, h_one_all, text)
        )
        first, second = first_ring, second_ring
        first_got = swap(first, "dp", 1)
        second_got = swap(second, "dp", 2)
        text_ring = ring(text)
        (w_attn,) = place_blocks((pool, other), *in_pool(np.arange(members), 0, 1))
        w_attn = w_attn.reshape(-1, width)
        qkv = project(h_one_all, w_attn).astype(low)
        attended, logs = self_attend(qkv, share)
        first = jnp.concatenate([first, first_got])
        second = jnp.concatenate([second, second_got])
        first, second, text_ring, attended, logs, w_attn, mlp_part = fence(
            (first, second, text_ring, attended, logs, w_attn, mlp_part)
        )
        w_mlp = lax.all_gather(mlp_part, "dp", axis=0, tiled=True)
        first_far, second_far = swap(first, "dp", 2), swap(second, "dp", 1)
        first_other, second_other = swap(first, "dp", 0), swap(second, "dp", 0)
        text_low = whole_text(jnp.stack(text_ring))
        mixed = exchanged(attended, own_keys(text_low, w_attn))
        first_far, second_far, first_other, second_other, mixed = fence(
            (first_far, second_far, first_other, second_other, mixed)
        )
        first_last, second_last = swap(first_far, "dp", 0), swap(second_far, "dp", 0)
        listing = np.arange(count * members)
        matrix, rank, head = listing // (count * per), listing // per % count, listing % per
        slot = lax.rem(me_tensor - rank + count, count)
        which, position = in_pool(matrix * per + head, slot, count)
        blocks = 2 * count
        w_full = place_blocks(
            (first, first_far, second, second_far, first_other, first_last, second_other, second_last),
            which * 4 + position // blocks,
            position % blocks,
            parts=4,
        )
        w_full = [part.reshape(width, width) for part in w_full]
    else:
        slots_low = master.astype(low)
        rows = jnp.take(slots_low, rank_of, axis=0, mode="clip")
        rows = lax.psum(jnp.where(mine[:, None, None], rows, jnp.zeros((), low)), "dp")
        w_attn = rows[np.array(group_attn)].reshape(-1, width)
        w_full = lax.all_gather(rows[np.array(group_full)], "tensor", axis=0)
        w_full = w_full.reshape(count, 4, share, width).swapaxes(0, 1).reshape(4, width, width)
        w_full = [w_full[i] for i in range(4)]
        w_mlp = rows[8 * per :]
        n_slots = ring(n_low)
        normed_all = jnp.concatenate(n_slots)
        grad_whole = lax.all_gather(out_grad[0], "tensor", axis=0)
        ids = caption_ids
        for bit in range(bits):
            ids = jnp.concatenate([ids, swap(ids, "dp", bit)])
        text = caption_terms(ids)
        for bit in reversed(range(bits)):
            text = text[: 1 << bit] + swap(text[1 << bit :], "dp", bit)
        text_low = whole_text(jnp.stack(ring(text[0])))
        h_one_all = modulated(normed_all)
        qkv = project(h_one_all, w_attn).astype(low)
        attended, logs = self_attend(qkv, share)
        mixed = exchanged(attended, own_keys(text_low, w_attn))
    w_cross = w_full
    w_out, c_query, c_value, c_out = w_full
    w_mlp = w_mlp.reshape(-1, width)

    rows = jnp.concatenate([mod_row(2), mod_row(3), mod_row(4)])
    (
        branch_one,
        first_low,
        cq_rows,
        ck_rows,
        cv_rows,
        crossed,
        second_res,
        normed_two,
        h_two,
        inverse_two,
    ) = cross_block(
        where, mixed, hidden_in[0], rows, text_low, *w_cross
    )

    h_slots = ring(h_two)
    out_slots = [
        choose(grad_whole, lax.rem(me_tensor - k + count, count), 0) for k in range(count)
    ]
    grad_slots = [(mod_row(5) * item.astype(jnp.float32)).astype(low) for item in out_slots]
    near = [k for k in range(1, count) if 2 * k != count]
    far = [k for k in range(1, count) if 2 * k == count]
    acts, grad_pres, grad_terms, order = [], [], [], []
    for members_now in ([0], near, far):
        act, grad_pre, *terms = mlp_core(
            [h_slots[k] for k in members_now],
            [grad_slots[k] for k in members_now],
            w_mlp,
            acts[-1:],
        )
        acts.append(act), grad_pres.append(grad_pre)
        order += members_now
        grad_terms += [
            shift(term, count - k) if k else term for k, term in zip(members_now, terms)
        ]
    mlp_grad = mlp_grads(
        grad_pres, acts, [h_slots[k] for k in order], [grad_slots[k] for k in order]
    ).reshape(-1, unit_rows, width)
    hidden_share = w_mlp.shape[0] // 2
    pieces = [
        [(which, row, 0, hidden_share, hidden_share)]
        for which, act in enumerate(acts)
        for row in range(0, act.shape[0], tokens)
    ]
    branch_terms, branch_sums = ranked_terms(
        where, acts, order, pieces, w_mlp, [out_slots[k] for k in order], "mlp_out"
    )
    branch_row = branch_sums[1]
    grad_terms, branch_terms = fence((grad_terms, branch_terms))
    if plane:
        mlp_sum = lax.psum_scatter(mlp_grad, "dp", scatter_dimension=0, tiled=True)

    (
        first_grad,
        cross_low,
        grad_cq,
        attn_low,
        grad_cv,
        row_sums,
        *grad_mixed,
    ) = cross_back(
        where,
        grad_terms,
        out_grad[0],
        rows,
        normed_two,
        inverse_two,
        branch_one,
        cq_rows,
        ck_rows,
        cv_rows,
        c_out,
        c_query,
        w_out,
    )

    grad_parts = [grad_mixed[0]] + [shift(grad_mixed[k], k) for k in range(1, count)]
    full_pairs = [
        ([(item, 0, share, None) for item in mixed], attn_low),
        ([(grad_cq, 0, width, 0)], first_low),
        ([(grad_cv, 0, width, 0)], text_low),
        ([(crossed, 0, width, 0)], cross_low),
    ]
    half = (share // HEAD_DIM // 2) * HEAD_DIM
    spans = [(0, half), (half, share)]

    def attention_pairs(grads, grad_parts):
        keys = sum(item[tokens:].astype(jnp.float32) for item in grad_parts).astype(low)
        pairs = [
            (
                [
                    (item, i * (end - begin), end - begin, begin)
                    for item, (begin, end) in zip(grads, spans)
                ],
                h_one_all,
            )
            for i in range(3)
        ]
        return pairs + [([(keys, 0, share, 0)], text_low)]

    def input_terms(grads):
        pieces = [
            [
                (which, slot * tokens, i * (end - begin), i * share + begin, end - begin)
                for which, (begin, end) in enumerate(spans)
                for i in range(3)
            ]
            for slot in range(count)
        ]
        return ranked_terms(where, grads, range(count), pieces, w_attn, n_slots, "attn_terms")

    if plane:
        x_bit, y_bit = (me_dp >> 1) & 1, (me_dp >> 2) & 1

        def split(total, bit, axis):
            return (choose(total, bit, axis), choose(total, 1 - bit, axis))

        branch_terms, grad_parts[0] = fence((branch_terms, grad_parts[0]))
        branch_two = lax.psum_scatter(
            branch_terms.reshape(-1, width), "tensor", scatter_dimension=0, tiled=True
        )
        kept, given = outer_halves(where, full_pairs, count, "full_grads")
        got = swap(given, "dp", 0)
        grad_parts, kept, got = fence((grad_parts, kept, got))
        box = (2, count, 2, 2, unit_rows, width)
        kept, got = kept.reshape(box), got.reshape(box)
        kept_one = choose(kept[0], x_bit, 2) + choose(got[0], x_bit, 2)
        given_one = choose(kept[0], 1 - x_bit, 2) + choose(got[0], 1 - x_bit, 2)
        kept_two = choose(kept[1], y_bit, 1) + choose(got[1], y_bit, 1)
        given_two = choose(kept[1], 1 - y_bit, 1) + choose(got[1], 1 - y_bit, 1)
        kept_one, given_one, kept_two, given_two, grad_parts = fence(
            (kept_one, given_one, kept_two, given_two, grad_parts)
        )
        got_one, got_two = swap(given_one, "dp", 1), swap(given_two, "dp", 2)
        grads_early = self_attend_back(qkv, grad_parts, attended, logs, share, *spans[0])
        kept_one, got_one, kept_two, got_two, grads_early, grad_parts = fence(
            (kept_one, got_one, kept_two, got_two, grads_early, grad_parts)
        )
        kept_one, given_one = split(kept_one + got_one, y_bit, 1)
        kept_two, given_two = split(kept_two + got_two, x_bit, 1)
        kept_one, given_one, kept_two, given_two, grad_parts = fence(
            (kept_one, given_one, kept_two, given_two, grad_parts)
        )
        got_one, got_two = swap(given_one, "dp", 2), swap(given_two, "dp", 1)
        grads_late = self_attend_back(qkv, grad_parts, attended, logs, share, *spans[1])
        kept_one, got_one, kept_two, got_two, grads_early, grads_late, branch_two, mlp_sum = fence(
            (kept_one, got_one, kept_two, got_two, grads_early, grads_late, branch_two, mlp_sum)
        )
        mlp_sum = lax.all_gather(mlp_sum, "dp", axis=0, tiled=True)
        full_parts = to_ring(jnp.stack([kept_one + got_one, kept_two + got_two], axis=1))
        full_parts = [full_parts[k] for k in range(count)]
        full_parts, grads_early, grads_late = fence((full_parts, grads_early, grads_late))
        grads_qkv = [grads_early, grads_late]
        full_got = [shift(full_parts[k], k) for k in range(1, count)]
        attn_kept, attn_given = outer_halves(
            where, attention_pairs(grads_qkv, grad_parts), 1, "attn_grads"
        )
        attn_got = swap(attn_given, "dp", 0)
        grad_h_terms, grad_h_sums = input_terms(grads_qkv)
        mod_terms = jnp.concatenate([grad_h_sums, row_sums, branch_row[None]])
        grad_h_one = lax.psum_scatter(
            grad_h_terms.reshape(-1, width), "tensor", scatter_dimension=0, tiled=True
        )
        attn_kept, attn_got, mod_terms = fence((attn_kept, attn_got, mod_terms))
        attn_all = (attn_kept + attn_got).reshape(2, 2, 2, unit_rows, width)
        one_kept, one_given = split(attn_all[0], x_bit, 1)
        two_kept, two_given = split(attn_all[1], y_bit, 0)
        one_got, two_got = swap(one_given, "dp", 1), swap(two_given, "dp", 2)
        mod_terms = mod_terms + swap(mod_terms, "dp", 0)
        full_own = full_parts[0]
        one_kept, one_got, two_kept, two_got, mod_terms, full_own, full_got = fence(
            (one_kept, one_got, two_kept, two_got, mod_terms, full_own, full_got)
        )
        full_sum = full_own.astype(jnp.float32)
        for part in full_got:
            full_sum = full_sum + part.astype(jnp.float32)
        full_sum = full_sum.astype(low)
        one_kept, one_given = split(one_kept + one_got, y_bit, 0)
        two_kept, two_given = split(two_kept + two_got, x_bit, 0)
        one_got, two_got = swap(one_given, "dp", 2), swap(two_given, "dp", 1)
        mod_terms = mod_terms + swap(mod_terms, "dp", 1)
        one_kept, one_got, two_kept, two_got, full_sum, mod_terms, mlp_sum = fence(
            (one_kept, one_got, two_kept, two_got, full_sum, mod_terms, mlp_sum)
        )
        first = jnp.stack([one_kept + one_got, full_sum[0]])
        second = jnp.stack([two_kept + two_got, full_sum[1]])
        first_got, second_got = swap(first, "dp", 1), swap(second, "dp", 2)
        first = jnp.concatenate([first, first_got])
        second = jnp.concatenate([second, second_got])
        mod_terms = mod_terms + swap(mod_terms, "dp", 2)
        first, second, mod_terms = fence((first, second, mod_terms))
        first_far, second_far = swap(first, "dp", 2), swap(second, "dp", 1)
        mod_terms = mod_terms + swap(mod_terms, "tensor", 0)
        first, first_far, second, second_far, mod_terms, grad_h_one = fence(
            (first, first_far, second, second_far, mod_terms, grad_h_one)
        )
        pool = jnp.concatenate([first, first_far, second, second_far])
        other = swap(pool, "dp", 0)
        for bit in range(1, count.bit_length() - 1):
            mod_terms = mod_terms + swap(mod_terms, "tensor", bit)
        pool, other, mod_grad = fence((pool, other, mod_terms))
        which, position = in_pool(member_of, np.where(is_attn, 0, 1), 2)
        which = jnp.where(is_mlp, 2, which)
        position = jnp.where(is_mlp, np.arange(units) - 8 * per, position)
        own = jnp.sum(jnp.where(match[:, :, None], jnp.stack([which, position], 1)[None], 0), axis=1)
        new_first, new_second, new_master = update_slots(
            master,
            first_moment,
            second_moment,
            filled.astype(jnp.int32),
            own[:, 0],
            own[:, 1],
            (pool, other, mlp_sum),
        )
    else:
        branch_two = lax.psum_scatter(
            branch_terms.reshape(-1, width), "tensor", scatter_dimension=0, tiled=True
        )
        grads_qkv = [self_attend_back(qkv, grad_parts, attended, logs, share, *span) for span in spans]
        attn_grads = [
            outer(array[:, lane : lane + lanes], right).astype(low)
            for left, right in attention_pairs(grads_qkv, grad_parts)
            for array, lane, lanes, row in left
        ]
        grad_h_terms, grad_h_sums = input_terms(grads_qkv)
        grad_h_one = lax.psum_scatter(
            grad_h_terms.reshape(-1, width), "tensor", scatter_dimension=0, tiled=True
        )
        mixed_all = from_ring(jnp.stack([item[:tokens] for item in mixed]), 1)
        mixed_all = mixed_all.transpose(1, 0, 2).reshape(tokens, width)
        full_grads = [outer(mixed_all, attn_low)]
        full_grads += [outer(left[0][0], right) for left, right in full_pairs[1:]]
        full_sum = [g.astype(low).reshape(count, share, width) for g in full_grads]
        full_sum = jnp.stack(full_sum, axis=1)
        full_sum = lax.psum_scatter(full_sum, "tensor", scatter_dimension=0, tiled=True)
        order = np.array(group_attn + group_full + group_mlp)
        sums = jnp.concatenate(
            [jnp.concatenate(attn_grads), full_sum.reshape(-1, width), mlp_grad.reshape(-1, width)]
        )
        sums = lax.psum(sums.reshape(units, unit_rows, width), "dp")
        owned = jnp.take(sums, jnp.array(np.argsort(order))[unit_of_slot], axis=0, mode="clip")
        mod_grad = total_sum(jnp.concatenate([grad_h_sums, row_sums, branch_row[None]]))
        new_first, new_second, new_master = adamw(
            master,
            first_moment,
            second_moment,
            owned.astype(jnp.float32),
            filled.astype(jnp.float32)[:, None, None],
            rate,
        )
    branch_two, second_res, grad_h_one, new_first = fence(
        (branch_two, second_res, grad_h_one, new_first)
    )
    grad_h_one = grad_h_one.astype(jnp.float32)
    block_out = second_res + mod_row(5) * branch_two.astype(jnp.float32)
    input_grad = first_grad + norm_back(grad_h_one, normed_one, inverse_one, mod_row(1))
    mod_new_first, mod_new_second, mod_new = adamw(
        mod_table, mod_first, mod_second, mod_grad, 1.0, table_rate
    )
    return (
        block_out[None],
        input_grad[None],
        new_first,
        new_second,
        new_master,
        mod_new_first,
        mod_new_second,
        mod_new,
    )


def solution(mesh):
    in_specs = (
        P("dp", "tensor", None),
        P("dp", None, None),
        P("dp", "tensor"),
        P("dp", None),
        P(),
        P("dp", "tensor", None),
        P("dp", "tensor", None),
        P("dp", "tensor", None),
        P(),
        P(),
        P(),
        P("dp", "tensor", None),
    )
    out_specs = (
        P("dp", "tensor", None),
        P("dp", "tensor", None),
        P("dp", "tensor", None),
        P("dp", "tensor", None),
        P("dp", "tensor", None),
        P(),
        P(),
        P(),
    )
    return jax.shard_map(
        on_device, mesh=mesh, in_specs=in_specs, out_specs=out_specs, check_vma=False
    )
```

```python
import math

import jax
import jax.numpy as jnp
import numpy as np
from jax import lax
from jax.experimental import pallas as pl
from jax.experimental.pallas import tpu as pltpu
from jax.sharding import PartitionSpec as P

HEAD_DIM = 72
STEP = 10


norm_eps = 1e-06
beta_one = 0.9
beta_two = 0.999
rate = 0.03
table_rate = 0.3
decay = 0.01
adam_eps = 1e-08
low = jnp.bfloat16


def ranks_of(owners):
    index = jnp.arange(owners.shape[0])
    before = (owners[None, :] == owners[:, None]) & (index[None, :] < index[:, None])
    return jnp.sum(before.astype(jnp.int32), axis=1)


def layer_norm(values):
    center = values - jnp.mean(values, axis=-1, keepdims=True)
    inverse = lax.rsqrt(jnp.mean(center * center, axis=-1, keepdims=True) + norm_eps)
    return (center * inverse, inverse)


def norm_back(grad_rows, normed, inverse, scale_row):
    scaled = grad_rows * (1.0 + scale_row)
    mean_one = jnp.mean(scaled, axis=-1, keepdims=True)
    mean_two = jnp.mean(scaled * normed, axis=-1, keepdims=True)
    return inverse * (scaled - mean_one - normed * mean_two)


def project(rows, weight):
    return jnp.einsum("ld,rd->lr", rows, weight, preferred_element_type=jnp.float32)


def expand(rows, weight):
    return jnp.einsum("lr,rd->ld", rows, weight, preferred_element_type=jnp.float32)


def outer(left, right):
    return jnp.einsum("lr,ld->rd", left, right, preferred_element_type=jnp.float32)


def shift(values, step):
    count = lax.axis_size("tensor")
    return lax.ppermute(values, "tensor", [(i, (i + step) % count) for i in range(count)])


def ring(values):
    return [values] + [shift(values, k) for k in range(1, lax.axis_size("tensor"))]


def to_ring(stacked):
    count = stacked.shape[0]
    twice = jnp.concatenate([stacked, stacked], axis=0)
    return lax.dynamic_slice_in_dim(twice, lax.axis_index("tensor"), count, 0)


def from_ring(stacked, sign):
    count = stacked.shape[0]
    me = lax.axis_index("tensor")
    place = lax.rem(sign * (jnp.arange(count) - me) + 2 * count, count)
    return jnp.take(stacked, place, axis=0, mode="clip")


cheap = pl.CostEstimate(flops=1000, bytes_accessed=1000, transcendentals=0)
costly = pl.CostEstimate(flops=10**10, bytes_accessed=10**7, transcendentals=0)


def self_attend(qkv, share):
    length = qkv.shape[0]
    rows = min(512, length)
    curve = HEAD_DIM ** (-0.5) * math.log2(math.e)
    heads = share // HEAD_DIM

    def body(qkv_ref, out_ref, log_ref):
        @pl.loop(0, length // rows)
        def _(step):
            here = pl.ds(pl.multiple_of(step * rows, rows), rows)
            parts = []
            for head in range(heads):
                at = head * HEAD_DIM
                q = qkv_ref[here, at : at + HEAD_DIM]
                k = qkv_ref[:, share + at : share + at + HEAD_DIM]
                v = qkv_ref[:, 2 * share + at : 2 * share + at + HEAD_DIM]
                scores = dot(k, q, nt)
                top = jnp.max(scores, axis=0, keepdims=True)
                expo = jnp.exp2((scores - top) * curve)
                total = jnp.sum(expo, axis=0, keepdims=True)
                log_ref[head : head + 1, here] = top * curve + jnp.log2(total)
                parts.append((dot(v, expo.astype(low), tn) * (1.0 / total)).T)
            out_ref[here, :] = jnp.concatenate(parts, axis=1).astype(low)

    return pl.pallas_call(
        body,
        out_shape=[
            jax.ShapeDtypeStruct((length, share), low),
            jax.ShapeDtypeStruct((heads, length), jnp.float32),
        ],
        compiler_params=pltpu.CompilerParams(vmem_limit_bytes=40 * 2**20),
        cost_estimate=cheap,
        name="self_attend",
    )(qkv)


def self_attend_back(qkv, grads, mixed, logs, share, begin, end):
    length = qkv.shape[0]
    rows = length // len(grads)
    span = end - begin
    scale = HEAD_DIM ** (-0.5)
    curve = scale * math.log2(math.e)

    def body(qkv_ref, mixed_ref, log_ref, *refs):
        grad_refs, (out_ref, grad_k, grad_v) = refs[: len(grads)], refs[len(grads) :]
        for step, grad_ref in enumerate(grad_refs):
            here = slice(step * rows, (step + 1) * rows)
            parts = []
            for head, at in enumerate(range(begin, end, HEAD_DIM)):
                q = qkv_ref[here, at : at + HEAD_DIM]
                k = qkv_ref[:, share + at : share + at + HEAD_DIM]
                v = qkv_ref[:, 2 * share + at : 2 * share + at + HEAD_DIM]
                g = grad_ref[0:rows, at : at + HEAD_DIM]
                o = mixed_ref[here, at : at + HEAD_DIM]
                inner = g.astype(jnp.float32) * o.astype(jnp.float32)
                inner = jnp.sum(inner.T, axis=0, keepdims=True)
                which = begin // HEAD_DIM + head
                probs = jnp.exp2(dot(k, q, nt) * curve - log_ref[which : which + 1, here])
                grad_scores = (probs * (dot(v, g, nt) - inner)).astype(low)
                to_v = dot(probs.astype(low), g)
                to_k = dot(grad_scores, q)
                if step:
                    grad_v[head] += to_v
                    grad_k[head] += to_k
                else:
                    grad_v[head] = to_v
                    grad_k[head] = to_k
                parts.append((dot(k, grad_scores, tn) * scale).T)
            out_ref[here, 0:span] = jnp.concatenate(parts, axis=1).astype(low)
        heads = range(span // HEAD_DIM)
        both = [grad_k[head] * scale for head in heads]
        out_ref[:, span : 2 * span] = jnp.concatenate(both, axis=1).astype(low)
        both = [grad_v[head] for head in heads]
        out_ref[:, 2 * span :] = jnp.concatenate(both, axis=1).astype(low)

    return pl.pallas_call(
        body,
        out_shape=jax.ShapeDtypeStruct((length, 3 * span), low),
        scratch_shapes=[pltpu.VMEM((span // HEAD_DIM, length, HEAD_DIM), jnp.float32)] * 2,
        compiler_params=pltpu.CompilerParams(vmem_limit_bytes=40 * 2**20),
        cost_estimate=cheap,
        name="self_attend_back",
    )(qkv, mixed, logs, *grads)


def mlp_core(rows_in, grads_in, w_mlp, after):
    groups = len(rows_in)
    tokens, width = rows_in[0].shape
    hidden = w_mlp.shape[0] // 2
    chunk = 384 if hidden % 384 == 0 else hidden
    steps = hidden // chunk
    curve = 0.7978845608028654

    def body(*refs):
        rows, grads = refs[:groups], refs[groups : 2 * groups]
        up, down = refs[2 * groups : 2 * groups + 2]
        act, grad_pre, *outs = refs[2 * groups + 2 + len(after) : -1]
        total = refs[-1]
        step = pl.program_id(0)
        for i in range(groups):
            pre = lax.dot_general(
                rows[i][...], up[...], (((1,), (1,)), ((), ())), preferred_element_type=jnp.float32
            )
            square = pre * pre
            bend = jnp.tanh(curve * pre * (1.0 + 0.044715 * square))
            half = 0.5 * (1.0 + bend)
            here = pl.ds(i * tokens, tokens)
            act[here, :] = (pre * half).astype(low)
            slope = half + (0.5 * curve) * pre * (1.0 - bend * bend) * (1.0 + 0.134145 * square)
            grad_act = lax.dot_general(
                grads[i][...], down[...], (((1,), (1,)), ((), ())), preferred_element_type=jnp.float32
            )
            grad_low = (grad_act * slope).astype(low)
            grad_pre[here, :] = grad_low
            term = jnp.dot(grad_low, up[...], preferred_element_type=jnp.float32)

            @pl.when(step == 0)
            def _():
                total[here, :] = term

            @pl.when(step > 0)
            def _():
                total[here, :] += term

            @pl.when(step == steps - 1)
            def _():
                outs[i][...] = total[here, :].astype(low)

    whole = pl.BlockSpec((tokens, width), lambda s: (0, 0))
    across = pl.BlockSpec((groups * tokens, chunk), lambda s: (0, s))
    return pl.pallas_call(
        body,
        grid=(steps,),
        in_specs=[whole] * (2 * groups)
        + [
            pl.BlockSpec((chunk, width), lambda s: (s, 0)),
            pl.BlockSpec((chunk, width), lambda s: (steps + s, 0)),
        ]
        + [pl.BlockSpec(memory_space=pl.ANY)] * len(after),
        out_specs=[across, across] + [whole] * groups,
        out_shape=[jax.ShapeDtypeStruct((groups * tokens, hidden), low)] * 2
        + [jax.ShapeDtypeStruct((tokens, width), low)] * groups,
        scratch_shapes=[pltpu.VMEM((groups * tokens, width), jnp.float32)],
        compiler_params=pltpu.CompilerParams(vmem_limit_bytes=60 * 2**20),
        cost_estimate=cheap,
        name="mlp_core",
    )(*rows_in, *grads_in, w_mlp, w_mlp, *after)


nt = (((1,), (1,)), ((), ()))
tn = (((0,), (0,)), ((), ()))


def dot(left, right, dims=(((1,), (0,)), ((), ()))):
    return lax.dot_general(left, right, dims, preferred_element_type=jnp.float32)


def softmax_keys(keys, queries):
    scores = dot(keys, queries, nt) * HEAD_DIM ** (-0.5)
    expo = jnp.exp(scores - jnp.max(scores, axis=0, keepdims=True))
    return expo * (1.0 / jnp.sum(expo, axis=0, keepdims=True))


def cuts_of(width):
    size = 384 if width % 384 == 0 else width
    return [slice(i, i + size) for i in range(0, width, size)]


def in_smem():
    return pl.BlockSpec(memory_space=pltpu.SMEM)


def in_vmem():
    return pl.BlockSpec(memory_space=pltpu.VMEM)


def line_slots(place, own, ups, downs, rows):
    count = len(ups) + 1
    tokens, width = own.shape

    def body(place_ref, *refs):
        own_ref, up_refs, down_refs = refs[0], refs[1:count], refs[count : 2 * count - 1]
        rows_ref, outs, out = refs[2 * count - 1], refs[2 * count : -1], refs[-1]
        me = place_ref[0]

        def modulate(slot, ref):
            value = ref[...].astype(jnp.float32)
            value = value * (1.0 + rows_ref[1:2, :]) + rows_ref[0:1, :]
            out[slot * tokens : (slot + 1) * tokens, :] = value.astype(low)

        modulate(0, own_ref)
        for k in range(1, count):
            for side, ref in ((me >= k, up_refs[k - 1]), (me < k, down_refs[count - k - 1])):

                @pl.when(side)
                def _():
                    outs[k - 1][...] = ref[...]
                    modulate(k, ref)

    shapes = [(tokens, width)] * (count - 1) + [(count * tokens, width)]
    return pl.pallas_call(
        body,
        in_specs=[in_smem()] + [in_vmem()] * (2 * count),
        out_shape=[jax.ShapeDtypeStruct(shape, low) for shape in shapes],
        compiler_params=pltpu.CompilerParams(vmem_limit_bytes=32 * 2**20),
        cost_estimate=cheap,
        name="line_slots",
    )(place, own, *ups, *downs, rows)


def cross_block(place, mixed, hidden, rows, text, w_out, c_query, c_value, c_out):
    count, share = len(mixed), mixed[0].shape[1]
    tokens, width = hidden.shape
    words = text.shape[0]
    per = share // HEAD_DIM

    def body(place_ref, *refs):
        parts = refs[:count]
        x_ref, rows_ref, text_ref = refs[count : count + 3]
        far = refs[count + 3 : count + 7]
        outs = refs[count + 7 : count + 16]
        inverse = refs[count + 16]
        wo, wq, wv, wc, *own = refs[count + 17 : -3]
        held, read, sems = refs[-3:]
        branch, res_low, cq, ck, cv, crossed, res, normed, out = own
        me = place_ref[0]
        loads = [
            pltpu.make_async_copy(source, target, read.at[i])
            for i, (source, target) in enumerate(zip(far, (wo, wq, wv, wc)))
        ]
        stores = [
            pltpu.make_async_copy(source, target, sems.at[i])
            for i, (source, target) in enumerate(zip(own, outs))
        ]
        for load in loads:
            load.start()
        loads[0].wait()
        for cut in cuts_of(width):
            total = jnp.zeros((tokens, cut.stop - cut.start), jnp.float32)
            for k in range(count):
                rank = lax.rem(me + k, count)
                here = pl.ds(pl.multiple_of(rank * share, 32), share)
                total += dot(parts[k][0:tokens, :], wo[here, cut])
            branch[:, cut] = total
            first = x_ref[:, cut].astype(jnp.float32) + rows_ref[0:1, cut] * total
            res[:, cut] = first
            res_low[:, cut] = first.astype(low)
        stores[0].start()
        stores[1].start()
        loads[1].wait()
        loads[2].wait()
        for cut in cuts_of(width):
            cq[:, cut] = dot(res_low[...], wq[cut, :], nt).astype(low)
            cv[:, cut] = dot(text_ref[...], wv[cut, :], nt).astype(low)
        for k in range(count):
            held[lax.rem(me + k, count)] = parts[k][tokens:, :]
        ck[...] = jnp.concatenate([held[rank] for rank in range(count)], axis=1)
        for i in (2, 3, 4):
            stores[i].start()
        parts_out = []
        for at in range(0, width, HEAD_DIM):
            head = slice(at, at + HEAD_DIM)
            probs = softmax_keys(ck[:, head], cq[:, head]).astype(low)
            parts_out.append(dot(cv[:, head], probs, tn).T)
        crossed[...] = jnp.concatenate(parts_out, axis=1).astype(low)
        stores[5].start()
        loads[3].wait()
        for cut in cuts_of(width):
            res[:, cut] += dot(crossed[...], wc[:, cut])
        second = res[...]
        center = second - jnp.mean(second, axis=-1, keepdims=True)
        spread = lax.rsqrt(jnp.mean(center * center, axis=-1, keepdims=True) + norm_eps)
        inverse[...] = spread
        scaled = center * spread
        normed[...] = scaled
        stores[6].start()
        stores[7].start()
        out[...] = (scaled * (1.0 + rows_ref[2:3, :]) + rows_ref[1:2, :]).astype(low)
        stores[8].start()
        for store in stores:
            store.wait()

    wide = (tokens, width)
    shapes = [
        (wide, jnp.float32),
        (wide, low),
        (wide, low),
        ((words, width), low),
        ((words, width), low),
        (wide, low),
        (wide, jnp.float32),
        (wide, jnp.float32),
        (wide, low),
    ]
    anywhere = pl.BlockSpec(memory_space=pl.ANY)
    return pl.pallas_call(
        body,
        in_specs=[in_smem()] + [in_vmem()] * (count + 3) + [anywhere] * 4,
        out_specs=[anywhere] * len(shapes) + [in_vmem()],
        out_shape=[jax.ShapeDtypeStruct(*item) for item in shapes]
        + [jax.ShapeDtypeStruct((tokens, 1), jnp.float32)],
        scratch_shapes=[pltpu.VMEM((width, width), low)] * 4
        + [pltpu.VMEM(*item) for item in shapes]
        + [
            pltpu.VMEM((count, words, share), low),
            pltpu.SemaphoreType.DMA((4,)),
            pltpu.SemaphoreType.DMA((len(shapes),)),
        ],
        compiler_params=pltpu.CompilerParams(vmem_limit_bytes=60 * 2**20),
        cost_estimate=cheap,
        name="cross_block",
    )(place, *mixed, hidden, rows, text, w_out, c_query, c_value, c_out)


def cross_back(
    place, terms, grad, rows, normed, inverse, branch, cq, ck, cv, c_out, c_query, w_out, after
):
    count = len(terms)
    tokens, width = grad.shape
    words = ck.shape[0]
    share = width // count
    scale = HEAD_DIM ** (-0.5)

    def body(place_ref, *refs):
        parts = refs[:count]
        grad_ref, rows_ref, i_ref, k_ref, v_ref = refs[count : count + 5]
        far = refs[count + 5 : count + 11]
        refs = refs[: count + 11] + refs[count + 11 + len(after) :]
        stored = refs[count + 11 : count + 15]
        grad_v, sums = refs[count + 15 : count + 17]
        outs = refs[count + 17 : 2 * count + 17]
        near = refs[2 * count + 17 : 2 * count + 23]
        n_ref, wc, q_ref, wq, wo, b_ref = near
        own = refs[2 * count + 23 : 2 * count + 27]
        first, cross_low, grad_q, attn_low = own
        back, held, read, sems = refs[2 * count + 27 :]
        me = place_ref[0]
        loads = [
            pltpu.make_async_copy(source, target, read.at[i])
            for i, (source, target) in enumerate(zip(far, near))
        ]
        stores = [
            pltpu.make_async_copy(source, target, sems.at[i])
            for i, (source, target) in enumerate(zip(own, stored))
        ]
        for load in loads:
            load.start()
        loads[0].wait()
        total = parts[0][...].astype(jnp.float32)
        for part in parts[1:]:
            total += part[...].astype(jnp.float32)
        n = n_ref[...]
        sums[1:2, :] = jnp.sum(total, axis=0, keepdims=True)
        sums[2:3, :] = jnp.sum(total * n, axis=0, keepdims=True)
        second = grad_ref[...].astype(jnp.float32) + norm_back(total, n, i_ref[...], rows_ref[2:3, :])
        first[...] = second
        cross_low[...] = second.astype(low)
        stores[1].start()
        loads[1].wait()
        loads[2].wait()
        for cut in cuts_of(width):
            back[:, cut] = dot(cross_low[...], wc[cut, :], nt).astype(low)
        grads = ([], [], [])
        for at in range(0, width, HEAD_DIM):
            head = slice(at, at + HEAD_DIM)
            q, k, v, g = q_ref[:, head], k_ref[:, head], v_ref[:, head], back[:, head]
            probs = softmax_keys(k, q)
            grad_probs = dot(v, g, nt)
            inner = jnp.sum(probs * grad_probs, axis=0, keepdims=True)
            grad_scores = (probs * (grad_probs - inner)).astype(low)
            grads[0].append((dot(k, grad_scores, tn) * scale).T)
            grads[1].append(dot(grad_scores, q) * scale)
            grads[2].append(dot(probs.astype(low), g))
        grad_q[...] = jnp.concatenate(grads[0], axis=1).astype(low)
        grad_v[...] = jnp.concatenate(grads[2], axis=1).astype(low)
        heads = share // HEAD_DIM
        for rank in range(count):
            pieces = grads[1][rank * heads : (rank + 1) * heads]
            held[rank] = jnp.concatenate(pieces, axis=1).astype(low)
        stores[2].start()
        for load in loads[3:]:
            load.wait()
        for cut in cuts_of(width):
            whole = first[:, cut] + dot(grad_q[...], wq[:, cut])
            first[:, cut] = whole
            attn_low[:, cut] = (rows_ref[0:1, cut] * whole).astype(low)
            sums[0:1, cut] = jnp.sum(b_ref[:, cut] * whole, axis=0, keepdims=True)
        stores[0].start()
        stores[3].start()
        for k in range(count):
            rank = lax.rem(me + k, count)
            here = pl.ds(pl.multiple_of(rank * share, 32), share)
            outs[k][0:tokens, :] = dot(attn_low[...], wo[here, :], nt).astype(low)
            outs[k][tokens:, :] = held[rank]
        for store in stores:
            store.wait()

    wide, square = (tokens, width), (width, width)
    shapes = [
        (wide, jnp.float32),
        (wide, low),
        (wide, low),
        (wide, low),
        ((words, width), low),
        ((3, width), jnp.float32),
    ] + [((tokens + words, share), low)] * count
    anywhere = pl.BlockSpec(memory_space=pl.ANY)
    loaded = [
        pltpu.VMEM(wide, jnp.float32),
        pltpu.VMEM(square, low),
        pltpu.VMEM(wide, low),
        pltpu.VMEM(square, low),
        pltpu.VMEM(square, low),
        pltpu.VMEM(wide, jnp.float32),
    ]
    return pl.pallas_call(
        body,
        in_specs=[in_smem()] + [in_vmem()] * (count + 5) + [anywhere] * (6 + len(after)),
        out_specs=[anywhere] * 4 + [in_vmem()] * (2 + count),
        out_shape=[jax.ShapeDtypeStruct(*item) for item in shapes],
        scratch_shapes=loaded
        + [pltpu.VMEM(*item) for item in shapes[:4]]
        + [
            pltpu.VMEM(wide, low),
            pltpu.VMEM((count, words, share), low),
            pltpu.SemaphoreType.DMA((6,)),
            pltpu.SemaphoreType.DMA((4,)),
        ],
        compiler_params=pltpu.CompilerParams(vmem_limit_bytes=60 * 2**20),
        cost_estimate=cheap,
        name="cross_back",
    )(
        place,
        *terms,
        grad,
        rows,
        inverse,
        ck,
        cv,
        normed,
        c_out,
        cq,
        c_query,
        w_out,
        branch,
        *after,
    )


def outer_halves(place, pairs, parts, name):
    width = pairs[0][1].shape[1]
    high = [sum(piece[2] for piece in left) for left, _ in pairs]
    size = high[0] // parts
    tokens = [right.shape[0] for _, right in pairs]
    flat = []

    def index_of(array):
        for i, other in enumerate(flat):
            if other is array:
                return i
        flat.append(array)
        return len(flat) - 1

    plans = [
        ([(index_of(array), *rest) for array, *rest in left], index_of(right))
        for left, right in pairs
    ]
    amount = len(pairs)

    def body(place_ref, *refs):
        ins, (kept, given), (held, sems) = refs[: len(flat)], refs[len(flat) :][:2], refs[-2:]
        turned = refs[len(flat) + 2 : -2]
        me, core = place_ref[0], place_ref[1]
        for i, (left, right) in enumerate(plans):
            for k, (which, lane, lanes, row) in enumerate(left):
                piece = ins[which][0 : tokens[i], lane : lane + lanes]
                piece = piece.astype(jnp.float32).T.astype(low)
                if row is None:
                    rank = lax.rem(me + k, len(left))
                    turned[i][pl.ds(pl.multiple_of(rank * lanes, 32), lanes), :] = piece
                else:
                    turned[i][row : row + lanes, :] = piece
            for part in range(parts):
                at = i * parts + part
                tile = dot(turned[i][part * size : (part + 1) * size, :], ins[right][...])
                held[at] = tile.astype(low)
                for out, side in ((kept, 0), (given, 1)):

                    @pl.when((core ^ (i & 1)) == side)
                    def _():
                        pltpu.make_async_copy(
                            held.at[at], out.at[i // 2, part], sems.at[at]
                        ).start()

        for at in range(amount * parts):
            pltpu.make_async_copy(held.at[at], kept.at[0, 0], sems.at[at]).wait()

    out = jax.ShapeDtypeStruct((amount // 2, parts, size, width), low)
    return pl.pallas_call(
        body,
        in_specs=[in_smem()] + [in_vmem()] * len(flat),
        out_specs=[pl.BlockSpec(memory_space=pl.ANY)] * 2,
        out_shape=[out, out],
        scratch_shapes=[pltpu.VMEM((high[i], tokens[i]), low) for i in range(amount)]
        + [
            pltpu.VMEM((amount * parts, size, width), low),
            pltpu.SemaphoreType.DMA((amount * parts,)),
        ],
        compiler_params=pltpu.CompilerParams(vmem_limit_bytes=60 * 2**20),
        cost_estimate=cheap if parts > 1 else costly,
        name=name,
    )(place, *flat)


def mlp_grads(grad_pres, acts, rows_in, grads_in):
    pieces, rights = len(acts), len(rows_in)
    tokens, width = rows_in[0].shape
    hidden = acts[0].shape[1]
    chunk = 384 if hidden % 384 == 0 else hidden
    steps = hidden // chunk

    def body(*refs):
        step = pl.program_id(0)
        lefts_up, lefts_down = refs[:pieces], refs[pieces : 2 * pieces]
        rights_up = refs[2 * pieces : 2 * pieces + rights]
        rights_down = refs[2 * pieces + rights : -1]
        out = refs[-1]

        def terms(lefts, turn, others):
            here = pl.ds(pl.multiple_of(turn * chunk, chunk), chunk)
            total = jnp.zeros((chunk, width), jnp.float32)
            cursor = 0
            for left in lefts:
                for i in range(left.shape[0] // tokens):
                    total += dot(left[i * tokens : (i + 1) * tokens, here], others[cursor][...], tn)
                    cursor += 1
            out[...] = total.astype(low)

        @pl.when(step < steps)
        def _():
            terms(lefts_up, step, rights_up)

        @pl.when(step >= steps)
        def _():
            terms(lefts_down, step - steps, rights_down)

    arrays = (*grad_pres, *acts, *rows_in, *grads_in)
    chunked = pl.BlockSpec((chunk, width), lambda s: (s, 0))
    return pl.pallas_call(
        body,
        grid=(2 * steps,),
        in_specs=[pl.BlockSpec(array.shape, lambda s: (0, 0)) for array in arrays],
        out_specs=chunked,
        out_shape=jax.ShapeDtypeStruct((2 * hidden, width), low),
        compiler_params=pltpu.CompilerParams(vmem_limit_bytes=60 * 2**20),
        cost_estimate=cheap,
        name="mlp_grads",
    )(*arrays)


def ranked_terms(place, lefts, order, pieces, weight, factors, name):
    tokens, width = factors[0].shape
    count = len(factors)

    def body(place_ref, *refs):
        ins, weight_ref = refs[: len(lefts)], refs[len(lefts)]
        others = refs[len(lefts) + 1 : len(lefts) + 1 + count]
        out, sums = refs[-2:]
        me = place_ref[0]
        for i, slot in enumerate(order):
            rank = lax.rem(me - slot + count, count)
            for cut in cuts_of(width):
                term = jnp.zeros((tokens, cut.stop - cut.start), jnp.float32)
                for which, row, lane, start, depth in pieces[i]:
                    term += dot(
                        ins[which][row : row + tokens, lane : lane + depth],
                        weight_ref[start : start + depth, cut],
                    )
                out[rank, :, cut] = term.astype(low)
                one = jnp.sum(term, axis=0, keepdims=True)
                two = jnp.sum(term * others[i][:, cut].astype(jnp.float32), axis=0, keepdims=True)
                if i:
                    one, two = one + sums[0:1, cut], two + sums[1:2, cut]
                sums[0:1, cut], sums[1:2, cut] = one, two

    return pl.pallas_call(
        body,
        in_specs=[in_smem()] + [in_vmem()] * (len(lefts) + 1 + count),
        out_shape=[
            jax.ShapeDtypeStruct((count, tokens, width), low),
            jax.ShapeDtypeStruct((2, width), jnp.float32),
        ],
        compiler_params=pltpu.CompilerParams(vmem_limit_bytes=60 * 2**20),
        cost_estimate=cheap if len(lefts) > 2 else costly,
        name=name,
    )(place, *lefts, weight, *factors)


def update_slots(master, first_moment, second_moment, filled, which, position, sources):
    capacity, unit_rows, width = master.shape

    group = math.gcd(capacity, 2)
    steps = capacity // group

    def body(filled_ref, which_ref, position_ref, weight, one, two, *rest):
        ins = rest[: len(sources)]
        new_one, new_two, new_weight, held, sems = rest[len(sources) :]
        step = pl.program_id(0)

        def fetch(turn):
            for i in range(group):
                slot = turn * group + i
                for source, ref in enumerate(ins):

                    @pl.when(which_ref[slot] == source)
                    def _():
                        pltpu.make_async_copy(
                            ref.at[position_ref[slot]], held.at[turn % 2, i], sems.at[turn % 2, i]
                        ).start()

        @pl.when(step == 0)
        def _():
            fetch(step)

        @pl.when(step < steps - 1)
        def _():
            fetch(step + 1)

        for i in range(group):
            pltpu.make_async_copy(
                ins[0].at[0], held.at[step % 2, i], sems.at[step % 2, i]
            ).wait()
            mask = (filled_ref[step * group + i] > 0).astype(jnp.float32)
            grad = held[step % 2, i].astype(jnp.float32)
            results = adamw(weight[i], one[i], two[i], grad, mask, rate)
            new_one[i], new_two[i], new_weight[i] = results

    block = pl.BlockSpec((group, unit_rows, width), lambda s, *_: (s, 0, 0))
    return pl.pallas_call(
        body,
        grid_spec=pltpu.PrefetchScalarGridSpec(
            num_scalar_prefetch=3,
            grid=(steps,),
            in_specs=[block] * 3 + [pl.BlockSpec(memory_space=pl.ANY)] * len(sources),
            out_specs=[block] * 3,
            scratch_shapes=[
                pltpu.VMEM((2, group, unit_rows, width), low),
                pltpu.SemaphoreType.DMA((2, group)),
            ],
        ),
        out_shape=[jax.ShapeDtypeStruct(master.shape, jnp.float32)] * 3,
        compiler_params=pltpu.CompilerParams(vmem_limit_bytes=56 * 2**20),
        cost_estimate=cheap,
        name="update_slots",
    )(filled, which, position, master, first_moment, second_moment, *sources)


def adamw(weight, moment_one, moment_two, gradient, filled, step_rate):
    new_one = beta_one * moment_one + (1.0 - beta_one) * gradient
    new_two = beta_two * moment_two + (1.0 - beta_two) * gradient * gradient
    fixed_one = new_one / (1.0 - beta_one**STEP)
    fixed_two = new_two / (1.0 - beta_two**STEP)
    updated = weight - step_rate * (fixed_one / (jnp.sqrt(fixed_two) + adam_eps) + decay * weight)
    return (new_one * filled, new_two * filled, updated * filled)


def swap(values, axis, bit):
    count = lax.axis_size(axis)
    return lax.ppermute(values, axis, [(i, i ^ (1 << bit)) for i in range(count)])


def choose(values, index, axis):
    return lax.dynamic_index_in_dim(values, index, axis, keepdims=False)


def total_sum(values):
    for axis in ("dp", "tensor"):
        for bit in range(lax.axis_size(axis).bit_length() - 1):
            values = values + swap(values, axis, bit)
    return values


def pick_units(master, slot_unit, state, kind, place, sizes, after=()):
    capacity, unit_rows, width = master.shape
    units = state.shape[0]

    def body(slot_ref, state_ref, kind_ref, place_ref, blocks, *rest):
        outs = rest[len(after) : len(after) + len(sizes)]
        highs, lows, zeros, read, sems = rest[len(after) + len(sizes) :]

        def start(source, unit):
            for which, out in enumerate(outs):

                @pl.when(kind_ref[unit] == which)
                def _():
                    pltpu.make_async_copy(source, out.at[place_ref[unit]], sems.at[unit]).start()

        @pl.loop(0, capacity)
        def _(slot):
            @pl.when(slot_ref[slot] >= 0)
            def _():
                pltpu.make_async_copy(blocks.at[slot], highs.at[slot], read.at[slot]).start()

        zeros[...] = jnp.zeros_like(zeros)

        @pl.loop(0, units)
        def _(unit):
            @pl.when(state_ref[unit] == 0)
            def _():
                start(zeros, unit)

        @pl.loop(0, capacity)
        def _(slot):
            @pl.when(slot_ref[slot] >= 0)
            def _():
                pltpu.make_async_copy(blocks.at[slot], highs.at[slot], read.at[slot]).wait()
                lows[slot] = highs[slot].astype(low)
                start(lows.at[slot], slot_ref[slot])

        @pl.loop(0, units)
        def _(unit):
            @pl.when(state_ref[unit] < 2)
            def _():
                pltpu.make_async_copy(zeros, outs[0].at[0], sems.at[unit]).wait()

    return pl.pallas_call(
        body,
        grid_spec=pltpu.PrefetchScalarGridSpec(
            num_scalar_prefetch=4,
            grid=(1,),
            in_specs=[pl.BlockSpec(memory_space=pl.ANY)] * (1 + len(after)),
            out_specs=[pl.BlockSpec(memory_space=pl.ANY)] * len(sizes),
            scratch_shapes=[
                pltpu.VMEM((capacity, unit_rows, width), jnp.float32),
                pltpu.VMEM((capacity, unit_rows, width), low),
                pltpu.VMEM((unit_rows, width), low),
                pltpu.SemaphoreType.DMA((capacity,)),
                pltpu.SemaphoreType.DMA((units,)),
            ],
        ),
        out_shape=[jax.ShapeDtypeStruct((size, unit_rows, width), low) for size in sizes],
        compiler_params=pltpu.CompilerParams(vmem_limit_bytes=56 * 2**20),
        cost_estimate=cheap,
        name="pick_units",
    )(slot_unit, state, kind, place, master, *after)


def place_blocks(sources, which, position, parts=1):
    amount = which.shape[0]
    shape = sources[0].shape[1:]
    size = amount // parts

    def body(which_ref, position_ref, *rest):
        ins, outs = rest[: len(sources)], rest[len(sources) : len(sources) + parts]
        held, read, sems = rest[len(sources) + parts :]

        @pl.loop(0, amount)
        def _(i):
            for source, ref in enumerate(ins):

                @pl.when(which_ref[i] == source)
                def _():
                    pltpu.make_async_copy(ref.at[position_ref[i]], held.at[i], read.at[i]).start()

        for part, out in enumerate(outs):

            @pl.loop(0, size)
            def _(j):
                i = part * size + j
                pltpu.make_async_copy(ins[0].at[0], held.at[i], read.at[i]).wait()
                pltpu.make_async_copy(held.at[i], out.at[j], sems.at[i]).start()

        @pl.loop(0, amount)
        def _(i):
            pltpu.make_async_copy(held.at[i], outs[0].at[0], sems.at[i]).wait()

    return pl.pallas_call(
        body,
        grid_spec=pltpu.PrefetchScalarGridSpec(
            num_scalar_prefetch=2,
            grid=(1,),
            in_specs=[pl.BlockSpec(memory_space=pl.ANY)] * len(sources),
            out_specs=[pl.BlockSpec(memory_space=pl.ANY)] * parts,
            scratch_shapes=[
                pltpu.VMEM((amount,) + shape, low),
                pltpu.SemaphoreType.DMA((amount,)),
                pltpu.SemaphoreType.DMA((amount,)),
            ],
        ),
        out_shape=[jax.ShapeDtypeStruct((size,) + shape, low)] * parts,
        compiler_params=pltpu.CompilerParams(vmem_limit_bytes=56 * 2**20),
        cost_estimate=cheap,
        name="place_blocks",
    )(which, position, *sources)


def stack_pairs(pairs):
    shape = (len(pairs),) + pairs[0].shape[1:]

    def body(*refs):
        for i, pair in enumerate(refs[:-2]):
            for half in range(2):
                refs[half - 2][i] = pair[half]

    return pl.pallas_call(
        body,
        out_shape=[jax.ShapeDtypeStruct(shape, low)] * 2,
        cost_estimate=costly,
        name="stack_pairs",
    )(*pairs)


def hops(values, step, turn):
    count = lax.axis_size("tensor")
    if step > 0:
        pairs = [(i, i + 1) for i in range(turn - 1, count - 1)]
    else:
        pairs = [(i, i - 1) for i in range(1, count - turn + 1)]
    return lax.ppermute(values, "tensor", pairs)


fence = lax.optimization_barrier


def in_pool(member, inner, inner_count):
    me = lax.axis_index("dp")
    half, core = member >> 3, ((member >> 2) & 1) ^ (me & 1)
    far_y, far_x = ((member >> 1) & 1) ^ ((me >> 2) & 1), (member & 1) ^ ((me >> 1) & 1)
    where_first = (far_y * 2 + far_x) * inner_count
    where_second = (4 + far_x * 2 + far_y) * inner_count
    return (core, jnp.where(half == 0, where_first, where_second) + inner)


def on_device(
    hidden_in,
    time_embed,
    caption_table,
    caption_ids,
    owners,
    master,
    first_moment,
    second_moment,
    mod_table,
    mod_first,
    mod_second,
    out_grad,
):
    count = lax.axis_size("tensor")
    dp_count = lax.axis_size("dp")
    me_dp = lax.axis_index("dp")
    me_tensor = lax.axis_index("tensor")
    capacity, unit_rows, width = master.shape
    units = owners.shape[0]
    tokens = hidden_in.shape[1]
    text_count = caption_ids.shape[1]
    share = width // count
    per = share // unit_rows
    ups = (units - 8 * per) // 2
    rank_of = ranks_of(owners)
    mine = owners == me_dp
    match = (rank_of[None, :] == jnp.arange(capacity)[:, None]) & mine[None, :]
    filled = jnp.any(match, axis=1)
    unit_of_slot = jnp.sum(jnp.where(match, jnp.arange(units)[None, :], 0), axis=1)

    square = [list(range(i * per, (i + 1) * per)) for i in range(8)]
    group_attn = square[0] + square[1] + square[2] + square[5]
    group_full = square[3] + square[4] + square[6] + square[7]
    group_mlp = list(range(8 * per, units))
    members = len(group_attn)
    plane = dp_count == 8 and members == 16 and len(group_mlp) % dp_count == 0
    member_of = np.zeros(units, np.int32)
    member_of[group_attn] = np.arange(members)
    member_of[group_full] = np.arange(members)
    is_attn = np.zeros(units, bool)
    is_attn[group_attn] = True
    is_mlp = np.zeros(units, bool)
    is_mlp[group_mlp] = True

    latent_in = hidden_in[0].astype(jnp.float32)
    modulate = mod_table + time_embed[0]

    def mod_row(which_row):
        return modulate[which_row][None, :]

    normed_one, inverse_one = layer_norm(latent_in)
    bits = dp_count.bit_length() - 1
    vocab_rows = caption_table.shape[0]

    def caption_terms(ids):
        chosen = ids.reshape(-1) - me_dp * vocab_rows
        onehot = (chosen[:, None] == jnp.arange(vocab_rows)[None, :]).astype(low)
        terms = jnp.dot(onehot, caption_table, preferred_element_type=jnp.float32).astype(low)
        return terms.reshape(dp_count, text_count, -1)

    def modulated(normed):
        return (normed.astype(jnp.float32) * (1.0 + mod_row(1)) + mod_row(0)).astype(low)

    def whole_text(text_ring):
        return from_ring(text_ring, -1).transpose(1, 0, 2).reshape(text_count, width)

    def own_keys(text_low, w_attn):
        return project(text_low, w_attn)[:, 3 * share :].astype(low)

    def exchanged(attended, keys):
        parts = [
            jnp.concatenate([attended[k * tokens : (k + 1) * tokens], keys]) for k in range(count)
        ]
        return [parts[0]] + [shift(parts[k], count - k) for k in range(1, count)]

    where = jnp.stack([me_tensor, me_dp & 1]).astype(jnp.int32)

    n_low = normed_one.astype(low)
    if plane:
        core, far_x, far_y = (
            ((member_of >> 2) & 1) ^ (me_dp & 1),
            (member_of & 1) ^ ((me_dp >> 1) & 1),
            ((member_of >> 1) & 1) ^ ((me_dp >> 2) & 1),
        )
        place = jnp.where(is_attn, far_x * 4 + far_y * 2, 8 + far_y * 4 + far_x * 2)
        place = jnp.where(is_mlp, np.arange(units) - 8 * per, place + (member_of >> 3))
        kind = jnp.where(is_mlp, 0, core)
        slot_mlp = unit_of_slot >= 8 * per
        owned_state = mine.astype(jnp.int32)
        ids = lax.all_gather(caption_ids, "dp", axis=0, tiled=True)
        ids = jnp.take(ids, me_dp ^ jnp.arange(dp_count), axis=0, mode="clip")
        up, down = hops(n_low, 1, 1), hops(n_low, -1, 1)
        kept, given = pick_units(
            master,
            jnp.where(filled & ~slot_mlp, unit_of_slot, -1),
            jnp.where(is_mlp, 2, owned_state),
            kind,
            place,
            (members, members),
        )
        got = swap(given, "dp", 0)
        (mlp_part,) = pick_units(
            master,
            jnp.where(filled & slot_mlp, unit_of_slot, -1),
            jnp.where(is_mlp, owned_state, 2),
            kind,
            place,
            (len(group_mlp),),
            (kept,),
        )
        mlp_part = lax.psum_scatter(mlp_part, "dp", scatter_dimension=0, tiled=True)
        n_up, n_down = [up], [down]
        kept, got, up, down, ids = fence((kept, got, up, down, ids))
        pieces = [kept[i : i + 4] + got[i : i + 4] for i in range(0, members, 4)]
        attn_two, attn_send, full_two, full_send = fence(tuple(pieces))
        up, down = hops(up, 1, 2), hops(down, -1, 2)
        attn_got = swap(attn_send, "dp", 1)
        full_got = swap(full_send, "dp", 2)
        text = caption_terms(ids)
        text = text[0:4] + swap(text[4:8], "dp", 2)
        n_up.append(up), n_down.append(down)
        attn_two, attn_got, full_two, full_got, up, down, text = fence(
            (attn_two, attn_got, full_two, full_got, up, down, text)
        )
        pieces = [x[i : i + 2] + y[i : i + 2] for x, y in ((attn_two, attn_got), (full_two, full_got)) for i in (0, 2)]
        attn_one, attn_send, full_one, full_send = fence(tuple(pieces))
        up, down = hops(up, 1, 3), hops(down, -1, 3)
        attn_got = swap(attn_send, "dp", 2)
        full_got = swap(full_send, "dp", 1)
        text = text[0:2] + swap(text[2:4], "dp", 1)
        n_up.append(up), n_down.append(down)
        attn_one, attn_got, full_one, full_got, up, down, text, mlp_part = fence(
            (attn_one, attn_got, full_one, full_got, up, down, text, mlp_part)
        )
        attn_one, full_one = attn_one + attn_got, full_one + full_got
        n_up[-1], n_down[-1] = up, down
        w_mlp = lax.all_gather(mlp_part, "dp", axis=0, tiled=True)
        first_ring, second_ring = stack_pairs(ring(full_one))
        first = jnp.concatenate([attn_one[0:1], swap(attn_one[0:1], "dp", 1)])
        second = jnp.concatenate([attn_one[1:2], swap(attn_one[1:2], "dp", 2)])
        pool = jnp.concatenate([first, swap(first, "dp", 2), second, swap(second, "dp", 1)])
        other = swap(pool, "dp", 0)
        text = text[0] + swap(text[1], "dp", 0)
        *n_slots, h_one_all = line_slots(
            where, n_low, n_up, n_down, jnp.concatenate([mod_row(0), mod_row(1)])
        )
        n_slots = [n_low] + n_slots
        grad_own = out_grad[0]
        pool, other, first_ring, second_ring, h_one_all, text, grad_own = fence(
            (pool, other, first_ring, second_ring, h_one_all, text, grad_own)
        )
        grad_whole = lax.all_gather(grad_own, "tensor", axis=0)
        first, second = first_ring, second_ring
        first_got = swap(first, "dp", 1)
        second_got = swap(second, "dp", 2)
        text_ring = ring(text)
        (w_attn,) = place_blocks((pool, other), *in_pool(np.arange(members), 0, 1))
        w_attn = w_attn.reshape(-1, width)
        qkv = project(h_one_all, w_attn).astype(low)
        attended, logs = self_attend(qkv, share)
        first = jnp.concatenate([first, first_got])
        second = jnp.concatenate([second, second_got])
        first, second, text_ring, attended, logs, w_attn, w_mlp = fence(
            (first, second, text_ring, attended, logs, w_attn, w_mlp)
        )
        first_far, second_far = swap(first, "dp", 2), swap(second, "dp", 1)
        first_other, second_other = swap(first, "dp", 0), swap(second, "dp", 0)
        text_low = whole_text(jnp.stack(text_ring))
        mixed = exchanged(attended, own_keys(text_low, w_attn))
        first_far, second_far, first_other, second_other, mixed, grad_whole = fence(
            (first_far, second_far, first_other, second_other, mixed, grad_whole)
        )
        first_last, second_last = swap(first_far, "dp", 0), swap(second_far, "dp", 0)
        listing = np.arange(count * members)
        matrix, rank, head = listing // (count * per), listing // per % count, listing % per
        slot = lax.rem(me_tensor - rank + count, count)
        which, position = in_pool(matrix * per + head, slot, count)
        blocks = 2 * count
        w_full = place_blocks(
            (first, first_far, second, second_far, first_other, first_last, second_other, second_last),
            which * 4 + position // blocks,
            position % blocks,
            parts=4,
        )
        w_full = [part.reshape(width, width) for part in w_full]
    else:
        slots_low = master.astype(low)
        rows = jnp.take(slots_low, rank_of, axis=0, mode="clip")
        rows = lax.psum(jnp.where(mine[:, None, None], rows, jnp.zeros((), low)), "dp")
        w_attn = rows[np.array(group_attn)].reshape(-1, width)
        w_full = lax.all_gather(rows[np.array(group_full)], "tensor", axis=0)
        w_full = w_full.reshape(count, 4, share, width).swapaxes(0, 1).reshape(4, width, width)
        w_full = [w_full[i] for i in range(4)]
        w_mlp = rows[8 * per :]
        n_slots = ring(n_low)
        normed_all = jnp.concatenate(n_slots)
        grad_whole = lax.all_gather(out_grad[0], "tensor", axis=0)
        ids = caption_ids
        for bit in range(bits):
            ids = jnp.concatenate([ids, swap(ids, "dp", bit)])
        text = caption_terms(ids)
        for bit in reversed(range(bits)):
            text = text[: 1 << bit] + swap(text[1 << bit :], "dp", bit)
        text_low = whole_text(jnp.stack(ring(text[0])))
        h_one_all = modulated(normed_all)
        qkv = project(h_one_all, w_attn).astype(low)
        attended, logs = self_attend(qkv, share)
        mixed = exchanged(attended, own_keys(text_low, w_attn))
    w_cross = w_full
    w_out, c_query, c_value, c_out = w_full
    w_mlp = w_mlp.reshape(-1, width)

    rows = jnp.concatenate([mod_row(2), mod_row(3), mod_row(4)])
    (
        branch_one,
        first_low,
        cq_rows,
        ck_rows,
        cv_rows,
        crossed,
        second_res,
        normed_two,
        h_two,
        inverse_two,
    ) = cross_block(
        where, mixed, hidden_in[0], rows, text_low, *w_cross
    )

    h_slots = ring(h_two)
    out_slots = [
        choose(grad_whole, lax.rem(me_tensor - k + count, count), 0) for k in range(count)
    ]
    grad_slots = [(mod_row(5) * item.astype(jnp.float32)).astype(low) for item in out_slots]
    near = [k for k in range(1, count) if 2 * k != count]
    far = [k for k in range(1, count) if 2 * k == count]
    acts, grad_pres, grad_terms, order = [], [], [], []
    for members_now in ([0], near, far):
        act, grad_pre, *terms = mlp_core(
            [h_slots[k] for k in members_now],
            [grad_slots[k] for k in members_now],
            w_mlp,
            acts[-1:],
        )
        acts.append(act), grad_pres.append(grad_pre)
        order += members_now
        grad_terms += [
            shift(term, count - k) if k else term for k, term in zip(members_now, terms)
        ]
    mlp_grad = mlp_grads(
        grad_pres, acts, [h_slots[k] for k in order], [grad_slots[k] for k in order]
    ).reshape(-1, unit_rows, width)
    hidden_share = w_mlp.shape[0] // 2
    pieces = [
        [(which, row, 0, hidden_share, hidden_share)]
        for which, act in enumerate(acts)
        for row in range(0, act.shape[0], tokens)
    ]
    branch_terms, branch_sums = ranked_terms(
        where, acts, order, pieces, w_mlp, [out_slots[k] for k in order], "mlp_out"
    )
    branch_row = branch_sums[1]
    grad_terms, branch_terms = fence((grad_terms, branch_terms))
    if plane:
        mlp_sum = lax.psum_scatter(mlp_grad, "dp", scatter_dimension=0, tiled=True)

    (
        first_grad,
        cross_low,
        grad_cq,
        attn_low,
        grad_cv,
        row_sums,
        *grad_mixed,
    ) = cross_back(
        where,
        grad_terms,
        out_grad[0],
        rows,
        normed_two,
        inverse_two,
        branch_one,
        cq_rows,
        ck_rows,
        cv_rows,
        c_out,
        c_query,
        w_out,
        (mlp_grad,),
    )

    grad_parts = [grad_mixed[0]] + [shift(grad_mixed[k], k) for k in range(1, count)]
    full_pairs = [
        ([(item, 0, share, None) for item in mixed], attn_low),
        ([(grad_cq, 0, width, 0)], first_low),
        ([(grad_cv, 0, width, 0)], text_low),
        ([(crossed, 0, width, 0)], cross_low),
    ]
    half = (share // HEAD_DIM // 2) * HEAD_DIM
    spans = [(0, half), (half, share)]

    def attention_pairs(grads, grad_parts):
        keys = sum(item[tokens:].astype(jnp.float32) for item in grad_parts).astype(low)
        pairs = [
            (
                [
                    (item, i * (end - begin), end - begin, begin)
                    for item, (begin, end) in zip(grads, spans)
                ],
                h_one_all,
            )
            for i in range(3)
        ]
        return pairs + [([(keys, 0, share, 0)], text_low)]

    def input_terms(grads):
        pieces = [
            [
                (which, slot * tokens, i * (end - begin), i * share + begin, end - begin)
                for which, (begin, end) in enumerate(spans)
                for i in range(3)
            ]
            for slot in range(count)
        ]
        return ranked_terms(where, grads, range(count), pieces, w_attn, n_slots, "attn_terms")

    if plane:
        x_bit, y_bit = (me_dp >> 1) & 1, (me_dp >> 2) & 1

        def split(total, bit, axis):
            return (choose(total, bit, axis), choose(total, 1 - bit, axis))

        kept, given = outer_halves(where, full_pairs, count, "full_grads")
        got = swap(given, "dp", 0)
        grad_parts, kept, got, branch_terms = fence((grad_parts, kept, got, branch_terms))
        branch_two = lax.psum_scatter(
            branch_terms.reshape(-1, width), "tensor", scatter_dimension=0, tiled=True
        )
        box = (2, count, 2, 2, unit_rows, width)
        kept, got = kept.reshape(box), got.reshape(box)
        kept_one = choose(kept[0], x_bit, 2) + choose(got[0], x_bit, 2)
        given_one = choose(kept[0], 1 - x_bit, 2) + choose(got[0], 1 - x_bit, 2)
        kept_two = choose(kept[1], y_bit, 1) + choose(got[1], y_bit, 1)
        given_two = choose(kept[1], 1 - y_bit, 1) + choose(got[1], 1 - y_bit, 1)
        kept_one, given_one, kept_two, given_two, grad_parts = fence(
            (kept_one, given_one, kept_two, given_two, grad_parts)
        )
        got_one, got_two = swap(given_one, "dp", 1), swap(given_two, "dp", 2)
        grads_early = self_attend_back(qkv, grad_parts, attended, logs, share, *spans[0])
        kept_one, got_one, kept_two, got_two, grads_early, grad_parts = fence(
            (kept_one, got_one, kept_two, got_two, grads_early, grad_parts)
        )
        kept_one, given_one = split(kept_one + got_one, y_bit, 1)
        kept_two, given_two = split(kept_two + got_two, x_bit, 1)
        kept_one, given_one, kept_two, given_two, grad_parts = fence(
            (kept_one, given_one, kept_two, given_two, grad_parts)
        )
        got_one, got_two = swap(given_one, "dp", 2), swap(given_two, "dp", 1)
        grads_late = self_attend_back(qkv, grad_parts, attended, logs, share, *spans[1])
        kept_one, got_one, kept_two, got_two, grads_early, grads_late, mlp_sum = fence(
            (kept_one, got_one, kept_two, got_two, grads_early, grads_late, mlp_sum)
        )
        mlp_sum = lax.all_gather(mlp_sum, "dp", axis=0, tiled=True)
        full_parts = to_ring(jnp.stack([kept_one + got_one, kept_two + got_two], axis=1))
        full_parts = [full_parts[k] for k in range(count)]
        full_parts, grads_early, grads_late = fence((full_parts, grads_early, grads_late))
        grads_qkv = [grads_early, grads_late]
        full_got = [shift(full_parts[k], k) for k in range(1, count)]
        attn_kept, attn_given = outer_halves(
            where, attention_pairs(grads_qkv, grad_parts), 1, "attn_grads"
        )
        attn_got = swap(attn_given, "dp", 0)
        grad_h_terms, grad_h_sums = input_terms(grads_qkv)
        mod_terms = jnp.concatenate([grad_h_sums, row_sums, branch_row[None]])
        grad_h_one = lax.psum_scatter(
            grad_h_terms.reshape(-1, width), "tensor", scatter_dimension=0, tiled=True
        )
        attn_kept, attn_got, mod_terms, branch_two = fence(
            (attn_kept, attn_got, mod_terms, branch_two)
        )
        attn_all = (attn_kept + attn_got).reshape(2, 2, 2, unit_rows, width)
        one_kept, one_given = split(attn_all[0], x_bit, 1)
        two_kept, two_given = split(attn_all[1], y_bit, 0)
        one_got, two_got = swap(one_given, "dp", 1), swap(two_given, "dp", 2)
        mod_terms = mod_terms + swap(mod_terms, "dp", 0)
        full_own = full_parts[0]
        one_kept, one_got, two_kept, two_got, mod_terms, full_own, full_got = fence(
            (one_kept, one_got, two_kept, two_got, mod_terms, full_own, full_got)
        )
        full_sum = full_own.astype(jnp.float32)
        for part in full_got:
            full_sum = full_sum + part.astype(jnp.float32)
        full_sum = full_sum.astype(low)
        one_kept, one_given = split(one_kept + one_got, y_bit, 0)
        two_kept, two_given = split(two_kept + two_got, x_bit, 0)
        one_got, two_got = swap(one_given, "dp", 2), swap(two_given, "dp", 1)
        mod_terms = mod_terms + swap(mod_terms, "dp", 1)
        one_kept, one_got, two_kept, two_got, full_sum, mod_terms, mlp_sum = fence(
            (one_kept, one_got, two_kept, two_got, full_sum, mod_terms, mlp_sum)
        )
        first = jnp.stack([one_kept + one_got, full_sum[0]])
        second = jnp.stack([two_kept + two_got, full_sum[1]])
        first_got, second_got = swap(first, "dp", 1), swap(second, "dp", 2)
        first = jnp.concatenate([first, first_got])
        second = jnp.concatenate([second, second_got])
        mod_terms = mod_terms + swap(mod_terms, "dp", 2)
        first, second, mod_terms = fence((first, second, mod_terms))
        first_far, second_far = swap(first, "dp", 2), swap(second, "dp", 1)
        mod_terms = mod_terms + swap(mod_terms, "tensor", 0)
        first, first_far, second, second_far, mod_terms, grad_h_one = fence(
            (first, first_far, second, second_far, mod_terms, grad_h_one)
        )
        pool = jnp.concatenate([first, first_far, second, second_far])
        other = swap(pool, "dp", 0)
        for bit in range(1, count.bit_length() - 1):
            mod_terms = mod_terms + swap(mod_terms, "tensor", bit)
        pool, other, mod_grad = fence((pool, other, mod_terms))
        which, position = in_pool(member_of, np.where(is_attn, 0, 1), 2)
        which = jnp.where(is_mlp, 2, which)
        position = jnp.where(is_mlp, np.arange(units) - 8 * per, position)
        own = jnp.sum(jnp.where(match[:, :, None], jnp.stack([which, position], 1)[None], 0), axis=1)
        new_first, new_second, new_master = update_slots(
            master,
            first_moment,
            second_moment,
            filled.astype(jnp.int32),
            own[:, 0],
            own[:, 1],
            (pool, other, mlp_sum),
        )
    else:
        branch_two = lax.psum_scatter(
            branch_terms.reshape(-1, width), "tensor", scatter_dimension=0, tiled=True
        )
        grads_qkv = [self_attend_back(qkv, grad_parts, attended, logs, share, *span) for span in spans]
        attn_grads = [
            outer(array[:, lane : lane + lanes], right).astype(low)
            for left, right in attention_pairs(grads_qkv, grad_parts)
            for array, lane, lanes, row in left
        ]
        grad_h_terms, grad_h_sums = input_terms(grads_qkv)
        grad_h_one = lax.psum_scatter(
            grad_h_terms.reshape(-1, width), "tensor", scatter_dimension=0, tiled=True
        )
        mixed_all = from_ring(jnp.stack([item[:tokens] for item in mixed]), 1)
        mixed_all = mixed_all.transpose(1, 0, 2).reshape(tokens, width)
        full_grads = [outer(mixed_all, attn_low)]
        full_grads += [outer(left[0][0], right) for left, right in full_pairs[1:]]
        full_sum = [g.astype(low).reshape(count, share, width) for g in full_grads]
        full_sum = jnp.stack(full_sum, axis=1)
        full_sum = lax.psum_scatter(full_sum, "tensor", scatter_dimension=0, tiled=True)
        order = np.array(group_attn + group_full + group_mlp)
        sums = jnp.concatenate(
            [jnp.concatenate(attn_grads), full_sum.reshape(-1, width), mlp_grad.reshape(-1, width)]
        )
        sums = lax.psum(sums.reshape(units, unit_rows, width), "dp")
        owned = jnp.take(sums, jnp.array(np.argsort(order))[unit_of_slot], axis=0, mode="clip")
        mod_grad = total_sum(jnp.concatenate([grad_h_sums, row_sums, branch_row[None]]))
        new_first, new_second, new_master = adamw(
            master,
            first_moment,
            second_moment,
            owned.astype(jnp.float32),
            filled.astype(jnp.float32)[:, None, None],
            rate,
        )
    branch_two, second_res, grad_h_one, new_first = fence(
        (branch_two, second_res, grad_h_one, new_first)
    )
    grad_h_one = grad_h_one.astype(jnp.float32)
    block_out = second_res + mod_row(5) * branch_two.astype(jnp.float32)
    input_grad = first_grad + norm_back(grad_h_one, normed_one, inverse_one, mod_row(1))
    mod_new_first, mod_new_second, mod_new = adamw(
        mod_table, mod_first, mod_second, mod_grad, 1.0, table_rate
    )
    return (
        block_out[None],
        input_grad[None],
        new_first,
        new_second,
        new_master,
        mod_new_first,
        mod_new_second,
        mod_new,
    )


def solution(mesh):
    in_specs = (
        P("dp", "tensor", None),
        P("dp", None, None),
        P("dp", "tensor"),
        P("dp", None),
        P(),
        P("dp", "tensor", None),
        P("dp", "tensor", None),
        P("dp", "tensor", None),
        P(),
        P(),
        P(),
        P("dp", "tensor", None),
    )
    out_specs = (
        P("dp", "tensor", None),
        P("dp", "tensor", None),
        P("dp", "tensor", None),
        P("dp", "tensor", None),
        P("dp", "tensor", None),
        P(),
        P(),
        P(),
    )
    return jax.shard_map(
        on_device, mesh=mesh, in_specs=in_specs, out_specs=out_specs, check_vma=False
    )
```

```python
import math

import jax
import jax.numpy as jnp
import numpy as np
from jax import lax
from jax.experimental import pallas as pl
from jax.experimental.pallas import tpu as pltpu
from jax.sharding import PartitionSpec as P

HEAD_DIM = 72
STEP = 10


norm_eps = 1e-06
beta_one = 0.9
beta_two = 0.999
rate = 0.03
table_rate = 0.3
decay = 0.01
adam_eps = 1e-08
low = jnp.bfloat16


def ranks_of(owners):
    index = jnp.arange(owners.shape[0])
    before = (owners[None, :] == owners[:, None]) & (index[None, :] < index[:, None])
    return jnp.sum(before.astype(jnp.int32), axis=1)


def layer_norm(values):
    center = values - jnp.mean(values, axis=-1, keepdims=True)
    inverse = lax.rsqrt(jnp.mean(center * center, axis=-1, keepdims=True) + norm_eps)
    return (center * inverse, inverse)


def norm_back(grad_rows, normed, inverse, scale_row):
    scaled = grad_rows * (1.0 + scale_row)
    mean_one = jnp.mean(scaled, axis=-1, keepdims=True)
    mean_two = jnp.mean(scaled * normed, axis=-1, keepdims=True)
    return inverse * (scaled - mean_one - normed * mean_two)


def project(rows, weight):
    return jnp.einsum("ld,rd->lr", rows, weight, preferred_element_type=jnp.float32)


def expand(rows, weight):
    return jnp.einsum("lr,rd->ld", rows, weight, preferred_element_type=jnp.float32)


def outer(left, right):
    return jnp.einsum("lr,ld->rd", left, right, preferred_element_type=jnp.float32)


def shift(values, step):
    count = lax.axis_size("tensor")
    return lax.ppermute(values, "tensor", [(i, (i + step) % count) for i in range(count)])


def ring(values):
    return [values] + [shift(values, k) for k in range(1, lax.axis_size("tensor"))]


def to_ring(stacked):
    count = stacked.shape[0]
    twice = jnp.concatenate([stacked, stacked], axis=0)
    return lax.dynamic_slice_in_dim(twice, lax.axis_index("tensor"), count, 0)


def from_ring(stacked, sign):
    count = stacked.shape[0]
    me = lax.axis_index("tensor")
    place = lax.rem(sign * (jnp.arange(count) - me) + 2 * count, count)
    return jnp.take(stacked, place, axis=0, mode="clip")


cheap = pl.CostEstimate(flops=1000, bytes_accessed=1000, transcendentals=0)
costly = pl.CostEstimate(flops=10**10, bytes_accessed=10**7, transcendentals=0)


def self_attend(qkv, share):
    length = qkv.shape[0]
    rows = min(512, length)
    curve = HEAD_DIM ** (-0.5) * math.log2(math.e)
    heads = share // HEAD_DIM

    def body(qkv_ref, out_ref, log_ref):
        @pl.loop(0, length // rows)
        def _(step):
            here = pl.ds(pl.multiple_of(step * rows, rows), rows)
            parts = []
            for head in range(heads):
                at = head * HEAD_DIM
                q = qkv_ref[here, at : at + HEAD_DIM]
                k = qkv_ref[:, share + at : share + at + HEAD_DIM]
                v = qkv_ref[:, 2 * share + at : 2 * share + at + HEAD_DIM]
                scores = dot(k, q, nt)
                top = jnp.max(scores, axis=0, keepdims=True)
                expo = jnp.exp2((scores - top) * curve)
                total = jnp.sum(expo, axis=0, keepdims=True)
                log_ref[head : head + 1, here] = top * curve + jnp.log2(total)
                parts.append((dot(v, expo.astype(low), tn) * (1.0 / total)).T)
            out_ref[here, :] = jnp.concatenate(parts, axis=1).astype(low)

    return pl.pallas_call(
        body,
        out_shape=[
            jax.ShapeDtypeStruct((length, share), low),
            jax.ShapeDtypeStruct((heads, length), jnp.float32),
        ],
        compiler_params=pltpu.CompilerParams(vmem_limit_bytes=40 * 2**20),
        cost_estimate=cheap,
        name="self_attend",
    )(qkv)


def self_attend_back(qkv, grads, mixed, logs, share, begin, end):
    length = qkv.shape[0]
    rows = length // len(grads)
    span = end - begin
    scale = HEAD_DIM ** (-0.5)
    curve = scale * math.log2(math.e)

    def body(qkv_ref, mixed_ref, log_ref, *refs):
        grad_refs, (out_ref, grad_k, grad_v) = refs[: len(grads)], refs[len(grads) :]
        for step, grad_ref in enumerate(grad_refs):
            here = slice(step * rows, (step + 1) * rows)
            parts = []
            for head, at in enumerate(range(begin, end, HEAD_DIM)):
                q = qkv_ref[here, at : at + HEAD_DIM]
                k = qkv_ref[:, share + at : share + at + HEAD_DIM]
                v = qkv_ref[:, 2 * share + at : 2 * share + at + HEAD_DIM]
                g = grad_ref[0:rows, at : at + HEAD_DIM]
                o = mixed_ref[here, at : at + HEAD_DIM]
                inner = g.astype(jnp.float32) * o.astype(jnp.float32)
                inner = jnp.sum(inner.T, axis=0, keepdims=True)
                which = begin // HEAD_DIM + head
                probs = jnp.exp2(dot(k, q, nt) * curve - log_ref[which : which + 1, here])
                grad_scores = (probs * (dot(v, g, nt) - inner)).astype(low)
                to_v = dot(probs.astype(low), g)
                to_k = dot(grad_scores, q)
                if step:
                    grad_v[head] += to_v
                    grad_k[head] += to_k
                else:
                    grad_v[head] = to_v
                    grad_k[head] = to_k
                parts.append((dot(k, grad_scores, tn) * scale).T)
            out_ref[here, 0:span] = jnp.concatenate(parts, axis=1).astype(low)
        heads = range(span // HEAD_DIM)
        both = [grad_k[head] * scale for head in heads]
        out_ref[:, span : 2 * span] = jnp.concatenate(both, axis=1).astype(low)
        both = [grad_v[head] for head in heads]
        out_ref[:, 2 * span :] = jnp.concatenate(both, axis=1).astype(low)

    return pl.pallas_call(
        body,
        out_shape=jax.ShapeDtypeStruct((length, 3 * span), low),
        scratch_shapes=[pltpu.VMEM((span // HEAD_DIM, length, HEAD_DIM), jnp.float32)] * 2,
        compiler_params=pltpu.CompilerParams(vmem_limit_bytes=40 * 2**20),
        cost_estimate=cheap,
        name="self_attend_back",
    )(qkv, mixed, logs, *grads)


def mlp_core(rows_in, grads_in, w_mlp, after):
    groups = len(rows_in)
    tokens, width = rows_in[0].shape
    hidden = w_mlp.shape[0] // 2
    chunk = 384 if hidden % 384 == 0 else hidden
    steps = hidden // chunk
    curve = 0.7978845608028654

    def body(*refs):
        rows, grads = refs[:groups], refs[groups : 2 * groups]
        up, down = refs[2 * groups : 2 * groups + 2]
        act, grad_pre, *outs = refs[2 * groups + 2 + len(after) : -1]
        total = refs[-1]
        step = pl.program_id(0)
        for i in range(groups):
            pre = lax.dot_general(
                rows[i][...], up[...], (((1,), (1,)), ((), ())), preferred_element_type=jnp.float32
            )
            square = pre * pre
            bend = jnp.tanh(curve * pre * (1.0 + 0.044715 * square))
            half = 0.5 * (1.0 + bend)
            here = pl.ds(i * tokens, tokens)
            act[here, :] = (pre * half).astype(low)
            slope = half + (0.5 * curve) * pre * (1.0 - bend * bend) * (1.0 + 0.134145 * square)
            grad_act = lax.dot_general(
                grads[i][...], down[...], (((1,), (1,)), ((), ())), preferred_element_type=jnp.float32
            )
            grad_low = (grad_act * slope).astype(low)
            grad_pre[here, :] = grad_low
            term = jnp.dot(grad_low, up[...], preferred_element_type=jnp.float32)

            @pl.when(step == 0)
            def _():
                total[here, :] = term

            @pl.when(step > 0)
            def _():
                total[here, :] += term

            @pl.when(step == steps - 1)
            def _():
                outs[i][...] = total[here, :].astype(low)

    whole = pl.BlockSpec((tokens, width), lambda s: (0, 0))
    across = pl.BlockSpec((groups * tokens, chunk), lambda s: (0, s))
    return pl.pallas_call(
        body,
        grid=(steps,),
        in_specs=[whole] * (2 * groups)
        + [
            pl.BlockSpec((chunk, width), lambda s: (s, 0)),
            pl.BlockSpec((chunk, width), lambda s: (steps + s, 0)),
        ]
        + [pl.BlockSpec(memory_space=pl.ANY)] * len(after),
        out_specs=[across, across] + [whole] * groups,
        out_shape=[jax.ShapeDtypeStruct((groups * tokens, hidden), low)] * 2
        + [jax.ShapeDtypeStruct((tokens, width), low)] * groups,
        scratch_shapes=[pltpu.VMEM((groups * tokens, width), jnp.float32)],
        compiler_params=pltpu.CompilerParams(vmem_limit_bytes=60 * 2**20),
        cost_estimate=cheap,
        name="mlp_core",
    )(*rows_in, *grads_in, w_mlp, w_mlp, *after)


nt = (((1,), (1,)), ((), ()))
tn = (((0,), (0,)), ((), ()))


def dot(left, right, dims=(((1,), (0,)), ((), ()))):
    return lax.dot_general(left, right, dims, preferred_element_type=jnp.float32)


def softmax_keys(keys, queries):
    scores = dot(keys, queries, nt) * HEAD_DIM ** (-0.5)
    expo = jnp.exp(scores - jnp.max(scores, axis=0, keepdims=True))
    return expo * (1.0 / jnp.sum(expo, axis=0, keepdims=True))


def cuts_of(width):
    size = 384 if width % 384 == 0 else width
    return [slice(i, i + size) for i in range(0, width, size)]


def in_smem():
    return pl.BlockSpec(memory_space=pltpu.SMEM)


def in_vmem():
    return pl.BlockSpec(memory_space=pltpu.VMEM)


def line_slots(place, own, ups, downs, rows):
    count = len(ups) + 1
    tokens, width = own.shape

    def body(place_ref, *refs):
        own_ref, up_refs, down_refs = refs[0], refs[1:count], refs[count : 2 * count - 1]
        rows_ref, outs, out = refs[2 * count - 1], refs[2 * count : -1], refs[-1]
        me = place_ref[0]

        def modulate(slot, ref):
            value = ref[...].astype(jnp.float32)
            value = value * (1.0 + rows_ref[1:2, :]) + rows_ref[0:1, :]
            out[slot * tokens : (slot + 1) * tokens, :] = value.astype(low)

        modulate(0, own_ref)
        for k in range(1, count):
            for side, ref in ((me >= k, up_refs[k - 1]), (me < k, down_refs[count - k - 1])):

                @pl.when(side)
                def _():
                    outs[k - 1][...] = ref[...]
                    modulate(k, ref)

    shapes = [(tokens, width)] * (count - 1) + [(count * tokens, width)]
    return pl.pallas_call(
        body,
        in_specs=[in_smem()] + [in_vmem()] * (2 * count),
        out_shape=[jax.ShapeDtypeStruct(shape, low) for shape in shapes],
        compiler_params=pltpu.CompilerParams(vmem_limit_bytes=32 * 2**20),
        cost_estimate=cheap,
        name="line_slots",
    )(place, own, *ups, *downs, rows)


def cross_block(place, mixed, hidden, rows, text, w_out, c_query, c_value, c_out):
    count, share = len(mixed), mixed[0].shape[1]
    tokens, width = hidden.shape
    words = text.shape[0]
    per = share // HEAD_DIM

    def body(place_ref, *refs):
        parts = refs[:count]
        x_ref, rows_ref, text_ref = refs[count : count + 3]
        far = refs[count + 3 : count + 7]
        outs = refs[count + 7 : count + 16]
        inverse = refs[count + 16]
        wo, wq, wv, wc, *own = refs[count + 17 : -3]
        held, read, sems = refs[-3:]
        branch, res_low, cq, ck, cv, crossed, res, normed, out = own
        me = place_ref[0]
        loads = [
            pltpu.make_async_copy(source, target, read.at[i])
            for i, (source, target) in enumerate(zip(far, (wo, wq, wv, wc)))
        ]
        stores = [
            pltpu.make_async_copy(source, target, sems.at[i])
            for i, (source, target) in enumerate(zip(own, outs))
        ]
        for load in loads:
            load.start()
        loads[0].wait()
        for cut in cuts_of(width):
            total = jnp.zeros((tokens, cut.stop - cut.start), jnp.float32)
            for k in range(count):
                rank = lax.rem(me + k, count)
                here = pl.ds(pl.multiple_of(rank * share, 32), share)
                total += dot(parts[k][0:tokens, :], wo[here, cut])
            branch[:, cut] = total
            first = x_ref[:, cut].astype(jnp.float32) + rows_ref[0:1, cut] * total
            res[:, cut] = first
            res_low[:, cut] = first.astype(low)
        stores[0].start()
        stores[1].start()
        loads[1].wait()
        loads[2].wait()
        for cut in cuts_of(width):
            cq[:, cut] = dot(res_low[...], wq[cut, :], nt).astype(low)
            cv[:, cut] = dot(text_ref[...], wv[cut, :], nt).astype(low)
        for k in range(count):
            held[lax.rem(me + k, count)] = parts[k][tokens:, :]
        ck[...] = jnp.concatenate([held[rank] for rank in range(count)], axis=1)
        for i in (2, 3, 4):
            stores[i].start()
        parts_out = []
        for at in range(0, width, HEAD_DIM):
            head = slice(at, at + HEAD_DIM)
            probs = softmax_keys(ck[:, head], cq[:, head]).astype(low)
            parts_out.append(dot(cv[:, head], probs, tn).T)
        crossed[...] = jnp.concatenate(parts_out, axis=1).astype(low)
        stores[5].start()
        loads[3].wait()
        for cut in cuts_of(width):
            res[:, cut] += dot(crossed[...], wc[:, cut])
        second = res[...]
        center = second - jnp.mean(second, axis=-1, keepdims=True)
        spread = lax.rsqrt(jnp.mean(center * center, axis=-1, keepdims=True) + norm_eps)
        inverse[...] = spread
        scaled = center * spread
        normed[...] = scaled
        stores[6].start()
        stores[7].start()
        out[...] = (scaled * (1.0 + rows_ref[2:3, :]) + rows_ref[1:2, :]).astype(low)
        stores[8].start()
        for store in stores:
            store.wait()

    wide = (tokens, width)
    shapes = [
        (wide, jnp.float32),
        (wide, low),
        (wide, low),
        ((words, width), low),
        ((words, width), low),
        (wide, low),
        (wide, jnp.float32),
        (wide, jnp.float32),
        (wide, low),
    ]
    anywhere = pl.BlockSpec(memory_space=pl.ANY)
    return pl.pallas_call(
        body,
        in_specs=[in_smem()] + [in_vmem()] * (count + 3) + [anywhere] * 4,
        out_specs=[anywhere] * len(shapes) + [in_vmem()],
        out_shape=[jax.ShapeDtypeStruct(*item) for item in shapes]
        + [jax.ShapeDtypeStruct((tokens, 1), jnp.float32)],
        scratch_shapes=[pltpu.VMEM((width, width), low)] * 4
        + [pltpu.VMEM(*item) for item in shapes]
        + [
            pltpu.VMEM((count, words, share), low),
            pltpu.SemaphoreType.DMA((4,)),
            pltpu.SemaphoreType.DMA((len(shapes),)),
        ],
        compiler_params=pltpu.CompilerParams(vmem_limit_bytes=60 * 2**20),
        cost_estimate=cheap,
        name="cross_block",
    )(place, *mixed, hidden, rows, text, w_out, c_query, c_value, c_out)


def cross_back(
    place, terms, grad, rows, normed, inverse, branch, cq, ck, cv, c_out, c_query, w_out, after
):
    count = len(terms)
    tokens, width = grad.shape
    words = ck.shape[0]
    share = width // count
    scale = HEAD_DIM ** (-0.5)

    def body(place_ref, *refs):
        parts = refs[:count]
        grad_ref, rows_ref, i_ref, k_ref, v_ref = refs[count : count + 5]
        far = refs[count + 5 : count + 11]
        refs = refs[: count + 11] + refs[count + 11 + len(after) :]
        stored = refs[count + 11 : count + 15]
        grad_v, sums = refs[count + 15 : count + 17]
        outs = refs[count + 17 : 2 * count + 17]
        near = refs[2 * count + 17 : 2 * count + 23]
        n_ref, wc, q_ref, wq, wo, b_ref = near
        own = refs[2 * count + 23 : 2 * count + 27]
        first, cross_low, grad_q, attn_low = own
        back, held, read, sems = refs[2 * count + 27 :]
        me = place_ref[0]
        loads = [
            pltpu.make_async_copy(source, target, read.at[i])
            for i, (source, target) in enumerate(zip(far, near))
        ]
        stores = [
            pltpu.make_async_copy(source, target, sems.at[i])
            for i, (source, target) in enumerate(zip(own, stored))
        ]
        for load in loads:
            load.start()
        loads[0].wait()
        total = parts[0][...].astype(jnp.float32)
        for part in parts[1:]:
            total += part[...].astype(jnp.float32)
        n = n_ref[...]
        sums[1:2, :] = jnp.sum(total, axis=0, keepdims=True)
        sums[2:3, :] = jnp.sum(total * n, axis=0, keepdims=True)
        second = grad_ref[...].astype(jnp.float32) + norm_back(total, n, i_ref[...], rows_ref[2:3, :])
        first[...] = second
        cross_low[...] = second.astype(low)
        stores[1].start()
        loads[1].wait()
        loads[2].wait()
        for cut in cuts_of(width):
            back[:, cut] = dot(cross_low[...], wc[cut, :], nt).astype(low)
        grads = ([], [], [])
        for at in range(0, width, HEAD_DIM):
            head = slice(at, at + HEAD_DIM)
            q, k, v, g = q_ref[:, head], k_ref[:, head], v_ref[:, head], back[:, head]
            probs = softmax_keys(k, q)
            grad_probs = dot(v, g, nt)
            inner = jnp.sum(probs * grad_probs, axis=0, keepdims=True)
            grad_scores = (probs * (grad_probs - inner)).astype(low)
            grads[0].append((dot(k, grad_scores, tn) * scale).T)
            grads[1].append(dot(grad_scores, q) * scale)
            grads[2].append(dot(probs.astype(low), g))
        grad_q[...] = jnp.concatenate(grads[0], axis=1).astype(low)
        grad_v[...] = jnp.concatenate(grads[2], axis=1).astype(low)
        heads = share // HEAD_DIM
        for rank in range(count):
            pieces = grads[1][rank * heads : (rank + 1) * heads]
            held[rank] = jnp.concatenate(pieces, axis=1).astype(low)
        stores[2].start()
        for load in loads[3:]:
            load.wait()
        for cut in cuts_of(width):
            whole = first[:, cut] + dot(grad_q[...], wq[:, cut])
            first[:, cut] = whole
            attn_low[:, cut] = (rows_ref[0:1, cut] * whole).astype(low)
            sums[0:1, cut] = jnp.sum(b_ref[:, cut] * whole, axis=0, keepdims=True)
        stores[0].start()
        stores[3].start()
        for k in range(count):
            rank = lax.rem(me + k, count)
            here = pl.ds(pl.multiple_of(rank * share, 32), share)
            outs[k][0:tokens, :] = dot(attn_low[...], wo[here, :], nt).astype(low)
            outs[k][tokens:, :] = held[rank]
        for store in stores:
            store.wait()

    wide, square = (tokens, width), (width, width)
    shapes = [
        (wide, jnp.float32),
        (wide, low),
        (wide, low),
        (wide, low),
        ((words, width), low),
        ((3, width), jnp.float32),
    ] + [((tokens + words, share), low)] * count
    anywhere = pl.BlockSpec(memory_space=pl.ANY)
    loaded = [
        pltpu.VMEM(wide, jnp.float32),
        pltpu.VMEM(square, low),
        pltpu.VMEM(wide, low),
        pltpu.VMEM(square, low),
        pltpu.VMEM(square, low),
        pltpu.VMEM(wide, jnp.float32),
    ]
    return pl.pallas_call(
        body,
        in_specs=[in_smem()] + [in_vmem()] * (count + 5) + [anywhere] * (6 + len(after)),
        out_specs=[anywhere] * 4 + [in_vmem()] * (2 + count),
        out_shape=[jax.ShapeDtypeStruct(*item) for item in shapes],
        scratch_shapes=loaded
        + [pltpu.VMEM(*item) for item in shapes[:4]]
        + [
            pltpu.VMEM(wide, low),
            pltpu.VMEM((count, words, share), low),
            pltpu.SemaphoreType.DMA((6,)),
            pltpu.SemaphoreType.DMA((4,)),
        ],
        compiler_params=pltpu.CompilerParams(vmem_limit_bytes=60 * 2**20),
        cost_estimate=cheap,
        name="cross_back",
    )(
        place,
        *terms,
        grad,
        rows,
        inverse,
        ck,
        cv,
        normed,
        c_out,
        cq,
        c_query,
        w_out,
        branch,
        *after,
    )


def outer_halves(place, pairs, parts, name):
    width = pairs[0][1].shape[1]
    high = [sum(piece[2] for piece in left) for left, _ in pairs]
    size = high[0] // parts
    tokens = [right.shape[0] for _, right in pairs]
    flat = []

    def index_of(array):
        for i, other in enumerate(flat):
            if other is array:
                return i
        flat.append(array)
        return len(flat) - 1

    plans = [
        ([(index_of(array), *rest) for array, *rest in left], index_of(right))
        for left, right in pairs
    ]
    amount = len(pairs)

    def body(place_ref, *refs):
        ins, (kept, given), (held, sems) = refs[: len(flat)], refs[len(flat) :][:2], refs[-2:]
        turned = refs[len(flat) + 2 : -2]
        me, core = place_ref[0], place_ref[1]
        for i, (left, right) in enumerate(plans):
            for k, (which, lane, lanes, row) in enumerate(left):
                piece = ins[which][0 : tokens[i], lane : lane + lanes]
                piece = piece.astype(jnp.float32).T.astype(low)
                if row is None:
                    rank = lax.rem(me + k, len(left))
                    turned[i][pl.ds(pl.multiple_of(rank * lanes, 32), lanes), :] = piece
                else:
                    turned[i][row : row + lanes, :] = piece
            for part in range(parts):
                at = i * parts + part
                tile = dot(turned[i][part * size : (part + 1) * size, :], ins[right][...])
                held[at] = tile.astype(low)
                for out, side in ((kept, 0), (given, 1)):

                    @pl.when((core ^ (i & 1)) == side)
                    def _():
                        pltpu.make_async_copy(
                            held.at[at], out.at[i // 2, part], sems.at[at]
                        ).start()

        for at in range(amount * parts):
            pltpu.make_async_copy(held.at[at], kept.at[0, 0], sems.at[at]).wait()

    out = jax.ShapeDtypeStruct((amount // 2, parts, size, width), low)
    return pl.pallas_call(
        body,
        in_specs=[in_smem()] + [in_vmem()] * len(flat),
        out_specs=[pl.BlockSpec(memory_space=pl.ANY)] * 2,
        out_shape=[out, out],
        scratch_shapes=[pltpu.VMEM((high[i], tokens[i]), low) for i in range(amount)]
        + [
            pltpu.VMEM((amount * parts, size, width), low),
            pltpu.SemaphoreType.DMA((amount * parts,)),
        ],
        compiler_params=pltpu.CompilerParams(vmem_limit_bytes=60 * 2**20),
        cost_estimate=cheap if parts > 1 else costly,
        name=name,
    )(place, *flat)


def mlp_grads(grad_pres, acts, rows_in, grads_in):
    pieces, rights = len(acts), len(rows_in)
    tokens, width = rows_in[0].shape
    hidden = acts[0].shape[1]
    chunk = 384 if hidden % 384 == 0 else hidden
    steps = hidden // chunk

    def body(*refs):
        step = pl.program_id(0)
        lefts_up, lefts_down = refs[:pieces], refs[pieces : 2 * pieces]
        rights_up = refs[2 * pieces : 2 * pieces + rights]
        rights_down = refs[2 * pieces + rights : -1]
        out = refs[-1]

        def terms(lefts, turn, others):
            here = pl.ds(pl.multiple_of(turn * chunk, chunk), chunk)
            total = jnp.zeros((chunk, width), jnp.float32)
            cursor = 0
            for left in lefts:
                for i in range(left.shape[0] // tokens):
                    total += dot(left[i * tokens : (i + 1) * tokens, here], others[cursor][...], tn)
                    cursor += 1
            out[...] = total.astype(low)

        @pl.when(step < steps)
        def _():
            terms(lefts_up, step, rights_up)

        @pl.when(step >= steps)
        def _():
            terms(lefts_down, step - steps, rights_down)

    arrays = (*grad_pres, *acts, *rows_in, *grads_in)
    chunked = pl.BlockSpec((chunk, width), lambda s: (s, 0))
    return pl.pallas_call(
        body,
        grid=(2 * steps,),
        in_specs=[pl.BlockSpec(array.shape, lambda s: (0, 0)) for array in arrays],
        out_specs=chunked,
        out_shape=jax.ShapeDtypeStruct((2 * hidden, width), low),
        compiler_params=pltpu.CompilerParams(vmem_limit_bytes=60 * 2**20),
        cost_estimate=cheap,
        name="mlp_grads",
    )(*arrays)


def ranked_terms(place, lefts, order, pieces, weight, factors, name):
    tokens, width = factors[0].shape
    count = len(factors)

    def body(place_ref, *refs):
        ins, weight_ref = refs[: len(lefts)], refs[len(lefts)]
        others = refs[len(lefts) + 1 : len(lefts) + 1 + count]
        out, sums = refs[-2:]
        me = place_ref[0]
        for i, slot in enumerate(order):
            rank = lax.rem(me - slot + count, count)
            for cut in cuts_of(width):
                term = jnp.zeros((tokens, cut.stop - cut.start), jnp.float32)
                for which, row, lane, start, depth in pieces[i]:
                    term += dot(
                        ins[which][row : row + tokens, lane : lane + depth],
                        weight_ref[start : start + depth, cut],
                    )
                out[rank, :, cut] = term.astype(low)
                one = jnp.sum(term, axis=0, keepdims=True)
                two = jnp.sum(term * others[i][:, cut].astype(jnp.float32), axis=0, keepdims=True)
                if i:
                    one, two = one + sums[0:1, cut], two + sums[1:2, cut]
                sums[0:1, cut], sums[1:2, cut] = one, two

    return pl.pallas_call(
        body,
        in_specs=[in_smem()] + [in_vmem()] * (len(lefts) + 1 + count),
        out_shape=[
            jax.ShapeDtypeStruct((count, tokens, width), low),
            jax.ShapeDtypeStruct((2, width), jnp.float32),
        ],
        compiler_params=pltpu.CompilerParams(vmem_limit_bytes=60 * 2**20),
        cost_estimate=cheap if len(lefts) > 2 else costly,
        name=name,
    )(place, *lefts, weight, *factors)


def sum_split(place, kept, got):
    count, unit_rows, width = kept.shape[1], kept.shape[4], kept.shape[5]

    def body(place_ref, one, two, keep_x, give_x, keep_y, give_y):
        x, y = place_ref[0], place_ref[1]

        def total(*index):
            return (one[index].astype(jnp.float32) + two[index].astype(jnp.float32)).astype(low)

        for j in range(2):
            keep_x[0, j] = total(0, 0, j, x)
            give_x[0, j] = total(0, 0, j, 1 - x)
            keep_y[0, j] = total(1, 0, y, j)
            give_y[0, j] = total(1, 0, 1 - y, j)

    block = pl.BlockSpec((2, 1, 2, 2, unit_rows, width), lambda r, *_: (0, r, 0, 0, 0, 0))
    part = pl.BlockSpec((1, 2, unit_rows, width), lambda r, *_: (r, 0, 0, 0))
    return pl.pallas_call(
        body,
        grid_spec=pltpu.PrefetchScalarGridSpec(
            num_scalar_prefetch=1, grid=(count,), in_specs=[block] * 2, out_specs=[part] * 4
        ),
        out_shape=[jax.ShapeDtypeStruct((count, 2, unit_rows, width), low)] * 4,
        compiler_params=pltpu.CompilerParams(vmem_limit_bytes=60 * 2**20),
        cost_estimate=cheap,
        name="sum_split",
    )(place, kept, got)


def update_slots(master, first_moment, second_moment, filled, which, position, sources):
    capacity, unit_rows, width = master.shape

    group = math.gcd(capacity, 2)
    steps = capacity // group

    def body(filled_ref, which_ref, position_ref, weight, one, two, *rest):
        ins = rest[: len(sources)]
        new_one, new_two, new_weight, held, sems = rest[len(sources) :]
        step = pl.program_id(0)

        def fetch(turn):
            for i in range(group):
                slot = turn * group + i
                for source, ref in enumerate(ins):

                    @pl.when(which_ref[slot] == source)
                    def _():
                        pltpu.make_async_copy(
                            ref.at[position_ref[slot]], held.at[turn % 2, i], sems.at[turn % 2, i]
                        ).start()

        @pl.when(step == 0)
        def _():
            fetch(step)

        @pl.when(step < steps - 1)
        def _():
            fetch(step + 1)

        for i in range(group):
            pltpu.make_async_copy(
                ins[0].at[0], held.at[step % 2, i], sems.at[step % 2, i]
            ).wait()
            mask = (filled_ref[step * group + i] > 0).astype(jnp.float32)
            grad = held[step % 2, i].astype(jnp.float32)
            results = adamw(weight[i], one[i], two[i], grad, mask, rate)
            new_one[i], new_two[i], new_weight[i] = results

    block = pl.BlockSpec((group, unit_rows, width), lambda s, *_: (s, 0, 0))
    return pl.pallas_call(
        body,
        grid_spec=pltpu.PrefetchScalarGridSpec(
            num_scalar_prefetch=3,
            grid=(steps,),
            in_specs=[block] * 3 + [pl.BlockSpec(memory_space=pl.ANY)] * len(sources),
            out_specs=[block] * 3,
            scratch_shapes=[
                pltpu.VMEM((2, group, unit_rows, width), low),
                pltpu.SemaphoreType.DMA((2, group)),
            ],
        ),
        out_shape=[jax.ShapeDtypeStruct(master.shape, jnp.float32)] * 3,
        compiler_params=pltpu.CompilerParams(vmem_limit_bytes=56 * 2**20),
        cost_estimate=cheap,
        name="update_slots",
    )(filled, which, position, master, first_moment, second_moment, *sources)


def adamw(weight, moment_one, moment_two, gradient, filled, step_rate):
    new_one = beta_one * moment_one + (1.0 - beta_one) * gradient
    new_two = beta_two * moment_two + (1.0 - beta_two) * gradient * gradient
    fixed_one = new_one / (1.0 - beta_one**STEP)
    fixed_two = new_two / (1.0 - beta_two**STEP)
    updated = weight - step_rate * (fixed_one / (jnp.sqrt(fixed_two) + adam_eps) + decay * weight)
    return (new_one * filled, new_two * filled, updated * filled)


def swap(values, axis, bit):
    count = lax.axis_size(axis)
    return lax.ppermute(values, axis, [(i, i ^ (1 << bit)) for i in range(count)])


def choose(values, index, axis):
    return lax.dynamic_index_in_dim(values, index, axis, keepdims=False)


def total_sum(values):
    for axis in ("dp", "tensor"):
        for bit in range(lax.axis_size(axis).bit_length() - 1):
            values = values + swap(values, axis, bit)
    return values


def pick_units(master, slot_unit, state, kind, place, sizes, after=()):
    capacity, unit_rows, width = master.shape
    units = state.shape[0]

    def body(slot_ref, state_ref, kind_ref, place_ref, blocks, *rest):
        outs = rest[len(after) : len(after) + len(sizes)]
        highs, lows, zeros, read, sems = rest[len(after) + len(sizes) :]

        def start(source, unit):
            for which, out in enumerate(outs):

                @pl.when(kind_ref[unit] == which)
                def _():
                    pltpu.make_async_copy(source, out.at[place_ref[unit]], sems.at[unit]).start()

        @pl.loop(0, capacity)
        def _(slot):
            @pl.when(slot_ref[slot] >= 0)
            def _():
                pltpu.make_async_copy(blocks.at[slot], highs.at[slot], read.at[slot]).start()

        zeros[...] = jnp.zeros_like(zeros)

        @pl.loop(0, units)
        def _(unit):
            @pl.when(state_ref[unit] == 0)
            def _():
                start(zeros, unit)

        @pl.loop(0, capacity)
        def _(slot):
            @pl.when(slot_ref[slot] >= 0)
            def _():
                pltpu.make_async_copy(blocks.at[slot], highs.at[slot], read.at[slot]).wait()
                lows[slot] = highs[slot].astype(low)
                start(lows.at[slot], slot_ref[slot])

        @pl.loop(0, units)
        def _(unit):
            @pl.when(state_ref[unit] < 2)
            def _():
                pltpu.make_async_copy(zeros, outs[0].at[0], sems.at[unit]).wait()

    return pl.pallas_call(
        body,
        grid_spec=pltpu.PrefetchScalarGridSpec(
            num_scalar_prefetch=4,
            grid=(1,),
            in_specs=[pl.BlockSpec(memory_space=pl.ANY)] * (1 + len(after)),
            out_specs=[pl.BlockSpec(memory_space=pl.ANY)] * len(sizes),
            scratch_shapes=[
                pltpu.VMEM((capacity, unit_rows, width), jnp.float32),
                pltpu.VMEM((capacity, unit_rows, width), low),
                pltpu.VMEM((unit_rows, width), low),
                pltpu.SemaphoreType.DMA((capacity,)),
                pltpu.SemaphoreType.DMA((units,)),
            ],
        ),
        out_shape=[jax.ShapeDtypeStruct((size, unit_rows, width), low) for size in sizes],
        compiler_params=pltpu.CompilerParams(vmem_limit_bytes=56 * 2**20),
        cost_estimate=cheap,
        name="pick_units",
    )(slot_unit, state, kind, place, master, *after)


def place_blocks(sources, which, position, parts=1):
    amount = which.shape[0]
    shape = sources[0].shape[1:]
    size = amount // parts

    def body(which_ref, position_ref, *rest):
        ins, outs = rest[: len(sources)], rest[len(sources) : len(sources) + parts]
        held, read, sems = rest[len(sources) + parts :]

        @pl.loop(0, amount)
        def _(i):
            for source, ref in enumerate(ins):

                @pl.when(which_ref[i] == source)
                def _():
                    pltpu.make_async_copy(ref.at[position_ref[i]], held.at[i], read.at[i]).start()

        for part, out in enumerate(outs):

            @pl.loop(0, size)
            def _(j):
                i = part * size + j
                pltpu.make_async_copy(ins[0].at[0], held.at[i], read.at[i]).wait()
                pltpu.make_async_copy(held.at[i], out.at[j], sems.at[i]).start()

        @pl.loop(0, amount)
        def _(i):
            pltpu.make_async_copy(held.at[i], outs[0].at[0], sems.at[i]).wait()

    return pl.pallas_call(
        body,
        grid_spec=pltpu.PrefetchScalarGridSpec(
            num_scalar_prefetch=2,
            grid=(1,),
            in_specs=[pl.BlockSpec(memory_space=pl.ANY)] * len(sources),
            out_specs=[pl.BlockSpec(memory_space=pl.ANY)] * parts,
            scratch_shapes=[
                pltpu.VMEM((amount,) + shape, low),
                pltpu.SemaphoreType.DMA((amount,)),
                pltpu.SemaphoreType.DMA((amount,)),
            ],
        ),
        out_shape=[jax.ShapeDtypeStruct((size,) + shape, low)] * parts,
        compiler_params=pltpu.CompilerParams(vmem_limit_bytes=56 * 2**20),
        cost_estimate=cheap,
        name="place_blocks",
    )(which, position, *sources)


def stack_pairs(pairs):
    shape = (len(pairs),) + pairs[0].shape[1:]

    def body(*refs):
        for i, pair in enumerate(refs[:-2]):
            for half in range(2):
                refs[half - 2][i] = pair[half]

    return pl.pallas_call(
        body,
        out_shape=[jax.ShapeDtypeStruct(shape, low)] * 2,
        cost_estimate=costly,
        name="stack_pairs",
    )(*pairs)


def hops(values, step, turn):
    count = lax.axis_size("tensor")
    if step > 0:
        pairs = [(i, i + 1) for i in range(turn - 1, count - 1)]
    else:
        pairs = [(i, i - 1) for i in range(1, count - turn + 1)]
    return lax.ppermute(values, "tensor", pairs)


fence = lax.optimization_barrier


def in_pool(member, inner, inner_count):
    me = lax.axis_index("dp")
    half, core = member >> 3, ((member >> 2) & 1) ^ (me & 1)
    far_y, far_x = ((member >> 1) & 1) ^ ((me >> 2) & 1), (member & 1) ^ ((me >> 1) & 1)
    where_first = (far_y * 2 + far_x) * inner_count
    where_second = (4 + far_x * 2 + far_y) * inner_count
    return (core, jnp.where(half == 0, where_first, where_second) + inner)


def on_device(
    hidden_in,
    time_embed,
    caption_table,
    caption_ids,
    owners,
    master,
    first_moment,
    second_moment,
    mod_table,
    mod_first,
    mod_second,
    out_grad,
):
    count = lax.axis_size("tensor")
    dp_count = lax.axis_size("dp")
    me_dp = lax.axis_index("dp")
    me_tensor = lax.axis_index("tensor")
    capacity, unit_rows, width = master.shape
    units = owners.shape[0]
    tokens = hidden_in.shape[1]
    text_count = caption_ids.shape[1]
    share = width // count
    per = share // unit_rows
    ups = (units - 8 * per) // 2
    rank_of = ranks_of(owners)
    mine = owners == me_dp
    match = (rank_of[None, :] == jnp.arange(capacity)[:, None]) & mine[None, :]
    filled = jnp.any(match, axis=1)
    unit_of_slot = jnp.sum(jnp.where(match, jnp.arange(units)[None, :], 0), axis=1)

    square = [list(range(i * per, (i + 1) * per)) for i in range(8)]
    group_attn = square[0] + square[1] + square[2] + square[5]
    group_full = square[3] + square[4] + square[6] + square[7]
    group_mlp = list(range(8 * per, units))
    members = len(group_attn)
    plane = dp_count == 8 and members == 16 and len(group_mlp) % dp_count == 0
    member_of = np.zeros(units, np.int32)
    member_of[group_attn] = np.arange(members)
    member_of[group_full] = np.arange(members)
    is_attn = np.zeros(units, bool)
    is_attn[group_attn] = True
    is_mlp = np.zeros(units, bool)
    is_mlp[group_mlp] = True

    latent_in = hidden_in[0].astype(jnp.float32)
    modulate = mod_table + time_embed[0]

    def mod_row(which_row):
        return modulate[which_row][None, :]

    normed_one, inverse_one = layer_norm(latent_in)
    bits = dp_count.bit_length() - 1
    vocab_rows = caption_table.shape[0]

    def caption_terms(ids):
        chosen = ids.reshape(-1) - me_dp * vocab_rows
        onehot = (chosen[:, None] == jnp.arange(vocab_rows)[None, :]).astype(low)
        terms = jnp.dot(onehot, caption_table, preferred_element_type=jnp.float32).astype(low)
        return terms.reshape(dp_count, text_count, -1)

    def modulated(normed):
        return (normed.astype(jnp.float32) * (1.0 + mod_row(1)) + mod_row(0)).astype(low)

    def whole_text(text_ring):
        return from_ring(text_ring, -1).transpose(1, 0, 2).reshape(text_count, width)

    def own_keys(text_low, w_attn):
        return project(text_low, w_attn)[:, 3 * share :].astype(low)

    def exchanged(attended, keys):
        parts = [
            jnp.concatenate([attended[k * tokens : (k + 1) * tokens], keys]) for k in range(count)
        ]
        return [parts[0]] + [shift(parts[k], count - k) for k in range(1, count)]

    where = jnp.stack([me_tensor, me_dp & 1]).astype(jnp.int32)

    n_low = normed_one.astype(low)
    if plane:
        core, far_x, far_y = (
            ((member_of >> 2) & 1) ^ (me_dp & 1),
            (member_of & 1) ^ ((me_dp >> 1) & 1),
            ((member_of >> 1) & 1) ^ ((me_dp >> 2) & 1),
        )
        place = jnp.where(is_attn, far_x * 4 + far_y * 2, 8 + far_y * 4 + far_x * 2)
        place = jnp.where(is_mlp, np.arange(units) - 8 * per, place + (member_of >> 3))
        kind = jnp.where(is_mlp, 0, core)
        slot_mlp = unit_of_slot >= 8 * per
        owned_state = mine.astype(jnp.int32)
        ids = lax.all_gather(caption_ids, "dp", axis=0, tiled=True)
        ids = jnp.take(ids, me_dp ^ jnp.arange(dp_count), axis=0, mode="clip")
        up, down = hops(n_low, 1, 1), hops(n_low, -1, 1)
        kept, given = pick_units(
            master,
            jnp.where(filled & ~slot_mlp, unit_of_slot, -1),
            jnp.where(is_mlp, 2, owned_state),
            kind,
            place,
            (members, members),
        )
        got = swap(given, "dp", 0)
        (mlp_part,) = pick_units(
            master,
            jnp.where(filled & slot_mlp, unit_of_slot, -1),
            jnp.where(is_mlp, owned_state, 2),
            kind,
            place,
            (len(group_mlp),),
            (kept,),
        )
        mlp_part = lax.psum_scatter(mlp_part, "dp", scatter_dimension=0, tiled=True)
        n_up, n_down = [up], [down]
        kept, got, up, down, ids = fence((kept, got, up, down, ids))
        pieces = [kept[i : i + 4] + got[i : i + 4] for i in range(0, members, 4)]
        attn_two, attn_send, full_two, full_send = fence(tuple(pieces))
        up, down = hops(up, 1, 2), hops(down, -1, 2)
        attn_got = swap(attn_send, "dp", 1)
        full_got = swap(full_send, "dp", 2)
        text = caption_terms(ids)
        text = text[0:4] + swap(text[4:8], "dp", 2)
        n_up.append(up), n_down.append(down)
        attn_two, attn_got, full_two, full_got, up, down, text = fence(
            (attn_two, attn_got, full_two, full_got, up, down, text)
        )
        pieces = [x[i : i + 2] + y[i : i + 2] for x, y in ((attn_two, attn_got), (full_two, full_got)) for i in (0, 2)]
        attn_one, attn_send, full_one, full_send = fence(tuple(pieces))
        up, down = hops(up, 1, 3), hops(down, -1, 3)
        attn_got = swap(attn_send, "dp", 2)
        full_got = swap(full_send, "dp", 1)
        text = text[0:2] + swap(text[2:4], "dp", 1)
        n_up.append(up), n_down.append(down)
        attn_one, attn_got, full_one, full_got, up, down, text, mlp_part = fence(
            (attn_one, attn_got, full_one, full_got, up, down, text, mlp_part)
        )
        attn_one, full_one = attn_one + attn_got, full_one + full_got
        n_up[-1], n_down[-1] = up, down
        w_mlp = lax.all_gather(mlp_part, "dp", axis=0, tiled=True)
        first_ring, second_ring = stack_pairs(ring(full_one))
        first = jnp.concatenate([attn_one[0:1], swap(attn_one[0:1], "dp", 1)])
        second = jnp.concatenate([attn_one[1:2], swap(attn_one[1:2], "dp", 2)])
        pool = jnp.concatenate([first, swap(first, "dp", 2), second, swap(second, "dp", 1)])
        other = swap(pool, "dp", 0)
        text = text[0] + swap(text[1], "dp", 0)
        *n_slots, h_one_all = line_slots(
            where, n_low, n_up, n_down, jnp.concatenate([mod_row(0), mod_row(1)])
        )
        n_slots = [n_low] + n_slots
        grad_own = out_grad[0]
        pool, other, first_ring, second_ring, h_one_all, text, grad_own = fence(
            (pool, other, first_ring, second_ring, h_one_all, text, grad_own)
        )
        grad_whole = lax.all_gather(grad_own, "tensor", axis=0)
        first, second = first_ring, second_ring
        first_got = swap(first, "dp", 1)
        second_got = swap(second, "dp", 2)
        text_ring = ring(text)
        (w_attn,) = place_blocks((pool, other), *in_pool(np.arange(members), 0, 1))
        w_attn = w_attn.reshape(-1, width)
        qkv = project(h_one_all, w_attn).astype(low)
        attended, logs = self_attend(qkv, share)
        first = jnp.concatenate([first, first_got])
        second = jnp.concatenate([second, second_got])
        first, second, text_ring, attended, logs, w_attn, w_mlp = fence(
            (first, second, text_ring, attended, logs, w_attn, w_mlp)
        )
        first_far, second_far = swap(first, "dp", 2), swap(second, "dp", 1)
        text_low = whole_text(jnp.stack(text_ring))
        mixed = exchanged(attended, own_keys(text_low, w_attn))
        first_far, second_far, mixed, grad_whole = fence(
            (first_far, second_far, mixed, grad_whole)
        )
        first_other, second_other = swap(first, "dp", 0), swap(second, "dp", 0)
        first_last, second_last = swap(first_far, "dp", 0), swap(second_far, "dp", 0)
        listing = np.arange(count * members)
        matrix, rank, head = listing // (count * per), listing // per % count, listing % per
        slot = lax.rem(me_tensor - rank + count, count)
        which, position = in_pool(matrix * per + head, slot, count)
        blocks = 2 * count
        w_full = place_blocks(
            (first, first_far, second, second_far, first_other, first_last, second_other, second_last),
            which * 4 + position // blocks,
            position % blocks,
            parts=4,
        )
        w_full = [part.reshape(width, width) for part in w_full]
    else:
        slots_low = master.astype(low)
        rows = jnp.take(slots_low, rank_of, axis=0, mode="clip")
        rows = lax.psum(jnp.where(mine[:, None, None], rows, jnp.zeros((), low)), "dp")
        w_attn = rows[np.array(group_attn)].reshape(-1, width)
        w_full = lax.all_gather(rows[np.array(group_full)], "tensor", axis=0)
        w_full = w_full.reshape(count, 4, share, width).swapaxes(0, 1).reshape(4, width, width)
        w_full = [w_full[i] for i in range(4)]
        w_mlp = rows[8 * per :]
        n_slots = ring(n_low)
        normed_all = jnp.concatenate(n_slots)
        grad_whole = lax.all_gather(out_grad[0], "tensor", axis=0)
        ids = caption_ids
        for bit in range(bits):
            ids = jnp.concatenate([ids, swap(ids, "dp", bit)])
        text = caption_terms(ids)
        for bit in reversed(range(bits)):
            text = text[: 1 << bit] + swap(text[1 << bit :], "dp", bit)
        text_low = whole_text(jnp.stack(ring(text[0])))
        h_one_all = modulated(normed_all)
        qkv = project(h_one_all, w_attn).astype(low)
        attended, logs = self_attend(qkv, share)
        mixed = exchanged(attended, own_keys(text_low, w_attn))
    w_cross = w_full
    w_out, c_query, c_value, c_out = w_full
    w_mlp = w_mlp.reshape(-1, width)

    rows = jnp.concatenate([mod_row(2), mod_row(3), mod_row(4)])
    (
        branch_one,
        first_low,
        cq_rows,
        ck_rows,
        cv_rows,
        crossed,
        second_res,
        normed_two,
        h_two,
        inverse_two,
    ) = cross_block(
        where, mixed, hidden_in[0], rows, text_low, *w_cross
    )

    h_slots = {0: h_two}
    out_slots = [
        choose(grad_whole, lax.rem(me_tensor - k + count, count), 0) for k in range(count)
    ]
    grad_slots = [(mod_row(5) * item.astype(jnp.float32)).astype(low) for item in out_slots]
    near = [k for k in range(1, count) if 2 * k != count]
    far = [k for k in range(1, count) if 2 * k == count]
    acts, grad_pres, grad_terms, order = [], [], [], []
    for k in near:
        h_slots[k] = shift(h_two, k)
    for members_now in ([0], near, far):
        act, grad_pre, *terms = mlp_core(
            [h_slots[k] for k in members_now],
            [grad_slots[k] for k in members_now],
            w_mlp,
            acts[-1:],
        )
        if members_now == [0]:
            h_two, act = fence((h_two, act))
            for k in far:
                h_slots[k] = shift(h_two, k)
        acts.append(act), grad_pres.append(grad_pre)
        order += members_now
        grad_terms += [
            shift(term, count - k) if k else term for k, term in zip(members_now, terms)
        ]
    mlp_grad = mlp_grads(
        grad_pres, acts, [h_slots[k] for k in order], [grad_slots[k] for k in order]
    ).reshape(-1, unit_rows, width)
    hidden_share = w_mlp.shape[0] // 2
    pieces = [
        [(which, row, 0, hidden_share, hidden_share)]
        for which, act in enumerate(acts)
        for row in range(0, act.shape[0], tokens)
    ]
    branch_terms, branch_sums = ranked_terms(
        where, acts, order, pieces, w_mlp, [out_slots[k] for k in order], "mlp_out"
    )
    branch_row = branch_sums[1]
    grad_terms, branch_terms = fence((grad_terms, branch_terms))
    if plane:
        mlp_sum = lax.psum_scatter(mlp_grad, "dp", scatter_dimension=0, tiled=True)

    (
        first_grad,
        cross_low,
        grad_cq,
        attn_low,
        grad_cv,
        row_sums,
        *grad_mixed,
    ) = cross_back(
        where,
        grad_terms,
        out_grad[0],
        rows,
        normed_two,
        inverse_two,
        branch_one,
        cq_rows,
        ck_rows,
        cv_rows,
        c_out,
        c_query,
        w_out,
        (mlp_grad,),
    )

    grad_parts = [grad_mixed[0]] + [shift(grad_mixed[k], k) for k in range(1, count)]
    full_pairs = [
        ([(item, 0, share, None) for item in mixed], attn_low),
        ([(grad_cq, 0, width, 0)], first_low),
        ([(grad_cv, 0, width, 0)], text_low),
        ([(crossed, 0, width, 0)], cross_low),
    ]
    half = (share // HEAD_DIM // 2) * HEAD_DIM
    spans = [(0, half), (half, share)]

    def attention_pairs(grads, grad_parts):
        keys = sum(item[tokens:].astype(jnp.float32) for item in grad_parts).astype(low)
        pairs = [
            (
                [
                    (item, i * (end - begin), end - begin, begin)
                    for item, (begin, end) in zip(grads, spans)
                ],
                h_one_all,
            )
            for i in range(3)
        ]
        return pairs + [([(keys, 0, share, 0)], text_low)]

    def input_terms(grads):
        pieces = [
            [
                (which, slot * tokens, i * (end - begin), i * share + begin, end - begin)
                for which, (begin, end) in enumerate(spans)
                for i in range(3)
            ]
            for slot in range(count)
        ]
        return ranked_terms(where, grads, range(count), pieces, w_attn, n_slots, "attn_terms")

    if plane:
        x_bit, y_bit = (me_dp >> 1) & 1, (me_dp >> 2) & 1

        def split(total, bit, axis):
            return (choose(total, bit, axis), choose(total, 1 - bit, axis))

        kept, given = outer_halves(where, full_pairs, count, "full_grads")
        got = swap(given, "dp", 0)
        grad_parts, kept, got, mlp_sum = fence((grad_parts, kept, got, mlp_sum))
        mlp_sum = lax.all_gather(mlp_sum, "dp", axis=0, tiled=True)
        box = (2, count, 2, 2, unit_rows, width)
        bits_here = jnp.stack([x_bit, y_bit]).astype(jnp.int32)
        kept_one, given_one, kept_two, given_two = sum_split(
            bits_here, kept.reshape(box), got.reshape(box)
        )
        got_one, got_two = swap(given_one, "dp", 1), swap(given_two, "dp", 2)
        grads_early = self_attend_back(qkv, grad_parts, attended, logs, share, *spans[0])
        kept_one, got_one, kept_two, got_two, grads_early, grad_parts, branch_terms = fence(
            (kept_one, got_one, kept_two, got_two, grads_early, grad_parts, branch_terms)
        )
        branch_two = lax.psum_scatter(
            branch_terms.reshape(-1, width), "tensor", scatter_dimension=0, tiled=True
        )
        kept_one, given_one = split(kept_one + got_one, y_bit, 1)
        kept_two, given_two = split(kept_two + got_two, x_bit, 1)
        kept_one, given_one, kept_two, given_two, grad_parts = fence(
            (kept_one, given_one, kept_two, given_two, grad_parts)
        )
        got_one, got_two = swap(given_one, "dp", 2), swap(given_two, "dp", 1)
        grads_late = self_attend_back(qkv, grad_parts, attended, logs, share, *spans[1])
        kept_one, got_one, kept_two, got_two, grads_early, grads_late, mlp_sum = fence(
            (kept_one, got_one, kept_two, got_two, grads_early, grads_late, mlp_sum)
        )
        full_parts = to_ring(jnp.stack([kept_one + got_one, kept_two + got_two], axis=1))
        full_parts = [full_parts[k] for k in range(count)]
        full_parts, grads_early, grads_late = fence((full_parts, grads_early, grads_late))
        grads_qkv = [grads_early, grads_late]
        full_got = [shift(full_parts[k], k) for k in range(1, count)]
        attn_kept, attn_given = outer_halves(
            where, attention_pairs(grads_qkv, grad_parts), 1, "attn_grads"
        )
        attn_got = swap(attn_given, "dp", 0)
        grad_h_terms, grad_h_sums = input_terms(grads_qkv)
        mod_terms = jnp.concatenate([grad_h_sums, row_sums, branch_row[None]])
        grad_h_one = lax.psum_scatter(
            grad_h_terms.reshape(-1, width), "tensor", scatter_dimension=0, tiled=True
        )
        attn_kept, attn_got, mod_terms, branch_two = fence(
            (attn_kept, attn_got, mod_terms, branch_two)
        )
        attn_all = (attn_kept + attn_got).reshape(2, 2, 2, unit_rows, width)
        one_kept, one_given = split(attn_all[0], x_bit, 1)
        two_kept, two_given = split(attn_all[1], y_bit, 0)
        one_got, two_got = swap(one_given, "dp", 1), swap(two_given, "dp", 2)
        mod_terms = mod_terms + swap(mod_terms, "dp", 0)
        full_own = full_parts[0]
        one_kept, one_got, two_kept, two_got, mod_terms, full_own, full_got = fence(
            (one_kept, one_got, two_kept, two_got, mod_terms, full_own, full_got)
        )
        full_sum = full_own.astype(jnp.float32)
        for part in full_got:
            full_sum = full_sum + part.astype(jnp.float32)
        full_sum = full_sum.astype(low)
        one_kept, one_given = split(one_kept + one_got, y_bit, 0)
        two_kept, two_given = split(two_kept + two_got, x_bit, 0)
        one_got, two_got = swap(one_given, "dp", 2), swap(two_given, "dp", 1)
        mod_terms = mod_terms + swap(mod_terms, "dp", 1)
        one_kept, one_got, two_kept, two_got, full_sum, mod_terms = fence(
            (one_kept, one_got, two_kept, two_got, full_sum, mod_terms)
        )
        first = jnp.stack([one_kept + one_got, full_sum[0]])
        second = jnp.stack([two_kept + two_got, full_sum[1]])
        first_got, second_got = swap(first, "dp", 1), swap(second, "dp", 2)
        first = jnp.concatenate([first, first_got])
        second = jnp.concatenate([second, second_got])
        mod_terms = mod_terms + swap(mod_terms, "dp", 2)
        first, second, mod_terms = fence((first, second, mod_terms))
        first_far, second_far = swap(first, "dp", 2), swap(second, "dp", 1)
        mod_terms = mod_terms + swap(mod_terms, "tensor", 0)
        first, first_far, second, second_far, mod_terms, grad_h_one = fence(
            (first, first_far, second, second_far, mod_terms, grad_h_one)
        )
        pool = jnp.concatenate([first, first_far, second, second_far])
        other = swap(pool, "dp", 0)
        for bit in range(1, count.bit_length() - 1):
            mod_terms = mod_terms + swap(mod_terms, "tensor", bit)
        pool, other, mod_grad = fence((pool, other, mod_terms))
        which, position = in_pool(member_of, np.where(is_attn, 0, 1), 2)
        which = jnp.where(is_mlp, 2, which)
        position = jnp.where(is_mlp, np.arange(units) - 8 * per, position)
        own = jnp.sum(jnp.where(match[:, :, None], jnp.stack([which, position], 1)[None], 0), axis=1)
        new_first, new_second, new_master = update_slots(
            master,
            first_moment,
            second_moment,
            filled.astype(jnp.int32),
            own[:, 0],
            own[:, 1],
            (pool, other, mlp_sum),
        )
    else:
        branch_two = lax.psum_scatter(
            branch_terms.reshape(-1, width), "tensor", scatter_dimension=0, tiled=True
        )
        grads_qkv = [self_attend_back(qkv, grad_parts, attended, logs, share, *span) for span in spans]
        attn_grads = [
            outer(array[:, lane : lane + lanes], right).astype(low)
            for left, right in attention_pairs(grads_qkv, grad_parts)
            for array, lane, lanes, row in left
        ]
        grad_h_terms, grad_h_sums = input_terms(grads_qkv)
        grad_h_one = lax.psum_scatter(
            grad_h_terms.reshape(-1, width), "tensor", scatter_dimension=0, tiled=True
        )
        mixed_all = from_ring(jnp.stack([item[:tokens] for item in mixed]), 1)
        mixed_all = mixed_all.transpose(1, 0, 2).reshape(tokens, width)
        full_grads = [outer(mixed_all, attn_low)]
        full_grads += [outer(left[0][0], right) for left, right in full_pairs[1:]]
        full_sum = [g.astype(low).reshape(count, share, width) for g in full_grads]
        full_sum = jnp.stack(full_sum, axis=1)
        full_sum = lax.psum_scatter(full_sum, "tensor", scatter_dimension=0, tiled=True)
        order = np.array(group_attn + group_full + group_mlp)
        sums = jnp.concatenate(
            [jnp.concatenate(attn_grads), full_sum.reshape(-1, width), mlp_grad.reshape(-1, width)]
        )
        sums = lax.psum(sums.reshape(units, unit_rows, width), "dp")
        owned = jnp.take(sums, jnp.array(np.argsort(order))[unit_of_slot], axis=0, mode="clip")
        mod_grad = total_sum(jnp.concatenate([grad_h_sums, row_sums, branch_row[None]]))
        new_first, new_second, new_master = adamw(
            master,
            first_moment,
            second_moment,
            owned.astype(jnp.float32),
            filled.astype(jnp.float32)[:, None, None],
            rate,
        )
    branch_two, second_res, grad_h_one, new_first = fence(
        (branch_two, second_res, grad_h_one, new_first)
    )
    grad_h_one = grad_h_one.astype(jnp.float32)
    block_out = second_res + mod_row(5) * branch_two.astype(jnp.float32)
    input_grad = first_grad + norm_back(grad_h_one, normed_one, inverse_one, mod_row(1))
    mod_new_first, mod_new_second, mod_new = adamw(
        mod_table, mod_first, mod_second, mod_grad, 1.0, table_rate
    )
    return (
        block_out[None],
        input_grad[None],
        new_first,
        new_second,
        new_master,
        mod_new_first,
        mod_new_second,
        mod_new,
    )


def solution(mesh):
    in_specs = (
        P("dp", "tensor", None),
        P("dp", None, None),
        P("dp", "tensor"),
        P("dp", None),
        P(),
        P("dp", "tensor", None),
        P("dp", "tensor", None),
        P("dp", "tensor", None),
        P(),
        P(),
        P(),
        P("dp", "tensor", None),
    )
    out_specs = (
        P("dp", "tensor", None),
        P("dp", "tensor", None),
        P("dp", "tensor", None),
        P("dp", "tensor", None),
        P("dp", "tensor", None),
        P(),
        P(),
        P(),
    )
    return jax.shard_map(
        on_device, mesh=mesh, in_specs=in_specs, out_specs=out_specs, check_vma=False
    )
```

```python
import math

import jax
import jax.numpy as jnp
import numpy as np
from jax import lax
from jax.experimental import pallas as pl
from jax.experimental.pallas import tpu as pltpu
from jax.sharding import PartitionSpec as P

HEAD_DIM = 72
STEP = 10


norm_eps = 1e-06
beta_one = 0.9
beta_two = 0.999
rate = 0.03
table_rate = 0.3
decay = 0.01
adam_eps = 1e-08
low = jnp.bfloat16


def ranks_of(owners):
    index = jnp.arange(owners.shape[0])
    before = (owners[None, :] == owners[:, None]) & (index[None, :] < index[:, None])
    return jnp.sum(before.astype(jnp.int32), axis=1)


def layer_norm(values):
    center = values - jnp.mean(values, axis=-1, keepdims=True)
    inverse = lax.rsqrt(jnp.mean(center * center, axis=-1, keepdims=True) + norm_eps)
    return (center * inverse, inverse)


def norm_back(grad_rows, normed, inverse, scale_row):
    scaled = grad_rows * (1.0 + scale_row)
    mean_one = jnp.mean(scaled, axis=-1, keepdims=True)
    mean_two = jnp.mean(scaled * normed, axis=-1, keepdims=True)
    return inverse * (scaled - mean_one - normed * mean_two)


def project(rows, weight):
    return jnp.einsum("ld,rd->lr", rows, weight, preferred_element_type=jnp.float32)


def expand(rows, weight):
    return jnp.einsum("lr,rd->ld", rows, weight, preferred_element_type=jnp.float32)


def outer(left, right):
    return jnp.einsum("lr,ld->rd", left, right, preferred_element_type=jnp.float32)


def shift(values, step):
    count = lax.axis_size("tensor")
    return lax.ppermute(values, "tensor", [(i, (i + step) % count) for i in range(count)])


def ring(values):
    return [values] + [shift(values, k) for k in range(1, lax.axis_size("tensor"))]


def to_ring(stacked):
    count = stacked.shape[0]
    twice = jnp.concatenate([stacked, stacked], axis=0)
    return lax.dynamic_slice_in_dim(twice, lax.axis_index("tensor"), count, 0)


def from_ring(stacked, sign):
    count = stacked.shape[0]
    me = lax.axis_index("tensor")
    place = lax.rem(sign * (jnp.arange(count) - me) + 2 * count, count)
    return jnp.take(stacked, place, axis=0, mode="clip")


cheap = pl.CostEstimate(flops=1000, bytes_accessed=1000, transcendentals=0)
costly = pl.CostEstimate(flops=10**10, bytes_accessed=10**7, transcendentals=0)


def self_attend(qkv, share):
    length = qkv.shape[0]
    rows = min(512, length)
    curve = HEAD_DIM ** (-0.5) * math.log2(math.e)
    heads = share // HEAD_DIM

    def body(qkv_ref, out_ref, log_ref):
        @pl.loop(0, length // rows)
        def _(step):
            here = pl.ds(pl.multiple_of(step * rows, rows), rows)
            parts = []
            for head in range(heads):
                at = head * HEAD_DIM
                q = qkv_ref[here, at : at + HEAD_DIM]
                k = qkv_ref[:, share + at : share + at + HEAD_DIM]
                v = qkv_ref[:, 2 * share + at : 2 * share + at + HEAD_DIM]
                scores = dot(k, q, nt)
                top = jnp.max(scores, axis=0, keepdims=True)
                expo = jnp.exp2((scores - top) * curve)
                total = jnp.sum(expo, axis=0, keepdims=True)
                log_ref[head : head + 1, here] = top * curve + jnp.log2(total)
                parts.append((dot(v, expo.astype(low), tn) * (1.0 / total)).T)
            out_ref[here, :] = jnp.concatenate(parts, axis=1).astype(low)

    return pl.pallas_call(
        body,
        out_shape=[
            jax.ShapeDtypeStruct((length, share), low),
            jax.ShapeDtypeStruct((heads, length), jnp.float32),
        ],
        compiler_params=pltpu.CompilerParams(vmem_limit_bytes=40 * 2**20),
        cost_estimate=cheap,
        name="self_attend",
    )(qkv)


def self_attend_back(qkv, grads, mixed, logs, share, begin, end):
    length = qkv.shape[0]
    rows = length // len(grads)
    span = end - begin
    scale = HEAD_DIM ** (-0.5)
    curve = scale * math.log2(math.e)

    def body(qkv_ref, mixed_ref, log_ref, *refs):
        grad_refs, (out_ref, grad_k, grad_v) = refs[: len(grads)], refs[len(grads) :]
        for step, grad_ref in enumerate(grad_refs):
            here = slice(step * rows, (step + 1) * rows)
            parts = []
            for head, at in enumerate(range(begin, end, HEAD_DIM)):
                q = qkv_ref[here, at : at + HEAD_DIM]
                k = qkv_ref[:, share + at : share + at + HEAD_DIM]
                v = qkv_ref[:, 2 * share + at : 2 * share + at + HEAD_DIM]
                g = grad_ref[0:rows, at : at + HEAD_DIM]
                o = mixed_ref[here, at : at + HEAD_DIM]
                inner = g.astype(jnp.float32) * o.astype(jnp.float32)
                inner = jnp.sum(inner.T, axis=0, keepdims=True)
                which = begin // HEAD_DIM + head
                probs = jnp.exp2(dot(k, q, nt) * curve - log_ref[which : which + 1, here])
                grad_scores = (probs * (dot(v, g, nt) - inner)).astype(low)
                to_v = dot(probs.astype(low), g)
                to_k = dot(grad_scores, q)
                if step:
                    grad_v[head] += to_v
                    grad_k[head] += to_k
                else:
                    grad_v[head] = to_v
                    grad_k[head] = to_k
                parts.append((dot(k, grad_scores, tn) * scale).T)
            out_ref[here, 0:span] = jnp.concatenate(parts, axis=1).astype(low)
        heads = range(span // HEAD_DIM)
        both = [grad_k[head] * scale for head in heads]
        out_ref[:, span : 2 * span] = jnp.concatenate(both, axis=1).astype(low)
        both = [grad_v[head] for head in heads]
        out_ref[:, 2 * span :] = jnp.concatenate(both, axis=1).astype(low)

    return pl.pallas_call(
        body,
        out_shape=jax.ShapeDtypeStruct((length, 3 * span), low),
        scratch_shapes=[pltpu.VMEM((span // HEAD_DIM, length, HEAD_DIM), jnp.float32)] * 2,
        compiler_params=pltpu.CompilerParams(vmem_limit_bytes=40 * 2**20),
        cost_estimate=cheap,
        name="self_attend_back",
    )(qkv, mixed, logs, *grads)


def mlp_core(rows_in, grads_in, w_mlp, after):
    groups = len(rows_in)
    tokens, width = rows_in[0].shape
    hidden = w_mlp.shape[0] // 2
    chunk = 384 if hidden % 384 == 0 else hidden
    steps = hidden // chunk
    curve = 0.7978845608028654

    def body(*refs):
        rows, grads = refs[:groups], refs[groups : 2 * groups]
        up, down = refs[2 * groups : 2 * groups + 2]
        act, grad_pre, *outs = refs[2 * groups + 2 + len(after) : -1]
        total = refs[-1]
        step = pl.program_id(0)
        for i in range(groups):
            pre = lax.dot_general(
                rows[i][...], up[...], (((1,), (1,)), ((), ())), preferred_element_type=jnp.float32
            )
            square = pre * pre
            bend = jnp.tanh(curve * pre * (1.0 + 0.044715 * square))
            half = 0.5 * (1.0 + bend)
            here = pl.ds(i * tokens, tokens)
            act[here, :] = (pre * half).astype(low)
            slope = half + (0.5 * curve) * pre * (1.0 - bend * bend) * (1.0 + 0.134145 * square)
            grad_act = lax.dot_general(
                grads[i][...], down[...], (((1,), (1,)), ((), ())), preferred_element_type=jnp.float32
            )
            grad_low = (grad_act * slope).astype(low)
            grad_pre[here, :] = grad_low
            term = jnp.dot(grad_low, up[...], preferred_element_type=jnp.float32)

            @pl.when(step == 0)
            def _():
                total[here, :] = term

            @pl.when(step > 0)
            def _():
                total[here, :] += term

            @pl.when(step == steps - 1)
            def _():
                outs[i][...] = total[here, :].astype(low)

    whole = pl.BlockSpec((tokens, width), lambda s: (0, 0))
    across = pl.BlockSpec((groups * tokens, chunk), lambda s: (0, s))
    return pl.pallas_call(
        body,
        grid=(steps,),
        in_specs=[whole] * (2 * groups)
        + [
            pl.BlockSpec((chunk, width), lambda s: (s, 0)),
            pl.BlockSpec((chunk, width), lambda s: (steps + s, 0)),
        ]
        + [pl.BlockSpec(memory_space=pl.ANY)] * len(after),
        out_specs=[across, across] + [whole] * groups,
        out_shape=[jax.ShapeDtypeStruct((groups * tokens, hidden), low)] * 2
        + [jax.ShapeDtypeStruct((tokens, width), low)] * groups,
        scratch_shapes=[pltpu.VMEM((groups * tokens, width), jnp.float32)],
        compiler_params=pltpu.CompilerParams(vmem_limit_bytes=60 * 2**20),
        cost_estimate=cheap,
        name="mlp_core",
    )(*rows_in, *grads_in, w_mlp, w_mlp, *after)


nt = (((1,), (1,)), ((), ()))
tn = (((0,), (0,)), ((), ()))


def dot(left, right, dims=(((1,), (0,)), ((), ()))):
    return lax.dot_general(left, right, dims, preferred_element_type=jnp.float32)


def softmax_keys(keys, queries):
    scores = dot(keys, queries, nt) * HEAD_DIM ** (-0.5)
    expo = jnp.exp(scores - jnp.max(scores, axis=0, keepdims=True))
    return expo * (1.0 / jnp.sum(expo, axis=0, keepdims=True))


def cuts_of(width):
    size = 384 if width % 384 == 0 else width
    return [slice(i, i + size) for i in range(0, width, size)]


def in_smem():
    return pl.BlockSpec(memory_space=pltpu.SMEM)


def in_vmem():
    return pl.BlockSpec(memory_space=pltpu.VMEM)


def line_slots(place, own, ups, downs, rows):
    count = len(ups) + 1
    tokens, width = own.shape

    def body(place_ref, *refs):
        own_ref, up_refs, down_refs = refs[0], refs[1:count], refs[count : 2 * count - 1]
        rows_ref, outs, out = refs[2 * count - 1], refs[2 * count : -1], refs[-1]
        me = place_ref[0]

        def modulate(slot, ref):
            value = ref[...].astype(jnp.float32)
            value = value * (1.0 + rows_ref[1:2, :]) + rows_ref[0:1, :]
            out[slot * tokens : (slot + 1) * tokens, :] = value.astype(low)

        modulate(0, own_ref)
        for k in range(1, count):
            for side, ref in ((me >= k, up_refs[k - 1]), (me < k, down_refs[count - k - 1])):

                @pl.when(side)
                def _():
                    outs[k - 1][...] = ref[...]
                    modulate(k, ref)

    shapes = [(tokens, width)] * (count - 1) + [(count * tokens, width)]
    return pl.pallas_call(
        body,
        in_specs=[in_smem()] + [in_vmem()] * (2 * count),
        out_shape=[jax.ShapeDtypeStruct(shape, low) for shape in shapes],
        compiler_params=pltpu.CompilerParams(vmem_limit_bytes=32 * 2**20),
        cost_estimate=cheap,
        name="line_slots",
    )(place, own, *ups, *downs, rows)


def cross_block(place, mixed, hidden, rows, text, w_out, c_query, c_value, c_out):
    count, share = len(mixed), mixed[0].shape[1]
    tokens, width = hidden.shape
    words = text.shape[0]
    per = share // HEAD_DIM

    def body(place_ref, *refs):
        parts = refs[:count]
        x_ref, rows_ref, text_ref = refs[count : count + 3]
        far = refs[count + 3 : count + 7]
        outs = refs[count + 7 : count + 16]
        inverse = refs[count + 16]
        wo, wq, wv, wc, *own = refs[count + 17 : -3]
        held, read, sems = refs[-3:]
        branch, res_low, cq, ck, cv, crossed, res, normed, out = own
        me = place_ref[0]
        loads = [
            pltpu.make_async_copy(source, target, read.at[i])
            for i, (source, target) in enumerate(zip(far, (wo, wq, wv, wc)))
        ]
        stores = [
            pltpu.make_async_copy(source, target, sems.at[i])
            for i, (source, target) in enumerate(zip(own, outs))
        ]
        for load in loads:
            load.start()
        loads[0].wait()
        for cut in cuts_of(width):
            total = jnp.zeros((tokens, cut.stop - cut.start), jnp.float32)
            for k in range(count):
                rank = lax.rem(me + k, count)
                here = pl.ds(pl.multiple_of(rank * share, 32), share)
                total += dot(parts[k][0:tokens, :], wo[here, cut])
            branch[:, cut] = total
            first = x_ref[:, cut].astype(jnp.float32) + rows_ref[0:1, cut] * total
            res[:, cut] = first
            res_low[:, cut] = first.astype(low)
        stores[0].start()
        stores[1].start()
        loads[1].wait()
        loads[2].wait()
        for cut in cuts_of(width):
            cq[:, cut] = dot(res_low[...], wq[cut, :], nt).astype(low)
            cv[:, cut] = dot(text_ref[...], wv[cut, :], nt).astype(low)
        for k in range(count):
            held[lax.rem(me + k, count)] = parts[k][tokens:, :]
        ck[...] = jnp.concatenate([held[rank] for rank in range(count)], axis=1)
        for i in (2, 3, 4):
            stores[i].start()
        parts_out = []
        for at in range(0, width, HEAD_DIM):
            head = slice(at, at + HEAD_DIM)
            probs = softmax_keys(ck[:, head], cq[:, head]).astype(low)
            parts_out.append(dot(cv[:, head], probs, tn).T)
        crossed[...] = jnp.concatenate(parts_out, axis=1).astype(low)
        stores[5].start()
        loads[3].wait()
        for cut in cuts_of(width):
            res[:, cut] += dot(crossed[...], wc[:, cut])
        second = res[...]
        center = second - jnp.mean(second, axis=-1, keepdims=True)
        spread = lax.rsqrt(jnp.mean(center * center, axis=-1, keepdims=True) + norm_eps)
        inverse[...] = spread
        scaled = center * spread
        normed[...] = scaled
        stores[6].start()
        stores[7].start()
        out[...] = (scaled * (1.0 + rows_ref[2:3, :]) + rows_ref[1:2, :]).astype(low)
        stores[8].start()
        for store in stores:
            store.wait()

    wide = (tokens, width)
    shapes = [
        (wide, jnp.float32),
        (wide, low),
        (wide, low),
        ((words, width), low),
        ((words, width), low),
        (wide, low),
        (wide, jnp.float32),
        (wide, jnp.float32),
        (wide, low),
    ]
    anywhere = pl.BlockSpec(memory_space=pl.ANY)
    return pl.pallas_call(
        body,
        in_specs=[in_smem()] + [in_vmem()] * (count + 3) + [anywhere] * 4,
        out_specs=[anywhere] * len(shapes) + [in_vmem()],
        out_shape=[jax.ShapeDtypeStruct(*item) for item in shapes]
        + [jax.ShapeDtypeStruct((tokens, 1), jnp.float32)],
        scratch_shapes=[pltpu.VMEM((width, width), low)] * 4
        + [pltpu.VMEM(*item) for item in shapes]
        + [
            pltpu.VMEM((count, words, share), low),
            pltpu.SemaphoreType.DMA((4,)),
            pltpu.SemaphoreType.DMA((len(shapes),)),
        ],
        compiler_params=pltpu.CompilerParams(vmem_limit_bytes=60 * 2**20),
        cost_estimate=cheap,
        name="cross_block",
    )(place, *mixed, hidden, rows, text, w_out, c_query, c_value, c_out)


def cross_back(
    place, terms, grad, rows, normed, inverse, branch, cq, ck, cv, c_out, c_query, w_out, after
):
    count = len(terms)
    tokens, width = grad.shape
    words = ck.shape[0]
    share = width // count
    scale = HEAD_DIM ** (-0.5)

    def body(place_ref, *refs):
        parts = refs[:count]
        grad_ref, rows_ref, i_ref, k_ref, v_ref = refs[count : count + 5]
        far = refs[count + 5 : count + 11]
        refs = refs[: count + 11] + refs[count + 11 + len(after) :]
        stored = refs[count + 11 : count + 15]
        grad_v, sums = refs[count + 15 : count + 17]
        outs = refs[count + 17 : 2 * count + 17]
        near = refs[2 * count + 17 : 2 * count + 23]
        n_ref, wc, q_ref, wq, wo, b_ref = near
        own = refs[2 * count + 23 : 2 * count + 27]
        first, cross_low, grad_q, attn_low = own
        back, held, read, sems = refs[2 * count + 27 :]
        me = place_ref[0]
        loads = [
            pltpu.make_async_copy(source, target, read.at[i])
            for i, (source, target) in enumerate(zip(far, near))
        ]
        stores = [
            pltpu.make_async_copy(source, target, sems.at[i])
            for i, (source, target) in enumerate(zip(own, stored))
        ]
        for load in loads:
            load.start()
        loads[0].wait()
        total = parts[0][...].astype(jnp.float32)
        for part in parts[1:]:
            total += part[...].astype(jnp.float32)
        n = n_ref[...]
        sums[1:2, :] = jnp.sum(total, axis=0, keepdims=True)
        sums[2:3, :] = jnp.sum(total * n, axis=0, keepdims=True)
        second = grad_ref[...].astype(jnp.float32) + norm_back(total, n, i_ref[...], rows_ref[2:3, :])
        first[...] = second
        cross_low[...] = second.astype(low)
        stores[1].start()
        loads[1].wait()
        loads[2].wait()
        for cut in cuts_of(width):
            back[:, cut] = dot(cross_low[...], wc[cut, :], nt).astype(low)
        grads = ([], [], [])
        for at in range(0, width, HEAD_DIM):
            head = slice(at, at + HEAD_DIM)
            q, k, v, g = q_ref[:, head], k_ref[:, head], v_ref[:, head], back[:, head]
            probs = softmax_keys(k, q)
            grad_probs = dot(v, g, nt)
            inner = jnp.sum(probs * grad_probs, axis=0, keepdims=True)
            grad_scores = (probs * (grad_probs - inner)).astype(low)
            grads[0].append((dot(k, grad_scores, tn) * scale).T)
            grads[1].append(dot(grad_scores, q) * scale)
            grads[2].append(dot(probs.astype(low), g))
        grad_q[...] = jnp.concatenate(grads[0], axis=1).astype(low)
        grad_v[...] = jnp.concatenate(grads[2], axis=1).astype(low)
        heads = share // HEAD_DIM
        for rank in range(count):
            pieces = grads[1][rank * heads : (rank + 1) * heads]
            held[rank] = jnp.concatenate(pieces, axis=1).astype(low)
        stores[2].start()
        for load in loads[3:]:
            load.wait()
        for cut in cuts_of(width):
            whole = first[:, cut] + dot(grad_q[...], wq[:, cut])
            first[:, cut] = whole
            attn_low[:, cut] = (rows_ref[0:1, cut] * whole).astype(low)
            sums[0:1, cut] = jnp.sum(b_ref[:, cut] * whole, axis=0, keepdims=True)
        stores[0].start()
        stores[3].start()
        for k in range(count):
            rank = lax.rem(me + k, count)
            here = pl.ds(pl.multiple_of(rank * share, 32), share)
            outs[k][0:tokens, :] = dot(attn_low[...], wo[here, :], nt).astype(low)
            outs[k][tokens:, :] = held[rank]
        for store in stores:
            store.wait()

    wide, square = (tokens, width), (width, width)
    shapes = [
        (wide, jnp.float32),
        (wide, low),
        (wide, low),
        (wide, low),
        ((words, width), low),
        ((3, width), jnp.float32),
    ] + [((tokens + words, share), low)] * count
    anywhere = pl.BlockSpec(memory_space=pl.ANY)
    loaded = [
        pltpu.VMEM(wide, jnp.float32),
        pltpu.VMEM(square, low),
        pltpu.VMEM(wide, low),
        pltpu.VMEM(square, low),
        pltpu.VMEM(square, low),
        pltpu.VMEM(wide, jnp.float32),
    ]
    return pl.pallas_call(
        body,
        in_specs=[in_smem()] + [in_vmem()] * (count + 5) + [anywhere] * (6 + len(after)),
        out_specs=[anywhere] * 4 + [in_vmem()] * (2 + count),
        out_shape=[jax.ShapeDtypeStruct(*item) for item in shapes],
        scratch_shapes=loaded
        + [pltpu.VMEM(*item) for item in shapes[:4]]
        + [
            pltpu.VMEM(wide, low),
            pltpu.VMEM((count, words, share), low),
            pltpu.SemaphoreType.DMA((6,)),
            pltpu.SemaphoreType.DMA((4,)),
        ],
        compiler_params=pltpu.CompilerParams(vmem_limit_bytes=60 * 2**20),
        cost_estimate=cheap,
        name="cross_back",
    )(
        place,
        *terms,
        grad,
        rows,
        inverse,
        ck,
        cv,
        normed,
        c_out,
        cq,
        c_query,
        w_out,
        branch,
        *after,
    )


def outer_halves(place, pairs, parts, name):
    width = pairs[0][1].shape[1]
    high = [sum(piece[2] for piece in left) for left, _ in pairs]
    size = high[0] // parts
    tokens = [right.shape[0] for _, right in pairs]
    flat = []

    def index_of(array):
        for i, other in enumerate(flat):
            if other is array:
                return i
        flat.append(array)
        return len(flat) - 1

    plans = [
        ([(index_of(array), *rest) for array, *rest in left], index_of(right))
        for left, right in pairs
    ]
    amount = len(pairs)

    def body(place_ref, *refs):
        ins, (kept, given), (held, sems) = refs[: len(flat)], refs[len(flat) :][:2], refs[-2:]
        turned = refs[len(flat) + 2 : -2]
        me, core = place_ref[0], place_ref[1]
        for i, (left, right) in enumerate(plans):
            for k, (which, lane, lanes, row) in enumerate(left):
                piece = ins[which][0 : tokens[i], lane : lane + lanes]
                piece = piece.astype(jnp.float32).T.astype(low)
                if row is None:
                    rank = lax.rem(me + k, len(left))
                    turned[i][pl.ds(pl.multiple_of(rank * lanes, 32), lanes), :] = piece
                else:
                    turned[i][row : row + lanes, :] = piece
            for part in range(parts):
                at = i * parts + part
                tile = dot(turned[i][part * size : (part + 1) * size, :], ins[right][...])
                held[at] = tile.astype(low)
                for out, side in ((kept, 0), (given, 1)):

                    @pl.when((core ^ (i & 1)) == side)
                    def _():
                        pltpu.make_async_copy(
                            held.at[at], out.at[i // 2, part], sems.at[at]
                        ).start()

        for at in range(amount * parts):
            pltpu.make_async_copy(held.at[at], kept.at[0, 0], sems.at[at]).wait()

    out = jax.ShapeDtypeStruct((amount // 2, parts, size, width), low)
    return pl.pallas_call(
        body,
        in_specs=[in_smem()] + [in_vmem()] * len(flat),
        out_specs=[pl.BlockSpec(memory_space=pl.ANY)] * 2,
        out_shape=[out, out],
        scratch_shapes=[pltpu.VMEM((high[i], tokens[i]), low) for i in range(amount)]
        + [
            pltpu.VMEM((amount * parts, size, width), low),
            pltpu.SemaphoreType.DMA((amount * parts,)),
        ],
        compiler_params=pltpu.CompilerParams(vmem_limit_bytes=60 * 2**20),
        cost_estimate=cheap if parts > 1 else costly,
        name=name,
    )(place, *flat)


def mlp_grads(grad_pres, acts, rows_in, grads_in):
    pieces, rights = len(acts), len(rows_in)
    tokens, width = rows_in[0].shape
    hidden = acts[0].shape[1]
    chunk = 384 if hidden % 384 == 0 else hidden
    steps = hidden // chunk

    def body(*refs):
        step = pl.program_id(0)
        lefts_up, lefts_down = refs[:pieces], refs[pieces : 2 * pieces]
        rights_up = refs[2 * pieces : 2 * pieces + rights]
        rights_down = refs[2 * pieces + rights : -1]
        out = refs[-1]

        def terms(lefts, turn, others):
            here = pl.ds(pl.multiple_of(turn * chunk, chunk), chunk)
            total = jnp.zeros((chunk, width), jnp.float32)
            cursor = 0
            for left in lefts:
                for i in range(left.shape[0] // tokens):
                    total += dot(left[i * tokens : (i + 1) * tokens, here], others[cursor][...], tn)
                    cursor += 1
            out[...] = total.astype(low)

        @pl.when(step < steps)
        def _():
            terms(lefts_up, step, rights_up)

        @pl.when(step >= steps)
        def _():
            terms(lefts_down, step - steps, rights_down)

    arrays = (*grad_pres, *acts, *rows_in, *grads_in)
    chunked = pl.BlockSpec((chunk, width), lambda s: (s, 0))
    return pl.pallas_call(
        body,
        grid=(2 * steps,),
        in_specs=[pl.BlockSpec(array.shape, lambda s: (0, 0)) for array in arrays],
        out_specs=chunked,
        out_shape=jax.ShapeDtypeStruct((2 * hidden, width), low),
        compiler_params=pltpu.CompilerParams(vmem_limit_bytes=60 * 2**20),
        cost_estimate=cheap,
        name="mlp_grads",
    )(*arrays)


def ranked_terms(place, lefts, order, pieces, weight, factors, name):
    tokens, width = factors[0].shape
    count = len(factors)

    def body(place_ref, *refs):
        ins, weight_ref = refs[: len(lefts)], refs[len(lefts)]
        others = refs[len(lefts) + 1 : len(lefts) + 1 + count]
        out, sums = refs[-2:]
        me = place_ref[0]
        for i, slot in enumerate(order):
            rank = lax.rem(me - slot + count, count)
            for cut in cuts_of(width):
                term = jnp.zeros((tokens, cut.stop - cut.start), jnp.float32)
                for which, row, lane, start, depth in pieces[i]:
                    term += dot(
                        ins[which][row : row + tokens, lane : lane + depth],
                        weight_ref[start : start + depth, cut],
                    )
                out[rank, :, cut] = term.astype(low)
                one = jnp.sum(term, axis=0, keepdims=True)
                two = jnp.sum(term * others[i][:, cut].astype(jnp.float32), axis=0, keepdims=True)
                if i:
                    one, two = one + sums[0:1, cut], two + sums[1:2, cut]
                sums[0:1, cut], sums[1:2, cut] = one, two

    return pl.pallas_call(
        body,
        in_specs=[in_smem()] + [in_vmem()] * (len(lefts) + 1 + count),
        out_shape=[
            jax.ShapeDtypeStruct((count, tokens, width), low),
            jax.ShapeDtypeStruct((2, width), jnp.float32),
        ],
        compiler_params=pltpu.CompilerParams(vmem_limit_bytes=60 * 2**20),
        cost_estimate=cheap if len(lefts) > 2 else costly,
        name=name,
    )(place, *lefts, weight, *factors)


def sum_split(place, kept, got):
    count, unit_rows, width = kept.shape[1], kept.shape[4], kept.shape[5]

    def body(place_ref, one, two, keep_x, give_x, keep_y, give_y):
        x, y = place_ref[0], place_ref[1]

        def total(*index):
            return (one[index].astype(jnp.float32) + two[index].astype(jnp.float32)).astype(low)

        for j in range(2):
            keep_x[0, j] = total(0, 0, j, x)
            give_x[0, j] = total(0, 0, j, 1 - x)
            keep_y[0, j] = total(1, 0, y, j)
            give_y[0, j] = total(1, 0, 1 - y, j)

    block = pl.BlockSpec((2, 1, 2, 2, unit_rows, width), lambda r, *_: (0, r, 0, 0, 0, 0))
    part = pl.BlockSpec((1, 2, unit_rows, width), lambda r, *_: (r, 0, 0, 0))
    return pl.pallas_call(
        body,
        grid_spec=pltpu.PrefetchScalarGridSpec(
            num_scalar_prefetch=1, grid=(count,), in_specs=[block] * 2, out_specs=[part] * 4
        ),
        out_shape=[jax.ShapeDtypeStruct((count, 2, unit_rows, width), low)] * 4,
        compiler_params=pltpu.CompilerParams(vmem_limit_bytes=60 * 2**20),
        cost_estimate=cheap,
        name="sum_split",
    )(place, kept, got)


def update_slots(master, first_moment, second_moment, filled, which, position, sources):
    capacity, unit_rows, width = master.shape

    group = math.gcd(capacity, 2)
    steps = capacity // group

    def body(filled_ref, which_ref, position_ref, weight, one, two, *rest):
        ins = rest[: len(sources)]
        new_one, new_two, new_weight, held, sems = rest[len(sources) :]
        step = pl.program_id(0)

        def fetch(turn):
            for i in range(group):
                slot = turn * group + i
                for source, ref in enumerate(ins):

                    @pl.when(which_ref[slot] == source)
                    def _():
                        pltpu.make_async_copy(
                            ref.at[position_ref[slot]], held.at[turn % 2, i], sems.at[turn % 2, i]
                        ).start()

        @pl.when(step == 0)
        def _():
            fetch(step)

        @pl.when(step < steps - 1)
        def _():
            fetch(step + 1)

        for i in range(group):
            pltpu.make_async_copy(
                ins[0].at[0], held.at[step % 2, i], sems.at[step % 2, i]
            ).wait()
            mask = (filled_ref[step * group + i] > 0).astype(jnp.float32)
            grad = held[step % 2, i].astype(jnp.float32)
            results = adamw(weight[i], one[i], two[i], grad, mask, rate)
            new_one[i], new_two[i], new_weight[i] = results

    block = pl.BlockSpec((group, unit_rows, width), lambda s, *_: (s, 0, 0))
    return pl.pallas_call(
        body,
        grid_spec=pltpu.PrefetchScalarGridSpec(
            num_scalar_prefetch=3,
            grid=(steps,),
            in_specs=[block] * 3 + [pl.BlockSpec(memory_space=pl.ANY)] * len(sources),
            out_specs=[block] * 3,
            scratch_shapes=[
                pltpu.VMEM((2, group, unit_rows, width), low),
                pltpu.SemaphoreType.DMA((2, group)),
            ],
        ),
        out_shape=[jax.ShapeDtypeStruct(master.shape, jnp.float32)] * 3,
        compiler_params=pltpu.CompilerParams(vmem_limit_bytes=56 * 2**20),
        cost_estimate=cheap,
        name="update_slots",
    )(filled, which, position, master, first_moment, second_moment, *sources)


def adamw(weight, moment_one, moment_two, gradient, filled, step_rate):
    new_one = beta_one * moment_one + (1.0 - beta_one) * gradient
    new_two = beta_two * moment_two + (1.0 - beta_two) * gradient * gradient
    fixed_one = new_one / (1.0 - beta_one**STEP)
    fixed_two = new_two / (1.0 - beta_two**STEP)
    updated = weight - step_rate * (fixed_one / (jnp.sqrt(fixed_two) + adam_eps) + decay * weight)
    return (new_one * filled, new_two * filled, updated * filled)


def swap(values, axis, bit):
    count = lax.axis_size(axis)
    return lax.ppermute(values, axis, [(i, i ^ (1 << bit)) for i in range(count)])


def choose(values, index, axis):
    return lax.dynamic_index_in_dim(values, index, axis, keepdims=False)


def total_sum(values):
    for axis in ("dp", "tensor"):
        for bit in range(lax.axis_size(axis).bit_length() - 1):
            values = values + swap(values, axis, bit)
    return values


def pick_units(master, slot_unit, state, kind, place, sizes, after=()):
    capacity, unit_rows, width = master.shape
    units = state.shape[0]

    def body(slot_ref, state_ref, kind_ref, place_ref, blocks, *rest):
        outs = rest[len(after) : len(after) + len(sizes)]
        highs, lows, zeros, read, sems = rest[len(after) + len(sizes) :]

        def start(source, unit):
            for which, out in enumerate(outs):

                @pl.when(kind_ref[unit] == which)
                def _():
                    pltpu.make_async_copy(source, out.at[place_ref[unit]], sems.at[unit]).start()

        @pl.loop(0, capacity)
        def _(slot):
            @pl.when(slot_ref[slot] >= 0)
            def _():
                pltpu.make_async_copy(blocks.at[slot], highs.at[slot], read.at[slot]).start()

        zeros[...] = jnp.zeros_like(zeros)

        @pl.loop(0, units)
        def _(unit):
            @pl.when(state_ref[unit] == 0)
            def _():
                start(zeros, unit)

        @pl.loop(0, capacity)
        def _(slot):
            @pl.when(slot_ref[slot] >= 0)
            def _():
                pltpu.make_async_copy(blocks.at[slot], highs.at[slot], read.at[slot]).wait()
                lows[slot] = highs[slot].astype(low)
                start(lows.at[slot], slot_ref[slot])

        @pl.loop(0, units)
        def _(unit):
            @pl.when(state_ref[unit] < 2)
            def _():
                pltpu.make_async_copy(zeros, outs[0].at[0], sems.at[unit]).wait()

    return pl.pallas_call(
        body,
        grid_spec=pltpu.PrefetchScalarGridSpec(
            num_scalar_prefetch=4,
            grid=(1,),
            in_specs=[pl.BlockSpec(memory_space=pl.ANY)] * (1 + len(after)),
            out_specs=[pl.BlockSpec(memory_space=pl.ANY)] * len(sizes),
            scratch_shapes=[
                pltpu.VMEM((capacity, unit_rows, width), jnp.float32),
                pltpu.VMEM((capacity, unit_rows, width), low),
                pltpu.VMEM((unit_rows, width), low),
                pltpu.SemaphoreType.DMA((capacity,)),
                pltpu.SemaphoreType.DMA((units,)),
            ],
        ),
        out_shape=[jax.ShapeDtypeStruct((size, unit_rows, width), low) for size in sizes],
        compiler_params=pltpu.CompilerParams(vmem_limit_bytes=56 * 2**20),
        cost_estimate=cheap,
        name="pick_units",
    )(slot_unit, state, kind, place, master, *after)


def place_blocks(sources, which, position, parts=1):
    amount = which.shape[0]
    shape = sources[0].shape[1:]
    size = amount // parts

    def body(which_ref, position_ref, *rest):
        ins, outs = rest[: len(sources)], rest[len(sources) : len(sources) + parts]
        held, read, sems = rest[len(sources) + parts :]

        @pl.loop(0, amount)
        def _(i):
            for source, ref in enumerate(ins):

                @pl.when(which_ref[i] == source)
                def _():
                    pltpu.make_async_copy(ref.at[position_ref[i]], held.at[i], read.at[i]).start()

        for part, out in enumerate(outs):

            @pl.loop(0, size)
            def _(j):
                i = part * size + j
                pltpu.make_async_copy(ins[0].at[0], held.at[i], read.at[i]).wait()
                pltpu.make_async_copy(held.at[i], out.at[j], sems.at[i]).start()

        @pl.loop(0, amount)
        def _(i):
            pltpu.make_async_copy(held.at[i], outs[0].at[0], sems.at[i]).wait()

    return pl.pallas_call(
        body,
        grid_spec=pltpu.PrefetchScalarGridSpec(
            num_scalar_prefetch=2,
            grid=(1,),
            in_specs=[pl.BlockSpec(memory_space=pl.ANY)] * len(sources),
            out_specs=[pl.BlockSpec(memory_space=pl.ANY)] * parts,
            scratch_shapes=[
                pltpu.VMEM((amount,) + shape, low),
                pltpu.SemaphoreType.DMA((amount,)),
                pltpu.SemaphoreType.DMA((amount,)),
            ],
        ),
        out_shape=[jax.ShapeDtypeStruct((size,) + shape, low)] * parts,
        compiler_params=pltpu.CompilerParams(vmem_limit_bytes=56 * 2**20),
        cost_estimate=cheap,
        name="place_blocks",
    )(which, position, *sources)


def stack_pairs(pairs):
    shape = (len(pairs),) + pairs[0].shape[1:]

    def body(*refs):
        for i, pair in enumerate(refs[:-2]):
            for half in range(2):
                refs[half - 2][i] = pair[half]

    return pl.pallas_call(
        body,
        out_shape=[jax.ShapeDtypeStruct(shape, low)] * 2,
        cost_estimate=costly,
        name="stack_pairs",
    )(*pairs)


def hops(values, step, turn):
    count = lax.axis_size("tensor")
    if step > 0:
        pairs = [(i, i + 1) for i in range(turn - 1, count - 1)]
    else:
        pairs = [(i, i - 1) for i in range(1, count - turn + 1)]
    return lax.ppermute(values, "tensor", pairs)


fence = lax.optimization_barrier


def in_pool(member, inner, inner_count):
    me = lax.axis_index("dp")
    half, core = member >> 3, ((member >> 2) & 1) ^ (me & 1)
    far_y, far_x = ((member >> 1) & 1) ^ ((me >> 2) & 1), (member & 1) ^ ((me >> 1) & 1)
    where_first = (far_y * 2 + far_x) * inner_count
    where_second = (4 + far_x * 2 + far_y) * inner_count
    return (core, jnp.where(half == 0, where_first, where_second) + inner)


def on_device(
    hidden_in,
    time_embed,
    caption_table,
    caption_ids,
    owners,
    master,
    first_moment,
    second_moment,
    mod_table,
    mod_first,
    mod_second,
    out_grad,
):
    count = lax.axis_size("tensor")
    dp_count = lax.axis_size("dp")
    me_dp = lax.axis_index("dp")
    me_tensor = lax.axis_index("tensor")
    capacity, unit_rows, width = master.shape
    units = owners.shape[0]
    tokens = hidden_in.shape[1]
    text_count = caption_ids.shape[1]
    share = width // count
    per = share // unit_rows
    ups = (units - 8 * per) // 2
    rank_of = ranks_of(owners)
    mine = owners == me_dp
    match = (rank_of[None, :] == jnp.arange(capacity)[:, None]) & mine[None, :]
    filled = jnp.any(match, axis=1)
    unit_of_slot = jnp.sum(jnp.where(match, jnp.arange(units)[None, :], 0), axis=1)

    square = [list(range(i * per, (i + 1) * per)) for i in range(8)]
    group_attn = square[0] + square[1] + square[2] + square[5]
    group_full = square[3] + square[4] + square[6] + square[7]
    group_mlp = list(range(8 * per, units))
    members = len(group_attn)
    plane = dp_count == 8 and members == 16 and len(group_mlp) % dp_count == 0
    member_of = np.zeros(units, np.int32)
    member_of[group_attn] = np.arange(members)
    member_of[group_full] = np.arange(members)
    is_attn = np.zeros(units, bool)
    is_attn[group_attn] = True
    is_mlp = np.zeros(units, bool)
    is_mlp[group_mlp] = True

    latent_in = hidden_in[0].astype(jnp.float32)
    modulate = mod_table + time_embed[0]

    def mod_row(which_row):
        return modulate[which_row][None, :]

    normed_one, inverse_one = layer_norm(latent_in)
    bits = dp_count.bit_length() - 1
    vocab_rows = caption_table.shape[0]

    def caption_terms(ids):
        chosen = ids.reshape(-1) - me_dp * vocab_rows
        onehot = (chosen[:, None] == jnp.arange(vocab_rows)[None, :]).astype(low)
        terms = jnp.dot(onehot, caption_table, preferred_element_type=jnp.float32).astype(low)
        return terms.reshape(dp_count, text_count, -1)

    def modulated(normed):
        return (normed.astype(jnp.float32) * (1.0 + mod_row(1)) + mod_row(0)).astype(low)

    def whole_text(text_ring):
        return from_ring(text_ring, -1).transpose(1, 0, 2).reshape(text_count, width)

    def own_keys(text_low, w_attn):
        return project(text_low, w_attn)[:, 3 * share :].astype(low)

    def exchanged(attended, keys):
        parts = [
            jnp.concatenate([attended[k * tokens : (k + 1) * tokens], keys]) for k in range(count)
        ]
        return [parts[0]] + [shift(parts[k], count - k) for k in range(1, count)]

    where = jnp.stack([me_tensor, me_dp & 1]).astype(jnp.int32)

    n_low = normed_one.astype(low)
    if plane:
        core, far_x, far_y = (
            ((member_of >> 2) & 1) ^ (me_dp & 1),
            (member_of & 1) ^ ((me_dp >> 1) & 1),
            ((member_of >> 1) & 1) ^ ((me_dp >> 2) & 1),
        )
        place = jnp.where(is_attn, far_x * 4 + far_y * 2, 8 + far_y * 4 + far_x * 2)
        place = jnp.where(is_mlp, np.arange(units) - 8 * per, place + (member_of >> 3))
        kind = jnp.where(is_mlp, 0, core)
        slot_mlp = unit_of_slot >= 8 * per
        owned_state = mine.astype(jnp.int32)
        ids = lax.all_gather(caption_ids, "dp", axis=0, tiled=True)
        ids = jnp.take(ids, me_dp ^ jnp.arange(dp_count), axis=0, mode="clip")
        up, down = hops(n_low, 1, 1), hops(n_low, -1, 1)
        kept, given = pick_units(
            master,
            jnp.where(filled & ~slot_mlp, unit_of_slot, -1),
            jnp.where(is_mlp, 2, owned_state),
            kind,
            place,
            (members, members),
        )
        got = swap(given, "dp", 0)
        (mlp_part,) = pick_units(
            master,
            jnp.where(filled & slot_mlp, unit_of_slot, -1),
            jnp.where(is_mlp, owned_state, 2),
            kind,
            place,
            (len(group_mlp),),
            (kept,),
        )
        mlp_part = lax.psum_scatter(mlp_part, "dp", scatter_dimension=0, tiled=True)
        n_up, n_down = [up], [down]
        kept, got, up, down, ids = fence((kept, got, up, down, ids))
        pieces = [kept[i : i + 4] + got[i : i + 4] for i in range(0, members, 4)]
        attn_two, attn_send, full_two, full_send = fence(tuple(pieces))
        up, down = hops(up, 1, 2), hops(down, -1, 2)
        attn_got = swap(attn_send, "dp", 1)
        full_got = swap(full_send, "dp", 2)
        text = caption_terms(ids)
        text = text[0:4] + swap(text[4:8], "dp", 2)
        n_up.append(up), n_down.append(down)
        attn_two, attn_got, full_two, full_got, up, down, text = fence(
            (attn_two, attn_got, full_two, full_got, up, down, text)
        )
        pieces = [x[i : i + 2] + y[i : i + 2] for x, y in ((attn_two, attn_got), (full_two, full_got)) for i in (0, 2)]
        attn_one, attn_send, full_one, full_send = fence(tuple(pieces))
        up, down = hops(up, 1, 3), hops(down, -1, 3)
        attn_got = swap(attn_send, "dp", 2)
        full_got = swap(full_send, "dp", 1)
        text = text[0:2] + swap(text[2:4], "dp", 1)
        n_up.append(up), n_down.append(down)
        attn_one, attn_got, full_one, full_got, up, down, text, mlp_part = fence(
            (attn_one, attn_got, full_one, full_got, up, down, text, mlp_part)
        )
        attn_one, full_one = attn_one + attn_got, full_one + full_got
        n_up[-1], n_down[-1] = up, down
        w_mlp = lax.all_gather(mlp_part, "dp", axis=0, tiled=True)
        first_ring, second_ring = stack_pairs(ring(full_one))
        first = jnp.concatenate([attn_one[0:1], swap(attn_one[0:1], "dp", 1)])
        second = jnp.concatenate([attn_one[1:2], swap(attn_one[1:2], "dp", 2)])
        pool = jnp.concatenate([first, swap(first, "dp", 2), second, swap(second, "dp", 1)])
        other = swap(pool, "dp", 0)
        text = text[0] + swap(text[1], "dp", 0)
        *n_slots, h_one_all = line_slots(
            where, n_low, n_up, n_down, jnp.concatenate([mod_row(0), mod_row(1)])
        )
        n_slots = [n_low] + n_slots
        grad_own = out_grad[0]
        pool, other, first_ring, second_ring, h_one_all, text, grad_own = fence(
            (pool, other, first_ring, second_ring, h_one_all, text, grad_own)
        )
        grad_whole = lax.all_gather(grad_own, "tensor", axis=0)
        first, second = first_ring, second_ring
        first_got = swap(first, "dp", 1)
        second_got = swap(second, "dp", 2)
        text_ring = ring(text)
        (w_attn,) = place_blocks((pool, other), *in_pool(np.arange(members), 0, 1))
        w_attn = w_attn.reshape(-1, width)
        qkv = project(h_one_all, w_attn).astype(low)
        attended, logs = self_attend(qkv, share)
        first = jnp.concatenate([first, first_got])
        second = jnp.concatenate([second, second_got])
        first, second, text_ring, attended, logs, w_attn, w_mlp = fence(
            (first, second, text_ring, attended, logs, w_attn, w_mlp)
        )
        first_far, second_far = swap(first, "dp", 2), swap(second, "dp", 1)
        text_low = whole_text(jnp.stack(text_ring))
        mixed = exchanged(attended, own_keys(text_low, w_attn))
        first_far, second_far, mixed = fence((first_far, second_far, mixed))
        first_other, second_other = swap(first, "dp", 0), swap(second, "dp", 0)
        first_last, second_last = swap(first_far, "dp", 0), swap(second_far, "dp", 0)
        listing = np.arange(count * members)
        matrix, rank, head = listing // (count * per), listing // per % count, listing % per
        slot = lax.rem(me_tensor - rank + count, count)
        which, position = in_pool(matrix * per + head, slot, count)
        blocks = 2 * count
        w_full = place_blocks(
            (first, first_far, second, second_far, first_other, first_last, second_other, second_last),
            which * 4 + position // blocks,
            position % blocks,
            parts=4,
        )
        w_full = [part.reshape(width, width) for part in w_full]
        w_full[3], grad_whole = fence((w_full[3], grad_whole))
    else:
        slots_low = master.astype(low)
        rows = jnp.take(slots_low, rank_of, axis=0, mode="clip")
        rows = lax.psum(jnp.where(mine[:, None, None], rows, jnp.zeros((), low)), "dp")
        w_attn = rows[np.array(group_attn)].reshape(-1, width)
        w_full = lax.all_gather(rows[np.array(group_full)], "tensor", axis=0)
        w_full = w_full.reshape(count, 4, share, width).swapaxes(0, 1).reshape(4, width, width)
        w_full = [w_full[i] for i in range(4)]
        w_mlp = rows[8 * per :]
        n_slots = ring(n_low)
        normed_all = jnp.concatenate(n_slots)
        grad_whole = lax.all_gather(out_grad[0], "tensor", axis=0)
        ids = caption_ids
        for bit in range(bits):
            ids = jnp.concatenate([ids, swap(ids, "dp", bit)])
        text = caption_terms(ids)
        for bit in reversed(range(bits)):
            text = text[: 1 << bit] + swap(text[1 << bit :], "dp", bit)
        text_low = whole_text(jnp.stack(ring(text[0])))
        h_one_all = modulated(normed_all)
        qkv = project(h_one_all, w_attn).astype(low)
        attended, logs = self_attend(qkv, share)
        mixed = exchanged(attended, own_keys(text_low, w_attn))
    w_cross = w_full
    w_out, c_query, c_value, c_out = w_full
    w_mlp = w_mlp.reshape(-1, width)

    rows = jnp.concatenate([mod_row(2), mod_row(3), mod_row(4)])
    (
        branch_one,
        first_low,
        cq_rows,
        ck_rows,
        cv_rows,
        crossed,
        second_res,
        normed_two,
        h_two,
        inverse_two,
    ) = cross_block(
        where, mixed, hidden_in[0], rows, text_low, *w_cross
    )

    h_slots = {0: h_two}
    out_slots = [
        choose(grad_whole, lax.rem(me_tensor - k + count, count), 0) for k in range(count)
    ]
    grad_slots = [(mod_row(5) * item.astype(jnp.float32)).astype(low) for item in out_slots]
    near = [k for k in range(1, count) if 2 * k != count]
    far = [k for k in range(1, count) if 2 * k == count]
    acts, grad_pres, grad_terms, order = [], [], [], []
    for k in near:
        h_slots[k] = shift(h_two, k)
    for members_now in ([0], near, far):
        act, grad_pre, *terms = mlp_core(
            [h_slots[k] for k in members_now],
            [grad_slots[k] for k in members_now],
            w_mlp,
            acts[-1:],
        )
        if members_now == [0]:
            h_two, act = fence((h_two, act))
            for k in far:
                h_slots[k] = shift(h_two, k)
        acts.append(act), grad_pres.append(grad_pre)
        order += members_now
        grad_terms += [
            shift(term, count - k) if k else term for k, term in zip(members_now, terms)
        ]
    mlp_grad = mlp_grads(
        grad_pres, acts, [h_slots[k] for k in order], [grad_slots[k] for k in order]
    ).reshape(-1, unit_rows, width)
    hidden_share = w_mlp.shape[0] // 2
    pieces = [
        [(which, row, 0, hidden_share, hidden_share)]
        for which, act in enumerate(acts)
        for row in range(0, act.shape[0], tokens)
    ]
    branch_terms, branch_sums = ranked_terms(
        where, acts, order, pieces, w_mlp, [out_slots[k] for k in order], "mlp_out"
    )
    branch_row = branch_sums[1]
    grad_terms, branch_terms = fence((grad_terms, branch_terms))
    if plane:
        mlp_sum = lax.psum_scatter(mlp_grad, "dp", scatter_dimension=0, tiled=True)

    (
        first_grad,
        cross_low,
        grad_cq,
        attn_low,
        grad_cv,
        row_sums,
        *grad_mixed,
    ) = cross_back(
        where,
        grad_terms,
        out_grad[0],
        rows,
        normed_two,
        inverse_two,
        branch_one,
        cq_rows,
        ck_rows,
        cv_rows,
        c_out,
        c_query,
        w_out,
        (mlp_grad,),
    )

    grad_parts = [grad_mixed[0]] + [shift(grad_mixed[k], k) for k in range(1, count)]
    full_pairs = [
        ([(item, 0, share, None) for item in mixed], attn_low),
        ([(grad_cq, 0, width, 0)], first_low),
        ([(grad_cv, 0, width, 0)], text_low),
        ([(crossed, 0, width, 0)], cross_low),
    ]
    half = (share // HEAD_DIM // 2) * HEAD_DIM
    spans = [(0, half), (half, share)]

    def attention_pairs(grads, grad_parts):
        keys = sum(item[tokens:].astype(jnp.float32) for item in grad_parts).astype(low)
        pairs = [
            (
                [
                    (item, i * (end - begin), end - begin, begin)
                    for item, (begin, end) in zip(grads, spans)
                ],
                h_one_all,
            )
            for i in range(3)
        ]
        return pairs + [([(keys, 0, share, 0)], text_low)]

    def input_terms(grads):
        pieces = [
            [
                (which, slot * tokens, i * (end - begin), i * share + begin, end - begin)
                for which, (begin, end) in enumerate(spans)
                for i in range(3)
            ]
            for slot in range(count)
        ]
        return ranked_terms(where, grads, range(count), pieces, w_attn, n_slots, "attn_terms")

    if plane:
        x_bit, y_bit = (me_dp >> 1) & 1, (me_dp >> 2) & 1

        def split(total, bit, axis):
            return (choose(total, bit, axis), choose(total, 1 - bit, axis))

        branch_terms, grad_parts[0] = fence((branch_terms, grad_parts[0]))
        branch_two = lax.psum_scatter(
            branch_terms.reshape(-1, width), "tensor", scatter_dimension=0, tiled=True
        )
        kept, given = outer_halves(where, full_pairs, count, "full_grads")
        got = swap(given, "dp", 0)
        grad_parts, kept, got = fence((grad_parts, kept, got))
        box = (2, count, 2, 2, unit_rows, width)
        bits_here = jnp.stack([x_bit, y_bit]).astype(jnp.int32)
        kept_one, given_one, kept_two, given_two = sum_split(
            bits_here, kept.reshape(box), got.reshape(box)
        )
        got_one, got_two = swap(given_one, "dp", 1), swap(given_two, "dp", 2)
        grads_early = self_attend_back(qkv, grad_parts, attended, logs, share, *spans[0])
        kept_one, got_one, kept_two, got_two, grads_early, grad_parts, mlp_sum = fence(
            (kept_one, got_one, kept_two, got_two, grads_early, grad_parts, mlp_sum)
        )
        mlp_sum = lax.all_gather(mlp_sum, "dp", axis=0, tiled=True)
        kept_one, given_one = split(kept_one + got_one, y_bit, 1)
        kept_two, given_two = split(kept_two + got_two, x_bit, 1)
        kept_one, given_one, kept_two, given_two, grad_parts = fence(
            (kept_one, given_one, kept_two, given_two, grad_parts)
        )
        got_one, got_two = swap(given_one, "dp", 2), swap(given_two, "dp", 1)
        grads_late = self_attend_back(qkv, grad_parts, attended, logs, share, *spans[1])
        kept_one, got_one, kept_two, got_two, grads_early, grads_late, branch_two = fence(
            (kept_one, got_one, kept_two, got_two, grads_early, grads_late, branch_two)
        )
        full_parts = to_ring(jnp.stack([kept_one + got_one, kept_two + got_two], axis=1))
        full_parts = [full_parts[k] for k in range(count)]
        full_parts, grads_early, grads_late = fence((full_parts, grads_early, grads_late))
        grads_qkv = [grads_early, grads_late]
        full_got = [shift(full_parts[k], k) for k in range(1, count)]
        attn_kept, attn_given = outer_halves(
            where, attention_pairs(grads_qkv, grad_parts), 1, "attn_grads"
        )
        attn_got = swap(attn_given, "dp", 0)
        grad_h_terms, grad_h_sums = input_terms(grads_qkv)
        mod_terms = jnp.concatenate([grad_h_sums, row_sums, branch_row[None]])
        grad_h_one = lax.psum_scatter(
            grad_h_terms.reshape(-1, width), "tensor", scatter_dimension=0, tiled=True
        )
        attn_kept, attn_got, mod_terms = fence((attn_kept, attn_got, mod_terms))
        attn_all = (attn_kept + attn_got).reshape(2, 2, 2, unit_rows, width)
        one_kept, one_given = split(attn_all[0], x_bit, 1)
        two_kept, two_given = split(attn_all[1], y_bit, 0)
        one_got, two_got = swap(one_given, "dp", 1), swap(two_given, "dp", 2)
        mod_terms = mod_terms + swap(mod_terms, "dp", 0)
        full_own = full_parts[0]
        one_kept, one_got, two_kept, two_got, mod_terms, full_own, full_got = fence(
            (one_kept, one_got, two_kept, two_got, mod_terms, full_own, full_got)
        )
        full_sum = full_own.astype(jnp.float32)
        for part in full_got:
            full_sum = full_sum + part.astype(jnp.float32)
        full_sum = full_sum.astype(low)
        one_kept, one_given = split(one_kept + one_got, y_bit, 0)
        two_kept, two_given = split(two_kept + two_got, x_bit, 0)
        one_got, two_got = swap(one_given, "dp", 2), swap(two_given, "dp", 1)
        mod_terms = mod_terms + swap(mod_terms, "dp", 1)
        one_kept, one_got, two_kept, two_got, full_sum, mod_terms, mlp_sum = fence(
            (one_kept, one_got, two_kept, two_got, full_sum, mod_terms, mlp_sum)
        )
        first = jnp.stack([one_kept + one_got, full_sum[0]])
        second = jnp.stack([two_kept + two_got, full_sum[1]])
        first_got, second_got = swap(first, "dp", 1), swap(second, "dp", 2)
        first = jnp.concatenate([first, first_got])
        second = jnp.concatenate([second, second_got])
        mod_terms = mod_terms + swap(mod_terms, "dp", 2)
        first, second, mod_terms = fence((first, second, mod_terms))
        first_far, second_far = swap(first, "dp", 2), swap(second, "dp", 1)
        mod_terms = mod_terms + swap(mod_terms, "tensor", 0)
        first, first_far, second, second_far, mod_terms, grad_h_one = fence(
            (first, first_far, second, second_far, mod_terms, grad_h_one)
        )
        pool = jnp.concatenate([first, first_far, second, second_far])
        other = swap(pool, "dp", 0)
        for bit in range(1, count.bit_length() - 1):
            mod_terms = mod_terms + swap(mod_terms, "tensor", bit)
        pool, other, mod_grad = fence((pool, other, mod_terms))
        which, position = in_pool(member_of, np.where(is_attn, 0, 1), 2)
        which = jnp.where(is_mlp, 2, which)
        position = jnp.where(is_mlp, np.arange(units) - 8 * per, position)
        own = jnp.sum(jnp.where(match[:, :, None], jnp.stack([which, position], 1)[None], 0), axis=1)
        new_first, new_second, new_master = update_slots(
            master,
            first_moment,
            second_moment,
            filled.astype(jnp.int32),
            own[:, 0],
            own[:, 1],
            (pool, other, mlp_sum),
        )
    else:
        branch_two = lax.psum_scatter(
            branch_terms.reshape(-1, width), "tensor", scatter_dimension=0, tiled=True
        )
        grads_qkv = [self_attend_back(qkv, grad_parts, attended, logs, share, *span) for span in spans]
        attn_grads = [
            outer(array[:, lane : lane + lanes], right).astype(low)
            for left, right in attention_pairs(grads_qkv, grad_parts)
            for array, lane, lanes, row in left
        ]
        grad_h_terms, grad_h_sums = input_terms(grads_qkv)
        grad_h_one = lax.psum_scatter(
            grad_h_terms.reshape(-1, width), "tensor", scatter_dimension=0, tiled=True
        )
        mixed_all = from_ring(jnp.stack([item[:tokens] for item in mixed]), 1)
        mixed_all = mixed_all.transpose(1, 0, 2).reshape(tokens, width)
        full_grads = [outer(mixed_all, attn_low)]
        full_grads += [outer(left[0][0], right) for left, right in full_pairs[1:]]
        full_sum = [g.astype(low).reshape(count, share, width) for g in full_grads]
        full_sum = jnp.stack(full_sum, axis=1)
        full_sum = lax.psum_scatter(full_sum, "tensor", scatter_dimension=0, tiled=True)
        order = np.array(group_attn + group_full + group_mlp)
        sums = jnp.concatenate(
            [jnp.concatenate(attn_grads), full_sum.reshape(-1, width), mlp_grad.reshape(-1, width)]
        )
        sums = lax.psum(sums.reshape(units, unit_rows, width), "dp")
        owned = jnp.take(sums, jnp.array(np.argsort(order))[unit_of_slot], axis=0, mode="clip")
        mod_grad = total_sum(jnp.concatenate([grad_h_sums, row_sums, branch_row[None]]))
        new_first, new_second, new_master = adamw(
            master,
            first_moment,
            second_moment,
            owned.astype(jnp.float32),
            filled.astype(jnp.float32)[:, None, None],
            rate,
        )
    branch_two, second_res, grad_h_one, new_first = fence(
        (branch_two, second_res, grad_h_one, new_first)
    )
    grad_h_one = grad_h_one.astype(jnp.float32)
    block_out = second_res + mod_row(5) * branch_two.astype(jnp.float32)
    input_grad = first_grad + norm_back(grad_h_one, normed_one, inverse_one, mod_row(1))
    mod_new_first, mod_new_second, mod_new = adamw(
        mod_table, mod_first, mod_second, mod_grad, 1.0, table_rate
    )
    return (
        block_out[None],
        input_grad[None],
        new_first,
        new_second,
        new_master,
        mod_new_first,
        mod_new_second,
        mod_new,
    )


def solution(mesh):
    in_specs = (
        P("dp", "tensor", None),
        P("dp", None, None),
        P("dp", "tensor"),
        P("dp", None),
        P(),
        P("dp", "tensor", None),
        P("dp", "tensor", None),
        P("dp", "tensor", None),
        P(),
        P(),
        P(),
        P("dp", "tensor", None),
    )
    out_specs = (
        P("dp", "tensor", None),
        P("dp", "tensor", None),
        P("dp", "tensor", None),
        P("dp", "tensor", None),
        P("dp", "tensor", None),
        P(),
        P(),
        P(),
    )
    return jax.shard_map(
        on_device, mesh=mesh, in_specs=in_specs, out_specs=out_specs, check_vma=False
    )
```

```python
import math

import jax
import jax.numpy as jnp
import numpy as np
from jax import lax
from jax.experimental import pallas as pl
from jax.experimental.pallas import tpu as pltpu
from jax.sharding import PartitionSpec as P

HEAD_DIM = 72
STEP = 10


norm_eps = 1e-06
beta_one = 0.9
beta_two = 0.999
rate = 0.03
table_rate = 0.3
decay = 0.01
adam_eps = 1e-08
low = jnp.bfloat16


def ranks_of(owners):
    index = jnp.arange(owners.shape[0])
    before = (owners[None, :] == owners[:, None]) & (index[None, :] < index[:, None])
    return jnp.sum(before.astype(jnp.int32), axis=1)


def layer_norm(values):
    center = values - jnp.mean(values, axis=-1, keepdims=True)
    inverse = lax.rsqrt(jnp.mean(center * center, axis=-1, keepdims=True) + norm_eps)
    return (center * inverse, inverse)


def norm_back(grad_rows, normed, inverse, scale_row):
    scaled = grad_rows * (1.0 + scale_row)
    mean_one = jnp.mean(scaled, axis=-1, keepdims=True)
    mean_two = jnp.mean(scaled * normed, axis=-1, keepdims=True)
    return inverse * (scaled - mean_one - normed * mean_two)


def project(rows, weight):
    return jnp.einsum("ld,rd->lr", rows, weight, preferred_element_type=jnp.float32)


def expand(rows, weight):
    return jnp.einsum("lr,rd->ld", rows, weight, preferred_element_type=jnp.float32)


def outer(left, right):
    return jnp.einsum("lr,ld->rd", left, right, preferred_element_type=jnp.float32)


def shift(values, step):
    count = lax.axis_size("tensor")
    return lax.ppermute(values, "tensor", [(i, (i + step) % count) for i in range(count)])


def ring(values):
    return [values] + [shift(values, k) for k in range(1, lax.axis_size("tensor"))]


def to_ring(stacked):
    count = stacked.shape[0]
    twice = jnp.concatenate([stacked, stacked], axis=0)
    return lax.dynamic_slice_in_dim(twice, lax.axis_index("tensor"), count, 0)


def from_ring(stacked, sign):
    count = stacked.shape[0]
    me = lax.axis_index("tensor")
    place = lax.rem(sign * (jnp.arange(count) - me) + 2 * count, count)
    return jnp.take(stacked, place, axis=0, mode="clip")


cheap = pl.CostEstimate(flops=1000, bytes_accessed=1000, transcendentals=0)
costly = pl.CostEstimate(flops=10**10, bytes_accessed=10**7, transcendentals=0)


def self_attend(qkv, share):
    length = qkv.shape[0]
    rows = min(512, length)
    curve = HEAD_DIM ** (-0.5) * math.log2(math.e)
    heads = share // HEAD_DIM

    def body(qkv_ref, out_ref, log_ref):
        @pl.loop(0, length // rows)
        def _(step):
            here = pl.ds(pl.multiple_of(step * rows, rows), rows)
            parts = []
            for head in range(heads):
                at = head * HEAD_DIM
                q = qkv_ref[here, at : at + HEAD_DIM]
                k = qkv_ref[:, share + at : share + at + HEAD_DIM]
                v = qkv_ref[:, 2 * share + at : 2 * share + at + HEAD_DIM]
                scores = dot(k, q, nt)
                top = jnp.max(scores, axis=0, keepdims=True)
                expo = jnp.exp2((scores - top) * curve)
                total = jnp.sum(expo, axis=0, keepdims=True)
                log_ref[head : head + 1, here] = top * curve + jnp.log2(total)
                parts.append((dot(v, expo.astype(low), tn) * (1.0 / total)).T)
            out_ref[here, :] = jnp.concatenate(parts, axis=1).astype(low)

    return pl.pallas_call(
        body,
        out_shape=[
            jax.ShapeDtypeStruct((length, share), low),
            jax.ShapeDtypeStruct((heads, length), jnp.float32),
        ],
        compiler_params=pltpu.CompilerParams(vmem_limit_bytes=40 * 2**20),
        cost_estimate=cheap,
        name="self_attend",
    )(qkv)


def self_attend_back(qkv, grads, mixed, logs, share, begin, end):
    length = qkv.shape[0]
    rows = length // len(grads)
    span = end - begin
    scale = HEAD_DIM ** (-0.5)
    curve = scale * math.log2(math.e)

    def body(qkv_ref, mixed_ref, log_ref, *refs):
        grad_refs, (out_ref, grad_k, grad_v) = refs[: len(grads)], refs[len(grads) :]
        for step, grad_ref in enumerate(grad_refs):
            here = slice(step * rows, (step + 1) * rows)
            parts = []
            for head, at in enumerate(range(begin, end, HEAD_DIM)):
                q = qkv_ref[here, at : at + HEAD_DIM]
                k = qkv_ref[:, share + at : share + at + HEAD_DIM]
                v = qkv_ref[:, 2 * share + at : 2 * share + at + HEAD_DIM]
                g = grad_ref[0:rows, at : at + HEAD_DIM]
                o = mixed_ref[here, at : at + HEAD_DIM]
                inner = g.astype(jnp.float32) * o.astype(jnp.float32)
                inner = jnp.sum(inner.T, axis=0, keepdims=True)
                which = begin // HEAD_DIM + head
                probs = jnp.exp2(dot(k, q, nt) * curve - log_ref[which : which + 1, here])
                grad_scores = (probs * (dot(v, g, nt) - inner)).astype(low)
                to_v = dot(probs.astype(low), g)
                to_k = dot(grad_scores, q)
                if step:
                    grad_v[head] += to_v
                    grad_k[head] += to_k
                else:
                    grad_v[head] = to_v
                    grad_k[head] = to_k
                parts.append((dot(k, grad_scores, tn) * scale).T)
            out_ref[here, 0:span] = jnp.concatenate(parts, axis=1).astype(low)
        heads = range(span // HEAD_DIM)
        both = [grad_k[head] * scale for head in heads]
        out_ref[:, span : 2 * span] = jnp.concatenate(both, axis=1).astype(low)
        both = [grad_v[head] for head in heads]
        out_ref[:, 2 * span :] = jnp.concatenate(both, axis=1).astype(low)

    return pl.pallas_call(
        body,
        out_shape=jax.ShapeDtypeStruct((length, 3 * span), low),
        scratch_shapes=[pltpu.VMEM((span // HEAD_DIM, length, HEAD_DIM), jnp.float32)] * 2,
        compiler_params=pltpu.CompilerParams(vmem_limit_bytes=40 * 2**20),
        cost_estimate=cheap,
        name="self_attend_back",
    )(qkv, mixed, logs, *grads)


def mlp_core(rows_in, grads_in, w_mlp, after):
    groups = len(rows_in)
    tokens, width = rows_in[0].shape
    hidden = w_mlp.shape[0] // 2
    chunk = 384 if hidden % 384 == 0 else hidden
    steps = hidden // chunk
    curve = 0.7978845608028654

    def body(*refs):
        rows, grads = refs[:groups], refs[groups : 2 * groups]
        up, down = refs[2 * groups : 2 * groups + 2]
        act, grad_pre, *outs = refs[2 * groups + 2 + len(after) : -1]
        total = refs[-1]
        step = pl.program_id(0)
        for i in range(groups):
            pre = lax.dot_general(
                rows[i][...], up[...], (((1,), (1,)), ((), ())), preferred_element_type=jnp.float32
            )
            square = pre * pre
            bend = jnp.tanh(curve * pre * (1.0 + 0.044715 * square))
            half = 0.5 * (1.0 + bend)
            here = pl.ds(i * tokens, tokens)
            act[here, :] = (pre * half).astype(low)
            slope = half + (0.5 * curve) * pre * (1.0 - bend * bend) * (1.0 + 0.134145 * square)
            grad_act = lax.dot_general(
                grads[i][...], down[...], (((1,), (1,)), ((), ())), preferred_element_type=jnp.float32
            )
            grad_low = (grad_act * slope).astype(low)
            grad_pre[here, :] = grad_low
            term = jnp.dot(grad_low, up[...], preferred_element_type=jnp.float32)

            @pl.when(step == 0)
            def _():
                total[here, :] = term

            @pl.when(step > 0)
            def _():
                total[here, :] += term

            @pl.when(step == steps - 1)
            def _():
                outs[i][...] = total[here, :].astype(low)

    whole = pl.BlockSpec((tokens, width), lambda s: (0, 0))
    across = pl.BlockSpec((groups * tokens, chunk), lambda s: (0, s))
    return pl.pallas_call(
        body,
        grid=(steps,),
        in_specs=[whole] * (2 * groups)
        + [
            pl.BlockSpec((chunk, width), lambda s: (s, 0)),
            pl.BlockSpec((chunk, width), lambda s: (steps + s, 0)),
        ]
        + [pl.BlockSpec(memory_space=pl.ANY)] * len(after),
        out_specs=[across, across] + [whole] * groups,
        out_shape=[jax.ShapeDtypeStruct((groups * tokens, hidden), low)] * 2
        + [jax.ShapeDtypeStruct((tokens, width), low)] * groups,
        scratch_shapes=[pltpu.VMEM((groups * tokens, width), jnp.float32)],
        compiler_params=pltpu.CompilerParams(vmem_limit_bytes=60 * 2**20),
        cost_estimate=cheap,
        name="mlp_core",
    )(*rows_in, *grads_in, w_mlp, w_mlp, *after)


nt = (((1,), (1,)), ((), ()))
tn = (((0,), (0,)), ((), ()))


def dot(left, right, dims=(((1,), (0,)), ((), ()))):
    return lax.dot_general(left, right, dims, preferred_element_type=jnp.float32)


def softmax_keys(keys, queries):
    scores = dot(keys, queries, nt) * HEAD_DIM ** (-0.5)
    expo = jnp.exp(scores - jnp.max(scores, axis=0, keepdims=True))
    return expo * (1.0 / jnp.sum(expo, axis=0, keepdims=True))


def cuts_of(width):
    size = 384 if width % 384 == 0 else width
    return [slice(i, i + size) for i in range(0, width, size)]


def in_smem():
    return pl.BlockSpec(memory_space=pltpu.SMEM)


def in_vmem():
    return pl.BlockSpec(memory_space=pltpu.VMEM)


def line_slots(place, own, ups, downs, rows):
    count = len(ups) + 1
    tokens, width = own.shape

    def body(place_ref, *refs):
        own_ref, up_refs, down_refs = refs[0], refs[1:count], refs[count : 2 * count - 1]
        rows_ref, outs, out = refs[2 * count - 1], refs[2 * count : -1], refs[-1]
        me = place_ref[0]

        def modulate(slot, ref):
            value = ref[...].astype(jnp.float32)
            value = value * (1.0 + rows_ref[1:2, :]) + rows_ref[0:1, :]
            out[slot * tokens : (slot + 1) * tokens, :] = value.astype(low)

        modulate(0, own_ref)
        for k in range(1, count):
            for side, ref in ((me >= k, up_refs[k - 1]), (me < k, down_refs[count - k - 1])):

                @pl.when(side)
                def _():
                    outs[k - 1][...] = ref[...]
                    modulate(k, ref)

    shapes = [(tokens, width)] * (count - 1) + [(count * tokens, width)]
    return pl.pallas_call(
        body,
        in_specs=[in_smem()] + [in_vmem()] * (2 * count),
        out_shape=[jax.ShapeDtypeStruct(shape, low) for shape in shapes],
        compiler_params=pltpu.CompilerParams(vmem_limit_bytes=32 * 2**20),
        cost_estimate=cheap,
        name="line_slots",
    )(place, own, *ups, *downs, rows)


def cross_block(place, mixed, hidden, rows, text, w_out, c_query, c_value, c_out):
    count, share = len(mixed), mixed[0].shape[1]
    tokens, width = hidden.shape
    words = text.shape[0]
    per = share // HEAD_DIM

    def body(place_ref, *refs):
        parts = refs[:count]
        x_ref, rows_ref, text_ref = refs[count : count + 3]
        far = refs[count + 3 : count + 7]
        outs = refs[count + 7 : count + 16]
        inverse = refs[count + 16]
        wo, wq, wv, wc, *own = refs[count + 17 : -3]
        held, read, sems = refs[-3:]
        branch, res_low, cq, ck, cv, crossed, res, normed, out = own
        me = place_ref[0]
        loads = [
            pltpu.make_async_copy(source, target, read.at[i])
            for i, (source, target) in enumerate(zip(far, (wo, wq, wv, wc)))
        ]
        stores = [
            pltpu.make_async_copy(source, target, sems.at[i])
            for i, (source, target) in enumerate(zip(own, outs))
        ]
        for load in loads:
            load.start()
        loads[0].wait()
        for cut in cuts_of(width):
            total = jnp.zeros((tokens, cut.stop - cut.start), jnp.float32)
            for k in range(count):
                rank = lax.rem(me + k, count)
                here = pl.ds(pl.multiple_of(rank * share, 32), share)
                total += dot(parts[k][0:tokens, :], wo[here, cut])
            branch[:, cut] = total
            first = x_ref[:, cut].astype(jnp.float32) + rows_ref[0:1, cut] * total
            res[:, cut] = first
            res_low[:, cut] = first.astype(low)
        stores[0].start()
        stores[1].start()
        loads[1].wait()
        loads[2].wait()
        for cut in cuts_of(width):
            cq[:, cut] = dot(res_low[...], wq[cut, :], nt).astype(low)
            cv[:, cut] = dot(text_ref[...], wv[cut, :], nt).astype(low)
        for k in range(count):
            held[lax.rem(me + k, count)] = parts[k][tokens:, :]
        ck[...] = jnp.concatenate([held[rank] for rank in range(count)], axis=1)
        for i in (2, 3, 4):
            stores[i].start()
        parts_out = []
        for at in range(0, width, HEAD_DIM):
            head = slice(at, at + HEAD_DIM)
            probs = softmax_keys(ck[:, head], cq[:, head]).astype(low)
            parts_out.append(dot(cv[:, head], probs, tn).T)
        crossed[...] = jnp.concatenate(parts_out, axis=1).astype(low)
        stores[5].start()
        loads[3].wait()
        for cut in cuts_of(width):
            res[:, cut] += dot(crossed[...], wc[:, cut])
        second = res[...]
        center = second - jnp.mean(second, axis=-1, keepdims=True)
        spread = lax.rsqrt(jnp.mean(center * center, axis=-1, keepdims=True) + norm_eps)
        inverse[...] = spread
        scaled = center * spread
        normed[...] = scaled
        stores[6].start()
        stores[7].start()
        out[...] = (scaled * (1.0 + rows_ref[2:3, :]) + rows_ref[1:2, :]).astype(low)
        stores[8].start()
        for store in stores:
            store.wait()

    wide = (tokens, width)
    shapes = [
        (wide, jnp.float32),
        (wide, low),
        (wide, low),
        ((words, width), low),
        ((words, width), low),
        (wide, low),
        (wide, jnp.float32),
        (wide, jnp.float32),
        (wide, low),
    ]
    anywhere = pl.BlockSpec(memory_space=pl.ANY)
    return pl.pallas_call(
        body,
        in_specs=[in_smem()] + [in_vmem()] * (count + 3) + [anywhere] * 4,
        out_specs=[anywhere] * len(shapes) + [in_vmem()],
        out_shape=[jax.ShapeDtypeStruct(*item) for item in shapes]
        + [jax.ShapeDtypeStruct((tokens, 1), jnp.float32)],
        scratch_shapes=[pltpu.VMEM((width, width), low)] * 4
        + [pltpu.VMEM(*item) for item in shapes]
        + [
            pltpu.VMEM((count, words, share), low),
            pltpu.SemaphoreType.DMA((4,)),
            pltpu.SemaphoreType.DMA((len(shapes),)),
        ],
        compiler_params=pltpu.CompilerParams(vmem_limit_bytes=60 * 2**20),
        cost_estimate=cheap,
        name="cross_block",
    )(place, *mixed, hidden, rows, text, w_out, c_query, c_value, c_out)


def cross_back(
    place, terms, grad, rows, normed, inverse, branch, cq, ck, cv, c_out, c_query, w_out, after
):
    count = len(terms)
    tokens, width = grad.shape
    words = ck.shape[0]
    share = width // count
    scale = HEAD_DIM ** (-0.5)

    def body(place_ref, *refs):
        parts = refs[:count]
        grad_ref, rows_ref, i_ref, k_ref, v_ref = refs[count : count + 5]
        far = refs[count + 5 : count + 11]
        refs = refs[: count + 11] + refs[count + 11 + len(after) :]
        stored = refs[count + 11 : count + 15]
        grad_v, sums = refs[count + 15 : count + 17]
        outs = refs[count + 17 : 2 * count + 17]
        near = refs[2 * count + 17 : 2 * count + 23]
        n_ref, wc, q_ref, wq, wo, b_ref = near
        own = refs[2 * count + 23 : 2 * count + 27]
        first, cross_low, grad_q, attn_low = own
        back, held, read, sems = refs[2 * count + 27 :]
        me = place_ref[0]
        loads = [
            pltpu.make_async_copy(source, target, read.at[i])
            for i, (source, target) in enumerate(zip(far, near))
        ]
        stores = [
            pltpu.make_async_copy(source, target, sems.at[i])
            for i, (source, target) in enumerate(zip(own, stored))
        ]
        for load in loads:
            load.start()
        loads[0].wait()
        total = parts[0][...].astype(jnp.float32)
        for part in parts[1:]:
            total += part[...].astype(jnp.float32)
        n = n_ref[...]
        sums[1:2, :] = jnp.sum(total, axis=0, keepdims=True)
        sums[2:3, :] = jnp.sum(total * n, axis=0, keepdims=True)
        second = grad_ref[...].astype(jnp.float32) + norm_back(total, n, i_ref[...], rows_ref[2:3, :])
        first[...] = second
        cross_low[...] = second.astype(low)
        stores[1].start()
        loads[1].wait()
        loads[2].wait()
        for cut in cuts_of(width):
            back[:, cut] = dot(cross_low[...], wc[cut, :], nt).astype(low)
        grads = ([], [], [])
        for at in range(0, width, HEAD_DIM):
            head = slice(at, at + HEAD_DIM)
            q, k, v, g = q_ref[:, head], k_ref[:, head], v_ref[:, head], back[:, head]
            probs = softmax_keys(k, q)
            grad_probs = dot(v, g, nt)
            inner = jnp.sum(probs * grad_probs, axis=0, keepdims=True)
            grad_scores = (probs * (grad_probs - inner)).astype(low)
            grads[0].append((dot(k, grad_scores, tn) * scale).T)
            grads[1].append(dot(grad_scores, q) * scale)
            grads[2].append(dot(probs.astype(low), g))
        grad_q[...] = jnp.concatenate(grads[0], axis=1).astype(low)
        grad_v[...] = jnp.concatenate(grads[2], axis=1).astype(low)
        heads = share // HEAD_DIM
        for rank in range(count):
            pieces = grads[1][rank * heads : (rank + 1) * heads]
            held[rank] = jnp.concatenate(pieces, axis=1).astype(low)
        stores[2].start()
        for load in loads[3:]:
            load.wait()
        for cut in cuts_of(width):
            whole = first[:, cut] + dot(grad_q[...], wq[:, cut])
            first[:, cut] = whole
            attn_low[:, cut] = (rows_ref[0:1, cut] * whole).astype(low)
            sums[0:1, cut] = jnp.sum(b_ref[:, cut] * whole, axis=0, keepdims=True)
        stores[0].start()
        stores[3].start()
        for k in range(count):
            rank = lax.rem(me + k, count)
            here = pl.ds(pl.multiple_of(rank * share, 32), share)
            outs[k][0:tokens, :] = dot(attn_low[...], wo[here, :], nt).astype(low)
            outs[k][tokens:, :] = held[rank]
        for store in stores:
            store.wait()

    wide, square = (tokens, width), (width, width)
    shapes = [
        (wide, jnp.float32),
        (wide, low),
        (wide, low),
        (wide, low),
        ((words, width), low),
        ((3, width), jnp.float32),
    ] + [((tokens + words, share), low)] * count
    anywhere = pl.BlockSpec(memory_space=pl.ANY)
    loaded = [
        pltpu.VMEM(wide, jnp.float32),
        pltpu.VMEM(square, low),
        pltpu.VMEM(wide, low),
        pltpu.VMEM(square, low),
        pltpu.VMEM(square, low),
        pltpu.VMEM(wide, jnp.float32),
    ]
    return pl.pallas_call(
        body,
        in_specs=[in_smem()] + [in_vmem()] * (count + 5) + [anywhere] * (6 + len(after)),
        out_specs=[anywhere] * 4 + [in_vmem()] * (2 + count),
        out_shape=[jax.ShapeDtypeStruct(*item) for item in shapes],
        scratch_shapes=loaded
        + [pltpu.VMEM(*item) for item in shapes[:4]]
        + [
            pltpu.VMEM(wide, low),
            pltpu.VMEM((count, words, share), low),
            pltpu.SemaphoreType.DMA((6,)),
            pltpu.SemaphoreType.DMA((4,)),
        ],
        compiler_params=pltpu.CompilerParams(vmem_limit_bytes=60 * 2**20),
        cost_estimate=cheap,
        name="cross_back",
    )(
        place,
        *terms,
        grad,
        rows,
        inverse,
        ck,
        cv,
        normed,
        c_out,
        cq,
        c_query,
        w_out,
        branch,
        *after,
    )


def outer_halves(place, pairs, parts, name):
    width = pairs[0][1].shape[1]
    high = [sum(piece[2] for piece in left) for left, _ in pairs]
    size = high[0] // parts
    tokens = [right.shape[0] for _, right in pairs]
    flat = []

    def index_of(array):
        for i, other in enumerate(flat):
            if other is array:
                return i
        flat.append(array)
        return len(flat) - 1

    plans = [
        ([(index_of(array), *rest) for array, *rest in left], index_of(right))
        for left, right in pairs
    ]
    amount = len(pairs)

    def body(place_ref, *refs):
        ins, (kept, given), (held, sems) = refs[: len(flat)], refs[len(flat) :][:2], refs[-2:]
        turned = refs[len(flat) + 2 : -2]
        me, core = place_ref[0], place_ref[1]
        for i, (left, right) in enumerate(plans):
            for k, (which, lane, lanes, row) in enumerate(left):
                piece = ins[which][0 : tokens[i], lane : lane + lanes]
                piece = piece.astype(jnp.float32).T.astype(low)
                if row is None:
                    rank = lax.rem(me + k, len(left))
                    turned[i][pl.ds(pl.multiple_of(rank * lanes, 32), lanes), :] = piece
                else:
                    turned[i][row : row + lanes, :] = piece
            for part in range(parts):
                at = i * parts + part
                tile = dot(turned[i][part * size : (part + 1) * size, :], ins[right][...])
                held[at] = tile.astype(low)
                for out, side in ((kept, 0), (given, 1)):

                    @pl.when((core ^ (i & 1)) == side)
                    def _():
                        pltpu.make_async_copy(
                            held.at[at], out.at[i // 2, part], sems.at[at]
                        ).start()

        for at in range(amount * parts):
            pltpu.make_async_copy(held.at[at], kept.at[0, 0], sems.at[at]).wait()

    out = jax.ShapeDtypeStruct((amount // 2, parts, size, width), low)
    return pl.pallas_call(
        body,
        in_specs=[in_smem()] + [in_vmem()] * len(flat),
        out_specs=[pl.BlockSpec(memory_space=pl.ANY)] * 2,
        out_shape=[out, out],
        scratch_shapes=[pltpu.VMEM((high[i], tokens[i]), low) for i in range(amount)]
        + [
            pltpu.VMEM((amount * parts, size, width), low),
            pltpu.SemaphoreType.DMA((amount * parts,)),
        ],
        compiler_params=pltpu.CompilerParams(vmem_limit_bytes=60 * 2**20),
        cost_estimate=cheap if parts > 1 else costly,
        name=name,
    )(place, *flat)


def mlp_grads(grad_pres, acts, rows_in, grads_in):
    pieces, rights = len(acts), len(rows_in)
    tokens, width = rows_in[0].shape
    hidden = acts[0].shape[1]
    chunk = 384 if hidden % 384 == 0 else hidden
    steps = hidden // chunk

    def body(*refs):
        step = pl.program_id(0)
        lefts_up, lefts_down = refs[:pieces], refs[pieces : 2 * pieces]
        rights_up = refs[2 * pieces : 2 * pieces + rights]
        rights_down = refs[2 * pieces + rights : -1]
        out = refs[-1]

        def terms(lefts, turn, others):
            here = pl.ds(pl.multiple_of(turn * chunk, chunk), chunk)
            total = jnp.zeros((chunk, width), jnp.float32)
            cursor = 0
            for left in lefts:
                for i in range(left.shape[0] // tokens):
                    total += dot(left[i * tokens : (i + 1) * tokens, here], others[cursor][...], tn)
                    cursor += 1
            out[...] = total.astype(low)

        @pl.when(step < steps)
        def _():
            terms(lefts_up, step, rights_up)

        @pl.when(step >= steps)
        def _():
            terms(lefts_down, step - steps, rights_down)

    arrays = (*grad_pres, *acts, *rows_in, *grads_in)
    chunked = pl.BlockSpec((chunk, width), lambda s: (s, 0))
    return pl.pallas_call(
        body,
        grid=(2 * steps,),
        in_specs=[pl.BlockSpec(array.shape, lambda s: (0, 0)) for array in arrays],
        out_specs=chunked,
        out_shape=jax.ShapeDtypeStruct((2 * hidden, width), low),
        compiler_params=pltpu.CompilerParams(vmem_limit_bytes=60 * 2**20),
        cost_estimate=cheap,
        name="mlp_grads",
    )(*arrays)


def ranked_terms(place, lefts, order, pieces, weight, factors, name):
    tokens, width = factors[0].shape
    count = len(factors)

    def body(place_ref, *refs):
        ins, weight_ref = refs[: len(lefts)], refs[len(lefts)]
        others = refs[len(lefts) + 1 : len(lefts) + 1 + count]
        out, sums = refs[-2:]
        me = place_ref[0]
        for i, slot in enumerate(order):
            rank = lax.rem(me - slot + count, count)
            for cut in cuts_of(width):
                term = jnp.zeros((tokens, cut.stop - cut.start), jnp.float32)
                for which, row, lane, start, depth in pieces[i]:
                    term += dot(
                        ins[which][row : row + tokens, lane : lane + depth],
                        weight_ref[start : start + depth, cut],
                    )
                out[rank, :, cut] = term.astype(low)
                one = jnp.sum(term, axis=0, keepdims=True)
                two = jnp.sum(term * others[i][:, cut].astype(jnp.float32), axis=0, keepdims=True)
                if i:
                    one, two = one + sums[0:1, cut], two + sums[1:2, cut]
                sums[0:1, cut], sums[1:2, cut] = one, two

    return pl.pallas_call(
        body,
        in_specs=[in_smem()] + [in_vmem()] * (len(lefts) + 1 + count),
        out_shape=[
            jax.ShapeDtypeStruct((count, tokens, width), low),
            jax.ShapeDtypeStruct((2, width), jnp.float32),
        ],
        compiler_params=pltpu.CompilerParams(vmem_limit_bytes=60 * 2**20),
        cost_estimate=cheap if len(lefts) > 2 else costly,
        name=name,
    )(place, *lefts, weight, *factors)


def sum_split(place, kept, got):
    count, unit_rows, width = kept.shape[1], kept.shape[4], kept.shape[5]

    def body(place_ref, one, two, keep_x, give_x, keep_y, give_y):
        x, y = place_ref[0], place_ref[1]

        def total(*index):
            return (one[index].astype(jnp.float32) + two[index].astype(jnp.float32)).astype(low)

        for j in range(2):
            keep_x[0, j] = total(0, 0, j, x)
            give_x[0, j] = total(0, 0, j, 1 - x)
            keep_y[0, j] = total(1, 0, y, j)
            give_y[0, j] = total(1, 0, 1 - y, j)

    block = pl.BlockSpec((2, 1, 2, 2, unit_rows, width), lambda r, *_: (0, r, 0, 0, 0, 0))
    part = pl.BlockSpec((1, 2, unit_rows, width), lambda r, *_: (r, 0, 0, 0))
    return pl.pallas_call(
        body,
        grid_spec=pltpu.PrefetchScalarGridSpec(
            num_scalar_prefetch=1, grid=(count,), in_specs=[block] * 2, out_specs=[part] * 4
        ),
        out_shape=[jax.ShapeDtypeStruct((count, 2, unit_rows, width), low)] * 4,
        compiler_params=pltpu.CompilerParams(vmem_limit_bytes=60 * 2**20),
        cost_estimate=cheap,
        name="sum_split",
    )(place, kept, got)


def update_slots(master, first_moment, second_moment, filled, which, position, sources):
    capacity, unit_rows, width = master.shape

    group = math.gcd(capacity, 2)
    steps = capacity // group

    def body(filled_ref, which_ref, position_ref, weight, one, two, *rest):
        ins = rest[: len(sources)]
        new_one, new_two, new_weight, held, sems = rest[len(sources) :]
        step = pl.program_id(0)

        def fetch(turn):
            for i in range(group):
                slot = turn * group + i
                for source, ref in enumerate(ins):

                    @pl.when(which_ref[slot] == source)
                    def _():
                        pltpu.make_async_copy(
                            ref.at[position_ref[slot]], held.at[turn % 2, i], sems.at[turn % 2, i]
                        ).start()

        @pl.when(step == 0)
        def _():
            fetch(step)

        @pl.when(step < steps - 1)
        def _():
            fetch(step + 1)

        for i in range(group):
            pltpu.make_async_copy(
                ins[0].at[0], held.at[step % 2, i], sems.at[step % 2, i]
            ).wait()
            mask = (filled_ref[step * group + i] > 0).astype(jnp.float32)
            grad = held[step % 2, i].astype(jnp.float32)
            results = adamw(weight[i], one[i], two[i], grad, mask, rate)
            new_one[i], new_two[i], new_weight[i] = results

    block = pl.BlockSpec((group, unit_rows, width), lambda s, *_: (s, 0, 0))
    return pl.pallas_call(
        body,
        grid_spec=pltpu.PrefetchScalarGridSpec(
            num_scalar_prefetch=3,
            grid=(steps,),
            in_specs=[block] * 3 + [pl.BlockSpec(memory_space=pl.ANY)] * len(sources),
            out_specs=[block] * 3,
            scratch_shapes=[
                pltpu.VMEM((2, group, unit_rows, width), low),
                pltpu.SemaphoreType.DMA((2, group)),
            ],
        ),
        out_shape=[jax.ShapeDtypeStruct(master.shape, jnp.float32)] * 3,
        compiler_params=pltpu.CompilerParams(vmem_limit_bytes=56 * 2**20),
        cost_estimate=cheap,
        name="update_slots",
    )(filled, which, position, master, first_moment, second_moment, *sources)


def adamw(weight, moment_one, moment_two, gradient, filled, step_rate):
    new_one = beta_one * moment_one + (1.0 - beta_one) * gradient
    new_two = beta_two * moment_two + (1.0 - beta_two) * gradient * gradient
    fixed_one = new_one / (1.0 - beta_one**STEP)
    fixed_two = new_two / (1.0 - beta_two**STEP)
    updated = weight - step_rate * (fixed_one / (jnp.sqrt(fixed_two) + adam_eps) + decay * weight)
    return (new_one * filled, new_two * filled, updated * filled)


def swap(values, axis, bit):
    count = lax.axis_size(axis)
    return lax.ppermute(values, axis, [(i, i ^ (1 << bit)) for i in range(count)])


def choose(values, index, axis):
    return lax.dynamic_index_in_dim(values, index, axis, keepdims=False)


def total_sum(values):
    for axis in ("dp", "tensor"):
        for bit in range(lax.axis_size(axis).bit_length() - 1):
            values = values + swap(values, axis, bit)
    return values


def pick_units(master, slot_unit, state, kind, place, sizes, after=()):
    capacity, unit_rows, width = master.shape
    units = state.shape[0]

    def body(slot_ref, state_ref, kind_ref, place_ref, blocks, *rest):
        outs = rest[len(after) : len(after) + len(sizes)]
        highs, lows, zeros, read, sems = rest[len(after) + len(sizes) :]

        def start(source, unit):
            for which, out in enumerate(outs):

                @pl.when(kind_ref[unit] == which)
                def _():
                    pltpu.make_async_copy(source, out.at[place_ref[unit]], sems.at[unit]).start()

        @pl.loop(0, capacity)
        def _(slot):
            @pl.when(slot_ref[slot] >= 0)
            def _():
                pltpu.make_async_copy(blocks.at[slot], highs.at[slot], read.at[slot]).start()

        zeros[...] = jnp.zeros_like(zeros)

        @pl.loop(0, units)
        def _(unit):
            @pl.when(state_ref[unit] == 0)
            def _():
                start(zeros, unit)

        @pl.loop(0, capacity)
        def _(slot):
            @pl.when(slot_ref[slot] >= 0)
            def _():
                pltpu.make_async_copy(blocks.at[slot], highs.at[slot], read.at[slot]).wait()
                lows[slot] = highs[slot].astype(low)
                start(lows.at[slot], slot_ref[slot])

        @pl.loop(0, units)
        def _(unit):
            @pl.when(state_ref[unit] < 2)
            def _():
                pltpu.make_async_copy(zeros, outs[0].at[0], sems.at[unit]).wait()

    return pl.pallas_call(
        body,
        grid_spec=pltpu.PrefetchScalarGridSpec(
            num_scalar_prefetch=4,
            grid=(1,),
            in_specs=[pl.BlockSpec(memory_space=pl.ANY)] * (1 + len(after)),
            out_specs=[pl.BlockSpec(memory_space=pl.ANY)] * len(sizes),
            scratch_shapes=[
                pltpu.VMEM((capacity, unit_rows, width), jnp.float32),
                pltpu.VMEM((capacity, unit_rows, width), low),
                pltpu.VMEM((unit_rows, width), low),
                pltpu.SemaphoreType.DMA((capacity,)),
                pltpu.SemaphoreType.DMA((units,)),
            ],
        ),
        out_shape=[jax.ShapeDtypeStruct((size, unit_rows, width), low) for size in sizes],
        compiler_params=pltpu.CompilerParams(vmem_limit_bytes=56 * 2**20),
        cost_estimate=cheap,
        name="pick_units",
    )(slot_unit, state, kind, place, master, *after)


def place_blocks(sources, which, position, parts=1):
    amount = which.shape[0]
    shape = sources[0].shape[1:]
    size = amount // parts

    def body(which_ref, position_ref, *rest):
        ins, outs = rest[: len(sources)], rest[len(sources) : len(sources) + parts]
        held, read, sems = rest[len(sources) + parts :]

        @pl.loop(0, amount)
        def _(i):
            for source, ref in enumerate(ins):

                @pl.when(which_ref[i] == source)
                def _():
                    pltpu.make_async_copy(ref.at[position_ref[i]], held.at[i], read.at[i]).start()

        for part, out in enumerate(outs):

            @pl.loop(0, size)
            def _(j):
                i = part * size + j
                pltpu.make_async_copy(ins[0].at[0], held.at[i], read.at[i]).wait()
                pltpu.make_async_copy(held.at[i], out.at[j], sems.at[i]).start()

        @pl.loop(0, amount)
        def _(i):
            pltpu.make_async_copy(held.at[i], outs[0].at[0], sems.at[i]).wait()

    return pl.pallas_call(
        body,
        grid_spec=pltpu.PrefetchScalarGridSpec(
            num_scalar_prefetch=2,
            grid=(1,),
            in_specs=[pl.BlockSpec(memory_space=pl.ANY)] * len(sources),
            out_specs=[pl.BlockSpec(memory_space=pl.ANY)] * parts,
            scratch_shapes=[
                pltpu.VMEM((amount,) + shape, low),
                pltpu.SemaphoreType.DMA((amount,)),
                pltpu.SemaphoreType.DMA((amount,)),
            ],
        ),
        out_shape=[jax.ShapeDtypeStruct((size,) + shape, low)] * parts,
        compiler_params=pltpu.CompilerParams(vmem_limit_bytes=56 * 2**20),
        cost_estimate=cheap,
        name="place_blocks",
    )(which, position, *sources)


def stack_pairs(pairs):
    shape = (len(pairs),) + pairs[0].shape[1:]

    def body(*refs):
        for i, pair in enumerate(refs[:-2]):
            for half in range(2):
                refs[half - 2][i] = pair[half]

    return pl.pallas_call(
        body,
        out_shape=[jax.ShapeDtypeStruct(shape, low)] * 2,
        cost_estimate=costly,
        name="stack_pairs",
    )(*pairs)


def hops(values, step, turn):
    count = lax.axis_size("tensor")
    if step > 0:
        pairs = [(i, i + 1) for i in range(turn - 1, count - 1)]
    else:
        pairs = [(i, i - 1) for i in range(1, count - turn + 1)]
    return lax.ppermute(values, "tensor", pairs)


fence = lax.optimization_barrier


def in_pool(member, inner, inner_count):
    me = lax.axis_index("dp")
    half, core = member >> 3, ((member >> 2) & 1) ^ (me & 1)
    far_y, far_x = ((member >> 1) & 1) ^ ((me >> 2) & 1), (member & 1) ^ ((me >> 1) & 1)
    where_first = (far_y * 2 + far_x) * inner_count
    where_second = (4 + far_x * 2 + far_y) * inner_count
    return (core, jnp.where(half == 0, where_first, where_second) + inner)


def on_device(
    hidden_in,
    time_embed,
    caption_table,
    caption_ids,
    owners,
    master,
    first_moment,
    second_moment,
    mod_table,
    mod_first,
    mod_second,
    out_grad,
):
    count = lax.axis_size("tensor")
    dp_count = lax.axis_size("dp")
    me_dp = lax.axis_index("dp")
    me_tensor = lax.axis_index("tensor")
    capacity, unit_rows, width = master.shape
    units = owners.shape[0]
    tokens = hidden_in.shape[1]
    text_count = caption_ids.shape[1]
    share = width // count
    per = share // unit_rows
    ups = (units - 8 * per) // 2
    rank_of = ranks_of(owners)
    mine = owners == me_dp
    match = (rank_of[None, :] == jnp.arange(capacity)[:, None]) & mine[None, :]
    filled = jnp.any(match, axis=1)
    unit_of_slot = jnp.sum(jnp.where(match, jnp.arange(units)[None, :], 0), axis=1)

    square = [list(range(i * per, (i + 1) * per)) for i in range(8)]
    group_attn = square[0] + square[1] + square[2] + square[5]
    group_full = square[3] + square[4] + square[6] + square[7]
    group_mlp = list(range(8 * per, units))
    members = len(group_attn)
    plane = dp_count == 8 and members == 16 and len(group_mlp) % dp_count == 0
    member_of = np.zeros(units, np.int32)
    member_of[group_attn] = np.arange(members)
    member_of[group_full] = np.arange(members)
    is_attn = np.zeros(units, bool)
    is_attn[group_attn] = True
    is_mlp = np.zeros(units, bool)
    is_mlp[group_mlp] = True

    latent_in = hidden_in[0].astype(jnp.float32)
    modulate = mod_table + time_embed[0]

    def mod_row(which_row):
        return modulate[which_row][None, :]

    normed_one, inverse_one = layer_norm(latent_in)
    bits = dp_count.bit_length() - 1
    vocab_rows = caption_table.shape[0]

    def caption_terms(ids):
        chosen = ids.reshape(-1) - me_dp * vocab_rows
        onehot = (chosen[:, None] == jnp.arange(vocab_rows)[None, :]).astype(low)
        terms = jnp.dot(onehot, caption_table, preferred_element_type=jnp.float32).astype(low)
        return terms.reshape(dp_count, text_count, -1)

    def modulated(normed):
        return (normed.astype(jnp.float32) * (1.0 + mod_row(1)) + mod_row(0)).astype(low)

    def whole_text(text_ring):
        return from_ring(text_ring, -1).transpose(1, 0, 2).reshape(text_count, width)

    def own_keys(text_low, w_attn):
        return project(text_low, w_attn)[:, 3 * share :].astype(low)

    def exchanged(attended, keys):
        parts = [
            jnp.concatenate([attended[k * tokens : (k + 1) * tokens], keys]) for k in range(count)
        ]
        return [parts[0]] + [shift(parts[k], count - k) for k in range(1, count)]

    where = jnp.stack([me_tensor, me_dp & 1]).astype(jnp.int32)

    n_low = normed_one.astype(low)
    if plane:
        core, far_x, far_y = (
            ((member_of >> 2) & 1) ^ (me_dp & 1),
            (member_of & 1) ^ ((me_dp >> 1) & 1),
            ((member_of >> 1) & 1) ^ ((me_dp >> 2) & 1),
        )
        place = jnp.where(is_attn, far_x * 4 + far_y * 2, 8 + far_y * 4 + far_x * 2)
        place = jnp.where(is_mlp, np.arange(units) - 8 * per, place + (member_of >> 3))
        kind = jnp.where(is_mlp, 0, core)
        slot_mlp = unit_of_slot >= 8 * per
        owned_state = mine.astype(jnp.int32)
        ids = lax.all_gather(caption_ids, "dp", axis=0, tiled=True)
        ids = jnp.take(ids, me_dp ^ jnp.arange(dp_count), axis=0, mode="clip")
        up, down = hops(n_low, 1, 1), hops(n_low, -1, 1)
        kept, given = pick_units(
            master,
            jnp.where(filled & ~slot_mlp, unit_of_slot, -1),
            jnp.where(is_mlp, 2, owned_state),
            kind,
            place,
            (members, members),
        )
        got = swap(given, "dp", 0)
        (mlp_part,) = pick_units(
            master,
            jnp.where(filled & slot_mlp, unit_of_slot, -1),
            jnp.where(is_mlp, owned_state, 2),
            kind,
            place,
            (len(group_mlp),),
            (kept,),
        )
        mlp_part = lax.psum_scatter(mlp_part, "dp", scatter_dimension=0, tiled=True)
        n_up, n_down = [up], [down]
        kept, got, up, down, ids = fence((kept, got, up, down, ids))
        pieces = [kept[i : i + 4] + got[i : i + 4] for i in range(0, members, 4)]
        attn_two, attn_send, full_two, full_send = fence(tuple(pieces))
        up, down = hops(up, 1, 2), hops(down, -1, 2)
        attn_got = swap(attn_send, "dp", 1)
        full_got = swap(full_send, "dp", 2)
        text = caption_terms(ids)
        text = text[0:4] + swap(text[4:8], "dp", 2)
        n_up.append(up), n_down.append(down)
        attn_two, attn_got, full_two, full_got, up, down, text = fence(
            (attn_two, attn_got, full_two, full_got, up, down, text)
        )
        pieces = [x[i : i + 2] + y[i : i + 2] for x, y in ((attn_two, attn_got), (full_two, full_got)) for i in (0, 2)]
        attn_one, attn_send, full_one, full_send = fence(tuple(pieces))
        up, down = hops(up, 1, 3), hops(down, -1, 3)
        attn_got = swap(attn_send, "dp", 2)
        full_got = swap(full_send, "dp", 1)
        text = text[0:2] + swap(text[2:4], "dp", 1)
        n_up.append(up), n_down.append(down)
        attn_one, attn_got, full_one, full_got, up, down, text, mlp_part = fence(
            (attn_one, attn_got, full_one, full_got, up, down, text, mlp_part)
        )
        attn_one, full_one = attn_one + attn_got, full_one + full_got
        n_up[-1], n_down[-1] = up, down
        w_mlp = lax.all_gather(mlp_part, "dp", axis=0, tiled=True)
        first_ring, second_ring = stack_pairs(ring(full_one))
        first = jnp.concatenate([attn_one[0:1], swap(attn_one[0:1], "dp", 1)])
        second = jnp.concatenate([attn_one[1:2], swap(attn_one[1:2], "dp", 2)])
        pool = jnp.concatenate([first, swap(first, "dp", 2), second, swap(second, "dp", 1)])
        other = swap(pool, "dp", 0)
        text = text[0] + swap(text[1], "dp", 0)
        *n_slots, h_one_all = line_slots(
            where, n_low, n_up, n_down, jnp.concatenate([mod_row(0), mod_row(1)])
        )
        n_slots = [n_low] + n_slots
        grad_own = out_grad[0]
        pool, other, first_ring, second_ring, h_one_all, text, grad_own = fence(
            (pool, other, first_ring, second_ring, h_one_all, text, grad_own)
        )
        grad_whole = lax.all_gather(grad_own, "tensor", axis=0)
        first, second = first_ring, second_ring
        first_got = swap(first, "dp", 1)
        second_got = swap(second, "dp", 2)
        text_ring = ring(text)
        (w_attn,) = place_blocks((pool, other), *in_pool(np.arange(members), 0, 1))
        w_attn = w_attn.reshape(-1, width)
        qkv = project(h_one_all, w_attn).astype(low)
        attended, logs = self_attend(qkv, share)
        first = jnp.concatenate([first, first_got])
        second = jnp.concatenate([second, second_got])
        first, second, text_ring, attended, logs, w_attn, w_mlp = fence(
            (first, second, text_ring, attended, logs, w_attn, w_mlp)
        )
        first_far, second_far = swap(first, "dp", 2), swap(second, "dp", 1)
        text_low = whole_text(jnp.stack(text_ring))
        mixed = exchanged(attended, own_keys(text_low, w_attn))
        first_far, second_far, mixed = fence((first_far, second_far, mixed))
        first_other, second_other = swap(first, "dp", 0), swap(second, "dp", 0)
        first_last, second_last = swap(first_far, "dp", 0), swap(second_far, "dp", 0)
        listing = np.arange(count * members)
        matrix, rank, head = listing // (count * per), listing // per % count, listing % per
        slot = lax.rem(me_tensor - rank + count, count)
        which, position = in_pool(matrix * per + head, slot, count)
        blocks = 2 * count
        w_full = place_blocks(
            (first, first_far, second, second_far, first_other, first_last, second_other, second_last),
            which * 4 + position // blocks,
            position % blocks,
            parts=4,
        )
        w_full = [part.reshape(width, width) for part in w_full]
        w_full[3], grad_whole = fence((w_full[3], grad_whole))
    else:
        slots_low = master.astype(low)
        rows = jnp.take(slots_low, rank_of, axis=0, mode="clip")
        rows = lax.psum(jnp.where(mine[:, None, None], rows, jnp.zeros((), low)), "dp")
        w_attn = rows[np.array(group_attn)].reshape(-1, width)
        w_full = lax.all_gather(rows[np.array(group_full)], "tensor", axis=0)
        w_full = w_full.reshape(count, 4, share, width).swapaxes(0, 1).reshape(4, width, width)
        w_full = [w_full[i] for i in range(4)]
        w_mlp = rows[8 * per :]
        n_slots = ring(n_low)
        normed_all = jnp.concatenate(n_slots)
        grad_whole = lax.all_gather(out_grad[0], "tensor", axis=0)
        ids = caption_ids
        for bit in range(bits):
            ids = jnp.concatenate([ids, swap(ids, "dp", bit)])
        text = caption_terms(ids)
        for bit in reversed(range(bits)):
            text = text[: 1 << bit] + swap(text[1 << bit :], "dp", bit)
        text_low = whole_text(jnp.stack(ring(text[0])))
        h_one_all = modulated(normed_all)
        qkv = project(h_one_all, w_attn).astype(low)
        attended, logs = self_attend(qkv, share)
        mixed = exchanged(attended, own_keys(text_low, w_attn))
    w_cross = w_full
    w_out, c_query, c_value, c_out = w_full
    w_mlp = w_mlp.reshape(-1, width)

    rows = jnp.concatenate([mod_row(2), mod_row(3), mod_row(4)])
    (
        branch_one,
        first_low,
        cq_rows,
        ck_rows,
        cv_rows,
        crossed,
        second_res,
        normed_two,
        h_two,
        inverse_two,
    ) = cross_block(
        where, mixed, hidden_in[0], rows, text_low, *w_cross
    )

    h_slots = {0: h_two}
    out_slots = [
        choose(grad_whole, lax.rem(me_tensor - k + count, count), 0) for k in range(count)
    ]
    grad_slots = [(mod_row(5) * item.astype(jnp.float32)).astype(low) for item in out_slots]
    near = [k for k in range(1, count) if 2 * k != count]
    far = [k for k in range(1, count) if 2 * k == count]
    acts, grad_pres, grad_terms, order = [], [], [], []
    for k in near:
        h_slots[k] = shift(h_two, k)
    for members_now in ([0], near, far):
        act, grad_pre, *terms = mlp_core(
            [h_slots[k] for k in members_now],
            [grad_slots[k] for k in members_now],
            w_mlp,
            acts[-1:],
        )
        if members_now == [0]:
            h_two, act = fence((h_two, act))
            for k in far:
                h_slots[k] = shift(h_two, k)
        acts.append(act), grad_pres.append(grad_pre)
        order += members_now
        grad_terms += [
            shift(term, count - k) if k else term for k, term in zip(members_now, terms)
        ]
    mlp_grad = mlp_grads(
        grad_pres, acts, [h_slots[k] for k in order], [grad_slots[k] for k in order]
    ).reshape(-1, unit_rows, width)
    hidden_share = w_mlp.shape[0] // 2
    pieces = [
        [(which, row, 0, hidden_share, hidden_share)]
        for which, act in enumerate(acts)
        for row in range(0, act.shape[0], tokens)
    ]
    branch_terms, branch_sums = ranked_terms(
        where, acts, order, pieces, w_mlp, [out_slots[k] for k in order], "mlp_out"
    )
    branch_row = branch_sums[1]
    grad_terms, branch_terms = fence((grad_terms, branch_terms))
    if plane:
        mlp_sum = lax.psum_scatter(mlp_grad, "dp", scatter_dimension=0, tiled=True)

    (
        first_grad,
        cross_low,
        grad_cq,
        attn_low,
        grad_cv,
        row_sums,
        *grad_mixed,
    ) = cross_back(
        where,
        grad_terms,
        out_grad[0],
        rows,
        normed_two,
        inverse_two,
        branch_one,
        cq_rows,
        ck_rows,
        cv_rows,
        c_out,
        c_query,
        w_out,
        (mlp_grad,),
    )

    grad_parts = [grad_mixed[0]] + [shift(grad_mixed[k], k) for k in range(1, count)]
    full_pairs = [
        ([(item, 0, share, None) for item in mixed], attn_low),
        ([(grad_cq, 0, width, 0)], first_low),
        ([(grad_cv, 0, width, 0)], text_low),
        ([(crossed, 0, width, 0)], cross_low),
    ]
    half = (share // HEAD_DIM // 2) * HEAD_DIM
    spans = [(0, half), (half, share)]

    def attention_pairs(grads, grad_parts):
        keys = sum(item[tokens:].astype(jnp.float32) for item in grad_parts).astype(low)
        pairs = [
            (
                [
                    (item, i * (end - begin), end - begin, begin)
                    for item, (begin, end) in zip(grads, spans)
                ],
                h_one_all,
            )
            for i in range(3)
        ]
        return pairs + [([(keys, 0, share, 0)], text_low)]

    def input_terms(grads):
        pieces = [
            [
                (which, slot * tokens, i * (end - begin), i * share + begin, end - begin)
                for which, (begin, end) in enumerate(spans)
                for i in range(3)
            ]
            for slot in range(count)
        ]
        return ranked_terms(where, grads, range(count), pieces, w_attn, n_slots, "attn_terms")

    if plane:
        x_bit, y_bit = (me_dp >> 1) & 1, (me_dp >> 2) & 1

        def split(total, bit, axis):
            return (choose(total, bit, axis), choose(total, 1 - bit, axis))

        kept, given = outer_halves(where, full_pairs, count, "full_grads")
        got = swap(given, "dp", 0)
        grad_parts, kept, got, branch_terms = fence((grad_parts, kept, got, branch_terms))
        branch_two = lax.psum_scatter(
            branch_terms.reshape(-1, width), "tensor", scatter_dimension=0, tiled=True
        )
        box = (2, count, 2, 2, unit_rows, width)
        bits_here = jnp.stack([x_bit, y_bit]).astype(jnp.int32)
        kept_one, given_one, kept_two, given_two = sum_split(
            bits_here, kept.reshape(box), got.reshape(box)
        )
        got_one, got_two = swap(given_one, "dp", 1), swap(given_two, "dp", 2)
        grads_early = self_attend_back(qkv, grad_parts, attended, logs, share, *spans[0])
        kept_one, got_one, kept_two, got_two, grads_early, grad_parts = fence(
            (kept_one, got_one, kept_two, got_two, grads_early, grad_parts)
        )
        kept_one, given_one = split(kept_one + got_one, y_bit, 1)
        kept_two, given_two = split(kept_two + got_two, x_bit, 1)
        kept_one, given_one, kept_two, given_two, grad_parts = fence(
            (kept_one, given_one, kept_two, given_two, grad_parts)
        )
        got_one, got_two = swap(given_one, "dp", 2), swap(given_two, "dp", 1)
        grads_late = self_attend_back(qkv, grad_parts, attended, logs, share, *spans[1])
        kept_one, got_one, kept_two, got_two, grads_early, grads_late, mlp_sum = fence(
            (kept_one, got_one, kept_two, got_two, grads_early, grads_late, mlp_sum)
        )
        mlp_sum = lax.all_gather(mlp_sum, "dp", axis=0, tiled=True)
        full_parts = to_ring(jnp.stack([kept_one + got_one, kept_two + got_two], axis=1))
        full_parts = [full_parts[k] for k in range(count)]
        full_parts, grads_early, grads_late = fence((full_parts, grads_early, grads_late))
        grads_qkv = [grads_early, grads_late]
        full_got = [shift(full_parts[k], k) for k in range(1, count)]
        attn_kept, attn_given = outer_halves(
            where, attention_pairs(grads_qkv, grad_parts), 1, "attn_grads"
        )
        attn_got = swap(attn_given, "dp", 0)
        grad_h_terms, grad_h_sums = input_terms(grads_qkv)
        mod_terms = jnp.concatenate([grad_h_sums, row_sums, branch_row[None]])
        grad_h_one = lax.psum_scatter(
            grad_h_terms.reshape(-1, width), "tensor", scatter_dimension=0, tiled=True
        )
        attn_kept, attn_got, mod_terms, branch_two = fence(
            (attn_kept, attn_got, mod_terms, branch_two)
        )
        attn_all = (attn_kept + attn_got).reshape(2, 2, 2, unit_rows, width)
        one_kept, one_given = split(attn_all[0], x_bit, 1)
        two_kept, two_given = split(attn_all[1], y_bit, 0)
        one_got, two_got = swap(one_given, "dp", 1), swap(two_given, "dp", 2)
        mod_terms = mod_terms + swap(mod_terms, "dp", 0)
        full_own = full_parts[0]
        one_kept, one_got, two_kept, two_got, mod_terms, full_own, full_got = fence(
            (one_kept, one_got, two_kept, two_got, mod_terms, full_own, full_got)
        )
        full_sum = full_own.astype(jnp.float32)
        for part in full_got:
            full_sum = full_sum + part.astype(jnp.float32)
        full_sum = full_sum.astype(low)
        one_kept, one_given = split(one_kept + one_got, y_bit, 0)
        two_kept, two_given = split(two_kept + two_got, x_bit, 0)
        one_got, two_got = swap(one_given, "dp", 2), swap(two_given, "dp", 1)
        mod_terms = mod_terms + swap(mod_terms, "dp", 1)
        one_kept, one_got, two_kept, two_got, full_sum, mod_terms, mlp_sum = fence(
            (one_kept, one_got, two_kept, two_got, full_sum, mod_terms, mlp_sum)
        )
        first = jnp.stack([one_kept + one_got, full_sum[0]])
        second = jnp.stack([two_kept + two_got, full_sum[1]])
        first_got, second_got = swap(first, "dp", 1), swap(second, "dp", 2)
        first = jnp.concatenate([first, first_got])
        second = jnp.concatenate([second, second_got])
        mod_terms = mod_terms + swap(mod_terms, "dp", 2)
        first, second, mod_terms = fence((first, second, mod_terms))
        first_far, second_far = swap(first, "dp", 2), swap(second, "dp", 1)
        mod_terms = mod_terms + swap(mod_terms, "tensor", 0)
        first, first_far, second, second_far, mod_terms, grad_h_one = fence(
            (first, first_far, second, second_far, mod_terms, grad_h_one)
        )
        pool = jnp.concatenate([first, first_far, second, second_far])
        other = swap(pool, "dp", 0)
        for bit in range(1, count.bit_length() - 1):
            mod_terms = mod_terms + swap(mod_terms, "tensor", bit)
        pool, other, mod_grad = fence((pool, other, mod_terms))
        which, position = in_pool(member_of, np.where(is_attn, 0, 1), 2)
        which = jnp.where(is_mlp, 2, which)
        position = jnp.where(is_mlp, np.arange(units) - 8 * per, position)
        own = jnp.sum(jnp.where(match[:, :, None], jnp.stack([which, position], 1)[None], 0), axis=1)
        new_first, new_second, new_master = update_slots(
            master,
            first_moment,
            second_moment,
            filled.astype(jnp.int32),
            own[:, 0],
            own[:, 1],
            (pool, other, mlp_sum),
        )
    else:
        branch_two = lax.psum_scatter(
            branch_terms.reshape(-1, width), "tensor", scatter_dimension=0, tiled=True
        )
        grads_qkv = [self_attend_back(qkv, grad_parts, attended, logs, share, *span) for span in spans]
        attn_grads = [
            outer(array[:, lane : lane + lanes], right).astype(low)
            for left, right in attention_pairs(grads_qkv, grad_parts)
            for array, lane, lanes, row in left
        ]
        grad_h_terms, grad_h_sums = input_terms(grads_qkv)
        grad_h_one = lax.psum_scatter(
            grad_h_terms.reshape(-1, width), "tensor", scatter_dimension=0, tiled=True
        )
        mixed_all = from_ring(jnp.stack([item[:tokens] for item in mixed]), 1)
        mixed_all = mixed_all.transpose(1, 0, 2).reshape(tokens, width)
        full_grads = [outer(mixed_all, attn_low)]
        full_grads += [outer(left[0][0], right) for left, right in full_pairs[1:]]
        full_sum = [g.astype(low).reshape(count, share, width) for g in full_grads]
        full_sum = jnp.stack(full_sum, axis=1)
        full_sum = lax.psum_scatter(full_sum, "tensor", scatter_dimension=0, tiled=True)
        order = np.array(group_attn + group_full + group_mlp)
        sums = jnp.concatenate(
            [jnp.concatenate(attn_grads), full_sum.reshape(-1, width), mlp_grad.reshape(-1, width)]
        )
        sums = lax.psum(sums.reshape(units, unit_rows, width), "dp")
        owned = jnp.take(sums, jnp.array(np.argsort(order))[unit_of_slot], axis=0, mode="clip")
        mod_grad = total_sum(jnp.concatenate([grad_h_sums, row_sums, branch_row[None]]))
        new_first, new_second, new_master = adamw(
            master,
            first_moment,
            second_moment,
            owned.astype(jnp.float32),
            filled.astype(jnp.float32)[:, None, None],
            rate,
        )
    branch_two, second_res, grad_h_one, new_first = fence(
        (branch_two, second_res, grad_h_one, new_first)
    )
    grad_h_one = grad_h_one.astype(jnp.float32)
    block_out = second_res + mod_row(5) * branch_two.astype(jnp.float32)
    input_grad = first_grad + norm_back(grad_h_one, normed_one, inverse_one, mod_row(1))
    mod_new_first, mod_new_second, mod_new = adamw(
        mod_table, mod_first, mod_second, mod_grad, 1.0, table_rate
    )
    return (
        block_out[None],
        input_grad[None],
        new_first,
        new_second,
        new_master,
        mod_new_first,
        mod_new_second,
        mod_new,
    )


def solution(mesh):
    in_specs = (
        P("dp", "tensor", None),
        P("dp", None, None),
        P("dp", "tensor"),
        P("dp", None),
        P(),
        P("dp", "tensor", None),
        P("dp", "tensor", None),
        P("dp", "tensor", None),
        P(),
        P(),
        P(),
        P("dp", "tensor", None),
    )
    out_specs = (
        P("dp", "tensor", None),
        P("dp", "tensor", None),
        P("dp", "tensor", None),
        P("dp", "tensor", None),
        P("dp", "tensor", None),
        P(),
        P(),
        P(),
    )
    return jax.shard_map(
        on_device, mesh=mesh, in_specs=in_specs, out_specs=out_specs, check_vma=False
    )
```

```python
import math

import jax
import jax.numpy as jnp
import numpy as np
from jax import lax
from jax.experimental import pallas as pl
from jax.experimental.pallas import tpu as pltpu
from jax.sharding import PartitionSpec as P

HEAD_DIM = 72
STEP = 10


norm_eps = 1e-06
beta_one = 0.9
beta_two = 0.999
rate = 0.03
table_rate = 0.3
decay = 0.01
adam_eps = 1e-08
low = jnp.bfloat16


def ranks_of(owners):
    index = jnp.arange(owners.shape[0])
    before = (owners[None, :] == owners[:, None]) & (index[None, :] < index[:, None])
    return jnp.sum(before.astype(jnp.int32), axis=1)


def layer_norm(values):
    center = values - jnp.mean(values, axis=-1, keepdims=True)
    inverse = lax.rsqrt(jnp.mean(center * center, axis=-1, keepdims=True) + norm_eps)
    return (center * inverse, inverse)


def norm_back(grad_rows, normed, inverse, scale_row):
    scaled = grad_rows * (1.0 + scale_row)
    mean_one = jnp.mean(scaled, axis=-1, keepdims=True)
    mean_two = jnp.mean(scaled * normed, axis=-1, keepdims=True)
    return inverse * (scaled - mean_one - normed * mean_two)


def project(rows, weight):
    return jnp.einsum("ld,rd->lr", rows, weight, preferred_element_type=jnp.float32)


def expand(rows, weight):
    return jnp.einsum("lr,rd->ld", rows, weight, preferred_element_type=jnp.float32)


def outer(left, right):
    return jnp.einsum("lr,ld->rd", left, right, preferred_element_type=jnp.float32)


def shift(values, step):
    count = lax.axis_size("tensor")
    return lax.ppermute(values, "tensor", [(i, (i + step) % count) for i in range(count)])


def ring(values):
    return [values] + [shift(values, k) for k in range(1, lax.axis_size("tensor"))]


def to_ring(stacked):
    count = stacked.shape[0]
    twice = jnp.concatenate([stacked, stacked], axis=0)
    return lax.dynamic_slice_in_dim(twice, lax.axis_index("tensor"), count, 0)


def from_ring(stacked, sign):
    count = stacked.shape[0]
    me = lax.axis_index("tensor")
    place = lax.rem(sign * (jnp.arange(count) - me) + 2 * count, count)
    return jnp.take(stacked, place, axis=0, mode="clip")


cheap = pl.CostEstimate(flops=1000, bytes_accessed=1000, transcendentals=0)
costly = pl.CostEstimate(flops=10**10, bytes_accessed=10**7, transcendentals=0)


def self_attend(qkv, share):
    length = qkv.shape[0]
    rows = min(512, length)
    curve = HEAD_DIM ** (-0.5) * math.log2(math.e)
    heads = share // HEAD_DIM

    def body(qkv_ref, out_ref, log_ref):
        @pl.loop(0, length // rows)
        def _(step):
            here = pl.ds(pl.multiple_of(step * rows, rows), rows)
            parts = []
            for head in range(heads):
                at = head * HEAD_DIM
                q = qkv_ref[here, at : at + HEAD_DIM]
                k = qkv_ref[:, share + at : share + at + HEAD_DIM]
                v = qkv_ref[:, 2 * share + at : 2 * share + at + HEAD_DIM]
                scores = dot(k, q, nt)
                top = jnp.max(scores, axis=0, keepdims=True)
                expo = jnp.exp2((scores - top) * curve)
                total = jnp.sum(expo, axis=0, keepdims=True)
                log_ref[head : head + 1, here] = top * curve + jnp.log2(total)
                parts.append((dot(v, expo.astype(low), tn) * (1.0 / total)).T)
            out_ref[here, :] = jnp.concatenate(parts, axis=1).astype(low)

    return pl.pallas_call(
        body,
        out_shape=[
            jax.ShapeDtypeStruct((length, share), low),
            jax.ShapeDtypeStruct((heads, length), jnp.float32),
        ],
        compiler_params=pltpu.CompilerParams(vmem_limit_bytes=40 * 2**20),
        cost_estimate=cheap,
        name="self_attend",
    )(qkv)


def self_attend_back(qkv, grads, mixed, logs, share, begin, end):
    length = qkv.shape[0]
    rows = length // len(grads)
    span = end - begin
    scale = HEAD_DIM ** (-0.5)
    curve = scale * math.log2(math.e)

    def body(qkv_ref, mixed_ref, log_ref, *refs):
        grad_refs, (out_ref, grad_k, grad_v) = refs[: len(grads)], refs[len(grads) :]
        for step, grad_ref in enumerate(grad_refs):
            here = slice(step * rows, (step + 1) * rows)
            parts = []
            for head, at in enumerate(range(begin, end, HEAD_DIM)):
                q = qkv_ref[here, at : at + HEAD_DIM]
                k = qkv_ref[:, share + at : share + at + HEAD_DIM]
                v = qkv_ref[:, 2 * share + at : 2 * share + at + HEAD_DIM]
                g = grad_ref[0:rows, at : at + HEAD_DIM]
                o = mixed_ref[here, at : at + HEAD_DIM]
                inner = g.astype(jnp.float32) * o.astype(jnp.float32)
                inner = jnp.sum(inner.T, axis=0, keepdims=True)
                which = begin // HEAD_DIM + head
                probs = jnp.exp2(dot(k, q, nt) * curve - log_ref[which : which + 1, here])
                grad_scores = (probs * (dot(v, g, nt) - inner)).astype(low)
                to_v = dot(probs.astype(low), g)
                to_k = dot(grad_scores, q)
                if step:
                    grad_v[head] += to_v
                    grad_k[head] += to_k
                else:
                    grad_v[head] = to_v
                    grad_k[head] = to_k
                parts.append((dot(k, grad_scores, tn) * scale).T)
            out_ref[here, 0:span] = jnp.concatenate(parts, axis=1).astype(low)
        heads = range(span // HEAD_DIM)
        both = [grad_k[head] * scale for head in heads]
        out_ref[:, span : 2 * span] = jnp.concatenate(both, axis=1).astype(low)
        both = [grad_v[head] for head in heads]
        out_ref[:, 2 * span :] = jnp.concatenate(both, axis=1).astype(low)

    return pl.pallas_call(
        body,
        out_shape=jax.ShapeDtypeStruct((length, 3 * span), low),
        scratch_shapes=[pltpu.VMEM((span // HEAD_DIM, length, HEAD_DIM), jnp.float32)] * 2,
        compiler_params=pltpu.CompilerParams(vmem_limit_bytes=40 * 2**20),
        cost_estimate=costly,
        name="self_attend_back",
    )(qkv, mixed, logs, *grads)


def mlp_core(rows_in, grads_in, w_mlp, after):
    groups = len(rows_in)
    tokens, width = rows_in[0].shape
    hidden = w_mlp.shape[0] // 2
    chunk = 384 if hidden % 384 == 0 else hidden
    steps = hidden // chunk
    curve = 0.7978845608028654

    def body(*refs):
        rows, grads = refs[:groups], refs[groups : 2 * groups]
        up, down = refs[2 * groups : 2 * groups + 2]
        act, grad_pre, *outs = refs[2 * groups + 2 + len(after) : -1]
        total = refs[-1]
        step = pl.program_id(0)
        for i in range(groups):
            pre = lax.dot_general(
                rows[i][...], up[...], (((1,), (1,)), ((), ())), preferred_element_type=jnp.float32
            )
            square = pre * pre
            bend = jnp.tanh(curve * pre * (1.0 + 0.044715 * square))
            half = 0.5 * (1.0 + bend)
            here = pl.ds(i * tokens, tokens)
            act[here, :] = (pre * half).astype(low)
            slope = half + (0.5 * curve) * pre * (1.0 - bend * bend) * (1.0 + 0.134145 * square)
            grad_act = lax.dot_general(
                grads[i][...], down[...], (((1,), (1,)), ((), ())), preferred_element_type=jnp.float32
            )
            grad_low = (grad_act * slope).astype(low)
            grad_pre[here, :] = grad_low
            term = jnp.dot(grad_low, up[...], preferred_element_type=jnp.float32)

            @pl.when(step == 0)
            def _():
                total[here, :] = term

            @pl.when(step > 0)
            def _():
                total[here, :] += term

            @pl.when(step == steps - 1)
            def _():
                outs[i][...] = total[here, :].astype(low)

    whole = pl.BlockSpec((tokens, width), lambda s: (0, 0))
    across = pl.BlockSpec((groups * tokens, chunk), lambda s: (0, s))
    return pl.pallas_call(
        body,
        grid=(steps,),
        in_specs=[whole] * (2 * groups)
        + [
            pl.BlockSpec((chunk, width), lambda s: (s, 0)),
            pl.BlockSpec((chunk, width), lambda s: (steps + s, 0)),
        ]
        + [pl.BlockSpec(memory_space=pl.ANY)] * len(after),
        out_specs=[across, across] + [whole] * groups,
        out_shape=[jax.ShapeDtypeStruct((groups * tokens, hidden), low)] * 2
        + [jax.ShapeDtypeStruct((tokens, width), low)] * groups,
        scratch_shapes=[pltpu.VMEM((groups * tokens, width), jnp.float32)],
        compiler_params=pltpu.CompilerParams(vmem_limit_bytes=60 * 2**20),
        cost_estimate=cheap,
        name="mlp_core",
    )(*rows_in, *grads_in, w_mlp, w_mlp, *after)


nt = (((1,), (1,)), ((), ()))
tn = (((0,), (0,)), ((), ()))


def dot(left, right, dims=(((1,), (0,)), ((), ()))):
    return lax.dot_general(left, right, dims, preferred_element_type=jnp.float32)


def softmax_keys(keys, queries):
    scores = dot(keys, queries, nt) * HEAD_DIM ** (-0.5)
    expo = jnp.exp(scores - jnp.max(scores, axis=0, keepdims=True))
    return expo * (1.0 / jnp.sum(expo, axis=0, keepdims=True))


def cuts_of(width):
    size = 384 if width % 384 == 0 else width
    return [slice(i, i + size) for i in range(0, width, size)]


def in_smem():
    return pl.BlockSpec(memory_space=pltpu.SMEM)


def in_vmem():
    return pl.BlockSpec(memory_space=pltpu.VMEM)


def line_slots(place, own, ups, downs, rows):
    count = len(ups) + 1
    tokens, width = own.shape

    def body(place_ref, *refs):
        own_ref, up_refs, down_refs = refs[0], refs[1:count], refs[count : 2 * count - 1]
        rows_ref, outs, out = refs[2 * count - 1], refs[2 * count : -1], refs[-1]
        me = place_ref[0]

        def modulate(slot, ref):
            value = ref[...].astype(jnp.float32)
            value = value * (1.0 + rows_ref[1:2, :]) + rows_ref[0:1, :]
            out[slot * tokens : (slot + 1) * tokens, :] = value.astype(low)

        modulate(0, own_ref)
        for k in range(1, count):
            for side, ref in ((me >= k, up_refs[k - 1]), (me < k, down_refs[count - k - 1])):

                @pl.when(side)
                def _():
                    outs[k - 1][...] = ref[...]
                    modulate(k, ref)

    shapes = [(tokens, width)] * (count - 1) + [(count * tokens, width)]
    return pl.pallas_call(
        body,
        in_specs=[in_smem()] + [in_vmem()] * (2 * count),
        out_shape=[jax.ShapeDtypeStruct(shape, low) for shape in shapes],
        compiler_params=pltpu.CompilerParams(vmem_limit_bytes=32 * 2**20),
        cost_estimate=cheap,
        name="line_slots",
    )(place, own, *ups, *downs, rows)


def cross_block(place, mixed, hidden, rows, text, w_out, c_query, c_value, c_out):
    count, share = len(mixed), mixed[0].shape[1]
    tokens, width = hidden.shape
    words = text.shape[0]
    per = share // HEAD_DIM

    def body(place_ref, *refs):
        parts = refs[:count]
        x_ref, rows_ref, text_ref = refs[count : count + 3]
        far = refs[count + 3 : count + 7]
        outs = refs[count + 7 : count + 16]
        inverse = refs[count + 16]
        wo, wq, wv, wc, *own = refs[count + 17 : -3]
        held, read, sems = refs[-3:]
        branch, res_low, cq, ck, cv, crossed, res, normed, out = own
        me = place_ref[0]
        loads = [
            pltpu.make_async_copy(source, target, read.at[i])
            for i, (source, target) in enumerate(zip(far, (wo, wq, wv, wc)))
        ]
        stores = [
            pltpu.make_async_copy(source, target, sems.at[i])
            for i, (source, target) in enumerate(zip(own, outs))
        ]
        for load in loads:
            load.start()
        loads[0].wait()
        for cut in cuts_of(width):
            total = jnp.zeros((tokens, cut.stop - cut.start), jnp.float32)
            for k in range(count):
                rank = lax.rem(me + k, count)
                here = pl.ds(pl.multiple_of(rank * share, 32), share)
                total += dot(parts[k][0:tokens, :], wo[here, cut])
            branch[:, cut] = total
            first = x_ref[:, cut].astype(jnp.float32) + rows_ref[0:1, cut] * total
            res[:, cut] = first
            res_low[:, cut] = first.astype(low)
        stores[0].start()
        stores[1].start()
        loads[1].wait()
        loads[2].wait()
        for cut in cuts_of(width):
            cq[:, cut] = dot(res_low[...], wq[cut, :], nt).astype(low)
            cv[:, cut] = dot(text_ref[...], wv[cut, :], nt).astype(low)
        for k in range(count):
            held[lax.rem(me + k, count)] = parts[k][tokens:, :]
        ck[...] = jnp.concatenate([held[rank] for rank in range(count)], axis=1)
        for i in (2, 3, 4):
            stores[i].start()
        parts_out = []
        for at in range(0, width, HEAD_DIM):
            head = slice(at, at + HEAD_DIM)
            probs = softmax_keys(ck[:, head], cq[:, head]).astype(low)
            parts_out.append(dot(cv[:, head], probs, tn).T)
        crossed[...] = jnp.concatenate(parts_out, axis=1).astype(low)
        stores[5].start()
        loads[3].wait()
        for cut in cuts_of(width):
            res[:, cut] += dot(crossed[...], wc[:, cut])
        second = res[...]
        center = second - jnp.mean(second, axis=-1, keepdims=True)
        spread = lax.rsqrt(jnp.mean(center * center, axis=-1, keepdims=True) + norm_eps)
        inverse[...] = spread
        scaled = center * spread
        normed[...] = scaled
        stores[6].start()
        stores[7].start()
        out[...] = (scaled * (1.0 + rows_ref[2:3, :]) + rows_ref[1:2, :]).astype(low)
        stores[8].start()
        for store in stores:
            store.wait()

    wide = (tokens, width)
    shapes = [
        (wide, jnp.float32),
        (wide, low),
        (wide, low),
        ((words, width), low),
        ((words, width), low),
        (wide, low),
        (wide, jnp.float32),
        (wide, jnp.float32),
        (wide, low),
    ]
    anywhere = pl.BlockSpec(memory_space=pl.ANY)
    return pl.pallas_call(
        body,
        in_specs=[in_smem()] + [in_vmem()] * (count + 3) + [anywhere] * 4,
        out_specs=[anywhere] * len(shapes) + [in_vmem()],
        out_shape=[jax.ShapeDtypeStruct(*item) for item in shapes]
        + [jax.ShapeDtypeStruct((tokens, 1), jnp.float32)],
        scratch_shapes=[pltpu.VMEM((width, width), low)] * 4
        + [pltpu.VMEM(*item) for item in shapes]
        + [
            pltpu.VMEM((count, words, share), low),
            pltpu.SemaphoreType.DMA((4,)),
            pltpu.SemaphoreType.DMA((len(shapes),)),
        ],
        compiler_params=pltpu.CompilerParams(vmem_limit_bytes=60 * 2**20),
        cost_estimate=cheap,
        name="cross_block",
    )(place, *mixed, hidden, rows, text, w_out, c_query, c_value, c_out)


def cross_back(
    place, terms, grad, rows, normed, inverse, branch, cq, ck, cv, c_out, c_query, w_out, after
):
    count = len(terms)
    tokens, width = grad.shape
    words = ck.shape[0]
    share = width // count
    scale = HEAD_DIM ** (-0.5)

    def body(place_ref, *refs):
        parts = refs[:count]
        grad_ref, rows_ref, i_ref, k_ref, v_ref = refs[count : count + 5]
        far = refs[count + 5 : count + 11]
        refs = refs[: count + 11] + refs[count + 11 + len(after) :]
        stored = refs[count + 11 : count + 15]
        grad_v, sums = refs[count + 15 : count + 17]
        outs = refs[count + 17 : 2 * count + 17]
        near = refs[2 * count + 17 : 2 * count + 23]
        n_ref, wc, q_ref, wq, wo, b_ref = near
        own = refs[2 * count + 23 : 2 * count + 27]
        first, cross_low, grad_q, attn_low = own
        back, held, read, sems = refs[2 * count + 27 :]
        me = place_ref[0]
        loads = [
            pltpu.make_async_copy(source, target, read.at[i])
            for i, (source, target) in enumerate(zip(far, near))
        ]
        stores = [
            pltpu.make_async_copy(source, target, sems.at[i])
            for i, (source, target) in enumerate(zip(own, stored))
        ]
        for load in loads:
            load.start()
        loads[0].wait()
        total = parts[0][...].astype(jnp.float32)
        for part in parts[1:]:
            total += part[...].astype(jnp.float32)
        n = n_ref[...]
        sums[1:2, :] = jnp.sum(total, axis=0, keepdims=True)
        sums[2:3, :] = jnp.sum(total * n, axis=0, keepdims=True)
        second = grad_ref[...].astype(jnp.float32) + norm_back(total, n, i_ref[...], rows_ref[2:3, :])
        first[...] = second
        cross_low[...] = second.astype(low)
        stores[1].start()
        loads[1].wait()
        loads[2].wait()
        for cut in cuts_of(width):
            back[:, cut] = dot(cross_low[...], wc[cut, :], nt).astype(low)
        grads = ([], [], [])
        for at in range(0, width, HEAD_DIM):
            head = slice(at, at + HEAD_DIM)
            q, k, v, g = q_ref[:, head], k_ref[:, head], v_ref[:, head], back[:, head]
            probs = softmax_keys(k, q)
            grad_probs = dot(v, g, nt)
            inner = jnp.sum(probs * grad_probs, axis=0, keepdims=True)
            grad_scores = (probs * (grad_probs - inner)).astype(low)
            grads[0].append((dot(k, grad_scores, tn) * scale).T)
            grads[1].append(dot(grad_scores, q) * scale)
            grads[2].append(dot(probs.astype(low), g))
        grad_q[...] = jnp.concatenate(grads[0], axis=1).astype(low)
        grad_v[...] = jnp.concatenate(grads[2], axis=1).astype(low)
        heads = share // HEAD_DIM
        for rank in range(count):
            pieces = grads[1][rank * heads : (rank + 1) * heads]
            held[rank] = jnp.concatenate(pieces, axis=1).astype(low)
        stores[2].start()
        for load in loads[3:]:
            load.wait()
        for cut in cuts_of(width):
            whole = first[:, cut] + dot(grad_q[...], wq[:, cut])
            first[:, cut] = whole
            attn_low[:, cut] = (rows_ref[0:1, cut] * whole).astype(low)
            sums[0:1, cut] = jnp.sum(b_ref[:, cut] * whole, axis=0, keepdims=True)
        stores[0].start()
        stores[3].start()
        for k in range(count):
            rank = lax.rem(me + k, count)
            here = pl.ds(pl.multiple_of(rank * share, 32), share)
            outs[k][0:tokens, :] = dot(attn_low[...], wo[here, :], nt).astype(low)
            outs[k][tokens:, :] = held[rank]
        for store in stores:
            store.wait()

    wide, square = (tokens, width), (width, width)
    shapes = [
        (wide, jnp.float32),
        (wide, low),
        (wide, low),
        (wide, low),
        ((words, width), low),
        ((3, width), jnp.float32),
    ] + [((tokens + words, share), low)] * count
    anywhere = pl.BlockSpec(memory_space=pl.ANY)
    loaded = [
        pltpu.VMEM(wide, jnp.float32),
        pltpu.VMEM(square, low),
        pltpu.VMEM(wide, low),
        pltpu.VMEM(square, low),
        pltpu.VMEM(square, low),
        pltpu.VMEM(wide, jnp.float32),
    ]
    return pl.pallas_call(
        body,
        in_specs=[in_smem()] + [in_vmem()] * (count + 5) + [anywhere] * (6 + len(after)),
        out_specs=[anywhere] * 4 + [in_vmem()] * (2 + count),
        out_shape=[jax.ShapeDtypeStruct(*item) for item in shapes],
        scratch_shapes=loaded
        + [pltpu.VMEM(*item) for item in shapes[:4]]
        + [
            pltpu.VMEM(wide, low),
            pltpu.VMEM((count, words, share), low),
            pltpu.SemaphoreType.DMA((6,)),
            pltpu.SemaphoreType.DMA((4,)),
        ],
        compiler_params=pltpu.CompilerParams(vmem_limit_bytes=60 * 2**20),
        cost_estimate=costly,
        name="cross_back",
    )(
        place,
        *terms,
        grad,
        rows,
        inverse,
        ck,
        cv,
        normed,
        c_out,
        cq,
        c_query,
        w_out,
        branch,
        *after,
    )


def outer_halves(place, pairs, parts, name):
    width = pairs[0][1].shape[1]
    high = [sum(piece[2] for piece in left) for left, _ in pairs]
    size = high[0] // parts
    tokens = [right.shape[0] for _, right in pairs]
    flat = []

    def index_of(array):
        for i, other in enumerate(flat):
            if other is array:
                return i
        flat.append(array)
        return len(flat) - 1

    plans = [
        ([(index_of(array), *rest) for array, *rest in left], index_of(right))
        for left, right in pairs
    ]
    amount = len(pairs)

    def body(place_ref, *refs):
        ins, (kept, given), (held, sems) = refs[: len(flat)], refs[len(flat) :][:2], refs[-2:]
        turned = refs[len(flat) + 2 : -2]
        me, core = place_ref[0], place_ref[1]
        for i, (left, right) in enumerate(plans):
            for k, (which, lane, lanes, row) in enumerate(left):
                piece = ins[which][0 : tokens[i], lane : lane + lanes]
                piece = piece.astype(jnp.float32).T.astype(low)
                if row is None:
                    rank = lax.rem(me + k, len(left))
                    turned[i][pl.ds(pl.multiple_of(rank * lanes, 32), lanes), :] = piece
                else:
                    turned[i][row : row + lanes, :] = piece
            for part in range(parts):
                at = i * parts + part
                tile = dot(turned[i][part * size : (part + 1) * size, :], ins[right][...])
                held[at] = tile.astype(low)
                for out, side in ((kept, 0), (given, 1)):

                    @pl.when((core ^ (i & 1)) == side)
                    def _():
                        pltpu.make_async_copy(
                            held.at[at], out.at[i // 2, part], sems.at[at]
                        ).start()

        for at in range(amount * parts):
            pltpu.make_async_copy(held.at[at], kept.at[0, 0], sems.at[at]).wait()

    out = jax.ShapeDtypeStruct((amount // 2, parts, size, width), low)
    return pl.pallas_call(
        body,
        in_specs=[in_smem()] + [in_vmem()] * len(flat),
        out_specs=[pl.BlockSpec(memory_space=pl.ANY)] * 2,
        out_shape=[out, out],
        scratch_shapes=[pltpu.VMEM((high[i], tokens[i]), low) for i in range(amount)]
        + [
            pltpu.VMEM((amount * parts, size, width), low),
            pltpu.SemaphoreType.DMA((amount * parts,)),
        ],
        compiler_params=pltpu.CompilerParams(vmem_limit_bytes=60 * 2**20),
        cost_estimate=cheap if parts > 1 else costly,
        name=name,
    )(place, *flat)


def mlp_grads(grad_pres, acts, rows_in, grads_in):
    pieces, rights = len(acts), len(rows_in)
    tokens, width = rows_in[0].shape
    hidden = acts[0].shape[1]
    chunk = 384 if hidden % 384 == 0 else hidden
    steps = hidden // chunk

    def body(*refs):
        step = pl.program_id(0)
        lefts_up, lefts_down = refs[:pieces], refs[pieces : 2 * pieces]
        rights_up = refs[2 * pieces : 2 * pieces + rights]
        rights_down = refs[2 * pieces + rights : -1]
        out = refs[-1]

        def terms(lefts, turn, others):
            here = pl.ds(pl.multiple_of(turn * chunk, chunk), chunk)
            total = jnp.zeros((chunk, width), jnp.float32)
            cursor = 0
            for left in lefts:
                for i in range(left.shape[0] // tokens):
                    total += dot(left[i * tokens : (i + 1) * tokens, here], others[cursor][...], tn)
                    cursor += 1
            out[...] = total.astype(low)

        @pl.when(step < steps)
        def _():
            terms(lefts_up, step, rights_up)

        @pl.when(step >= steps)
        def _():
            terms(lefts_down, step - steps, rights_down)

    arrays = (*grad_pres, *acts, *rows_in, *grads_in)
    chunked = pl.BlockSpec((chunk, width), lambda s: (s, 0))
    return pl.pallas_call(
        body,
        grid=(2 * steps,),
        in_specs=[pl.BlockSpec(array.shape, lambda s: (0, 0)) for array in arrays],
        out_specs=chunked,
        out_shape=jax.ShapeDtypeStruct((2 * hidden, width), low),
        compiler_params=pltpu.CompilerParams(vmem_limit_bytes=60 * 2**20),
        cost_estimate=cheap,
        name="mlp_grads",
    )(*arrays)


def ranked_terms(place, lefts, order, pieces, weight, factors, name):
    tokens, width = factors[0].shape
    count = len(factors)

    def body(place_ref, *refs):
        ins, weight_ref = refs[: len(lefts)], refs[len(lefts)]
        others = refs[len(lefts) + 1 : len(lefts) + 1 + count]
        out, sums = refs[-2:]
        me = place_ref[0]
        for i, slot in enumerate(order):
            rank = lax.rem(me - slot + count, count)
            for cut in cuts_of(width):
                term = jnp.zeros((tokens, cut.stop - cut.start), jnp.float32)
                for which, row, lane, start, depth in pieces[i]:
                    term += dot(
                        ins[which][row : row + tokens, lane : lane + depth],
                        weight_ref[start : start + depth, cut],
                    )
                out[rank, :, cut] = term.astype(low)
                one = jnp.sum(term, axis=0, keepdims=True)
                two = jnp.sum(term * others[i][:, cut].astype(jnp.float32), axis=0, keepdims=True)
                if i:
                    one, two = one + sums[0:1, cut], two + sums[1:2, cut]
                sums[0:1, cut], sums[1:2, cut] = one, two

    return pl.pallas_call(
        body,
        in_specs=[in_smem()] + [in_vmem()] * (len(lefts) + 1 + count),
        out_shape=[
            jax.ShapeDtypeStruct((count, tokens, width), low),
            jax.ShapeDtypeStruct((2, width), jnp.float32),
        ],
        compiler_params=pltpu.CompilerParams(vmem_limit_bytes=60 * 2**20),
        cost_estimate=cheap if len(lefts) > 2 else costly,
        name=name,
    )(place, *lefts, weight, *factors)


def sum_split(place, kept, got):
    count, unit_rows, width = kept.shape[1], kept.shape[4], kept.shape[5]

    def body(place_ref, one, two, keep_x, give_x, keep_y, give_y):
        x, y = place_ref[0], place_ref[1]

        def total(*index):
            return (one[index].astype(jnp.float32) + two[index].astype(jnp.float32)).astype(low)

        for j in range(2):
            keep_x[0, j] = total(0, 0, j, x)
            give_x[0, j] = total(0, 0, j, 1 - x)
            keep_y[0, j] = total(1, 0, y, j)
            give_y[0, j] = total(1, 0, 1 - y, j)

    block = pl.BlockSpec((2, 1, 2, 2, unit_rows, width), lambda r, *_: (0, r, 0, 0, 0, 0))
    part = pl.BlockSpec((1, 2, unit_rows, width), lambda r, *_: (r, 0, 0, 0))
    return pl.pallas_call(
        body,
        grid_spec=pltpu.PrefetchScalarGridSpec(
            num_scalar_prefetch=1, grid=(count,), in_specs=[block] * 2, out_specs=[part] * 4
        ),
        out_shape=[jax.ShapeDtypeStruct((count, 2, unit_rows, width), low)] * 4,
        compiler_params=pltpu.CompilerParams(vmem_limit_bytes=60 * 2**20),
        cost_estimate=costly,
        name="sum_split",
    )(place, kept, got)


def update_slots(master, first_moment, second_moment, filled, which, position, sources):
    capacity, unit_rows, width = master.shape

    group = math.gcd(capacity, 2)
    steps = capacity // group

    def body(filled_ref, which_ref, position_ref, weight, one, two, *rest):
        ins = rest[: len(sources)]
        new_one, new_two, new_weight, held, sems = rest[len(sources) :]
        step = pl.program_id(0)

        def fetch(turn):
            for i in range(group):
                slot = turn * group + i
                for source, ref in enumerate(ins):

                    @pl.when(which_ref[slot] == source)
                    def _():
                        pltpu.make_async_copy(
                            ref.at[position_ref[slot]], held.at[turn % 2, i], sems.at[turn % 2, i]
                        ).start()

        @pl.when(step == 0)
        def _():
            fetch(step)

        @pl.when(step < steps - 1)
        def _():
            fetch(step + 1)

        for i in range(group):
            pltpu.make_async_copy(
                ins[0].at[0], held.at[step % 2, i], sems.at[step % 2, i]
            ).wait()
            mask = (filled_ref[step * group + i] > 0).astype(jnp.float32)
            grad = held[step % 2, i].astype(jnp.float32)
            results = adamw(weight[i], one[i], two[i], grad, mask, rate)
            new_one[i], new_two[i], new_weight[i] = results

    block = pl.BlockSpec((group, unit_rows, width), lambda s, *_: (s, 0, 0))
    return pl.pallas_call(
        body,
        grid_spec=pltpu.PrefetchScalarGridSpec(
            num_scalar_prefetch=3,
            grid=(steps,),
            in_specs=[block] * 3 + [pl.BlockSpec(memory_space=pl.ANY)] * len(sources),
            out_specs=[block] * 3,
            scratch_shapes=[
                pltpu.VMEM((2, group, unit_rows, width), low),
                pltpu.SemaphoreType.DMA((2, group)),
            ],
        ),
        out_shape=[jax.ShapeDtypeStruct(master.shape, jnp.float32)] * 3,
        compiler_params=pltpu.CompilerParams(vmem_limit_bytes=56 * 2**20),
        cost_estimate=cheap,
        name="update_slots",
    )(filled, which, position, master, first_moment, second_moment, *sources)


def adamw(weight, moment_one, moment_two, gradient, filled, step_rate):
    new_one = beta_one * moment_one + (1.0 - beta_one) * gradient
    new_two = beta_two * moment_two + (1.0 - beta_two) * gradient * gradient
    fixed_one = new_one / (1.0 - beta_one**STEP)
    fixed_two = new_two / (1.0 - beta_two**STEP)
    updated = weight - step_rate * (fixed_one / (jnp.sqrt(fixed_two) + adam_eps) + decay * weight)
    return (new_one * filled, new_two * filled, updated * filled)


def swap(values, axis, bit):
    count = lax.axis_size(axis)
    return lax.ppermute(values, axis, [(i, i ^ (1 << bit)) for i in range(count)])


def choose(values, index, axis):
    return lax.dynamic_index_in_dim(values, index, axis, keepdims=False)


def total_sum(values):
    for axis in ("dp", "tensor"):
        for bit in range(lax.axis_size(axis).bit_length() - 1):
            values = values + swap(values, axis, bit)
    return values


def pick_units(master, slot_unit, state, kind, place, sizes, after=()):
    capacity, unit_rows, width = master.shape
    units = state.shape[0]

    def body(slot_ref, state_ref, kind_ref, place_ref, blocks, *rest):
        outs = rest[len(after) : len(after) + len(sizes)]
        highs, lows, zeros, read, sems = rest[len(after) + len(sizes) :]

        def start(source, unit):
            for which, out in enumerate(outs):

                @pl.when(kind_ref[unit] == which)
                def _():
                    pltpu.make_async_copy(source, out.at[place_ref[unit]], sems.at[unit]).start()

        @pl.loop(0, capacity)
        def _(slot):
            @pl.when(slot_ref[slot] >= 0)
            def _():
                pltpu.make_async_copy(blocks.at[slot], highs.at[slot], read.at[slot]).start()

        zeros[...] = jnp.zeros_like(zeros)

        @pl.loop(0, units)
        def _(unit):
            @pl.when(state_ref[unit] == 0)
            def _():
                start(zeros, unit)

        @pl.loop(0, capacity)
        def _(slot):
            @pl.when(slot_ref[slot] >= 0)
            def _():
                pltpu.make_async_copy(blocks.at[slot], highs.at[slot], read.at[slot]).wait()
                lows[slot] = highs[slot].astype(low)
                start(lows.at[slot], slot_ref[slot])

        @pl.loop(0, units)
        def _(unit):
            @pl.when(state_ref[unit] < 2)
            def _():
                pltpu.make_async_copy(zeros, outs[0].at[0], sems.at[unit]).wait()

    return pl.pallas_call(
        body,
        grid_spec=pltpu.PrefetchScalarGridSpec(
            num_scalar_prefetch=4,
            grid=(1,),
            in_specs=[pl.BlockSpec(memory_space=pl.ANY)] * (1 + len(after)),
            out_specs=[pl.BlockSpec(memory_space=pl.ANY)] * len(sizes),
            scratch_shapes=[
                pltpu.VMEM((capacity, unit_rows, width), jnp.float32),
                pltpu.VMEM((capacity, unit_rows, width), low),
                pltpu.VMEM((unit_rows, width), low),
                pltpu.SemaphoreType.DMA((capacity,)),
                pltpu.SemaphoreType.DMA((units,)),
            ],
        ),
        out_shape=[jax.ShapeDtypeStruct((size, unit_rows, width), low) for size in sizes],
        compiler_params=pltpu.CompilerParams(vmem_limit_bytes=56 * 2**20),
        cost_estimate=cheap,
        name="pick_units",
    )(slot_unit, state, kind, place, master, *after)


def place_blocks(sources, which, position, parts=1):
    amount = which.shape[0]
    shape = sources[0].shape[1:]
    size = amount // parts

    def body(which_ref, position_ref, *rest):
        ins, outs = rest[: len(sources)], rest[len(sources) : len(sources) + parts]
        held, read, sems = rest[len(sources) + parts :]

        @pl.loop(0, amount)
        def _(i):
            for source, ref in enumerate(ins):

                @pl.when(which_ref[i] == source)
                def _():
                    pltpu.make_async_copy(ref.at[position_ref[i]], held.at[i], read.at[i]).start()

        for part, out in enumerate(outs):

            @pl.loop(0, size)
            def _(j):
                i = part * size + j
                pltpu.make_async_copy(ins[0].at[0], held.at[i], read.at[i]).wait()
                pltpu.make_async_copy(held.at[i], out.at[j], sems.at[i]).start()

        @pl.loop(0, amount)
        def _(i):
            pltpu.make_async_copy(held.at[i], outs[0].at[0], sems.at[i]).wait()

    return pl.pallas_call(
        body,
        grid_spec=pltpu.PrefetchScalarGridSpec(
            num_scalar_prefetch=2,
            grid=(1,),
            in_specs=[pl.BlockSpec(memory_space=pl.ANY)] * len(sources),
            out_specs=[pl.BlockSpec(memory_space=pl.ANY)] * parts,
            scratch_shapes=[
                pltpu.VMEM((amount,) + shape, low),
                pltpu.SemaphoreType.DMA((amount,)),
                pltpu.SemaphoreType.DMA((amount,)),
            ],
        ),
        out_shape=[jax.ShapeDtypeStruct((size,) + shape, low)] * parts,
        compiler_params=pltpu.CompilerParams(vmem_limit_bytes=56 * 2**20),
        cost_estimate=cheap,
        name="place_blocks",
    )(which, position, *sources)


def stack_pairs(pairs):
    shape = (len(pairs),) + pairs[0].shape[1:]

    def body(*refs):
        for i, pair in enumerate(refs[:-2]):
            for half in range(2):
                refs[half - 2][i] = pair[half]

    return pl.pallas_call(
        body,
        out_shape=[jax.ShapeDtypeStruct(shape, low)] * 2,
        cost_estimate=costly,
        name="stack_pairs",
    )(*pairs)


def hops(values, step, turn):
    count = lax.axis_size("tensor")
    if step > 0:
        pairs = [(i, i + 1) for i in range(turn - 1, count - 1)]
    else:
        pairs = [(i, i - 1) for i in range(1, count - turn + 1)]
    return lax.ppermute(values, "tensor", pairs)


fence = lax.optimization_barrier


def in_pool(member, inner, inner_count):
    me = lax.axis_index("dp")
    half, core = member >> 3, ((member >> 2) & 1) ^ (me & 1)
    far_y, far_x = ((member >> 1) & 1) ^ ((me >> 2) & 1), (member & 1) ^ ((me >> 1) & 1)
    where_first = (far_y * 2 + far_x) * inner_count
    where_second = (4 + far_x * 2 + far_y) * inner_count
    return (core, jnp.where(half == 0, where_first, where_second) + inner)


def on_device(
    hidden_in,
    time_embed,
    caption_table,
    caption_ids,
    owners,
    master,
    first_moment,
    second_moment,
    mod_table,
    mod_first,
    mod_second,
    out_grad,
):
    count = lax.axis_size("tensor")
    dp_count = lax.axis_size("dp")
    me_dp = lax.axis_index("dp")
    me_tensor = lax.axis_index("tensor")
    capacity, unit_rows, width = master.shape
    units = owners.shape[0]
    tokens = hidden_in.shape[1]
    text_count = caption_ids.shape[1]
    share = width // count
    per = share // unit_rows
    ups = (units - 8 * per) // 2
    rank_of = ranks_of(owners)
    mine = owners == me_dp
    match = (rank_of[None, :] == jnp.arange(capacity)[:, None]) & mine[None, :]
    filled = jnp.any(match, axis=1)
    unit_of_slot = jnp.sum(jnp.where(match, jnp.arange(units)[None, :], 0), axis=1)

    square = [list(range(i * per, (i + 1) * per)) for i in range(8)]
    group_attn = square[0] + square[1] + square[2] + square[5]
    group_full = square[3] + square[4] + square[6] + square[7]
    group_mlp = list(range(8 * per, units))
    members = len(group_attn)
    plane = dp_count == 8 and members == 16 and len(group_mlp) % dp_count == 0
    member_of = np.zeros(units, np.int32)
    member_of[group_attn] = np.arange(members)
    member_of[group_full] = np.arange(members)
    is_attn = np.zeros(units, bool)
    is_attn[group_attn] = True
    is_mlp = np.zeros(units, bool)
    is_mlp[group_mlp] = True

    latent_in = hidden_in[0].astype(jnp.float32)
    modulate = mod_table + time_embed[0]

    def mod_row(which_row):
        return modulate[which_row][None, :]

    normed_one, inverse_one = layer_norm(latent_in)
    bits = dp_count.bit_length() - 1
    vocab_rows = caption_table.shape[0]

    def caption_terms(ids):
        chosen = ids.reshape(-1) - me_dp * vocab_rows
        onehot = (chosen[:, None] == jnp.arange(vocab_rows)[None, :]).astype(low)
        terms = jnp.dot(onehot, caption_table, preferred_element_type=jnp.float32).astype(low)
        return terms.reshape(dp_count, text_count, -1)

    def modulated(normed):
        return (normed.astype(jnp.float32) * (1.0 + mod_row(1)) + mod_row(0)).astype(low)

    def whole_text(text_ring):
        return from_ring(text_ring, -1).transpose(1, 0, 2).reshape(text_count, width)

    def own_keys(text_low, w_attn):
        return project(text_low, w_attn)[:, 3 * share :].astype(low)

    def exchanged(attended, keys):
        parts = [
            jnp.concatenate([attended[k * tokens : (k + 1) * tokens], keys]) for k in range(count)
        ]
        return [parts[0]] + [shift(parts[k], count - k) for k in range(1, count)]

    where = jnp.stack([me_tensor, me_dp & 1]).astype(jnp.int32)

    n_low = normed_one.astype(low)
    if plane:
        core, far_x, far_y = (
            ((member_of >> 2) & 1) ^ (me_dp & 1),
            (member_of & 1) ^ ((me_dp >> 1) & 1),
            ((member_of >> 1) & 1) ^ ((me_dp >> 2) & 1),
        )
        place = jnp.where(is_attn, far_x * 4 + far_y * 2, 8 + far_y * 4 + far_x * 2)
        place = jnp.where(is_mlp, np.arange(units) - 8 * per, place + (member_of >> 3))
        kind = jnp.where(is_mlp, 0, core)
        slot_mlp = unit_of_slot >= 8 * per
        owned_state = mine.astype(jnp.int32)
        ids = lax.all_gather(caption_ids, "dp", axis=0, tiled=True)
        ids = jnp.take(ids, me_dp ^ jnp.arange(dp_count), axis=0, mode="clip")
        up, down = hops(n_low, 1, 1), hops(n_low, -1, 1)
        kept, given = pick_units(
            master,
            jnp.where(filled & ~slot_mlp, unit_of_slot, -1),
            jnp.where(is_mlp, 2, owned_state),
            kind,
            place,
            (members, members),
        )
        got = swap(given, "dp", 0)
        (mlp_part,) = pick_units(
            master,
            jnp.where(filled & slot_mlp, unit_of_slot, -1),
            jnp.where(is_mlp, owned_state, 2),
            kind,
            place,
            (len(group_mlp),),
            (kept,),
        )
        mlp_part = lax.psum_scatter(mlp_part, "dp", scatter_dimension=0, tiled=True)
        n_up, n_down = [up], [down]
        kept, got, up, down, ids = fence((kept, got, up, down, ids))
        pieces = [kept[i : i + 4] + got[i : i + 4] for i in range(0, members, 4)]
        attn_two, attn_send, full_two, full_send = fence(tuple(pieces))
        up, down = hops(up, 1, 2), hops(down, -1, 2)
        attn_got = swap(attn_send, "dp", 1)
        full_got = swap(full_send, "dp", 2)
        text = caption_terms(ids)
        text = text[0:4] + swap(text[4:8], "dp", 2)
        n_up.append(up), n_down.append(down)
        attn_two, attn_got, full_two, full_got, up, down, text = fence(
            (attn_two, attn_got, full_two, full_got, up, down, text)
        )
        pieces = [x[i : i + 2] + y[i : i + 2] for x, y in ((attn_two, attn_got), (full_two, full_got)) for i in (0, 2)]
        attn_one, attn_send, full_one, full_send = fence(tuple(pieces))
        up, down = hops(up, 1, 3), hops(down, -1, 3)
        attn_got = swap(attn_send, "dp", 2)
        full_got = swap(full_send, "dp", 1)
        text = text[0:2] + swap(text[2:4], "dp", 1)
        n_up.append(up), n_down.append(down)
        attn_one, attn_got, full_one, full_got, up, down, text, mlp_part = fence(
            (attn_one, attn_got, full_one, full_got, up, down, text, mlp_part)
        )
        attn_one, full_one = attn_one + attn_got, full_one + full_got
        n_up[-1], n_down[-1] = up, down
        w_mlp = lax.all_gather(mlp_part, "dp", axis=0, tiled=True)
        first_ring, second_ring = stack_pairs(ring(full_one))
        first = jnp.concatenate([attn_one[0:1], swap(attn_one[0:1], "dp", 1)])
        second = jnp.concatenate([attn_one[1:2], swap(attn_one[1:2], "dp", 2)])
        pool = jnp.concatenate([first, swap(first, "dp", 2), second, swap(second, "dp", 1)])
        other = swap(pool, "dp", 0)
        text = text[0] + swap(text[1], "dp", 0)
        *n_slots, h_one_all = line_slots(
            where, n_low, n_up, n_down, jnp.concatenate([mod_row(0), mod_row(1)])
        )
        n_slots = [n_low] + n_slots
        grad_own = out_grad[0]
        pool, other, first_ring, second_ring, h_one_all, text, grad_own = fence(
            (pool, other, first_ring, second_ring, h_one_all, text, grad_own)
        )
        grad_whole = lax.all_gather(grad_own, "tensor", axis=0)
        first, second = first_ring, second_ring
        first_got = swap(first, "dp", 1)
        second_got = swap(second, "dp", 2)
        text_ring = ring(text)
        (w_attn,) = place_blocks((pool, other), *in_pool(np.arange(members), 0, 1))
        w_attn = w_attn.reshape(-1, width)
        qkv = project(h_one_all, w_attn).astype(low)
        attended, logs = self_attend(qkv, share)
        first = jnp.concatenate([first, first_got])
        second = jnp.concatenate([second, second_got])
        first, second, text_ring, attended, logs, w_attn, w_mlp = fence(
            (first, second, text_ring, attended, logs, w_attn, w_mlp)
        )
        first_far, second_far = swap(first, "dp", 2), swap(second, "dp", 1)
        text_low = whole_text(jnp.stack(text_ring))
        mixed = exchanged(attended, own_keys(text_low, w_attn))
        first_far, second_far, mixed = fence((first_far, second_far, mixed))
        first_other, second_other = swap(first, "dp", 0), swap(second, "dp", 0)
        first_last, second_last = swap(first_far, "dp", 0), swap(second_far, "dp", 0)
        listing = np.arange(count * members)
        matrix, rank, head = listing // (count * per), listing // per % count, listing % per
        slot = lax.rem(me_tensor - rank + count, count)
        which, position = in_pool(matrix * per + head, slot, count)
        blocks = 2 * count
        w_full = place_blocks(
            (first, first_far, second, second_far, first_other, first_last, second_other, second_last),
            which * 4 + position // blocks,
            position % blocks,
            parts=4,
        )
        w_full = [part.reshape(width, width) for part in w_full]
        w_full[3], grad_whole = fence((w_full[3], grad_whole))
    else:
        slots_low = master.astype(low)
        rows = jnp.take(slots_low, rank_of, axis=0, mode="clip")
        rows = lax.psum(jnp.where(mine[:, None, None], rows, jnp.zeros((), low)), "dp")
        w_attn = rows[np.array(group_attn)].reshape(-1, width)
        w_full = lax.all_gather(rows[np.array(group_full)], "tensor", axis=0)
        w_full = w_full.reshape(count, 4, share, width).swapaxes(0, 1).reshape(4, width, width)
        w_full = [w_full[i] for i in range(4)]
        w_mlp = rows[8 * per :]
        n_slots = ring(n_low)
        normed_all = jnp.concatenate(n_slots)
        grad_whole = lax.all_gather(out_grad[0], "tensor", axis=0)
        ids = caption_ids
        for bit in range(bits):
            ids = jnp.concatenate([ids, swap(ids, "dp", bit)])
        text = caption_terms(ids)
        for bit in reversed(range(bits)):
            text = text[: 1 << bit] + swap(text[1 << bit :], "dp", bit)
        text_low = whole_text(jnp.stack(ring(text[0])))
        h_one_all = modulated(normed_all)
        qkv = project(h_one_all, w_attn).astype(low)
        attended, logs = self_attend(qkv, share)
        mixed = exchanged(attended, own_keys(text_low, w_attn))
    w_cross = w_full
    w_out, c_query, c_value, c_out = w_full
    w_mlp = w_mlp.reshape(-1, width)

    rows = jnp.concatenate([mod_row(2), mod_row(3), mod_row(4)])
    (
        branch_one,
        first_low,
        cq_rows,
        ck_rows,
        cv_rows,
        crossed,
        second_res,
        normed_two,
        h_two,
        inverse_two,
    ) = cross_block(
        where, mixed, hidden_in[0], rows, text_low, *w_cross
    )

    h_slots = {0: h_two}
    out_slots = [
        choose(grad_whole, lax.rem(me_tensor - k + count, count), 0) for k in range(count)
    ]
    grad_slots = [(mod_row(5) * item.astype(jnp.float32)).astype(low) for item in out_slots]
    near = [k for k in range(1, count) if 2 * k != count]
    far = [k for k in range(1, count) if 2 * k == count]
    acts, grad_pres, grad_terms, order = [], [], [], []
    for k in near:
        h_slots[k] = shift(h_two, k)
    for members_now in ([0], near, far):
        act, grad_pre, *terms = mlp_core(
            [h_slots[k] for k in members_now],
            [grad_slots[k] for k in members_now],
            w_mlp,
            acts[-1:],
        )
        if members_now == [0]:
            h_two, act = fence((h_two, act))
            for k in far:
                h_slots[k] = shift(h_two, k)
        acts.append(act), grad_pres.append(grad_pre)
        order += members_now
        grad_terms += [
            shift(term, count - k) if k else term for k, term in zip(members_now, terms)
        ]
    mlp_grad = mlp_grads(
        grad_pres, acts, [h_slots[k] for k in order], [grad_slots[k] for k in order]
    ).reshape(-1, unit_rows, width)
    hidden_share = w_mlp.shape[0] // 2
    pieces = [
        [(which, row, 0, hidden_share, hidden_share)]
        for which, act in enumerate(acts)
        for row in range(0, act.shape[0], tokens)
    ]
    branch_terms, branch_sums = ranked_terms(
        where, acts, order, pieces, w_mlp, [out_slots[k] for k in order], "mlp_out"
    )
    branch_row = branch_sums[1]
    grad_terms, branch_terms = fence((grad_terms, branch_terms))
    if plane:
        mlp_sum = lax.psum_scatter(mlp_grad, "dp", scatter_dimension=0, tiled=True)

    (
        first_grad,
        cross_low,
        grad_cq,
        attn_low,
        grad_cv,
        row_sums,
        *grad_mixed,
    ) = cross_back(
        where,
        grad_terms,
        out_grad[0],
        rows,
        normed_two,
        inverse_two,
        branch_one,
        cq_rows,
        ck_rows,
        cv_rows,
        c_out,
        c_query,
        w_out,
        (mlp_grad,),
    )

    grad_parts = [grad_mixed[0]] + [shift(grad_mixed[k], k) for k in range(1, count)]
    full_pairs = [
        ([(item, 0, share, None) for item in mixed], attn_low),
        ([(grad_cq, 0, width, 0)], first_low),
        ([(grad_cv, 0, width, 0)], text_low),
        ([(crossed, 0, width, 0)], cross_low),
    ]
    half = (share // HEAD_DIM // 2) * HEAD_DIM
    spans = [(0, half), (half, share)]

    def attention_pairs(grads, grad_parts):
        keys = sum(item[tokens:].astype(jnp.float32) for item in grad_parts).astype(low)
        pairs = [
            (
                [
                    (item, i * (end - begin), end - begin, begin)
                    for item, (begin, end) in zip(grads, spans)
                ],
                h_one_all,
            )
            for i in range(3)
        ]
        return pairs + [([(keys, 0, share, 0)], text_low)]

    def input_terms(grads):
        pieces = [
            [
                (which, slot * tokens, i * (end - begin), i * share + begin, end - begin)
                for which, (begin, end) in enumerate(spans)
                for i in range(3)
            ]
            for slot in range(count)
        ]
        return ranked_terms(where, grads, range(count), pieces, w_attn, n_slots, "attn_terms")

    if plane:
        x_bit, y_bit = (me_dp >> 1) & 1, (me_dp >> 2) & 1

        def split(total, bit, axis):
            return (choose(total, bit, axis), choose(total, 1 - bit, axis))

        kept, given = outer_halves(where, full_pairs, count, "full_grads")
        got = swap(given, "dp", 0)
        grad_parts, kept, got, branch_terms = fence((grad_parts, kept, got, branch_terms))
        branch_two = lax.psum_scatter(
            branch_terms.reshape(-1, width), "tensor", scatter_dimension=0, tiled=True
        )
        box = (2, count, 2, 2, unit_rows, width)
        bits_here = jnp.stack([x_bit, y_bit]).astype(jnp.int32)
        kept_one, given_one, kept_two, given_two = sum_split(
            bits_here, kept.reshape(box), got.reshape(box)
        )
        got_one, got_two = swap(given_one, "dp", 1), swap(given_two, "dp", 2)
        grads_early = self_attend_back(qkv, grad_parts, attended, logs, share, *spans[0])
        kept_one, got_one, kept_two, got_two, grads_early, grad_parts = fence(
            (kept_one, got_one, kept_two, got_two, grads_early, grad_parts)
        )
        kept_one, given_one = split(kept_one + got_one, y_bit, 1)
        kept_two, given_two = split(kept_two + got_two, x_bit, 1)
        kept_one, given_one, kept_two, given_two, grad_parts = fence(
            (kept_one, given_one, kept_two, given_two, grad_parts)
        )
        got_one, got_two = swap(given_one, "dp", 2), swap(given_two, "dp", 1)
        grads_late = self_attend_back(qkv, grad_parts, attended, logs, share, *spans[1])
        kept_one, got_one, kept_two, got_two, grads_early, grads_late, mlp_sum = fence(
            (kept_one, got_one, kept_two, got_two, grads_early, grads_late, mlp_sum)
        )
        mlp_sum = lax.all_gather(mlp_sum, "dp", axis=0, tiled=True)
        full_parts = to_ring(jnp.stack([kept_one + got_one, kept_two + got_two], axis=1))
        full_parts = [full_parts[k] for k in range(count)]
        full_parts, grads_early, grads_late = fence((full_parts, grads_early, grads_late))
        grads_qkv = [grads_early, grads_late]
        full_got = [shift(full_parts[k], k) for k in range(1, count)]
        attn_kept, attn_given = outer_halves(
            where, attention_pairs(grads_qkv, grad_parts), 1, "attn_grads"
        )
        attn_got = swap(attn_given, "dp", 0)
        grad_h_terms, grad_h_sums = input_terms(grads_qkv)
        mod_terms = jnp.concatenate([grad_h_sums, row_sums, branch_row[None]])
        grad_h_one = lax.psum_scatter(
            grad_h_terms.reshape(-1, width), "tensor", scatter_dimension=0, tiled=True
        )
        attn_kept, attn_got, mod_terms, branch_two = fence(
            (attn_kept, attn_got, mod_terms, branch_two)
        )
        attn_all = (attn_kept + attn_got).reshape(2, 2, 2, unit_rows, width)
        one_kept, one_given = split(attn_all[0], x_bit, 1)
        two_kept, two_given = split(attn_all[1], y_bit, 0)
        one_got, two_got = swap(one_given, "dp", 1), swap(two_given, "dp", 2)
        mod_terms = mod_terms + swap(mod_terms, "dp", 0)
        full_own = full_parts[0]
        one_kept, one_got, two_kept, two_got, mod_terms, full_own, full_got = fence(
            (one_kept, one_got, two_kept, two_got, mod_terms, full_own, full_got)
        )
        full_sum = full_own.astype(jnp.float32)
        for part in full_got:
            full_sum = full_sum + part.astype(jnp.float32)
        full_sum = full_sum.astype(low)
        one_kept, one_given = split(one_kept + one_got, y_bit, 0)
        two_kept, two_given = split(two_kept + two_got, x_bit, 0)
        one_got, two_got = swap(one_given, "dp", 2), swap(two_given, "dp", 1)
        mod_terms = mod_terms + swap(mod_terms, "dp", 1)
        one_kept, one_got, two_kept, two_got, full_sum, mod_terms, mlp_sum = fence(
            (one_kept, one_got, two_kept, two_got, full_sum, mod_terms, mlp_sum)
        )
        first = jnp.stack([one_kept + one_got, full_sum[0]])
        second = jnp.stack([two_kept + two_got, full_sum[1]])
        first_got, second_got = swap(first, "dp", 1), swap(second, "dp", 2)
        first = jnp.concatenate([first, first_got])
        second = jnp.concatenate([second, second_got])
        mod_terms = mod_terms + swap(mod_terms, "dp", 2)
        first, second, mod_terms = fence((first, second, mod_terms))
        first_far, second_far = swap(first, "dp", 2), swap(second, "dp", 1)
        mod_terms = mod_terms + swap(mod_terms, "tensor", 0)
        first, first_far, second, second_far, mod_terms = fence(
            (first, first_far, second, second_far, mod_terms)
        )
        pool = jnp.concatenate([first, first_far, second, second_far])
        other = swap(pool, "dp", 0)
        for bit in range(1, count.bit_length() - 1):
            mod_terms = mod_terms + swap(mod_terms, "tensor", bit)
        pool, other, mod_grad = fence((pool, other, mod_terms))
        which, position = in_pool(member_of, np.where(is_attn, 0, 1), 2)
        which = jnp.where(is_mlp, 2, which)
        position = jnp.where(is_mlp, np.arange(units) - 8 * per, position)
        own = jnp.sum(jnp.where(match[:, :, None], jnp.stack([which, position], 1)[None], 0), axis=1)
        new_first, new_second, new_master = update_slots(
            master,
            first_moment,
            second_moment,
            filled.astype(jnp.int32),
            own[:, 0],
            own[:, 1],
            (pool, other, mlp_sum),
        )
    else:
        branch_two = lax.psum_scatter(
            branch_terms.reshape(-1, width), "tensor", scatter_dimension=0, tiled=True
        )
        grads_qkv = [self_attend_back(qkv, grad_parts, attended, logs, share, *span) for span in spans]
        attn_grads = [
            outer(array[:, lane : lane + lanes], right).astype(low)
            for left, right in attention_pairs(grads_qkv, grad_parts)
            for array, lane, lanes, row in left
        ]
        grad_h_terms, grad_h_sums = input_terms(grads_qkv)
        grad_h_one = lax.psum_scatter(
            grad_h_terms.reshape(-1, width), "tensor", scatter_dimension=0, tiled=True
        )
        mixed_all = from_ring(jnp.stack([item[:tokens] for item in mixed]), 1)
        mixed_all = mixed_all.transpose(1, 0, 2).reshape(tokens, width)
        full_grads = [outer(mixed_all, attn_low)]
        full_grads += [outer(left[0][0], right) for left, right in full_pairs[1:]]
        full_sum = [g.astype(low).reshape(count, share, width) for g in full_grads]
        full_sum = jnp.stack(full_sum, axis=1)
        full_sum = lax.psum_scatter(full_sum, "tensor", scatter_dimension=0, tiled=True)
        order = np.array(group_attn + group_full + group_mlp)
        sums = jnp.concatenate(
            [jnp.concatenate(attn_grads), full_sum.reshape(-1, width), mlp_grad.reshape(-1, width)]
        )
        sums = lax.psum(sums.reshape(units, unit_rows, width), "dp")
        owned = jnp.take(sums, jnp.array(np.argsort(order))[unit_of_slot], axis=0, mode="clip")
        mod_grad = total_sum(jnp.concatenate([grad_h_sums, row_sums, branch_row[None]]))
        new_first, new_second, new_master = adamw(
            master,
            first_moment,
            second_moment,
            owned.astype(jnp.float32),
            filled.astype(jnp.float32)[:, None, None],
            rate,
        )
    branch_two, second_res, grad_h_one, new_first = fence(
        (branch_two, second_res, grad_h_one, new_first)
    )
    grad_h_one = grad_h_one.astype(jnp.float32)
    block_out = second_res + mod_row(5) * branch_two.astype(jnp.float32)
    input_grad = first_grad + norm_back(grad_h_one, normed_one, inverse_one, mod_row(1))
    mod_new_first, mod_new_second, mod_new = adamw(
        mod_table, mod_first, mod_second, mod_grad, 1.0, table_rate
    )
    return (
        block_out[None],
        input_grad[None],
        new_first,
        new_second,
        new_master,
        mod_new_first,
        mod_new_second,
        mod_new,
    )


def solution(mesh):
    in_specs = (
        P("dp", "tensor", None),
        P("dp", None, None),
        P("dp", "tensor"),
        P("dp", None),
        P(),
        P("dp", "tensor", None),
        P("dp", "tensor", None),
        P("dp", "tensor", None),
        P(),
        P(),
        P(),
        P("dp", "tensor", None),
    )
    out_specs = (
        P("dp", "tensor", None),
        P("dp", "tensor", None),
        P("dp", "tensor", None),
        P("dp", "tensor", None),
        P("dp", "tensor", None),
        P(),
        P(),
        P(),
    )
    return jax.shard_map(
        on_device, mesh=mesh, in_specs=in_specs, out_specs=out_specs, check_vma=False
    )
```

```python
import math

import jax
import jax.numpy as jnp
import numpy as np
from jax import lax
from jax.experimental import pallas as pl
from jax.experimental.pallas import tpu as pltpu
from jax.sharding import PartitionSpec as P

HEAD_DIM = 72
STEP = 10


norm_eps = 1e-06
beta_one = 0.9
beta_two = 0.999
rate = 0.03
table_rate = 0.3
decay = 0.01
adam_eps = 1e-08
low = jnp.bfloat16


def ranks_of(owners):
    index = jnp.arange(owners.shape[0])
    before = (owners[None, :] == owners[:, None]) & (index[None, :] < index[:, None])
    return jnp.sum(before.astype(jnp.int32), axis=1)


def layer_norm(values):
    center = values - jnp.mean(values, axis=-1, keepdims=True)
    inverse = lax.rsqrt(jnp.mean(center * center, axis=-1, keepdims=True) + norm_eps)
    return (center * inverse, inverse)


def norm_back(grad_rows, normed, inverse, scale_row):
    scaled = grad_rows * (1.0 + scale_row)
    mean_one = jnp.mean(scaled, axis=-1, keepdims=True)
    mean_two = jnp.mean(scaled * normed, axis=-1, keepdims=True)
    return inverse * (scaled - mean_one - normed * mean_two)


def project(rows, weight):
    return jnp.einsum("ld,rd->lr", rows, weight, preferred_element_type=jnp.float32)


def expand(rows, weight):
    return jnp.einsum("lr,rd->ld", rows, weight, preferred_element_type=jnp.float32)


def outer(left, right):
    return jnp.einsum("lr,ld->rd", left, right, preferred_element_type=jnp.float32)


def shift(values, step):
    count = lax.axis_size("tensor")
    return lax.ppermute(values, "tensor", [(i, (i + step) % count) for i in range(count)])


def ring(values):
    return [values] + [shift(values, k) for k in range(1, lax.axis_size("tensor"))]


def to_ring(stacked):
    count = stacked.shape[0]
    twice = jnp.concatenate([stacked, stacked], axis=0)
    return lax.dynamic_slice_in_dim(twice, lax.axis_index("tensor"), count, 0)


def from_ring(stacked, sign):
    count = stacked.shape[0]
    me = lax.axis_index("tensor")
    place = lax.rem(sign * (jnp.arange(count) - me) + 2 * count, count)
    return jnp.take(stacked, place, axis=0, mode="clip")


cheap = pl.CostEstimate(flops=1000, bytes_accessed=1000, transcendentals=0)
costly = pl.CostEstimate(flops=10**10, bytes_accessed=10**7, transcendentals=0)


def self_attend(qkv, share):
    length = qkv.shape[0]
    rows = min(512, length)
    curve = HEAD_DIM ** (-0.5) * math.log2(math.e)
    heads = share // HEAD_DIM

    def body(qkv_ref, out_ref, log_ref):
        @pl.loop(0, length // rows)
        def _(step):
            here = pl.ds(pl.multiple_of(step * rows, rows), rows)
            parts = []
            for head in range(heads):
                at = head * HEAD_DIM
                q = qkv_ref[here, at : at + HEAD_DIM]
                k = qkv_ref[:, share + at : share + at + HEAD_DIM]
                v = qkv_ref[:, 2 * share + at : 2 * share + at + HEAD_DIM]
                scores = dot(k, q, nt)
                top = jnp.max(scores, axis=0, keepdims=True)
                expo = jnp.exp2((scores - top) * curve)
                total = jnp.sum(expo, axis=0, keepdims=True)
                log_ref[head : head + 1, here] = top * curve + jnp.log2(total)
                parts.append((dot(v, expo.astype(low), tn) * (1.0 / total)).T)
            out_ref[here, :] = jnp.concatenate(parts, axis=1).astype(low)

    return pl.pallas_call(
        body,
        out_shape=[
            jax.ShapeDtypeStruct((length, share), low),
            jax.ShapeDtypeStruct((heads, length), jnp.float32),
        ],
        compiler_params=pltpu.CompilerParams(vmem_limit_bytes=40 * 2**20),
        cost_estimate=cheap,
        name="self_attend",
    )(qkv)


def self_attend_back(qkv, grads, mixed, logs, share, begin, end):
    length = qkv.shape[0]
    rows = length // len(grads)
    span = end - begin
    scale = HEAD_DIM ** (-0.5)
    curve = scale * math.log2(math.e)

    def body(qkv_ref, mixed_ref, log_ref, *refs):
        grad_refs, (out_ref, grad_k, grad_v) = refs[: len(grads)], refs[len(grads) :]
        for step, grad_ref in enumerate(grad_refs):
            here = slice(step * rows, (step + 1) * rows)
            parts = []
            for head, at in enumerate(range(begin, end, HEAD_DIM)):
                q = qkv_ref[here, at : at + HEAD_DIM]
                k = qkv_ref[:, share + at : share + at + HEAD_DIM]
                v = qkv_ref[:, 2 * share + at : 2 * share + at + HEAD_DIM]
                g = grad_ref[0:rows, at : at + HEAD_DIM]
                o = mixed_ref[here, at : at + HEAD_DIM]
                inner = g.astype(jnp.float32) * o.astype(jnp.float32)
                inner = jnp.sum(inner.T, axis=0, keepdims=True)
                which = begin // HEAD_DIM + head
                probs = jnp.exp2(dot(k, q, nt) * curve - log_ref[which : which + 1, here])
                grad_scores = (probs * (dot(v, g, nt) - inner)).astype(low)
                to_v = dot(probs.astype(low), g)
                to_k = dot(grad_scores, q)
                if step:
                    grad_v[head] += to_v
                    grad_k[head] += to_k
                else:
                    grad_v[head] = to_v
                    grad_k[head] = to_k
                parts.append((dot(k, grad_scores, tn) * scale).T)
            out_ref[here, 0:span] = jnp.concatenate(parts, axis=1).astype(low)
        heads = range(span // HEAD_DIM)
        both = [grad_k[head] * scale for head in heads]
        out_ref[:, span : 2 * span] = jnp.concatenate(both, axis=1).astype(low)
        both = [grad_v[head] for head in heads]
        out_ref[:, 2 * span :] = jnp.concatenate(both, axis=1).astype(low)

    return pl.pallas_call(
        body,
        out_shape=jax.ShapeDtypeStruct((length, 3 * span), low),
        scratch_shapes=[pltpu.VMEM((span // HEAD_DIM, length, HEAD_DIM), jnp.float32)] * 2,
        compiler_params=pltpu.CompilerParams(vmem_limit_bytes=40 * 2**20),
        cost_estimate=costly,
        name="self_attend_back",
    )(qkv, mixed, logs, *grads)


def mlp_core(rows_in, grads_in, w_mlp, after):
    groups = len(rows_in)
    tokens, width = rows_in[0].shape
    hidden = w_mlp.shape[0] // 2
    chunk = 384 if hidden % 384 == 0 else hidden
    steps = hidden // chunk
    curve = 0.7978845608028654

    def body(*refs):
        rows, grads = refs[:groups], refs[groups : 2 * groups]
        up, down = refs[2 * groups : 2 * groups + 2]
        act, grad_pre, *outs = refs[2 * groups + 2 + len(after) : -1]
        total = refs[-1]
        step = pl.program_id(0)
        for i in range(groups):
            pre = lax.dot_general(
                rows[i][...], up[...], (((1,), (1,)), ((), ())), preferred_element_type=jnp.float32
            )
            square = pre * pre
            bend = jnp.tanh(curve * pre * (1.0 + 0.044715 * square))
            half = 0.5 * (1.0 + bend)
            here = pl.ds(i * tokens, tokens)
            act[here, :] = (pre * half).astype(low)
            slope = half + (0.5 * curve) * pre * (1.0 - bend * bend) * (1.0 + 0.134145 * square)
            grad_act = lax.dot_general(
                grads[i][...], down[...], (((1,), (1,)), ((), ())), preferred_element_type=jnp.float32
            )
            grad_low = (grad_act * slope).astype(low)
            grad_pre[here, :] = grad_low
            term = jnp.dot(grad_low, up[...], preferred_element_type=jnp.float32)

            @pl.when(step == 0)
            def _():
                total[here, :] = term

            @pl.when(step > 0)
            def _():
                total[here, :] += term

            @pl.when(step == steps - 1)
            def _():
                outs[i][...] = total[here, :].astype(low)

    whole = pl.BlockSpec((tokens, width), lambda s: (0, 0))
    across = pl.BlockSpec((groups * tokens, chunk), lambda s: (0, s))
    return pl.pallas_call(
        body,
        grid=(steps,),
        in_specs=[whole] * (2 * groups)
        + [
            pl.BlockSpec((chunk, width), lambda s: (s, 0)),
            pl.BlockSpec((chunk, width), lambda s: (steps + s, 0)),
        ]
        + [pl.BlockSpec(memory_space=pl.ANY)] * len(after),
        out_specs=[across, across] + [whole] * groups,
        out_shape=[jax.ShapeDtypeStruct((groups * tokens, hidden), low)] * 2
        + [jax.ShapeDtypeStruct((tokens, width), low)] * groups,
        scratch_shapes=[pltpu.VMEM((groups * tokens, width), jnp.float32)],
        compiler_params=pltpu.CompilerParams(vmem_limit_bytes=60 * 2**20),
        cost_estimate=cheap,
        name="mlp_core",
    )(*rows_in, *grads_in, w_mlp, w_mlp, *after)


nt = (((1,), (1,)), ((), ()))
tn = (((0,), (0,)), ((), ()))


def dot(left, right, dims=(((1,), (0,)), ((), ()))):
    return lax.dot_general(left, right, dims, preferred_element_type=jnp.float32)


def softmax_keys(keys, queries):
    scores = dot(keys, queries, nt) * HEAD_DIM ** (-0.5)
    expo = jnp.exp(scores - jnp.max(scores, axis=0, keepdims=True))
    return expo * (1.0 / jnp.sum(expo, axis=0, keepdims=True))


def cuts_of(width):
    size = 384 if width % 384 == 0 else width
    return [slice(i, i + size) for i in range(0, width, size)]


def in_smem():
    return pl.BlockSpec(memory_space=pltpu.SMEM)


def in_vmem():
    return pl.BlockSpec(memory_space=pltpu.VMEM)


def line_slots(place, own, ups, downs, rows):
    count = len(ups) + 1
    tokens, width = own.shape

    def body(place_ref, *refs):
        own_ref, up_refs, down_refs = refs[0], refs[1:count], refs[count : 2 * count - 1]
        rows_ref, outs, out = refs[2 * count - 1], refs[2 * count : -1], refs[-1]
        me = place_ref[0]

        def modulate(slot, ref):
            value = ref[...].astype(jnp.float32)
            value = value * (1.0 + rows_ref[1:2, :]) + rows_ref[0:1, :]
            out[slot * tokens : (slot + 1) * tokens, :] = value.astype(low)

        modulate(0, own_ref)
        for k in range(1, count):
            for side, ref in ((me >= k, up_refs[k - 1]), (me < k, down_refs[count - k - 1])):

                @pl.when(side)
                def _():
                    outs[k - 1][...] = ref[...]
                    modulate(k, ref)

    shapes = [(tokens, width)] * (count - 1) + [(count * tokens, width)]
    return pl.pallas_call(
        body,
        in_specs=[in_smem()] + [in_vmem()] * (2 * count),
        out_shape=[jax.ShapeDtypeStruct(shape, low) for shape in shapes],
        compiler_params=pltpu.CompilerParams(vmem_limit_bytes=32 * 2**20),
        cost_estimate=cheap,
        name="line_slots",
    )(place, own, *ups, *downs, rows)


def cross_block(place, mixed, hidden, rows, text, w_out, c_query, c_value, c_out):
    count, share = len(mixed), mixed[0].shape[1]
    tokens, width = hidden.shape
    words = text.shape[0]
    per = share // HEAD_DIM

    def body(place_ref, *refs):
        parts = refs[:count]
        x_ref, rows_ref, text_ref = refs[count : count + 3]
        far = refs[count + 3 : count + 7]
        outs = refs[count + 7 : count + 16]
        inverse = refs[count + 16]
        wo, wq, wv, wc, *own = refs[count + 17 : -3]
        held, read, sems = refs[-3:]
        branch, res_low, cq, ck, cv, crossed, res, normed, out = own
        me = place_ref[0]
        loads = [
            pltpu.make_async_copy(source, target, read.at[i])
            for i, (source, target) in enumerate(zip(far, (wo, wq, wv, wc)))
        ]
        stores = [
            pltpu.make_async_copy(source, target, sems.at[i])
            for i, (source, target) in enumerate(zip(own, outs))
        ]
        for load in loads:
            load.start()
        loads[0].wait()
        for cut in cuts_of(width):
            total = jnp.zeros((tokens, cut.stop - cut.start), jnp.float32)
            for k in range(count):
                rank = lax.rem(me + k, count)
                here = pl.ds(pl.multiple_of(rank * share, 32), share)
                total += dot(parts[k][0:tokens, :], wo[here, cut])
            branch[:, cut] = total
            first = x_ref[:, cut].astype(jnp.float32) + rows_ref[0:1, cut] * total
            res[:, cut] = first
            res_low[:, cut] = first.astype(low)
        stores[0].start()
        stores[1].start()
        loads[1].wait()
        loads[2].wait()
        for cut in cuts_of(width):
            cq[:, cut] = dot(res_low[...], wq[cut, :], nt).astype(low)
            cv[:, cut] = dot(text_ref[...], wv[cut, :], nt).astype(low)
        for k in range(count):
            held[lax.rem(me + k, count)] = parts[k][tokens:, :]
        ck[...] = jnp.concatenate([held[rank] for rank in range(count)], axis=1)
        for i in (2, 3, 4):
            stores[i].start()
        parts_out = []
        for at in range(0, width, HEAD_DIM):
            head = slice(at, at + HEAD_DIM)
            probs = softmax_keys(ck[:, head], cq[:, head]).astype(low)
            parts_out.append(dot(cv[:, head], probs, tn).T)
        crossed[...] = jnp.concatenate(parts_out, axis=1).astype(low)
        stores[5].start()
        loads[3].wait()
        for cut in cuts_of(width):
            res[:, cut] += dot(crossed[...], wc[:, cut])
        second = res[...]
        center = second - jnp.mean(second, axis=-1, keepdims=True)
        spread = lax.rsqrt(jnp.mean(center * center, axis=-1, keepdims=True) + norm_eps)
        inverse[...] = spread
        scaled = center * spread
        normed[...] = scaled
        stores[6].start()
        stores[7].start()
        out[...] = (scaled * (1.0 + rows_ref[2:3, :]) + rows_ref[1:2, :]).astype(low)
        stores[8].start()
        for store in stores:
            store.wait()

    wide = (tokens, width)
    shapes = [
        (wide, jnp.float32),
        (wide, low),
        (wide, low),
        ((words, width), low),
        ((words, width), low),
        (wide, low),
        (wide, jnp.float32),
        (wide, jnp.float32),
        (wide, low),
    ]
    anywhere = pl.BlockSpec(memory_space=pl.ANY)
    return pl.pallas_call(
        body,
        in_specs=[in_smem()] + [in_vmem()] * (count + 3) + [anywhere] * 4,
        out_specs=[anywhere] * len(shapes) + [in_vmem()],
        out_shape=[jax.ShapeDtypeStruct(*item) for item in shapes]
        + [jax.ShapeDtypeStruct((tokens, 1), jnp.float32)],
        scratch_shapes=[pltpu.VMEM((width, width), low)] * 4
        + [pltpu.VMEM(*item) for item in shapes]
        + [
            pltpu.VMEM((count, words, share), low),
            pltpu.SemaphoreType.DMA((4,)),
            pltpu.SemaphoreType.DMA((len(shapes),)),
        ],
        compiler_params=pltpu.CompilerParams(vmem_limit_bytes=60 * 2**20),
        cost_estimate=cheap,
        name="cross_block",
    )(place, *mixed, hidden, rows, text, w_out, c_query, c_value, c_out)


def cross_back(
    place, terms, grad, rows, normed, inverse, branch, cq, ck, cv, c_out, c_query, w_out, after
):
    count = len(terms)
    tokens, width = grad.shape
    words = ck.shape[0]
    share = width // count
    scale = HEAD_DIM ** (-0.5)

    def body(place_ref, *refs):
        parts = refs[:count]
        grad_ref, rows_ref, i_ref, k_ref, v_ref = refs[count : count + 5]
        far = refs[count + 5 : count + 11]
        refs = refs[: count + 11] + refs[count + 11 + len(after) :]
        stored = refs[count + 11 : count + 15]
        grad_v, sums = refs[count + 15 : count + 17]
        outs = refs[count + 17 : 2 * count + 17]
        near = refs[2 * count + 17 : 2 * count + 23]
        n_ref, wc, q_ref, wq, wo, b_ref = near
        own = refs[2 * count + 23 : 2 * count + 27]
        first, cross_low, grad_q, attn_low = own
        back, held, read, sems = refs[2 * count + 27 :]
        me = place_ref[0]
        loads = [
            pltpu.make_async_copy(source, target, read.at[i])
            for i, (source, target) in enumerate(zip(far, near))
        ]
        stores = [
            pltpu.make_async_copy(source, target, sems.at[i])
            for i, (source, target) in enumerate(zip(own, stored))
        ]
        for load in loads:
            load.start()
        loads[0].wait()
        total = parts[0][...].astype(jnp.float32)
        for part in parts[1:]:
            total += part[...].astype(jnp.float32)
        n = n_ref[...]
        sums[1:2, :] = jnp.sum(total, axis=0, keepdims=True)
        sums[2:3, :] = jnp.sum(total * n, axis=0, keepdims=True)
        second = grad_ref[...].astype(jnp.float32) + norm_back(total, n, i_ref[...], rows_ref[2:3, :])
        first[...] = second
        cross_low[...] = second.astype(low)
        stores[1].start()
        loads[1].wait()
        loads[2].wait()
        for cut in cuts_of(width):
            back[:, cut] = dot(cross_low[...], wc[cut, :], nt).astype(low)
        grads = ([], [], [])
        for at in range(0, width, HEAD_DIM):
            head = slice(at, at + HEAD_DIM)
            q, k, v, g = q_ref[:, head], k_ref[:, head], v_ref[:, head], back[:, head]
            probs = softmax_keys(k, q)
            grad_probs = dot(v, g, nt)
            inner = jnp.sum(probs * grad_probs, axis=0, keepdims=True)
            grad_scores = (probs * (grad_probs - inner)).astype(low)
            grads[0].append((dot(k, grad_scores, tn) * scale).T)
            grads[1].append(dot(grad_scores, q) * scale)
            grads[2].append(dot(probs.astype(low), g))
        grad_q[...] = jnp.concatenate(grads[0], axis=1).astype(low)
        grad_v[...] = jnp.concatenate(grads[2], axis=1).astype(low)
        heads = share // HEAD_DIM
        for rank in range(count):
            pieces = grads[1][rank * heads : (rank + 1) * heads]
            held[rank] = jnp.concatenate(pieces, axis=1).astype(low)
        stores[2].start()
        for load in loads[3:]:
            load.wait()
        for cut in cuts_of(width):
            whole = first[:, cut] + dot(grad_q[...], wq[:, cut])
            first[:, cut] = whole
            attn_low[:, cut] = (rows_ref[0:1, cut] * whole).astype(low)
            sums[0:1, cut] = jnp.sum(b_ref[:, cut] * whole, axis=0, keepdims=True)
        stores[0].start()
        stores[3].start()
        for k in range(count):
            rank = lax.rem(me + k, count)
            here = pl.ds(pl.multiple_of(rank * share, 32), share)
            outs[k][0:tokens, :] = dot(attn_low[...], wo[here, :], nt).astype(low)
            outs[k][tokens:, :] = held[rank]
        for store in stores:
            store.wait()

    wide, square = (tokens, width), (width, width)
    shapes = [
        (wide, jnp.float32),
        (wide, low),
        (wide, low),
        (wide, low),
        ((words, width), low),
        ((3, width), jnp.float32),
    ] + [((tokens + words, share), low)] * count
    anywhere = pl.BlockSpec(memory_space=pl.ANY)
    loaded = [
        pltpu.VMEM(wide, jnp.float32),
        pltpu.VMEM(square, low),
        pltpu.VMEM(wide, low),
        pltpu.VMEM(square, low),
        pltpu.VMEM(square, low),
        pltpu.VMEM(wide, jnp.float32),
    ]
    return pl.pallas_call(
        body,
        in_specs=[in_smem()] + [in_vmem()] * (count + 5) + [anywhere] * (6 + len(after)),
        out_specs=[anywhere] * 4 + [in_vmem()] * (2 + count),
        out_shape=[jax.ShapeDtypeStruct(*item) for item in shapes],
        scratch_shapes=loaded
        + [pltpu.VMEM(*item) for item in shapes[:4]]
        + [
            pltpu.VMEM(wide, low),
            pltpu.VMEM((count, words, share), low),
            pltpu.SemaphoreType.DMA((6,)),
            pltpu.SemaphoreType.DMA((4,)),
        ],
        compiler_params=pltpu.CompilerParams(vmem_limit_bytes=60 * 2**20),
        cost_estimate=costly,
        name="cross_back",
    )(
        place,
        *terms,
        grad,
        rows,
        inverse,
        ck,
        cv,
        normed,
        c_out,
        cq,
        c_query,
        w_out,
        branch,
        *after,
    )


def outer_halves(place, pairs, parts, name):
    width = pairs[0][1].shape[1]
    high = [sum(piece[2] for piece in left) for left, _ in pairs]
    size = high[0] // parts
    tokens = [right.shape[0] for _, right in pairs]
    flat = []

    def index_of(array):
        for i, other in enumerate(flat):
            if other is array:
                return i
        flat.append(array)
        return len(flat) - 1

    plans = [
        ([(index_of(array), *rest) for array, *rest in left], index_of(right))
        for left, right in pairs
    ]
    amount = len(pairs)

    def body(place_ref, *refs):
        ins, (kept, given), (held, sems) = refs[: len(flat)], refs[len(flat) :][:2], refs[-2:]
        turned = refs[len(flat) + 2 : -2]
        me, core = place_ref[0], place_ref[1]
        for i, (left, right) in enumerate(plans):
            for k, (which, lane, lanes, row) in enumerate(left):
                piece = ins[which][0 : tokens[i], lane : lane + lanes]
                piece = piece.astype(jnp.float32).T.astype(low)
                if row is None:
                    rank = lax.rem(me + k, len(left))
                    turned[i][pl.ds(pl.multiple_of(rank * lanes, 32), lanes), :] = piece
                else:
                    turned[i][row : row + lanes, :] = piece
            for part in range(parts):
                at = i * parts + part
                tile = dot(turned[i][part * size : (part + 1) * size, :], ins[right][...])
                held[at] = tile.astype(low)
                for out, side in ((kept, 0), (given, 1)):

                    @pl.when((core ^ (i & 1)) == side)
                    def _():
                        pltpu.make_async_copy(
                            held.at[at], out.at[i // 2, part], sems.at[at]
                        ).start()

        for at in range(amount * parts):
            pltpu.make_async_copy(held.at[at], kept.at[0, 0], sems.at[at]).wait()

    out = jax.ShapeDtypeStruct((amount // 2, parts, size, width), low)
    return pl.pallas_call(
        body,
        in_specs=[in_smem()] + [in_vmem()] * len(flat),
        out_specs=[pl.BlockSpec(memory_space=pl.ANY)] * 2,
        out_shape=[out, out],
        scratch_shapes=[pltpu.VMEM((high[i], tokens[i]), low) for i in range(amount)]
        + [
            pltpu.VMEM((amount * parts, size, width), low),
            pltpu.SemaphoreType.DMA((amount * parts,)),
        ],
        compiler_params=pltpu.CompilerParams(vmem_limit_bytes=60 * 2**20),
        cost_estimate=cheap if parts > 1 else costly,
        name=name,
    )(place, *flat)


def mlp_grads(grad_pres, acts, rows_in, grads_in, after):
    pieces, rights = len(acts), len(rows_in)
    tokens, width = rows_in[0].shape
    hidden = acts[0].shape[1]
    chunk = 384 if hidden % 384 == 0 else hidden
    steps = hidden // chunk

    def body(*refs):
        step = pl.program_id(0)
        lefts_up, lefts_down = refs[:pieces], refs[pieces : 2 * pieces]
        rights_up = refs[2 * pieces : 2 * pieces + rights]
        rights_down = refs[2 * pieces + rights : 2 * pieces + 2 * rights]
        out = refs[-1]

        def terms(lefts, turn, others):
            here = pl.ds(pl.multiple_of(turn * chunk, chunk), chunk)
            total = jnp.zeros((chunk, width), jnp.float32)
            cursor = 0
            for left in lefts:
                for i in range(left.shape[0] // tokens):
                    total += dot(left[i * tokens : (i + 1) * tokens, here], others[cursor][...], tn)
                    cursor += 1
            out[...] = total.astype(low)

        @pl.when(step < steps)
        def _():
            terms(lefts_up, step, rights_up)

        @pl.when(step >= steps)
        def _():
            terms(lefts_down, step - steps, rights_down)

    arrays = (*grad_pres, *acts, *rows_in, *grads_in)
    chunked = pl.BlockSpec((chunk, width), lambda s: (s, 0))
    return pl.pallas_call(
        body,
        grid=(2 * steps,),
        in_specs=[pl.BlockSpec(array.shape, lambda s: (0, 0)) for array in arrays]
        + [pl.BlockSpec(memory_space=pl.ANY)] * len(after),
        out_specs=chunked,
        out_shape=jax.ShapeDtypeStruct((2 * hidden, width), low),
        compiler_params=pltpu.CompilerParams(vmem_limit_bytes=60 * 2**20),
        cost_estimate=cheap,
        name="mlp_grads",
    )(*arrays, *after)


def ranked_terms(place, lefts, order, pieces, weight, factors, name):
    tokens, width = factors[0].shape
    count = len(factors)

    def body(place_ref, *refs):
        ins, weight_ref = refs[: len(lefts)], refs[len(lefts)]
        others = refs[len(lefts) + 1 : len(lefts) + 1 + count]
        out, sums = refs[-2:]
        me = place_ref[0]
        for i, slot in enumerate(order):
            rank = lax.rem(me - slot + count, count)
            for cut in cuts_of(width):
                term = jnp.zeros((tokens, cut.stop - cut.start), jnp.float32)
                for which, row, lane, start, depth in pieces[i]:
                    term += dot(
                        ins[which][row : row + tokens, lane : lane + depth],
                        weight_ref[start : start + depth, cut],
                    )
                out[rank, :, cut] = term.astype(low)
                one = jnp.sum(term, axis=0, keepdims=True)
                two = jnp.sum(term * others[i][:, cut].astype(jnp.float32), axis=0, keepdims=True)
                if i:
                    one, two = one + sums[0:1, cut], two + sums[1:2, cut]
                sums[0:1, cut], sums[1:2, cut] = one, two

    return pl.pallas_call(
        body,
        in_specs=[in_smem()] + [in_vmem()] * (len(lefts) + 1 + count),
        out_shape=[
            jax.ShapeDtypeStruct((count, tokens, width), low),
            jax.ShapeDtypeStruct((2, width), jnp.float32),
        ],
        compiler_params=pltpu.CompilerParams(vmem_limit_bytes=60 * 2**20),
        cost_estimate=cheap if len(lefts) > 2 else costly,
        name=name,
    )(place, *lefts, weight, *factors)


def sum_split(place, kept, got):
    count, unit_rows, width = kept.shape[1], kept.shape[4], kept.shape[5]

    def body(place_ref, one, two, keep_x, give_x, keep_y, give_y):
        x, y = place_ref[0], place_ref[1]

        def total(*index):
            return (one[index].astype(jnp.float32) + two[index].astype(jnp.float32)).astype(low)

        for j in range(2):
            keep_x[0, j] = total(0, 0, j, x)
            give_x[0, j] = total(0, 0, j, 1 - x)
            keep_y[0, j] = total(1, 0, y, j)
            give_y[0, j] = total(1, 0, 1 - y, j)

    block = pl.BlockSpec((2, 1, 2, 2, unit_rows, width), lambda r, *_: (0, r, 0, 0, 0, 0))
    part = pl.BlockSpec((1, 2, unit_rows, width), lambda r, *_: (r, 0, 0, 0))
    return pl.pallas_call(
        body,
        grid_spec=pltpu.PrefetchScalarGridSpec(
            num_scalar_prefetch=1, grid=(count,), in_specs=[block] * 2, out_specs=[part] * 4
        ),
        out_shape=[jax.ShapeDtypeStruct((count, 2, unit_rows, width), low)] * 4,
        compiler_params=pltpu.CompilerParams(vmem_limit_bytes=60 * 2**20),
        cost_estimate=costly,
        name="sum_split",
    )(place, kept, got)


def update_slots(master, first_moment, second_moment, filled, which, position, sources):
    capacity, unit_rows, width = master.shape

    group = math.gcd(capacity, 2)
    steps = capacity // group

    def body(filled_ref, which_ref, position_ref, weight, one, two, *rest):
        ins = rest[: len(sources)]
        new_one, new_two, new_weight, held, sems = rest[len(sources) :]
        step = pl.program_id(0)

        def fetch(turn):
            for i in range(group):
                slot = turn * group + i
                for source, ref in enumerate(ins):

                    @pl.when(which_ref[slot] == source)
                    def _():
                        pltpu.make_async_copy(
                            ref.at[position_ref[slot]], held.at[turn % 2, i], sems.at[turn % 2, i]
                        ).start()

        @pl.when(step == 0)
        def _():
            fetch(step)

        @pl.when(step < steps - 1)
        def _():
            fetch(step + 1)

        for i in range(group):
            pltpu.make_async_copy(
                ins[0].at[0], held.at[step % 2, i], sems.at[step % 2, i]
            ).wait()
            mask = (filled_ref[step * group + i] > 0).astype(jnp.float32)
            grad = held[step % 2, i].astype(jnp.float32)
            results = adamw(weight[i], one[i], two[i], grad, mask, rate)
            new_one[i], new_two[i], new_weight[i] = results

    block = pl.BlockSpec((group, unit_rows, width), lambda s, *_: (s, 0, 0))
    return pl.pallas_call(
        body,
        grid_spec=pltpu.PrefetchScalarGridSpec(
            num_scalar_prefetch=3,
            grid=(steps,),
            in_specs=[block] * 3 + [pl.BlockSpec(memory_space=pl.ANY)] * len(sources),
            out_specs=[block] * 3,
            scratch_shapes=[
                pltpu.VMEM((2, group, unit_rows, width), low),
                pltpu.SemaphoreType.DMA((2, group)),
            ],
        ),
        out_shape=[jax.ShapeDtypeStruct(master.shape, jnp.float32)] * 3,
        compiler_params=pltpu.CompilerParams(vmem_limit_bytes=56 * 2**20),
        cost_estimate=cheap,
        name="update_slots",
    )(filled, which, position, master, first_moment, second_moment, *sources)


def adamw(weight, moment_one, moment_two, gradient, filled, step_rate):
    new_one = beta_one * moment_one + (1.0 - beta_one) * gradient
    new_two = beta_two * moment_two + (1.0 - beta_two) * gradient * gradient
    fixed_one = new_one / (1.0 - beta_one**STEP)
    fixed_two = new_two / (1.0 - beta_two**STEP)
    updated = weight - step_rate * (fixed_one / (jnp.sqrt(fixed_two) + adam_eps) + decay * weight)
    return (new_one * filled, new_two * filled, updated * filled)


def swap(values, axis, bit):
    count = lax.axis_size(axis)
    return lax.ppermute(values, axis, [(i, i ^ (1 << bit)) for i in range(count)])


def choose(values, index, axis):
    return lax.dynamic_index_in_dim(values, index, axis, keepdims=False)


def total_sum(values):
    for axis in ("dp", "tensor"):
        for bit in range(lax.axis_size(axis).bit_length() - 1):
            values = values + swap(values, axis, bit)
    return values


def pick_units(master, slot_unit, state, kind, place, sizes, after=()):
    capacity, unit_rows, width = master.shape
    units = state.shape[0]

    def body(slot_ref, state_ref, kind_ref, place_ref, blocks, *rest):
        outs = rest[len(after) : len(after) + len(sizes)]
        highs, lows, zeros, read, sems = rest[len(after) + len(sizes) :]

        def start(source, unit):
            for which, out in enumerate(outs):

                @pl.when(kind_ref[unit] == which)
                def _():
                    pltpu.make_async_copy(source, out.at[place_ref[unit]], sems.at[unit]).start()

        @pl.loop(0, capacity)
        def _(slot):
            @pl.when(slot_ref[slot] >= 0)
            def _():
                pltpu.make_async_copy(blocks.at[slot], highs.at[slot], read.at[slot]).start()

        zeros[...] = jnp.zeros_like(zeros)

        @pl.loop(0, units)
        def _(unit):
            @pl.when(state_ref[unit] == 0)
            def _():
                start(zeros, unit)

        @pl.loop(0, capacity)
        def _(slot):
            @pl.when(slot_ref[slot] >= 0)
            def _():
                pltpu.make_async_copy(blocks.at[slot], highs.at[slot], read.at[slot]).wait()
                lows[slot] = highs[slot].astype(low)
                start(lows.at[slot], slot_ref[slot])

        @pl.loop(0, units)
        def _(unit):
            @pl.when(state_ref[unit] < 2)
            def _():
                pltpu.make_async_copy(zeros, outs[0].at[0], sems.at[unit]).wait()

    return pl.pallas_call(
        body,
        grid_spec=pltpu.PrefetchScalarGridSpec(
            num_scalar_prefetch=4,
            grid=(1,),
            in_specs=[pl.BlockSpec(memory_space=pl.ANY)] * (1 + len(after)),
            out_specs=[pl.BlockSpec(memory_space=pl.ANY)] * len(sizes),
            scratch_shapes=[
                pltpu.VMEM((capacity, unit_rows, width), jnp.float32),
                pltpu.VMEM((capacity, unit_rows, width), low),
                pltpu.VMEM((unit_rows, width), low),
                pltpu.SemaphoreType.DMA((capacity,)),
                pltpu.SemaphoreType.DMA((units,)),
            ],
        ),
        out_shape=[jax.ShapeDtypeStruct((size, unit_rows, width), low) for size in sizes],
        compiler_params=pltpu.CompilerParams(vmem_limit_bytes=56 * 2**20),
        cost_estimate=cheap,
        name="pick_units",
    )(slot_unit, state, kind, place, master, *after)


def place_blocks(sources, which, position, parts=1):
    amount = which.shape[0]
    shape = sources[0].shape[1:]
    size = amount // parts

    def body(which_ref, position_ref, *rest):
        ins, outs = rest[: len(sources)], rest[len(sources) : len(sources) + parts]
        held, read, sems = rest[len(sources) + parts :]

        @pl.loop(0, amount)
        def _(i):
            for source, ref in enumerate(ins):

                @pl.when(which_ref[i] == source)
                def _():
                    pltpu.make_async_copy(ref.at[position_ref[i]], held.at[i], read.at[i]).start()

        for part, out in enumerate(outs):

            @pl.loop(0, size)
            def _(j):
                i = part * size + j
                pltpu.make_async_copy(ins[0].at[0], held.at[i], read.at[i]).wait()
                pltpu.make_async_copy(held.at[i], out.at[j], sems.at[i]).start()

        @pl.loop(0, amount)
        def _(i):
            pltpu.make_async_copy(held.at[i], outs[0].at[0], sems.at[i]).wait()

    return pl.pallas_call(
        body,
        grid_spec=pltpu.PrefetchScalarGridSpec(
            num_scalar_prefetch=2,
            grid=(1,),
            in_specs=[pl.BlockSpec(memory_space=pl.ANY)] * len(sources),
            out_specs=[pl.BlockSpec(memory_space=pl.ANY)] * parts,
            scratch_shapes=[
                pltpu.VMEM((amount,) + shape, low),
                pltpu.SemaphoreType.DMA((amount,)),
                pltpu.SemaphoreType.DMA((amount,)),
            ],
        ),
        out_shape=[jax.ShapeDtypeStruct((size,) + shape, low)] * parts,
        compiler_params=pltpu.CompilerParams(vmem_limit_bytes=56 * 2**20),
        cost_estimate=cheap,
        name="place_blocks",
    )(which, position, *sources)


def stack_pairs(pairs):
    shape = (len(pairs),) + pairs[0].shape[1:]

    def body(*refs):
        for i, pair in enumerate(refs[:-2]):
            for half in range(2):
                refs[half - 2][i] = pair[half]

    return pl.pallas_call(
        body,
        out_shape=[jax.ShapeDtypeStruct(shape, low)] * 2,
        cost_estimate=costly,
        name="stack_pairs",
    )(*pairs)


def hops(values, step, turn):
    count = lax.axis_size("tensor")
    if step > 0:
        pairs = [(i, i + 1) for i in range(turn - 1, count - 1)]
    else:
        pairs = [(i, i - 1) for i in range(1, count - turn + 1)]
    return lax.ppermute(values, "tensor", pairs)


fence = lax.optimization_barrier


def in_pool(member, inner, inner_count):
    me = lax.axis_index("dp")
    half, core = member >> 3, ((member >> 2) & 1) ^ (me & 1)
    far_y, far_x = ((member >> 1) & 1) ^ ((me >> 2) & 1), (member & 1) ^ ((me >> 1) & 1)
    where_first = (far_y * 2 + far_x) * inner_count
    where_second = (4 + far_x * 2 + far_y) * inner_count
    return (core, jnp.where(half == 0, where_first, where_second) + inner)


def on_device(
    hidden_in,
    time_embed,
    caption_table,
    caption_ids,
    owners,
    master,
    first_moment,
    second_moment,
    mod_table,
    mod_first,
    mod_second,
    out_grad,
):
    count = lax.axis_size("tensor")
    dp_count = lax.axis_size("dp")
    me_dp = lax.axis_index("dp")
    me_tensor = lax.axis_index("tensor")
    capacity, unit_rows, width = master.shape
    units = owners.shape[0]
    tokens = hidden_in.shape[1]
    text_count = caption_ids.shape[1]
    share = width // count
    per = share // unit_rows
    ups = (units - 8 * per) // 2
    rank_of = ranks_of(owners)
    mine = owners == me_dp
    match = (rank_of[None, :] == jnp.arange(capacity)[:, None]) & mine[None, :]
    filled = jnp.any(match, axis=1)
    unit_of_slot = jnp.sum(jnp.where(match, jnp.arange(units)[None, :], 0), axis=1)

    square = [list(range(i * per, (i + 1) * per)) for i in range(8)]
    group_attn = square[0] + square[1] + square[2] + square[5]
    group_full = square[3] + square[4] + square[6] + square[7]
    group_mlp = list(range(8 * per, units))
    members = len(group_attn)
    plane = dp_count == 8 and members == 16 and len(group_mlp) % dp_count == 0
    member_of = np.zeros(units, np.int32)
    member_of[group_attn] = np.arange(members)
    member_of[group_full] = np.arange(members)
    is_attn = np.zeros(units, bool)
    is_attn[group_attn] = True
    is_mlp = np.zeros(units, bool)
    is_mlp[group_mlp] = True

    latent_in = hidden_in[0].astype(jnp.float32)
    modulate = mod_table + time_embed[0]

    def mod_row(which_row):
        return modulate[which_row][None, :]

    normed_one, inverse_one = layer_norm(latent_in)
    bits = dp_count.bit_length() - 1
    vocab_rows = caption_table.shape[0]

    def caption_terms(ids):
        chosen = ids.reshape(-1) - me_dp * vocab_rows
        onehot = (chosen[:, None] == jnp.arange(vocab_rows)[None, :]).astype(low)
        terms = jnp.dot(onehot, caption_table, preferred_element_type=jnp.float32).astype(low)
        return terms.reshape(dp_count, text_count, -1)

    def modulated(normed):
        return (normed.astype(jnp.float32) * (1.0 + mod_row(1)) + mod_row(0)).astype(low)

    def whole_text(text_ring):
        return from_ring(text_ring, -1).transpose(1, 0, 2).reshape(text_count, width)

    def own_keys(text_low, w_attn):
        return project(text_low, w_attn)[:, 3 * share :].astype(low)

    def exchanged(attended, keys):
        parts = [
            jnp.concatenate([attended[k * tokens : (k + 1) * tokens], keys]) for k in range(count)
        ]
        return [parts[0]] + [shift(parts[k], count - k) for k in range(1, count)]

    where = jnp.stack([me_tensor, me_dp & 1]).astype(jnp.int32)

    n_low = normed_one.astype(low)
    if plane:
        core, far_x, far_y = (
            ((member_of >> 2) & 1) ^ (me_dp & 1),
            (member_of & 1) ^ ((me_dp >> 1) & 1),
            ((member_of >> 1) & 1) ^ ((me_dp >> 2) & 1),
        )
        place = jnp.where(is_attn, far_x * 4 + far_y * 2, 8 + far_y * 4 + far_x * 2)
        place = jnp.where(is_mlp, np.arange(units) - 8 * per, place + (member_of >> 3))
        kind = jnp.where(is_mlp, 0, core)
        slot_mlp = unit_of_slot >= 8 * per
        owned_state = mine.astype(jnp.int32)
        ids = lax.all_gather(caption_ids, "dp", axis=0, tiled=True)
        ids = jnp.take(ids, me_dp ^ jnp.arange(dp_count), axis=0, mode="clip")
        up, down = hops(n_low, 1, 1), hops(n_low, -1, 1)
        kept, given = pick_units(
            master,
            jnp.where(filled & ~slot_mlp, unit_of_slot, -1),
            jnp.where(is_mlp, 2, owned_state),
            kind,
            place,
            (members, members),
        )
        got = swap(given, "dp", 0)
        (mlp_part,) = pick_units(
            master,
            jnp.where(filled & slot_mlp, unit_of_slot, -1),
            jnp.where(is_mlp, owned_state, 2),
            kind,
            place,
            (len(group_mlp),),
            (kept,),
        )
        mlp_part = lax.psum_scatter(mlp_part, "dp", scatter_dimension=0, tiled=True)
        n_up, n_down = [up], [down]
        kept, got, up, down, ids = fence((kept, got, up, down, ids))
        pieces = [kept[i : i + 4] + got[i : i + 4] for i in range(0, members, 4)]
        attn_two, attn_send, full_two, full_send = fence(tuple(pieces))
        up, down = hops(up, 1, 2), hops(down, -1, 2)
        attn_got = swap(attn_send, "dp", 1)
        full_got = swap(full_send, "dp", 2)
        text = caption_terms(ids)
        text = text[0:4] + swap(text[4:8], "dp", 2)
        n_up.append(up), n_down.append(down)
        attn_two, attn_got, full_two, full_got, up, down, text = fence(
            (attn_two, attn_got, full_two, full_got, up, down, text)
        )
        pieces = [x[i : i + 2] + y[i : i + 2] for x, y in ((attn_two, attn_got), (full_two, full_got)) for i in (0, 2)]
        attn_one, attn_send, full_one, full_send = fence(tuple(pieces))
        up, down = hops(up, 1, 3), hops(down, -1, 3)
        attn_got = swap(attn_send, "dp", 2)
        full_got = swap(full_send, "dp", 1)
        text = text[0:2] + swap(text[2:4], "dp", 1)
        n_up.append(up), n_down.append(down)
        attn_one, attn_got, full_one, full_got, up, down, text, mlp_part = fence(
            (attn_one, attn_got, full_one, full_got, up, down, text, mlp_part)
        )
        attn_one, full_one = attn_one + attn_got, full_one + full_got
        n_up[-1], n_down[-1] = up, down
        w_mlp = lax.all_gather(mlp_part, "dp", axis=0, tiled=True)
        first_ring, second_ring = stack_pairs(ring(full_one))
        first = jnp.concatenate([attn_one[0:1], swap(attn_one[0:1], "dp", 1)])
        second = jnp.concatenate([attn_one[1:2], swap(attn_one[1:2], "dp", 2)])
        pool = jnp.concatenate([first, swap(first, "dp", 2), second, swap(second, "dp", 1)])
        other = swap(pool, "dp", 0)
        text = text[0] + swap(text[1], "dp", 0)
        *n_slots, h_one_all = line_slots(
            where, n_low, n_up, n_down, jnp.concatenate([mod_row(0), mod_row(1)])
        )
        n_slots = [n_low] + n_slots
        grad_own = out_grad[0]
        pool, other, first_ring, second_ring, h_one_all, text, grad_own = fence(
            (pool, other, first_ring, second_ring, h_one_all, text, grad_own)
        )
        grad_whole = lax.all_gather(grad_own, "tensor", axis=0)
        first, second = first_ring, second_ring
        first_got = swap(first, "dp", 1)
        second_got = swap(second, "dp", 2)
        text_ring = ring(text)
        (w_attn,) = place_blocks((pool, other), *in_pool(np.arange(members), 0, 1))
        w_attn = w_attn.reshape(-1, width)
        qkv = project(h_one_all, w_attn).astype(low)
        attended, logs = self_attend(qkv, share)
        first = jnp.concatenate([first, first_got])
        second = jnp.concatenate([second, second_got])
        first, second, text_ring, attended, logs, w_attn, w_mlp = fence(
            (first, second, text_ring, attended, logs, w_attn, w_mlp)
        )
        first_far, second_far = swap(first, "dp", 2), swap(second, "dp", 1)
        text_low = whole_text(jnp.stack(text_ring))
        mixed = exchanged(attended, own_keys(text_low, w_attn))
        first_far, second_far, mixed = fence((first_far, second_far, mixed))
        first_other, second_other = swap(first, "dp", 0), swap(second, "dp", 0)
        first_last, second_last = swap(first_far, "dp", 0), swap(second_far, "dp", 0)
        listing = np.arange(count * members)
        matrix, rank, head = listing // (count * per), listing // per % count, listing % per
        slot = lax.rem(me_tensor - rank + count, count)
        which, position = in_pool(matrix * per + head, slot, count)
        blocks = 2 * count
        w_full = place_blocks(
            (first, first_far, second, second_far, first_other, first_last, second_other, second_last),
            which * 4 + position // blocks,
            position % blocks,
            parts=4,
        )
        w_full = [part.reshape(width, width) for part in w_full]
        w_full[3], grad_whole = fence((w_full[3], grad_whole))
    else:
        slots_low = master.astype(low)
        rows = jnp.take(slots_low, rank_of, axis=0, mode="clip")
        rows = lax.psum(jnp.where(mine[:, None, None], rows, jnp.zeros((), low)), "dp")
        w_attn = rows[np.array(group_attn)].reshape(-1, width)
        w_full = lax.all_gather(rows[np.array(group_full)], "tensor", axis=0)
        w_full = w_full.reshape(count, 4, share, width).swapaxes(0, 1).reshape(4, width, width)
        w_full = [w_full[i] for i in range(4)]
        w_mlp = rows[8 * per :]
        n_slots = ring(n_low)
        normed_all = jnp.concatenate(n_slots)
        grad_whole = lax.all_gather(out_grad[0], "tensor", axis=0)
        ids = caption_ids
        for bit in range(bits):
            ids = jnp.concatenate([ids, swap(ids, "dp", bit)])
        text = caption_terms(ids)
        for bit in reversed(range(bits)):
            text = text[: 1 << bit] + swap(text[1 << bit :], "dp", bit)
        text_low = whole_text(jnp.stack(ring(text[0])))
        h_one_all = modulated(normed_all)
        qkv = project(h_one_all, w_attn).astype(low)
        attended, logs = self_attend(qkv, share)
        mixed = exchanged(attended, own_keys(text_low, w_attn))
    w_cross = w_full
    w_out, c_query, c_value, c_out = w_full
    w_mlp = w_mlp.reshape(-1, width)

    rows = jnp.concatenate([mod_row(2), mod_row(3), mod_row(4)])
    (
        branch_one,
        first_low,
        cq_rows,
        ck_rows,
        cv_rows,
        crossed,
        second_res,
        normed_two,
        h_two,
        inverse_two,
    ) = cross_block(
        where, mixed, hidden_in[0], rows, text_low, *w_cross
    )

    h_slots = {0: h_two}
    out_slots = [
        choose(grad_whole, lax.rem(me_tensor - k + count, count), 0) for k in range(count)
    ]
    grad_slots = [(mod_row(5) * item.astype(jnp.float32)).astype(low) for item in out_slots]
    near = [k for k in range(1, count) if 2 * k != count]
    far = [k for k in range(1, count) if 2 * k == count]
    acts, grad_pres, grad_terms, order = [], [], [], []
    for k in near:
        h_slots[k] = shift(h_two, k)
    for members_now in ([0], near, far):
        act, grad_pre, *terms = mlp_core(
            [h_slots[k] for k in members_now],
            [grad_slots[k] for k in members_now],
            w_mlp,
            acts[-1:],
        )
        if members_now == [0]:
            h_two, act = fence((h_two, act))
            for k in far:
                h_slots[k] = shift(h_two, k)
        acts.append(act), grad_pres.append(grad_pre)
        order += members_now
        grad_terms += [
            shift(term, count - k) if k else term for k, term in zip(members_now, terms)
        ]
    mlp_grad = mlp_grads(
        grad_pres,
        acts,
        [h_slots[k] for k in order],
        [grad_slots[k] for k in order],
        grad_terms[1:2],
    ).reshape(-1, unit_rows, width)
    hidden_share = w_mlp.shape[0] // 2
    pieces = [
        [(which, row, 0, hidden_share, hidden_share)]
        for which, act in enumerate(acts)
        for row in range(0, act.shape[0], tokens)
    ]
    branch_terms, branch_sums = ranked_terms(
        where, acts, order, pieces, w_mlp, [out_slots[k] for k in order], "mlp_out"
    )
    branch_row = branch_sums[1]
    grad_terms, branch_terms = fence((grad_terms, branch_terms))
    if plane:
        mlp_sum = lax.psum_scatter(mlp_grad, "dp", scatter_dimension=0, tiled=True)

    (
        first_grad,
        cross_low,
        grad_cq,
        attn_low,
        grad_cv,
        row_sums,
        *grad_mixed,
    ) = cross_back(
        where,
        grad_terms,
        out_grad[0],
        rows,
        normed_two,
        inverse_two,
        branch_one,
        cq_rows,
        ck_rows,
        cv_rows,
        c_out,
        c_query,
        w_out,
        (),
    )

    grad_parts = [grad_mixed[0]] + [shift(grad_mixed[k], k) for k in range(1, count)]
    full_pairs = [
        ([(item, 0, share, None) for item in mixed], attn_low),
        ([(grad_cq, 0, width, 0)], first_low),
        ([(grad_cv, 0, width, 0)], text_low),
        ([(crossed, 0, width, 0)], cross_low),
    ]
    half = (share // HEAD_DIM // 2) * HEAD_DIM
    spans = [(0, half), (half, share)]

    def attention_pairs(grads, grad_parts):
        keys = sum(item[tokens:].astype(jnp.float32) for item in grad_parts).astype(low)
        pairs = [
            (
                [
                    (item, i * (end - begin), end - begin, begin)
                    for item, (begin, end) in zip(grads, spans)
                ],
                h_one_all,
            )
            for i in range(3)
        ]
        return pairs + [([(keys, 0, share, 0)], text_low)]

    def input_terms(grads):
        pieces = [
            [
                (which, slot * tokens, i * (end - begin), i * share + begin, end - begin)
                for which, (begin, end) in enumerate(spans)
                for i in range(3)
            ]
            for slot in range(count)
        ]
        return ranked_terms(where, grads, range(count), pieces, w_attn, n_slots, "attn_terms")

    if plane:
        x_bit, y_bit = (me_dp >> 1) & 1, (me_dp >> 2) & 1

        def split(total, bit, axis):
            return (choose(total, bit, axis), choose(total, 1 - bit, axis))

        kept, given = outer_halves(where, full_pairs, count, "full_grads")
        got = swap(given, "dp", 0)
        grad_parts, kept, got, branch_terms = fence((grad_parts, kept, got, branch_terms))
        branch_two = lax.psum_scatter(
            branch_terms.reshape(-1, width), "tensor", scatter_dimension=0, tiled=True
        )
        box = (2, count, 2, 2, unit_rows, width)
        bits_here = jnp.stack([x_bit, y_bit]).astype(jnp.int32)
        kept_one, given_one, kept_two, given_two = sum_split(
            bits_here, kept.reshape(box), got.reshape(box)
        )
        got_one, got_two = swap(given_one, "dp", 1), swap(given_two, "dp", 2)
        grads_early = self_attend_back(qkv, grad_parts, attended, logs, share, *spans[0])
        kept_one, got_one, kept_two, got_two, grads_early, grad_parts = fence(
            (kept_one, got_one, kept_two, got_two, grads_early, grad_parts)
        )
        kept_one, given_one = split(kept_one + got_one, y_bit, 1)
        kept_two, given_two = split(kept_two + got_two, x_bit, 1)
        kept_one, given_one, kept_two, given_two, grad_parts = fence(
            (kept_one, given_one, kept_two, given_two, grad_parts)
        )
        got_one, got_two = swap(given_one, "dp", 2), swap(given_two, "dp", 1)
        grads_late = self_attend_back(qkv, grad_parts, attended, logs, share, *spans[1])
        kept_one, got_one, kept_two, got_two, grads_early, grads_late, mlp_sum = fence(
            (kept_one, got_one, kept_two, got_two, grads_early, grads_late, mlp_sum)
        )
        mlp_sum = lax.all_gather(mlp_sum, "dp", axis=0, tiled=True)
        full_parts = to_ring(jnp.stack([kept_one + got_one, kept_two + got_two], axis=1))
        full_parts = [full_parts[k] for k in range(count)]
        full_parts, grads_early, grads_late = fence((full_parts, grads_early, grads_late))
        grads_qkv = [grads_early, grads_late]
        full_got = [shift(full_parts[k], k) for k in range(1, count)]
        attn_kept, attn_given = outer_halves(
            where, attention_pairs(grads_qkv, grad_parts), 1, "attn_grads"
        )
        attn_got = swap(attn_given, "dp", 0)
        grad_h_terms, grad_h_sums = input_terms(grads_qkv)
        mod_terms = jnp.concatenate([grad_h_sums, row_sums, branch_row[None]])
        grad_h_one = lax.psum_scatter(
            grad_h_terms.reshape(-1, width), "tensor", scatter_dimension=0, tiled=True
        )
        attn_kept, attn_got, mod_terms, branch_two = fence(
            (attn_kept, attn_got, mod_terms, branch_two)
        )
        attn_all = (attn_kept + attn_got).reshape(2, 2, 2, unit_rows, width)
        one_kept, one_given = split(attn_all[0], x_bit, 1)
        two_kept, two_given = split(attn_all[1], y_bit, 0)
        one_got, two_got = swap(one_given, "dp", 1), swap(two_given, "dp", 2)
        for bit in range(2):
            mod_terms = mod_terms + swap(mod_terms, "dp", bit)
        full_own = full_parts[0]
        one_kept, one_got, two_kept, two_got, mod_terms, full_own, full_got = fence(
            (one_kept, one_got, two_kept, two_got, mod_terms, full_own, full_got)
        )
        full_sum = full_own.astype(jnp.float32)
        for part in full_got:
            full_sum = full_sum + part.astype(jnp.float32)
        full_sum = full_sum.astype(low)
        one_kept, one_given = split(one_kept + one_got, y_bit, 0)
        two_kept, two_given = split(two_kept + two_got, x_bit, 0)
        one_got, two_got = swap(one_given, "dp", 2), swap(two_given, "dp", 1)
        mod_terms = mod_terms + swap(mod_terms, "dp", 2)
        one_kept, one_got, two_kept, two_got, full_sum, mod_terms, mlp_sum = fence(
            (one_kept, one_got, two_kept, two_got, full_sum, mod_terms, mlp_sum)
        )
        first = jnp.stack([one_kept + one_got, full_sum[0]])
        second = jnp.stack([two_kept + two_got, full_sum[1]])
        first_got, second_got = swap(first, "dp", 1), swap(second, "dp", 2)
        first = jnp.concatenate([first, first_got])
        second = jnp.concatenate([second, second_got])
        mod_terms = mod_terms + swap(mod_terms, "tensor", 0)
        first, second, mod_terms = fence((first, second, mod_terms))
        first_far, second_far = swap(first, "dp", 2), swap(second, "dp", 1)
        for bit in range(1, count.bit_length() - 1):
            mod_terms = mod_terms + swap(mod_terms, "tensor", bit)
        first, first_far, second, second_far, mod_terms = fence(
            (first, first_far, second, second_far, mod_terms)
        )
        pool = jnp.concatenate([first, first_far, second, second_far])
        other = swap(pool, "dp", 0)
        mod_grad = mod_terms
        pool, other = fence((pool, other))
        which, position = in_pool(member_of, np.where(is_attn, 0, 1), 2)
        which = jnp.where(is_mlp, 2, which)
        position = jnp.where(is_mlp, np.arange(units) - 8 * per, position)
        own = jnp.sum(jnp.where(match[:, :, None], jnp.stack([which, position], 1)[None], 0), axis=1)
        new_first, new_second, new_master = update_slots(
            master,
            first_moment,
            second_moment,
            filled.astype(jnp.int32),
            own[:, 0],
            own[:, 1],
            (pool, other, mlp_sum),
        )
    else:
        branch_two = lax.psum_scatter(
            branch_terms.reshape(-1, width), "tensor", scatter_dimension=0, tiled=True
        )
        grads_qkv = [self_attend_back(qkv, grad_parts, attended, logs, share, *span) for span in spans]
        attn_grads = [
            outer(array[:, lane : lane + lanes], right).astype(low)
            for left, right in attention_pairs(grads_qkv, grad_parts)
            for array, lane, lanes, row in left
        ]
        grad_h_terms, grad_h_sums = input_terms(grads_qkv)
        grad_h_one = lax.psum_scatter(
            grad_h_terms.reshape(-1, width), "tensor", scatter_dimension=0, tiled=True
        )
        mixed_all = from_ring(jnp.stack([item[:tokens] for item in mixed]), 1)
        mixed_all = mixed_all.transpose(1, 0, 2).reshape(tokens, width)
        full_grads = [outer(mixed_all, attn_low)]
        full_grads += [outer(left[0][0], right) for left, right in full_pairs[1:]]
        full_sum = [g.astype(low).reshape(count, share, width) for g in full_grads]
        full_sum = jnp.stack(full_sum, axis=1)
        full_sum = lax.psum_scatter(full_sum, "tensor", scatter_dimension=0, tiled=True)
        order = np.array(group_attn + group_full + group_mlp)
        sums = jnp.concatenate(
            [jnp.concatenate(attn_grads), full_sum.reshape(-1, width), mlp_grad.reshape(-1, width)]
        )
        sums = lax.psum(sums.reshape(units, unit_rows, width), "dp")
        owned = jnp.take(sums, jnp.array(np.argsort(order))[unit_of_slot], axis=0, mode="clip")
        mod_grad = total_sum(jnp.concatenate([grad_h_sums, row_sums, branch_row[None]]))
        new_first, new_second, new_master = adamw(
            master,
            first_moment,
            second_moment,
            owned.astype(jnp.float32),
            filled.astype(jnp.float32)[:, None, None],
            rate,
        )
    branch_two, second_res, grad_h_one, new_first = fence(
        (branch_two, second_res, grad_h_one, new_first)
    )
    grad_h_one = grad_h_one.astype(jnp.float32)
    block_out = second_res + mod_row(5) * branch_two.astype(jnp.float32)
    input_grad = first_grad + norm_back(grad_h_one, normed_one, inverse_one, mod_row(1))
    mod_new_first, mod_new_second, mod_new = adamw(
        mod_table, mod_first, mod_second, mod_grad, 1.0, table_rate
    )
    return (
        block_out[None],
        input_grad[None],
        new_first,
        new_second,
        new_master,
        mod_new_first,
        mod_new_second,
        mod_new,
    )


def solution(mesh):
    in_specs = (
        P("dp", "tensor", None),
        P("dp", None, None),
        P("dp", "tensor"),
        P("dp", None),
        P(),
        P("dp", "tensor", None),
        P("dp", "tensor", None),
        P("dp", "tensor", None),
        P(),
        P(),
        P(),
        P("dp", "tensor", None),
    )
    out_specs = (
        P("dp", "tensor", None),
        P("dp", "tensor", None),
        P("dp", "tensor", None),
        P("dp", "tensor", None),
        P("dp", "tensor", None),
        P(),
        P(),
        P(),
    )
    return jax.shard_map(
        on_device, mesh=mesh, in_specs=in_specs, out_specs=out_specs, check_vma=False
    )
```

```python
import math

import jax
import jax.numpy as jnp
import numpy as np
from jax import lax
from jax.experimental import pallas as pl
from jax.experimental.pallas import tpu as pltpu
from jax.sharding import PartitionSpec as P

HEAD_DIM = 72
STEP = 10


norm_eps = 1e-06
beta_one = 0.9
beta_two = 0.999
rate = 0.03
table_rate = 0.3
decay = 0.01
adam_eps = 1e-08
low = jnp.bfloat16


def ranks_of(owners):
    index = jnp.arange(owners.shape[0])
    before = (owners[None, :] == owners[:, None]) & (index[None, :] < index[:, None])
    return jnp.sum(before.astype(jnp.int32), axis=1)


def layer_norm(values):
    center = values - jnp.mean(values, axis=-1, keepdims=True)
    inverse = lax.rsqrt(jnp.mean(center * center, axis=-1, keepdims=True) + norm_eps)
    return (center * inverse, inverse)


def norm_back(grad_rows, normed, inverse, scale_row):
    scaled = grad_rows * (1.0 + scale_row)
    mean_one = jnp.mean(scaled, axis=-1, keepdims=True)
    mean_two = jnp.mean(scaled * normed, axis=-1, keepdims=True)
    return inverse * (scaled - mean_one - normed * mean_two)


def project(rows, weight):
    return jnp.einsum("ld,rd->lr", rows, weight, preferred_element_type=jnp.float32)


def expand(rows, weight):
    return jnp.einsum("lr,rd->ld", rows, weight, preferred_element_type=jnp.float32)


def outer(left, right):
    return jnp.einsum("lr,ld->rd", left, right, preferred_element_type=jnp.float32)


def shift(values, step):
    count = lax.axis_size("tensor")
    return lax.ppermute(values, "tensor", [(i, (i + step) % count) for i in range(count)])


def ring(values):
    return [values] + [shift(values, k) for k in range(1, lax.axis_size("tensor"))]


def to_ring(stacked):
    count = stacked.shape[0]
    twice = jnp.concatenate([stacked, stacked], axis=0)
    return lax.dynamic_slice_in_dim(twice, lax.axis_index("tensor"), count, 0)


def from_ring(stacked, sign):
    count = stacked.shape[0]
    me = lax.axis_index("tensor")
    place = lax.rem(sign * (jnp.arange(count) - me) + 2 * count, count)
    return jnp.take(stacked, place, axis=0, mode="clip")


cheap = pl.CostEstimate(flops=1000, bytes_accessed=1000, transcendentals=0)
costly = pl.CostEstimate(flops=10**10, bytes_accessed=10**7, transcendentals=0)


def self_attend(qkv, share):
    length = qkv.shape[0]
    rows = min(512, length)
    curve = HEAD_DIM ** (-0.5) * math.log2(math.e)
    heads = share // HEAD_DIM

    def body(qkv_ref, out_ref, log_ref):
        @pl.loop(0, length // rows)
        def _(step):
            here = pl.ds(pl.multiple_of(step * rows, rows), rows)
            parts = []
            for head in range(heads):
                at = head * HEAD_DIM
                q = qkv_ref[here, at : at + HEAD_DIM]
                k = qkv_ref[:, share + at : share + at + HEAD_DIM]
                v = qkv_ref[:, 2 * share + at : 2 * share + at + HEAD_DIM]
                scores = dot(k, q, nt)
                top = jnp.max(scores, axis=0, keepdims=True)
                expo = jnp.exp2((scores - top) * curve)
                total = jnp.sum(expo, axis=0, keepdims=True)
                log_ref[head : head + 1, here] = top * curve + jnp.log2(total)
                parts.append((dot(v, expo.astype(low), tn) * (1.0 / total)).T)
            out_ref[here, :] = jnp.concatenate(parts, axis=1).astype(low)

    return pl.pallas_call(
        body,
        out_shape=[
            jax.ShapeDtypeStruct((length, share), low),
            jax.ShapeDtypeStruct((heads, length), jnp.float32),
        ],
        compiler_params=pltpu.CompilerParams(vmem_limit_bytes=40 * 2**20),
        cost_estimate=cheap,
        name="self_attend",
    )(qkv)


def self_attend_back(qkv, grads, mixed, logs, share, begin, end):
    length = qkv.shape[0]
    rows = length // len(grads)
    span = end - begin
    scale = HEAD_DIM ** (-0.5)
    curve = scale * math.log2(math.e)

    def body(qkv_ref, mixed_ref, log_ref, *refs):
        grad_refs, (out_ref, grad_k, grad_v) = refs[: len(grads)], refs[len(grads) :]
        for step, grad_ref in enumerate(grad_refs):
            here = slice(step * rows, (step + 1) * rows)
            parts = []
            for head, at in enumerate(range(begin, end, HEAD_DIM)):
                q = qkv_ref[here, at : at + HEAD_DIM]
                k = qkv_ref[:, share + at : share + at + HEAD_DIM]
                v = qkv_ref[:, 2 * share + at : 2 * share + at + HEAD_DIM]
                g = grad_ref[0:rows, at : at + HEAD_DIM]
                o = mixed_ref[here, at : at + HEAD_DIM]
                inner = g.astype(jnp.float32) * o.astype(jnp.float32)
                inner = jnp.sum(inner.T, axis=0, keepdims=True)
                which = begin // HEAD_DIM + head
                probs = jnp.exp2(dot(k, q, nt) * curve - log_ref[which : which + 1, here])
                grad_scores = (probs * (dot(v, g, nt) - inner)).astype(low)
                to_v = dot(probs.astype(low), g)
                to_k = dot(grad_scores, q)
                if step:
                    grad_v[head] += to_v
                    grad_k[head] += to_k
                else:
                    grad_v[head] = to_v
                    grad_k[head] = to_k
                parts.append((dot(k, grad_scores, tn) * scale).T)
            out_ref[here, 0:span] = jnp.concatenate(parts, axis=1).astype(low)
        heads = range(span // HEAD_DIM)
        both = [grad_k[head] * scale for head in heads]
        out_ref[:, span : 2 * span] = jnp.concatenate(both, axis=1).astype(low)
        both = [grad_v[head] for head in heads]
        out_ref[:, 2 * span :] = jnp.concatenate(both, axis=1).astype(low)

    return pl.pallas_call(
        body,
        out_shape=jax.ShapeDtypeStruct((length, 3 * span), low),
        scratch_shapes=[pltpu.VMEM((span // HEAD_DIM, length, HEAD_DIM), jnp.float32)] * 2,
        compiler_params=pltpu.CompilerParams(vmem_limit_bytes=40 * 2**20),
        cost_estimate=costly,
        name="self_attend_back",
    )(qkv, mixed, logs, *grads)


def mlp_core(rows_in, grads_in, w_mlp, after):
    groups = len(rows_in)
    tokens, width = rows_in[0].shape
    hidden = w_mlp.shape[0] // 2
    chunk = 384 if hidden % 384 == 0 else hidden
    steps = hidden // chunk
    curve = 0.7978845608028654

    def body(*refs):
        rows, grads = refs[:groups], refs[groups : 2 * groups]
        up, down = refs[2 * groups : 2 * groups + 2]
        act, grad_pre, *outs = refs[2 * groups + 2 + len(after) : -1]
        total = refs[-1]
        step = pl.program_id(0)
        for i in range(groups):
            pre = lax.dot_general(
                rows[i][...], up[...], (((1,), (1,)), ((), ())), preferred_element_type=jnp.float32
            )
            square = pre * pre
            bend = jnp.tanh(curve * pre * (1.0 + 0.044715 * square))
            half = 0.5 * (1.0 + bend)
            here = pl.ds(i * tokens, tokens)
            act[here, :] = (pre * half).astype(low)
            slope = half + (0.5 * curve) * pre * (1.0 - bend * bend) * (1.0 + 0.134145 * square)
            grad_act = lax.dot_general(
                grads[i][...], down[...], (((1,), (1,)), ((), ())), preferred_element_type=jnp.float32
            )
            grad_low = (grad_act * slope).astype(low)
            grad_pre[here, :] = grad_low
            term = jnp.dot(grad_low, up[...], preferred_element_type=jnp.float32)

            @pl.when(step == 0)
            def _():
                total[here, :] = term

            @pl.when(step > 0)
            def _():
                total[here, :] += term

            @pl.when(step == steps - 1)
            def _():
                outs[i][...] = total[here, :].astype(low)

    whole = pl.BlockSpec((tokens, width), lambda s: (0, 0))
    across = pl.BlockSpec((groups * tokens, chunk), lambda s: (0, s))
    return pl.pallas_call(
        body,
        grid=(steps,),
        in_specs=[whole] * (2 * groups)
        + [
            pl.BlockSpec((chunk, width), lambda s: (s, 0)),
            pl.BlockSpec((chunk, width), lambda s: (steps + s, 0)),
        ]
        + [pl.BlockSpec(memory_space=pl.ANY)] * len(after),
        out_specs=[across, across] + [whole] * groups,
        out_shape=[jax.ShapeDtypeStruct((groups * tokens, hidden), low)] * 2
        + [jax.ShapeDtypeStruct((tokens, width), low)] * groups,
        scratch_shapes=[pltpu.VMEM((groups * tokens, width), jnp.float32)],
        compiler_params=pltpu.CompilerParams(vmem_limit_bytes=60 * 2**20),
        cost_estimate=cheap,
        name="mlp_core",
    )(*rows_in, *grads_in, w_mlp, w_mlp, *after)


nt = (((1,), (1,)), ((), ()))
tn = (((0,), (0,)), ((), ()))


def dot(left, right, dims=(((1,), (0,)), ((), ()))):
    return lax.dot_general(left, right, dims, preferred_element_type=jnp.float32)


def softmax_keys(keys, queries):
    scores = dot(keys, queries, nt) * HEAD_DIM ** (-0.5)
    expo = jnp.exp(scores - jnp.max(scores, axis=0, keepdims=True))
    return expo * (1.0 / jnp.sum(expo, axis=0, keepdims=True))


def cuts_of(width):
    size = 384 if width % 384 == 0 else width
    return [slice(i, i + size) for i in range(0, width, size)]


def in_smem():
    return pl.BlockSpec(memory_space=pltpu.SMEM)


def in_vmem():
    return pl.BlockSpec(memory_space=pltpu.VMEM)


def line_slots(place, both, rows):
    count, _, tokens, width = both.shape

    def body(place_ref, both_ref, rows_ref, out, *refs):
        plain, grads, gated = refs[:count], refs[count : 2 * count], refs[2 * count :]
        me = place_ref[0]
        for slot in range(count):
            rank = lax.rem(me - slot + count, count)
            value = both_ref[rank, 0]
            plain[slot][...] = value
            value = value.astype(jnp.float32) * (1.0 + rows_ref[1:2, :]) + rows_ref[0:1, :]
            out[slot * tokens : (slot + 1) * tokens, :] = value.astype(low)
            value = both_ref[rank, 1]
            grads[slot][...] = value
            gated[slot][...] = (value.astype(jnp.float32) * rows_ref[2:3, :]).astype(low)

    shapes = [(count * tokens, width)] + [(tokens, width)] * (3 * count)
    return pl.pallas_call(
        body,
        in_specs=[in_smem()] + [in_vmem()] * 2,
        out_shape=[jax.ShapeDtypeStruct(shape, low) for shape in shapes],
        compiler_params=pltpu.CompilerParams(vmem_limit_bytes=60 * 2**20),
        cost_estimate=cheap,
        name="line_slots",
    )(place, both, rows)


def cross_block(place, mixed, hidden, rows, text, w_out, c_query, c_value, c_out):
    count, share = len(mixed), mixed[0].shape[1]
    tokens, width = hidden.shape
    words = text.shape[0]
    per = share // HEAD_DIM

    def body(place_ref, *refs):
        parts = refs[:count]
        x_ref, rows_ref, text_ref = refs[count : count + 3]
        far = refs[count + 3 : count + 7]
        outs = refs[count + 7 : count + 16]
        inverse = refs[count + 16]
        wo, wq, wv, wc, *own = refs[count + 17 : -3]
        held, read, sems = refs[-3:]
        branch, res_low, cq, ck, cv, crossed, res, normed, out = own
        me = place_ref[0]
        loads = [
            pltpu.make_async_copy(source, target, read.at[i])
            for i, (source, target) in enumerate(zip(far, (wo, wq, wv, wc)))
        ]
        stores = [
            pltpu.make_async_copy(source, target, sems.at[i])
            for i, (source, target) in enumerate(zip(own, outs))
        ]
        for load in loads:
            load.start()
        loads[0].wait()
        for cut in cuts_of(width):
            total = jnp.zeros((tokens, cut.stop - cut.start), jnp.float32)
            for k in range(count):
                rank = lax.rem(me + k, count)
                here = pl.ds(pl.multiple_of(rank * share, 32), share)
                total += dot(parts[k][0:tokens, :], wo[here, cut])
            branch[:, cut] = total
            first = x_ref[:, cut].astype(jnp.float32) + rows_ref[0:1, cut] * total
            res[:, cut] = first
            res_low[:, cut] = first.astype(low)
        stores[0].start()
        stores[1].start()
        loads[1].wait()
        loads[2].wait()
        for cut in cuts_of(width):
            cq[:, cut] = dot(res_low[...], wq[cut, :], nt).astype(low)
            cv[:, cut] = dot(text_ref[...], wv[cut, :], nt).astype(low)
        for k in range(count):
            held[lax.rem(me + k, count)] = parts[k][tokens:, :]
        ck[...] = jnp.concatenate([held[rank] for rank in range(count)], axis=1)
        for i in (2, 3, 4):
            stores[i].start()
        parts_out = []
        for at in range(0, width, HEAD_DIM):
            head = slice(at, at + HEAD_DIM)
            probs = softmax_keys(ck[:, head], cq[:, head]).astype(low)
            parts_out.append(dot(cv[:, head], probs, tn).T)
        crossed[...] = jnp.concatenate(parts_out, axis=1).astype(low)
        stores[5].start()
        loads[3].wait()
        for cut in cuts_of(width):
            res[:, cut] += dot(crossed[...], wc[:, cut])
        second = res[...]
        center = second - jnp.mean(second, axis=-1, keepdims=True)
        spread = lax.rsqrt(jnp.mean(center * center, axis=-1, keepdims=True) + norm_eps)
        inverse[...] = spread
        scaled = center * spread
        normed[...] = scaled
        stores[6].start()
        stores[7].start()
        out[...] = (scaled * (1.0 + rows_ref[2:3, :]) + rows_ref[1:2, :]).astype(low)
        stores[8].start()
        for store in stores:
            store.wait()

    wide = (tokens, width)
    shapes = [
        (wide, jnp.float32),
        (wide, low),
        (wide, low),
        ((words, width), low),
        ((words, width), low),
        (wide, low),
        (wide, jnp.float32),
        (wide, jnp.float32),
        (wide, low),
    ]
    anywhere = pl.BlockSpec(memory_space=pl.ANY)
    return pl.pallas_call(
        body,
        in_specs=[in_smem()] + [in_vmem()] * (count + 3) + [anywhere] * 4,
        out_specs=[anywhere] * len(shapes) + [in_vmem()],
        out_shape=[jax.ShapeDtypeStruct(*item) for item in shapes]
        + [jax.ShapeDtypeStruct((tokens, 1), jnp.float32)],
        scratch_shapes=[pltpu.VMEM((width, width), low)] * 4
        + [pltpu.VMEM(*item) for item in shapes]
        + [
            pltpu.VMEM((count, words, share), low),
            pltpu.SemaphoreType.DMA((4,)),
            pltpu.SemaphoreType.DMA((len(shapes),)),
        ],
        compiler_params=pltpu.CompilerParams(vmem_limit_bytes=60 * 2**20),
        cost_estimate=cheap,
        name="cross_block",
    )(place, *mixed, hidden, rows, text, w_out, c_query, c_value, c_out)


def cross_back(
    place, terms, grad, rows, normed, inverse, branch, cq, ck, cv, c_out, c_query, w_out, after
):
    count = len(terms)
    tokens, width = grad.shape
    words = ck.shape[0]
    share = width // count
    scale = HEAD_DIM ** (-0.5)

    def body(place_ref, *refs):
        parts = refs[:count]
        grad_ref, rows_ref, i_ref, k_ref, v_ref = refs[count : count + 5]
        far = refs[count + 5 : count + 11]
        refs = refs[: count + 11] + refs[count + 11 + len(after) :]
        stored = refs[count + 11 : count + 15]
        grad_v, sums = refs[count + 15 : count + 17]
        outs = refs[count + 17 : 2 * count + 17]
        near = refs[2 * count + 17 : 2 * count + 23]
        n_ref, wc, q_ref, wq, wo, b_ref = near
        own = refs[2 * count + 23 : 2 * count + 27]
        first, cross_low, grad_q, attn_low = own
        back, held, read, sems = refs[2 * count + 27 :]
        me = place_ref[0]
        loads = [
            pltpu.make_async_copy(source, target, read.at[i])
            for i, (source, target) in enumerate(zip(far, near))
        ]
        stores = [
            pltpu.make_async_copy(source, target, sems.at[i])
            for i, (source, target) in enumerate(zip(own, stored))
        ]
        for load in loads:
            load.start()
        loads[0].wait()
        total = parts[0][...].astype(jnp.float32)
        for part in parts[1:]:
            total += part[...].astype(jnp.float32)
        n = n_ref[...]
        sums[1:2, :] = jnp.sum(total, axis=0, keepdims=True)
        sums[2:3, :] = jnp.sum(total * n, axis=0, keepdims=True)
        second = grad_ref[...].astype(jnp.float32) + norm_back(total, n, i_ref[...], rows_ref[2:3, :])
        first[...] = second
        cross_low[...] = second.astype(low)
        stores[1].start()
        loads[1].wait()
        loads[2].wait()
        for cut in cuts_of(width):
            back[:, cut] = dot(cross_low[...], wc[cut, :], nt).astype(low)
        grads = ([], [], [])
        for at in range(0, width, HEAD_DIM):
            head = slice(at, at + HEAD_DIM)
            q, k, v, g = q_ref[:, head], k_ref[:, head], v_ref[:, head], back[:, head]
            probs = softmax_keys(k, q)
            grad_probs = dot(v, g, nt)
            inner = jnp.sum(probs * grad_probs, axis=0, keepdims=True)
            grad_scores = (probs * (grad_probs - inner)).astype(low)
            grads[0].append((dot(k, grad_scores, tn) * scale).T)
            grads[1].append(dot(grad_scores, q) * scale)
            grads[2].append(dot(probs.astype(low), g))
        grad_q[...] = jnp.concatenate(grads[0], axis=1).astype(low)
        grad_v[...] = jnp.concatenate(grads[2], axis=1).astype(low)
        heads = share // HEAD_DIM
        for rank in range(count):
            pieces = grads[1][rank * heads : (rank + 1) * heads]
            held[rank] = jnp.concatenate(pieces, axis=1).astype(low)
        stores[2].start()
        for load in loads[3:]:
            load.wait()
        for cut in cuts_of(width):
            whole = first[:, cut] + dot(grad_q[...], wq[:, cut])
            first[:, cut] = whole
            attn_low[:, cut] = (rows_ref[0:1, cut] * whole).astype(low)
            sums[0:1, cut] = jnp.sum(b_ref[:, cut] * whole, axis=0, keepdims=True)
        stores[0].start()
        stores[3].start()
        for k in range(count):
            rank = lax.rem(me + k, count)
            here = pl.ds(pl.multiple_of(rank * share, 32), share)
            outs[k][0:tokens, :] = dot(attn_low[...], wo[here, :], nt).astype(low)
            outs[k][tokens:, :] = held[rank]
        for store in stores:
            store.wait()

    wide, square = (tokens, width), (width, width)
    shapes = [
        (wide, jnp.float32),
        (wide, low),
        (wide, low),
        (wide, low),
        ((words, width), low),
        ((3, width), jnp.float32),
    ] + [((tokens + words, share), low)] * count
    anywhere = pl.BlockSpec(memory_space=pl.ANY)
    loaded = [
        pltpu.VMEM(wide, jnp.float32),
        pltpu.VMEM(square, low),
        pltpu.VMEM(wide, low),
        pltpu.VMEM(square, low),
        pltpu.VMEM(square, low),
        pltpu.VMEM(wide, jnp.float32),
    ]
    return pl.pallas_call(
        body,
        in_specs=[in_smem()] + [in_vmem()] * (count + 5) + [anywhere] * (6 + len(after)),
        out_specs=[anywhere] * 4 + [in_vmem()] * (2 + count),
        out_shape=[jax.ShapeDtypeStruct(*item) for item in shapes],
        scratch_shapes=loaded
        + [pltpu.VMEM(*item) for item in shapes[:4]]
        + [
            pltpu.VMEM(wide, low),
            pltpu.VMEM((count, words, share), low),
            pltpu.SemaphoreType.DMA((6,)),
            pltpu.SemaphoreType.DMA((4,)),
        ],
        compiler_params=pltpu.CompilerParams(vmem_limit_bytes=60 * 2**20),
        cost_estimate=costly,
        name="cross_back",
    )(
        place,
        *terms,
        grad,
        rows,
        inverse,
        ck,
        cv,
        normed,
        c_out,
        cq,
        c_query,
        w_out,
        branch,
        *after,
    )


def outer_halves(place, pairs, parts, name):
    width = pairs[0][1].shape[1]
    high = [sum(piece[2] for piece in left) for left, _ in pairs]
    size = high[0] // parts
    tokens = [right.shape[0] for _, right in pairs]
    flat = []

    def index_of(array):
        for i, other in enumerate(flat):
            if other is array:
                return i
        flat.append(array)
        return len(flat) - 1

    plans = [
        ([(index_of(array), *rest) for array, *rest in left], index_of(right))
        for left, right in pairs
    ]
    amount = len(pairs)

    def body(place_ref, *refs):
        ins, (kept, given), (held, sems) = refs[: len(flat)], refs[len(flat) :][:2], refs[-2:]
        turned = refs[len(flat) + 2 : -2]
        me, core = place_ref[0], place_ref[1]
        for i, (left, right) in enumerate(plans):
            for k, (which, lane, lanes, row) in enumerate(left):
                piece = ins[which][0 : tokens[i], lane : lane + lanes]
                piece = piece.astype(jnp.float32).T.astype(low)
                if row is None:
                    rank = lax.rem(me + k, len(left))
                    turned[i][pl.ds(pl.multiple_of(rank * lanes, 32), lanes), :] = piece
                else:
                    turned[i][row : row + lanes, :] = piece
            for part in range(parts):
                at = i * parts + part
                tile = dot(turned[i][part * size : (part + 1) * size, :], ins[right][...])
                held[at] = tile.astype(low)
                for out, side in ((kept, 0), (given, 1)):

                    @pl.when((core ^ (i & 1)) == side)
                    def _():
                        pltpu.make_async_copy(
                            held.at[at], out.at[i // 2, part], sems.at[at]
                        ).start()

        for at in range(amount * parts):
            pltpu.make_async_copy(held.at[at], kept.at[0, 0], sems.at[at]).wait()

    out = jax.ShapeDtypeStruct((amount // 2, parts, size, width), low)
    return pl.pallas_call(
        body,
        in_specs=[in_smem()] + [in_vmem()] * len(flat),
        out_specs=[pl.BlockSpec(memory_space=pl.ANY)] * 2,
        out_shape=[out, out],
        scratch_shapes=[pltpu.VMEM((high[i], tokens[i]), low) for i in range(amount)]
        + [
            pltpu.VMEM((amount * parts, size, width), low),
            pltpu.SemaphoreType.DMA((amount * parts,)),
        ],
        compiler_params=pltpu.CompilerParams(vmem_limit_bytes=60 * 2**20),
        cost_estimate=cheap if parts > 1 else costly,
        name=name,
    )(place, *flat)


def mlp_grads(grad_pres, acts, rows_in, grads_in, after):
    pieces, rights = len(acts), len(rows_in)
    tokens, width = rows_in[0].shape
    hidden = acts[0].shape[1]
    chunk = 384 if hidden % 384 == 0 else hidden
    steps = hidden // chunk

    def body(*refs):
        step = pl.program_id(0)
        lefts_up, lefts_down = refs[:pieces], refs[pieces : 2 * pieces]
        rights_up = refs[2 * pieces : 2 * pieces + rights]
        rights_down = refs[2 * pieces + rights : 2 * pieces + 2 * rights]
        out = refs[-1]

        def terms(lefts, turn, others):
            here = pl.ds(pl.multiple_of(turn * chunk, chunk), chunk)
            total = jnp.zeros((chunk, width), jnp.float32)
            cursor = 0
            for left in lefts:
                for i in range(left.shape[0] // tokens):
                    total += dot(left[i * tokens : (i + 1) * tokens, here], others[cursor][...], tn)
                    cursor += 1
            out[...] = total.astype(low)

        @pl.when(step < steps)
        def _():
            terms(lefts_up, step, rights_up)

        @pl.when(step >= steps)
        def _():
            terms(lefts_down, step - steps, rights_down)

    arrays = (*grad_pres, *acts, *rows_in, *grads_in)
    chunked = pl.BlockSpec((chunk, width), lambda s: (s, 0))
    return pl.pallas_call(
        body,
        grid=(2 * steps,),
        in_specs=[pl.BlockSpec(array.shape, lambda s: (0, 0)) for array in arrays]
        + [pl.BlockSpec(memory_space=pl.ANY)] * len(after),
        out_specs=chunked,
        out_shape=jax.ShapeDtypeStruct((2 * hidden, width), low),
        compiler_params=pltpu.CompilerParams(vmem_limit_bytes=60 * 2**20),
        cost_estimate=cheap,
        name="mlp_grads",
    )(*arrays, *after)


def ranked_terms(place, lefts, order, pieces, weight, factors, name):
    tokens, width = factors[0].shape
    count = len(factors)

    def body(place_ref, *refs):
        ins, weight_ref = refs[: len(lefts)], refs[len(lefts)]
        others = refs[len(lefts) + 1 : len(lefts) + 1 + count]
        out, sums = refs[-2:]
        me = place_ref[0]
        for i, slot in enumerate(order):
            rank = lax.rem(me - slot + count, count)
            for cut in cuts_of(width):
                term = jnp.zeros((tokens, cut.stop - cut.start), jnp.float32)
                for which, row, lane, start, depth in pieces[i]:
                    term += dot(
                        ins[which][row : row + tokens, lane : lane + depth],
                        weight_ref[start : start + depth, cut],
                    )
                out[rank, :, cut] = term.astype(low)
                one = jnp.sum(term, axis=0, keepdims=True)
                two = jnp.sum(term * others[i][:, cut].astype(jnp.float32), axis=0, keepdims=True)
                if i:
                    one, two = one + sums[0:1, cut], two + sums[1:2, cut]
                sums[0:1, cut], sums[1:2, cut] = one, two

    return pl.pallas_call(
        body,
        in_specs=[in_smem()] + [in_vmem()] * (len(lefts) + 1 + count),
        out_shape=[
            jax.ShapeDtypeStruct((count, tokens, width), low),
            jax.ShapeDtypeStruct((2, width), jnp.float32),
        ],
        compiler_params=pltpu.CompilerParams(vmem_limit_bytes=60 * 2**20),
        cost_estimate=cheap if len(lefts) > 2 else costly,
        name=name,
    )(place, *lefts, weight, *factors)


def sum_split(place, kept, got):
    count, unit_rows, width = kept.shape[1], kept.shape[4], kept.shape[5]

    def body(place_ref, one, two, keep_x, give_x, keep_y, give_y):
        x, y = place_ref[0], place_ref[1]

        def total(*index):
            return (one[index].astype(jnp.float32) + two[index].astype(jnp.float32)).astype(low)

        for j in range(2):
            keep_x[0, j] = total(0, 0, j, x)
            give_x[0, j] = total(0, 0, j, 1 - x)
            keep_y[0, j] = total(1, 0, y, j)
            give_y[0, j] = total(1, 0, 1 - y, j)

    block = pl.BlockSpec((2, 1, 2, 2, unit_rows, width), lambda r, *_: (0, r, 0, 0, 0, 0))
    part = pl.BlockSpec((1, 2, unit_rows, width), lambda r, *_: (r, 0, 0, 0))
    return pl.pallas_call(
        body,
        grid_spec=pltpu.PrefetchScalarGridSpec(
            num_scalar_prefetch=1, grid=(count,), in_specs=[block] * 2, out_specs=[part] * 4
        ),
        out_shape=[jax.ShapeDtypeStruct((count, 2, unit_rows, width), low)] * 4,
        compiler_params=pltpu.CompilerParams(vmem_limit_bytes=60 * 2**20),
        cost_estimate=costly,
        name="sum_split",
    )(place, kept, got)


def update_slots(master, first_moment, second_moment, filled, which, position, sources):
    capacity, unit_rows, width = master.shape

    group = math.gcd(capacity, 2)
    steps = capacity // group

    def body(filled_ref, which_ref, position_ref, weight, one, two, *rest):
        ins = rest[: len(sources)]
        new_one, new_two, new_weight, held, sems = rest[len(sources) :]
        step = pl.program_id(0)

        def fetch(turn):
            for i in range(group):
                slot = turn * group + i
                for source, ref in enumerate(ins):

                    @pl.when(which_ref[slot] == source)
                    def _():
                        pltpu.make_async_copy(
                            ref.at[position_ref[slot]], held.at[turn % 2, i], sems.at[turn % 2, i]
                        ).start()

        @pl.when(step == 0)
        def _():
            fetch(step)

        @pl.when(step < steps - 1)
        def _():
            fetch(step + 1)

        for i in range(group):
            pltpu.make_async_copy(
                ins[0].at[0], held.at[step % 2, i], sems.at[step % 2, i]
            ).wait()
            mask = (filled_ref[step * group + i] > 0).astype(jnp.float32)
            grad = held[step % 2, i].astype(jnp.float32)
            results = adamw(weight[i], one[i], two[i], grad, mask, rate)
            new_one[i], new_two[i], new_weight[i] = results

    block = pl.BlockSpec((group, unit_rows, width), lambda s, *_: (s, 0, 0))
    return pl.pallas_call(
        body,
        grid_spec=pltpu.PrefetchScalarGridSpec(
            num_scalar_prefetch=3,
            grid=(steps,),
            in_specs=[block] * 3 + [pl.BlockSpec(memory_space=pl.ANY)] * len(sources),
            out_specs=[block] * 3,
            scratch_shapes=[
                pltpu.VMEM((2, group, unit_rows, width), low),
                pltpu.SemaphoreType.DMA((2, group)),
            ],
        ),
        out_shape=[jax.ShapeDtypeStruct(master.shape, jnp.float32)] * 3,
        compiler_params=pltpu.CompilerParams(vmem_limit_bytes=56 * 2**20),
        cost_estimate=cheap,
        name="update_slots",
    )(filled, which, position, master, first_moment, second_moment, *sources)


def adamw(weight, moment_one, moment_two, gradient, filled, step_rate):
    new_one = beta_one * moment_one + (1.0 - beta_one) * gradient
    new_two = beta_two * moment_two + (1.0 - beta_two) * gradient * gradient
    fixed_one = new_one / (1.0 - beta_one**STEP)
    fixed_two = new_two / (1.0 - beta_two**STEP)
    updated = weight - step_rate * (fixed_one / (jnp.sqrt(fixed_two) + adam_eps) + decay * weight)
    return (new_one * filled, new_two * filled, updated * filled)


def swap(values, axis, bit):
    count = lax.axis_size(axis)
    return lax.ppermute(values, axis, [(i, i ^ (1 << bit)) for i in range(count)])


def choose(values, index, axis):
    return lax.dynamic_index_in_dim(values, index, axis, keepdims=False)


def total_sum(values):
    for axis in ("dp", "tensor"):
        for bit in range(lax.axis_size(axis).bit_length() - 1):
            values = values + swap(values, axis, bit)
    return values


def pick_units(master, slot_unit, state, kind, place, sizes, after=()):
    capacity, unit_rows, width = master.shape
    units = state.shape[0]

    def body(slot_ref, state_ref, kind_ref, place_ref, blocks, *rest):
        outs = rest[len(after) : len(after) + len(sizes)]
        highs, lows, zeros, read, sems = rest[len(after) + len(sizes) :]

        def start(source, unit):
            for which, out in enumerate(outs):

                @pl.when(kind_ref[unit] == which)
                def _():
                    pltpu.make_async_copy(source, out.at[place_ref[unit]], sems.at[unit]).start()

        @pl.loop(0, capacity)
        def _(slot):
            @pl.when(slot_ref[slot] >= 0)
            def _():
                pltpu.make_async_copy(blocks.at[slot], highs.at[slot], read.at[slot]).start()

        zeros[...] = jnp.zeros_like(zeros)

        @pl.loop(0, units)
        def _(unit):
            @pl.when(state_ref[unit] == 0)
            def _():
                start(zeros, unit)

        @pl.loop(0, capacity)
        def _(slot):
            @pl.when(slot_ref[slot] >= 0)
            def _():
                pltpu.make_async_copy(blocks.at[slot], highs.at[slot], read.at[slot]).wait()
                lows[slot] = highs[slot].astype(low)
                start(lows.at[slot], slot_ref[slot])

        @pl.loop(0, units)
        def _(unit):
            @pl.when(state_ref[unit] < 2)
            def _():
                pltpu.make_async_copy(zeros, outs[0].at[0], sems.at[unit]).wait()

    return pl.pallas_call(
        body,
        grid_spec=pltpu.PrefetchScalarGridSpec(
            num_scalar_prefetch=4,
            grid=(1,),
            in_specs=[pl.BlockSpec(memory_space=pl.ANY)] * (1 + len(after)),
            out_specs=[pl.BlockSpec(memory_space=pl.ANY)] * len(sizes),
            scratch_shapes=[
                pltpu.VMEM((capacity, unit_rows, width), jnp.float32),
                pltpu.VMEM((capacity, unit_rows, width), low),
                pltpu.VMEM((unit_rows, width), low),
                pltpu.SemaphoreType.DMA((capacity,)),
                pltpu.SemaphoreType.DMA((units,)),
            ],
        ),
        out_shape=[jax.ShapeDtypeStruct((size, unit_rows, width), low) for size in sizes],
        compiler_params=pltpu.CompilerParams(vmem_limit_bytes=56 * 2**20),
        cost_estimate=cheap,
        name="pick_units",
    )(slot_unit, state, kind, place, master, *after)


def place_blocks(sources, which, position, parts=1):
    amount = which.shape[0]
    shape = sources[0].shape[1:]
    size = amount // parts

    def body(which_ref, position_ref, *rest):
        ins, outs = rest[: len(sources)], rest[len(sources) : len(sources) + parts]
        held, read, sems = rest[len(sources) + parts :]

        @pl.loop(0, amount)
        def _(i):
            for source, ref in enumerate(ins):

                @pl.when(which_ref[i] == source)
                def _():
                    pltpu.make_async_copy(ref.at[position_ref[i]], held.at[i], read.at[i]).start()

        for part, out in enumerate(outs):

            @pl.loop(0, size)
            def _(j):
                i = part * size + j
                pltpu.make_async_copy(ins[0].at[0], held.at[i], read.at[i]).wait()
                pltpu.make_async_copy(held.at[i], out.at[j], sems.at[i]).start()

        @pl.loop(0, amount)
        def _(i):
            pltpu.make_async_copy(held.at[i], outs[0].at[0], sems.at[i]).wait()

    return pl.pallas_call(
        body,
        grid_spec=pltpu.PrefetchScalarGridSpec(
            num_scalar_prefetch=2,
            grid=(1,),
            in_specs=[pl.BlockSpec(memory_space=pl.ANY)] * len(sources),
            out_specs=[pl.BlockSpec(memory_space=pl.ANY)] * parts,
            scratch_shapes=[
                pltpu.VMEM((amount,) + shape, low),
                pltpu.SemaphoreType.DMA((amount,)),
                pltpu.SemaphoreType.DMA((amount,)),
            ],
        ),
        out_shape=[jax.ShapeDtypeStruct((size,) + shape, low)] * parts,
        compiler_params=pltpu.CompilerParams(vmem_limit_bytes=56 * 2**20),
        cost_estimate=cheap,
        name="place_blocks",
    )(which, position, *sources)


def stack_pairs(pairs):
    shape = (len(pairs),) + pairs[0].shape[1:]

    def body(*refs):
        for i, pair in enumerate(refs[:-2]):
            for half in range(2):
                refs[half - 2][i] = pair[half]

    return pl.pallas_call(
        body,
        out_shape=[jax.ShapeDtypeStruct(shape, low)] * 2,
        cost_estimate=costly,
        name="stack_pairs",
    )(*pairs)


fence = lax.optimization_barrier


def in_pool(member, inner, inner_count):
    me = lax.axis_index("dp")
    half, core = member >> 3, ((member >> 2) & 1) ^ (me & 1)
    far_y, far_x = ((member >> 1) & 1) ^ ((me >> 2) & 1), (member & 1) ^ ((me >> 1) & 1)
    where_first = (far_y * 2 + far_x) * inner_count
    where_second = (4 + far_x * 2 + far_y) * inner_count
    return (core, jnp.where(half == 0, where_first, where_second) + inner)


def on_device(
    hidden_in,
    time_embed,
    caption_table,
    caption_ids,
    owners,
    master,
    first_moment,
    second_moment,
    mod_table,
    mod_first,
    mod_second,
    out_grad,
):
    count = lax.axis_size("tensor")
    dp_count = lax.axis_size("dp")
    me_dp = lax.axis_index("dp")
    me_tensor = lax.axis_index("tensor")
    capacity, unit_rows, width = master.shape
    units = owners.shape[0]
    tokens = hidden_in.shape[1]
    text_count = caption_ids.shape[1]
    share = width // count
    per = share // unit_rows
    ups = (units - 8 * per) // 2
    rank_of = ranks_of(owners)
    mine = owners == me_dp
    match = (rank_of[None, :] == jnp.arange(capacity)[:, None]) & mine[None, :]
    filled = jnp.any(match, axis=1)
    unit_of_slot = jnp.sum(jnp.where(match, jnp.arange(units)[None, :], 0), axis=1)

    square = [list(range(i * per, (i + 1) * per)) for i in range(8)]
    group_attn = square[0] + square[1] + square[2] + square[5]
    group_full = square[3] + square[4] + square[6] + square[7]
    group_mlp = list(range(8 * per, units))
    members = len(group_attn)
    plane = dp_count == 8 and members == 16 and len(group_mlp) % dp_count == 0
    member_of = np.zeros(units, np.int32)
    member_of[group_attn] = np.arange(members)
    member_of[group_full] = np.arange(members)
    is_attn = np.zeros(units, bool)
    is_attn[group_attn] = True
    is_mlp = np.zeros(units, bool)
    is_mlp[group_mlp] = True

    latent_in = hidden_in[0].astype(jnp.float32)
    modulate = mod_table + time_embed[0]

    def mod_row(which_row):
        return modulate[which_row][None, :]

    normed_one, inverse_one = layer_norm(latent_in)
    bits = dp_count.bit_length() - 1
    vocab_rows = caption_table.shape[0]

    def caption_terms(ids):
        chosen = ids.reshape(-1) - me_dp * vocab_rows
        onehot = (chosen[:, None] == jnp.arange(vocab_rows)[None, :]).astype(low)
        terms = jnp.dot(onehot, caption_table, preferred_element_type=jnp.float32).astype(low)
        return terms.reshape(dp_count, text_count, -1)

    def modulated(normed):
        return (normed.astype(jnp.float32) * (1.0 + mod_row(1)) + mod_row(0)).astype(low)

    def whole_text(text_ring):
        return from_ring(text_ring, -1).transpose(1, 0, 2).reshape(text_count, width)

    def own_keys(text_low, w_attn):
        return project(text_low, w_attn)[:, 3 * share :].astype(low)

    def exchanged(attended, keys):
        parts = [
            jnp.concatenate([attended[k * tokens : (k + 1) * tokens], keys]) for k in range(count)
        ]
        return [parts[0]] + [shift(parts[k], count - k) for k in range(1, count)]

    where = jnp.stack([me_tensor, me_dp & 1]).astype(jnp.int32)

    n_low = normed_one.astype(low)
    if plane:
        core, far_x, far_y = (
            ((member_of >> 2) & 1) ^ (me_dp & 1),
            (member_of & 1) ^ ((me_dp >> 1) & 1),
            ((member_of >> 1) & 1) ^ ((me_dp >> 2) & 1),
        )
        place = jnp.where(is_attn, far_x * 4 + far_y * 2, 8 + far_y * 4 + far_x * 2)
        place = jnp.where(is_mlp, np.arange(units) - 8 * per, place + (member_of >> 3))
        kind = jnp.where(is_mlp, 0, core)
        slot_mlp = unit_of_slot >= 8 * per
        owned_state = mine.astype(jnp.int32)
        ids = lax.all_gather(caption_ids, "dp", axis=0, tiled=True)
        ids = jnp.take(ids, me_dp ^ jnp.arange(dp_count), axis=0, mode="clip")
        both = lax.all_gather(jnp.stack([n_low, out_grad[0]]), "tensor", axis=0)
        kept, given = pick_units(
            master,
            jnp.where(filled & ~slot_mlp, unit_of_slot, -1),
            jnp.where(is_mlp, 2, owned_state),
            kind,
            place,
            (members, members),
        )
        got = swap(given, "dp", 0)
        (mlp_part,) = pick_units(
            master,
            jnp.where(filled & slot_mlp, unit_of_slot, -1),
            jnp.where(is_mlp, owned_state, 2),
            kind,
            place,
            (len(group_mlp),),
            (kept,),
        )
        mlp_part = lax.psum_scatter(mlp_part, "dp", scatter_dimension=0, tiled=True)
        kept, got, ids = fence((kept, got, ids))
        pieces = [kept[i : i + 4] + got[i : i + 4] for i in range(0, members, 4)]
        attn_two, attn_send, full_two, full_send = fence(tuple(pieces))
        attn_got = swap(attn_send, "dp", 1)
        full_got = swap(full_send, "dp", 2)
        text = caption_terms(ids)
        text = text[0:4] + swap(text[4:8], "dp", 2)
        attn_two, attn_got, full_two, full_got, text = fence(
            (attn_two, attn_got, full_two, full_got, text)
        )
        pieces = [x[i : i + 2] + y[i : i + 2] for x, y in ((attn_two, attn_got), (full_two, full_got)) for i in (0, 2)]
        attn_one, attn_send, full_one, full_send = fence(tuple(pieces))
        attn_got = swap(attn_send, "dp", 2)
        full_got = swap(full_send, "dp", 1)
        text = text[0:2] + swap(text[2:4], "dp", 1)
        attn_one, attn_got, full_one, full_got, text = fence(
            (attn_one, attn_got, full_one, full_got, text)
        )
        attn_one, full_one = attn_one + attn_got, full_one + full_got
        first_ring, second_ring = stack_pairs(ring(full_one))
        first = jnp.concatenate([attn_one[0:1], swap(attn_one[0:1], "dp", 1)])
        second = jnp.concatenate([attn_one[1:2], swap(attn_one[1:2], "dp", 2)])
        pool = jnp.concatenate([first, swap(first, "dp", 2), second, swap(second, "dp", 1)])
        other = swap(pool, "dp", 0)
        text = text[0] + swap(text[1], "dp", 0)
        h_one_all, *slots = line_slots(
            where, both, jnp.concatenate([mod_row(0), mod_row(1), mod_row(5)])
        )
        n_slots, out_slots, grad_slots = (slots[i * count : (i + 1) * count] for i in range(3))
        pool, other, first_ring, second_ring, h_one_all, text = fence(
            (pool, other, first_ring, second_ring, h_one_all, text)
        )
        first, second = first_ring, second_ring
        first_got = swap(first, "dp", 1)
        second_got = swap(second, "dp", 2)
        text_ring = ring(text)
        (w_attn,) = place_blocks((pool, other), *in_pool(np.arange(members), 0, 1))
        w_attn = w_attn.reshape(-1, width)
        qkv = project(h_one_all, w_attn).astype(low)
        attended, logs = self_attend(qkv, share)
        first = jnp.concatenate([first, first_got])
        second = jnp.concatenate([second, second_got])
        first, second, text_ring, attended, logs, w_attn, mlp_part = fence(
            (first, second, text_ring, attended, logs, w_attn, mlp_part)
        )
        w_mlp = lax.all_gather(mlp_part, "dp", axis=0, tiled=True)
        first_far, second_far = swap(first, "dp", 2), swap(second, "dp", 1)
        text_low = whole_text(jnp.stack(text_ring))
        mixed = exchanged(attended, own_keys(text_low, w_attn))
        first_far, second_far, mixed = fence((first_far, second_far, mixed))
        first_other, second_other = swap(first, "dp", 0), swap(second, "dp", 0)
        first_last, second_last = swap(first_far, "dp", 0), swap(second_far, "dp", 0)
        listing = np.arange(count * members)
        matrix, rank, head = listing // (count * per), listing // per % count, listing % per
        slot = lax.rem(me_tensor - rank + count, count)
        which, position = in_pool(matrix * per + head, slot, count)
        blocks = 2 * count
        w_full = place_blocks(
            (first, first_far, second, second_far, first_other, first_last, second_other, second_last),
            which * 4 + position // blocks,
            position % blocks,
            parts=4,
        )
        w_full = [part.reshape(width, width) for part in w_full]
        w_full[3], w_mlp = fence((w_full[3], w_mlp))
    else:
        slots_low = master.astype(low)
        rows = jnp.take(slots_low, rank_of, axis=0, mode="clip")
        rows = lax.psum(jnp.where(mine[:, None, None], rows, jnp.zeros((), low)), "dp")
        w_attn = rows[np.array(group_attn)].reshape(-1, width)
        w_full = lax.all_gather(rows[np.array(group_full)], "tensor", axis=0)
        w_full = w_full.reshape(count, 4, share, width).swapaxes(0, 1).reshape(4, width, width)
        w_full = [w_full[i] for i in range(4)]
        w_mlp = rows[8 * per :]
        n_slots = ring(n_low)
        normed_all = jnp.concatenate(n_slots)
        out_slots = ring(out_grad[0])
        grad_slots = [(mod_row(5) * item.astype(jnp.float32)).astype(low) for item in out_slots]
        ids = caption_ids
        for bit in range(bits):
            ids = jnp.concatenate([ids, swap(ids, "dp", bit)])
        text = caption_terms(ids)
        for bit in reversed(range(bits)):
            text = text[: 1 << bit] + swap(text[1 << bit :], "dp", bit)
        text_low = whole_text(jnp.stack(ring(text[0])))
        h_one_all = modulated(normed_all)
        qkv = project(h_one_all, w_attn).astype(low)
        attended, logs = self_attend(qkv, share)
        mixed = exchanged(attended, own_keys(text_low, w_attn))
    w_cross = w_full
    w_out, c_query, c_value, c_out = w_full
    w_mlp = w_mlp.reshape(-1, width)

    rows = jnp.concatenate([mod_row(2), mod_row(3), mod_row(4)])
    (
        branch_one,
        first_low,
        cq_rows,
        ck_rows,
        cv_rows,
        crossed,
        second_res,
        normed_two,
        h_two,
        inverse_two,
    ) = cross_block(
        where, mixed, hidden_in[0], rows, text_low, *w_cross
    )

    h_slots = {0: h_two}
    near = [k for k in range(1, count) if 2 * k != count]
    far = [k for k in range(1, count) if 2 * k == count]
    acts, grad_pres, grad_terms, order = [], [], [], []
    for k in near:
        h_slots[k] = shift(h_two, k)
    for members_now in ([0], near, far):
        act, grad_pre, *terms = mlp_core(
            [h_slots[k] for k in members_now],
            [grad_slots[k] for k in members_now],
            w_mlp,
            acts[-1:],
        )
        if members_now == [0]:
            h_two, act = fence((h_two, act))
            for k in far:
                h_slots[k] = shift(h_two, k)
        acts.append(act), grad_pres.append(grad_pre)
        order += members_now
        grad_terms += [
            shift(term, count - k) if k else term for k, term in zip(members_now, terms)
        ]
    mlp_grad = mlp_grads(
        grad_pres,
        acts,
        [h_slots[k] for k in order],
        [grad_slots[k] for k in order],
        grad_terms[1:],
    ).reshape(-1, unit_rows, width)
    hidden_share = w_mlp.shape[0] // 2
    pieces = [
        [(which, row, 0, hidden_share, hidden_share)]
        for which, act in enumerate(acts)
        for row in range(0, act.shape[0], tokens)
    ]
    branch_terms, branch_sums = ranked_terms(
        where, acts, order, pieces, w_mlp, [out_slots[k] for k in order], "mlp_out"
    )
    branch_row = branch_sums[1]
    grad_terms, branch_terms = fence((grad_terms, branch_terms))
    if plane:
        mlp_sum = lax.psum_scatter(mlp_grad, "dp", scatter_dimension=0, tiled=True)

    (
        first_grad,
        cross_low,
        grad_cq,
        attn_low,
        grad_cv,
        row_sums,
        *grad_mixed,
    ) = cross_back(
        where,
        grad_terms,
        out_grad[0],
        rows,
        normed_two,
        inverse_two,
        branch_one,
        cq_rows,
        ck_rows,
        cv_rows,
        c_out,
        c_query,
        w_out,
        (),
    )

    grad_parts = [grad_mixed[0]] + [shift(grad_mixed[k], k) for k in range(1, count)]
    full_pairs = [
        ([(item, 0, share, None) for item in mixed], attn_low),
        ([(grad_cq, 0, width, 0)], first_low),
        ([(grad_cv, 0, width, 0)], text_low),
        ([(crossed, 0, width, 0)], cross_low),
    ]
    half = (share // HEAD_DIM // 2) * HEAD_DIM
    spans = [(0, half), (half, share)]

    def attention_pairs(grads, grad_parts):
        keys = sum(item[tokens:].astype(jnp.float32) for item in grad_parts).astype(low)
        pairs = [
            (
                [
                    (item, i * (end - begin), end - begin, begin)
                    for item, (begin, end) in zip(grads, spans)
                ],
                h_one_all,
            )
            for i in range(3)
        ]
        return pairs + [([(keys, 0, share, 0)], text_low)]

    def input_terms(grads):
        pieces = [
            [
                (which, slot * tokens, i * (end - begin), i * share + begin, end - begin)
                for which, (begin, end) in enumerate(spans)
                for i in range(3)
            ]
            for slot in range(count)
        ]
        return ranked_terms(where, grads, range(count), pieces, w_attn, n_slots, "attn_terms")

    if plane:
        x_bit, y_bit = (me_dp >> 1) & 1, (me_dp >> 2) & 1

        def split(total, bit, axis):
            return (choose(total, bit, axis), choose(total, 1 - bit, axis))

        kept, given = outer_halves(where, full_pairs, count, "full_grads")
        got = swap(given, "dp", 0)
        grad_parts, kept, got, branch_terms = fence((grad_parts, kept, got, branch_terms))
        branch_two = lax.psum_scatter(
            branch_terms.reshape(-1, width), "tensor", scatter_dimension=0, tiled=True
        )
        box = (2, count, 2, 2, unit_rows, width)
        bits_here = jnp.stack([x_bit, y_bit]).astype(jnp.int32)
        kept_one, given_one, kept_two, given_two = sum_split(
            bits_here, kept.reshape(box), got.reshape(box)
        )
        got_one, got_two = swap(given_one, "dp", 1), swap(given_two, "dp", 2)
        grads_early = self_attend_back(qkv, grad_parts, attended, logs, share, *spans[0])
        kept_one, got_one, kept_two, got_two, grads_early, grad_parts = fence(
            (kept_one, got_one, kept_two, got_two, grads_early, grad_parts)
        )
        kept_one, given_one = split(kept_one + got_one, y_bit, 1)
        kept_two, given_two = split(kept_two + got_two, x_bit, 1)
        kept_one, given_one, kept_two, given_two, grad_parts = fence(
            (kept_one, given_one, kept_two, given_two, grad_parts)
        )
        got_one, got_two = swap(given_one, "dp", 2), swap(given_two, "dp", 1)
        grads_late = self_attend_back(qkv, grad_parts, attended, logs, share, *spans[1])
        kept_one, got_one, kept_two, got_two, grads_early, grads_late, mlp_sum = fence(
            (kept_one, got_one, kept_two, got_two, grads_early, grads_late, mlp_sum)
        )
        mlp_sum = lax.all_gather(mlp_sum, "dp", axis=0, tiled=True)
        full_parts = to_ring(jnp.stack([kept_one + got_one, kept_two + got_two], axis=1))
        full_parts = [full_parts[k] for k in range(count)]
        full_parts, grads_early, grads_late = fence((full_parts, grads_early, grads_late))
        grads_qkv = [grads_early, grads_late]
        full_got = [shift(full_parts[k], k) for k in range(1, count)]
        attn_kept, attn_given = outer_halves(
            where, attention_pairs(grads_qkv, grad_parts), 1, "attn_grads"
        )
        attn_got = swap(attn_given, "dp", 0)
        grad_h_terms, grad_h_sums = input_terms(grads_qkv)
        mod_terms = jnp.concatenate([grad_h_sums, row_sums, branch_row[None]])
        grad_h_one = lax.psum_scatter(
            grad_h_terms.reshape(-1, width), "tensor", scatter_dimension=0, tiled=True
        )
        attn_kept, attn_got, mod_terms, branch_two = fence(
            (attn_kept, attn_got, mod_terms, branch_two)
        )
        attn_all = (attn_kept + attn_got).reshape(2, 2, 2, unit_rows, width)
        one_kept, one_given = split(attn_all[0], x_bit, 1)
        two_kept, two_given = split(attn_all[1], y_bit, 0)
        one_got, two_got = swap(one_given, "dp", 1), swap(two_given, "dp", 2)
        for bit in range(2):
            mod_terms = mod_terms + swap(mod_terms, "dp", bit)
        full_own = full_parts[0]
        one_kept, one_got, two_kept, two_got, mod_terms, full_own, full_got = fence(
            (one_kept, one_got, two_kept, two_got, mod_terms, full_own, full_got)
        )
        full_sum = full_own.astype(jnp.float32)
        for part in full_got:
            full_sum = full_sum + part.astype(jnp.float32)
        full_sum = full_sum.astype(low)
        one_kept, one_given = split(one_kept + one_got, y_bit, 0)
        two_kept, two_given = split(two_kept + two_got, x_bit, 0)
        one_got, two_got = swap(one_given, "dp", 2), swap(two_given, "dp", 1)
        mod_terms = mod_terms + swap(mod_terms, "dp", 2)
        one_kept, one_got, two_kept, two_got, full_sum, mod_terms, mlp_sum = fence(
            (one_kept, one_got, two_kept, two_got, full_sum, mod_terms, mlp_sum)
        )
        first = jnp.stack([one_kept + one_got, full_sum[0]])
        second = jnp.stack([two_kept + two_got, full_sum[1]])
        first_got, second_got = swap(first, "dp", 1), swap(second, "dp", 2)
        first = jnp.concatenate([first, first_got])
        second = jnp.concatenate([second, second_got])
        mod_terms = mod_terms + swap(mod_terms, "tensor", 0)
        first, second, mod_terms = fence((first, second, mod_terms))
        first_far, second_far = swap(first, "dp", 2), swap(second, "dp", 1)
        for bit in range(1, count.bit_length() - 1):
            mod_terms = mod_terms + swap(mod_terms, "tensor", bit)
        first, first_far, second, second_far, mod_terms = fence(
            (first, first_far, second, second_far, mod_terms)
        )
        pool = jnp.concatenate([first, first_far, second, second_far])
        other = swap(pool, "dp", 0)
        mod_grad = mod_terms
        pool, other = fence((pool, other))
        which, position = in_pool(member_of, np.where(is_attn, 0, 1), 2)
        which = jnp.where(is_mlp, 2, which)
        position = jnp.where(is_mlp, np.arange(units) - 8 * per, position)
        own = jnp.sum(jnp.where(match[:, :, None], jnp.stack([which, position], 1)[None], 0), axis=1)
        new_first, new_second, new_master = update_slots(
            master,
            first_moment,
            second_moment,
            filled.astype(jnp.int32),
            own[:, 0],
            own[:, 1],
            (pool, other, mlp_sum),
        )
    else:
        branch_two = lax.psum_scatter(
            branch_terms.reshape(-1, width), "tensor", scatter_dimension=0, tiled=True
        )
        grads_qkv = [self_attend_back(qkv, grad_parts, attended, logs, share, *span) for span in spans]
        attn_grads = [
            outer(array[:, lane : lane + lanes], right).astype(low)
            for left, right in attention_pairs(grads_qkv, grad_parts)
            for array, lane, lanes, row in left
        ]
        grad_h_terms, grad_h_sums = input_terms(grads_qkv)
        grad_h_one = lax.psum_scatter(
            grad_h_terms.reshape(-1, width), "tensor", scatter_dimension=0, tiled=True
        )
        mixed_all = from_ring(jnp.stack([item[:tokens] for item in mixed]), 1)
        mixed_all = mixed_all.transpose(1, 0, 2).reshape(tokens, width)
        full_grads = [outer(mixed_all, attn_low)]
        full_grads += [outer(left[0][0], right) for left, right in full_pairs[1:]]
        full_sum = [g.astype(low).reshape(count, share, width) for g in full_grads]
        full_sum = jnp.stack(full_sum, axis=1)
        full_sum = lax.psum_scatter(full_sum, "tensor", scatter_dimension=0, tiled=True)
        order = np.array(group_attn + group_full + group_mlp)
        sums = jnp.concatenate(
            [jnp.concatenate(attn_grads), full_sum.reshape(-1, width), mlp_grad.reshape(-1, width)]
        )
        sums = lax.psum(sums.reshape(units, unit_rows, width), "dp")
        owned = jnp.take(sums, jnp.array(np.argsort(order))[unit_of_slot], axis=0, mode="clip")
        mod_grad = total_sum(jnp.concatenate([grad_h_sums, row_sums, branch_row[None]]))
        new_first, new_second, new_master = adamw(
            master,
            first_moment,
            second_moment,
            owned.astype(jnp.float32),
            filled.astype(jnp.float32)[:, None, None],
            rate,
        )
    branch_two, second_res, grad_h_one, new_first = fence(
        (branch_two, second_res, grad_h_one, new_first)
    )
    grad_h_one = grad_h_one.astype(jnp.float32)
    block_out = second_res + mod_row(5) * branch_two.astype(jnp.float32)
    input_grad = first_grad + norm_back(grad_h_one, normed_one, inverse_one, mod_row(1))
    mod_new_first, mod_new_second, mod_new = adamw(
        mod_table, mod_first, mod_second, mod_grad, 1.0, table_rate
    )
    return (
        block_out[None],
        input_grad[None],
        new_first,
        new_second,
        new_master,
        mod_new_first,
        mod_new_second,
        mod_new,
    )


def solution(mesh):
    in_specs = (
        P("dp", "tensor", None),
        P("dp", None, None),
        P("dp", "tensor"),
        P("dp", None),
        P(),
        P("dp", "tensor", None),
        P("dp", "tensor", None),
        P("dp", "tensor", None),
        P(),
        P(),
        P(),
        P("dp", "tensor", None),
    )
    out_specs = (
        P("dp", "tensor", None),
        P("dp", "tensor", None),
        P("dp", "tensor", None),
        P("dp", "tensor", None),
        P("dp", "tensor", None),
        P(),
        P(),
        P(),
    )
    return jax.shard_map(
        on_device, mesh=mesh, in_specs=in_specs, out_specs=out_specs, check_vma=False
    )
```

```python
import math

import jax
import jax.numpy as jnp
import numpy as np
from jax import lax
from jax.experimental import pallas as pl
from jax.experimental.pallas import tpu as pltpu
from jax.sharding import PartitionSpec as P

HEAD_DIM = 72
STEP = 10


norm_eps = 1e-06
beta_one = 0.9
beta_two = 0.999
rate = 0.03
table_rate = 0.3
decay = 0.01
adam_eps = 1e-08
low = jnp.bfloat16


def ranks_of(owners):
    index = jnp.arange(owners.shape[0])
    before = (owners[None, :] == owners[:, None]) & (index[None, :] < index[:, None])
    return jnp.sum(before.astype(jnp.int32), axis=1)


def layer_norm(values):
    center = values - jnp.mean(values, axis=-1, keepdims=True)
    inverse = lax.rsqrt(jnp.mean(center * center, axis=-1, keepdims=True) + norm_eps)
    return (center * inverse, inverse)


def norm_back(grad_rows, normed, inverse, scale_row):
    scaled = grad_rows * (1.0 + scale_row)
    mean_one = jnp.mean(scaled, axis=-1, keepdims=True)
    mean_two = jnp.mean(scaled * normed, axis=-1, keepdims=True)
    return inverse * (scaled - mean_one - normed * mean_two)


def project(rows, weight):
    return jnp.einsum("ld,rd->lr", rows, weight, preferred_element_type=jnp.float32)


def expand(rows, weight):
    return jnp.einsum("lr,rd->ld", rows, weight, preferred_element_type=jnp.float32)


def outer(left, right):
    return jnp.einsum("lr,ld->rd", left, right, preferred_element_type=jnp.float32)


def shift(values, step):
    count = lax.axis_size("tensor")
    return lax.ppermute(values, "tensor", [(i, (i + step) % count) for i in range(count)])


def ring(values):
    return [values] + [shift(values, k) for k in range(1, lax.axis_size("tensor"))]


def to_ring(stacked):
    count = stacked.shape[0]
    twice = jnp.concatenate([stacked, stacked], axis=0)
    return lax.dynamic_slice_in_dim(twice, lax.axis_index("tensor"), count, 0)


def from_ring(stacked, sign):
    count = stacked.shape[0]
    me = lax.axis_index("tensor")
    place = lax.rem(sign * (jnp.arange(count) - me) + 2 * count, count)
    return jnp.take(stacked, place, axis=0, mode="clip")


cheap = pl.CostEstimate(flops=1000, bytes_accessed=1000, transcendentals=0)
costly = pl.CostEstimate(flops=10**10, bytes_accessed=10**7, transcendentals=0)


def self_attend(qkv, share):
    length = qkv.shape[0]
    rows = min(512, length)
    curve = HEAD_DIM ** (-0.5) * math.log2(math.e)
    heads = share // HEAD_DIM

    def body(qkv_ref, out_ref, log_ref):
        @pl.loop(0, length // rows)
        def _(step):
            here = pl.ds(pl.multiple_of(step * rows, rows), rows)
            parts = []
            for head in range(heads):
                at = head * HEAD_DIM
                q = qkv_ref[here, at : at + HEAD_DIM]
                k = qkv_ref[:, share + at : share + at + HEAD_DIM]
                v = qkv_ref[:, 2 * share + at : 2 * share + at + HEAD_DIM]
                scores = dot(k, q, nt)
                top = jnp.max(scores, axis=0, keepdims=True)
                expo = jnp.exp2((scores - top) * curve)
                total = jnp.sum(expo, axis=0, keepdims=True)
                log_ref[head : head + 1, here] = top * curve + jnp.log2(total)
                parts.append((dot(v, expo.astype(low), tn) * (1.0 / total)).T)
            out_ref[here, :] = jnp.concatenate(parts, axis=1).astype(low)

    return pl.pallas_call(
        body,
        out_shape=[
            jax.ShapeDtypeStruct((length, share), low),
            jax.ShapeDtypeStruct((heads, length), jnp.float32),
        ],
        compiler_params=pltpu.CompilerParams(vmem_limit_bytes=40 * 2**20),
        cost_estimate=cheap,
        name="self_attend",
    )(qkv)


def self_attend_back(qkv, grads, mixed, logs, share, begin, end):
    length = qkv.shape[0]
    rows = length // len(grads)
    span = end - begin
    scale = HEAD_DIM ** (-0.5)
    curve = scale * math.log2(math.e)

    def body(qkv_ref, mixed_ref, log_ref, *refs):
        grad_refs, (out_ref, grad_k, grad_v) = refs[: len(grads)], refs[len(grads) :]
        for step, grad_ref in enumerate(grad_refs):
            here = slice(step * rows, (step + 1) * rows)
            parts = []
            for head, at in enumerate(range(begin, end, HEAD_DIM)):
                q = qkv_ref[here, at : at + HEAD_DIM]
                k = qkv_ref[:, share + at : share + at + HEAD_DIM]
                v = qkv_ref[:, 2 * share + at : 2 * share + at + HEAD_DIM]
                g = grad_ref[0:rows, at : at + HEAD_DIM]
                o = mixed_ref[here, at : at + HEAD_DIM]
                inner = g.astype(jnp.float32) * o.astype(jnp.float32)
                inner = jnp.sum(inner.T, axis=0, keepdims=True)
                which = begin // HEAD_DIM + head
                probs = jnp.exp2(dot(k, q, nt) * curve - log_ref[which : which + 1, here])
                grad_scores = (probs * (dot(v, g, nt) - inner)).astype(low)
                to_v = dot(probs.astype(low), g)
                to_k = dot(grad_scores, q)
                if step:
                    grad_v[head] += to_v
                    grad_k[head] += to_k
                else:
                    grad_v[head] = to_v
                    grad_k[head] = to_k
                parts.append((dot(k, grad_scores, tn) * scale).T)
            out_ref[here, 0:span] = jnp.concatenate(parts, axis=1).astype(low)
        heads = range(span // HEAD_DIM)
        both = [grad_k[head] * scale for head in heads]
        out_ref[:, span : 2 * span] = jnp.concatenate(both, axis=1).astype(low)
        both = [grad_v[head] for head in heads]
        out_ref[:, 2 * span :] = jnp.concatenate(both, axis=1).astype(low)

    return pl.pallas_call(
        body,
        out_shape=jax.ShapeDtypeStruct((length, 3 * span), low),
        scratch_shapes=[pltpu.VMEM((span // HEAD_DIM, length, HEAD_DIM), jnp.float32)] * 2,
        compiler_params=pltpu.CompilerParams(vmem_limit_bytes=40 * 2**20),
        cost_estimate=costly,
        name="self_attend_back",
    )(qkv, mixed, logs, *grads)


def mlp_core(rows_in, grads_in, w_mlp, after):
    groups = len(rows_in)
    tokens, width = rows_in[0].shape
    hidden = w_mlp.shape[0] // 2
    chunk = 384 if hidden % 384 == 0 else hidden
    steps = hidden // chunk
    curve = 0.7978845608028654

    def body(*refs):
        rows, grads = refs[:groups], refs[groups : 2 * groups]
        up, down = refs[2 * groups : 2 * groups + 2]
        act, grad_pre, *outs = refs[2 * groups + 2 + len(after) : -1]
        total = refs[-1]
        step = pl.program_id(0)
        for i in range(groups):
            pre = lax.dot_general(
                rows[i][...], up[...], (((1,), (1,)), ((), ())), preferred_element_type=jnp.float32
            )
            square = pre * pre
            bend = jnp.tanh(curve * pre * (1.0 + 0.044715 * square))
            half = 0.5 * (1.0 + bend)
            here = pl.ds(i * tokens, tokens)
            act[here, :] = (pre * half).astype(low)
            slope = half + (0.5 * curve) * pre * (1.0 - bend * bend) * (1.0 + 0.134145 * square)
            grad_act = lax.dot_general(
                grads[i][...], down[...], (((1,), (1,)), ((), ())), preferred_element_type=jnp.float32
            )
            grad_low = (grad_act * slope).astype(low)
            grad_pre[here, :] = grad_low
            term = jnp.dot(grad_low, up[...], preferred_element_type=jnp.float32)

            @pl.when(step == 0)
            def _():
                total[here, :] = term

            @pl.when(step > 0)
            def _():
                total[here, :] += term

            @pl.when(step == steps - 1)
            def _():
                outs[i][...] = total[here, :].astype(low)

    whole = pl.BlockSpec((tokens, width), lambda s: (0, 0))
    across = pl.BlockSpec((groups * tokens, chunk), lambda s: (0, s))
    return pl.pallas_call(
        body,
        grid=(steps,),
        in_specs=[whole] * (2 * groups)
        + [
            pl.BlockSpec((chunk, width), lambda s: (s, 0)),
            pl.BlockSpec((chunk, width), lambda s: (steps + s, 0)),
        ]
        + [pl.BlockSpec(memory_space=pl.ANY)] * len(after),
        out_specs=[across, across] + [whole] * groups,
        out_shape=[jax.ShapeDtypeStruct((groups * tokens, hidden), low)] * 2
        + [jax.ShapeDtypeStruct((tokens, width), low)] * groups,
        scratch_shapes=[pltpu.VMEM((groups * tokens, width), jnp.float32)],
        compiler_params=pltpu.CompilerParams(vmem_limit_bytes=60 * 2**20),
        cost_estimate=cheap,
        name="mlp_core",
    )(*rows_in, *grads_in, w_mlp, w_mlp, *after)


nt = (((1,), (1,)), ((), ()))
tn = (((0,), (0,)), ((), ()))


def dot(left, right, dims=(((1,), (0,)), ((), ()))):
    return lax.dot_general(left, right, dims, preferred_element_type=jnp.float32)


def softmax_keys(keys, queries):
    scores = dot(keys, queries, nt) * HEAD_DIM ** (-0.5)
    expo = jnp.exp(scores - jnp.max(scores, axis=0, keepdims=True))
    return expo * (1.0 / jnp.sum(expo, axis=0, keepdims=True))


def cuts_of(width):
    size = 384 if width % 384 == 0 else width
    return [slice(i, i + size) for i in range(0, width, size)]


def in_smem():
    return pl.BlockSpec(memory_space=pltpu.SMEM)


def in_vmem():
    return pl.BlockSpec(memory_space=pltpu.VMEM)


def line_slots(place, own, ups, downs, rows):
    count = len(ups) + 1
    tokens, width = own.shape

    def body(place_ref, *refs):
        own_ref, up_refs, down_refs = refs[0], refs[1:count], refs[count : 2 * count - 1]
        rows_ref, outs, out = refs[2 * count - 1], refs[2 * count : -1], refs[-1]
        me = place_ref[0]

        def modulate(slot, ref):
            value = ref[...].astype(jnp.float32)
            value = value * (1.0 + rows_ref[1:2, :]) + rows_ref[0:1, :]
            out[slot * tokens : (slot + 1) * tokens, :] = value.astype(low)

        modulate(0, own_ref)
        for k in range(1, count):
            for side, ref in ((me >= k, up_refs[k - 1]), (me < k, down_refs[count - k - 1])):

                @pl.when(side)
                def _():
                    outs[k - 1][...] = ref[...]
                    modulate(k, ref)

    shapes = [(tokens, width)] * (count - 1) + [(count * tokens, width)]
    return pl.pallas_call(
        body,
        in_specs=[in_smem()] + [in_vmem()] * (2 * count),
        out_shape=[jax.ShapeDtypeStruct(shape, low) for shape in shapes],
        compiler_params=pltpu.CompilerParams(vmem_limit_bytes=32 * 2**20),
        cost_estimate=cheap,
        name="line_slots",
    )(place, own, *ups, *downs, rows)


def cross_block(place, mixed, hidden, rows, text, w_out, c_query, c_value, c_out):
    count, share = len(mixed), mixed[0].shape[1]
    tokens, width = hidden.shape
    words = text.shape[0]
    per = share // HEAD_DIM

    def body(place_ref, *refs):
        parts = refs[:count]
        x_ref, rows_ref, text_ref = refs[count : count + 3]
        far = refs[count + 3 : count + 7]
        outs = refs[count + 7 : count + 16]
        inverse = refs[count + 16]
        wo, wq, wv, wc, *own = refs[count + 17 : -3]
        held, read, sems = refs[-3:]
        branch, res_low, cq, ck, cv, crossed, res, normed, out = own
        me = place_ref[0]
        loads = [
            pltpu.make_async_copy(source, target, read.at[i])
            for i, (source, target) in enumerate(zip(far, (wo, wq, wv, wc)))
        ]
        stores = [
            pltpu.make_async_copy(source, target, sems.at[i])
            for i, (source, target) in enumerate(zip(own, outs))
        ]
        for load in loads:
            load.start()
        loads[0].wait()
        for cut in cuts_of(width):
            total = jnp.zeros((tokens, cut.stop - cut.start), jnp.float32)
            for k in range(count):
                rank = lax.rem(me + k, count)
                here = pl.ds(pl.multiple_of(rank * share, 32), share)
                total += dot(parts[k][0:tokens, :], wo[here, cut])
            branch[:, cut] = total
            first = x_ref[:, cut].astype(jnp.float32) + rows_ref[0:1, cut] * total
            res[:, cut] = first
            res_low[:, cut] = first.astype(low)
        stores[0].start()
        stores[1].start()
        loads[1].wait()
        loads[2].wait()
        for cut in cuts_of(width):
            cq[:, cut] = dot(res_low[...], wq[cut, :], nt).astype(low)
            cv[:, cut] = dot(text_ref[...], wv[cut, :], nt).astype(low)
        for k in range(count):
            held[lax.rem(me + k, count)] = parts[k][tokens:, :]
        ck[...] = jnp.concatenate([held[rank] for rank in range(count)], axis=1)
        for i in (2, 3, 4):
            stores[i].start()
        parts_out = []
        for at in range(0, width, HEAD_DIM):
            head = slice(at, at + HEAD_DIM)
            probs = softmax_keys(ck[:, head], cq[:, head]).astype(low)
            parts_out.append(dot(cv[:, head], probs, tn).T)
        crossed[...] = jnp.concatenate(parts_out, axis=1).astype(low)
        stores[5].start()
        loads[3].wait()
        for cut in cuts_of(width):
            res[:, cut] += dot(crossed[...], wc[:, cut])
        second = res[...]
        center = second - jnp.mean(second, axis=-1, keepdims=True)
        spread = lax.rsqrt(jnp.mean(center * center, axis=-1, keepdims=True) + norm_eps)
        inverse[...] = spread
        scaled = center * spread
        normed[...] = scaled
        stores[6].start()
        stores[7].start()
        out[...] = (scaled * (1.0 + rows_ref[2:3, :]) + rows_ref[1:2, :]).astype(low)
        stores[8].start()
        for store in stores:
            store.wait()

    wide = (tokens, width)
    shapes = [
        (wide, jnp.float32),
        (wide, low),
        (wide, low),
        ((words, width), low),
        ((words, width), low),
        (wide, low),
        (wide, jnp.float32),
        (wide, jnp.float32),
        (wide, low),
    ]
    anywhere = pl.BlockSpec(memory_space=pl.ANY)
    return pl.pallas_call(
        body,
        in_specs=[in_smem()] + [in_vmem()] * (count + 3) + [anywhere] * 4,
        out_specs=[anywhere] * len(shapes) + [in_vmem()],
        out_shape=[jax.ShapeDtypeStruct(*item) for item in shapes]
        + [jax.ShapeDtypeStruct((tokens, 1), jnp.float32)],
        scratch_shapes=[pltpu.VMEM((width, width), low)] * 4
        + [pltpu.VMEM(*item) for item in shapes]
        + [
            pltpu.VMEM((count, words, share), low),
            pltpu.SemaphoreType.DMA((4,)),
            pltpu.SemaphoreType.DMA((len(shapes),)),
        ],
        compiler_params=pltpu.CompilerParams(vmem_limit_bytes=60 * 2**20),
        cost_estimate=cheap,
        name="cross_block",
    )(place, *mixed, hidden, rows, text, w_out, c_query, c_value, c_out)


def cross_back(
    place, terms, grad, rows, normed, inverse, branch, cq, ck, cv, c_out, c_query, w_out, after
):
    count = len(terms)
    tokens, width = grad.shape
    words = ck.shape[0]
    share = width // count
    scale = HEAD_DIM ** (-0.5)

    def body(place_ref, *refs):
        parts = refs[:count]
        grad_ref, rows_ref, i_ref, k_ref, v_ref = refs[count : count + 5]
        far = refs[count + 5 : count + 11]
        refs = refs[: count + 11] + refs[count + 11 + len(after) :]
        stored = refs[count + 11 : count + 15]
        grad_v, sums = refs[count + 15 : count + 17]
        outs = refs[count + 17 : 2 * count + 17]
        near = refs[2 * count + 17 : 2 * count + 23]
        n_ref, wc, q_ref, wq, wo, b_ref = near
        own = refs[2 * count + 23 : 2 * count + 27]
        first, cross_low, grad_q, attn_low = own
        back, held, read, sems = refs[2 * count + 27 :]
        me = place_ref[0]
        loads = [
            pltpu.make_async_copy(source, target, read.at[i])
            for i, (source, target) in enumerate(zip(far, near))
        ]
        stores = [
            pltpu.make_async_copy(source, target, sems.at[i])
            for i, (source, target) in enumerate(zip(own, stored))
        ]
        for load in loads:
            load.start()
        loads[0].wait()
        total = parts[0][...].astype(jnp.float32)
        for part in parts[1:]:
            total += part[...].astype(jnp.float32)
        n = n_ref[...]
        sums[1:2, :] = jnp.sum(total, axis=0, keepdims=True)
        sums[2:3, :] = jnp.sum(total * n, axis=0, keepdims=True)
        second = grad_ref[...].astype(jnp.float32) + norm_back(total, n, i_ref[...], rows_ref[2:3, :])
        first[...] = second
        cross_low[...] = second.astype(low)
        stores[1].start()
        loads[1].wait()
        loads[2].wait()
        for cut in cuts_of(width):
            back[:, cut] = dot(cross_low[...], wc[cut, :], nt).astype(low)
        grads = ([], [], [])
        for at in range(0, width, HEAD_DIM):
            head = slice(at, at + HEAD_DIM)
            q, k, v, g = q_ref[:, head], k_ref[:, head], v_ref[:, head], back[:, head]
            probs = softmax_keys(k, q)
            grad_probs = dot(v, g, nt)
            inner = jnp.sum(probs * grad_probs, axis=0, keepdims=True)
            grad_scores = (probs * (grad_probs - inner)).astype(low)
            grads[0].append((dot(k, grad_scores, tn) * scale).T)
            grads[1].append(dot(grad_scores, q) * scale)
            grads[2].append(dot(probs.astype(low), g))
        grad_q[...] = jnp.concatenate(grads[0], axis=1).astype(low)
        grad_v[...] = jnp.concatenate(grads[2], axis=1).astype(low)
        heads = share // HEAD_DIM
        for rank in range(count):
            pieces = grads[1][rank * heads : (rank + 1) * heads]
            held[rank] = jnp.concatenate(pieces, axis=1).astype(low)
        stores[2].start()
        for load in loads[3:]:
            load.wait()
        for cut in cuts_of(width):
            whole = first[:, cut] + dot(grad_q[...], wq[:, cut])
            first[:, cut] = whole
            attn_low[:, cut] = (rows_ref[0:1, cut] * whole).astype(low)
            sums[0:1, cut] = jnp.sum(b_ref[:, cut] * whole, axis=0, keepdims=True)
        stores[0].start()
        stores[3].start()
        for k in range(count):
            rank = lax.rem(me + k, count)
            here = pl.ds(pl.multiple_of(rank * share, 32), share)
            outs[k][0:tokens, :] = dot(attn_low[...], wo[here, :], nt).astype(low)
            outs[k][tokens:, :] = held[rank]
        for store in stores:
            store.wait()

    wide, square = (tokens, width), (width, width)
    shapes = [
        (wide, jnp.float32),
        (wide, low),
        (wide, low),
        (wide, low),
        ((words, width), low),
        ((3, width), jnp.float32),
    ] + [((tokens + words, share), low)] * count
    anywhere = pl.BlockSpec(memory_space=pl.ANY)
    loaded = [
        pltpu.VMEM(wide, jnp.float32),
        pltpu.VMEM(square, low),
        pltpu.VMEM(wide, low),
        pltpu.VMEM(square, low),
        pltpu.VMEM(square, low),
        pltpu.VMEM(wide, jnp.float32),
    ]
    return pl.pallas_call(
        body,
        in_specs=[in_smem()] + [in_vmem()] * (count + 5) + [anywhere] * (6 + len(after)),
        out_specs=[anywhere] * 4 + [in_vmem()] * (2 + count),
        out_shape=[jax.ShapeDtypeStruct(*item) for item in shapes],
        scratch_shapes=loaded
        + [pltpu.VMEM(*item) for item in shapes[:4]]
        + [
            pltpu.VMEM(wide, low),
            pltpu.VMEM((count, words, share), low),
            pltpu.SemaphoreType.DMA((6,)),
            pltpu.SemaphoreType.DMA((4,)),
        ],
        compiler_params=pltpu.CompilerParams(vmem_limit_bytes=60 * 2**20),
        cost_estimate=costly,
        name="cross_back",
    )(
        place,
        *terms,
        grad,
        rows,
        inverse,
        ck,
        cv,
        normed,
        c_out,
        cq,
        c_query,
        w_out,
        branch,
        *after,
    )


def outer_halves(place, pairs, parts, name):
    width = pairs[0][1].shape[1]
    high = [sum(piece[2] for piece in left) for left, _ in pairs]
    size = high[0] // parts
    tokens = [right.shape[0] for _, right in pairs]
    flat = []

    def index_of(array):
        for i, other in enumerate(flat):
            if other is array:
                return i
        flat.append(array)
        return len(flat) - 1

    plans = [
        ([(index_of(array), *rest) for array, *rest in left], index_of(right))
        for left, right in pairs
    ]
    amount = len(pairs)

    def body(place_ref, *refs):
        ins, (kept, given), (held, sems) = refs[: len(flat)], refs[len(flat) :][:2], refs[-2:]
        turned = refs[len(flat) + 2 : -2]
        me, core = place_ref[0], place_ref[1]
        for i, (left, right) in enumerate(plans):
            for k, (which, lane, lanes, row) in enumerate(left):
                piece = ins[which][0 : tokens[i], lane : lane + lanes]
                piece = piece.astype(jnp.float32).T.astype(low)
                if row is None:
                    rank = lax.rem(me + k, len(left))
                    turned[i][pl.ds(pl.multiple_of(rank * lanes, 32), lanes), :] = piece
                else:
                    turned[i][row : row + lanes, :] = piece
            for part in range(parts):
                at = i * parts + part
                tile = dot(turned[i][part * size : (part + 1) * size, :], ins[right][...])
                held[at] = tile.astype(low)
                for out, side in ((kept, 0), (given, 1)):

                    @pl.when((core ^ (i & 1)) == side)
                    def _():
                        pltpu.make_async_copy(
                            held.at[at], out.at[i // 2, part], sems.at[at]
                        ).start()

        for at in range(amount * parts):
            pltpu.make_async_copy(held.at[at], kept.at[0, 0], sems.at[at]).wait()

    out = jax.ShapeDtypeStruct((amount // 2, parts, size, width), low)
    return pl.pallas_call(
        body,
        in_specs=[in_smem()] + [in_vmem()] * len(flat),
        out_specs=[pl.BlockSpec(memory_space=pl.ANY)] * 2,
        out_shape=[out, out],
        scratch_shapes=[pltpu.VMEM((high[i], tokens[i]), low) for i in range(amount)]
        + [
            pltpu.VMEM((amount * parts, size, width), low),
            pltpu.SemaphoreType.DMA((amount * parts,)),
        ],
        compiler_params=pltpu.CompilerParams(vmem_limit_bytes=60 * 2**20),
        cost_estimate=cheap if parts > 1 else costly,
        name=name,
    )(place, *flat)


def mlp_grads(grad_pres, acts, rows_in, grads_in, after):
    pieces, rights = len(acts), len(rows_in)
    tokens, width = rows_in[0].shape
    hidden = acts[0].shape[1]
    chunk = 384 if hidden % 384 == 0 else hidden
    steps = hidden // chunk

    def body(*refs):
        step = pl.program_id(0)
        lefts_up, lefts_down = refs[:pieces], refs[pieces : 2 * pieces]
        rights_up = refs[2 * pieces : 2 * pieces + rights]
        rights_down = refs[2 * pieces + rights : 2 * pieces + 2 * rights]
        out = refs[-1]

        def terms(lefts, turn, others):
            here = pl.ds(pl.multiple_of(turn * chunk, chunk), chunk)
            total = jnp.zeros((chunk, width), jnp.float32)
            cursor = 0
            for left in lefts:
                for i in range(left.shape[0] // tokens):
                    total += dot(left[i * tokens : (i + 1) * tokens, here], others[cursor][...], tn)
                    cursor += 1
            out[...] = total.astype(low)

        @pl.when(step < steps)
        def _():
            terms(lefts_up, step, rights_up)

        @pl.when(step >= steps)
        def _():
            terms(lefts_down, step - steps, rights_down)

    arrays = (*grad_pres, *acts, *rows_in, *grads_in)
    chunked = pl.BlockSpec((chunk, width), lambda s: (s, 0))
    return pl.pallas_call(
        body,
        grid=(2 * steps,),
        in_specs=[pl.BlockSpec(array.shape, lambda s: (0, 0)) for array in arrays]
        + [pl.BlockSpec(memory_space=pl.ANY)] * len(after),
        out_specs=chunked,
        out_shape=jax.ShapeDtypeStruct((2 * hidden, width), low),
        compiler_params=pltpu.CompilerParams(vmem_limit_bytes=60 * 2**20),
        cost_estimate=cheap,
        name="mlp_grads",
    )(*arrays, *after)


def ranked_terms(place, lefts, order, pieces, weight, factors, name):
    tokens, width = factors[0].shape
    count = len(factors)

    def body(place_ref, *refs):
        ins, weight_ref = refs[: len(lefts)], refs[len(lefts)]
        others = refs[len(lefts) + 1 : len(lefts) + 1 + count]
        out, sums = refs[-2:]
        me = place_ref[0]
        for i, slot in enumerate(order):
            rank = lax.rem(me - slot + count, count)
            for cut in cuts_of(width):
                term = jnp.zeros((tokens, cut.stop - cut.start), jnp.float32)
                for which, row, lane, start, depth in pieces[i]:
                    term += dot(
                        ins[which][row : row + tokens, lane : lane + depth],
                        weight_ref[start : start + depth, cut],
                    )
                out[rank, :, cut] = term.astype(low)
                one = jnp.sum(term, axis=0, keepdims=True)
                two = jnp.sum(term * others[i][:, cut].astype(jnp.float32), axis=0, keepdims=True)
                if i:
                    one, two = one + sums[0:1, cut], two + sums[1:2, cut]
                sums[0:1, cut], sums[1:2, cut] = one, two

    return pl.pallas_call(
        body,
        in_specs=[in_smem()] + [in_vmem()] * (len(lefts) + 1 + count),
        out_shape=[
            jax.ShapeDtypeStruct((count, tokens, width), low),
            jax.ShapeDtypeStruct((2, width), jnp.float32),
        ],
        compiler_params=pltpu.CompilerParams(vmem_limit_bytes=60 * 2**20),
        cost_estimate=cheap if len(lefts) > 2 else costly,
        name=name,
    )(place, *lefts, weight, *factors)


def sum_split(place, kept, got):
    count, unit_rows, width = kept.shape[1], kept.shape[4], kept.shape[5]

    def body(place_ref, one, two, keep_x, give_x, keep_y, give_y):
        x, y = place_ref[0], place_ref[1]

        def total(*index):
            return (one[index].astype(jnp.float32) + two[index].astype(jnp.float32)).astype(low)

        for j in range(2):
            keep_x[0, j] = total(0, 0, j, x)
            give_x[0, j] = total(0, 0, j, 1 - x)
            keep_y[0, j] = total(1, 0, y, j)
            give_y[0, j] = total(1, 0, 1 - y, j)

    block = pl.BlockSpec((2, 1, 2, 2, unit_rows, width), lambda r, *_: (0, r, 0, 0, 0, 0))
    part = pl.BlockSpec((1, 2, unit_rows, width), lambda r, *_: (r, 0, 0, 0))
    return pl.pallas_call(
        body,
        grid_spec=pltpu.PrefetchScalarGridSpec(
            num_scalar_prefetch=1, grid=(count,), in_specs=[block] * 2, out_specs=[part] * 4
        ),
        out_shape=[jax.ShapeDtypeStruct((count, 2, unit_rows, width), low)] * 4,
        compiler_params=pltpu.CompilerParams(vmem_limit_bytes=60 * 2**20),
        cost_estimate=costly,
        name="sum_split",
    )(place, kept, got)


def update_slots(master, first_moment, second_moment, filled, which, position, sources):
    capacity, unit_rows, width = master.shape

    group = math.gcd(capacity, 2)
    steps = capacity // group

    def body(filled_ref, which_ref, position_ref, weight, one, two, *rest):
        ins = rest[: len(sources)]
        new_one, new_two, new_weight, held, sems = rest[len(sources) :]
        step = pl.program_id(0)

        def fetch(turn):
            for i in range(group):
                slot = turn * group + i
                for source, ref in enumerate(ins):

                    @pl.when(which_ref[slot] == source)
                    def _():
                        pltpu.make_async_copy(
                            ref.at[position_ref[slot]], held.at[turn % 2, i], sems.at[turn % 2, i]
                        ).start()

        @pl.when(step == 0)
        def _():
            fetch(step)

        @pl.when(step < steps - 1)
        def _():
            fetch(step + 1)

        for i in range(group):
            pltpu.make_async_copy(
                ins[0].at[0], held.at[step % 2, i], sems.at[step % 2, i]
            ).wait()
            mask = (filled_ref[step * group + i] > 0).astype(jnp.float32)
            grad = held[step % 2, i].astype(jnp.float32)
            results = adamw(weight[i], one[i], two[i], grad, mask, rate)
            new_one[i], new_two[i], new_weight[i] = results

    block = pl.BlockSpec((group, unit_rows, width), lambda s, *_: (s, 0, 0))
    return pl.pallas_call(
        body,
        grid_spec=pltpu.PrefetchScalarGridSpec(
            num_scalar_prefetch=3,
            grid=(steps,),
            in_specs=[block] * 3 + [pl.BlockSpec(memory_space=pl.ANY)] * len(sources),
            out_specs=[block] * 3,
            scratch_shapes=[
                pltpu.VMEM((2, group, unit_rows, width), low),
                pltpu.SemaphoreType.DMA((2, group)),
            ],
        ),
        out_shape=[jax.ShapeDtypeStruct(master.shape, jnp.float32)] * 3,
        compiler_params=pltpu.CompilerParams(vmem_limit_bytes=56 * 2**20),
        cost_estimate=cheap,
        name="update_slots",
    )(filled, which, position, master, first_moment, second_moment, *sources)


def adamw(weight, moment_one, moment_two, gradient, filled, step_rate):
    new_one = beta_one * moment_one + (1.0 - beta_one) * gradient
    new_two = beta_two * moment_two + (1.0 - beta_two) * gradient * gradient
    fixed_one = new_one / (1.0 - beta_one**STEP)
    fixed_two = new_two / (1.0 - beta_two**STEP)
    updated = weight - step_rate * (fixed_one / (jnp.sqrt(fixed_two) + adam_eps) + decay * weight)
    return (new_one * filled, new_two * filled, updated * filled)


def swap(values, axis, bit):
    count = lax.axis_size(axis)
    return lax.ppermute(values, axis, [(i, i ^ (1 << bit)) for i in range(count)])


def choose(values, index, axis):
    return lax.dynamic_index_in_dim(values, index, axis, keepdims=False)


def total_sum(values):
    for axis in ("dp", "tensor"):
        for bit in range(lax.axis_size(axis).bit_length() - 1):
            values = values + swap(values, axis, bit)
    return values


def pick_units(master, slot_unit, state, kind, place, sizes, after=()):
    capacity, unit_rows, width = master.shape
    units = state.shape[0]

    def body(slot_ref, state_ref, kind_ref, place_ref, blocks, *rest):
        outs = rest[len(after) : len(after) + len(sizes)]
        highs, lows, zeros, read, sems = rest[len(after) + len(sizes) :]

        def start(source, unit):
            for which, out in enumerate(outs):

                @pl.when(kind_ref[unit] == which)
                def _():
                    pltpu.make_async_copy(source, out.at[place_ref[unit]], sems.at[unit]).start()

        @pl.loop(0, capacity)
        def _(slot):
            @pl.when(slot_ref[slot] >= 0)
            def _():
                pltpu.make_async_copy(blocks.at[slot], highs.at[slot], read.at[slot]).start()

        zeros[...] = jnp.zeros_like(zeros)

        @pl.loop(0, units)
        def _(unit):
            @pl.when(state_ref[unit] == 0)
            def _():
                start(zeros, unit)

        @pl.loop(0, capacity)
        def _(slot):
            @pl.when(slot_ref[slot] >= 0)
            def _():
                pltpu.make_async_copy(blocks.at[slot], highs.at[slot], read.at[slot]).wait()
                lows[slot] = highs[slot].astype(low)
                start(lows.at[slot], slot_ref[slot])

        @pl.loop(0, units)
        def _(unit):
            @pl.when(state_ref[unit] < 2)
            def _():
                pltpu.make_async_copy(zeros, outs[0].at[0], sems.at[unit]).wait()

    return pl.pallas_call(
        body,
        grid_spec=pltpu.PrefetchScalarGridSpec(
            num_scalar_prefetch=4,
            grid=(1,),
            in_specs=[pl.BlockSpec(memory_space=pl.ANY)] * (1 + len(after)),
            out_specs=[pl.BlockSpec(memory_space=pl.ANY)] * len(sizes),
            scratch_shapes=[
                pltpu.VMEM((capacity, unit_rows, width), jnp.float32),
                pltpu.VMEM((capacity, unit_rows, width), low),
                pltpu.VMEM((unit_rows, width), low),
                pltpu.SemaphoreType.DMA((capacity,)),
                pltpu.SemaphoreType.DMA((units,)),
            ],
        ),
        out_shape=[jax.ShapeDtypeStruct((size, unit_rows, width), low) for size in sizes],
        compiler_params=pltpu.CompilerParams(vmem_limit_bytes=56 * 2**20),
        cost_estimate=cheap,
        name="pick_units",
    )(slot_unit, state, kind, place, master, *after)


def place_blocks(sources, which, position, parts=1):
    amount = which.shape[0]
    shape = sources[0].shape[1:]
    size = amount // parts

    def body(which_ref, position_ref, *rest):
        ins, outs = rest[: len(sources)], rest[len(sources) : len(sources) + parts]
        held, read, sems = rest[len(sources) + parts :]

        @pl.loop(0, amount)
        def _(i):
            for source, ref in enumerate(ins):

                @pl.when(which_ref[i] == source)
                def _():
                    pltpu.make_async_copy(ref.at[position_ref[i]], held.at[i], read.at[i]).start()

        for part, out in enumerate(outs):

            @pl.loop(0, size)
            def _(j):
                i = part * size + j
                pltpu.make_async_copy(ins[0].at[0], held.at[i], read.at[i]).wait()
                pltpu.make_async_copy(held.at[i], out.at[j], sems.at[i]).start()

        @pl.loop(0, amount)
        def _(i):
            pltpu.make_async_copy(held.at[i], outs[0].at[0], sems.at[i]).wait()

    return pl.pallas_call(
        body,
        grid_spec=pltpu.PrefetchScalarGridSpec(
            num_scalar_prefetch=2,
            grid=(1,),
            in_specs=[pl.BlockSpec(memory_space=pl.ANY)] * len(sources),
            out_specs=[pl.BlockSpec(memory_space=pl.ANY)] * parts,
            scratch_shapes=[
                pltpu.VMEM((amount,) + shape, low),
                pltpu.SemaphoreType.DMA((amount,)),
                pltpu.SemaphoreType.DMA((amount,)),
            ],
        ),
        out_shape=[jax.ShapeDtypeStruct((size,) + shape, low)] * parts,
        compiler_params=pltpu.CompilerParams(vmem_limit_bytes=56 * 2**20),
        cost_estimate=cheap,
        name="place_blocks",
    )(which, position, *sources)


def stack_pairs(pairs):
    shape = (len(pairs),) + pairs[0].shape[1:]

    def body(*refs):
        for i, pair in enumerate(refs[:-2]):
            for half in range(2):
                refs[half - 2][i] = pair[half]

    return pl.pallas_call(
        body,
        out_shape=[jax.ShapeDtypeStruct(shape, low)] * 2,
        cost_estimate=costly,
        name="stack_pairs",
    )(*pairs)


def hops(values, step, turn):
    count = lax.axis_size("tensor")
    if step > 0:
        pairs = [(i, i + 1) for i in range(turn - 1, count - 1)]
    else:
        pairs = [(i, i - 1) for i in range(1, count - turn + 1)]
    return lax.ppermute(values, "tensor", pairs)


fence = lax.optimization_barrier


def in_pool(member, inner, inner_count):
    me = lax.axis_index("dp")
    half, core = member >> 3, ((member >> 2) & 1) ^ (me & 1)
    far_y, far_x = ((member >> 1) & 1) ^ ((me >> 2) & 1), (member & 1) ^ ((me >> 1) & 1)
    where_first = (far_y * 2 + far_x) * inner_count
    where_second = (4 + far_x * 2 + far_y) * inner_count
    return (core, jnp.where(half == 0, where_first, where_second) + inner)


def on_device(
    hidden_in,
    time_embed,
    caption_table,
    caption_ids,
    owners,
    master,
    first_moment,
    second_moment,
    mod_table,
    mod_first,
    mod_second,
    out_grad,
):
    count = lax.axis_size("tensor")
    dp_count = lax.axis_size("dp")
    me_dp = lax.axis_index("dp")
    me_tensor = lax.axis_index("tensor")
    capacity, unit_rows, width = master.shape
    units = owners.shape[0]
    tokens = hidden_in.shape[1]
    text_count = caption_ids.shape[1]
    share = width // count
    per = share // unit_rows
    ups = (units - 8 * per) // 2
    rank_of = ranks_of(owners)
    mine = owners == me_dp
    match = (rank_of[None, :] == jnp.arange(capacity)[:, None]) & mine[None, :]
    filled = jnp.any(match, axis=1)
    unit_of_slot = jnp.sum(jnp.where(match, jnp.arange(units)[None, :], 0), axis=1)

    square = [list(range(i * per, (i + 1) * per)) for i in range(8)]
    group_attn = square[0] + square[1] + square[2] + square[5]
    group_full = square[3] + square[4] + square[6] + square[7]
    group_mlp = list(range(8 * per, units))
    members = len(group_attn)
    plane = dp_count == 8 and members == 16 and len(group_mlp) % dp_count == 0
    member_of = np.zeros(units, np.int32)
    member_of[group_attn] = np.arange(members)
    member_of[group_full] = np.arange(members)
    is_attn = np.zeros(units, bool)
    is_attn[group_attn] = True
    is_mlp = np.zeros(units, bool)
    is_mlp[group_mlp] = True

    latent_in = hidden_in[0].astype(jnp.float32)
    modulate = mod_table + time_embed[0]

    def mod_row(which_row):
        return modulate[which_row][None, :]

    normed_one, inverse_one = layer_norm(latent_in)
    bits = dp_count.bit_length() - 1
    vocab_rows = caption_table.shape[0]

    def caption_terms(ids):
        chosen = ids.reshape(-1) - me_dp * vocab_rows
        onehot = (chosen[:, None] == jnp.arange(vocab_rows)[None, :]).astype(low)
        terms = jnp.dot(onehot, caption_table, preferred_element_type=jnp.float32).astype(low)
        return terms.reshape(dp_count, text_count, -1)

    def modulated(normed):
        return (normed.astype(jnp.float32) * (1.0 + mod_row(1)) + mod_row(0)).astype(low)

    def whole_text(text_ring):
        return from_ring(text_ring, -1).transpose(1, 0, 2).reshape(text_count, width)

    def own_keys(text_low, w_attn):
        return project(text_low, w_attn)[:, 3 * share :].astype(low)

    def exchanged(attended, keys):
        parts = [
            jnp.concatenate([attended[k * tokens : (k + 1) * tokens], keys]) for k in range(count)
        ]
        return [parts[0]] + [shift(parts[k], count - k) for k in range(1, count)]

    where = jnp.stack([me_tensor, me_dp & 1]).astype(jnp.int32)

    n_low = normed_one.astype(low)
    if plane:
        core, far_x, far_y = (
            ((member_of >> 2) & 1) ^ (me_dp & 1),
            (member_of & 1) ^ ((me_dp >> 1) & 1),
            ((member_of >> 1) & 1) ^ ((me_dp >> 2) & 1),
        )
        place = jnp.where(is_attn, far_x * 4 + far_y * 2, 8 + far_y * 4 + far_x * 2)
        place = jnp.where(is_mlp, np.arange(units) - 8 * per, place + (member_of >> 3))
        kind = jnp.where(is_mlp, 0, core)
        slot_mlp = unit_of_slot >= 8 * per
        owned_state = mine.astype(jnp.int32)
        ids = lax.all_gather(caption_ids, "dp", axis=0, tiled=True)
        ids = jnp.take(ids, me_dp ^ jnp.arange(dp_count), axis=0, mode="clip")
        up, down = hops(n_low, 1, 1), hops(n_low, -1, 1)
        kept, given = pick_units(
            master,
            jnp.where(filled & ~slot_mlp, unit_of_slot, -1),
            jnp.where(is_mlp, 2, owned_state),
            kind,
            place,
            (members, members),
        )
        got = swap(given, "dp", 0)
        (mlp_part,) = pick_units(
            master,
            jnp.where(filled & slot_mlp, unit_of_slot, -1),
            jnp.where(is_mlp, owned_state, 2),
            kind,
            place,
            (len(group_mlp),),
            (kept,),
        )
        mlp_part = lax.psum_scatter(mlp_part, "dp", scatter_dimension=0, tiled=True)
        n_up, n_down = [up], [down]
        kept, got, up, down, ids = fence((kept, got, up, down, ids))
        pieces = [kept[i : i + 4] + got[i : i + 4] for i in range(0, members, 4)]
        attn_two, attn_send, full_two, full_send = fence(tuple(pieces))
        up, down = hops(up, 1, 2), hops(down, -1, 2)
        attn_got = swap(attn_send, "dp", 1)
        full_got = swap(full_send, "dp", 2)
        text = caption_terms(ids)
        text = text[0:4] + swap(text[4:8], "dp", 2)
        n_up.append(up), n_down.append(down)
        attn_two, attn_got, full_two, full_got, up, down, text = fence(
            (attn_two, attn_got, full_two, full_got, up, down, text)
        )
        pieces = [x[i : i + 2] + y[i : i + 2] for x, y in ((attn_two, attn_got), (full_two, full_got)) for i in (0, 2)]
        attn_one, attn_send, full_one, full_send = fence(tuple(pieces))
        up, down = hops(up, 1, 3), hops(down, -1, 3)
        attn_got = swap(attn_send, "dp", 2)
        full_got = swap(full_send, "dp", 1)
        text = text[0:2] + swap(text[2:4], "dp", 1)
        n_up.append(up), n_down.append(down)
        attn_one, attn_got, full_one, full_got, up, down, text, mlp_part = fence(
            (attn_one, attn_got, full_one, full_got, up, down, text, mlp_part)
        )
        attn_one, full_one = attn_one + attn_got, full_one + full_got
        n_up[-1], n_down[-1] = up, down
        w_mlp = lax.all_gather(mlp_part, "dp", axis=0, tiled=True)
        first_ring, second_ring = stack_pairs(ring(full_one))
        first = jnp.concatenate([attn_one[0:1], swap(attn_one[0:1], "dp", 1)])
        second = jnp.concatenate([attn_one[1:2], swap(attn_one[1:2], "dp", 2)])
        pool = jnp.concatenate([first, swap(first, "dp", 2), second, swap(second, "dp", 1)])
        other = swap(pool, "dp", 0)
        text = text[0] + swap(text[1], "dp", 0)
        *n_slots, h_one_all = line_slots(
            where, n_low, n_up, n_down, jnp.concatenate([mod_row(0), mod_row(1)])
        )
        n_slots = [n_low] + n_slots
        grad_own = out_grad[0]
        pool, other, first_ring, second_ring, h_one_all, text, grad_own = fence(
            (pool, other, first_ring, second_ring, h_one_all, text, grad_own)
        )
        grad_whole = lax.all_gather(grad_own, "tensor", axis=0)
        first, second = first_ring, second_ring
        first_got = swap(first, "dp", 1)
        second_got = swap(second, "dp", 2)
        text_ring = ring(text)
        (w_attn,) = place_blocks((pool, other), *in_pool(np.arange(members), 0, 1))
        w_attn = w_attn.reshape(-1, width)
        qkv = project(h_one_all, w_attn).astype(low)
        attended, logs = self_attend(qkv, share)
        first = jnp.concatenate([first, first_got])
        second = jnp.concatenate([second, second_got])
        first, second, text_ring, attended, logs, w_attn, w_mlp = fence(
            (first, second, text_ring, attended, logs, w_attn, w_mlp)
        )
        first_far, second_far = swap(first, "dp", 2), swap(second, "dp", 1)
        text_low = whole_text(jnp.stack(text_ring))
        mixed = exchanged(attended, own_keys(text_low, w_attn))
        first_far, second_far, mixed = fence((first_far, second_far, mixed))
        first_other, second_other = swap(first, "dp", 0), swap(second, "dp", 0)
        first_last, second_last = swap(first_far, "dp", 0), swap(second_far, "dp", 0)
        listing = np.arange(count * members)
        matrix, rank, head = listing // (count * per), listing // per % count, listing % per
        slot = lax.rem(me_tensor - rank + count, count)
        which, position = in_pool(matrix * per + head, slot, count)
        blocks = 2 * count
        w_full = place_blocks(
            (first, first_far, second, second_far, first_other, first_last, second_other, second_last),
            which * 4 + position // blocks,
            position % blocks,
            parts=4,
        )
        w_full = [part.reshape(width, width) for part in w_full]
        w_full[3], grad_whole = fence((w_full[3], grad_whole))
    else:
        slots_low = master.astype(low)
        rows = jnp.take(slots_low, rank_of, axis=0, mode="clip")
        rows = lax.psum(jnp.where(mine[:, None, None], rows, jnp.zeros((), low)), "dp")
        w_attn = rows[np.array(group_attn)].reshape(-1, width)
        w_full = lax.all_gather(rows[np.array(group_full)], "tensor", axis=0)
        w_full = w_full.reshape(count, 4, share, width).swapaxes(0, 1).reshape(4, width, width)
        w_full = [w_full[i] for i in range(4)]
        w_mlp = rows[8 * per :]
        n_slots = ring(n_low)
        normed_all = jnp.concatenate(n_slots)
        grad_whole = lax.all_gather(out_grad[0], "tensor", axis=0)
        ids = caption_ids
        for bit in range(bits):
            ids = jnp.concatenate([ids, swap(ids, "dp", bit)])
        text = caption_terms(ids)
        for bit in reversed(range(bits)):
            text = text[: 1 << bit] + swap(text[1 << bit :], "dp", bit)
        text_low = whole_text(jnp.stack(ring(text[0])))
        h_one_all = modulated(normed_all)
        qkv = project(h_one_all, w_attn).astype(low)
        attended, logs = self_attend(qkv, share)
        mixed = exchanged(attended, own_keys(text_low, w_attn))
    w_cross = w_full
    w_out, c_query, c_value, c_out = w_full
    w_mlp = w_mlp.reshape(-1, width)

    rows = jnp.concatenate([mod_row(2), mod_row(3), mod_row(4)])
    (
        branch_one,
        first_low,
        cq_rows,
        ck_rows,
        cv_rows,
        crossed,
        second_res,
        normed_two,
        h_two,
        inverse_two,
    ) = cross_block(
        where, mixed, hidden_in[0], rows, text_low, *w_cross
    )

    h_slots = {0: h_two}
    out_slots = [
        choose(grad_whole, lax.rem(me_tensor - k + count, count), 0) for k in range(count)
    ]
    grad_slots = [(mod_row(5) * item.astype(jnp.float32)).astype(low) for item in out_slots]
    near = [k for k in range(1, count) if 2 * k != count]
    far = [k for k in range(1, count) if 2 * k == count]
    acts, grad_pres, grad_terms, order = [], [], [], []
    for k in near:
        h_slots[k] = shift(h_two, k)
    for members_now in ([0], near, far):
        act, grad_pre, *terms = mlp_core(
            [h_slots[k] for k in members_now],
            [grad_slots[k] for k in members_now],
            w_mlp,
            acts[-1:],
        )
        if members_now == [0]:
            h_two, act = fence((h_two, act))
            for k in far:
                h_slots[k] = shift(h_two, k)
        acts.append(act), grad_pres.append(grad_pre)
        order += members_now
        grad_terms += [
            shift(term, count - k) if k else term for k, term in zip(members_now, terms)
        ]
    mlp_grad = mlp_grads(
        grad_pres,
        acts,
        [h_slots[k] for k in order],
        [grad_slots[k] for k in order],
        grad_terms[1:],
    ).reshape(-1, unit_rows, width)
    hidden_share = w_mlp.shape[0] // 2
    pieces = [
        [(which, row, 0, hidden_share, hidden_share)]
        for which, act in enumerate(acts)
        for row in range(0, act.shape[0], tokens)
    ]
    branch_terms, branch_sums = ranked_terms(
        where, acts, order, pieces, w_mlp, [out_slots[k] for k in order], "mlp_out"
    )
    branch_row = branch_sums[1]
    if plane:
        mlp_sum = lax.psum_scatter(mlp_grad, "dp", scatter_dimension=0, tiled=True)

    (
        first_grad,
        cross_low,
        grad_cq,
        attn_low,
        grad_cv,
        row_sums,
        *grad_mixed,
    ) = cross_back(
        where,
        grad_terms,
        out_grad[0],
        rows,
        normed_two,
        inverse_two,
        branch_one,
        cq_rows,
        ck_rows,
        cv_rows,
        c_out,
        c_query,
        w_out,
        (),
    )

    grad_parts = [grad_mixed[0]] + [shift(grad_mixed[k], k) for k in range(1, count)]
    full_pairs = [
        ([(item, 0, share, None) for item in mixed], attn_low),
        ([(grad_cq, 0, width, 0)], first_low),
        ([(grad_cv, 0, width, 0)], text_low),
        ([(crossed, 0, width, 0)], cross_low),
    ]
    half = (share // HEAD_DIM // 2) * HEAD_DIM
    spans = [(0, half), (half, share)]

    def attention_pairs(grads, grad_parts):
        keys = sum(item[tokens:].astype(jnp.float32) for item in grad_parts).astype(low)
        pairs = [
            (
                [
                    (item, i * (end - begin), end - begin, begin)
                    for item, (begin, end) in zip(grads, spans)
                ],
                h_one_all,
            )
            for i in range(3)
        ]
        return pairs + [([(keys, 0, share, 0)], text_low)]

    def input_terms(grads):
        pieces = [
            [
                (which, slot * tokens, i * (end - begin), i * share + begin, end - begin)
                for which, (begin, end) in enumerate(spans)
                for i in range(3)
            ]
            for slot in range(count)
        ]
        return ranked_terms(where, grads, range(count), pieces, w_attn, n_slots, "attn_terms")

    if plane:
        x_bit, y_bit = (me_dp >> 1) & 1, (me_dp >> 2) & 1

        def split(total, bit, axis):
            return (choose(total, bit, axis), choose(total, 1 - bit, axis))

        kept, given = outer_halves(where, full_pairs, count, "full_grads")
        got = swap(given, "dp", 0)
        grad_parts, kept, got, branch_terms = fence((grad_parts, kept, got, branch_terms))
        branch_two = lax.psum_scatter(
            branch_terms.reshape(-1, width), "tensor", scatter_dimension=0, tiled=True
        )
        box = (2, count, 2, 2, unit_rows, width)
        bits_here = jnp.stack([x_bit, y_bit]).astype(jnp.int32)
        kept_one, given_one, kept_two, given_two = sum_split(
            bits_here, kept.reshape(box), got.reshape(box)
        )
        got_one, got_two = swap(given_one, "dp", 1), swap(given_two, "dp", 2)
        grads_early = self_attend_back(qkv, grad_parts, attended, logs, share, *spans[0])
        kept_one, got_one, kept_two, got_two, grads_early, grad_parts = fence(
            (kept_one, got_one, kept_two, got_two, grads_early, grad_parts)
        )
        kept_one, given_one = split(kept_one + got_one, y_bit, 1)
        kept_two, given_two = split(kept_two + got_two, x_bit, 1)
        kept_one, given_one, kept_two, given_two, grad_parts = fence(
            (kept_one, given_one, kept_two, given_two, grad_parts)
        )
        got_one, got_two = swap(given_one, "dp", 2), swap(given_two, "dp", 1)
        grads_late = self_attend_back(qkv, grad_parts, attended, logs, share, *spans[1])
        kept_one, got_one, kept_two, got_two, grads_early, grads_late, mlp_sum = fence(
            (kept_one, got_one, kept_two, got_two, grads_early, grads_late, mlp_sum)
        )
        mlp_sum = lax.all_gather(mlp_sum, "dp", axis=0, tiled=True)
        full_parts = to_ring(jnp.stack([kept_one + got_one, kept_two + got_two], axis=1))
        full_parts = [full_parts[k] for k in range(count)]
        full_parts, grads_early, grads_late = fence((full_parts, grads_early, grads_late))
        grads_qkv = [grads_early, grads_late]
        full_got = [shift(full_parts[k], k) for k in range(1, count)]
        attn_kept, attn_given = outer_halves(
            where, attention_pairs(grads_qkv, grad_parts), 1, "attn_grads"
        )
        attn_got = swap(attn_given, "dp", 0)
        grad_h_terms, grad_h_sums = input_terms(grads_qkv)
        mod_terms = jnp.concatenate([grad_h_sums, row_sums, branch_row[None]])
        grad_h_one = lax.psum_scatter(
            grad_h_terms.reshape(-1, width), "tensor", scatter_dimension=0, tiled=True
        )
        attn_kept, attn_got, mod_terms, branch_two = fence(
            (attn_kept, attn_got, mod_terms, branch_two)
        )
        attn_all = (attn_kept + attn_got).reshape(2, 2, 2, unit_rows, width)
        one_kept, one_given = split(attn_all[0], x_bit, 1)
        two_kept, two_given = split(attn_all[1], y_bit, 0)
        one_got, two_got = swap(one_given, "dp", 1), swap(two_given, "dp", 2)
        for bit in range(2):
            mod_terms = mod_terms + swap(mod_terms, "dp", bit)
        full_own = full_parts[0]
        one_kept, one_got, two_kept, two_got, mod_terms, full_own, full_got = fence(
            (one_kept, one_got, two_kept, two_got, mod_terms, full_own, full_got)
        )
        full_sum = full_own.astype(jnp.float32)
        for part in full_got:
            full_sum = full_sum + part.astype(jnp.float32)
        full_sum = full_sum.astype(low)
        one_kept, one_given = split(one_kept + one_got, y_bit, 0)
        two_kept, two_given = split(two_kept + two_got, x_bit, 0)
        one_got, two_got = swap(one_given, "dp", 2), swap(two_given, "dp", 1)
        mod_terms = mod_terms + swap(mod_terms, "dp", 2)
        one_kept, one_got, two_kept, two_got, full_sum, mod_terms, mlp_sum = fence(
            (one_kept, one_got, two_kept, two_got, full_sum, mod_terms, mlp_sum)
        )
        first = jnp.stack([one_kept + one_got, full_sum[0]])
        second = jnp.stack([two_kept + two_got, full_sum[1]])
        first_got, second_got = swap(first, "dp", 1), swap(second, "dp", 2)
        first = jnp.concatenate([first, first_got])
        second = jnp.concatenate([second, second_got])
        mod_terms = mod_terms + swap(mod_terms, "tensor", 0)
        first, second, mod_terms = fence((first, second, mod_terms))
        first_far, second_far = swap(first, "dp", 2), swap(second, "dp", 1)
        for bit in range(1, count.bit_length() - 1):
            mod_terms = mod_terms + swap(mod_terms, "tensor", bit)
        first, first_far, second, second_far, mod_terms = fence(
            (first, first_far, second, second_far, mod_terms)
        )
        pool = jnp.concatenate([first, first_far, second, second_far])
        other = swap(pool, "dp", 0)
        mod_grad = mod_terms
        pool, other = fence((pool, other))
        which, position = in_pool(member_of, np.where(is_attn, 0, 1), 2)
        which = jnp.where(is_mlp, 2, which)
        position = jnp.where(is_mlp, np.arange(units) - 8 * per, position)
        own = jnp.sum(jnp.where(match[:, :, None], jnp.stack([which, position], 1)[None], 0), axis=1)
        new_first, new_second, new_master = update_slots(
            master,
            first_moment,
            second_moment,
            filled.astype(jnp.int32),
            own[:, 0],
            own[:, 1],
            (pool, other, mlp_sum),
        )
    else:
        branch_two = lax.psum_scatter(
            branch_terms.reshape(-1, width), "tensor", scatter_dimension=0, tiled=True
        )
        grads_qkv = [self_attend_back(qkv, grad_parts, attended, logs, share, *span) for span in spans]
        attn_grads = [
            outer(array[:, lane : lane + lanes], right).astype(low)
            for left, right in attention_pairs(grads_qkv, grad_parts)
            for array, lane, lanes, row in left
        ]
        grad_h_terms, grad_h_sums = input_terms(grads_qkv)
        grad_h_one = lax.psum_scatter(
            grad_h_terms.reshape(-1, width), "tensor", scatter_dimension=0, tiled=True
        )
        mixed_all = from_ring(jnp.stack([item[:tokens] for item in mixed]), 1)
        mixed_all = mixed_all.transpose(1, 0, 2).reshape(tokens, width)
        full_grads = [outer(mixed_all, attn_low)]
        full_grads += [outer(left[0][0], right) for left, right in full_pairs[1:]]
        full_sum = [g.astype(low).reshape(count, share, width) for g in full_grads]
        full_sum = jnp.stack(full_sum, axis=1)
        full_sum = lax.psum_scatter(full_sum, "tensor", scatter_dimension=0, tiled=True)
        order = np.array(group_attn + group_full + group_mlp)
        sums = jnp.concatenate(
            [jnp.concatenate(attn_grads), full_sum.reshape(-1, width), mlp_grad.reshape(-1, width)]
        )
        sums = lax.psum(sums.reshape(units, unit_rows, width), "dp")
        owned = jnp.take(sums, jnp.array(np.argsort(order))[unit_of_slot], axis=0, mode="clip")
        mod_grad = total_sum(jnp.concatenate([grad_h_sums, row_sums, branch_row[None]]))
        new_first, new_second, new_master = adamw(
            master,
            first_moment,
            second_moment,
            owned.astype(jnp.float32),
            filled.astype(jnp.float32)[:, None, None],
            rate,
        )
    branch_two, second_res, grad_h_one, new_first = fence(
        (branch_two, second_res, grad_h_one, new_first)
    )
    grad_h_one = grad_h_one.astype(jnp.float32)
    block_out = second_res + mod_row(5) * branch_two.astype(jnp.float32)
    input_grad = first_grad + norm_back(grad_h_one, normed_one, inverse_one, mod_row(1))
    mod_new_first, mod_new_second, mod_new = adamw(
        mod_table, mod_first, mod_second, mod_grad, 1.0, table_rate
    )
    return (
        block_out[None],
        input_grad[None],
        new_first,
        new_second,
        new_master,
        mod_new_first,
        mod_new_second,
        mod_new,
    )


def solution(mesh):
    in_specs = (
        P("dp", "tensor", None),
        P("dp", None, None),
        P("dp", "tensor"),
        P("dp", None),
        P(),
        P("dp", "tensor", None),
        P("dp", "tensor", None),
        P("dp", "tensor", None),
        P(),
        P(),
        P(),
        P("dp", "tensor", None),
    )
    out_specs = (
        P("dp", "tensor", None),
        P("dp", "tensor", None),
        P("dp", "tensor", None),
        P("dp", "tensor", None),
        P("dp", "tensor", None),
        P(),
        P(),
        P(),
    )
    return jax.shard_map(
        on_device, mesh=mesh, in_specs=in_specs, out_specs=out_specs, check_vma=False
    )
```

```python
import math

import jax
import jax.numpy as jnp
import numpy as np
from jax import lax
from jax.experimental import pallas as pl
from jax.experimental.pallas import tpu as pltpu
from jax.sharding import PartitionSpec as P

HEAD_DIM = 72
STEP = 10


norm_eps = 1e-06
beta_one = 0.9
beta_two = 0.999
rate = 0.03
table_rate = 0.3
decay = 0.01
adam_eps = 1e-08
low = jnp.bfloat16


def ranks_of(owners):
    index = jnp.arange(owners.shape[0])
    before = (owners[None, :] == owners[:, None]) & (index[None, :] < index[:, None])
    return jnp.sum(before.astype(jnp.int32), axis=1)


def layer_norm(values):
    center = values - jnp.mean(values, axis=-1, keepdims=True)
    inverse = lax.rsqrt(jnp.mean(center * center, axis=-1, keepdims=True) + norm_eps)
    return (center * inverse, inverse)


def norm_back(grad_rows, normed, inverse, scale_row):
    scaled = grad_rows * (1.0 + scale_row)
    mean_one = jnp.mean(scaled, axis=-1, keepdims=True)
    mean_two = jnp.mean(scaled * normed, axis=-1, keepdims=True)
    return inverse * (scaled - mean_one - normed * mean_two)


def project(rows, weight):
    return jnp.einsum("ld,rd->lr", rows, weight, preferred_element_type=jnp.float32)


def expand(rows, weight):
    return jnp.einsum("lr,rd->ld", rows, weight, preferred_element_type=jnp.float32)


def outer(left, right):
    return jnp.einsum("lr,ld->rd", left, right, preferred_element_type=jnp.float32)


def shift(values, step):
    count = lax.axis_size("tensor")
    return lax.ppermute(values, "tensor", [(i, (i + step) % count) for i in range(count)])


def ring(values):
    return [values] + [shift(values, k) for k in range(1, lax.axis_size("tensor"))]


def to_ring(stacked):
    count = stacked.shape[0]
    twice = jnp.concatenate([stacked, stacked], axis=0)
    return lax.dynamic_slice_in_dim(twice, lax.axis_index("tensor"), count, 0)


def from_ring(stacked, sign):
    count = stacked.shape[0]
    me = lax.axis_index("tensor")
    place = lax.rem(sign * (jnp.arange(count) - me) + 2 * count, count)
    return jnp.take(stacked, place, axis=0, mode="clip")


cheap = pl.CostEstimate(flops=1000, bytes_accessed=1000, transcendentals=0)
costly = pl.CostEstimate(flops=10**10, bytes_accessed=10**7, transcendentals=0)


def self_attend(qkv, share):
    length = qkv.shape[0]
    rows = min(512, length)
    curve = HEAD_DIM ** (-0.5) * math.log2(math.e)
    heads = share // HEAD_DIM

    def body(qkv_ref, out_ref, log_ref):
        @pl.loop(0, length // rows)
        def _(step):
            here = pl.ds(pl.multiple_of(step * rows, rows), rows)
            parts = []
            for head in range(heads):
                at = head * HEAD_DIM
                q = qkv_ref[here, at : at + HEAD_DIM]
                k = qkv_ref[:, share + at : share + at + HEAD_DIM]
                v = qkv_ref[:, 2 * share + at : 2 * share + at + HEAD_DIM]
                scores = dot(k, q, nt)
                top = jnp.max(scores, axis=0, keepdims=True)
                expo = jnp.exp2((scores - top) * curve)
                total = jnp.sum(expo, axis=0, keepdims=True)
                log_ref[head : head + 1, here] = top * curve + jnp.log2(total)
                parts.append((dot(v, expo.astype(low), tn) * (1.0 / total)).T)
            out_ref[here, :] = jnp.concatenate(parts, axis=1).astype(low)

    return pl.pallas_call(
        body,
        out_shape=[
            jax.ShapeDtypeStruct((length, share), low),
            jax.ShapeDtypeStruct((heads, length), jnp.float32),
        ],
        compiler_params=pltpu.CompilerParams(vmem_limit_bytes=40 * 2**20),
        cost_estimate=cheap,
        name="self_attend",
    )(qkv)


def self_attend_back(qkv, grads, mixed, logs, share, begin, end):
    length = qkv.shape[0]
    rows = length // len(grads)
    span = end - begin
    scale = HEAD_DIM ** (-0.5)
    curve = scale * math.log2(math.e)

    def body(qkv_ref, mixed_ref, log_ref, *refs):
        grad_refs, (out_ref, grad_k, grad_v) = refs[: len(grads)], refs[len(grads) :]
        for step, grad_ref in enumerate(grad_refs):
            here = slice(step * rows, (step + 1) * rows)
            parts = []
            for head, at in enumerate(range(begin, end, HEAD_DIM)):
                q = qkv_ref[here, at : at + HEAD_DIM]
                k = qkv_ref[:, share + at : share + at + HEAD_DIM]
                v = qkv_ref[:, 2 * share + at : 2 * share + at + HEAD_DIM]
                g = grad_ref[0:rows, at : at + HEAD_DIM]
                o = mixed_ref[here, at : at + HEAD_DIM]
                inner = g.astype(jnp.float32) * o.astype(jnp.float32)
                inner = jnp.sum(inner.T, axis=0, keepdims=True)
                which = begin // HEAD_DIM + head
                probs = jnp.exp2(dot(k, q, nt) * curve - log_ref[which : which + 1, here])
                grad_scores = (probs * (dot(v, g, nt) - inner)).astype(low)
                to_v = dot(probs.astype(low), g)
                to_k = dot(grad_scores, q)
                if step:
                    grad_v[head] += to_v
                    grad_k[head] += to_k
                else:
                    grad_v[head] = to_v
                    grad_k[head] = to_k
                parts.append((dot(k, grad_scores, tn) * scale).T)
            out_ref[here, 0:span] = jnp.concatenate(parts, axis=1).astype(low)
        heads = range(span // HEAD_DIM)
        both = [grad_k[head] * scale for head in heads]
        out_ref[:, span : 2 * span] = jnp.concatenate(both, axis=1).astype(low)
        both = [grad_v[head] for head in heads]
        out_ref[:, 2 * span :] = jnp.concatenate(both, axis=1).astype(low)

    return pl.pallas_call(
        body,
        out_shape=jax.ShapeDtypeStruct((length, 3 * span), low),
        scratch_shapes=[pltpu.VMEM((span // HEAD_DIM, length, HEAD_DIM), jnp.float32)] * 2,
        compiler_params=pltpu.CompilerParams(vmem_limit_bytes=40 * 2**20),
        cost_estimate=costly,
        name="self_attend_back",
    )(qkv, mixed, logs, *grads)


def mlp_core(rows_in, grads_in, w_mlp, after):
    groups = len(rows_in)
    tokens, width = rows_in[0].shape
    hidden = w_mlp.shape[0] // 2
    chunk = 384 if hidden % 384 == 0 else hidden
    steps = hidden // chunk
    curve = 0.7978845608028654

    def body(*refs):
        rows, grads = refs[:groups], refs[groups : 2 * groups]
        up, down = refs[2 * groups : 2 * groups + 2]
        act, grad_pre, *outs = refs[2 * groups + 2 + len(after) : -1]
        total = refs[-1]
        step = pl.program_id(0)
        for i in range(groups):
            pre = lax.dot_general(
                rows[i][...], up[...], (((1,), (1,)), ((), ())), preferred_element_type=jnp.float32
            )
            square = pre * pre
            bend = jnp.tanh(curve * pre * (1.0 + 0.044715 * square))
            half = 0.5 * (1.0 + bend)
            here = pl.ds(i * tokens, tokens)
            act[here, :] = (pre * half).astype(low)
            slope = half + (0.5 * curve) * pre * (1.0 - bend * bend) * (1.0 + 0.134145 * square)
            grad_act = lax.dot_general(
                grads[i][...], down[...], (((1,), (1,)), ((), ())), preferred_element_type=jnp.float32
            )
            grad_low = (grad_act * slope).astype(low)
            grad_pre[here, :] = grad_low
            term = jnp.dot(grad_low, up[...], preferred_element_type=jnp.float32)

            @pl.when(step == 0)
            def _():
                total[here, :] = term

            @pl.when(step > 0)
            def _():
                total[here, :] += term

            @pl.when(step == steps - 1)
            def _():
                outs[i][...] = total[here, :].astype(low)

    whole = pl.BlockSpec((tokens, width), lambda s: (0, 0))
    across = pl.BlockSpec((groups * tokens, chunk), lambda s: (0, s))
    return pl.pallas_call(
        body,
        grid=(steps,),
        in_specs=[whole] * (2 * groups)
        + [
            pl.BlockSpec((chunk, width), lambda s: (s, 0)),
            pl.BlockSpec((chunk, width), lambda s: (steps + s, 0)),
        ]
        + [pl.BlockSpec(memory_space=pl.ANY)] * len(after),
        out_specs=[across, across] + [whole] * groups,
        out_shape=[jax.ShapeDtypeStruct((groups * tokens, hidden), low)] * 2
        + [jax.ShapeDtypeStruct((tokens, width), low)] * groups,
        scratch_shapes=[pltpu.VMEM((groups * tokens, width), jnp.float32)],
        compiler_params=pltpu.CompilerParams(vmem_limit_bytes=60 * 2**20),
        cost_estimate=cheap,
        name="mlp_core",
    )(*rows_in, *grads_in, w_mlp, w_mlp, *after)


nt = (((1,), (1,)), ((), ()))
tn = (((0,), (0,)), ((), ()))


def dot(left, right, dims=(((1,), (0,)), ((), ()))):
    return lax.dot_general(left, right, dims, preferred_element_type=jnp.float32)


def softmax_keys(keys, queries):
    scores = dot(keys, queries, nt) * HEAD_DIM ** (-0.5)
    expo = jnp.exp(scores - jnp.max(scores, axis=0, keepdims=True))
    return expo * (1.0 / jnp.sum(expo, axis=0, keepdims=True))


def cuts_of(width):
    size = 384 if width % 384 == 0 else width
    return [slice(i, i + size) for i in range(0, width, size)]


def in_smem():
    return pl.BlockSpec(memory_space=pltpu.SMEM)


def in_vmem():
    return pl.BlockSpec(memory_space=pltpu.VMEM)


def line_slots(place, own, ups, downs, rows):
    count = len(ups) + 1
    tokens, width = own.shape

    def body(place_ref, *refs):
        own_ref, up_refs, down_refs = refs[0], refs[1:count], refs[count : 2 * count - 1]
        rows_ref, outs, out = refs[2 * count - 1], refs[2 * count : -1], refs[-1]
        me = place_ref[0]

        def modulate(slot, ref):
            value = ref[...].astype(jnp.float32)
            value = value * (1.0 + rows_ref[1:2, :]) + rows_ref[0:1, :]
            out[slot * tokens : (slot + 1) * tokens, :] = value.astype(low)

        modulate(0, own_ref)
        for k in range(1, count):
            for side, ref in ((me >= k, up_refs[k - 1]), (me < k, down_refs[count - k - 1])):

                @pl.when(side)
                def _():
                    outs[k - 1][...] = ref[...]
                    modulate(k, ref)

    shapes = [(tokens, width)] * (count - 1) + [(count * tokens, width)]
    return pl.pallas_call(
        body,
        in_specs=[in_smem()] + [in_vmem()] * (2 * count),
        out_shape=[jax.ShapeDtypeStruct(shape, low) for shape in shapes],
        compiler_params=pltpu.CompilerParams(vmem_limit_bytes=32 * 2**20),
        cost_estimate=cheap,
        name="line_slots",
    )(place, own, *ups, *downs, rows)


def cross_block(place, mixed, hidden, rows, text, w_out, c_query, c_value, c_out):
    count, share = len(mixed), mixed[0].shape[1]
    tokens, width = hidden.shape
    words = text.shape[0]
    per = share // HEAD_DIM

    def body(place_ref, *refs):
        parts = refs[:count]
        x_ref, rows_ref, text_ref = refs[count : count + 3]
        far = refs[count + 3 : count + 7]
        outs = refs[count + 7 : count + 16]
        inverse = refs[count + 16]
        wo, wq, wv, wc, *own = refs[count + 17 : -3]
        held, read, sems = refs[-3:]
        branch, res_low, cq, ck, cv, crossed, res, normed, out = own
        me = place_ref[0]
        loads = [
            pltpu.make_async_copy(source, target, read.at[i])
            for i, (source, target) in enumerate(zip(far, (wo, wq, wv, wc)))
        ]
        stores = [
            pltpu.make_async_copy(source, target, sems.at[i])
            for i, (source, target) in enumerate(zip(own, outs))
        ]
        for load in loads:
            load.start()
        loads[0].wait()
        for cut in cuts_of(width):
            total = jnp.zeros((tokens, cut.stop - cut.start), jnp.float32)
            for k in range(count):
                rank = lax.rem(me + k, count)
                here = pl.ds(pl.multiple_of(rank * share, 32), share)
                total += dot(parts[k][0:tokens, :], wo[here, cut])
            branch[:, cut] = total
            first = x_ref[:, cut].astype(jnp.float32) + rows_ref[0:1, cut] * total
            res[:, cut] = first
            res_low[:, cut] = first.astype(low)
        stores[0].start()
        stores[1].start()
        loads[1].wait()
        loads[2].wait()
        for cut in cuts_of(width):
            cq[:, cut] = dot(res_low[...], wq[cut, :], nt).astype(low)
            cv[:, cut] = dot(text_ref[...], wv[cut, :], nt).astype(low)
        for k in range(count):
            held[lax.rem(me + k, count)] = parts[k][tokens:, :]
        ck[...] = jnp.concatenate([held[rank] for rank in range(count)], axis=1)
        for i in (2, 3, 4):
            stores[i].start()
        parts_out = []
        for at in range(0, width, HEAD_DIM):
            head = slice(at, at + HEAD_DIM)
            probs = softmax_keys(ck[:, head], cq[:, head]).astype(low)
            parts_out.append(dot(cv[:, head], probs, tn).T)
        crossed[...] = jnp.concatenate(parts_out, axis=1).astype(low)
        stores[5].start()
        loads[3].wait()
        for cut in cuts_of(width):
            res[:, cut] += dot(crossed[...], wc[:, cut])
        second = res[...]
        center = second - jnp.mean(second, axis=-1, keepdims=True)
        spread = lax.rsqrt(jnp.mean(center * center, axis=-1, keepdims=True) + norm_eps)
        inverse[...] = spread
        scaled = center * spread
        normed[...] = scaled
        stores[6].start()
        stores[7].start()
        out[...] = (scaled * (1.0 + rows_ref[2:3, :]) + rows_ref[1:2, :]).astype(low)
        stores[8].start()
        for store in stores:
            store.wait()

    wide = (tokens, width)
    shapes = [
        (wide, jnp.float32),
        (wide, low),
        (wide, low),
        ((words, width), low),
        ((words, width), low),
        (wide, low),
        (wide, jnp.float32),
        (wide, jnp.float32),
        (wide, low),
    ]
    anywhere = pl.BlockSpec(memory_space=pl.ANY)
    return pl.pallas_call(
        body,
        in_specs=[in_smem()] + [in_vmem()] * (count + 3) + [anywhere] * 4,
        out_specs=[anywhere] * len(shapes) + [in_vmem()],
        out_shape=[jax.ShapeDtypeStruct(*item) for item in shapes]
        + [jax.ShapeDtypeStruct((tokens, 1), jnp.float32)],
        scratch_shapes=[pltpu.VMEM((width, width), low)] * 4
        + [pltpu.VMEM(*item) for item in shapes]
        + [
            pltpu.VMEM((count, words, share), low),
            pltpu.SemaphoreType.DMA((4,)),
            pltpu.SemaphoreType.DMA((len(shapes),)),
        ],
        compiler_params=pltpu.CompilerParams(vmem_limit_bytes=60 * 2**20),
        cost_estimate=cheap,
        name="cross_block",
    )(place, *mixed, hidden, rows, text, w_out, c_query, c_value, c_out)


def cross_back(
    place, terms, grad, rows, normed, inverse, branch, cq, ck, cv, c_out, c_query, w_out, after
):
    count = len(terms)
    tokens, width = grad.shape
    words = ck.shape[0]
    share = width // count
    scale = HEAD_DIM ** (-0.5)

    def body(place_ref, *refs):
        parts = refs[:count]
        grad_ref, rows_ref, i_ref, k_ref, v_ref = refs[count : count + 5]
        far = refs[count + 5 : count + 11]
        refs = refs[: count + 11] + refs[count + 11 + len(after) :]
        stored = refs[count + 11 : count + 15]
        grad_v, sums = refs[count + 15 : count + 17]
        outs = refs[count + 17 : 2 * count + 17]
        near = refs[2 * count + 17 : 2 * count + 23]
        n_ref, wc, q_ref, wq, wo, b_ref = near
        own = refs[2 * count + 23 : 2 * count + 27]
        first, cross_low, grad_q, attn_low = own
        back, held, read, sems = refs[2 * count + 27 :]
        me = place_ref[0]
        loads = [
            pltpu.make_async_copy(source, target, read.at[i])
            for i, (source, target) in enumerate(zip(far, near))
        ]
        stores = [
            pltpu.make_async_copy(source, target, sems.at[i])
            for i, (source, target) in enumerate(zip(own, stored))
        ]
        for load in loads:
            load.start()
        loads[0].wait()
        total = parts[0][...].astype(jnp.float32)
        for part in parts[1:]:
            total += part[...].astype(jnp.float32)
        n = n_ref[...]
        sums[1:2, :] = jnp.sum(total, axis=0, keepdims=True)
        sums[2:3, :] = jnp.sum(total * n, axis=0, keepdims=True)
        second = grad_ref[...].astype(jnp.float32) + norm_back(total, n, i_ref[...], rows_ref[2:3, :])
        first[...] = second
        cross_low[...] = second.astype(low)
        stores[1].start()
        loads[1].wait()
        loads[2].wait()
        for cut in cuts_of(width):
            back[:, cut] = dot(cross_low[...], wc[cut, :], nt).astype(low)
        grads = ([], [], [])
        for at in range(0, width, HEAD_DIM):
            head = slice(at, at + HEAD_DIM)
            q, k, v, g = q_ref[:, head], k_ref[:, head], v_ref[:, head], back[:, head]
            probs = softmax_keys(k, q)
            grad_probs = dot(v, g, nt)
            inner = jnp.sum(probs * grad_probs, axis=0, keepdims=True)
            grad_scores = (probs * (grad_probs - inner)).astype(low)
            grads[0].append((dot(k, grad_scores, tn) * scale).T)
            grads[1].append(dot(grad_scores, q) * scale)
            grads[2].append(dot(probs.astype(low), g))
        grad_q[...] = jnp.concatenate(grads[0], axis=1).astype(low)
        grad_v[...] = jnp.concatenate(grads[2], axis=1).astype(low)
        heads = share // HEAD_DIM
        for rank in range(count):
            pieces = grads[1][rank * heads : (rank + 1) * heads]
            held[rank] = jnp.concatenate(pieces, axis=1).astype(low)
        stores[2].start()
        for load in loads[3:]:
            load.wait()
        for cut in cuts_of(width):
            whole = first[:, cut] + dot(grad_q[...], wq[:, cut])
            first[:, cut] = whole
            attn_low[:, cut] = (rows_ref[0:1, cut] * whole).astype(low)
            sums[0:1, cut] = jnp.sum(b_ref[:, cut] * whole, axis=0, keepdims=True)
        stores[0].start()
        stores[3].start()
        for k in range(count):
            rank = lax.rem(me + k, count)
            here = pl.ds(pl.multiple_of(rank * share, 32), share)
            outs[k][0:tokens, :] = dot(attn_low[...], wo[here, :], nt).astype(low)
            outs[k][tokens:, :] = held[rank]
        for store in stores:
            store.wait()

    wide, square = (tokens, width), (width, width)
    shapes = [
        (wide, jnp.float32),
        (wide, low),
        (wide, low),
        (wide, low),
        ((words, width), low),
        ((3, width), jnp.float32),
    ] + [((tokens + words, share), low)] * count
    anywhere = pl.BlockSpec(memory_space=pl.ANY)
    loaded = [
        pltpu.VMEM(wide, jnp.float32),
        pltpu.VMEM(square, low),
        pltpu.VMEM(wide, low),
        pltpu.VMEM(square, low),
        pltpu.VMEM(square, low),
        pltpu.VMEM(wide, jnp.float32),
    ]
    return pl.pallas_call(
        body,
        in_specs=[in_smem()] + [in_vmem()] * (count + 5) + [anywhere] * (6 + len(after)),
        out_specs=[anywhere] * 4 + [in_vmem()] * (2 + count),
        out_shape=[jax.ShapeDtypeStruct(*item) for item in shapes],
        scratch_shapes=loaded
        + [pltpu.VMEM(*item) for item in shapes[:4]]
        + [
            pltpu.VMEM(wide, low),
            pltpu.VMEM((count, words, share), low),
            pltpu.SemaphoreType.DMA((6,)),
            pltpu.SemaphoreType.DMA((4,)),
        ],
        compiler_params=pltpu.CompilerParams(vmem_limit_bytes=60 * 2**20),
        cost_estimate=costly,
        name="cross_back",
    )(
        place,
        *terms,
        grad,
        rows,
        inverse,
        ck,
        cv,
        normed,
        c_out,
        cq,
        c_query,
        w_out,
        branch,
        *after,
    )


def outer_halves(place, pairs, parts, name):
    width = pairs[0][1].shape[1]
    high = [sum(piece[2] for piece in left) for left, _ in pairs]
    size = high[0] // parts
    tokens = [right.shape[0] for _, right in pairs]
    flat = []

    def index_of(array):
        for i, other in enumerate(flat):
            if other is array:
                return i
        flat.append(array)
        return len(flat) - 1

    plans = [
        ([(index_of(array), *rest) for array, *rest in left], index_of(right))
        for left, right in pairs
    ]
    amount = len(pairs)

    def body(place_ref, *refs):
        ins, (kept, given), (held, sems) = refs[: len(flat)], refs[len(flat) :][:2], refs[-2:]
        turned = refs[len(flat) + 2 : -2]
        me, core = place_ref[0], place_ref[1]
        for i, (left, right) in enumerate(plans):
            for k, (which, lane, lanes, row) in enumerate(left):
                piece = ins[which][0 : tokens[i], lane : lane + lanes]
                piece = piece.astype(jnp.float32).T.astype(low)
                if row is None:
                    rank = lax.rem(me + k, len(left))
                    turned[i][pl.ds(pl.multiple_of(rank * lanes, 32), lanes), :] = piece
                else:
                    turned[i][row : row + lanes, :] = piece
            for part in range(parts):
                at = i * parts + part
                tile = dot(turned[i][part * size : (part + 1) * size, :], ins[right][...])
                held[at] = tile.astype(low)
                for out, side in ((kept, 0), (given, 1)):

                    @pl.when((core ^ (i & 1)) == side)
                    def _():
                        pltpu.make_async_copy(
                            held.at[at], out.at[i // 2, part], sems.at[at]
                        ).start()

        for at in range(amount * parts):
            pltpu.make_async_copy(held.at[at], kept.at[0, 0], sems.at[at]).wait()

    out = jax.ShapeDtypeStruct((amount // 2, parts, size, width), low)
    return pl.pallas_call(
        body,
        in_specs=[in_smem()] + [in_vmem()] * len(flat),
        out_specs=[pl.BlockSpec(memory_space=pl.ANY)] * 2,
        out_shape=[out, out],
        scratch_shapes=[pltpu.VMEM((high[i], tokens[i]), low) for i in range(amount)]
        + [
            pltpu.VMEM((amount * parts, size, width), low),
            pltpu.SemaphoreType.DMA((amount * parts,)),
        ],
        compiler_params=pltpu.CompilerParams(vmem_limit_bytes=60 * 2**20),
        cost_estimate=cheap if parts > 1 else costly,
        name=name,
    )(place, *flat)


def mlp_grads(grad_pres, acts, rows_in, grads_in, after):
    pieces, rights = len(acts), len(rows_in)
    tokens, width = rows_in[0].shape
    hidden = acts[0].shape[1]
    chunk = 384 if hidden % 384 == 0 else hidden
    steps = hidden // chunk

    def body(*refs):
        step = pl.program_id(0)
        lefts_up, lefts_down = refs[:pieces], refs[pieces : 2 * pieces]
        rights_up = refs[2 * pieces : 2 * pieces + rights]
        rights_down = refs[2 * pieces + rights : 2 * pieces + 2 * rights]
        out = refs[-1]

        def terms(lefts, turn, others):
            here = pl.ds(pl.multiple_of(turn * chunk, chunk), chunk)
            total = jnp.zeros((chunk, width), jnp.float32)
            cursor = 0
            for left in lefts:
                for i in range(left.shape[0] // tokens):
                    total += dot(left[i * tokens : (i + 1) * tokens, here], others[cursor][...], tn)
                    cursor += 1
            out[...] = total.astype(low)

        @pl.when(step < steps)
        def _():
            terms(lefts_up, step, rights_up)

        @pl.when(step >= steps)
        def _():
            terms(lefts_down, step - steps, rights_down)

    arrays = (*grad_pres, *acts, *rows_in, *grads_in)
    chunked = pl.BlockSpec((chunk, width), lambda s: (s, 0))
    return pl.pallas_call(
        body,
        grid=(2 * steps,),
        in_specs=[pl.BlockSpec(array.shape, lambda s: (0, 0)) for array in arrays]
        + [pl.BlockSpec(memory_space=pl.ANY)] * len(after),
        out_specs=chunked,
        out_shape=jax.ShapeDtypeStruct((2 * hidden, width), low),
        compiler_params=pltpu.CompilerParams(vmem_limit_bytes=60 * 2**20),
        cost_estimate=cheap,
        name="mlp_grads",
    )(*arrays, *after)


def ranked_terms(place, lefts, order, pieces, weight, factors, name):
    tokens, width = factors[0].shape
    count = len(factors)

    def body(place_ref, *refs):
        ins, weight_ref = refs[: len(lefts)], refs[len(lefts)]
        others = refs[len(lefts) + 1 : len(lefts) + 1 + count]
        out, sums = refs[-2:]
        me = place_ref[0]
        for i, slot in enumerate(order):
            rank = lax.rem(me - slot + count, count)
            for cut in cuts_of(width):
                term = jnp.zeros((tokens, cut.stop - cut.start), jnp.float32)
                for which, row, lane, start, depth in pieces[i]:
                    term += dot(
                        ins[which][row : row + tokens, lane : lane + depth],
                        weight_ref[start : start + depth, cut],
                    )
                out[rank, :, cut] = term.astype(low)
                one = jnp.sum(term, axis=0, keepdims=True)
                two = jnp.sum(term * others[i][:, cut].astype(jnp.float32), axis=0, keepdims=True)
                if i:
                    one, two = one + sums[0:1, cut], two + sums[1:2, cut]
                sums[0:1, cut], sums[1:2, cut] = one, two

    return pl.pallas_call(
        body,
        in_specs=[in_smem()] + [in_vmem()] * (len(lefts) + 1 + count),
        out_shape=[
            jax.ShapeDtypeStruct((count, tokens, width), low),
            jax.ShapeDtypeStruct((2, width), jnp.float32),
        ],
        compiler_params=pltpu.CompilerParams(vmem_limit_bytes=60 * 2**20),
        cost_estimate=cheap if len(lefts) > 2 else costly,
        name=name,
    )(place, *lefts, weight, *factors)


def sum_split(place, kept, got):
    count, unit_rows, width = kept.shape[1], kept.shape[4], kept.shape[5]

    def body(place_ref, one, two, keep_x, give_x, keep_y, give_y):
        x, y = place_ref[0], place_ref[1]

        def total(*index):
            return (one[index].astype(jnp.float32) + two[index].astype(jnp.float32)).astype(low)

        for j in range(2):
            keep_x[0, j] = total(0, 0, j, x)
            give_x[0, j] = total(0, 0, j, 1 - x)
            keep_y[0, j] = total(1, 0, y, j)
            give_y[0, j] = total(1, 0, 1 - y, j)

    block = pl.BlockSpec((2, 1, 2, 2, unit_rows, width), lambda r, *_: (0, r, 0, 0, 0, 0))
    part = pl.BlockSpec((1, 2, unit_rows, width), lambda r, *_: (r, 0, 0, 0))
    return pl.pallas_call(
        body,
        grid_spec=pltpu.PrefetchScalarGridSpec(
            num_scalar_prefetch=1, grid=(count,), in_specs=[block] * 2, out_specs=[part] * 4
        ),
        out_shape=[jax.ShapeDtypeStruct((count, 2, unit_rows, width), low)] * 4,
        compiler_params=pltpu.CompilerParams(vmem_limit_bytes=60 * 2**20),
        cost_estimate=costly,
        name="sum_split",
    )(place, kept, got)


def update_slots(master, first_moment, second_moment, filled, which, position, sources):
    capacity, unit_rows, width = master.shape

    group = math.gcd(capacity, 2)
    steps = capacity // group

    def body(filled_ref, which_ref, position_ref, weight, one, two, *rest):
        ins = rest[: len(sources)]
        new_one, new_two, new_weight, held, sems = rest[len(sources) :]
        step = pl.program_id(0)

        def fetch(turn):
            for i in range(group):
                slot = turn * group + i
                for source, ref in enumerate(ins):

                    @pl.when(which_ref[slot] == source)
                    def _():
                        pltpu.make_async_copy(
                            ref.at[position_ref[slot]], held.at[turn % 2, i], sems.at[turn % 2, i]
                        ).start()

        @pl.when(step == 0)
        def _():
            fetch(step)

        @pl.when(step < steps - 1)
        def _():
            fetch(step + 1)

        for i in range(group):
            pltpu.make_async_copy(
                ins[0].at[0], held.at[step % 2, i], sems.at[step % 2, i]
            ).wait()
            mask = (filled_ref[step * group + i] > 0).astype(jnp.float32)
            grad = held[step % 2, i].astype(jnp.float32)
            results = adamw(weight[i], one[i], two[i], grad, mask, rate)
            new_one[i], new_two[i], new_weight[i] = results

    block = pl.BlockSpec((group, unit_rows, width), lambda s, *_: (s, 0, 0))
    return pl.pallas_call(
        body,
        grid_spec=pltpu.PrefetchScalarGridSpec(
            num_scalar_prefetch=3,
            grid=(steps,),
            in_specs=[block] * 3 + [pl.BlockSpec(memory_space=pl.ANY)] * len(sources),
            out_specs=[block] * 3,
            scratch_shapes=[
                pltpu.VMEM((2, group, unit_rows, width), low),
                pltpu.SemaphoreType.DMA((2, group)),
            ],
        ),
        out_shape=[jax.ShapeDtypeStruct(master.shape, jnp.float32)] * 3,
        compiler_params=pltpu.CompilerParams(vmem_limit_bytes=56 * 2**20),
        cost_estimate=cheap,
        name="update_slots",
    )(filled, which, position, master, first_moment, second_moment, *sources)


def adamw(weight, moment_one, moment_two, gradient, filled, step_rate):
    new_one = beta_one * moment_one + (1.0 - beta_one) * gradient
    new_two = beta_two * moment_two + (1.0 - beta_two) * gradient * gradient
    fixed_one = new_one / (1.0 - beta_one**STEP)
    fixed_two = new_two / (1.0 - beta_two**STEP)
    updated = weight - step_rate * (fixed_one / (jnp.sqrt(fixed_two) + adam_eps) + decay * weight)
    return (new_one * filled, new_two * filled, updated * filled)


def swap(values, axis, bit):
    count = lax.axis_size(axis)
    return lax.ppermute(values, axis, [(i, i ^ (1 << bit)) for i in range(count)])


def choose(values, index, axis):
    return lax.dynamic_index_in_dim(values, index, axis, keepdims=False)


def total_sum(values):
    for axis in ("dp", "tensor"):
        for bit in range(lax.axis_size(axis).bit_length() - 1):
            values = values + swap(values, axis, bit)
    return values


def pick_units(master, slot_unit, state, kind, place, sizes, after=()):
    capacity, unit_rows, width = master.shape
    units = state.shape[0]

    def body(slot_ref, state_ref, kind_ref, place_ref, blocks, *rest):
        outs = rest[len(after) : len(after) + len(sizes)]
        highs, lows, zeros, read, sems = rest[len(after) + len(sizes) :]

        def start(source, unit):
            for which, out in enumerate(outs):

                @pl.when(kind_ref[unit] == which)
                def _():
                    pltpu.make_async_copy(source, out.at[place_ref[unit]], sems.at[unit]).start()

        @pl.loop(0, capacity)
        def _(slot):
            @pl.when(slot_ref[slot] >= 0)
            def _():
                pltpu.make_async_copy(blocks.at[slot], highs.at[slot], read.at[slot]).start()

        zeros[...] = jnp.zeros_like(zeros)

        @pl.loop(0, units)
        def _(unit):
            @pl.when(state_ref[unit] == 0)
            def _():
                start(zeros, unit)

        @pl.loop(0, capacity)
        def _(slot):
            @pl.when(slot_ref[slot] >= 0)
            def _():
                pltpu.make_async_copy(blocks.at[slot], highs.at[slot], read.at[slot]).wait()
                lows[slot] = highs[slot].astype(low)
                start(lows.at[slot], slot_ref[slot])

        @pl.loop(0, units)
        def _(unit):
            @pl.when(state_ref[unit] < 2)
            def _():
                pltpu.make_async_copy(zeros, outs[0].at[0], sems.at[unit]).wait()

    return pl.pallas_call(
        body,
        grid_spec=pltpu.PrefetchScalarGridSpec(
            num_scalar_prefetch=4,
            grid=(1,),
            in_specs=[pl.BlockSpec(memory_space=pl.ANY)] * (1 + len(after)),
            out_specs=[pl.BlockSpec(memory_space=pl.ANY)] * len(sizes),
            scratch_shapes=[
                pltpu.VMEM((capacity, unit_rows, width), jnp.float32),
                pltpu.VMEM((capacity, unit_rows, width), low),
                pltpu.VMEM((unit_rows, width), low),
                pltpu.SemaphoreType.DMA((capacity,)),
                pltpu.SemaphoreType.DMA((units,)),
            ],
        ),
        out_shape=[jax.ShapeDtypeStruct((size, unit_rows, width), low) for size in sizes],
        compiler_params=pltpu.CompilerParams(vmem_limit_bytes=56 * 2**20),
        cost_estimate=cheap,
        name="pick_units",
    )(slot_unit, state, kind, place, master, *after)


def place_blocks(sources, which, position, parts=1):
    amount = which.shape[0]
    shape = sources[0].shape[1:]
    size = amount // parts

    def body(which_ref, position_ref, *rest):
        ins, outs = rest[: len(sources)], rest[len(sources) : len(sources) + parts]
        held, read, sems = rest[len(sources) + parts :]

        @pl.loop(0, amount)
        def _(i):
            for source, ref in enumerate(ins):

                @pl.when(which_ref[i] == source)
                def _():
                    pltpu.make_async_copy(ref.at[position_ref[i]], held.at[i], read.at[i]).start()

        for part, out in enumerate(outs):

            @pl.loop(0, size)
            def _(j):
                i = part * size + j
                pltpu.make_async_copy(ins[0].at[0], held.at[i], read.at[i]).wait()
                pltpu.make_async_copy(held.at[i], out.at[j], sems.at[i]).start()

        @pl.loop(0, amount)
        def _(i):
            pltpu.make_async_copy(held.at[i], outs[0].at[0], sems.at[i]).wait()

    return pl.pallas_call(
        body,
        grid_spec=pltpu.PrefetchScalarGridSpec(
            num_scalar_prefetch=2,
            grid=(1,),
            in_specs=[pl.BlockSpec(memory_space=pl.ANY)] * len(sources),
            out_specs=[pl.BlockSpec(memory_space=pl.ANY)] * parts,
            scratch_shapes=[
                pltpu.VMEM((amount,) + shape, low),
                pltpu.SemaphoreType.DMA((amount,)),
                pltpu.SemaphoreType.DMA((amount,)),
            ],
        ),
        out_shape=[jax.ShapeDtypeStruct((size,) + shape, low)] * parts,
        compiler_params=pltpu.CompilerParams(vmem_limit_bytes=56 * 2**20),
        cost_estimate=cheap,
        name="place_blocks",
    )(which, position, *sources)


def stack_pairs(pairs):
    shape = (len(pairs),) + pairs[0].shape[1:]

    def body(*refs):
        for i, pair in enumerate(refs[:-2]):
            for half in range(2):
                refs[half - 2][i] = pair[half]

    return pl.pallas_call(
        body,
        out_shape=[jax.ShapeDtypeStruct(shape, low)] * 2,
        cost_estimate=costly,
        name="stack_pairs",
    )(*pairs)


def hops(values, step, turn):
    count = lax.axis_size("tensor")
    if step > 0:
        pairs = [(i, i + 1) for i in range(turn - 1, count - 1)]
    else:
        pairs = [(i, i - 1) for i in range(1, count - turn + 1)]
    return lax.ppermute(values, "tensor", pairs)


fence = lax.optimization_barrier


def in_pool(member, inner, inner_count):
    me = lax.axis_index("dp")
    half, core = member >> 3, ((member >> 2) & 1) ^ (me & 1)
    far_y, far_x = ((member >> 1) & 1) ^ ((me >> 2) & 1), (member & 1) ^ ((me >> 1) & 1)
    where_first = (far_y * 2 + far_x) * inner_count
    where_second = (4 + far_x * 2 + far_y) * inner_count
    return (core, jnp.where(half == 0, where_first, where_second) + inner)


def on_device(
    hidden_in,
    time_embed,
    caption_table,
    caption_ids,
    owners,
    master,
    first_moment,
    second_moment,
    mod_table,
    mod_first,
    mod_second,
    out_grad,
):
    count = lax.axis_size("tensor")
    dp_count = lax.axis_size("dp")
    me_dp = lax.axis_index("dp")
    me_tensor = lax.axis_index("tensor")
    capacity, unit_rows, width = master.shape
    units = owners.shape[0]
    tokens = hidden_in.shape[1]
    text_count = caption_ids.shape[1]
    share = width // count
    per = share // unit_rows
    ups = (units - 8 * per) // 2
    rank_of = ranks_of(owners)
    mine = owners == me_dp
    match = (rank_of[None, :] == jnp.arange(capacity)[:, None]) & mine[None, :]
    filled = jnp.any(match, axis=1)
    unit_of_slot = jnp.sum(jnp.where(match, jnp.arange(units)[None, :], 0), axis=1)

    square = [list(range(i * per, (i + 1) * per)) for i in range(8)]
    group_attn = square[0] + square[1] + square[2] + square[5]
    group_full = square[3] + square[4] + square[6] + square[7]
    group_mlp = list(range(8 * per, units))
    members = len(group_attn)
    plane = dp_count == 8 and members == 16 and len(group_mlp) % dp_count == 0
    member_of = np.zeros(units, np.int32)
    member_of[group_attn] = np.arange(members)
    member_of[group_full] = np.arange(members)
    is_attn = np.zeros(units, bool)
    is_attn[group_attn] = True
    is_mlp = np.zeros(units, bool)
    is_mlp[group_mlp] = True

    latent_in = hidden_in[0].astype(jnp.float32)
    modulate = mod_table + time_embed[0]

    def mod_row(which_row):
        return modulate[which_row][None, :]

    normed_one, inverse_one = layer_norm(latent_in)
    bits = dp_count.bit_length() - 1
    vocab_rows = caption_table.shape[0]

    def caption_terms(ids):
        chosen = ids.reshape(-1) - me_dp * vocab_rows
        onehot = (chosen[:, None] == jnp.arange(vocab_rows)[None, :]).astype(low)
        terms = jnp.dot(onehot, caption_table, preferred_element_type=jnp.float32).astype(low)
        return terms.reshape(dp_count, text_count, -1)

    def modulated(normed):
        return (normed.astype(jnp.float32) * (1.0 + mod_row(1)) + mod_row(0)).astype(low)

    def whole_text(text_ring):
        return from_ring(text_ring, -1).transpose(1, 0, 2).reshape(text_count, width)

    def own_keys(text_low, w_attn):
        return project(text_low, w_attn)[:, 3 * share :].astype(low)

    def exchanged(attended, keys):
        parts = [
            jnp.concatenate([attended[k * tokens : (k + 1) * tokens], keys]) for k in range(count)
        ]
        return [parts[0]] + [shift(parts[k], count - k) for k in range(1, count)]

    where = jnp.stack([me_tensor, me_dp & 1]).astype(jnp.int32)

    n_low = normed_one.astype(low)
    if plane:
        core, far_x, far_y = (
            ((member_of >> 2) & 1) ^ (me_dp & 1),
            (member_of & 1) ^ ((me_dp >> 1) & 1),
            ((member_of >> 1) & 1) ^ ((me_dp >> 2) & 1),
        )
        place = jnp.where(is_attn, far_x * 4 + far_y * 2, 8 + far_y * 4 + far_x * 2)
        place = jnp.where(is_mlp, np.arange(units) - 8 * per, place + (member_of >> 3))
        kind = jnp.where(is_mlp, 0, core)
        slot_mlp = unit_of_slot >= 8 * per
        owned_state = mine.astype(jnp.int32)
        ids = lax.all_gather(caption_ids, "dp", axis=0, tiled=True)
        ids = jnp.take(ids, me_dp ^ jnp.arange(dp_count), axis=0, mode="clip")
        up, down = hops(n_low, 1, 1), hops(n_low, -1, 1)
        kept, given = pick_units(
            master,
            jnp.where(filled & ~slot_mlp, unit_of_slot, -1),
            jnp.where(is_mlp, 2, owned_state),
            kind,
            place,
            (members, members),
        )
        got = swap(given, "dp", 0)
        (mlp_part,) = pick_units(
            master,
            jnp.where(filled & slot_mlp, unit_of_slot, -1),
            jnp.where(is_mlp, owned_state, 2),
            kind,
            place,
            (len(group_mlp),),
            (kept,),
        )
        mlp_part = lax.psum_scatter(mlp_part, "dp", scatter_dimension=0, tiled=True)
        n_up, n_down = [up], [down]
        kept, got, up, down, ids = fence((kept, got, up, down, ids))
        pieces = [kept[i : i + 4] + got[i : i + 4] for i in range(0, members, 4)]
        attn_two, attn_send, full_two, full_send = fence(tuple(pieces))
        up, down = hops(up, 1, 2), hops(down, -1, 2)
        attn_got = swap(attn_send, "dp", 1)
        full_got = swap(full_send, "dp", 2)
        text = caption_terms(ids)
        n_up.append(up), n_down.append(down)
        attn_two, attn_got, full_two, full_got, up, down, text = fence(
            (attn_two, attn_got, full_two, full_got, up, down, text)
        )
        pieces = [x[i : i + 2] + y[i : i + 2] for x, y in ((attn_two, attn_got), (full_two, full_got)) for i in (0, 2)]
        attn_one, attn_send, full_one, full_send = fence(tuple(pieces))
        up, down = hops(up, 1, 3), hops(down, -1, 3)
        attn_got = swap(attn_send, "dp", 2)
        full_got = swap(full_send, "dp", 1)
        text = text[0:4] + swap(text[4:8], "dp", 2)
        n_up.append(up), n_down.append(down)
        attn_one, attn_got, full_one, full_got, up, down, text, mlp_part = fence(
            (attn_one, attn_got, full_one, full_got, up, down, text, mlp_part)
        )
        attn_one, full_one = attn_one + attn_got, full_one + full_got
        n_up[-1], n_down[-1] = up, down
        w_mlp = lax.all_gather(mlp_part, "dp", axis=0, tiled=True)
        first_ring, second_ring = stack_pairs(ring(full_one))
        first = jnp.concatenate([attn_one[0:1], swap(attn_one[0:1], "dp", 1)])
        second = jnp.concatenate([attn_one[1:2], swap(attn_one[1:2], "dp", 2)])
        pool = jnp.concatenate([first, swap(first, "dp", 2), second, swap(second, "dp", 1)])
        other = swap(pool, "dp", 0)
        text = text[0:2] + swap(text[2:4], "dp", 1)
        text = text[0] + swap(text[1], "dp", 0)
        *n_slots, h_one_all = line_slots(
            where, n_low, n_up, n_down, jnp.concatenate([mod_row(0), mod_row(1)])
        )
        n_slots = [n_low] + n_slots
        grad_own = out_grad[0]
        pool, other, first_ring, second_ring, h_one_all, text, grad_own = fence(
            (pool, other, first_ring, second_ring, h_one_all, text, grad_own)
        )
        grad_whole = lax.all_gather(grad_own, "tensor", axis=0)
        first, second = first_ring, second_ring
        first_got = swap(first, "dp", 1)
        second_got = swap(second, "dp", 2)
        text_ring = ring(text)
        (w_attn,) = place_blocks((pool, other), *in_pool(np.arange(members), 0, 1))
        w_attn = w_attn.reshape(-1, width)
        qkv = project(h_one_all, w_attn).astype(low)
        attended, logs = self_attend(qkv, share)
        first = jnp.concatenate([first, first_got])
        second = jnp.concatenate([second, second_got])
        first, second, text_ring, attended, logs, w_attn, w_mlp = fence(
            (first, second, text_ring, attended, logs, w_attn, w_mlp)
        )
        first_far, second_far = swap(first, "dp", 2), swap(second, "dp", 1)
        text_low = whole_text(jnp.stack(text_ring))
        mixed = exchanged(attended, own_keys(text_low, w_attn))
        first_far, second_far, mixed = fence((first_far, second_far, mixed))
        first_other, second_other = swap(first, "dp", 0), swap(second, "dp", 0)
        first_last, second_last = swap(first_far, "dp", 0), swap(second_far, "dp", 0)
        listing = np.arange(count * members)
        matrix, rank, head = listing // (count * per), listing // per % count, listing % per
        slot = lax.rem(me_tensor - rank + count, count)
        which, position = in_pool(matrix * per + head, slot, count)
        blocks = 2 * count
        w_full = place_blocks(
            (first, first_far, second, second_far, first_other, first_last, second_other, second_last),
            which * 4 + position // blocks,
            position % blocks,
            parts=4,
        )
        w_full = [part.reshape(width, width) for part in w_full]
        w_full[3], grad_whole = fence((w_full[3], grad_whole))
    else:
        slots_low = master.astype(low)
        rows = jnp.take(slots_low, rank_of, axis=0, mode="clip")
        rows = lax.psum(jnp.where(mine[:, None, None], rows, jnp.zeros((), low)), "dp")
        w_attn = rows[np.array(group_attn)].reshape(-1, width)
        w_full = lax.all_gather(rows[np.array(group_full)], "tensor", axis=0)
        w_full = w_full.reshape(count, 4, share, width).swapaxes(0, 1).reshape(4, width, width)
        w_full = [w_full[i] for i in range(4)]
        w_mlp = rows[8 * per :]
        n_slots = ring(n_low)
        normed_all = jnp.concatenate(n_slots)
        grad_whole = lax.all_gather(out_grad[0], "tensor", axis=0)
        ids = caption_ids
        for bit in range(bits):
            ids = jnp.concatenate([ids, swap(ids, "dp", bit)])
        text = caption_terms(ids)
        for bit in reversed(range(bits)):
            text = text[: 1 << bit] + swap(text[1 << bit :], "dp", bit)
        text_low = whole_text(jnp.stack(ring(text[0])))
        h_one_all = modulated(normed_all)
        qkv = project(h_one_all, w_attn).astype(low)
        attended, logs = self_attend(qkv, share)
        mixed = exchanged(attended, own_keys(text_low, w_attn))
    w_cross = w_full
    w_out, c_query, c_value, c_out = w_full
    w_mlp = w_mlp.reshape(-1, width)

    rows = jnp.concatenate([mod_row(2), mod_row(3), mod_row(4)])
    (
        branch_one,
        first_low,
        cq_rows,
        ck_rows,
        cv_rows,
        crossed,
        second_res,
        normed_two,
        h_two,
        inverse_two,
    ) = cross_block(
        where, mixed, hidden_in[0], rows, text_low, *w_cross
    )

    h_slots = {0: h_two}
    out_slots = [
        choose(grad_whole, lax.rem(me_tensor - k + count, count), 0) for k in range(count)
    ]
    grad_slots = [(mod_row(5) * item.astype(jnp.float32)).astype(low) for item in out_slots]
    near = [k for k in range(1, count) if 2 * k != count]
    far = [k for k in range(1, count) if 2 * k == count]
    acts, grad_pres, grad_terms, order = [], [], [], []
    for k in near:
        h_slots[k] = shift(h_two, k)
    for members_now in ([0], near, far):
        act, grad_pre, *terms = mlp_core(
            [h_slots[k] for k in members_now],
            [grad_slots[k] for k in members_now],
            w_mlp,
            acts[-1:],
        )
        if members_now == [0]:
            h_two, act = fence((h_two, act))
            for k in far:
                h_slots[k] = shift(h_two, k)
        acts.append(act), grad_pres.append(grad_pre)
        order += members_now
        grad_terms += [
            shift(term, count - k) if k else term for k, term in zip(members_now, terms)
        ]
    mlp_grad = mlp_grads(
        grad_pres,
        acts,
        [h_slots[k] for k in order],
        [grad_slots[k] for k in order],
        grad_terms[1:],
    ).reshape(-1, unit_rows, width)
    hidden_share = w_mlp.shape[0] // 2
    pieces = [
        [(which, row, 0, hidden_share, hidden_share)]
        for which, act in enumerate(acts)
        for row in range(0, act.shape[0], tokens)
    ]
    branch_terms, branch_sums = ranked_terms(
        where, acts, order, pieces, w_mlp, [out_slots[k] for k in order], "mlp_out"
    )
    branch_row = branch_sums[1]
    if plane:
        mlp_sum = lax.psum_scatter(mlp_grad, "dp", scatter_dimension=0, tiled=True)

    (
        first_grad,
        cross_low,
        grad_cq,
        attn_low,
        grad_cv,
        row_sums,
        *grad_mixed,
    ) = cross_back(
        where,
        grad_terms,
        out_grad[0],
        rows,
        normed_two,
        inverse_two,
        branch_one,
        cq_rows,
        ck_rows,
        cv_rows,
        c_out,
        c_query,
        w_out,
        (),
    )

    grad_parts = [grad_mixed[0]] + [shift(grad_mixed[k], k) for k in range(1, count)]
    full_pairs = [
        ([(item, 0, share, None) for item in mixed], attn_low),
        ([(grad_cq, 0, width, 0)], first_low),
        ([(grad_cv, 0, width, 0)], text_low),
        ([(crossed, 0, width, 0)], cross_low),
    ]
    half = (share // HEAD_DIM // 2) * HEAD_DIM
    spans = [(0, half), (half, share)]

    def attention_pairs(grads, grad_parts):
        keys = sum(item[tokens:].astype(jnp.float32) for item in grad_parts).astype(low)
        pairs = [
            (
                [
                    (item, i * (end - begin), end - begin, begin)
                    for item, (begin, end) in zip(grads, spans)
                ],
                h_one_all,
            )
            for i in range(3)
        ]
        return pairs + [([(keys, 0, share, 0)], text_low)]

    def input_terms(grads):
        pieces = [
            [
                (which, slot * tokens, i * (end - begin), i * share + begin, end - begin)
                for which, (begin, end) in enumerate(spans)
                for i in range(3)
            ]
            for slot in range(count)
        ]
        return ranked_terms(where, grads, range(count), pieces, w_attn, n_slots, "attn_terms")

    if plane:
        x_bit, y_bit = (me_dp >> 1) & 1, (me_dp >> 2) & 1

        def split(total, bit, axis):
            return (choose(total, bit, axis), choose(total, 1 - bit, axis))

        kept, given = outer_halves(where, full_pairs, count, "full_grads")
        got = swap(given, "dp", 0)
        grad_parts, kept, got, branch_terms = fence((grad_parts, kept, got, branch_terms))
        branch_two = lax.psum_scatter(
            branch_terms.reshape(-1, width), "tensor", scatter_dimension=0, tiled=True
        )
        box = (2, count, 2, 2, unit_rows, width)
        bits_here = jnp.stack([x_bit, y_bit]).astype(jnp.int32)
        kept_one, given_one, kept_two, given_two = sum_split(
            bits_here, kept.reshape(box), got.reshape(box)
        )
        got_one, got_two = swap(given_one, "dp", 1), swap(given_two, "dp", 2)
        grads_early = self_attend_back(qkv, grad_parts, attended, logs, share, *spans[0])
        kept_one, got_one, kept_two, got_two, grads_early, grad_parts = fence(
            (kept_one, got_one, kept_two, got_two, grads_early, grad_parts)
        )
        kept_one, given_one = split(kept_one + got_one, y_bit, 1)
        kept_two, given_two = split(kept_two + got_two, x_bit, 1)
        kept_one, given_one, kept_two, given_two, grad_parts = fence(
            (kept_one, given_one, kept_two, given_two, grad_parts)
        )
        got_one, got_two = swap(given_one, "dp", 2), swap(given_two, "dp", 1)
        grads_late = self_attend_back(qkv, grad_parts, attended, logs, share, *spans[1])
        kept_one, got_one, kept_two, got_two, grads_early, grads_late, mlp_sum = fence(
            (kept_one, got_one, kept_two, got_two, grads_early, grads_late, mlp_sum)
        )
        mlp_sum = lax.all_gather(mlp_sum, "dp", axis=0, tiled=True)
        full_parts = to_ring(jnp.stack([kept_one + got_one, kept_two + got_two], axis=1))
        full_parts = [full_parts[k] for k in range(count)]
        full_parts, grads_early, grads_late = fence((full_parts, grads_early, grads_late))
        grads_qkv = [grads_early, grads_late]
        full_got = [shift(full_parts[k], k) for k in range(1, count)]
        attn_kept, attn_given = outer_halves(
            where, attention_pairs(grads_qkv, grad_parts), 1, "attn_grads"
        )
        attn_got = swap(attn_given, "dp", 0)
        grad_h_terms, grad_h_sums = input_terms(grads_qkv)
        mod_terms = jnp.concatenate([grad_h_sums, row_sums, branch_row[None]])
        grad_h_one = lax.psum_scatter(
            grad_h_terms.reshape(-1, width), "tensor", scatter_dimension=0, tiled=True
        )
        attn_kept, attn_got, mod_terms, branch_two = fence(
            (attn_kept, attn_got, mod_terms, branch_two)
        )
        attn_all = (attn_kept + attn_got).reshape(2, 2, 2, unit_rows, width)
        one_kept, one_given = split(attn_all[0], x_bit, 1)
        two_kept, two_given = split(attn_all[1], y_bit, 0)
        one_got, two_got = swap(one_given, "dp", 1), swap(two_given, "dp", 2)
        for bit in range(2):
            mod_terms = mod_terms + swap(mod_terms, "dp", bit)
        full_own = full_parts[0]
        one_kept, one_got, two_kept, two_got, mod_terms, full_own, full_got = fence(
            (one_kept, one_got, two_kept, two_got, mod_terms, full_own, full_got)
        )
        full_sum = full_own.astype(jnp.float32)
        for part in full_got:
            full_sum = full_sum + part.astype(jnp.float32)
        full_sum = full_sum.astype(low)
        one_kept, one_given = split(one_kept + one_got, y_bit, 0)
        two_kept, two_given = split(two_kept + two_got, x_bit, 0)
        one_got, two_got = swap(one_given, "dp", 2), swap(two_given, "dp", 1)
        mod_terms = mod_terms + swap(mod_terms, "dp", 2)
        one_kept, one_got, two_kept, two_got, full_sum, mod_terms, mlp_sum = fence(
            (one_kept, one_got, two_kept, two_got, full_sum, mod_terms, mlp_sum)
        )
        first = jnp.stack([one_kept + one_got, full_sum[0]])
        second = jnp.stack([two_kept + two_got, full_sum[1]])
        first_got, second_got = swap(first, "dp", 1), swap(second, "dp", 2)
        first = jnp.concatenate([first, first_got])
        second = jnp.concatenate([second, second_got])
        mod_terms = mod_terms + swap(mod_terms, "tensor", 0)
        first, second, mod_terms = fence((first, second, mod_terms))
        first_far, second_far = swap(first, "dp", 2), swap(second, "dp", 1)
        for bit in range(1, count.bit_length() - 1):
            mod_terms = mod_terms + swap(mod_terms, "tensor", bit)
        first, first_far, second, second_far, mod_terms = fence(
            (first, first_far, second, second_far, mod_terms)
        )
        pool = jnp.concatenate([first, first_far, second, second_far])
        other = swap(pool, "dp", 0)
        mod_grad = mod_terms
        pool, other = fence((pool, other))
        which, position = in_pool(member_of, np.where(is_attn, 0, 1), 2)
        which = jnp.where(is_mlp, 2, which)
        position = jnp.where(is_mlp, np.arange(units) - 8 * per, position)
        own = jnp.sum(jnp.where(match[:, :, None], jnp.stack([which, position], 1)[None], 0), axis=1)
        new_first, new_second, new_master = update_slots(
            master,
            first_moment,
            second_moment,
            filled.astype(jnp.int32),
            own[:, 0],
            own[:, 1],
            (pool, other, mlp_sum),
        )
    else:
        branch_two = lax.psum_scatter(
            branch_terms.reshape(-1, width), "tensor", scatter_dimension=0, tiled=True
        )
        grads_qkv = [self_attend_back(qkv, grad_parts, attended, logs, share, *span) for span in spans]
        attn_grads = [
            outer(array[:, lane : lane + lanes], right).astype(low)
            for left, right in attention_pairs(grads_qkv, grad_parts)
            for array, lane, lanes, row in left
        ]
        grad_h_terms, grad_h_sums = input_terms(grads_qkv)
        grad_h_one = lax.psum_scatter(
            grad_h_terms.reshape(-1, width), "tensor", scatter_dimension=0, tiled=True
        )
        mixed_all = from_ring(jnp.stack([item[:tokens] for item in mixed]), 1)
        mixed_all = mixed_all.transpose(1, 0, 2).reshape(tokens, width)
        full_grads = [outer(mixed_all, attn_low)]
        full_grads += [outer(left[0][0], right) for left, right in full_pairs[1:]]
        full_sum = [g.astype(low).reshape(count, share, width) for g in full_grads]
        full_sum = jnp.stack(full_sum, axis=1)
        full_sum = lax.psum_scatter(full_sum, "tensor", scatter_dimension=0, tiled=True)
        order = np.array(group_attn + group_full + group_mlp)
        sums = jnp.concatenate(
            [jnp.concatenate(attn_grads), full_sum.reshape(-1, width), mlp_grad.reshape(-1, width)]
        )
        sums = lax.psum(sums.reshape(units, unit_rows, width), "dp")
        owned = jnp.take(sums, jnp.array(np.argsort(order))[unit_of_slot], axis=0, mode="clip")
        mod_grad = total_sum(jnp.concatenate([grad_h_sums, row_sums, branch_row[None]]))
        new_first, new_second, new_master = adamw(
            master,
            first_moment,
            second_moment,
            owned.astype(jnp.float32),
            filled.astype(jnp.float32)[:, None, None],
            rate,
        )
    branch_two, second_res, grad_h_one, new_first = fence(
        (branch_two, second_res, grad_h_one, new_first)
    )
    grad_h_one = grad_h_one.astype(jnp.float32)
    block_out = second_res + mod_row(5) * branch_two.astype(jnp.float32)
    input_grad = first_grad + norm_back(grad_h_one, normed_one, inverse_one, mod_row(1))
    mod_new_first, mod_new_second, mod_new = adamw(
        mod_table, mod_first, mod_second, mod_grad, 1.0, table_rate
    )
    return (
        block_out[None],
        input_grad[None],
        new_first,
        new_second,
        new_master,
        mod_new_first,
        mod_new_second,
        mod_new,
    )


def solution(mesh):
    in_specs = (
        P("dp", "tensor", None),
        P("dp", None, None),
        P("dp", "tensor"),
        P("dp", None),
        P(),
        P("dp", "tensor", None),
        P("dp", "tensor", None),
        P("dp", "tensor", None),
        P(),
        P(),
        P(),
        P("dp", "tensor", None),
    )
    out_specs = (
        P("dp", "tensor", None),
        P("dp", "tensor", None),
        P("dp", "tensor", None),
        P("dp", "tensor", None),
        P("dp", "tensor", None),
        P(),
        P(),
        P(),
    )
    return jax.shard_map(
        on_device, mesh=mesh, in_specs=in_specs, out_specs=out_specs, check_vma=False
    )
```
